32 devices in a mesh: seq: 8 (over y, x, core), mp: 4 (over z).
Axes of the slice: x: 2, y: 2, z: 4, core: 2. Of those that a mesh axis runs over, the one named last changes fastest.
Arguments:
- stream: float32 [8, 1024, 2048], P(None, 'seq'), may hold values from -6 to 6
- norm_in: float32 [2048], replicated, may hold values from 0.5 to 1.5
- w_branch: bfloat16 [2048, 2560], P(None, 'mp'), may hold values from -0.125 to 0.125
- w_input: bfloat16 [2048, 2560], P(None, 'mp'), may hold values from -0.125 to 0.125
- conv_kernel: float32 [4, 2560], P(None, 'mp'), may hold values from -3 to 3
- conv_bias: float32 [2560], P('mp'), may hold values from -3 to 3
- gate_r: bfloat16 [16, 160, 160], P('mp'), may hold values from -0.5 to 0.5
- bias_r: float32 [2560], P('mp'), may hold values from -3 to 3
- gate_i: bfloat16 [16, 160, 160], P('mp'), may hold values from -0.5 to 0.5
- bias_i: float32 [2560], P('mp'), may hold values from -3 to 3
- decay_param: float32 [2560], P('mp'), may hold values from 4.5 to 9.3
- w_out: bfloat16 [2560, 2048], P('mp'), may hold values from -0.15625 to 0.15625
- norm_mlp: float32 [2048], replicated, may hold values from 0.5 to 1.5
- w_gate: bfloat16 [2048, 6144], P(None, 'mp'), may hold values from -0.125 to 0.125
- w_up: bfloat16 [2048, 6144], P(None, 'mp'), may hold values from -0.125 to 0.125
- w_down: bfloat16 [6144, 2048], P('mp'), may hold values from -0.15625 to 0.15625
- state_init: float32 [8, 2560], P(None, 'mp'), may hold values from -6 to 6
- conv_init: float32 [8, 3, 2560], P(None, None, 'mp'), may hold values from -6 to 6
- fresh_rows: int32 [8], replicated, may hold values from 0 to 1, as said below
- out_grad: float32 [8, 1024, 2048], P(None, 'seq'), may hold values from -8 to 8
Outputs:
- block_out: float32 [8, 1024, 2048], P(None, 'seq')
- stream_grad: float32 [8, 1024, 2048], P(None, 'seq')
- norm_in_grad: float32 [2048], replicated
- w_branch_grad: float32 [2048, 2560], P('seq', 'mp')
- w_input_grad: float32 [2048, 2560], P('seq', 'mp')
- conv_kernel_grad: float32 [4, 2560], P(None, 'mp')
- conv_bias_grad: float32 [2560], P('mp')
- gate_r_grad: float32 [16, 160, 160], P('mp')
- bias_r_grad: float32 [2560], P('mp')
- gate_i_grad: float32 [16, 160, 160], P('mp')
- bias_i_grad: float32 [2560], P('mp')
- decay_grad: float32 [2560], P('mp')
- w_out_grad: float32 [2560, 2048], P('mp', 'seq')
- norm_mlp_grad: float32 [2048], replicated
- w_gate_grad: float32 [2048, 6144], P('seq', 'mp')
- w_up_grad: float32 [2048, 6144], P('seq', 'mp')
- w_down_grad: float32 [6144, 2048], P('mp', 'seq')
- final_state: float32 [8, 2560], P(None, 'mp')
- final_conv: float32 [8, 3, 2560], P(None, None, 'mp')
The draws below stay inside these ranges and needn't reach their ends.
Inputs may be any that keep to these rules, and one draw needn't show every extreme that they name: `fresh_rows`: half of the 8 sequences, chosen by the seed, are fresh.
All inputs are finite; a program needn't handle non-finite values.
Results may differ from the reference program's by a relative error of at most 0.0087.
Values sent between devices are 32-bit elements; how exact they have to be, the bound alone decides.
A program may use at most 320 MiB of HBM per device.

```python
import math
import jax
import jax.numpy as jnp
from jax import lax

D = 2048
R = 2560
H = 16
BW = 160
F = 6144
KW = 4
SEQS = 8
LENGTH = 1024


def draw_fresh_rows(key, part):
    key = jax.random.fold_in(key, 5)
    shuffled = jax.random.permutation(key, SEQS)
    return (shuffled < SEQS // 2).astype(jnp.int32)


def draw_decay_param(key, part):
    key = jax.random.fold_in(key, 9)
    upper_rate = 0.01
    rate_value = jnp.exp(jax.random.uniform(key, (R,), jnp.float32, math.log(0.0001), math.log(upper_rate)))
    return -jnp.log(jnp.expm1(rate_value))


def strengthened(entries, rng, source, target, parts, factor):
    def block_of(dim):
        return (jnp.arange(entries.shape[dim]) // (entries.shape[dim] // parts)).reshape((-1,) + (1,) * (entries.ndim - 1 - dim))

    first = jax.random.permutation(rng, parts)[block_of(target)]
    far = (block_of(target) + parts // 2) % parts
    return jnp.where((block_of(source) == first) | (block_of(source) == far), factor * entries, entries)


def shard_levels(stream_key, extent, shards, smallest, largest):
    factor_of = 1.0
    for position, blocks in shards:
        heights = jax.random.uniform(jax.random.fold_in(jax.random.fold_in(stream_key, 6), position), (blocks,), jnp.float32, smallest / len(shards), largest / len(shards))
        factor_of = factor_of * jnp.repeat(jnp.exp(heights), extent[position] // blocks).reshape((-1,) + (1,) * (len(extent) - 1 - position))
    return factor_of


def noise(rng, dims, scale, limit, cuts=(), dtype=jnp.bfloat16):
    drawn = jax.random.normal(rng, dims, jnp.float32) * scale
    if len(cuts) > 0:
        drawn = shard_levels(rng, dims, cuts, -0.22, 0.18) * drawn
    return jnp.clip(drawn, min=-limit, max=limit).astype(dtype)


def heavy_noise(rng, dims, deviation, reach, split, heavy, kind=jnp.bfloat16):
    values = deviation * jax.random.normal(rng, dims, jnp.float32)
    if split:
        values = values * shard_levels(rng, dims, split, -0.22, 0.18)
    return jnp.clip(strengthened(values, jax.random.fold_in(rng, 3), *heavy), -reach, reach).astype(kind)


def setup_inputs(seed: int = 0) -> dict:
    key_of = jax.random.split(jax.random.key(seed), 21)
    return {
        "stream": noise(key_of[0], (SEQS, LENGTH, D), 1.0, 6.0, ((1, 8),), jnp.float32),
        "norm_in": jnp.clip(1.0 + 0.1 * jax.random.normal(key_of[1], (D,), jnp.float32), 0.5, 1.5),
        "w_branch": noise(key_of[2], (D, R), D ** -0.5, 0.125, ((1, 4),)),
        "w_input": noise(key_of[3], (D, R), D ** -0.5, 0.125, ((1, 4),)),
        "conv_kernel": noise(key_of[4], (KW, R), 0.5, 3.0, ((1, 4),), jnp.float32),
        "conv_bias": noise(key_of[5], (R,), 0.5, 3.0, ((0, 4),), jnp.float32),
        "gate_r": noise(key_of[6], (H, BW, BW), BW ** -0.5, 0.5, ((0, 4),)),
        "bias_r": noise(key_of[7], (R,), 0.5, 3.0, ((0, 4),), jnp.float32),
        "gate_i": noise(key_of[8], (H, BW, BW), BW ** -0.5, 0.5, ((0, 4),)),
        "bias_i": noise(key_of[9], (R,), 0.5, 3.0, ((0, 4),), jnp.float32),
        "decay_param": draw_decay_param(jax.random.fold_in(key_of[20], 71), 0),
        "w_out": noise(key_of[11], (R, D), (R // 2) ** -0.5, 0.15625, ((0, 4),)),
        "norm_mlp": jnp.clip(1.0 + 0.1 * jax.random.normal(key_of[12], (D,), jnp.float32), 0.5, 1.5),
        "w_gate": noise(key_of[13], (D, F), D ** -0.5, 0.125, ((1, 4),)),
        "w_up": noise(key_of[14], (D, F), D ** -0.5, 0.125, ((1, 4),)),
        "w_down": noise(key_of[15], (F, D), (F // 4) ** -0.5, 0.15625, ((0, 4),)),
        "state_init": noise(key_of[16], (SEQS, R), 1.0, 6.0, ((1, 4),), jnp.float32),
        "conv_init": noise(key_of[17], (SEQS, KW - 1, R), 1.0, 6.0, ((2, 4),), jnp.float32),
        "fresh_rows": draw_fresh_rows(jax.random.fold_in(key_of[20], 71), 0),
        "out_grad": heavy_noise(key_of[19], (SEQS, LENGTH, D), 1.0, 8.0, ((1, 8),), (1, 2, 8, 2.0), jnp.float32),
    }


@jax.custom_vjp
def low(v):
    return lax.optimization_barrier(v.astype(jnp.bfloat16)).astype(jnp.float32)

@jax.custom_vjp
def low_back(v):
    return v

def low_keep(v):
    return (low(v), None)

def low_pass(kept, grad):
    return (grad,)

def back_keep(v):
    return (v, None)

def back_low(kept, grad):
    return (low(grad),)
low.defvjp(low_keep, low_pass)
low_back.defvjp(back_keep, back_low)
RATE_SCALE = 8.0
HIGHEST = lax.Precision.HIGHEST

def rms_scale(values, gain):
    return values * lax.rsqrt(lax.optimization_barrier(jnp.mean(values * values, axis=-1, keepdims=True)) + 1e-06) * gain

def matmul(left_side, right_side):
    return jnp.dot(left_side, right_side, precision=HIGHEST)

def linear_combine(first, second):
    return (first[0] * second[0], second[0] * first[1] + second[1])

def block_forward(params, state_init, conv_init, keep_state):
    stream, norm_in, w_branch, w_input, conv_kernel, conv_bias, gate_r, bias_r, gate_i, bias_i, decay_param, w_out, norm_mlp, w_gate, w_up, w_down = params
    normed_in = low(rms_scale(stream, norm_in))
    branch_pre = low_back(matmul(normed_in, w_branch))
    conv_in = low_back(matmul(normed_in, w_input))
    length = conv_in.shape[1]
    padded = jnp.concatenate([conv_init * keep_state[:, None, None], conv_in], axis=1)
    conv_out = conv_bias + sum((conv_kernel[offset] * padded[:, offset:offset + length] for offset in range(KW)))
    heads_in = low(conv_out).reshape(conv_out.shape[:2] + (H, BW))
    gate_pre_r = low_back(jnp.einsum('sthi,hij->sthj', heads_in, gate_r, precision=HIGHEST)).reshape(conv_out.shape) + bias_r
    gate_pre_i = low_back(jnp.einsum('sthi,hij->sthj', heads_in, gate_i, precision=HIGHEST)).reshape(conv_out.shape) + bias_i
    recall = jax.nn.sigmoid(gate_pre_r)
    input_gate = jax.nn.sigmoid(gate_pre_i)
    log_decay = -RATE_SCALE * jax.nn.softplus(-decay_param) * recall
    decay_step = jnp.exp(log_decay)
    scaled_in = jnp.sqrt(-jnp.expm1(2.0 * log_decay)) * input_gate * conv_out
    prod_decay, local_state = lax.associative_scan(linear_combine, (decay_step, scaled_in), axis=1)
    hidden_state = local_state + prod_decay * (state_init * keep_state[:, None])[:, None, :]
    mixed_rows = low(hidden_state * jax.nn.gelu(branch_pre))
    residual = stream + low_back(matmul(mixed_rows, w_out))
    normed_mlp = low(rms_scale(residual, norm_mlp))
    gate_val = low_back(matmul(normed_mlp, w_gate))
    up_val = low_back(matmul(normed_mlp, w_up))
    hidden_mlp = low(jax.nn.gelu(gate_val) * up_val)
    output = residual + low_back(matmul(hidden_mlp, w_down))
    return (output, (hidden_state[:, -1, :], conv_in[:, length - (KW - 1):, :]))

def reference(stream, norm_in, w_branch, w_input, conv_kernel, conv_bias, gate_r, bias_r, gate_i, bias_i, decay_param, w_out, norm_mlp, w_gate, w_up, w_down, state_init, conv_init, fresh_rows, out_grad):
    keep_state = 1.0 - fresh_rows.astype(jnp.float32)
    params = tuple((member.astype(jnp.float32) for member in (stream, norm_in, w_branch, w_input, conv_kernel, conv_bias, gate_r, bias_r, gate_i, bias_i, decay_param, w_out, norm_mlp, w_gate, w_up, w_down)))
    output, pullback, finals = jax.vjp(lambda weights: block_forward(weights, state_init, conv_init, keep_state), params, has_aux=True)
    gradients = pullback(out_grad)[0]
    return (output, gradients[0], gradients[1], gradients[2], gradients[3], gradients[4], gradients[5], gradients[6], gradients[7], gradients[8], gradients[9], gradients[10], gradients[11], gradients[12], gradients[13], gradients[14], gradients[15], finals[0], finals[1])
```

```python
import functools

import jax
import jax.numpy as jnp
from jax import lax
from jax.experimental import pallas as pl
from jax.experimental.pallas import tpu as pltpu
from jax.sharding import PartitionSpec as P

MESH = pl.DeviceIdType.MESH
RATE_SCALE = 8.0
EPS = 1e-06
GELU_C = 0.7978845608028654
GELU_K = 0.044715
CONTRACT_ROWS = (((0,), (0,)), ((), ()))
CONTRACT_LAST = (((1,), (1,)), ((), ()))
TILE = 8
LANES = 128
ROWS = 32
F32 = jnp.float32
BF16 = jnp.bfloat16
VMEM = pl.BlockSpec(memory_space=pltpu.VMEM)


def dot(a, b):
    return jnp.dot(a, b, preferred_element_type=F32)


def matmul_back(a, b):
    return lax.dot_general(a, b, CONTRACT_LAST, preferred_element_type=F32)


def block(i, size):
    return pl.ds(pl.multiple_of(i * size, size), size)


def gelu(x):
    t = jnp.tanh(GELU_C * (x + GELU_K * (x * x * x)))
    return 0.5 * x * (1.0 + t)


def gelu_both(x):
    x2 = x * x
    t = jnp.tanh(GELU_C * (x + GELU_K * (x2 * x)))
    half = 0.5 * (1.0 + t)
    slope = half + 0.5 * x * (1.0 - t * t) * (GELU_C * (1.0 + (3.0 * GELU_K) * x2))
    return x * half, slope


def one_minus_square(log_a, a):
    y = 2.0 * log_a
    s = 1.0 + y * (1.0 / 8.0)
    for k in (7, 6, 5, 4, 3, 2):
        s = 1.0 + (y * (1.0 / k)) * s
    return jnp.where(y > -0.35, -y * s, 1.0 - a * a)


def get(ref, at):
    return jnp.concatenate([ref[j, at, :] for j in range(ref.shape[0])], axis=-1)


def put(ref, at, value):
    for j in range(ref.shape[0]):
        ref[j, at, :] = value[:, j * LANES : (j + 1) * LANES]


def enter(axis):
    size, me = lax.axis_size(axis), lax.axis_index(axis)
    barrier = pltpu.get_barrier_semaphore()
    for d in range(1, size):
        pl.semaphore_signal(
            barrier, 1, device_id={axis: lax.rem(me + d, size)}, device_id_type=MESH
        )
    pl.semaphore_wait(barrier, size - 1)


def to_all(axis, src, slots, send, recv):
    size, me = lax.axis_size(axis), lax.axis_index(axis)
    return [
        pltpu.make_async_remote_copy(
            src_ref=src,
            dst_ref=slots.at[me],
            send_sem=send.at[d - 1],
            recv_sem=recv.at[d - 1],
            device_id={axis: lax.rem(me + d, size)},
            device_id_type=MESH,
        )
        for d in range(1, size)
    ]


def to_one(axis, distance, src, dst, send, recv):
    size, me = lax.axis_size(axis), lax.axis_index(axis)
    return pltpu.make_async_remote_copy(
        src_ref=src,
        dst_ref=dst,
        send_sem=send,
        recv_sem=recv,
        device_id={axis: lax.rem(me + distance + size, size)},
        device_id_type=MESH,
    )


def forward_kernel(
    span,
    x_ref,
    gain_ref,
    w_branch_ref,
    w_input_ref,
    taps_ref,
    vec_ref,
    gates_ref,
    gate_bias_ref,
    state0_ref,
    conv0_ref,
    normed_ref,
    branch_ref,
    pad_ref,
    pre_ref,
    hidden_ref,
    mixed_ref,
    carry_ref,
    sums_ref,
    a_ref,
    b_ref,
    conv_ref,
    tail_ref,
    tail_in,
    mine_ref,
    send1,
    recv1,
    send_t,
    recv_t,
):
    seqs = state0_ref.shape[0]
    width = taps_ref.shape[1]
    taps = taps_ref.shape[0]
    rows = seqs * span
    devices, me = lax.axis_size("seq"), lax.axis_index("seq")
    enter("seq")

    group = 2 * span

    @pl.loop(0, rows // group)
    def _(g):
        @pl.loop(0, group // ROWS)
        def _(q):
            at = block(g * (group // ROWS) + q, ROWS)
            x = x_ref[at, :]
            scale = lax.rsqrt(jnp.mean(x * x, axis=-1, keepdims=True) + EPS)
            normed_ref[at, :] = (x * scale * gain_ref[...]).astype(BF16)

        conv = dot(normed_ref[block(g, group), :], w_input_ref[...])
        for j in range(group // span):
            pad_ref[g * (group // span) + j, pl.ds(TILE, span), :] = conv[
                j * span : (j + 1) * span
            ]

    for s in range(seqs):
        tail_ref[s] = pad_ref[s, pl.ds(span, TILE), :]
    tail_copy = to_one("seq", 1, tail_ref, tail_in, send_t.at[0], recv_t.at[0])
    tail_copy.start()

    @pl.loop(0, rows // group)
    def _(g):
        branch_ref[block(g, group), :] = dot(normed_ref[block(g, group), :], w_branch_ref[...])

    tail_copy.wait()
    for s in range(seqs):
        pad_ref[s, pl.ds(0, TILE), :] = jnp.where(me == 0, conv0_ref[s], tail_in[s])

    def conv_rows(s, q):
        part = pad_ref[s, pl.ds(pl.multiple_of(q * ROWS, ROWS), ROWS + TILE), :]
        total = vec_ref[0:1, :]
        for k in range(taps):
            first = TILE - (taps - 1) + k
            total = total + taps_ref[k : k + 1, :] * part[first : first + ROWS]
        return total

    @pl.loop(0, seqs)
    def _(s):
        @pl.loop(0, span // ROWS)
        def _(q):
            conv_ref[block(q, ROWS), :] = conv_rows(s, q)

        pre_ref[block(s, span), :] = (
            dot(conv_ref[...].astype(BF16), gates_ref[...]) + gate_bias_ref[...]
        )

        @pl.loop(0, span // ROWS)
        def _(q):
            at = block(s * (span // ROWS) + q, ROWS)
            conv = conv_ref[block(q, ROWS), :]
            recall = jax.nn.sigmoid(pre_ref[at, :width])
            gate = jax.nn.sigmoid(pre_ref[at, width:])
            log_a = (-RATE_SCALE * vec_ref[1:2, :]) * recall
            a = jnp.exp(log_a)
            put(a_ref, at, a)
            put(b_ref, at, jnp.sqrt(one_minus_square(log_a, a)) * gate * conv)

    def at_time(ref, t):
        return get(ref, pl.ds(t, seqs, stride=span))

    def local(t, value):
        prod, state = value
        a = at_time(a_ref, t)
        return prod * a, a * state + at_time(b_ref, t)

    ones = jnp.ones((seqs, width), F32)
    prod, state = lax.fori_loop(0, span, local, (ones, jnp.zeros_like(ones)), unroll=8)
    mine_ref[0] = prod
    mine_ref[1] = state
    sums_ref[me] = mine_ref[...]
    copies = to_all("seq", mine_ref, sums_ref, send1, recv1)
    for copy in copies:
        copy.start()
    for copy in copies:
        copy.wait()

    def carry_step(j, carry):
        both = sums_ref[j]
        return jnp.where(j < me, both[0] * carry + both[1], carry)

    carry = lax.fori_loop(0, devices - 1, carry_step, state0_ref[...])
    carry_ref[...] = carry

    def final(t, state):
        state = at_time(a_ref, t) * state + at_time(b_ref, t)
        put(hidden_ref, pl.ds(t, seqs, stride=span), state)
        return state

    lax.fori_loop(0, span, final, carry, unroll=8)

    @pl.loop(0, rows // ROWS)
    def _(q):
        at = block(q, ROWS)
        mixed_ref[at, :] = (get(hidden_ref, at) * gelu(branch_ref[at, :])).astype(BF16)


def backward_kernel(
    span,
    grad_ref,
    branch_ref,
    hidden_ref,
    carry_ref,
    pre_ref,
    pad_ref,
    sums_ref,
    taps_ref,
    vec_ref,
    gates_t_ref,
    grad_branch_ref,
    input_ref,
    heads_ref,
    low_ref,
    acc_ref,
    a_ref,
    gd_ref,
    gs_ref,
    direct_ref,
    gpad_ref,
    mine_ref,
    entries_ref,
    head_ref,
    head_in,
    send1,
    recv1,
    send_t,
    recv_t,
):
    seqs, width = carry_ref.shape
    taps = taps_ref.shape[0]
    rows = seqs * span
    devices, me = lax.axis_size("seq"), lax.axis_index("seq")
    enter("seq")

    def decay(at):
        recall = jax.nn.sigmoid(pre_ref[at, :width])
        log_a = (-RATE_SCALE * vec_ref[1:2, :]) * recall
        return recall, log_a, jnp.exp(log_a)

    @pl.loop(0, rows // ROWS)
    def _(q):
        at = block(q, ROWS)
        put(a_ref, at, decay(at)[2])
        act, slope = gelu_both(branch_ref[at, :])
        grad = grad_ref[at, :]
        put(gd_ref, at, grad * act)
        grad_branch_ref[at, :] = (grad * get(hidden_ref, at) * slope).astype(BF16)

    def at_time(ref, t):
        return get(ref, pl.ds(t, seqs, stride=span))

    def local(k, through):
        t = span - 1 - k
        return at_time(a_ref, t) * (at_time(gd_ref, t) + through)

    zero = jnp.zeros((seqs, width), F32)
    mine_ref[...] = lax.fori_loop(0, span, local, zero, unroll=8)
    entries_ref[me] = mine_ref[...]
    copies = to_all("seq", mine_ref, entries_ref, send1, recv1)
    for copy in copies:
        copy.start()
    acc_ref[...] = jnp.zeros_like(acc_ref)
    for copy in copies:
        copy.wait()

    def back_step(k, through):
        j = devices - 1 - k
        return jnp.where(j > me, entries_ref[j] + sums_ref[j, 0] * through, through)

    incoming = lax.fori_loop(0, devices - 1, back_step, zero)

    def final(k, through):
        t = span - 1 - k
        grad = at_time(gd_ref, t) + through
        put(gs_ref, pl.ds(t, seqs, stride=span), grad)
        return at_time(a_ref, t) * grad

    lax.fori_loop(0, span, final, incoming, unroll=8)

    def add(k, value):
        total = value[0:TILE]
        for i in range(1, value.shape[0] // TILE):
            total = total + value[i * TILE : (i + 1) * TILE]
        acc_ref[k] += total

    @pl.loop(0, seqs)
    def _(s):
        @pl.loop(0, span // ROWS)
        def _(q):
            at = block(s * (span // ROWS) + q, ROWS)
            part = pad_ref[s, pl.ds(pl.multiple_of(q * ROWS, ROWS), ROWS + TILE), :]
            conv = vec_ref[0:1, :]
            for k in range(taps):
                first = TILE - (taps - 1) + k
                conv = conv + taps_ref[k : k + 1, :] * part[first : first + ROWS]
            heads_ref[at, :] = conv.astype(BF16)
            recall, log_a, a = decay(at)
            gate = jax.nn.sigmoid(pre_ref[at, width:])
            square = one_minus_square(log_a, a)
            inverse = lax.rsqrt(square)
            root = jnp.sqrt(square)
            grad = get(gs_ref, at)
            hidden = get(hidden_ref, at)
            before_at = pl.multiple_of(jnp.maximum(s * span + q * ROWS - TILE, 0), TILE)
            earlier = get(hidden_ref, pl.ds(before_at, TILE))
            first_row = jnp.where(q == 0, carry_ref[pl.ds(s, 1), :], earlier[TILE - 1 :])
            place = lax.broadcasted_iota(jnp.int32, (ROWS, width), 0)
            prev = jnp.where(place == 0, first_row, pltpu.roll(hidden, 1, 0))
            grad_log = grad * a * (prev - gate * conv * a * inverse)
            through = grad_log * recall
            pre_r = through * (1.0 - recall) * (-RATE_SCALE * vec_ref[1:2, :])
            direct = grad * root * gate
            pre_i = direct * conv * (1.0 - gate)
            low_ref[at, :width] = pre_r.astype(BF16)
            low_ref[at, width:] = pre_i.astype(BF16)
            direct_ref[block(q, ROWS), :] = direct
            add(0, through)
            add(1, pre_r)
            add(2, pre_i)

        whole = direct_ref[...] + dot(low_ref[block(s, span), :], gates_t_ref[...])
        gpad_ref[s, pl.ds(0, span), :] = whole
        head_ref[s] = whole[:TILE]

    head_copy = to_one("seq", -1, head_ref, head_in, send_t.at[0], recv_t.at[0])
    head_copy.start()

    @pl.loop(0, seqs)
    def _(s):
        @pl.loop(0, span // ROWS)
        def _(q):
            at = pl.multiple_of(q * ROWS, ROWS)
            part = pad_ref[s, pl.ds(at, ROWS + TILE), :]
            grad = gpad_ref[s, pl.ds(at, ROWS), :]
            add(3, grad)
            for k in range(taps):
                first = TILE - (taps - 1) + k
                add(4 + k, grad * part[first : first + ROWS])

    head_copy.wait()
    for s in range(seqs):
        gpad_ref[s, pl.ds(span, TILE), :] = jnp.where(me == devices - 1, 0.0, head_in[s])

    @pl.loop(0, seqs)
    def _(s):
        @pl.loop(0, span // ROWS)
        def _(q):
            part = gpad_ref[s, pl.ds(pl.multiple_of(q * ROWS, ROWS), ROWS + TILE), :]
            total = taps_ref[taps - 1 : taps, :] * part[0:ROWS]
            for k in range(taps - 1):
                first = taps - 1 - k
                total = total + taps_ref[k : k + 1, :] * part[first : first + ROWS]
            input_ref[block(s * (span // ROWS) + q, ROWS), :] = total.astype(BF16)


def params(collective, megabytes=60):
    return pltpu.CompilerParams(
        collective_id=collective, has_side_effects=True, vmem_limit_bytes=megabytes << 20
    )


def shape(dims, dtype=F32):
    return jax.ShapeDtypeStruct(dims, dtype)


def recurrence_forward(span, *args):
    x, _, w_branch = args[:3]
    state0 = args[8]
    rows, model = x.shape
    seqs, width = state0.shape
    devices = lax.axis_size("seq")
    dma = pltpu.SemaphoreType.DMA
    return pl.pallas_call(
        functools.partial(forward_kernel, span),
        out_shape=(
            shape((rows, model), BF16),
            shape((rows, width)),
            shape((seqs, span + TILE, width)),
            shape((rows, 2 * width)),
            shape((width // LANES, rows, LANES)),
            shape((rows, width), BF16),
            shape((seqs, width)),
            shape((devices, 2, seqs, width)),
        ),
        in_specs=[VMEM] * len(args),
        out_specs=(VMEM,) * 8,
        scratch_shapes=[
            pltpu.VMEM((width // LANES, rows, LANES), F32),
            pltpu.VMEM((width // LANES, rows, LANES), F32),
            pltpu.VMEM((span, width), F32),
            pltpu.VMEM((seqs, TILE, width), F32),
            pltpu.VMEM((seqs, TILE, width), F32),
            pltpu.VMEM((2, seqs, width), F32),
            dma((devices - 1,)),
            dma((devices - 1,)),
            dma((1,)),
            dma((1,)),
        ],
        compiler_params=params(0),
        name="recurrence_forward",
    )(*args)


def recurrence_backward(span, *args):
    rows, width = args[0].shape
    seqs = args[3].shape[0]
    taps = args[7].shape[0]
    devices = lax.axis_size("seq")
    dma = pltpu.SemaphoreType.DMA
    return pl.pallas_call(
        functools.partial(backward_kernel, span),
        out_shape=(
            shape((rows, width), BF16),
            shape((rows, width), BF16),
            shape((rows, width), BF16),
            shape((rows, 2 * width), BF16),
            shape((4 + taps, TILE, width)),
        ),
        in_specs=[VMEM] * len(args),
        out_specs=(VMEM,) * 5,
        scratch_shapes=[
            pltpu.VMEM((width // LANES, rows, LANES), F32),
            pltpu.VMEM((width // LANES, rows, LANES), F32),
            pltpu.VMEM((width // LANES, rows, LANES), F32),
            pltpu.VMEM((span, width), F32),
            pltpu.VMEM((seqs, span + TILE, width), F32),
            pltpu.VMEM((seqs, width), F32),
            pltpu.VMEM((devices, seqs, width), F32),
            pltpu.VMEM((seqs, TILE, width), F32),
            pltpu.VMEM((seqs, TILE, width), F32),
            dma((devices - 1,)),
            dma((devices - 1,)),
            dma((1,)),
            dma((1,)),
        ],
        compiler_params=params(1),
        name="recurrence_backward",
    )(*args)


def rms_scale(values, gain):
    return values * lax.rsqrt(jnp.mean(values * values, axis=-1, keepdims=True) + EPS) * gain


def norm_back(values, gain, grad):
    q = lax.rsqrt(jnp.mean(values * values, axis=-1, keepdims=True) + EPS)
    e = gain * grad
    back = q * e - values * (q * q * q) * jnp.mean(e * values, axis=-1, keepdims=True)
    return back, jnp.sum(grad * values * q, axis=0)


def widen(array, width):
    short = width - array.shape[-1]
    if short == 0:
        return array
    return jnp.pad(array, [(0, 0)] * (array.ndim - 1) + [(0, short)])


def diagonal(gates, width):
    heads, size, _ = gates.shape
    spread = jnp.eye(heads, dtype=gates.dtype)[:, None, :, None] * gates[:, :, None, :]
    flat = spread.reshape(heads * size, heads * size)
    short = width - heads * size
    return jnp.pad(flat, ((0, short), (0, short))) if short else flat


def per_device(
    stream,
    norm_in,
    w_branch,
    w_input,
    conv_kernel,
    conv_bias,
    gate_r,
    bias_r,
    gate_i,
    bias_i,
    decay_param,
    w_out,
    norm_mlp,
    w_gate,
    w_up,
    w_down,
    state_init,
    conv_init,
    fresh_rows,
    out_grad,
):
    seqs, span, model = stream.shape
    channels = w_branch.shape[1]
    mlp_dev = w_gate.shape[1]
    heads, head_width = gate_r.shape[:2]
    taps = conv_kernel.shape[0]
    edge = taps - 1
    rows = seqs * span
    devices = lax.axis_size("seq")
    position = lax.axis_index("seq")
    width = -(-channels // 128) * 128

    keep = 1.0 - fresh_rows.astype(F32)
    flat_in = stream.reshape(rows, model)
    flat_grad = out_grad.reshape(rows, model)
    w_branch_p = widen(w_branch, width)
    w_input_p = widen(w_input, width)
    w_out_p = jnp.pad(w_out, ((0, width - channels), (0, 0))) if width > channels else w_out
    taps_p = widen(conv_kernel, width)
    rate = jax.nn.softplus(-decay_param)
    rate_p = jnp.pad(rate, (0, width - channels), constant_values=1.0)
    vec = jnp.stack([widen(conv_bias, width), rate_p])
    gates = jnp.concatenate([diagonal(gate_r, width), diagonal(gate_i, width)], axis=1)
    gates_t = jnp.concatenate(
        [
            diagonal(jnp.swapaxes(gate_r, 1, 2), width),
            diagonal(jnp.swapaxes(gate_i, 1, 2), width),
        ],
        axis=0,
    )
    gate_bias = jnp.concatenate([widen(bias_r, width), widen(bias_i, width)])[None]
    state0 = widen(state_init * keep[:, None], width)
    conv0 = jnp.pad(
        conv_init * keep[:, None, None], ((0, 0), (TILE - edge, 0), (0, width - channels))
    )

    normed, branch, padded, pre, hidden, mixed, carry, sums = recurrence_forward(
        span,
        flat_in,
        norm_in[None],
        w_branch_p,
        w_input_p,
        taps_p,
        vec,
        gates,
        gate_bias,
        state0,
        conv0,
    )
    residual = flat_in + lax.psum(dot(mixed, w_out_p), "mp")
    normed_mlp = rms_scale(residual, norm_mlp).astype(BF16)
    gate_val = dot(normed_mlp, w_gate)
    up_val = dot(normed_mlp, w_up)
    act, slope = gelu_both(gate_val)
    hidden_mlp = (act * up_val).astype(BF16)
    block_out = residual + lax.psum(dot(hidden_mlp, w_down), "mp")
    grad_low = flat_grad.astype(BF16)
    grad_hidden = matmul_back(grad_low, w_down)
    grad_gate = (grad_hidden * up_val * slope).astype(BF16)
    grad_up = (grad_hidden * act).astype(BF16)
    grad_normed_mlp = lax.psum(matmul_back(grad_gate, w_gate) + matmul_back(grad_up, w_up), "mp")
    back, norm_mlp_grad = norm_back(residual, norm_mlp, grad_normed_mlp)
    grad_resid = flat_grad + back
    resid_low = grad_resid.astype(BF16)
    grad_mixed = matmul_back(resid_low, w_out_p)
    grad_branch, input_low, heads_in, pre_low, acc = recurrence_backward(
        span,
        grad_mixed,
        branch,
        hidden,
        carry,
        pre,
        padded,
        sums,
        taps_p,
        vec,
        gates_t,
    )
    grad_normed = lax.psum(
        matmul_back(grad_branch, w_branch_p) + matmul_back(input_low, w_input_p), "mp"
    )
    back, norm_in_grad = norm_back(flat_in, norm_in, grad_normed)
    stream_grad = grad_resid + back

    def weight(left, right):
        return lax.dot_general(left, right, CONTRACT_ROWS, preferred_element_type=F32)

    def scatter(array, dim):
        return lax.psum_scatter(array, "seq", scatter_dimension=dim, tiled=True)

    w_down_grad = scatter(weight(grad_low, hidden_mlp), 0)
    w_gate_grad = scatter(weight(normed_mlp, grad_gate), 0)
    w_up_grad = scatter(weight(normed_mlp, grad_up), 0)
    w_out_grad = scatter(weight(resid_low, mixed), 0)
    w_branch_grad = scatter(weight(normed, grad_branch), 0)
    w_input_grad = scatter(weight(normed, input_low), 0)

    gates_grad = weight(heads_in, pre_low)

    def blocks(array):
        return jnp.stack(
            [
                array[h * head_width : (h + 1) * head_width, h * head_width : (h + 1) * head_width]
                for h in range(heads)
            ]
        )

    acc = jnp.sum(acc, axis=1)[:, :channels]
    last = position == devices - 1
    last_hidden = hidden.reshape(-1, seqs, span, LANES)[:, :, -1]
    last_hidden = jnp.swapaxes(last_hidden, 0, 1).reshape(seqs, width)[:, :channels]
    final_state = jnp.where(last, last_hidden, 0.0)
    final_conv = jnp.where(last, padded[:, span + TILE - edge :, :channels], 0.0)
    small = lax.psum(
        (
            norm_in_grad,
            norm_mlp_grad,
            acc,
            blocks(gates_grad[:, :width]),
            blocks(gates_grad[:, width:]),
            final_state,
            final_conv,
        ),
        "seq",
    )
    norm_in_grad, norm_mlp_grad, acc, gate_r_grad, gate_i_grad, final_state, final_conv = small
    decay_grad = acc[0] * (RATE_SCALE * jax.nn.sigmoid(-decay_param))
    return (
        block_out.reshape(stream.shape),
        stream_grad.reshape(stream.shape),
        norm_in_grad,
        w_branch_grad[:, :channels],
        w_input_grad[:, :channels],
        acc[4:],
        acc[3],
        gate_r_grad,
        acc[1],
        gate_i_grad,
        acc[2],
        decay_grad,
        w_out_grad[:, :channels].T,
        norm_mlp_grad,
        w_gate_grad,
        w_up_grad,
        w_down_grad.T,
        final_state,
        final_conv,
    )


def solution(mesh):
    seq_rows = P(None, "seq", None)
    columns = P(None, "mp")
    channel = P("mp")
    return jax.shard_map(
        per_device,
        mesh=mesh,
        in_specs=(
            seq_rows,
            P(),
            columns,
            columns,
            columns,
            channel,
            P("mp", None, None),
            channel,
            P("mp", None, None),
            channel,
            channel,
            P("mp", None),
            P(),
            columns,
            columns,
            P("mp", None),
            columns,
            P(None, None, "mp"),
            P(),
            seq_rows,
        ),
        out_specs=(
            seq_rows,
            seq_rows,
            P(),
            P("seq", "mp"),
            P("seq", "mp"),
            columns,
            channel,
            P("mp", None, None),
            channel,
            P("mp", None, None),
            channel,
            channel,
            P("mp", "seq"),
            P(),
            P("seq", "mp"),
            P("seq", "mp"),
            P("mp", "seq"),
            columns,
            P(None, None, "mp"),
        ),
        check_vma=False,
    )
```

```python
import functools

import jax
import jax.numpy as jnp
from jax import lax
from jax.experimental import pallas as pl
from jax.experimental.pallas import tpu as pltpu
from jax.sharding import PartitionSpec as P

MESH = pl.DeviceIdType.MESH
RATE_SCALE = 8.0
EPS = 1e-06
GELU_C = 0.7978845608028654
GELU_K = 0.044715
CONTRACT_ROWS = (((0,), (0,)), ((), ()))
CONTRACT_LAST = (((1,), (1,)), ((), ()))
TILE = 8
LANES = 128
ROWS = 32
CHUNK = 32
SKEW = 2
F32 = jnp.float32
BF16 = jnp.bfloat16
VMEM = pl.BlockSpec(memory_space=pltpu.VMEM)


def dot(a, b):
    return jnp.dot(a, b, preferred_element_type=F32)


def matmul_back(a, b):
    return lax.dot_general(a, b, CONTRACT_LAST, preferred_element_type=F32)


def block(i, size):
    return pl.ds(pl.multiple_of(i * size, size), size)


def gelu(x):
    t = jnp.tanh(GELU_C * (x + GELU_K * (x * x * x)))
    return 0.5 * x * (1.0 + t)


def gelu_both(x):
    x2 = x * x
    t = jnp.tanh(GELU_C * (x + GELU_K * (x2 * x)))
    half = 0.5 * (1.0 + t)
    slope = half + 0.5 * x * (1.0 - t * t) * (GELU_C * (1.0 + (3.0 * GELU_K) * x2))
    return x * half, slope


def one_minus_square(log_a, a):
    y = 2.0 * log_a
    s = 1.0 + y * (1.0 / 8.0)
    for k in (7, 6, 5, 4, 3, 2):
        s = 1.0 + (y * (1.0 / k)) * s
    return jnp.where(y > -0.35, -y * s, 1.0 - a * a)


def get(ref, at):
    return jnp.concatenate([ref[j, at, :] for j in range(ref.shape[0])], axis=-1)


def put(ref, at, value):
    for j in range(ref.shape[0]):
        ref[j, at, :] = value[:, j * LANES : (j + 1) * LANES]


def enter(axis):
    size, me = lax.axis_size(axis), lax.axis_index(axis)
    barrier = pltpu.get_barrier_semaphore()
    for d in range(1, size):
        pl.semaphore_signal(
            barrier, 1, device_id={axis: lax.rem(me + d, size)}, device_id_type=MESH
        )
    pl.semaphore_wait(barrier, size - 1)


def to_all(axis, src, slots, send, recv):
    size, me = lax.axis_size(axis), lax.axis_index(axis)
    return [
        pltpu.make_async_remote_copy(
            src_ref=src,
            dst_ref=slots.at[me],
            send_sem=send.at[d - 1],
            recv_sem=recv.at[d - 1],
            device_id={axis: lax.rem(me + d, size)},
            device_id_type=MESH,
        )
        for d in range(1, size)
    ]


def to_one(axis, distance, src, dst, send, recv):
    size, me = lax.axis_size(axis), lax.axis_index(axis)
    return pltpu.make_async_remote_copy(
        src_ref=src,
        dst_ref=dst,
        send_sem=send,
        recv_sem=recv,
        device_id={axis: lax.rem(me + distance + size, size)},
        device_id_type=MESH,
    )


def forward_kernel(
    span,
    x_ref,
    gain_ref,
    w_branch_ref,
    w_input_ref,
    taps_ref,
    vec_ref,
    gates_ref,
    gate_bias_ref,
    state0_ref,
    conv0_ref,
    normed_ref,
    branch_ref,
    pad_ref,
    pre_ref,
    hidden_ref,
    mixed_ref,
    carry_ref,
    sums_ref,
    a_ref,
    b_ref,
    conv_ref,
    tail_ref,
    tail_in,
    mine_ref,
    send1,
    recv1,
    send_t,
    recv_t,
):
    seqs = state0_ref.shape[0]
    width = taps_ref.shape[1]
    taps = taps_ref.shape[0]
    rows = seqs * span
    devices, me = lax.axis_size("seq"), lax.axis_index("seq")
    enter("seq")

    group = 2 * span

    @pl.loop(0, rows // group)
    def _(g):
        @pl.loop(0, group // ROWS)
        def _(q):
            at = block(g * (group // ROWS) + q, ROWS)
            x = x_ref[at, :]
            scale = lax.rsqrt(jnp.mean(x * x, axis=-1, keepdims=True) + EPS)
            normed_ref[at, :] = (x * scale * gain_ref[...]).astype(BF16)

        conv = dot(normed_ref[block(g, group), :], w_input_ref[...])
        for j in range(group // span):
            pad_ref[g * (group // span) + j, pl.ds(TILE, span), :] = conv[
                j * span : (j + 1) * span
            ]

    for s in range(seqs):
        tail_ref[s] = pad_ref[s, pl.ds(span, TILE), :]
    tail_copy = to_one("seq", 1, tail_ref, tail_in, send_t.at[0], recv_t.at[0])
    tail_copy.start()

    @pl.loop(0, rows // group)
    def _(g):
        branch_ref[block(g, group), :] = dot(normed_ref[block(g, group), :], w_branch_ref[...])

    tail_copy.wait()
    for s in range(seqs):
        pad_ref[s, pl.ds(0, TILE), :] = jnp.where(me == 0, conv0_ref[s], tail_in[s])

    def conv_rows(s, q):
        part = pad_ref[s, pl.ds(pl.multiple_of(q * ROWS, ROWS), ROWS + TILE), :]
        total = vec_ref[0:1, :]
        for k in range(taps):
            first = TILE - (taps - 1) + k
            total = total + taps_ref[k : k + 1, :] * part[first : first + ROWS]
        return total

    @pl.loop(0, seqs)
    def _(s):
        @pl.loop(0, span // ROWS)
        def _(q):
            conv_ref[block(q, ROWS), :] = conv_rows(s, q)

        pre_ref[block(s, span), :] = (
            dot(conv_ref[...].astype(BF16), gates_ref[...]) + gate_bias_ref[...]
        )

        @pl.loop(0, span // ROWS)
        def _(q):
            at = block(s * (span // ROWS) + q, ROWS)
            conv = conv_ref[block(q, ROWS), :]
            recall = jax.nn.sigmoid(pre_ref[at, :width])
            gate = jax.nn.sigmoid(pre_ref[at, width:])
            log_a = (-RATE_SCALE * vec_ref[1:2, :]) * recall
            a = jnp.exp(log_a)
            put(a_ref, at, a)
            put(b_ref, at, jnp.sqrt(one_minus_square(log_a, a)) * gate * conv)

    def at_time(ref, t):
        return get(ref, pl.ds(t, seqs, stride=span))

    def local(t, value):
        prod, state = value
        a = at_time(a_ref, t)
        return prod * a, a * state + at_time(b_ref, t)

    ones = jnp.ones((seqs, width), F32)
    prod, state = lax.fori_loop(0, span, local, (ones, jnp.zeros_like(ones)), unroll=8)
    mine_ref[0] = prod
    mine_ref[1] = state
    sums_ref[me] = mine_ref[...]
    copies = to_all("seq", mine_ref, sums_ref, send1, recv1)
    for copy in copies:
        copy.start()
    for copy in copies:
        copy.wait()

    def carry_step(j, carry):
        both = sums_ref[j]
        return jnp.where(j < me, both[0] * carry + both[1], carry)

    carry = lax.fori_loop(0, devices - 1, carry_step, state0_ref[...])
    carry_ref[...] = carry

    def final(t, state):
        state = at_time(a_ref, t) * state + at_time(b_ref, t)
        put(hidden_ref, pl.ds(t, seqs, stride=span), state)
        return state

    lax.fori_loop(0, span, final, carry, unroll=8)

    @pl.loop(0, rows // ROWS)
    def _(q):
        at = block(q, ROWS)
        mixed_ref[at, :] = (get(hidden_ref, at) * gelu(branch_ref[at, :])).astype(BF16)


def backward_kernel(
    span,
    grad_ref,
    branch_ref,
    hidden_ref,
    carry_ref,
    pre_ref,
    pad_ref,
    sums_ref,
    taps_ref,
    vec_ref,
    gates_t_ref,
    grad_branch_ref,
    input_ref,
    heads_ref,
    low_ref,
    acc_ref,
    a_ref,
    gd_ref,
    gs_ref,
    direct_ref,
    gpad_ref,
    mine_ref,
    entries_ref,
    head_ref,
    head_in,
    send1,
    recv1,
    send_t,
    recv_t,
):
    seqs, width = carry_ref.shape
    taps = taps_ref.shape[0]
    rows = seqs * span
    devices, me = lax.axis_size("seq"), lax.axis_index("seq")
    enter("seq")

    def decay(at):
        recall = jax.nn.sigmoid(pre_ref[at, :width])
        log_a = (-RATE_SCALE * vec_ref[1:2, :]) * recall
        return recall, log_a, jnp.exp(log_a)

    @pl.loop(0, rows // ROWS)
    def _(q):
        at = block(q, ROWS)
        put(a_ref, at, decay(at)[2])
        act, slope = gelu_both(branch_ref[at, :])
        grad = grad_ref[at, :]
        put(gd_ref, at, grad * act)
        grad_branch_ref[at, :] = (grad * get(hidden_ref, at) * slope).astype(BF16)

    def at_time(ref, t):
        return get(ref, pl.ds(t, seqs, stride=span))

    def local(k, through):
        t = span - 1 - k
        return at_time(a_ref, t) * (at_time(gd_ref, t) + through)

    zero = jnp.zeros((seqs, width), F32)
    mine_ref[...] = lax.fori_loop(0, span, local, zero, unroll=8)
    entries_ref[me] = mine_ref[...]
    copies = to_all("seq", mine_ref, entries_ref, send1, recv1)
    for copy in copies:
        copy.start()
    acc_ref[...] = jnp.zeros_like(acc_ref)
    for copy in copies:
        copy.wait()

    def back_step(k, through):
        j = devices - 1 - k
        return jnp.where(j > me, entries_ref[j] + sums_ref[j, 0] * through, through)

    incoming = lax.fori_loop(0, devices - 1, back_step, zero)

    def final(k, through):
        t = span - 1 - k
        grad = at_time(gd_ref, t) + through
        put(gs_ref, pl.ds(t, seqs, stride=span), grad)
        return at_time(a_ref, t) * grad

    lax.fori_loop(0, span, final, incoming, unroll=8)

    def add(k, value):
        total = value[0:TILE]
        for i in range(1, value.shape[0] // TILE):
            total = total + value[i * TILE : (i + 1) * TILE]
        acc_ref[k] += total

    @pl.loop(0, seqs)
    def _(s):
        @pl.loop(0, span // ROWS)
        def _(q):
            at = block(s * (span // ROWS) + q, ROWS)
            part = pad_ref[s, pl.ds(pl.multiple_of(q * ROWS, ROWS), ROWS + TILE), :]
            conv = vec_ref[0:1, :]
            for k in range(taps):
                first = TILE - (taps - 1) + k
                conv = conv + taps_ref[k : k + 1, :] * part[first : first + ROWS]
            heads_ref[at, :] = conv.astype(BF16)
            recall, log_a, a = decay(at)
            gate = jax.nn.sigmoid(pre_ref[at, width:])
            square = one_minus_square(log_a, a)
            inverse = lax.rsqrt(square)
            root = jnp.sqrt(square)
            grad = get(gs_ref, at)
            hidden = get(hidden_ref, at)
            before_at = pl.multiple_of(jnp.maximum(s * span + q * ROWS - TILE, 0), TILE)
            earlier = get(hidden_ref, pl.ds(before_at, TILE))
            first_row = jnp.where(q == 0, carry_ref[pl.ds(s, 1), :], earlier[TILE - 1 :])
            place = lax.broadcasted_iota(jnp.int32, (ROWS, width), 0)
            prev = jnp.where(place == 0, first_row, pltpu.roll(hidden, 1, 0))
            grad_log = grad * a * (prev - gate * conv * a * inverse)
            through = grad_log * recall
            pre_r = through * (1.0 - recall) * (-RATE_SCALE * vec_ref[1:2, :])
            direct = grad * root * gate
            pre_i = direct * conv * (1.0 - gate)
            low_ref[at, :width] = pre_r.astype(BF16)
            low_ref[at, width:] = pre_i.astype(BF16)
            direct_ref[block(q, ROWS), :] = direct
            add(0, through)
            add(1, pre_r)
            add(2, pre_i)

        whole = direct_ref[...] + dot(low_ref[block(s, span), :], gates_t_ref[...])
        gpad_ref[s, pl.ds(0, span), :] = whole
        head_ref[s] = whole[:TILE]

    head_copy = to_one("seq", -1, head_ref, head_in, send_t.at[0], recv_t.at[0])
    head_copy.start()

    @pl.loop(0, seqs)
    def _(s):
        @pl.loop(0, span // ROWS)
        def _(q):
            at = pl.multiple_of(q * ROWS, ROWS)
            part = pad_ref[s, pl.ds(at, ROWS + TILE), :]
            grad = gpad_ref[s, pl.ds(at, ROWS), :]
            add(3, grad)
            for k in range(taps):
                first = TILE - (taps - 1) + k
                add(4 + k, grad * part[first : first + ROWS])

    head_copy.wait()
    for s in range(seqs):
        gpad_ref[s, pl.ds(span, TILE), :] = jnp.where(me == devices - 1, 0.0, head_in[s])

    @pl.loop(0, seqs)
    def _(s):
        @pl.loop(0, span // ROWS)
        def _(q):
            part = gpad_ref[s, pl.ds(pl.multiple_of(q * ROWS, ROWS), ROWS + TILE), :]
            total = taps_ref[taps - 1 : taps, :] * part[0:ROWS]
            for k in range(taps - 1):
                first = taps - 1 - k
                total = total + taps_ref[k : k + 1, :] * part[first : first + ROWS]
            input_ref[block(s * (span // ROWS) + q, ROWS), :] = total.astype(BF16)


def line_sum(axis, chunk, part, inbox, out, sems, fill, root, arrive):
    send_up, send_down, recv_up, recv_down = sems
    n, z = lax.axis_size(axis), lax.axis_index(axis)
    count = part.shape[0] // chunk
    depth = n // 2

    barrier = pltpu.get_barrier_semaphore()
    for step in (-1, 1):
        inside = z > 0 if step < 0 else z < n - 1

        @pl.when(inside)
        def _():
            pl.semaphore_signal(barrier, 1, device_id={axis: z + step}, device_id_type=MESH)

    pl.semaphore_wait(barrier, jnp.where(jnp.logical_or(z == 0, z == n - 1), 1, 2))

    def root_of(c):
        return depth - 1 + lax.rem(c, 2)

    def up(c, step, side):
        at = block(c, chunk)
        return pltpu.make_async_remote_copy(
            src_ref=part.at[at],
            dst_ref=inbox.at[side, at],
            send_sem=send_up.at[c],
            recv_sem=recv_up.at[side, c],
            device_id={axis: z + step},
            device_id_type=MESH,
        )

    def down(c, step, side):
        at = block(c, chunk)
        return pltpu.make_async_remote_copy(
            src_ref=out.at[at],
            dst_ref=out.at[at],
            send_sem=send_down.at[side, c],
            recv_sem=recv_down.at[c],
            device_id={axis: z + step},
            device_id_type=MESH,
        )

    @pl.loop(0, count + SKEW * n)
    def _(k):
        @pl.when(k < count)
        def _():
            fill(k)

        for i in reversed(range(n + 1)):
            c = k - SKEW * i
            valid = jnp.logical_and(c >= 0, c < count)
            c = jnp.clip(c, 0, count - 1)
            at = block(c, chunk)
            r = root_of(c)
            step = jnp.where(z < r, 1, -1)
            side = jnp.where(z < r, 0, 1)
            if i > depth:
                here = jnp.logical_and(z != r, jnp.abs(z - r) == i - depth)

                @pl.when(jnp.logical_and(valid, here))
                def _():
                    down(c, -step, side).wait_recv()

                    @pl.when(jnp.logical_and(z > 0, z < n - 1))
                    def _():
                        down(c, -step, side).start()

                    arrive(at)
            elif i == depth:

                @pl.when(jnp.logical_and(valid, z == r))
                def _():
                    up(c, 1, 0).wait_recv()
                    up(c, -1, 1).wait_recv()
                    root(c, at, part[at, :] + inbox[0, at, :] + inbox[1, at, :])
                    down(c, -1, 0).start()
                    down(c, 1, 1).start()
                    arrive(at)
            else:
                here = jnp.where(z < r, z, n - 1 - z) == i

                @pl.when(jnp.logical_and(valid, jnp.logical_and(z != r, here)))
                def _():
                    if i > 0:
                        up(c, step, side).wait_recv()
                        part[at, :] += inbox[side, at, :]
                    up(c, step, side).start()

    @pl.loop(0, count)
    def _(c):
        r = root_of(c)
        step = jnp.where(z < r, 1, -1)
        side = jnp.where(z < r, 0, 1)

        @pl.when(z == r)
        def _():
            down(c, -1, 0).wait_send()
            down(c, 1, 1).wait_send()

        @pl.when(z != r)
        def _():
            up(c, step, side).wait_send()

        @pl.when(jnp.logical_and(z != r, jnp.logical_and(z > 0, z < n - 1)))
        def _():
            down(c, -step, side).wait_send()


def mean_square(x):
    return lax.rsqrt(jnp.mean(x * x, axis=-1, keepdims=True) + EPS)


def nothing(*_):
    pass


def residual_kernel(part_in, x_ref, gain_ref, normed_ref, own_ref, part, inbox, out, *sems):
    chunk = CHUNK
    part[...] = part_in[...]

    def root(c, at, total):
        value = x_ref[at, :] + total
        own_ref[block(c // 2, chunk), :] = value
        out[at, :] = (value * mean_square(value) * gain_ref[...]).astype(BF16).astype(F32)

    def arrive(at):
        normed_ref[at, :] = out[at, :].astype(BF16)

    line_sum("mp", chunk, part, inbox, out, sems, nothing, root, arrive)


def fold(value):
    total = value[0:TILE]
    for i in range(1, value.shape[0] // TILE):
        total = total + value[i * TILE : (i + 1) * TILE]
    return total


def norm_grad(value, gain, grad, acc_ref):
    q = mean_square(value)
    e = gain * grad
    acc_ref[...] += fold(grad * value * q)
    return q * e - value * (q * q * q) * jnp.mean(e * value, axis=-1, keepdims=True)


def mlp_norm_kernel(
    part_in, own_in, og_ref, gain_ref, low_ref, own_ref, acc_ref, part, inbox, out, *sems
):
    chunk = CHUNK
    part[...] = part_in[...]
    acc_ref[...] = jnp.zeros_like(acc_ref)

    def root(c, at, total):
        mine = block(c // 2, chunk)
        value = og_ref[at, :] + norm_grad(own_in[mine, :], gain_ref[...], total, acc_ref)
        own_ref[mine, :] = value
        out[at, :] = value

    def arrive(at):
        low_ref[at, :] = out[at, :].astype(BF16)

    line_sum("mp", chunk, part, inbox, out, sems, nothing, root, arrive)


def input_norm_kernel(part_in, own_in, x_ref, gain_ref, grad_ref, acc_ref, part, inbox, out, *sems):
    chunk = CHUNK
    part[...] = part_in[...]
    acc_ref[...] = jnp.zeros_like(acc_ref)

    def root(c, at, total):
        back = norm_grad(x_ref[at, :], gain_ref[...], total, acc_ref)
        out[at, :] = own_in[block(c // 2, chunk), :] + back

    def arrive(at):
        grad_ref[at, :] = out[at, :]

    line_sum("mp", chunk, part, inbox, out, sems, nothing, root, arrive)


def line_call(kernel, collective, outs, *args):
    rows, model = args[0].shape
    count = rows // CHUNK
    dma = pltpu.SemaphoreType.DMA
    return pl.pallas_call(
        kernel,
        out_shape=outs,
        in_specs=[VMEM] * len(args),
        out_specs=(VMEM,) * len(outs),
        scratch_shapes=[
            pltpu.VMEM((rows, model), F32),
            pltpu.VMEM((2, rows, model), F32),
            pltpu.VMEM((rows, model), F32),
            dma((count,)),
            dma((2, count)),
            dma((2, count)),
            dma((count,)),
        ],
        compiler_params=params(collective, 63),
        name=kernel.__name__,
    )(*args)


def params(collective, megabytes=60):
    return pltpu.CompilerParams(
        collective_id=collective, has_side_effects=True, vmem_limit_bytes=megabytes << 20
    )


def shape(dims, dtype=F32):
    return jax.ShapeDtypeStruct(dims, dtype)


def recurrence_forward(span, *args):
    x, _, w_branch = args[:3]
    state0 = args[8]
    rows, model = x.shape
    seqs, width = state0.shape
    devices = lax.axis_size("seq")
    dma = pltpu.SemaphoreType.DMA
    return pl.pallas_call(
        functools.partial(forward_kernel, span),
        out_shape=(
            shape((rows, model), BF16),
            shape((rows, width)),
            shape((seqs, span + TILE, width)),
            shape((rows, 2 * width)),
            shape((width // LANES, rows, LANES)),
            shape((rows, width), BF16),
            shape((seqs, width)),
            shape((devices, 2, seqs, width)),
        ),
        in_specs=[VMEM] * len(args),
        out_specs=(VMEM,) * 8,
        scratch_shapes=[
            pltpu.VMEM((width // LANES, rows, LANES), F32),
            pltpu.VMEM((width // LANES, rows, LANES), F32),
            pltpu.VMEM((span, width), F32),
            pltpu.VMEM((seqs, TILE, width), F32),
            pltpu.VMEM((seqs, TILE, width), F32),
            pltpu.VMEM((2, seqs, width), F32),
            dma((devices - 1,)),
            dma((devices - 1,)),
            dma((1,)),
            dma((1,)),
        ],
        compiler_params=params(0),
        name="recurrence_forward",
    )(*args)


def recurrence_backward(span, *args):
    rows, width = args[0].shape
    seqs = args[3].shape[0]
    taps = args[7].shape[0]
    devices = lax.axis_size("seq")
    dma = pltpu.SemaphoreType.DMA
    return pl.pallas_call(
        functools.partial(backward_kernel, span),
        out_shape=(
            shape((rows, width), BF16),
            shape((rows, width), BF16),
            shape((rows, width), BF16),
            shape((rows, 2 * width), BF16),
            shape((4 + taps, TILE, width)),
        ),
        in_specs=[VMEM] * len(args),
        out_specs=(VMEM,) * 5,
        scratch_shapes=[
            pltpu.VMEM((width // LANES, rows, LANES), F32),
            pltpu.VMEM((width // LANES, rows, LANES), F32),
            pltpu.VMEM((width // LANES, rows, LANES), F32),
            pltpu.VMEM((span, width), F32),
            pltpu.VMEM((seqs, span + TILE, width), F32),
            pltpu.VMEM((seqs, width), F32),
            pltpu.VMEM((devices, seqs, width), F32),
            pltpu.VMEM((seqs, TILE, width), F32),
            pltpu.VMEM((seqs, TILE, width), F32),
            dma((devices - 1,)),
            dma((devices - 1,)),
            dma((1,)),
            dma((1,)),
        ],
        compiler_params=params(1),
        name="recurrence_backward",
    )(*args)


def rms_scale(values, gain):
    return values * lax.rsqrt(jnp.mean(values * values, axis=-1, keepdims=True) + EPS) * gain


def norm_back(values, gain, grad):
    q = lax.rsqrt(jnp.mean(values * values, axis=-1, keepdims=True) + EPS)
    e = gain * grad
    back = q * e - values * (q * q * q) * jnp.mean(e * values, axis=-1, keepdims=True)
    return back, jnp.sum(grad * values * q, axis=0)


def widen(array, width):
    short = width - array.shape[-1]
    if short == 0:
        return array
    return jnp.pad(array, [(0, 0)] * (array.ndim - 1) + [(0, short)])


def diagonal(gates, width):
    heads, size, _ = gates.shape
    spread = jnp.eye(heads, dtype=gates.dtype)[:, None, :, None] * gates[:, :, None, :]
    flat = spread.reshape(heads * size, heads * size)
    short = width - heads * size
    return jnp.pad(flat, ((0, short), (0, short))) if short else flat


def per_device(
    stream,
    norm_in,
    w_branch,
    w_input,
    conv_kernel,
    conv_bias,
    gate_r,
    bias_r,
    gate_i,
    bias_i,
    decay_param,
    w_out,
    norm_mlp,
    w_gate,
    w_up,
    w_down,
    state_init,
    conv_init,
    fresh_rows,
    out_grad,
):
    seqs, span, model = stream.shape
    channels = w_branch.shape[1]
    mlp_dev = w_gate.shape[1]
    heads, head_width = gate_r.shape[:2]
    taps = conv_kernel.shape[0]
    edge = taps - 1
    rows = seqs * span
    devices = lax.axis_size("seq")
    position = lax.axis_index("seq")
    width = -(-channels // 128) * 128

    keep = 1.0 - fresh_rows.astype(F32)
    flat_in = stream.reshape(rows, model)
    flat_grad = out_grad.reshape(rows, model)
    w_branch_p = widen(w_branch, width)
    w_input_p = widen(w_input, width)
    w_out_p = jnp.pad(w_out, ((0, width - channels), (0, 0))) if width > channels else w_out
    taps_p = widen(conv_kernel, width)
    rate = jax.nn.softplus(-decay_param)
    rate_p = jnp.pad(rate, (0, width - channels), constant_values=1.0)
    vec = jnp.stack([widen(conv_bias, width), rate_p])
    gates = jnp.concatenate([diagonal(gate_r, width), diagonal(gate_i, width)], axis=1)
    gates_t = jnp.concatenate(
        [
            diagonal(jnp.swapaxes(gate_r, 1, 2), width),
            diagonal(jnp.swapaxes(gate_i, 1, 2), width),
        ],
        axis=0,
    )
    gate_bias = jnp.concatenate([widen(bias_r, width), widen(bias_i, width)])[None]
    state0 = widen(state_init * keep[:, None], width)
    conv0 = jnp.pad(
        conv_init * keep[:, None, None], ((0, 0), (TILE - edge, 0), (0, width - channels))
    )

    normed, branch, padded, pre, hidden, mixed, carry, sums = recurrence_forward(
        span,
        flat_in,
        norm_in[None],
        w_branch_p,
        w_input_p,
        taps_p,
        vec,
        gates,
        gate_bias,
        state0,
        conv0,
    )
    normed_mlp, own = line_call(
        residual_kernel,
        2,
        (shape((rows, model), BF16), shape((rows // 2, model))),
        dot(mixed, w_out_p),
        flat_in,
        norm_mlp[None],
    )
    gate_val = dot(normed_mlp, w_gate)
    up_val = dot(normed_mlp, w_up)
    act, slope = gelu_both(gate_val)
    hidden_mlp = (act * up_val).astype(BF16)
    grad_low = flat_grad.astype(BF16)
    grad_hidden = matmul_back(grad_low, w_down)
    grad_gate = (grad_hidden * up_val * slope).astype(BF16)
    grad_up = (grad_hidden * act).astype(BF16)
    resid_low, own_grad, norm_mlp_acc = line_call(
        mlp_norm_kernel,
        3,
        (shape((rows, model), BF16), shape((rows // 2, model)), shape((TILE, model))),
        matmul_back(grad_gate, w_gate) + matmul_back(grad_up, w_up),
        own,
        flat_grad,
        norm_mlp[None],
    )
    middle = lax.axis_size("mp") // 2
    plane = lax.axis_index("mp")
    parity = (lax.broadcasted_iota(jnp.int32, (rows // CHUNK // 2, 2, CHUNK, model), 1)) + middle - 1
    spread = jnp.where(parity == plane, own.reshape(-1, 1, CHUNK, model), 0.0)
    block_out = lax.psum(dot(hidden_mlp, w_down) + spread.reshape(rows, model), "mp")
    grad_mixed = matmul_back(resid_low, w_out_p)
    grad_branch, input_low, heads_in, pre_low, acc = recurrence_backward(
        span,
        grad_mixed,
        branch,
        hidden,
        carry,
        pre,
        padded,
        sums,
        taps_p,
        vec,
        gates_t,
    )
    stream_grad, norm_in_acc = line_call(
        input_norm_kernel,
        4,
        (shape((rows, model)), shape((TILE, model))),
        matmul_back(grad_branch, w_branch_p) + matmul_back(input_low, w_input_p),
        own_grad,
        flat_in,
        norm_in[None],
    )
    norm_grads = lax.psum((jnp.sum(norm_in_acc, 0), jnp.sum(norm_mlp_acc, 0)), ("seq", "mp"))
    norm_in_grad, norm_mlp_grad = norm_grads

    def weight(left, right):
        return lax.dot_general(left, right, CONTRACT_ROWS, preferred_element_type=F32)

    def scatter(array, dim):
        return lax.psum_scatter(array, "seq", scatter_dimension=dim, tiled=True)

    w_down_grad = scatter(weight(grad_low, hidden_mlp), 0)
    w_gate_grad = scatter(weight(normed_mlp, grad_gate), 0)
    w_up_grad = scatter(weight(normed_mlp, grad_up), 0)
    w_out_grad = scatter(weight(resid_low, mixed), 0)
    w_branch_grad = scatter(weight(normed, grad_branch), 0)
    w_input_grad = scatter(weight(normed, input_low), 0)

    gates_grad = weight(heads_in, pre_low)

    def blocks(array):
        return jnp.stack(
            [
                array[h * head_width : (h + 1) * head_width, h * head_width : (h + 1) * head_width]
                for h in range(heads)
            ]
        )

    acc = jnp.sum(acc, axis=1)[:, :channels]
    last = position == devices - 1
    last_hidden = hidden.reshape(-1, seqs, span, LANES)[:, :, -1]
    last_hidden = jnp.swapaxes(last_hidden, 0, 1).reshape(seqs, width)[:, :channels]
    final_state = jnp.where(last, last_hidden, 0.0)
    final_conv = jnp.where(last, padded[:, span + TILE - edge :, :channels], 0.0)
    small = lax.psum(
        (
            acc,
            blocks(gates_grad[:, :width]),
            blocks(gates_grad[:, width:]),
            final_state,
            final_conv,
        ),
        "seq",
    )
    acc, gate_r_grad, gate_i_grad, final_state, final_conv = small
    decay_grad = acc[0] * (RATE_SCALE * jax.nn.sigmoid(-decay_param))
    return (
        block_out.reshape(stream.shape),
        stream_grad.reshape(stream.shape),
        norm_in_grad,
        w_branch_grad[:, :channels],
        w_input_grad[:, :channels],
        acc[4:],
        acc[3],
        gate_r_grad,
        acc[1],
        gate_i_grad,
        acc[2],
        decay_grad,
        w_out_grad[:, :channels].T,
        norm_mlp_grad,
        w_gate_grad,
        w_up_grad,
        w_down_grad.T,
        final_state,
        final_conv,
    )


def solution(mesh):
    seq_rows = P(None, "seq", None)
    columns = P(None, "mp")
    channel = P("mp")
    return jax.shard_map(
        per_device,
        mesh=mesh,
        in_specs=(
            seq_rows,
            P(),
            columns,
            columns,
            columns,
            channel,
            P("mp", None, None),
            channel,
            P("mp", None, None),
            channel,
            channel,
            P("mp", None),
            P(),
            columns,
            columns,
            P("mp", None),
            columns,
            P(None, None, "mp"),
            P(),
            seq_rows,
        ),
        out_specs=(
            seq_rows,
            seq_rows,
            P(),
            P("seq", "mp"),
            P("seq", "mp"),
            columns,
            channel,
            P("mp", None, None),
            channel,
            P("mp", None, None),
            channel,
            channel,
            P("mp", "seq"),
            P(),
            P("seq", "mp"),
            P("seq", "mp"),
            P("mp", "seq"),
            columns,
            P(None, None, "mp"),
        ),
        check_vma=False,
    )
```

```python
import functools

import jax
import jax.numpy as jnp
from jax import lax
from jax.experimental import pallas as pl
from jax.experimental.pallas import tpu as pltpu
from jax.sharding import PartitionSpec as P

MESH = pl.DeviceIdType.MESH
RATE_SCALE = 8.0
EPS = 1e-06
GELU_C = 0.7978845608028654
GELU_K = 0.044715
CONTRACT_ROWS = (((0,), (0,)), ((), ()))
CONTRACT_LAST = (((1,), (1,)), ((), ()))
TILE = 8
LANES = 128
ROWS = 32
CHUNK = 32
SKEW = 2
RING = 16
GROUP = 8
TURN = 256
F32 = jnp.float32
BF16 = jnp.bfloat16
VMEM = pl.BlockSpec(memory_space=pltpu.VMEM)


def dot(a, b):
    return jnp.dot(a, b, preferred_element_type=F32)


def matmul_back(a, b):
    return lax.dot_general(a, b, CONTRACT_LAST, preferred_element_type=F32)


def block(i, size):
    return pl.ds(pl.multiple_of(i * size, size), size)


def gelu(x):
    t = jnp.tanh(GELU_C * (x + GELU_K * (x * x * x)))
    return 0.5 * x * (1.0 + t)


def gelu_both(x):
    x2 = x * x
    t = jnp.tanh(GELU_C * (x + GELU_K * (x2 * x)))
    half = 0.5 * (1.0 + t)
    slope = half + 0.5 * x * (1.0 - t * t) * (GELU_C * (1.0 + (3.0 * GELU_K) * x2))
    return x * half, slope


def one_minus_square(log_a, a):
    y = 2.0 * log_a
    s = 1.0 + y * (1.0 / 8.0)
    for k in (7, 6, 5, 4, 3, 2):
        s = 1.0 + (y * (1.0 / k)) * s
    return jnp.where(y > -0.35, -y * s, 1.0 - a * a)


def get(ref, at):
    return jnp.concatenate([ref[j, at, :] for j in range(ref.shape[0])], axis=-1)


def put(ref, at, value):
    for j in range(ref.shape[0]):
        ref[j, at, :] = value[:, j * LANES : (j + 1) * LANES]


def to_all(axis, src, slots, send, recv):
    size, me = lax.axis_size(axis), lax.axis_index(axis)
    return [
        pltpu.make_async_remote_copy(
            src_ref=src,
            dst_ref=slots.at[me],
            send_sem=send.at[d - 1],
            recv_sem=recv.at[d - 1],
            device_id={axis: lax.rem(me + d, size)},
            device_id_type=MESH,
        )
        for d in range(1, size)
    ]


def to_one(axis, distance, src, dst, send, recv):
    size, me = lax.axis_size(axis), lax.axis_index(axis)
    return pltpu.make_async_remote_copy(
        src_ref=src,
        dst_ref=dst,
        send_sem=send,
        recv_sem=recv,
        device_id={axis: lax.rem(me + distance + size, size)},
        device_id_type=MESH,
    )


def forward_kernel(
    span,
    x_ref,
    gain_ref,
    w_branch_ref,
    w_input_ref,
    taps_ref,
    vec_ref,
    gates_ref,
    gate_bias_ref,
    state0_ref,
    conv0_ref,
    normed_ref,
    branch_ref,
    pad_ref,
    pre_ref,
    hidden_ref,
    mixed_ref,
    carry_ref,
    sums_ref,
    a_ref,
    b_ref,
    conv_ref,
    tail_ref,
    tail_in,
    mine_ref,
    send1,
    recv1,
    send_t,
    recv_t,
):
    seqs = state0_ref.shape[0]
    width = taps_ref.shape[1]
    taps = taps_ref.shape[0]
    rows = seqs * span
    devices, me = lax.axis_size("seq"), lax.axis_index("seq")
    enter_all(("seq",))

    group = 2 * span

    @pl.loop(0, rows // group)
    def _(g):
        @pl.loop(0, group // ROWS)
        def _(q):
            at = block(g * (group // ROWS) + q, ROWS)
            x = x_ref[at, :]
            scale = lax.rsqrt(jnp.mean(x * x, axis=-1, keepdims=True) + EPS)
            normed_ref[at, :] = (x * scale * gain_ref[...]).astype(BF16)

        conv = dot(normed_ref[block(g, group), :], w_input_ref[...])
        for j in range(group // span):
            pad_ref[g * (group // span) + j, pl.ds(TILE, span), :] = conv[
                j * span : (j + 1) * span
            ]

    for s in range(seqs):
        tail_ref[s] = pad_ref[s, pl.ds(span, TILE), :]
    tail_copy = to_one("seq", 1, tail_ref, tail_in, send_t.at[0], recv_t.at[0])
    tail_copy.start()

    @pl.loop(0, rows // group)
    def _(g):
        branch_ref[block(g, group), :] = dot(normed_ref[block(g, group), :], w_branch_ref[...])

    tail_copy.wait()
    for s in range(seqs):
        pad_ref[s, pl.ds(0, TILE), :] = jnp.where(me == 0, conv0_ref[s], tail_in[s])

    def conv_rows(s, q):
        part = pad_ref[s, pl.ds(pl.multiple_of(q * ROWS, ROWS), ROWS + TILE), :]
        total = vec_ref[0:1, :]
        for k in range(taps):
            first = TILE - (taps - 1) + k
            total = total + taps_ref[k : k + 1, :] * part[first : first + ROWS]
        return total

    @pl.loop(0, seqs)
    def _(s):
        @pl.loop(0, span // ROWS)
        def _(q):
            conv_ref[block(q, ROWS), :] = conv_rows(s, q)

        pre_ref[block(s, span), :] = (
            dot(conv_ref[...].astype(BF16), gates_ref[...]) + gate_bias_ref[...]
        )

        @pl.loop(0, span // ROWS)
        def _(q):
            at = block(s * (span // ROWS) + q, ROWS)
            conv = conv_ref[block(q, ROWS), :]
            recall = jax.nn.sigmoid(pre_ref[at, :width])
            gate = jax.nn.sigmoid(pre_ref[at, width:])
            log_a = (-RATE_SCALE * vec_ref[1:2, :]) * recall
            a = jnp.exp(log_a)
            put(a_ref, at, a)
            put(b_ref, at, jnp.sqrt(one_minus_square(log_a, a)) * gate * conv)

    def at_time(ref, t):
        return get(ref, pl.ds(t, seqs, stride=span))

    def local(t, value):
        prod, state = value
        a = at_time(a_ref, t)
        return prod * a, a * state + at_time(b_ref, t)

    ones = jnp.ones((seqs, width), F32)
    prod, state = lax.fori_loop(0, span, local, (ones, jnp.zeros_like(ones)), unroll=8)
    mine_ref[0] = prod
    mine_ref[1] = state
    sums_ref[me] = mine_ref[...]
    copies = to_all("seq", mine_ref, sums_ref, send1, recv1)
    for copy in copies:
        copy.start()
    for copy in copies:
        copy.wait()

    def carry_step(j, carry):
        both = sums_ref[j]
        return jnp.where(j < me, both[0] * carry + both[1], carry)

    carry = lax.fori_loop(0, devices - 1, carry_step, state0_ref[...])
    carry_ref[...] = carry

    def final(t, state):
        state = at_time(a_ref, t) * state + at_time(b_ref, t)
        put(hidden_ref, pl.ds(t, seqs, stride=span), state)
        return state

    lax.fori_loop(0, span, final, carry, unroll=8)

    @pl.loop(0, rows // ROWS)
    def _(q):
        at = block(q, ROWS)
        mixed_ref[at, :] = (get(hidden_ref, at) * gelu(branch_ref[at, :])).astype(BF16)


def backward_kernel(
    span,
    grad_ref,
    branch_ref,
    hidden_ref,
    carry_ref,
    pre_ref,
    pad_ref,
    sums_ref,
    taps_ref,
    vec_ref,
    gates_t_ref,
    grad_branch_ref,
    input_ref,
    heads_ref,
    low_ref,
    acc_ref,
    a_ref,
    gd_ref,
    gs_ref,
    direct_ref,
    gpad_ref,
    mine_ref,
    entries_ref,
    head_ref,
    head_in,
    send1,
    recv1,
    send_t,
    recv_t,
):
    seqs, width = carry_ref.shape
    taps = taps_ref.shape[0]
    rows = seqs * span
    devices, me = lax.axis_size("seq"), lax.axis_index("seq")
    enter_all(("seq",))

    def decay(at):
        recall = jax.nn.sigmoid(pre_ref[at, :width])
        log_a = (-RATE_SCALE * vec_ref[1:2, :]) * recall
        return recall, log_a, jnp.exp(log_a)

    @pl.loop(0, rows // ROWS)
    def _(q):
        at = block(q, ROWS)
        put(a_ref, at, decay(at)[2])
        act, slope = gelu_both(branch_ref[at, :])
        grad = grad_ref[at, :]
        put(gd_ref, at, grad * act)
        grad_branch_ref[at, :] = (grad * get(hidden_ref, at) * slope).astype(BF16)

    def at_time(ref, t):
        return get(ref, pl.ds(t, seqs, stride=span))

    def local(k, through):
        t = span - 1 - k
        return at_time(a_ref, t) * (at_time(gd_ref, t) + through)

    zero = jnp.zeros((seqs, width), F32)
    mine_ref[...] = lax.fori_loop(0, span, local, zero, unroll=8)
    entries_ref[me] = mine_ref[...]
    copies = to_all("seq", mine_ref, entries_ref, send1, recv1)
    for copy in copies:
        copy.start()
    acc_ref[...] = jnp.zeros_like(acc_ref)
    for copy in copies:
        copy.wait()

    def back_step(k, through):
        j = devices - 1 - k
        return jnp.where(j > me, entries_ref[j] + sums_ref[j, 0] * through, through)

    incoming = lax.fori_loop(0, devices - 1, back_step, zero)

    def final(k, through):
        t = span - 1 - k
        grad = at_time(gd_ref, t) + through
        put(gs_ref, pl.ds(t, seqs, stride=span), grad)
        return at_time(a_ref, t) * grad

    lax.fori_loop(0, span, final, incoming, unroll=8)

    def add(k, value):
        total = value[0:TILE]
        for i in range(1, value.shape[0] // TILE):
            total = total + value[i * TILE : (i + 1) * TILE]
        acc_ref[k] += total

    @pl.loop(0, seqs)
    def _(s):
        @pl.loop(0, span // ROWS)
        def _(q):
            at = block(s * (span // ROWS) + q, ROWS)
            part = pad_ref[s, pl.ds(pl.multiple_of(q * ROWS, ROWS), ROWS + TILE), :]
            conv = vec_ref[0:1, :]
            for k in range(taps):
                first = TILE - (taps - 1) + k
                conv = conv + taps_ref[k : k + 1, :] * part[first : first + ROWS]
            heads_ref[at, :] = conv.astype(BF16)
            recall, log_a, a = decay(at)
            gate = jax.nn.sigmoid(pre_ref[at, width:])
            square = one_minus_square(log_a, a)
            inverse = lax.rsqrt(square)
            root = jnp.sqrt(square)
            grad = get(gs_ref, at)
            hidden = get(hidden_ref, at)
            before_at = pl.multiple_of(jnp.maximum(s * span + q * ROWS - TILE, 0), TILE)
            earlier = get(hidden_ref, pl.ds(before_at, TILE))
            first_row = jnp.where(q == 0, carry_ref[pl.ds(s, 1), :], earlier[TILE - 1 :])
            place = lax.broadcasted_iota(jnp.int32, (ROWS, width), 0)
            prev = jnp.where(place == 0, first_row, pltpu.roll(hidden, 1, 0))
            grad_log = grad * a * (prev - gate * conv * a * inverse)
            through = grad_log * recall
            pre_r = through * (1.0 - recall) * (-RATE_SCALE * vec_ref[1:2, :])
            direct = grad * root * gate
            pre_i = direct * conv * (1.0 - gate)
            low_ref[at, :width] = pre_r.astype(BF16)
            low_ref[at, width:] = pre_i.astype(BF16)
            direct_ref[block(q, ROWS), :] = direct
            add(0, through)
            add(1, pre_r)
            add(2, pre_i)

        whole = direct_ref[...] + dot(low_ref[block(s, span), :], gates_t_ref[...])
        gpad_ref[s, pl.ds(0, span), :] = whole
        head_ref[s] = whole[:TILE]

    head_copy = to_one("seq", -1, head_ref, head_in, send_t.at[0], recv_t.at[0])
    head_copy.start()

    @pl.loop(0, seqs)
    def _(s):
        @pl.loop(0, span // ROWS)
        def _(q):
            at = pl.multiple_of(q * ROWS, ROWS)
            part = pad_ref[s, pl.ds(at, ROWS + TILE), :]
            grad = gpad_ref[s, pl.ds(at, ROWS), :]
            add(3, grad)
            for k in range(taps):
                first = TILE - (taps - 1) + k
                add(4 + k, grad * part[first : first + ROWS])

    head_copy.wait()
    for s in range(seqs):
        gpad_ref[s, pl.ds(span, TILE), :] = jnp.where(me == devices - 1, 0.0, head_in[s])

    @pl.loop(0, seqs)
    def _(s):
        @pl.loop(0, span // ROWS)
        def _(q):
            part = gpad_ref[s, pl.ds(pl.multiple_of(q * ROWS, ROWS), ROWS + TILE), :]
            total = taps_ref[taps - 1 : taps, :] * part[0:ROWS]
            for k in range(taps - 1):
                first = taps - 1 - k
                total = total + taps_ref[k : k + 1, :] * part[first : first + ROWS]
            input_ref[block(s * (span // ROWS) + q, ROWS), :] = total.astype(BF16)


def line_sum(axis, total, period, chunk, part, inbox, out, sems, before, root, arrive, leave):
    send_up, send_down, recv_up, recv_down = sems
    n, z = lax.axis_size(axis), lax.axis_index(axis)
    depth = n // 2

    def root_of(c):
        return depth - 1 + lax.rem(c, 2)

    def up(c, step, side):
        slot = lax.rem(c, RING)
        return pltpu.make_async_remote_copy(
            src_ref=part.at[block(lax.rem(c, period), chunk)],
            dst_ref=inbox.at[side, slot],
            send_sem=send_up.at[slot],
            recv_sem=recv_up.at[side, slot],
            device_id={axis: z + step},
            device_id_type=MESH,
        )

    def down(c, step, side):
        slot = lax.rem(c, RING)
        return pltpu.make_async_remote_copy(
            src_ref=out.at[slot],
            dst_ref=out.at[slot],
            send_sem=send_down.at[side, slot],
            recv_sem=recv_down.at[slot],
            device_id={axis: z + step},
            device_id_type=MESH,
        )

    inner = jnp.logical_and(z > 0, z < n - 1)

    @pl.loop(0, total + RING)
    def _(k):
        @pl.when(k >= RING)
        def _():
            c = k - RING
            r = root_of(c)
            step = jnp.where(z < r, 1, -1)
            side = jnp.where(z < r, 0, 1)

            @pl.when(z == r)
            def _():
                down(c, -1, 0).wait_send()
                down(c, 1, 1).wait_send()

            @pl.when(z != r)
            def _():
                up(c, step, side).wait_send()

            @pl.when(jnp.logical_and(z != r, inner))
            def _():
                down(c, -step, side).wait_send()

            leave(c, lax.rem(c, RING))

        before(k)

        for i in reversed(range(n + 1)):
            c = k - SKEW * i
            valid = jnp.logical_and(c >= 0, c < total)
            c = jnp.clip(c, 0, total - 1)
            at = block(lax.rem(c, period), chunk)
            slot = lax.rem(c, RING)
            r = root_of(c)
            step = jnp.where(z < r, 1, -1)
            side = jnp.where(z < r, 0, 1)
            if i > depth:
                here = jnp.logical_and(z != r, jnp.abs(z - r) == i - depth)

                @pl.when(jnp.logical_and(valid, here))
                def _():
                    down(c, -step, side).wait_recv()

                    @pl.when(inner)
                    def _():
                        down(c, -step, side).start()

                    arrive(c, slot)
            elif i == depth:

                @pl.when(jnp.logical_and(valid, z == r))
                def _():
                    up(c, 1, 0).wait_recv()
                    up(c, -1, 1).wait_recv()
                    root(c, slot, part[at, :] + inbox[0, slot] + inbox[1, slot])
                    down(c, -1, 0).start()
                    down(c, 1, 1).start()
                    arrive(c, slot)
            else:
                here = jnp.where(z < r, z, n - 1 - z) == i

                @pl.when(jnp.logical_and(valid, jnp.logical_and(z != r, here)))
                def _():
                    if i > 0:
                        up(c, step, side).wait_recv()
                        part[at, :] += inbox[side, slot]
                    up(c, step, side).start()


def enter_line(axis):
    n, z = lax.axis_size(axis), lax.axis_index(axis)
    barrier = pltpu.get_barrier_semaphore()

    @pl.when(z > 0)
    def _():
        pl.semaphore_signal(barrier, 1, device_id={axis: z - 1}, device_id_type=MESH)

    @pl.when(z < n - 1)
    def _():
        pl.semaphore_signal(barrier, 1, device_id={axis: z + 1}, device_id_type=MESH)

    pl.semaphore_wait(barrier, jnp.where(jnp.logical_or(z == 0, z == n - 1), 1, 2))


def line_scratch(rows, model):
    dma = pltpu.SemaphoreType.DMA
    return [
        pltpu.VMEM((rows, model), F32),
        pltpu.VMEM((2, RING, CHUNK, model), F32),
        pltpu.VMEM((RING, CHUNK, model), F32),
        dma((RING,)),
        dma((2, RING)),
        dma((2, RING)),
        dma((RING,)),
    ]


def mean_square(x):
    return lax.rsqrt(jnp.mean(x * x, axis=-1, keepdims=True) + EPS)


def nothing(*_):
    pass


def fold(value):
    total = value[0:TILE]
    for i in range(1, value.shape[0] // TILE):
        total = total + value[i * TILE : (i + 1) * TILE]
    return total


def norm_grad(value, gain, grad, acc_ref):
    q = mean_square(value)
    e = gain * grad
    acc_ref[...] += fold(grad * value * q)
    return q * e - value * (q * q * q) * jnp.mean(e * value, axis=-1, keepdims=True)


def residual_kernel(part_in, x_ref, gain_ref, normed_ref, own_ref, part, inbox, out, *sems):
    count = part.shape[0] // CHUNK
    enter_line("mp")
    part[...] = part_in[...]

    def root(c, slot, total):
        value = x_ref[block(c, CHUNK), :] + total
        own_ref[block(c // 2, CHUNK), :] = value
        out[slot] = (value * mean_square(value) * gain_ref[...]).astype(BF16).astype(F32)

    def arrive(c, slot):
        normed_ref[block(c, CHUNK), :] = out[slot].astype(BF16)

    line_sum("mp", count, count, CHUNK, part, inbox, out, sems, nothing, root, arrive, nothing)


def mlp_norm_kernel(
    part_in, own_in, og_ref, gain_ref, low_ref, own_ref, acc_ref, part, inbox, out, *sems
):
    count = part.shape[0] // CHUNK
    enter_line("mp")
    part[...] = part_in[...]
    acc_ref[...] = jnp.zeros_like(acc_ref)

    def root(c, slot, total):
        mine = block(c // 2, CHUNK)
        back = norm_grad(own_in[mine, :], gain_ref[...], total, acc_ref)
        value = og_ref[block(c, CHUNK), :] + back
        own_ref[mine, :] = value
        out[slot] = value

    def arrive(c, slot):
        low_ref[block(c, CHUNK), :] = out[slot].astype(BF16)

    line_sum("mp", count, count, CHUNK, part, inbox, out, sems, nothing, root, arrive, nothing)


def last_kernel(
    block_part,
    grad_part,
    own_ref,
    own_grad_ref,
    x_ref,
    gain_ref,
    block_ref,
    grad_ref,
    norm_ref,
    part,
    inbox,
    out,
    send_up,
    send_down,
    recv_up,
    recv_down,
    load_sem,
    store_sem,
    acc_ref,
    mine_ref,
    seq_in,
    mp_in,
    send_s,
    recv_s,
    send_m,
    recv_m,
):
    count = part.shape[0] // CHUNK
    group = GROUP * CHUNK
    groups = count // GROUP
    sems = (send_up, send_down, recv_up, recv_down)
    enter_all(("seq", "mp"))
    acc_ref[...] = jnp.zeros_like(acc_ref)

    def load(source, g):
        at = block(lax.rem(g, groups), group)
        return pltpu.make_async_copy(source.at[at], part.at[at], load_sem.at[lax.rem(g, 2)])

    def start_load(g):
        @pl.when(g < groups)
        def _():
            load(block_part, g).start()

        @pl.when(jnp.logical_and(g >= groups, g < 2 * groups))
        def _():
            load(grad_part, g).start()

    start_load(jnp.int32(0))

    def before(k):
        @pl.when(jnp.logical_and(lax.rem(k, GROUP) == 0, k < 2 * count))
        def _():
            g = k // GROUP
            load(block_part, g).wait()
            start_load(g + 1)

    def root(c, slot, total):
        j = lax.rem(c, count)
        mine = block(j // 2, CHUNK)

        @pl.when(c < count)
        def _():
            out[slot] = own_ref[mine, :] + total

        @pl.when(c >= count)
        def _():
            back = norm_grad(x_ref[block(j, CHUNK), :], gain_ref[...], total, acc_ref)
            out[slot] = own_grad_ref[mine, :] + back

    def store(target, c, slot):
        at = block(lax.rem(c, count), CHUNK)
        return pltpu.make_async_copy(out.at[slot], target.at[at], store_sem.at[slot])

    def arrive(c, slot):
        @pl.when(c < count)
        def _():
            store(block_ref, c, slot).start()

        @pl.when(c >= count)
        def _():
            store(grad_ref, c, slot).start()

    def leave(c, slot):
        store(block_ref, c, slot).wait()

    line_sum("mp", 2 * count, count, CHUNK, part, inbox, out, sems, before, root, arrive, leave)

    for axis, inbox_ref, send, recv in (
        ("seq", seq_in, send_s, recv_s),
        ("mp", mp_in, send_m, recv_m),
    ):
        if axis == "seq":
            mine_ref[0] = jnp.sum(acc_ref[...], axis=0, keepdims=True)
        else:
            mine_ref[1] = jnp.sum(seq_in[...], axis=0)
        source = mine_ref.at[0 if axis == "seq" else 1]
        inbox_ref[lax.axis_index(axis)] = source[...]
        copies = to_all(axis, source, inbox_ref, send, recv)
        for copy in copies:
            copy.start()
        for copy in copies:
            copy.wait()
    norm_ref[...] = jnp.sum(mp_in[...], axis=0)


def enter_all(axes):
    barrier = pltpu.get_barrier_semaphore()
    count = 0
    for axis in axes:
        size, me = lax.axis_size(axis), lax.axis_index(axis)
        for d in range(1, size):
            pl.semaphore_signal(
                barrier, 1, device_id={axis: lax.rem(me + d, size)}, device_id_type=MESH
            )
        count += size - 1
    pl.semaphore_wait(barrier, count)


def cost(micros):
    return pl.CostEstimate(flops=int(micros * 1e9), bytes_accessed=1 << 20, transcendentals=0)


def line_call(kernel, collective, outs, *args):
    rows, model = args[0].shape
    return pl.pallas_call(
        kernel,
        out_shape=outs,
        in_specs=[VMEM] * len(args),
        out_specs=(VMEM,) * len(outs),
        scratch_shapes=line_scratch(rows, model),
        compiler_params=params(collective, 63),
        cost_estimate=cost(200),
        name=kernel.__name__,
    )(*args)


def last_call(*args):
    rows, model = args[0].shape
    dma = pltpu.SemaphoreType.DMA
    nseq, nmp = lax.axis_size("seq"), lax.axis_size("mp")
    hbm = pl.BlockSpec(memory_space=pl.ANY)
    return pl.pallas_call(
        last_kernel,
        out_shape=(shape((rows, model)), shape((rows, model)), shape((1, model))),
        in_specs=[hbm, hbm, VMEM, VMEM, VMEM, VMEM],
        out_specs=(hbm, hbm, VMEM),
        scratch_shapes=line_scratch(rows, model)
        + [
            dma((2,)),
            dma((RING,)),
            pltpu.VMEM((TILE, model), F32),
            pltpu.VMEM((2, 1, model), F32),
            pltpu.VMEM((nseq, 1, model), F32),
            pltpu.VMEM((nmp, 1, model), F32),
            dma((nseq - 1,)),
            dma((nseq - 1,)),
            dma((nmp - 1,)),
            dma((nmp - 1,)),
        ],
        compiler_params=params(4, 60),
        cost_estimate=cost(380),
        name="last_sums",
    )(*args)


def weight_kernel(plan, lefts, *refs):
    left_refs, right_refs = refs[:lefts], refs[lefts:-2]
    out_ref, turned = refs[-2:]
    j = pl.program_id(0)
    begin = 0
    held = None
    for (left, blocks), right in zip(plan, right_refs):
        if left != held:
            held = left

            @pl.when(j == begin)
            def _():
                rows = left_refs[left].shape[0]
                for i in range(left_refs[left].shape[1] // TURN):
                    at = slice(i * TURN, (i + 1) * TURN)
                    turned[at, :] = left_refs[left][:, at].T

        @pl.when(jnp.logical_and(j >= begin, j < begin + blocks))
        def _():
            size = turned.shape[0] // 4

            @pl.loop(0, 4)
            def _(i):
                out_ref[block(i, size), :] = dot(turned[block(i, size), :], right[...])

        begin += blocks


def weight_grads(lefts, pairs, width):
    rows, model = lefts[0].shape
    plan = tuple((left, right.shape[1] // width) for left, right in pairs)
    steps = sum(blocks for _, blocks in plan)
    whole = pl.BlockSpec((rows, model), lambda j: (0, 0))
    specs = [whole] * len(lefts)
    begin = 0
    for _, blocks in plan:
        specs.append(
            pl.BlockSpec(
                (rows, width),
                lambda j, first=begin, n=blocks: (0, jnp.clip(j - first, 0, n - 1)),
            )
        )
        begin += blocks
    return pl.pallas_call(
        functools.partial(weight_kernel, plan, len(lefts)),
        out_shape=shape((model, steps * width)),
        grid=(steps,),
        in_specs=specs,
        out_specs=pl.BlockSpec((model, width), lambda j: (0, j)),
        scratch_shapes=[pltpu.VMEM((model, rows), BF16)],
        compiler_params=pltpu.CompilerParams(vmem_limit_bytes=60 << 20),
        cost_estimate=cost(30),
        name="weight_grads",
    )(*lefts, *(right for _, right in pairs))


def params(collective, megabytes=60):
    return pltpu.CompilerParams(
        collective_id=collective, has_side_effects=True, vmem_limit_bytes=megabytes << 20
    )


def shape(dims, dtype=F32):
    return jax.ShapeDtypeStruct(dims, dtype)


def recurrence_forward(span, *args):
    x, _, w_branch = args[:3]
    state0 = args[8]
    rows, model = x.shape
    seqs, width = state0.shape
    devices = lax.axis_size("seq")
    dma = pltpu.SemaphoreType.DMA
    return pl.pallas_call(
        functools.partial(forward_kernel, span),
        out_shape=(
            shape((rows, model), BF16),
            shape((rows, width)),
            shape((seqs, span + TILE, width)),
            shape((rows, 2 * width)),
            shape((width // LANES, rows, LANES)),
            shape((rows, width), BF16),
            shape((seqs, width)),
            shape((devices, 2, seqs, width)),
        ),
        in_specs=[VMEM] * len(args),
        out_specs=(VMEM,) * 8,
        scratch_shapes=[
            pltpu.VMEM((width // LANES, rows, LANES), F32),
            pltpu.VMEM((width // LANES, rows, LANES), F32),
            pltpu.VMEM((span, width), F32),
            pltpu.VMEM((seqs, TILE, width), F32),
            pltpu.VMEM((seqs, TILE, width), F32),
            pltpu.VMEM((2, seqs, width), F32),
            dma((devices - 1,)),
            dma((devices - 1,)),
            dma((1,)),
            dma((1,)),
        ],
        compiler_params=params(0),
        cost_estimate=cost(50),
        name="recurrence_forward",
    )(*args)


def recurrence_backward(span, *args):
    rows, width = args[0].shape
    seqs = args[3].shape[0]
    taps = args[7].shape[0]
    devices = lax.axis_size("seq")
    dma = pltpu.SemaphoreType.DMA
    return pl.pallas_call(
        functools.partial(backward_kernel, span),
        out_shape=(
            shape((rows, width), BF16),
            shape((rows, width), BF16),
            shape((rows, width), BF16),
            shape((rows, 2 * width), BF16),
            shape((4 + taps, TILE, width)),
        ),
        in_specs=[VMEM] * len(args),
        out_specs=(VMEM,) * 5,
        scratch_shapes=[
            pltpu.VMEM((width // LANES, rows, LANES), F32),
            pltpu.VMEM((width // LANES, rows, LANES), F32),
            pltpu.VMEM((width // LANES, rows, LANES), F32),
            pltpu.VMEM((span, width), F32),
            pltpu.VMEM((seqs, span + TILE, width), F32),
            pltpu.VMEM((seqs, width), F32),
            pltpu.VMEM((devices, seqs, width), F32),
            pltpu.VMEM((seqs, TILE, width), F32),
            pltpu.VMEM((seqs, TILE, width), F32),
            dma((devices - 1,)),
            dma((devices - 1,)),
            dma((1,)),
            dma((1,)),
        ],
        compiler_params=params(1),
        cost_estimate=cost(50),
        name="recurrence_backward",
    )(*args)


def widen(array, width):
    short = width - array.shape[-1]
    if short == 0:
        return array
    return jnp.pad(array, [(0, 0)] * (array.ndim - 1) + [(0, short)])


def diagonal(gates, width):
    heads, size, _ = gates.shape
    spread = jnp.eye(heads, dtype=gates.dtype)[:, None, :, None] * gates[:, :, None, :]
    flat = spread.reshape(heads * size, heads * size)
    short = width - heads * size
    return jnp.pad(flat, ((0, short), (0, short))) if short else flat


def per_device(
    stream,
    norm_in,
    w_branch,
    w_input,
    conv_kernel,
    conv_bias,
    gate_r,
    bias_r,
    gate_i,
    bias_i,
    decay_param,
    w_out,
    norm_mlp,
    w_gate,
    w_up,
    w_down,
    state_init,
    conv_init,
    fresh_rows,
    out_grad,
):
    seqs, span, model = stream.shape
    channels = w_branch.shape[1]
    mlp_dev = w_gate.shape[1]
    heads, head_width = gate_r.shape[:2]
    taps = conv_kernel.shape[0]
    edge = taps - 1
    rows = seqs * span
    devices = lax.axis_size("seq")
    position = lax.axis_index("seq")
    width = -(-channels // 128) * 128

    keep = 1.0 - fresh_rows.astype(F32)
    flat_in = stream.reshape(rows, model)
    flat_grad = out_grad.reshape(rows, model)
    w_branch_p = widen(w_branch, width)
    w_input_p = widen(w_input, width)
    w_out_p = jnp.pad(w_out, ((0, width - channels), (0, 0))) if width > channels else w_out
    taps_p = widen(conv_kernel, width)
    rate = jax.nn.softplus(-decay_param)
    rate_p = jnp.pad(rate, (0, width - channels), constant_values=1.0)
    vec = jnp.stack([widen(conv_bias, width), rate_p])
    gates = jnp.concatenate([diagonal(gate_r, width), diagonal(gate_i, width)], axis=1)
    gates_t = jnp.concatenate(
        [
            diagonal(jnp.swapaxes(gate_r, 1, 2), width),
            diagonal(jnp.swapaxes(gate_i, 1, 2), width),
        ],
        axis=0,
    )
    gate_bias = jnp.concatenate([widen(bias_r, width), widen(bias_i, width)])[None]
    state0 = widen(state_init * keep[:, None], width)
    conv0 = jnp.pad(
        conv_init * keep[:, None, None], ((0, 0), (TILE - edge, 0), (0, width - channels))
    )

    normed, branch, padded, pre, hidden, mixed, carry, sums = recurrence_forward(
        span,
        flat_in,
        norm_in[None],
        w_branch_p,
        w_input_p,
        taps_p,
        vec,
        gates,
        gate_bias,
        state0,
        conv0,
    )
    normed_mlp, own = line_call(
        residual_kernel,
        2,
        (shape((rows, model), BF16), shape((rows // 2, model))),
        dot(mixed, w_out_p),
        flat_in,
        norm_mlp[None],
    )
    gate_val = dot(normed_mlp, w_gate)
    up_val = dot(normed_mlp, w_up)
    act, slope = gelu_both(gate_val)
    hidden_mlp = (act * up_val).astype(BF16)
    grad_low = flat_grad.astype(BF16)
    grad_hidden = matmul_back(grad_low, w_down)
    grad_gate = (grad_hidden * up_val * slope).astype(BF16)
    grad_up = (grad_hidden * act).astype(BF16)
    grad_part = matmul_back(grad_gate, w_gate) + matmul_back(grad_up, w_up)
    mlp_grads = weight_grads(
        (normed_mlp, grad_low), ((0, grad_gate), (0, grad_up), (1, hidden_mlp)), mlp_dev // 3
    )
    mlp_grads, grad_part = lax.optimization_barrier((mlp_grads, grad_part))
    mlp_grads = lax.psum_scatter(mlp_grads, "seq", scatter_dimension=0, tiled=True)
    resid_low, own_grad, norm_mlp_acc = line_call(
        mlp_norm_kernel,
        3,
        (shape((rows, model), BF16), shape((rows // 2, model)), shape((TILE, model))),
        grad_part,
        own,
        flat_grad,
        norm_mlp[None],
    )
    block_part = dot(hidden_mlp, w_down)
    grad_mixed = matmul_back(resid_low, w_out_p)
    grad_branch, input_low, heads_in, pre_low, acc = recurrence_backward(
        span,
        grad_mixed,
        branch,
        hidden,
        carry,
        pre,
        padded,
        sums,
        taps_p,
        vec,
        gates_t,
    )
    grad_part = matmul_back(grad_branch, w_branch_p) + matmul_back(input_low, w_input_p)
    rec_grads = weight_grads(
        (resid_low, normed), ((0, mixed), (1, grad_branch), (1, input_low)), width
    )
    gates_grad = lax.dot_general(heads_in, pre_low, CONTRACT_ROWS, preferred_element_type=F32)

    def blocks(array):
        return jnp.stack(
            [
                array[h * head_width : (h + 1) * head_width, h * head_width : (h + 1) * head_width]
                for h in range(heads)
            ]
        )

    def place(array):
        flat = array.reshape(-1)
        return jnp.pad(flat, (0, -flat.size % 1024)).reshape(-1, LANES)

    last = position == devices - 1
    last_hidden = hidden.reshape(-1, seqs, span, LANES)[:, :, -1]
    last_hidden = jnp.swapaxes(last_hidden, 0, 1).reshape(seqs, width)[:, :channels]
    final_state = jnp.where(last, last_hidden, 0.0)
    final_conv = jnp.where(last, padded[:, span + TILE - edge :, :channels], 0.0)
    pieces = (
        jnp.sum(norm_mlp_acc, 0),
        jnp.sum(acc, axis=1)[:, :channels],
        blocks(gates_grad[:, :width]),
        blocks(gates_grad[:, width:]),
        final_state,
        final_conv,
    )
    small = jnp.concatenate([place(piece) for piece in pieces], axis=0)
    small, rec_grads, grad_part, mlp_grads = lax.optimization_barrier(
        (small, rec_grads, grad_part, mlp_grads)
    )
    rec_grads = lax.psum_scatter(rec_grads, "seq", scatter_dimension=0, tiled=True)
    small = lax.psum(small, "seq")

    block_out, stream_grad, norm_in_grad = last_call(
        block_part,
        grad_part,
        own,
        own_grad,
        flat_in,
        norm_in[None],
    )

    summed = []
    begin = 0
    for piece in pieces:
        lines = -(-piece.size // 1024) * 8
        flat = small[begin : begin + lines].reshape(-1)
        summed.append(flat[: piece.size].reshape(piece.shape))
        begin += lines
    norm_mlp_grad, acc, gate_r_grad, gate_i_grad, final_state, final_conv = summed
    norm_mlp_grad = lax.psum(norm_mlp_grad, "mp")
    norm_in_grad = norm_in_grad[0]
    decay_grad = acc[0] * (RATE_SCALE * jax.nn.sigmoid(-decay_param))
    w_gate_grad = mlp_grads[:, :mlp_dev]
    w_up_grad = mlp_grads[:, mlp_dev : 2 * mlp_dev]
    w_down_grad = mlp_grads[:, 2 * mlp_dev :]
    w_out_grad = rec_grads[:, :width]
    w_branch_grad = rec_grads[:, width : 2 * width]
    w_input_grad = rec_grads[:, 2 * width :]
    return (
        block_out.reshape(stream.shape),
        stream_grad.reshape(stream.shape),
        norm_in_grad,
        w_branch_grad[:, :channels],
        w_input_grad[:, :channels],
        acc[4:],
        acc[3],
        gate_r_grad,
        acc[1],
        gate_i_grad,
        acc[2],
        decay_grad,
        w_out_grad[:, :channels].T,
        norm_mlp_grad,
        w_gate_grad,
        w_up_grad,
        w_down_grad.T,
        final_state,
        final_conv,
    )


def solution(mesh):
    seq_rows = P(None, "seq", None)
    columns = P(None, "mp")
    channel = P("mp")
    return jax.shard_map(
        per_device,
        mesh=mesh,
        in_specs=(
            seq_rows,
            P(),
            columns,
            columns,
            columns,
            channel,
            P("mp", None, None),
            channel,
            P("mp", None, None),
            channel,
            channel,
            P("mp", None),
            P(),
            columns,
            columns,
            P("mp", None),
            columns,
            P(None, None, "mp"),
            P(),
            seq_rows,
        ),
        out_specs=(
            seq_rows,
            seq_rows,
            P(),
            P("seq", "mp"),
            P("seq", "mp"),
            columns,
            channel,
            P("mp", None, None),
            channel,
            P("mp", None, None),
            channel,
            channel,
            P("mp", "seq"),
            P(),
            P("seq", "mp"),
            P("seq", "mp"),
            P("mp", "seq"),
            columns,
            P(None, None, "mp"),
        ),
        check_vma=False,
    )
```

```python
import functools

import jax
import jax.numpy as jnp
from jax import lax
from jax.experimental import pallas as pl
from jax.experimental.pallas import tpu as pltpu
from jax.sharding import PartitionSpec as P

MESH = pl.DeviceIdType.MESH
RATE_SCALE = 8.0
EPS = 1e-06
GELU_C = 0.7978845608028654
GELU_K = 0.044715
CONTRACT_ROWS = (((0,), (0,)), ((), ()))
CONTRACT_LAST = (((1,), (1,)), ((), ()))
TILE = 8
LANES = 128
ROWS = 32
CHUNK = 16
SKEW = 2
GROUP = 16
TURN = 256
F32 = jnp.float32
BF16 = jnp.bfloat16
VMEM = pl.BlockSpec(memory_space=pltpu.VMEM)
HBM = pl.BlockSpec(memory_space=pl.ANY)


def dot(a, b):
    return jnp.dot(a, b, preferred_element_type=F32)


def matmul_back(a, b):
    return lax.dot_general(a, b, CONTRACT_LAST, preferred_element_type=F32)


def block(i, size):
    return pl.ds(pl.multiple_of(i * size, size), size)


def gelu(x):
    t = jnp.tanh(GELU_C * (x + GELU_K * (x * x * x)))
    return 0.5 * x * (1.0 + t)


def gelu_both(x):
    x2 = x * x
    t = jnp.tanh(GELU_C * (x + GELU_K * (x2 * x)))
    half = 0.5 * (1.0 + t)
    slope = half + 0.5 * x * (1.0 - t * t) * (GELU_C * (1.0 + (3.0 * GELU_K) * x2))
    return x * half, slope


def one_minus_square(log_a, a):
    y = 2.0 * log_a
    s = 1.0 + y * (1.0 / 8.0)
    for k in (7, 6, 5, 4, 3, 2):
        s = 1.0 + (y * (1.0 / k)) * s
    return jnp.where(y > -0.35, -y * s, 1.0 - a * a)


def get(ref, at):
    return jnp.concatenate([ref[j, at, :] for j in range(ref.shape[0])], axis=-1)


def put(ref, at, value):
    for j in range(ref.shape[0]):
        ref[j, at, :] = value[:, j * LANES : (j + 1) * LANES]


def to_all(axis, src, slots, send, recv):
    size, me = lax.axis_size(axis), lax.axis_index(axis)
    return [
        pltpu.make_async_remote_copy(
            src_ref=src,
            dst_ref=slots.at[me],
            send_sem=send.at[d - 1],
            recv_sem=recv.at[d - 1],
            device_id={axis: lax.rem(me + d, size)},
            device_id_type=MESH,
        )
        for d in range(1, size)
    ]


def to_one(axis, distance, src, dst, send, recv):
    size, me = lax.axis_size(axis), lax.axis_index(axis)
    return pltpu.make_async_remote_copy(
        src_ref=src,
        dst_ref=dst,
        send_sem=send,
        recv_sem=recv,
        device_id={axis: lax.rem(me + distance + size, size)},
        device_id_type=MESH,
    )


def forward_kernel(
    span,
    x_ref,
    gain_ref,
    w_branch_ref,
    w_input_ref,
    taps_ref,
    vec_ref,
    gates_ref,
    gate_bias_ref,
    state0_ref,
    conv0_ref,
    normed_ref,
    branch_ref,
    pad_ref,
    pre_ref,
    hidden_ref,
    mixed_ref,
    carry_ref,
    sums_ref,
    a_ref,
    b_ref,
    conv_ref,
    tail_ref,
    tail_in,
    mine_ref,
    send1,
    recv1,
    send_t,
    recv_t,
):
    seqs = state0_ref.shape[0]
    width = taps_ref.shape[1]
    taps = taps_ref.shape[0]
    rows = seqs * span
    devices, me = lax.axis_size("seq"), lax.axis_index("seq")
    enter_all(("seq",))

    group = 2 * span

    @pl.loop(0, rows // group)
    def _(g):
        @pl.loop(0, group // ROWS)
        def _(q):
            at = block(g * (group // ROWS) + q, ROWS)
            x = x_ref[at, :]
            scale = lax.rsqrt(jnp.mean(x * x, axis=-1, keepdims=True) + EPS)
            normed_ref[at, :] = (x * scale * gain_ref[...]).astype(BF16)

        conv = dot(normed_ref[block(g, group), :], w_input_ref[...])
        for j in range(group // span):
            pad_ref[g * (group // span) + j, pl.ds(TILE, span), :] = conv[
                j * span : (j + 1) * span
            ]

    for s in range(seqs):
        tail_ref[s] = pad_ref[s, pl.ds(span, TILE), :]
    tail_copy = to_one("seq", 1, tail_ref, tail_in, send_t.at[0], recv_t.at[0])
    tail_copy.start()

    @pl.loop(0, rows // group)
    def _(g):
        branch_ref[block(g, group), :] = dot(normed_ref[block(g, group), :], w_branch_ref[...])

    tail_copy.wait()
    for s in range(seqs):
        pad_ref[s, pl.ds(0, TILE), :] = jnp.where(me == 0, conv0_ref[s], tail_in[s])

    def conv_rows(s, q):
        part = pad_ref[s, pl.ds(pl.multiple_of(q * ROWS, ROWS), ROWS + TILE), :]
        total = vec_ref[0:1, :]
        for k in range(taps):
            first = TILE - (taps - 1) + k
            total = total + taps_ref[k : k + 1, :] * part[first : first + ROWS]
        return total

    @pl.loop(0, seqs)
    def _(s):
        @pl.loop(0, span // ROWS)
        def _(q):
            conv_ref[block(q, ROWS), :] = conv_rows(s, q)

        pre_ref[block(s, span), :] = (
            dot(conv_ref[...].astype(BF16), gates_ref[...]) + gate_bias_ref[...]
        )

        @pl.loop(0, span // ROWS)
        def _(q):
            at = block(s * (span // ROWS) + q, ROWS)
            conv = conv_ref[block(q, ROWS), :]
            recall = jax.nn.sigmoid(pre_ref[at, :width])
            gate = jax.nn.sigmoid(pre_ref[at, width:])
            log_a = (-RATE_SCALE * vec_ref[1:2, :]) * recall
            a = jnp.exp(log_a)
            put(a_ref, at, a)
            put(b_ref, at, jnp.sqrt(one_minus_square(log_a, a)) * gate * conv)

    def at_time(ref, t):
        return get(ref, pl.ds(t, seqs, stride=span))

    def local(t, value):
        prod, state = value
        a = at_time(a_ref, t)
        return prod * a, a * state + at_time(b_ref, t)

    ones = jnp.ones((seqs, width), F32)
    prod, state = lax.fori_loop(0, span, local, (ones, jnp.zeros_like(ones)), unroll=8)
    mine_ref[0] = prod
    mine_ref[1] = state
    sums_ref[me] = mine_ref[...]
    copies = to_all("seq", mine_ref, sums_ref, send1, recv1)
    for copy in copies:
        copy.start()
    for copy in copies:
        copy.wait()

    def carry_step(j, carry):
        both = sums_ref[j]
        return jnp.where(j < me, both[0] * carry + both[1], carry)

    carry = lax.fori_loop(0, devices - 1, carry_step, state0_ref[...])
    carry_ref[...] = carry

    def final(t, state):
        state = at_time(a_ref, t) * state + at_time(b_ref, t)
        put(hidden_ref, pl.ds(t, seqs, stride=span), state)
        return state

    lax.fori_loop(0, span, final, carry, unroll=8)

    @pl.loop(0, rows // ROWS)
    def _(q):
        at = block(q, ROWS)
        mixed_ref[at, :] = (get(hidden_ref, at) * gelu(branch_ref[at, :])).astype(BF16)


def backward_kernel(
    span,
    grad_ref,
    branch_ref,
    hidden_ref,
    carry_ref,
    pre_ref,
    pad_ref,
    sums_ref,
    taps_ref,
    vec_ref,
    gates_t_ref,
    grad_branch_ref,
    input_ref,
    heads_ref,
    low_ref,
    acc_ref,
    a_ref,
    gd_ref,
    gs_ref,
    direct_ref,
    gpad_ref,
    mine_ref,
    entries_ref,
    head_ref,
    head_in,
    send1,
    recv1,
    send_t,
    recv_t,
):
    seqs, width = carry_ref.shape
    taps = taps_ref.shape[0]
    rows = seqs * span
    devices, me = lax.axis_size("seq"), lax.axis_index("seq")
    enter_all(("seq",))

    def decay(at):
        recall = jax.nn.sigmoid(pre_ref[at, :width])
        log_a = (-RATE_SCALE * vec_ref[1:2, :]) * recall
        return recall, log_a, jnp.exp(log_a)

    @pl.loop(0, rows // ROWS)
    def _(q):
        at = block(q, ROWS)
        put(a_ref, at, decay(at)[2])
        act, slope = gelu_both(branch_ref[at, :])
        grad = grad_ref[at, :]
        put(gd_ref, at, grad * act)
        grad_branch_ref[at, :] = (grad * get(hidden_ref, at) * slope).astype(BF16)

    def at_time(ref, t):
        return get(ref, pl.ds(t, seqs, stride=span))

    def local(k, through):
        t = span - 1 - k
        return at_time(a_ref, t) * (at_time(gd_ref, t) + through)

    zero = jnp.zeros((seqs, width), F32)
    mine_ref[...] = lax.fori_loop(0, span, local, zero, unroll=8)
    entries_ref[me] = mine_ref[...]
    copies = to_all("seq", mine_ref, entries_ref, send1, recv1)
    for copy in copies:
        copy.start()
    acc_ref[...] = jnp.zeros_like(acc_ref)
    for copy in copies:
        copy.wait()

    def back_step(k, through):
        j = devices - 1 - k
        return jnp.where(j > me, entries_ref[j] + sums_ref[j, 0] * through, through)

    incoming = lax.fori_loop(0, devices - 1, back_step, zero)

    def final(k, through):
        t = span - 1 - k
        grad = at_time(gd_ref, t) + through
        put(gs_ref, pl.ds(t, seqs, stride=span), grad)
        return at_time(a_ref, t) * grad

    lax.fori_loop(0, span, final, incoming, unroll=8)

    def add(k, value):
        total = value[0:TILE]
        for i in range(1, value.shape[0] // TILE):
            total = total + value[i * TILE : (i + 1) * TILE]
        acc_ref[k] += total

    @pl.loop(0, seqs)
    def _(s):
        @pl.loop(0, span // ROWS)
        def _(q):
            at = block(s * (span // ROWS) + q, ROWS)
            part = pad_ref[s, pl.ds(pl.multiple_of(q * ROWS, ROWS), ROWS + TILE), :]
            conv = vec_ref[0:1, :]
            for k in range(taps):
                first = TILE - (taps - 1) + k
                conv = conv + taps_ref[k : k + 1, :] * part[first : first + ROWS]
            heads_ref[at, :] = conv.astype(BF16)
            recall, log_a, a = decay(at)
            gate = jax.nn.sigmoid(pre_ref[at, width:])
            square = one_minus_square(log_a, a)
            inverse = lax.rsqrt(square)
            root = jnp.sqrt(square)
            grad = get(gs_ref, at)
            hidden = get(hidden_ref, at)
            before_at = pl.multiple_of(jnp.maximum(s * span + q * ROWS - TILE, 0), TILE)
            earlier = get(hidden_ref, pl.ds(before_at, TILE))
            first_row = jnp.where(q == 0, carry_ref[pl.ds(s, 1), :], earlier[TILE - 1 :])
            place = lax.broadcasted_iota(jnp.int32, (ROWS, width), 0)
            prev = jnp.where(place == 0, first_row, pltpu.roll(hidden, 1, 0))
            grad_log = grad * a * (prev - gate * conv * a * inverse)
            through = grad_log * recall
            pre_r = through * (1.0 - recall) * (-RATE_SCALE * vec_ref[1:2, :])
            direct = grad * root * gate
            pre_i = direct * conv * (1.0 - gate)
            low_ref[at, :width] = pre_r.astype(BF16)
            low_ref[at, width:] = pre_i.astype(BF16)
            direct_ref[block(q, ROWS), :] = direct
            add(0, through)
            add(1, pre_r)
            add(2, pre_i)

        whole = direct_ref[...] + dot(low_ref[block(s, span), :], gates_t_ref[...])
        gpad_ref[s, pl.ds(0, span), :] = whole
        head_ref[s] = whole[:TILE]

    head_copy = to_one("seq", -1, head_ref, head_in, send_t.at[0], recv_t.at[0])
    head_copy.start()

    @pl.loop(0, seqs)
    def _(s):
        @pl.loop(0, span // ROWS)
        def _(q):
            at = pl.multiple_of(q * ROWS, ROWS)
            part = pad_ref[s, pl.ds(at, ROWS + TILE), :]
            grad = gpad_ref[s, pl.ds(at, ROWS), :]
            add(3, grad)
            for k in range(taps):
                first = TILE - (taps - 1) + k
                add(4 + k, grad * part[first : first + ROWS])

    head_copy.wait()
    for s in range(seqs):
        gpad_ref[s, pl.ds(span, TILE), :] = jnp.where(me == devices - 1, 0.0, head_in[s])

    @pl.loop(0, seqs)
    def _(s):
        @pl.loop(0, span // ROWS)
        def _(q):
            part = gpad_ref[s, pl.ds(pl.multiple_of(q * ROWS, ROWS), ROWS + TILE), :]
            total = taps_ref[taps - 1 : taps, :] * part[0:ROWS]
            for k in range(taps - 1):
                first = taps - 1 - k
                total = total + taps_ref[k : k + 1, :] * part[first : first + ROWS]
            input_ref[block(s * (span // ROWS) + q, ROWS), :] = total.astype(BF16)


def line_sum(axis, total, period, part, inbox, out, sems, before, root, arrive, leave):
    send_up, send_down, recv_up, recv_down = sems
    n, z = lax.axis_size(axis), lax.axis_index(axis)
    depth = n // 2
    ring = out.shape[0]

    def root_of(c):
        return depth - 1 + lax.rem(c, 2)

    def up(c, step, side):
        slot = lax.rem(c, ring)
        return pltpu.make_async_remote_copy(
            src_ref=part.at[block(lax.rem(c, period), CHUNK)],
            dst_ref=inbox.at[side, slot],
            send_sem=send_up.at[slot],
            recv_sem=recv_up.at[side, slot],
            device_id={axis: z + step},
            device_id_type=MESH,
        )

    def down(c, step, side):
        slot = lax.rem(c, ring)
        return pltpu.make_async_remote_copy(
            src_ref=out.at[slot],
            dst_ref=out.at[slot],
            send_sem=send_down.at[side, slot],
            recv_sem=recv_down.at[slot],
            device_id={axis: z + step},
            device_id_type=MESH,
        )

    inner = jnp.logical_and(z > 0, z < n - 1)

    @pl.loop(0, total + ring)
    def _(k):
        @pl.when(k >= ring)
        def _():
            c = k - ring
            r = root_of(c)
            step = jnp.where(z < r, 1, -1)
            side = jnp.where(z < r, 0, 1)

            @pl.when(z == r)
            def _():
                down(c, -1, 0).wait_send()
                down(c, 1, 1).wait_send()

            @pl.when(z != r)
            def _():
                up(c, step, side).wait_send()

            @pl.when(jnp.logical_and(z != r, inner))
            def _():
                down(c, -step, side).wait_send()

            leave(c, lax.rem(c, ring))

        before(k)

        for i in reversed(range(n + 1)):
            c = k - SKEW * i
            valid = jnp.logical_and(c >= 0, c < total)
            c = jnp.clip(c, 0, total - 1)
            at = block(lax.rem(c, period), CHUNK)
            slot = lax.rem(c, ring)
            r = root_of(c)
            step = jnp.where(z < r, 1, -1)
            side = jnp.where(z < r, 0, 1)
            if i > depth:
                here = jnp.logical_and(z != r, jnp.abs(z - r) == i - depth)

                @pl.when(jnp.logical_and(valid, here))
                def _():
                    down(c, -step, side).wait_recv()

                    @pl.when(inner)
                    def _():
                        down(c, -step, side).start()

                    arrive(c, slot)
            elif i == depth:

                @pl.when(jnp.logical_and(valid, z == r))
                def _():
                    up(c, 1, 0).wait_recv()
                    up(c, -1, 1).wait_recv()
                    root(c, slot, part[at, :] + inbox[0, slot] + inbox[1, slot])
                    down(c, -1, 0).start()
                    down(c, 1, 1).start()
                    arrive(c, slot)
            else:
                here = jnp.where(z < r, z, n - 1 - z) == i

                @pl.when(jnp.logical_and(valid, jnp.logical_and(z != r, here)))
                def _():
                    if i > 0:
                        up(c, step, side).wait_recv()
                        part[at, :] += inbox[side, slot]
                    up(c, step, side).start()


def ring_size(axis):
    return 2 * SKEW * lax.axis_size(axis)


def line_scratch(axis, rows, model):
    dma = pltpu.SemaphoreType.DMA
    ring = ring_size(axis)
    return [
        pltpu.VMEM((rows, model), F32),
        pltpu.VMEM((2, ring, CHUNK, model), F32),
        pltpu.VMEM((ring, CHUNK, model), F32),
        dma((ring,)),
        dma((2, ring)),
        dma((2, ring)),
        dma((ring,)),
    ]


def mean_square(x):
    return lax.rsqrt(jnp.mean(x * x, axis=-1, keepdims=True) + EPS)


def nothing(*_):
    pass


def fold(value):
    total = value[0:TILE]
    for i in range(1, value.shape[0] // TILE):
        total = total + value[i * TILE : (i + 1) * TILE]
    return total


def norm_grad(value, gain, grad, acc_ref):
    q = mean_square(value)
    e = gain * grad
    acc_ref[...] += fold(grad * value * q)
    return q * e - value * (q * q * q) * jnp.mean(e * value, axis=-1, keepdims=True)


def middle_kernel(
    mixed_in,
    w_out_in,
    x_in,
    og_in,
    gain_ref,
    w_gate_in,
    w_up_in,
    w_down_in,
    normed_out,
    hidden_out,
    gate_out,
    up_out,
    glow_out,
    block_out,
    low_out,
    own_grad_out,
    own_ref,
    acc_ref,
    part,
    inbox,
    out,
    send_up,
    send_down,
    recv_up,
    recv_down,
    mixed,
    w_out,
    w_gate,
    w_up,
    w_down,
    normed,
    rows_ref,
    og_ref,
    glow,
    gate_val,
    up_val,
    grad_hidden,
    hidden,
    grad_gate,
    grad_up,
    block_part,
    low,
    weight_sem,
    row_sem,
    og_sem,
    act_sem,
    low_sem,
    own_sem,
):
    n, z = lax.axis_size("mp"), lax.axis_index("mp")
    count = part.shape[0] // CHUNK
    size = GROUP * CHUNK
    groups = count // GROUP
    ring = out.shape[0]
    sems = (send_up, send_down, recv_up, recv_down)
    local = pltpu.make_async_copy

    loads = [
        local(source, target, weight_sem.at[i])
        for i, (source, target) in enumerate(
            (
                (mixed_in, mixed),
                (w_out_in, w_out),
                (w_gate_in, w_gate),
                (w_up_in, w_up),
                (w_down_in, w_down),
            )
        )
    ]
    for copy in loads:
        copy.start()

    def og_load(g):
        return local(og_in.at[block(g, size)], og_ref, og_sem.at[0])

    og_load(0).start()
    enter_all(("mp",))
    acc_ref[...] = jnp.zeros_like(acc_ref)
    loads[0].wait()
    loads[1].wait()

    def is_root(c):
        return z == n // 2 - 1 + lax.rem(c, 2)

    def row_load(source, c):
        slot = lax.rem(c, ring)
        at = block(lax.rem(c, count), CHUNK)
        return local(source.at[at], rows_ref.at[slot], row_sem.at[slot])

    acts = (
        (normed, normed_out),
        (glow, glow_out),
        (hidden, hidden_out),
        (grad_gate, gate_out),
        (grad_up, up_out),
        (block_part, block_out),
    )

    def act_store(i, g):
        source, target = acts[i]
        source = source.at[lax.rem(g, 2)] if i == 0 else source
        return local(source, target.at[block(g, size)], act_sem.at[i])

    def at_tick(k, first, work):
        g = (k - first) // GROUP

        @pl.when(
            jnp.logical_and(
                jnp.logical_and(k >= first, k < first + GROUP * groups),
                lax.rem(k - first, GROUP) == 0,
            )
        )
        def _():
            work(g)

    def project(g):
        part[block(g, size), :] = dot(mixed[block(g, size), :], w_out[...])

    def piece_gate(g):
        @pl.when(g == 0)
        def _():
            for copy in loads[2:]:
                copy.wait()

        gate_val[...] = dot(normed[lax.rem(g, 2)], w_gate[...])
        act_store(0, g).start()

    def piece_up(g):
        up_val[...] = dot(normed[lax.rem(g, 2)], w_up[...])

        @pl.when(g > 0)
        def _():
            for i in range(1, 6):
                act_store(i, g - 1).wait()

    def piece_low(g):
        og_load(g).wait()

        @pl.loop(0, size // ROWS)
        def _(q):
            glow[block(q, ROWS), :] = og_ref[block(q, ROWS), :].astype(BF16)

        @pl.when(g + 1 < groups)
        def _():
            og_load(g + 1).start()

        act_store(1, g).start()

    def piece_hidden(g):
        grad_hidden[...] = matmul_back(glow[...], w_down[...])

    def piece_act(g):
        @pl.loop(0, size // CHUNK)
        def _(q):
            at = block(q, CHUNK)
            up = up_val[at, :]
            grad = grad_hidden[at, :]
            act, slope = gelu_both(gate_val[at, :])
            hidden[at, :] = (act * up).astype(BF16)
            grad_gate[at, :] = (grad * up * slope).astype(BF16)
            grad_up[at, :] = (grad * act).astype(BF16)

        for i in range(2, 5):
            act_store(i, g).start()

    def piece_down(g):
        block_part[...] = dot(hidden[...], w_down[...])
        act_store(5, g).start()
        act_store(0, g).wait()

    def piece_back_gate(g):
        part[block(g, size), :] = matmul_back(grad_gate[...], w_gate[...])

    def piece_back_up(g):
        part[block(g, size), :] += matmul_back(grad_up[...], w_up[...])

    first = GROUP + SKEW * n

    def before(k):
        @pl.when(jnp.logical_and(k < count, is_root(k)))
        def _():
            row_load(x_in, k).start()

        @pl.when(
            jnp.logical_and(jnp.logical_and(k >= count, k < 2 * count), is_root(k))
        )
        def _():
            row_load(og_in, k).start()

        at_tick(k, 0, project)
        at_tick(k, first, piece_gate)
        at_tick(k, first + 1, piece_up)
        at_tick(k, first + 2, piece_low)
        at_tick(k, first + 3, piece_hidden)
        at_tick(k, first + 4, piece_act)
        at_tick(k, first + 6, piece_down)
        at_tick(k, GROUP + ring, piece_back_gate)
        at_tick(k, GROUP + ring + 2, piece_back_up)

    def root(c, slot, total):
        j = lax.rem(c, count)
        mine = block(j // 2, CHUNK)
        row_load(x_in, c).wait()

        @pl.when(c < count)
        def _():
            value = rows_ref[slot] + total
            own_ref[mine, :] = value
            out[slot] = (value * mean_square(value) * gain_ref[...]).astype(BF16).astype(F32)

        @pl.when(c >= count)
        def _():
            back = norm_grad(own_ref[mine, :], gain_ref[...], total, acc_ref)
            out[slot] = rows_ref[slot] + back

    def low_store(c, slot):
        at = block(lax.rem(c, count), CHUNK)
        return local(low.at[slot], low_out.at[at], low_sem.at[slot])

    def own_store(c, slot):
        at = block(lax.rem(c, count) // 2, CHUNK)
        return local(out.at[slot], own_grad_out.at[at], own_sem.at[slot])

    def arrive(c, slot):
        @pl.when(c < count)
        def _():
            normed[lax.rem(c // GROUP, 2), block(lax.rem(c, GROUP), CHUNK), :] = out[slot].astype(BF16)

        @pl.when(c >= count)
        def _():
            low[slot] = out[slot].astype(BF16)
            low_store(c, slot).start()

            @pl.when(is_root(c))
            def _():
                own_store(c, slot).start()

    def leave(c, slot):
        @pl.when(c >= count)
        def _():
            low_store(c, slot).wait()

            @pl.when(is_root(c))
            def _():
                own_store(c, slot).wait()

    line_sum("mp", 2 * count, count, part, inbox, out, sems, before, root, arrive, leave)

    for i in range(1, 6):
        act_store(i, groups - 1).wait()


def middle_call(*args):
    mixed, w_out, x, og, gain, w_gate, w_up, w_down = args
    rows, model = x.shape
    width, hidden = mixed.shape[1], w_gate.shape[1]
    size = GROUP * CHUNK
    dma = pltpu.SemaphoreType.DMA
    ring = ring_size("mp")
    act = shape((rows, hidden), BF16)
    tall = shape((rows, model), BF16)
    return pl.pallas_call(
        middle_kernel,
        out_shape=(
            tall,
            act,
            act,
            act,
            tall,
            shape((rows, model)),
            tall,
            shape((rows // 2, model)),
            shape((rows // 2, model)),
            shape((TILE, model)),
        ),
        in_specs=[HBM] * 4 + [VMEM] + [HBM] * 3,
        out_specs=(HBM,) * 8 + (VMEM,) * 2,
        scratch_shapes=line_scratch("mp", rows, model)
        + [
            pltpu.VMEM((rows, width), BF16),
            pltpu.VMEM((width, model), BF16),
            pltpu.VMEM((model, hidden), BF16),
            pltpu.VMEM((model, hidden), BF16),
            pltpu.VMEM((hidden, model), BF16),
            pltpu.VMEM((2, size, model), BF16),
            pltpu.VMEM((ring, CHUNK, model), F32),
            pltpu.VMEM((size, model), F32),
            pltpu.VMEM((size, model), BF16),
            pltpu.VMEM((size, hidden), F32),
            pltpu.VMEM((size, hidden), F32),
            pltpu.VMEM((size, hidden), F32),
            pltpu.VMEM((size, hidden), BF16),
            pltpu.VMEM((size, hidden), BF16),
            pltpu.VMEM((size, hidden), BF16),
            pltpu.VMEM((size, model), F32),
            pltpu.VMEM((ring, CHUNK, model), BF16),
            dma((5,)),
            dma((ring,)),
            dma((1,)),
            dma((6,)),
            dma((ring,)),
            dma((ring,)),
        ],
        compiler_params=params(2, 63),
        cost_estimate=cost(400),
        name="middle",
    )(*args)


def last_kernel(
    block_part,
    grad_part,
    own_ref,
    own_grad_ref,
    x_ref,
    gain_ref,
    other_acc,
    block_ref,
    grad_ref,
    norm_ref,
    part,
    inbox,
    out,
    send_up,
    send_down,
    recv_up,
    recv_down,
    load_sem,
    store_sem,
    acc_ref,
    mine_ref,
    seq_in,
    mp_in,
    send_s,
    recv_s,
    send_m,
    recv_m,
):
    count = part.shape[0] // CHUNK
    group = GROUP * CHUNK
    groups = count // GROUP
    sems = (send_up, send_down, recv_up, recv_down)
    enter_all(("seq", "mp"))
    acc_ref[...] = jnp.zeros_like(acc_ref)
    mine_ref[...] = jnp.zeros_like(mine_ref)

    def load(source, g):
        at = block(lax.rem(g, groups), group)
        return pltpu.make_async_copy(source.at[at], part.at[at], load_sem.at[lax.rem(g, 2)])

    def start_load(g):
        @pl.when(g < groups)
        def _():
            load(block_part, g).start()

        @pl.when(jnp.logical_and(g >= groups, g < 2 * groups))
        def _():
            load(grad_part, g).start()

    start_load(jnp.int32(0))

    def before(k):
        @pl.when(jnp.logical_and(lax.rem(k, GROUP) == 0, k < 2 * count))
        def _():
            g = k // GROUP
            load(block_part, g).wait()
            start_load(g + 1)

    def root(c, slot, total):
        j = lax.rem(c, count)
        mine = block(j // 2, CHUNK)

        @pl.when(c < count)
        def _():
            out[slot] = own_ref[mine, :] + total

        @pl.when(c >= count)
        def _():
            back = norm_grad(x_ref[block(j, CHUNK), :], gain_ref[...], total, acc_ref)
            out[slot] = own_grad_ref[mine, :] + back

    def store(target, c, slot):
        at = block(lax.rem(c, count), CHUNK)
        return pltpu.make_async_copy(out.at[slot], target.at[at], store_sem.at[slot])

    def arrive(c, slot):
        @pl.when(c < count)
        def _():
            store(block_ref, c, slot).start()

        @pl.when(c >= count)
        def _():
            store(grad_ref, c, slot).start()

    def leave(c, slot):
        store(block_ref, c, slot).wait()

    line_sum("mp", 2 * count, count, part, inbox, out, sems, before, root, arrive, leave)

    mine_ref[0, 0:1, :] = jnp.sum(acc_ref[...], axis=0, keepdims=True)
    mine_ref[0, 1:2, :] = jnp.sum(other_acc[...], axis=0, keepdims=True)
    for i, (axis, place, send, recv) in enumerate(
        (("seq", seq_in, send_s, recv_s), ("mp", mp_in, send_m, recv_m))
    ):
        if i == 1:
            mine_ref[1] = jnp.sum(seq_in[...], axis=0)
        place[lax.axis_index(axis)] = mine_ref[i]
        copies = to_all(axis, mine_ref.at[i], place, send, recv)
        for copy in copies:
            copy.start()
        for copy in copies:
            copy.wait()
    norm_ref[...] = jnp.sum(mp_in[...], axis=0)


def enter_all(axes):
    barrier = pltpu.get_barrier_semaphore()
    count = 0
    for axis in axes:
        size, me = lax.axis_size(axis), lax.axis_index(axis)
        for d in range(1, size):
            pl.semaphore_signal(
                barrier, 1, device_id={axis: lax.rem(me + d, size)}, device_id_type=MESH
            )
        count += size - 1
    pl.semaphore_wait(barrier, count)


def cost(micros):
    return pl.CostEstimate(flops=int(micros * 1e9), bytes_accessed=1 << 20, transcendentals=0)


def last_call(*args):
    rows, model = args[0].shape
    dma = pltpu.SemaphoreType.DMA
    nseq, nmp = lax.axis_size("seq"), lax.axis_size("mp")
    return pl.pallas_call(
        last_kernel,
        out_shape=(shape((rows, model)), shape((rows, model)), shape((TILE, model))),
        in_specs=[HBM, HBM] + [VMEM] * 5,
        out_specs=(HBM, HBM, VMEM),
        scratch_shapes=line_scratch("mp", rows, model)
        + [
            dma((2,)),
            dma((ring_size("mp"),)),
            pltpu.VMEM((TILE, model), F32),
            pltpu.VMEM((2, TILE, model), F32),
            pltpu.VMEM((nseq, TILE, model), F32),
            pltpu.VMEM((nmp, TILE, model), F32),
            dma((nseq - 1,)),
            dma((nseq - 1,)),
            dma((nmp - 1,)),
            dma((nmp - 1,)),
        ],
        compiler_params=params(4, 60),
        cost_estimate=cost(380),
        name="last_sums",
    )(*args)


def weight_kernel(plan, lefts, *refs):
    left_refs, right_refs = refs[:lefts], refs[lefts:-2]
    out_ref, turned = refs[-2:]
    j = pl.program_id(0)
    begin = 0
    held = None
    for (left, blocks), right in zip(plan, right_refs):
        if left != held:
            held = left

            @pl.when(j == begin)
            def _():
                rows = left_refs[left].shape[0]
                for i in range(left_refs[left].shape[1] // TURN):
                    at = slice(i * TURN, (i + 1) * TURN)
                    turned[at, :] = left_refs[left][:, at].T

        @pl.when(jnp.logical_and(j >= begin, j < begin + blocks))
        def _():
            size = turned.shape[0] // 4

            @pl.loop(0, 4)
            def _(i):
                out_ref[block(i, size), :] = dot(turned[block(i, size), :], right[...])

        begin += blocks


def weight_grads(lefts, pairs, width):
    rows, model = lefts[0].shape
    plan = tuple((left, right.shape[1] // width) for left, right in pairs)
    steps = sum(blocks for _, blocks in plan)
    whole = pl.BlockSpec((rows, model), lambda j: (0, 0))
    specs = [whole] * len(lefts)
    begin = 0
    for _, blocks in plan:
        specs.append(
            pl.BlockSpec(
                (rows, width),
                lambda j, first=begin, n=blocks: (0, jnp.clip(j - first, 0, n - 1)),
            )
        )
        begin += blocks
    return pl.pallas_call(
        functools.partial(weight_kernel, plan, len(lefts)),
        out_shape=shape((model, steps * width)),
        grid=(steps,),
        in_specs=specs,
        out_specs=pl.BlockSpec((model, width), lambda j: (0, j)),
        scratch_shapes=[pltpu.VMEM((model, rows), BF16)],
        compiler_params=pltpu.CompilerParams(vmem_limit_bytes=60 << 20),
        cost_estimate=cost(30),
        name="weight_grads",
    )(*lefts, *(right for _, right in pairs))


def params(collective, megabytes=60):
    return pltpu.CompilerParams(
        collective_id=collective, has_side_effects=True, vmem_limit_bytes=megabytes << 20
    )


def shape(dims, dtype=F32):
    return jax.ShapeDtypeStruct(dims, dtype)


def recurrence_forward(span, *args):
    x, _, w_branch = args[:3]
    state0 = args[8]
    rows, model = x.shape
    seqs, width = state0.shape
    devices = lax.axis_size("seq")
    dma = pltpu.SemaphoreType.DMA
    return pl.pallas_call(
        functools.partial(forward_kernel, span),
        out_shape=(
            shape((rows, model), BF16),
            shape((rows, width)),
            shape((seqs, span + TILE, width)),
            shape((rows, 2 * width)),
            shape((width // LANES, rows, LANES)),
            shape((rows, width), BF16),
            shape((seqs, width)),
            shape((devices, 2, seqs, width)),
        ),
        in_specs=[VMEM] * len(args),
        out_specs=(VMEM,) * 8,
        scratch_shapes=[
            pltpu.VMEM((width // LANES, rows, LANES), F32),
            pltpu.VMEM((width // LANES, rows, LANES), F32),
            pltpu.VMEM((span, width), F32),
            pltpu.VMEM((seqs, TILE, width), F32),
            pltpu.VMEM((seqs, TILE, width), F32),
            pltpu.VMEM((2, seqs, width), F32),
            dma((devices - 1,)),
            dma((devices - 1,)),
            dma((1,)),
            dma((1,)),
        ],
        compiler_params=params(0),
        cost_estimate=cost(50),
        name="recurrence_forward",
    )(*args)


def recurrence_backward(span, *args):
    rows, width = args[0].shape
    seqs = args[3].shape[0]
    taps = args[7].shape[0]
    devices = lax.axis_size("seq")
    dma = pltpu.SemaphoreType.DMA
    return pl.pallas_call(
        functools.partial(backward_kernel, span),
        out_shape=(
            shape((rows, width), BF16),
            shape((rows, width), BF16),
            shape((rows, width), BF16),
            shape((rows, 2 * width), BF16),
            shape((4 + taps, TILE, width)),
        ),
        in_specs=[VMEM] * len(args),
        out_specs=(VMEM,) * 5,
        scratch_shapes=[
            pltpu.VMEM((width // LANES, rows, LANES), F32),
            pltpu.VMEM((width // LANES, rows, LANES), F32),
            pltpu.VMEM((width // LANES, rows, LANES), F32),
            pltpu.VMEM((span, width), F32),
            pltpu.VMEM((seqs, span + TILE, width), F32),
            pltpu.VMEM((seqs, width), F32),
            pltpu.VMEM((devices, seqs, width), F32),
            pltpu.VMEM((seqs, TILE, width), F32),
            pltpu.VMEM((seqs, TILE, width), F32),
            dma((devices - 1,)),
            dma((devices - 1,)),
            dma((1,)),
            dma((1,)),
        ],
        compiler_params=params(1),
        cost_estimate=cost(50),
        name="recurrence_backward",
    )(*args)


def widen(array, width):
    short = width - array.shape[-1]
    if short == 0:
        return array
    return jnp.pad(array, [(0, 0)] * (array.ndim - 1) + [(0, short)])


def diagonal(gates, width):
    heads, size, _ = gates.shape
    spread = jnp.eye(heads, dtype=gates.dtype)[:, None, :, None] * gates[:, :, None, :]
    flat = spread.reshape(heads * size, heads * size)
    short = width - heads * size
    return jnp.pad(flat, ((0, short), (0, short))) if short else flat


def per_device(
    stream,
    norm_in,
    w_branch,
    w_input,
    conv_kernel,
    conv_bias,
    gate_r,
    bias_r,
    gate_i,
    bias_i,
    decay_param,
    w_out,
    norm_mlp,
    w_gate,
    w_up,
    w_down,
    state_init,
    conv_init,
    fresh_rows,
    out_grad,
):
    seqs, span, model = stream.shape
    channels = w_branch.shape[1]
    mlp_dev = w_gate.shape[1]
    heads, head_width = gate_r.shape[:2]
    taps = conv_kernel.shape[0]
    edge = taps - 1
    rows = seqs * span
    devices = lax.axis_size("seq")
    position = lax.axis_index("seq")
    width = -(-channels // 128) * 128

    keep = 1.0 - fresh_rows.astype(F32)
    flat_in = stream.reshape(rows, model)
    flat_grad = out_grad.reshape(rows, model)
    w_branch_p = widen(w_branch, width)
    w_input_p = widen(w_input, width)
    w_out_p = jnp.pad(w_out, ((0, width - channels), (0, 0))) if width > channels else w_out
    taps_p = widen(conv_kernel, width)
    rate = jax.nn.softplus(-decay_param)
    rate_p = jnp.pad(rate, (0, width - channels), constant_values=1.0)
    vec = jnp.stack([widen(conv_bias, width), rate_p])
    gates = jnp.concatenate([diagonal(gate_r, width), diagonal(gate_i, width)], axis=1)
    gates_t = jnp.concatenate(
        [
            diagonal(jnp.swapaxes(gate_r, 1, 2), width),
            diagonal(jnp.swapaxes(gate_i, 1, 2), width),
        ],
        axis=0,
    )
    gate_bias = jnp.concatenate([widen(bias_r, width), widen(bias_i, width)])[None]
    state0 = widen(state_init * keep[:, None], width)
    conv0 = jnp.pad(
        conv_init * keep[:, None, None], ((0, 0), (TILE - edge, 0), (0, width - channels))
    )

    normed, branch, padded, pre, hidden, mixed, carry, sums = recurrence_forward(
        span,
        flat_in,
        norm_in[None],
        w_branch_p,
        w_input_p,
        taps_p,
        vec,
        gates,
        gate_bias,
        state0,
        conv0,
    )
    (
        normed_mlp,
        hidden_mlp,
        grad_gate,
        grad_up,
        grad_low,
        block_part,
        resid_low,
        own_grad,
        own,
        norm_mlp_acc,
    ) = middle_call(mixed, w_out_p, flat_in, flat_grad, norm_mlp[None], w_gate, w_up, w_down)
    mlp_grads = weight_grads(
        (normed_mlp, grad_low), ((0, grad_gate), (0, grad_up), (1, hidden_mlp)), mlp_dev // 3
    )
    mlp_grads, resid_low = lax.optimization_barrier((mlp_grads, resid_low))
    mlp_grads = lax.psum_scatter(mlp_grads, "seq", scatter_dimension=0, tiled=True)
    grad_mixed = matmul_back(resid_low, w_out_p)
    grad_branch, input_low, heads_in, pre_low, acc = recurrence_backward(
        span,
        grad_mixed,
        branch,
        hidden,
        carry,
        pre,
        padded,
        sums,
        taps_p,
        vec,
        gates_t,
    )
    grad_part = matmul_back(grad_branch, w_branch_p) + matmul_back(input_low, w_input_p)
    rec_grads = weight_grads(
        (resid_low, normed), ((0, mixed), (1, grad_branch), (1, input_low)), width
    )
    gates_grad = lax.dot_general(heads_in, pre_low, CONTRACT_ROWS, preferred_element_type=F32)

    def blocks(array):
        return jnp.stack(
            [
                array[h * head_width : (h + 1) * head_width, h * head_width : (h + 1) * head_width]
                for h in range(heads)
            ]
        )

    def place(array):
        flat = array.reshape(-1)
        return jnp.pad(flat, (0, -flat.size % 1024)).reshape(-1, LANES)

    last = position == devices - 1
    last_hidden = hidden.reshape(-1, seqs, span, LANES)[:, :, -1]
    last_hidden = jnp.swapaxes(last_hidden, 0, 1).reshape(seqs, width)[:, :channels]
    final_state = jnp.where(last, last_hidden, 0.0)
    final_conv = jnp.where(last, padded[:, span + TILE - edge :, :channels], 0.0)
    pieces = (
        jnp.sum(acc, axis=1)[:, :channels],
        blocks(gates_grad[:, :width]),
        blocks(gates_grad[:, width:]),
        final_state,
        final_conv,
    )
    small = jnp.concatenate([place(piece) for piece in pieces], axis=0)
    small, rec_grads, grad_part, mlp_grads = lax.optimization_barrier(
        (small, rec_grads, grad_part, mlp_grads)
    )
    rec_grads = lax.psum_scatter(rec_grads, "seq", scatter_dimension=0, tiled=True)
    small = lax.psum(small, "seq")

    block_out, stream_grad, norm_grads = last_call(
        block_part,
        grad_part,
        own,
        own_grad,
        flat_in,
        norm_in[None],
        norm_mlp_acc,
    )

    summed = []
    begin = 0
    for piece in pieces:
        lines = -(-piece.size // 1024) * 8
        flat = small[begin : begin + lines].reshape(-1)
        summed.append(flat[: piece.size].reshape(piece.shape))
        begin += lines
    acc, gate_r_grad, gate_i_grad, final_state, final_conv = summed
    norm_in_grad = norm_grads[0]
    norm_mlp_grad = norm_grads[1]
    decay_grad = acc[0] * (RATE_SCALE * jax.nn.sigmoid(-decay_param))
    w_gate_grad = mlp_grads[:, :mlp_dev]
    w_up_grad = mlp_grads[:, mlp_dev : 2 * mlp_dev]
    w_down_grad = mlp_grads[:, 2 * mlp_dev :]
    w_out_grad = rec_grads[:, :width]
    w_branch_grad = rec_grads[:, width : 2 * width]
    w_input_grad = rec_grads[:, 2 * width :]
    return (
        block_out.reshape(stream.shape),
        stream_grad.reshape(stream.shape),
        norm_in_grad,
        w_branch_grad[:, :channels],
        w_input_grad[:, :channels],
        acc[4:],
        acc[3],
        gate_r_grad,
        acc[1],
        gate_i_grad,
        acc[2],
        decay_grad,
        w_out_grad[:, :channels].T,
        norm_mlp_grad,
        w_gate_grad,
        w_up_grad,
        w_down_grad.T,
        final_state,
        final_conv,
    )


def solution(mesh):
    seq_rows = P(None, "seq", None)
    columns = P(None, "mp")
    channel = P("mp")
    return jax.shard_map(
        per_device,
        mesh=mesh,
        in_specs=(
            seq_rows,
            P(),
            columns,
            columns,
            columns,
            channel,
            P("mp", None, None),
            channel,
            P("mp", None, None),
            channel,
            channel,
            P("mp", None),
            P(),
            columns,
            columns,
            P("mp", None),
            columns,
            P(None, None, "mp"),
            P(),
            seq_rows,
        ),
        out_specs=(
            seq_rows,
            seq_rows,
            P(),
            P("seq", "mp"),
            P("seq", "mp"),
            columns,
            channel,
            P("mp", None, None),
            channel,
            P("mp", None, None),
            channel,
            channel,
            P("mp", "seq"),
            P(),
            P("seq", "mp"),
            P("seq", "mp"),
            P("mp", "seq"),
            columns,
            P(None, None, "mp"),
        ),
        check_vma=False,
    )
```

```python
import functools

import jax
import jax.numpy as jnp
from jax import lax
from jax.experimental import pallas as pl
from jax.experimental.pallas import tpu as pltpu
from jax.sharding import PartitionSpec as P

MESH = pl.DeviceIdType.MESH
RATE_SCALE = 8.0
EPS = 1e-06
GELU_C = 0.7978845608028654
GELU_K = 0.044715
CONTRACT_ROWS = (((0,), (0,)), ((), ()))
CONTRACT_LAST = (((1,), (1,)), ((), ()))
TILE = 8
LANES = 128
ROWS = 32
CHUNK = 16
SKEW = 3
GROUP = 16
TURN = 256
F32 = jnp.float32
BF16 = jnp.bfloat16
VMEM = pl.BlockSpec(memory_space=pltpu.VMEM)
HBM = pl.BlockSpec(memory_space=pl.ANY)


def dot(a, b):
    return jnp.dot(a, b, preferred_element_type=F32)


def matmul_back(a, b):
    return lax.dot_general(a, b, CONTRACT_LAST, preferred_element_type=F32)


def block(i, size):
    return pl.ds(pl.multiple_of(i * size, size), size)


def gelu(x):
    t = jnp.tanh(GELU_C * (x + GELU_K * (x * x * x)))
    return 0.5 * x * (1.0 + t)


def gelu_both(x):
    x2 = x * x
    t = jnp.tanh(GELU_C * (x + GELU_K * (x2 * x)))
    half = 0.5 * (1.0 + t)
    slope = half + 0.5 * x * (1.0 - t * t) * (GELU_C * (1.0 + (3.0 * GELU_K) * x2))
    return x * half, slope


def one_minus_square(log_a, a):
    y = 2.0 * log_a
    s = 1.0 + y * (1.0 / 8.0)
    for k in (7, 6, 5, 4, 3, 2):
        s = 1.0 + (y * (1.0 / k)) * s
    return jnp.where(y > -0.35, -y * s, 1.0 - a * a)


def get(ref, at):
    return jnp.concatenate([ref[j, at, :] for j in range(ref.shape[0])], axis=-1)


def put(ref, at, value):
    for j in range(ref.shape[0]):
        ref[j, at, :] = value[:, j * LANES : (j + 1) * LANES]


def to_all(axis, src, slots, send, recv):
    size, me = lax.axis_size(axis), lax.axis_index(axis)
    return [
        pltpu.make_async_remote_copy(
            src_ref=src,
            dst_ref=slots.at[me],
            send_sem=send.at[d - 1],
            recv_sem=recv.at[d - 1],
            device_id={axis: lax.rem(me + d, size)},
            device_id_type=MESH,
        )
        for d in range(1, size)
    ]


def to_one(axis, distance, src, dst, send, recv):
    size, me = lax.axis_size(axis), lax.axis_index(axis)
    return pltpu.make_async_remote_copy(
        src_ref=src,
        dst_ref=dst,
        send_sem=send,
        recv_sem=recv,
        device_id={axis: lax.rem(me + distance + size, size)},
        device_id_type=MESH,
    )


def forward_kernel(
    span,
    x_ref,
    gain_ref,
    w_branch_ref,
    w_input_ref,
    taps_ref,
    vec_ref,
    gates_ref,
    gate_bias_ref,
    state0_ref,
    conv0_ref,
    normed_ref,
    branch_ref,
    pad_ref,
    pre_ref,
    hidden_ref,
    mixed_ref,
    carry_ref,
    sums_ref,
    a_ref,
    b_ref,
    conv_ref,
    tail_ref,
    tail_in,
    mine_ref,
    send1,
    recv1,
    send_t,
    recv_t,
):
    seqs = state0_ref.shape[0]
    width = taps_ref.shape[1]
    taps = taps_ref.shape[0]
    rows = seqs * span
    devices, me = lax.axis_size("seq"), lax.axis_index("seq")
    enter_all(("seq",))

    group = 2 * span

    @pl.loop(0, rows // group)
    def _(g):
        @pl.loop(0, group // ROWS)
        def _(q):
            at = block(g * (group // ROWS) + q, ROWS)
            x = x_ref[at, :]
            scale = lax.rsqrt(jnp.mean(x * x, axis=-1, keepdims=True) + EPS)
            normed_ref[at, :] = (x * scale * gain_ref[...]).astype(BF16)

        conv = dot(normed_ref[block(g, group), :], w_input_ref[...])
        for j in range(group // span):
            pad_ref[g * (group // span) + j, pl.ds(TILE, span), :] = conv[
                j * span : (j + 1) * span
            ]

    for s in range(seqs):
        tail_ref[s] = pad_ref[s, pl.ds(span, TILE), :]
    tail_copy = to_one("seq", 1, tail_ref, tail_in, send_t.at[0], recv_t.at[0])
    tail_copy.start()

    @pl.loop(0, rows // group)
    def _(g):
        branch_ref[block(g, group), :] = dot(normed_ref[block(g, group), :], w_branch_ref[...])

    tail_copy.wait()
    for s in range(seqs):
        pad_ref[s, pl.ds(0, TILE), :] = jnp.where(me == 0, conv0_ref[s], tail_in[s])

    def conv_rows(s, q):
        part = pad_ref[s, pl.ds(pl.multiple_of(q * ROWS, ROWS), ROWS + TILE), :]
        total = vec_ref[0:1, :]
        for k in range(taps):
            first = TILE - (taps - 1) + k
            total = total + taps_ref[k : k + 1, :] * part[first : first + ROWS]
        return total

    @pl.loop(0, seqs)
    def _(s):
        @pl.loop(0, span // ROWS)
        def _(q):
            conv_ref[block(q, ROWS), :] = conv_rows(s, q)

        pre_ref[block(s, span), :] = (
            dot(conv_ref[...].astype(BF16), gates_ref[...]) + gate_bias_ref[...]
        )

        @pl.loop(0, span // ROWS)
        def _(q):
            at = block(s * (span // ROWS) + q, ROWS)
            conv = conv_ref[block(q, ROWS), :]
            recall = jax.nn.sigmoid(pre_ref[at, :width])
            gate = jax.nn.sigmoid(pre_ref[at, width:])
            log_a = (-RATE_SCALE * vec_ref[1:2, :]) * recall
            a = jnp.exp(log_a)
            put(a_ref, at, a)
            put(b_ref, at, jnp.sqrt(one_minus_square(log_a, a)) * gate * conv)

    def at_time(ref, t):
        return get(ref, pl.ds(t, seqs, stride=span))

    def local(t, value):
        prod, state = value
        a = at_time(a_ref, t)
        return prod * a, a * state + at_time(b_ref, t)

    ones = jnp.ones((seqs, width), F32)
    prod, state = lax.fori_loop(0, span, local, (ones, jnp.zeros_like(ones)), unroll=8)
    mine_ref[0] = prod
    mine_ref[1] = state
    sums_ref[me] = mine_ref[...]
    copies = to_all("seq", mine_ref, sums_ref, send1, recv1)
    for copy in copies:
        copy.start()
    for copy in copies:
        copy.wait()

    def carry_step(j, carry):
        both = sums_ref[j]
        return jnp.where(j < me, both[0] * carry + both[1], carry)

    carry = lax.fori_loop(0, devices - 1, carry_step, state0_ref[...])
    carry_ref[...] = carry

    def final(t, state):
        state = at_time(a_ref, t) * state + at_time(b_ref, t)
        put(hidden_ref, pl.ds(t, seqs, stride=span), state)
        return state

    lax.fori_loop(0, span, final, carry, unroll=8)

    @pl.loop(0, rows // ROWS)
    def _(q):
        at = block(q, ROWS)
        mixed_ref[at, :] = (get(hidden_ref, at) * gelu(branch_ref[at, :])).astype(BF16)


def backward_kernel(
    span,
    grad_ref,
    branch_ref,
    hidden_ref,
    carry_ref,
    pre_ref,
    pad_ref,
    sums_ref,
    taps_ref,
    vec_ref,
    gates_t_ref,
    grad_branch_ref,
    input_ref,
    heads_ref,
    low_ref,
    acc_ref,
    a_ref,
    gd_ref,
    gs_ref,
    direct_ref,
    gpad_ref,
    mine_ref,
    entries_ref,
    head_ref,
    head_in,
    send1,
    recv1,
    send_t,
    recv_t,
):
    seqs, width = carry_ref.shape
    taps = taps_ref.shape[0]
    rows = seqs * span
    devices, me = lax.axis_size("seq"), lax.axis_index("seq")
    enter_all(("seq",))

    def decay(at):
        recall = jax.nn.sigmoid(pre_ref[at, :width])
        log_a = (-RATE_SCALE * vec_ref[1:2, :]) * recall
        return recall, log_a, jnp.exp(log_a)

    @pl.loop(0, rows // ROWS)
    def _(q):
        at = block(q, ROWS)
        put(a_ref, at, decay(at)[2])
        act, slope = gelu_both(branch_ref[at, :])
        grad = grad_ref[at, :]
        put(gd_ref, at, grad * act)
        grad_branch_ref[at, :] = (grad * get(hidden_ref, at) * slope).astype(BF16)

    def at_time(ref, t):
        return get(ref, pl.ds(t, seqs, stride=span))

    def local(k, through):
        t = span - 1 - k
        return at_time(a_ref, t) * (at_time(gd_ref, t) + through)

    zero = jnp.zeros((seqs, width), F32)
    mine_ref[...] = lax.fori_loop(0, span, local, zero, unroll=8)
    entries_ref[me] = mine_ref[...]
    copies = to_all("seq", mine_ref, entries_ref, send1, recv1)
    for copy in copies:
        copy.start()
    acc_ref[...] = jnp.zeros_like(acc_ref)
    for copy in copies:
        copy.wait()

    def back_step(k, through):
        j = devices - 1 - k
        return jnp.where(j > me, entries_ref[j] + sums_ref[j, 0] * through, through)

    incoming = lax.fori_loop(0, devices - 1, back_step, zero)

    def final(k, through):
        t = span - 1 - k
        grad = at_time(gd_ref, t) + through
        put(gs_ref, pl.ds(t, seqs, stride=span), grad)
        return at_time(a_ref, t) * grad

    lax.fori_loop(0, span, final, incoming, unroll=8)

    def add(k, value):
        total = value[0:TILE]
        for i in range(1, value.shape[0] // TILE):
            total = total + value[i * TILE : (i + 1) * TILE]
        acc_ref[k] += total

    @pl.loop(0, seqs)
    def _(s):
        @pl.loop(0, span // ROWS)
        def _(q):
            at = block(s * (span // ROWS) + q, ROWS)
            part = pad_ref[s, pl.ds(pl.multiple_of(q * ROWS, ROWS), ROWS + TILE), :]
            conv = vec_ref[0:1, :]
            for k in range(taps):
                first = TILE - (taps - 1) + k
                conv = conv + taps_ref[k : k + 1, :] * part[first : first + ROWS]
            heads_ref[at, :] = conv.astype(BF16)
            recall, log_a, a = decay(at)
            gate = jax.nn.sigmoid(pre_ref[at, width:])
            square = one_minus_square(log_a, a)
            inverse = lax.rsqrt(square)
            root = jnp.sqrt(square)
            grad = get(gs_ref, at)
            hidden = get(hidden_ref, at)
            before_at = pl.multiple_of(jnp.maximum(s * span + q * ROWS - TILE, 0), TILE)
            earlier = get(hidden_ref, pl.ds(before_at, TILE))
            first_row = jnp.where(q == 0, carry_ref[pl.ds(s, 1), :], earlier[TILE - 1 :])
            place = lax.broadcasted_iota(jnp.int32, (ROWS, width), 0)
            prev = jnp.where(place == 0, first_row, pltpu.roll(hidden, 1, 0))
            grad_log = grad * a * (prev - gate * conv * a * inverse)
            through = grad_log * recall
            pre_r = through * (1.0 - recall) * (-RATE_SCALE * vec_ref[1:2, :])
            direct = grad * root * gate
            pre_i = direct * conv * (1.0 - gate)
            low_ref[at, :width] = pre_r.astype(BF16)
            low_ref[at, width:] = pre_i.astype(BF16)
            direct_ref[block(q, ROWS), :] = direct
            add(0, through)
            add(1, pre_r)
            add(2, pre_i)

        whole = direct_ref[...] + dot(low_ref[block(s, span), :], gates_t_ref[...])
        gpad_ref[s, pl.ds(0, span), :] = whole
        head_ref[s] = whole[:TILE]

    head_copy = to_one("seq", -1, head_ref, head_in, send_t.at[0], recv_t.at[0])
    head_copy.start()

    @pl.loop(0, seqs)
    def _(s):
        @pl.loop(0, span // ROWS)
        def _(q):
            at = pl.multiple_of(q * ROWS, ROWS)
            part = pad_ref[s, pl.ds(at, ROWS + TILE), :]
            grad = gpad_ref[s, pl.ds(at, ROWS), :]
            add(3, grad)
            for k in range(taps):
                first = TILE - (taps - 1) + k
                add(4 + k, grad * part[first : first + ROWS])

    head_copy.wait()
    for s in range(seqs):
        gpad_ref[s, pl.ds(span, TILE), :] = jnp.where(me == devices - 1, 0.0, head_in[s])

    @pl.loop(0, seqs)
    def _(s):
        @pl.loop(0, span // ROWS)
        def _(q):
            part = gpad_ref[s, pl.ds(pl.multiple_of(q * ROWS, ROWS), ROWS + TILE), :]
            total = taps_ref[taps - 1 : taps, :] * part[0:ROWS]
            for k in range(taps - 1):
                first = taps - 1 - k
                total = total + taps_ref[k : k + 1, :] * part[first : first + ROWS]
            input_ref[block(s * (span // ROWS) + q, ROWS), :] = total.astype(BF16)


def line_sum(axis, total, period, part, inbox, out, sems, before, root, arrive, leave):
    send_up, send_down, recv_up, recv_down = sems
    n, z = lax.axis_size(axis), lax.axis_index(axis)
    depth = n // 2
    ring = out.shape[0]

    def root_of(c):
        return depth - 1 + lax.rem(c, 2)

    def up(c, step, side):
        slot = lax.rem(c, ring)
        return pltpu.make_async_remote_copy(
            src_ref=part.at[block(lax.rem(c, period), CHUNK)],
            dst_ref=inbox.at[side, slot],
            send_sem=send_up.at[slot],
            recv_sem=recv_up.at[side, slot],
            device_id={axis: z + step},
            device_id_type=MESH,
        )

    def down(c, step, side):
        slot = lax.rem(c, ring)
        return pltpu.make_async_remote_copy(
            src_ref=out.at[slot],
            dst_ref=out.at[slot],
            send_sem=send_down.at[side, slot],
            recv_sem=recv_down.at[slot],
            device_id={axis: z + step},
            device_id_type=MESH,
        )

    inner = jnp.logical_and(z > 0, z < n - 1)

    @pl.loop(0, total + ring)
    def _(k):
        @pl.when(k >= ring)
        def _():
            c = k - ring
            r = root_of(c)
            step = jnp.where(z < r, 1, -1)
            side = jnp.where(z < r, 0, 1)

            @pl.when(z == r)
            def _():
                down(c, -1, 0).wait_send()
                down(c, 1, 1).wait_send()

            @pl.when(z != r)
            def _():
                up(c, step, side).wait_send()

            @pl.when(jnp.logical_and(z != r, inner))
            def _():
                down(c, -step, side).wait_send()

            leave(c, lax.rem(c, ring))

        before(k)

        for i in reversed(range(n + 1)):
            c = k - SKEW * i
            valid = jnp.logical_and(c >= 0, c < total)
            c = jnp.clip(c, 0, total - 1)
            at = block(lax.rem(c, period), CHUNK)
            slot = lax.rem(c, ring)
            r = root_of(c)
            step = jnp.where(z < r, 1, -1)
            side = jnp.where(z < r, 0, 1)
            if i > depth:
                here = jnp.logical_and(z != r, jnp.abs(z - r) == i - depth)

                @pl.when(jnp.logical_and(valid, here))
                def _():
                    down(c, -step, side).wait_recv()

                    @pl.when(inner)
                    def _():
                        down(c, -step, side).start()

                    arrive(c, slot)
            elif i == depth:

                @pl.when(jnp.logical_and(valid, z == r))
                def _():
                    up(c, 1, 0).wait_recv()
                    up(c, -1, 1).wait_recv()
                    root(c, slot, part[at, :] + inbox[0, slot] + inbox[1, slot])
                    down(c, -1, 0).start()
                    down(c, 1, 1).start()
                    arrive(c, slot)
            else:
                here = jnp.where(z < r, z, n - 1 - z) == i

                @pl.when(jnp.logical_and(valid, jnp.logical_and(z != r, here)))
                def _():
                    if i > 0:
                        up(c, step, side).wait_recv()
                        part[at, :] += inbox[side, slot]
                    up(c, step, side).start()


def ring_size(axis):
    return SKEW * lax.axis_size(axis) + 4


def line_scratch(axis, rows, model):
    dma = pltpu.SemaphoreType.DMA
    ring = ring_size(axis)
    return [
        pltpu.VMEM((rows, model), F32),
        pltpu.VMEM((2, ring, CHUNK, model), F32),
        pltpu.VMEM((ring, CHUNK, model), F32),
        dma((ring,)),
        dma((2, ring)),
        dma((2, ring)),
        dma((ring,)),
    ]


def mean_square(x):
    return lax.rsqrt(jnp.mean(x * x, axis=-1, keepdims=True) + EPS)


def nothing(*_):
    pass


def fold(value):
    total = value[0:TILE]
    for i in range(1, value.shape[0] // TILE):
        total = total + value[i * TILE : (i + 1) * TILE]
    return total


def norm_grad(value, gain, grad, acc_ref):
    q = mean_square(value)
    e = gain * grad
    acc_ref[...] += fold(grad * value * q)
    return q * e - value * (q * q * q) * jnp.mean(e * value, axis=-1, keepdims=True)


def middle_kernel(
    mixed_in,
    w_out_in,
    x_in,
    og_in,
    gain_ref,
    w_gate_in,
    w_up_in,
    w_down_in,
    normed_out,
    hidden_out,
    gate_out,
    up_out,
    glow_out,
    block_out,
    low_out,
    own_grad_out,
    own_ref,
    acc_ref,
    part,
    inbox,
    out,
    send_up,
    send_down,
    recv_up,
    recv_down,
    mixed,
    w_out,
    w_gate,
    w_up,
    w_down,
    normed,
    rows_ref,
    og_ref,
    glow,
    gate_val,
    up_val,
    grad_hidden,
    hidden,
    grad_gate,
    grad_up,
    block_part,
    low,
    weight_sem,
    row_sem,
    og_sem,
    act_sem,
    low_sem,
    own_sem,
):
    n, z = lax.axis_size("mp"), lax.axis_index("mp")
    count = part.shape[0] // CHUNK
    size = GROUP * CHUNK
    groups = count // GROUP
    ring = out.shape[0]
    sems = (send_up, send_down, recv_up, recv_down)
    local = pltpu.make_async_copy

    loads = [
        local(source, target, weight_sem.at[i])
        for i, (source, target) in enumerate(
            (
                (mixed_in, mixed),
                (w_out_in, w_out),
                (w_gate_in, w_gate),
                (w_up_in, w_up),
                (w_down_in, w_down),
            )
        )
    ]
    for copy in loads:
        copy.start()

    def og_load(g):
        return local(og_in.at[block(g, size)], og_ref, og_sem.at[0])

    og_load(0).start()
    enter_all(("mp",))
    acc_ref[...] = jnp.zeros_like(acc_ref)
    loads[0].wait()
    loads[1].wait()

    def is_root(c):
        return z == n // 2 - 1 + lax.rem(c, 2)

    def row_load(source, c):
        slot = lax.rem(c, ring)
        at = block(lax.rem(c, count), CHUNK)
        return local(source.at[at], rows_ref.at[slot], row_sem.at[slot])

    acts = (
        (normed, normed_out),
        (glow, glow_out),
        (hidden, hidden_out),
        (grad_gate, gate_out),
        (grad_up, up_out),
        (block_part, block_out),
    )

    def act_store(i, g):
        source, target = acts[i]
        source = source.at[lax.rem(g, 2)] if i == 0 else source
        return local(source, target.at[block(g, size)], act_sem.at[i])

    def at_tick(k, first, work):
        g = (k - first) // GROUP

        @pl.when(
            jnp.logical_and(
                jnp.logical_and(k >= first, k < first + GROUP * groups),
                lax.rem(k - first, GROUP) == 0,
            )
        )
        def _():
            work(g)

    def project(g):
        part[block(g, size), :] = dot(mixed[block(g, size), :], w_out[...])

    def piece_gate(g):
        @pl.when(g == 0)
        def _():
            for copy in loads[2:]:
                copy.wait()

        gate_val[...] = dot(normed[lax.rem(g, 2)], w_gate[...])
        act_store(0, g).start()

    def piece_up(g):
        up_val[...] = dot(normed[lax.rem(g, 2)], w_up[...])

        @pl.when(g > 0)
        def _():
            for i in range(1, 6):
                act_store(i, g - 1).wait()

    def piece_low(g):
        og_load(g).wait()

        @pl.loop(0, size // ROWS)
        def _(q):
            glow[block(q, ROWS), :] = og_ref[block(q, ROWS), :].astype(BF16)

        @pl.when(g + 1 < groups)
        def _():
            og_load(g + 1).start()

        act_store(1, g).start()
        act_store(0, g).wait()

    def piece_hidden(g):
        grad_hidden[...] = matmul_back(glow[...], w_down[...])

    def piece_act(g):
        @pl.loop(0, size // CHUNK)
        def _(q):
            at = block(q, CHUNK)
            up = up_val[at, :]
            grad = grad_hidden[at, :]
            act, slope = gelu_both(gate_val[at, :])
            hidden[at, :] = (act * up).astype(BF16)
            grad_gate[at, :] = (grad * up * slope).astype(BF16)
            grad_up[at, :] = (grad * act).astype(BF16)

        for i in range(2, 5):
            act_store(i, g).start()

    def piece_down(g):
        block_part[...] = dot(hidden[...], w_down[...])
        act_store(5, g).start()

    def piece_back_gate(g):
        part[block(g, size), :] = matmul_back(grad_gate[...], w_gate[...])

    def piece_back_up(g):
        part[block(g, size), :] += matmul_back(grad_up[...], w_up[...])

    first = GROUP + SKEW * n

    def before(k):
        @pl.when(jnp.logical_and(k < count, is_root(k)))
        def _():
            row_load(x_in, k).start()

        @pl.when(
            jnp.logical_and(jnp.logical_and(k >= count, k < 2 * count), is_root(k))
        )
        def _():
            row_load(og_in, k).start()

        at_tick(k, 0, project)
        at_tick(k, first, piece_gate)
        at_tick(k, first + 1, piece_up)
        at_tick(k, first + 2, piece_low)
        at_tick(k, first + 3, piece_hidden)
        at_tick(k, first + 4, piece_act)
        at_tick(k, first + 6, piece_down)
        at_tick(k, GROUP + ring, piece_back_gate)
        at_tick(k, GROUP + ring + 2, piece_back_up)

    def root(c, slot, total):
        j = lax.rem(c, count)
        mine = block(j // 2, CHUNK)
        row_load(x_in, c).wait()

        @pl.when(c < count)
        def _():
            value = rows_ref[slot] + total
            own_ref[mine, :] = value
            out[slot] = (value * mean_square(value) * gain_ref[...]).astype(BF16).astype(F32)

        @pl.when(c >= count)
        def _():
            back = norm_grad(own_ref[mine, :], gain_ref[...], total, acc_ref)
            out[slot] = rows_ref[slot] + back

    def low_store(c, slot):
        at = block(lax.rem(c, count), CHUNK)
        return local(low.at[slot], low_out.at[at], low_sem.at[slot])

    def own_store(c, slot):
        at = block(lax.rem(c, count) // 2, CHUNK)
        return local(out.at[slot], own_grad_out.at[at], own_sem.at[slot])

    def arrive(c, slot):
        @pl.when(c < count)
        def _():
            normed[lax.rem(c // GROUP, 2), block(lax.rem(c, GROUP), CHUNK), :] = out[slot].astype(BF16)

        @pl.when(c >= count)
        def _():
            low[slot] = out[slot].astype(BF16)
            low_store(c, slot).start()

            @pl.when(is_root(c))
            def _():
                own_store(c, slot).start()

    def leave(c, slot):
        @pl.when(c >= count)
        def _():
            low_store(c, slot).wait()

            @pl.when(is_root(c))
            def _():
                own_store(c, slot).wait()

    line_sum("mp", 2 * count, count, part, inbox, out, sems, before, root, arrive, leave)

    for i in range(1, 6):
        act_store(i, groups - 1).wait()


def middle_call(*args):
    mixed, w_out, x, og, gain, w_gate, w_up, w_down = args
    rows, model = x.shape
    width, hidden = mixed.shape[1], w_gate.shape[1]
    size = GROUP * CHUNK
    dma = pltpu.SemaphoreType.DMA
    ring = ring_size("mp")
    act = shape((rows, hidden), BF16)
    tall = shape((rows, model), BF16)
    return pl.pallas_call(
        middle_kernel,
        out_shape=(
            tall,
            act,
            act,
            act,
            tall,
            shape((rows, model)),
            tall,
            shape((rows // 2, model)),
            shape((rows // 2, model)),
            shape((TILE, model)),
        ),
        in_specs=[HBM] * 4 + [VMEM] + [HBM] * 3,
        out_specs=(HBM,) * 8 + (VMEM,) * 2,
        scratch_shapes=line_scratch("mp", rows, model)
        + [
            pltpu.VMEM((rows, width), BF16),
            pltpu.VMEM((width, model), BF16),
            pltpu.VMEM((model, hidden), BF16),
            pltpu.VMEM((model, hidden), BF16),
            pltpu.VMEM((hidden, model), BF16),
            pltpu.VMEM((2, size, model), BF16),
            pltpu.VMEM((ring, CHUNK, model), F32),
            pltpu.VMEM((size, model), F32),
            pltpu.VMEM((size, model), BF16),
            pltpu.VMEM((size, hidden), F32),
            pltpu.VMEM((size, hidden), F32),
            pltpu.VMEM((size, hidden), F32),
            pltpu.VMEM((size, hidden), BF16),
            pltpu.VMEM((size, hidden), BF16),
            pltpu.VMEM((size, hidden), BF16),
            pltpu.VMEM((size, model), F32),
            pltpu.VMEM((ring, CHUNK, model), BF16),
            dma((5,)),
            dma((ring,)),
            dma((1,)),
            dma((6,)),
            dma((ring,)),
            dma((ring,)),
        ],
        compiler_params=params(2, 63),
        cost_estimate=cost(400),
        name="middle",
    )(*args)


def last_kernel(
    block_part,
    grad_part,
    own_ref,
    own_grad_ref,
    x_ref,
    gain_ref,
    other_acc,
    block_ref,
    grad_ref,
    norm_ref,
    part,
    inbox,
    out,
    send_up,
    send_down,
    recv_up,
    recv_down,
    load_sem,
    store_sem,
    acc_ref,
    mine_ref,
    seq_in,
    mp_in,
    send_s,
    recv_s,
    send_m,
    recv_m,
):
    count = part.shape[0] // CHUNK
    group = GROUP * CHUNK
    groups = count // GROUP
    sems = (send_up, send_down, recv_up, recv_down)
    enter_all(("seq", "mp"))
    acc_ref[...] = jnp.zeros_like(acc_ref)
    mine_ref[...] = jnp.zeros_like(mine_ref)

    def load(source, g):
        at = block(lax.rem(g, groups), group)
        return pltpu.make_async_copy(source.at[at], part.at[at], load_sem.at[lax.rem(g, 2)])

    def start_load(g):
        @pl.when(g < groups)
        def _():
            load(block_part, g).start()

        @pl.when(jnp.logical_and(g >= groups, g < 2 * groups))
        def _():
            load(grad_part, g).start()

    start_load(jnp.int32(0))

    def before(k):
        @pl.when(jnp.logical_and(lax.rem(k, GROUP) == 0, k < 2 * count))
        def _():
            g = k // GROUP
            load(block_part, g).wait()
            start_load(g + 1)

    def root(c, slot, total):
        j = lax.rem(c, count)
        mine = block(j // 2, CHUNK)

        @pl.when(c < count)
        def _():
            out[slot] = own_ref[mine, :] + total

        @pl.when(c >= count)
        def _():
            back = norm_grad(x_ref[block(j, CHUNK), :], gain_ref[...], total, acc_ref)
            out[slot] = own_grad_ref[mine, :] + back

    def store(target, c, slot):
        at = block(lax.rem(c, count), CHUNK)
        return pltpu.make_async_copy(out.at[slot], target.at[at], store_sem.at[slot])

    def arrive(c, slot):
        @pl.when(c < count)
        def _():
            store(block_ref, c, slot).start()

        @pl.when(c >= count)
        def _():
            store(grad_ref, c, slot).start()

    def leave(c, slot):
        store(block_ref, c, slot).wait()

    line_sum("mp", 2 * count, count, part, inbox, out, sems, before, root, arrive, leave)

    mine_ref[0, 0:1, :] = jnp.sum(acc_ref[...], axis=0, keepdims=True)
    mine_ref[0, 1:2, :] = jnp.sum(other_acc[...], axis=0, keepdims=True)
    for i, (axis, place, send, recv) in enumerate(
        (("seq", seq_in, send_s, recv_s), ("mp", mp_in, send_m, recv_m))
    ):
        if i == 1:
            mine_ref[1] = jnp.sum(seq_in[...], axis=0)
        place[lax.axis_index(axis)] = mine_ref[i]
        copies = to_all(axis, mine_ref.at[i], place, send, recv)
        for copy in copies:
            copy.start()
        for copy in copies:
            copy.wait()
    norm_ref[...] = jnp.sum(mp_in[...], axis=0)


def enter_all(axes):
    barrier = pltpu.get_barrier_semaphore()
    count = 0
    for axis in axes:
        size, me = lax.axis_size(axis), lax.axis_index(axis)
        for d in range(1, size):
            pl.semaphore_signal(
                barrier, 1, device_id={axis: lax.rem(me + d, size)}, device_id_type=MESH
            )
        count += size - 1
    pl.semaphore_wait(barrier, count)


def cost(micros):
    return pl.CostEstimate(flops=int(micros * 1e9), bytes_accessed=1 << 20, transcendentals=0)


def last_call(*args):
    rows, model = args[0].shape
    dma = pltpu.SemaphoreType.DMA
    nseq, nmp = lax.axis_size("seq"), lax.axis_size("mp")
    return pl.pallas_call(
        last_kernel,
        out_shape=(shape((rows, model)), shape((rows, model)), shape((TILE, model))),
        in_specs=[HBM, HBM] + [VMEM] * 5,
        out_specs=(HBM, HBM, VMEM),
        scratch_shapes=line_scratch("mp", rows, model)
        + [
            dma((2,)),
            dma((ring_size("mp"),)),
            pltpu.VMEM((TILE, model), F32),
            pltpu.VMEM((2, TILE, model), F32),
            pltpu.VMEM((nseq, TILE, model), F32),
            pltpu.VMEM((nmp, TILE, model), F32),
            dma((nseq - 1,)),
            dma((nseq - 1,)),
            dma((nmp - 1,)),
            dma((nmp - 1,)),
        ],
        compiler_params=params(4, 60),
        cost_estimate=cost(380),
        name="last_sums",
    )(*args)


def weight_kernel(plan, lefts, *refs):
    left_refs, right_refs = refs[:lefts], refs[lefts:-2]
    out_ref, turned = refs[-2:]
    j = pl.program_id(0)
    begin = 0
    held = None
    for (left, blocks), right in zip(plan, right_refs):
        if left != held:
            held = left

            @pl.when(j == begin)
            def _():
                rows = left_refs[left].shape[0]
                for i in range(left_refs[left].shape[1] // TURN):
                    at = slice(i * TURN, (i + 1) * TURN)
                    turned[at, :] = left_refs[left][:, at].T

        @pl.when(jnp.logical_and(j >= begin, j < begin + blocks))
        def _():
            size = turned.shape[0] // 4

            @pl.loop(0, 4)
            def _(i):
                out_ref[block(i, size), :] = dot(turned[block(i, size), :], right[...])

        begin += blocks


def weight_grads(lefts, pairs, width):
    rows, model = lefts[0].shape
    plan = tuple((left, right.shape[1] // width) for left, right in pairs)
    steps = sum(blocks for _, blocks in plan)
    whole = pl.BlockSpec((rows, model), lambda j: (0, 0))
    specs = [whole] * len(lefts)
    begin = 0
    for _, blocks in plan:
        specs.append(
            pl.BlockSpec(
                (rows, width),
                lambda j, first=begin, n=blocks: (0, jnp.clip(j - first, 0, n - 1)),
            )
        )
        begin += blocks
    return pl.pallas_call(
        functools.partial(weight_kernel, plan, len(lefts)),
        out_shape=shape((model, steps * width)),
        grid=(steps,),
        in_specs=specs,
        out_specs=pl.BlockSpec((model, width), lambda j: (0, j)),
        scratch_shapes=[pltpu.VMEM((model, rows), BF16)],
        compiler_params=pltpu.CompilerParams(vmem_limit_bytes=60 << 20),
        cost_estimate=cost(30),
        name="weight_grads",
    )(*lefts, *(right for _, right in pairs))


def params(collective, megabytes=60):
    return pltpu.CompilerParams(
        collective_id=collective, has_side_effects=True, vmem_limit_bytes=megabytes << 20
    )


def shape(dims, dtype=F32):
    return jax.ShapeDtypeStruct(dims, dtype)


def recurrence_forward(span, *args):
    x, _, w_branch = args[:3]
    state0 = args[8]
    rows, model = x.shape
    seqs, width = state0.shape
    devices = lax.axis_size("seq")
    dma = pltpu.SemaphoreType.DMA
    return pl.pallas_call(
        functools.partial(forward_kernel, span),
        out_shape=(
            shape((rows, model), BF16),
            shape((rows, width)),
            shape((seqs, span + TILE, width)),
            shape((rows, 2 * width)),
            shape((width // LANES, rows, LANES)),
            shape((rows, width), BF16),
            shape((seqs, width)),
            shape((devices, 2, seqs, width)),
        ),
        in_specs=[VMEM] * len(args),
        out_specs=(VMEM,) * 8,
        scratch_shapes=[
            pltpu.VMEM((width // LANES, rows, LANES), F32),
            pltpu.VMEM((width // LANES, rows, LANES), F32),
            pltpu.VMEM((span, width), F32),
            pltpu.VMEM((seqs, TILE, width), F32),
            pltpu.VMEM((seqs, TILE, width), F32),
            pltpu.VMEM((2, seqs, width), F32),
            dma((devices - 1,)),
            dma((devices - 1,)),
            dma((1,)),
            dma((1,)),
        ],
        compiler_params=params(0),
        cost_estimate=cost(50),
        name="recurrence_forward",
    )(*args)


def recurrence_backward(span, *args):
    rows, width = args[0].shape
    seqs = args[3].shape[0]
    taps = args[7].shape[0]
    devices = lax.axis_size("seq")
    dma = pltpu.SemaphoreType.DMA
    return pl.pallas_call(
        functools.partial(backward_kernel, span),
        out_shape=(
            shape((rows, width), BF16),
            shape((rows, width), BF16),
            shape((rows, width), BF16),
            shape((rows, 2 * width), BF16),
            shape((4 + taps, TILE, width)),
        ),
        in_specs=[VMEM] * len(args),
        out_specs=(VMEM,) * 5,
        scratch_shapes=[
            pltpu.VMEM((width // LANES, rows, LANES), F32),
            pltpu.VMEM((width // LANES, rows, LANES), F32),
            pltpu.VMEM((width // LANES, rows, LANES), F32),
            pltpu.VMEM((span, width), F32),
            pltpu.VMEM((seqs, span + TILE, width), F32),
            pltpu.VMEM((seqs, width), F32),
            pltpu.VMEM((devices, seqs, width), F32),
            pltpu.VMEM((seqs, TILE, width), F32),
            pltpu.VMEM((seqs, TILE, width), F32),
            dma((devices - 1,)),
            dma((devices - 1,)),
            dma((1,)),
            dma((1,)),
        ],
        compiler_params=params(1),
        cost_estimate=cost(50),
        name="recurrence_backward",
    )(*args)


def widen(array, width):
    short = width - array.shape[-1]
    if short == 0:
        return array
    return jnp.pad(array, [(0, 0)] * (array.ndim - 1) + [(0, short)])


def diagonal(gates, width):
    heads, size, _ = gates.shape
    spread = jnp.eye(heads, dtype=gates.dtype)[:, None, :, None] * gates[:, :, None, :]
    flat = spread.reshape(heads * size, heads * size)
    short = width - heads * size
    return jnp.pad(flat, ((0, short), (0, short))) if short else flat


def per_device(
    stream,
    norm_in,
    w_branch,
    w_input,
    conv_kernel,
    conv_bias,
    gate_r,
    bias_r,
    gate_i,
    bias_i,
    decay_param,
    w_out,
    norm_mlp,
    w_gate,
    w_up,
    w_down,
    state_init,
    conv_init,
    fresh_rows,
    out_grad,
):
    seqs, span, model = stream.shape
    channels = w_branch.shape[1]
    mlp_dev = w_gate.shape[1]
    heads, head_width = gate_r.shape[:2]
    taps = conv_kernel.shape[0]
    edge = taps - 1
    rows = seqs * span
    devices = lax.axis_size("seq")
    position = lax.axis_index("seq")
    width = -(-channels // 128) * 128

    keep = 1.0 - fresh_rows.astype(F32)
    flat_in = stream.reshape(rows, model)
    flat_grad = out_grad.reshape(rows, model)
    w_branch_p = widen(w_branch, width)
    w_input_p = widen(w_input, width)
    w_out_p = jnp.pad(w_out, ((0, width - channels), (0, 0))) if width > channels else w_out
    taps_p = widen(conv_kernel, width)
    rate = jax.nn.softplus(-decay_param)
    rate_p = jnp.pad(rate, (0, width - channels), constant_values=1.0)
    vec = jnp.stack([widen(conv_bias, width), rate_p])
    gates = jnp.concatenate([diagonal(gate_r, width), diagonal(gate_i, width)], axis=1)
    gates_t = jnp.concatenate(
        [
            diagonal(jnp.swapaxes(gate_r, 1, 2), width),
            diagonal(jnp.swapaxes(gate_i, 1, 2), width),
        ],
        axis=0,
    )
    gate_bias = jnp.concatenate([widen(bias_r, width), widen(bias_i, width)])[None]
    state0 = widen(state_init * keep[:, None], width)
    conv0 = jnp.pad(
        conv_init * keep[:, None, None], ((0, 0), (TILE - edge, 0), (0, width - channels))
    )

    normed, branch, padded, pre, hidden, mixed, carry, sums = recurrence_forward(
        span,
        flat_in,
        norm_in[None],
        w_branch_p,
        w_input_p,
        taps_p,
        vec,
        gates,
        gate_bias,
        state0,
        conv0,
    )
    (
        normed_mlp,
        hidden_mlp,
        grad_gate,
        grad_up,
        grad_low,
        block_part,
        resid_low,
        own_grad,
        own,
        norm_mlp_acc,
    ) = middle_call(mixed, w_out_p, flat_in, flat_grad, norm_mlp[None], w_gate, w_up, w_down)
    mlp_grads = weight_grads(
        (normed_mlp, grad_low), ((0, grad_gate), (0, grad_up), (1, hidden_mlp)), mlp_dev // 3
    )
    mlp_grads, resid_low = lax.optimization_barrier((mlp_grads, resid_low))
    mlp_grads = lax.psum_scatter(mlp_grads, "seq", scatter_dimension=0, tiled=True)
    grad_mixed = matmul_back(resid_low, w_out_p)
    grad_branch, input_low, heads_in, pre_low, acc = recurrence_backward(
        span,
        grad_mixed,
        branch,
        hidden,
        carry,
        pre,
        padded,
        sums,
        taps_p,
        vec,
        gates_t,
    )
    grad_part = matmul_back(grad_branch, w_branch_p) + matmul_back(input_low, w_input_p)
    rec_grads = weight_grads(
        (resid_low, normed), ((0, mixed), (1, grad_branch), (1, input_low)), width
    )
    gates_grad = lax.dot_general(heads_in, pre_low, CONTRACT_ROWS, preferred_element_type=F32)

    def blocks(array):
        return jnp.stack(
            [
                array[h * head_width : (h + 1) * head_width, h * head_width : (h + 1) * head_width]
                for h in range(heads)
            ]
        )

    def place(array):
        flat = array.reshape(-1)
        return jnp.pad(flat, (0, -flat.size % 1024)).reshape(-1, LANES)

    last = position == devices - 1
    last_hidden = hidden.reshape(-1, seqs, span, LANES)[:, :, -1]
    last_hidden = jnp.swapaxes(last_hidden, 0, 1).reshape(seqs, width)[:, :channels]
    final_state = jnp.where(last, last_hidden, 0.0)
    final_conv = jnp.where(last, padded[:, span + TILE - edge :, :channels], 0.0)
    pieces = (
        jnp.sum(acc, axis=1)[:, :channels],
        blocks(gates_grad[:, :width]),
        blocks(gates_grad[:, width:]),
        final_state,
        final_conv,
    )
    small = jnp.concatenate([place(piece) for piece in pieces], axis=0)
    small, rec_grads, grad_part = lax.optimization_barrier((small, rec_grads, grad_part))
    rec_grads = lax.psum_scatter(rec_grads, "seq", scatter_dimension=0, tiled=True)
    small = lax.psum(small, "seq")

    block_out, stream_grad, norm_grads = last_call(
        block_part,
        grad_part,
        own,
        own_grad,
        flat_in,
        norm_in[None],
        norm_mlp_acc,
    )

    summed = []
    begin = 0
    for piece in pieces:
        lines = -(-piece.size // 1024) * 8
        flat = small[begin : begin + lines].reshape(-1)
        summed.append(flat[: piece.size].reshape(piece.shape))
        begin += lines
    acc, gate_r_grad, gate_i_grad, final_state, final_conv = summed
    norm_in_grad = norm_grads[0]
    norm_mlp_grad = norm_grads[1]
    decay_grad = acc[0] * (RATE_SCALE * jax.nn.sigmoid(-decay_param))
    w_gate_grad = mlp_grads[:, :mlp_dev]
    w_up_grad = mlp_grads[:, mlp_dev : 2 * mlp_dev]
    w_down_grad = mlp_grads[:, 2 * mlp_dev :]
    w_out_grad = rec_grads[:, :width]
    w_branch_grad = rec_grads[:, width : 2 * width]
    w_input_grad = rec_grads[:, 2 * width :]
    return (
        block_out.reshape(stream.shape),
        stream_grad.reshape(stream.shape),
        norm_in_grad,
        w_branch_grad[:, :channels],
        w_input_grad[:, :channels],
        acc[4:],
        acc[3],
        gate_r_grad,
        acc[1],
        gate_i_grad,
        acc[2],
        decay_grad,
        w_out_grad[:, :channels].T,
        norm_mlp_grad,
        w_gate_grad,
        w_up_grad,
        w_down_grad.T,
        final_state,
        final_conv,
    )


def solution(mesh):
    seq_rows = P(None, "seq", None)
    columns = P(None, "mp")
    channel = P("mp")
    return jax.shard_map(
        per_device,
        mesh=mesh,
        in_specs=(
            seq_rows,
            P(),
            columns,
            columns,
            columns,
            channel,
            P("mp", None, None),
            channel,
            P("mp", None, None),
            channel,
            channel,
            P("mp", None),
            P(),
            columns,
            columns,
            P("mp", None),
            columns,
            P(None, None, "mp"),
            P(),
            seq_rows,
        ),
        out_specs=(
            seq_rows,
            seq_rows,
            P(),
            P("seq", "mp"),
            P("seq", "mp"),
            columns,
            channel,
            P("mp", None, None),
            channel,
            P("mp", None, None),
            channel,
            channel,
            P("mp", "seq"),
            P(),
            P("seq", "mp"),
            P("seq", "mp"),
            P("mp", "seq"),
            columns,
            P(None, None, "mp"),
        ),
        check_vma=False,
    )
```

```python
import functools

import jax
import jax.numpy as jnp
from jax import lax
from jax.experimental import pallas as pl
from jax.experimental.pallas import tpu as pltpu
from jax.sharding import PartitionSpec as P

MESH = pl.DeviceIdType.MESH
RATE_SCALE = 8.0
EPS = 1e-06
GELU_C = 0.7978845608028654
GELU_K = 0.044715
CONTRACT_ROWS = (((0,), (0,)), ((), ()))
CONTRACT_LAST = (((1,), (1,)), ((), ()))
TILE = 8
LANES = 128
ROWS = 32
CHUNK = 16
SKEW = 2
GROUP = 16
TURN = 256
WEIGHT_STEPS = 8
F32 = jnp.float32
BF16 = jnp.bfloat16
VMEM = pl.BlockSpec(memory_space=pltpu.VMEM)
HBM = pl.BlockSpec(memory_space=pl.ANY)


def dot(a, b):
    return jnp.dot(a, b, preferred_element_type=F32)


def matmul_back(a, b):
    return lax.dot_general(a, b, CONTRACT_LAST, preferred_element_type=F32)


def block(i, size):
    return pl.ds(pl.multiple_of(i * size, size), size)


def gelu(x):
    t = jnp.tanh(GELU_C * (x + GELU_K * (x * x * x)))
    return 0.5 * x * (1.0 + t)


def gelu_both(x):
    x2 = x * x
    t = jnp.tanh(GELU_C * (x + GELU_K * (x2 * x)))
    half = 0.5 * (1.0 + t)
    slope = half + 0.5 * x * (1.0 - t * t) * (GELU_C * (1.0 + (3.0 * GELU_K) * x2))
    return x * half, slope


def one_minus_square(log_a, a):
    y = 2.0 * log_a
    s = 1.0 + y * (1.0 / 8.0)
    for k in (7, 6, 5, 4, 3, 2):
        s = 1.0 + (y * (1.0 / k)) * s
    return jnp.where(y > -0.35, -y * s, 1.0 - a * a)


def get(ref, at):
    return jnp.concatenate([ref[j, at, :] for j in range(ref.shape[0])], axis=-1)


def put(ref, at, value):
    for j in range(ref.shape[0]):
        ref[j, at, :] = value[:, j * LANES : (j + 1) * LANES]


def to_all(axis, src, slots, send, recv):
    size, me = lax.axis_size(axis), lax.axis_index(axis)
    return [
        pltpu.make_async_remote_copy(
            src_ref=src,
            dst_ref=slots.at[me],
            send_sem=send.at[d - 1],
            recv_sem=recv.at[d - 1],
            device_id={axis: lax.rem(me + d, size)},
            device_id_type=MESH,
        )
        for d in range(1, size)
    ]


def to_one(axis, distance, src, dst, send, recv):
    size, me = lax.axis_size(axis), lax.axis_index(axis)
    return pltpu.make_async_remote_copy(
        src_ref=src,
        dst_ref=dst,
        send_sem=send,
        recv_sem=recv,
        device_id={axis: lax.rem(me + distance + size, size)},
        device_id_type=MESH,
    )


def spread_gates(blocks_ref, out_ref, start, width):
    heads, size = blocks_ref.shape[:2]
    for h in range(heads):
        block_h = blocks_ref[h].astype(F32)
        parts = [block_h]
        if h > 0:
            parts.insert(0, jnp.zeros((size, h * size), F32))
        if width > (h + 1) * size:
            parts.append(jnp.zeros((size, width - (h + 1) * size), F32))
        row = jnp.concatenate(parts, axis=1).astype(BF16)
        out_ref[h * size : (h + 1) * size, start : start + width] = row
    if width > heads * size:
        rest = jnp.zeros((width - heads * size, width), BF16)
        out_ref[heads * size : width, start : start + width] = rest


def forward_kernel(
    span,
    x_ref,
    gain_ref,
    w_branch_ref,
    w_input_ref,
    taps_ref,
    vec_in,
    gate_r_ref,
    gate_i_ref,
    fresh_ref,
    state_ref,
    conv_init_ref,
    normed_ref,
    branch_ref,
    pad_ref,
    pre_ref,
    hidden_ref,
    mixed_ref,
    carry_ref,
    sums_ref,
    gates_ref,
    vec_ref,
    a_ref,
    b_ref,
    conv_ref,
    tail_ref,
    tail_in,
    mine_ref,
    send1,
    recv1,
    send_t,
    recv_t,
):
    seqs = state_ref.shape[0]
    width = taps_ref.shape[1]
    taps = taps_ref.shape[0]
    rows = seqs * span
    devices, me = lax.axis_size("seq"), lax.axis_index("seq")
    enter_all(("seq",))
    spread_gates(gate_r_ref, gates_ref, 0, width)
    spread_gates(gate_i_ref, gates_ref, width, width)
    vec_ref[0:1, :] = vec_in[0:1, :]
    vec_ref[1:2, :] = jax.nn.softplus(-vec_in[1:2, :])
    gate_bias = jnp.concatenate([vec_in[2:3, :], vec_in[3:4, :]], axis=1)
    keep = 1.0 - fresh_ref[...].astype(F32)

    group = 2 * span

    @pl.loop(0, rows // group)
    def _(g):
        @pl.loop(0, group // ROWS)
        def _(q):
            at = block(g * (group // ROWS) + q, ROWS)
            x = x_ref[at, :]
            scale = lax.rsqrt(jnp.mean(x * x, axis=-1, keepdims=True) + EPS)
            normed_ref[at, :] = (x * scale * gain_ref[...]).astype(BF16)

        conv = dot(normed_ref[block(g, group), :], w_input_ref[...])
        for j in range(group // span):
            pad_ref[g * (group // span) + j, pl.ds(TILE, span), :] = conv[
                j * span : (j + 1) * span
            ]

    for s in range(seqs):
        tail_ref[s] = pad_ref[s, pl.ds(span, TILE), :]
    tail_copy = to_one("seq", 1, tail_ref, tail_in, send_t.at[0], recv_t.at[0])
    tail_copy.start()

    @pl.loop(0, rows // group)
    def _(g):
        branch_ref[block(g, group), :] = dot(normed_ref[block(g, group), :], w_branch_ref[...])

    tail_copy.wait()
    lead = jnp.zeros((TILE - taps + 1, width), F32)
    for s in range(seqs):
        initial = jnp.concatenate([lead, conv_init_ref[s] * keep[s : s + 1, :]], axis=0)
        pad_ref[s, pl.ds(0, TILE), :] = jnp.where(me == 0, initial, tail_in[s])

    def conv_rows(s, q):
        part = pad_ref[s, pl.ds(pl.multiple_of(q * ROWS, ROWS), ROWS + TILE), :]
        total = vec_ref[0:1, :]
        for k in range(taps):
            first = TILE - (taps - 1) + k
            total = total + taps_ref[k : k + 1, :] * part[first : first + ROWS]
        return total

    @pl.loop(0, seqs)
    def _(s):
        @pl.loop(0, span // ROWS)
        def _(q):
            conv_ref[block(q, ROWS), :] = conv_rows(s, q)

        pre_ref[block(s, span), :] = (
            dot(conv_ref[...].astype(BF16), gates_ref[...]) + gate_bias
        )

        @pl.loop(0, span // ROWS)
        def _(q):
            at = block(s * (span // ROWS) + q, ROWS)
            conv = conv_ref[block(q, ROWS), :]
            recall = jax.nn.sigmoid(pre_ref[at, :width])
            gate = jax.nn.sigmoid(pre_ref[at, width:])
            log_a = (-RATE_SCALE * vec_ref[1:2, :]) * recall
            a = jnp.exp(log_a)
            put(a_ref, at, a)
            put(b_ref, at, jnp.sqrt(one_minus_square(log_a, a)) * gate * conv)

    def at_time(ref, t):
        return get(ref, pl.ds(t, seqs, stride=span))

    def local(t, value):
        prod, state = value
        a = at_time(a_ref, t)
        return prod * a, a * state + at_time(b_ref, t)

    ones = jnp.ones((seqs, width), F32)
    prod, state = lax.fori_loop(0, span, local, (ones, jnp.zeros_like(ones)), unroll=8)
    mine_ref[0] = prod
    mine_ref[1] = state
    sums_ref[me] = mine_ref[...]
    copies = to_all("seq", mine_ref, sums_ref, send1, recv1)
    for copy in copies:
        copy.start()
    for copy in copies:
        copy.wait()

    def carry_step(j, carry):
        both = sums_ref[j]
        return jnp.where(j < me, both[0] * carry + both[1], carry)

    carry = lax.fori_loop(0, devices - 1, carry_step, state_ref[...] * keep)
    carry_ref[...] = carry

    def final(t, state):
        state = at_time(a_ref, t) * state + at_time(b_ref, t)
        put(hidden_ref, pl.ds(t, seqs, stride=span), state)
        return state

    lax.fori_loop(0, span, final, carry, unroll=8)

    @pl.loop(0, rows // ROWS)
    def _(q):
        at = block(q, ROWS)
        mixed_ref[at, :] = (get(hidden_ref, at) * gelu(branch_ref[at, :])).astype(BF16)


def backward_kernel(
    span,
    block_part_in,
    own_in,
    low_in,
    w_out_in,
    branch_in,
    hidden_in,
    pre_in,
    pad_in,
    normed_in,
    mixed_in,
    carry_ref,
    sums_ref,
    taps_ref,
    vec_ref,
    gates_ref,
    block_out,
    rec_out,
    gates_out,
    grad_branch_ref,
    input_ref,
    acc_ref,
    part,
    inbox,
    out,
    send_up,
    send_down,
    recv_up,
    recv_down,
    own_ref,
    resid_low,
    w_out_ref,
    branch_ref,
    hidden_ref,
    pre_ref,
    pad_ref,
    normed_ref,
    mixed_ref,
    a_ref,
    gd_ref,
    grad_ref,
    direct_ref,
    gpad_ref,
    heads_ref,
    low_ref,
    gates_grad,
    stage_ref,
    mine_ref,
    entries_ref,
    head_ref,
    head_in,
    load_sem,
    part_sem,
    store_sem,
    gates_sem,
    stage_sem,
    send1,
    recv1,
    send_t,
    recv_t,
):
    seqs, width = carry_ref.shape
    taps = taps_ref.shape[0]
    rows = seqs * span
    devices, me = lax.axis_size("seq"), lax.axis_index("seq")
    n, z = lax.axis_size("mp"), lax.axis_index("mp")
    chunks = rows // CHUNK
    size = GROUP * CHUNK
    held = part.shape[0] // size
    groups = chunks // GROUP
    sems = (send_up, send_down, recv_up, recv_down)
    local = pltpu.make_async_copy

    def part_load(g):
        slot = lax.rem(g, held)
        return local(block_part_in.at[block(g, size)], part.at[block(slot, size)], part_sem.at[slot])

    loads = [
        local(source, target, load_sem.at[i])
        for i, (source, target) in enumerate(
            (
                (own_in, own_ref),
                (low_in, resid_low),
                (w_out_in, w_out_ref),
                (pre_in, pre_ref),
                (branch_in, branch_ref),
                (hidden_in, hidden_ref),
                (pad_in, pad_ref),
                (mixed_in, mixed_ref),
                (normed_in, normed_ref),
            )
        )
    ]
    part_load(0).start()
    for copy in loads[:6]:
        copy.start()
    for g in range(1, held):
        part_load(g).start()
    for copy in loads[6:]:
        copy.start()
    acc_ref[...] = jnp.zeros_like(acc_ref)
    enter_all(("seq", "mp"))

    def decay(at):
        recall = jax.nn.sigmoid(pre_ref[at, :width])
        log_a = (-RATE_SCALE * vec_ref[1:2, :]) * recall
        return recall, log_a, jnp.exp(log_a)

    def piece_direct(s):
        @pl.when(s == 0)
        def _():
            for copy in loads[1:6]:
                copy.wait()

        grad_ref[...] = matmul_back(resid_low[block(s, span), :], w_out_ref[...])

        @pl.loop(0, span // ROWS)
        def _(q):
            at = block(s * (span // ROWS) + q, ROWS)
            put(a_ref, at, decay(at)[2])
            act, slope = gelu_both(branch_ref[at, :])
            grad = grad_ref[block(q, ROWS), :]
            put(gd_ref, at, grad * act)
            grad_branch_ref[at, :] = (grad * get(hidden_ref, at) * slope).astype(BF16)

    def at_time(ref, t):
        return get(ref, pl.ds(t, seqs, stride=span))

    zero = jnp.zeros((seqs, width), F32)
    entry_copies = to_all("seq", mine_ref, entries_ref, send1, recv1)

    def piece_entry(_):
        def step(k, through):
            t = span - 1 - k
            return at_time(a_ref, t) * (at_time(gd_ref, t) + through)

        mine_ref[...] = lax.fori_loop(0, span, step, zero, unroll=8)
        entries_ref[me] = mine_ref[...]
        for copy in entry_copies:
            copy.start()

    def piece_state(_):
        for copy in entry_copies:
            copy.wait()

        def back_step(k, through):
            j = devices - 1 - k
            return jnp.where(j > me, entries_ref[j] + sums_ref[j, 0] * through, through)

        incoming = lax.fori_loop(0, devices - 1, back_step, zero)

        def final(k, through):
            t = span - 1 - k
            grad = at_time(gd_ref, t) + through
            put(gd_ref, pl.ds(t, seqs, stride=span), grad)
            return at_time(a_ref, t) * grad

        lax.fori_loop(0, span, final, incoming, unroll=8)

    def add(k, value):
        acc_ref[k] += fold(value)

    def piece_gates(s):
        @pl.when(s == 0)
        def _():
            loads[6].wait()

        @pl.loop(0, span // ROWS)
        def _(q):
            at = block(s * (span // ROWS) + q, ROWS)
            part_rows = pad_ref[s, pl.ds(pl.multiple_of(q * ROWS, ROWS), ROWS + TILE), :]
            conv = vec_ref[0:1, :]
            for k in range(taps):
                first = TILE - (taps - 1) + k
                conv = conv + taps_ref[k : k + 1, :] * part_rows[first : first + ROWS]
            heads_ref[at, :] = conv.astype(BF16)
            recall, log_a, a = decay(at)
            gate = jax.nn.sigmoid(pre_ref[at, width:])
            square = one_minus_square(log_a, a)
            inverse = lax.rsqrt(square)
            root = jnp.sqrt(square)
            grad = get(gd_ref, at)
            hidden = get(hidden_ref, at)
            before_at = pl.multiple_of(jnp.maximum(s * span + q * ROWS - TILE, 0), TILE)
            earlier = get(hidden_ref, pl.ds(before_at, TILE))
            first_row = jnp.where(q == 0, carry_ref[pl.ds(s, 1), :], earlier[TILE - 1 :])
            place = lax.broadcasted_iota(jnp.int32, (ROWS, width), 0)
            prev = jnp.where(place == 0, first_row, pltpu.roll(hidden, 1, 0))
            grad_log = grad * a * (prev - gate * conv * a * inverse)
            through = grad_log * recall
            pre_r = through * (1.0 - recall) * (-RATE_SCALE * vec_ref[1:2, :])
            direct = grad * root * gate
            pre_i = direct * conv * (1.0 - gate)
            low_ref[at, :width] = pre_r.astype(BF16)
            low_ref[at, width:] = pre_i.astype(BF16)
            direct_ref[block(q, ROWS), :] = direct
            add(0, through)
            add(1, pre_r)
            add(2, pre_i)

        whole = direct_ref[...] + matmul_back(low_ref[block(s, span), :], gates_ref[...])
        gpad_ref[s, pl.ds(0, span), :] = whole
        head_ref[s] = whole[:TILE]

    head_copy = to_one("seq", -1, head_ref, head_in, send_t.at[0], recv_t.at[0])

    def piece_head(_):
        head_copy.start()

    def piece_taps(s):
        @pl.loop(0, span // ROWS)
        def _(q):
            at = pl.multiple_of(q * ROWS, ROWS)
            part_rows = pad_ref[s, pl.ds(at, ROWS + TILE), :]
            grad = gpad_ref[s, pl.ds(at, ROWS), :]
            add(3, grad)
            for k in range(taps):
                first = TILE - (taps - 1) + k
                add(4 + k, grad * part_rows[first : first + ROWS])

    def piece_tail(_):
        head_copy.wait()
        for s in range(seqs):
            gpad_ref[s, pl.ds(span, TILE), :] = jnp.where(me == devices - 1, 0.0, head_in[s])

    def piece_input(s):
        @pl.loop(0, span // ROWS)
        def _(q):
            part_rows = gpad_ref[s, pl.ds(pl.multiple_of(q * ROWS, ROWS), ROWS + TILE), :]
            total = taps_ref[taps - 1 : taps, :] * part_rows[0:ROWS]
            for k in range(taps - 1):
                first = taps - 1 - k
                total = total + taps_ref[k : k + 1, :] * part_rows[first : first + ROWS]
            input_ref[block(s * (span // ROWS) + q, ROWS), :] = total.astype(BF16)

    def contract(left, right):
        return lax.dot_general(left, right, CONTRACT_ROWS, preferred_element_type=F32)

    def gates_store(i):
        return local(gates_grad.at[i], gates_out.at[i], gates_sem.at[i])

    def piece_gates_grad(i):
        @pl.when(i == 0)
        def _():
            gates_grad[0] = contract(heads_ref[...], low_ref[:, :width])

        @pl.when(i == 1)
        def _():
            gates_grad[1] = contract(heads_ref[...], low_ref[:, width:])

        gates_store(i).start()

    tall = resid_low.shape[1] // WEIGHT_STEPS

    def stage_store(i):
        at = block(lax.rem(i, WEIGHT_STEPS), tall)
        slot = lax.rem(i, 2)
        return local(stage_ref.at[slot], rec_out.at[i // WEIGHT_STEPS, at], stage_sem.at[slot])

    def piece_weight(i):
        @pl.when(i == 0)
        def _():
            loads[7].wait()
            loads[8].wait()

        @pl.when(i >= 2)
        def _():
            stage_store(i - 2).wait()

        at = block(lax.rem(i, WEIGHT_STEPS), tall)
        slot = lax.rem(i, 2)
        for which, (left, right) in enumerate(
            ((resid_low, mixed_ref), (normed_ref, grad_branch_ref), (normed_ref, input_ref))
        ):
            @pl.when(i // WEIGHT_STEPS == which)
            def _():
                stage_ref[slot] = contract(left[:, at], right[...])

        stage_store(i).start()

    weights = 3 * WEIGHT_STEPS
    plan = []
    begin = 0
    for work, times, gap in (
        (piece_direct, seqs, 0),
        (piece_entry, 1, 1),
        (piece_state, 1, 0),
        (piece_gates, seqs, 0),
        (piece_head, 1, 0),
        (piece_taps, seqs, 0),
        (piece_tail, 1, 0),
        (piece_input, seqs, 0),
        (piece_gates_grad, 2, 0),
        (piece_weight, weights, 0),
    ):
        plan.append((work, begin, times))
        begin += times + gap

    def run(step):
        for work, first, times in plan:
            @pl.when(jnp.logical_and(step >= first, step < first + times))
            def _():
                work(step - first)

    def before(k):
        @pl.when(k == 0)
        def _():
            loads[0].wait()

        @pl.when(jnp.logical_and(lax.rem(k, GROUP) == 0, k < chunks))
        def _():
            part_load(k // GROUP).wait()

        g = (k - out.shape[0]) // GROUP - 1 + held

        @pl.when(
            jnp.logical_and(
                jnp.logical_and(k >= out.shape[0] + GROUP, lax.rem(k - out.shape[0], GROUP) == 0),
                g < groups,
            )
        )
        def _():
            part_load(g).start()

        run(k)

    def root(c, slot, total):
        out[slot] = own_ref[block(c // 2, CHUNK), :] + total

    def store(c, slot):
        return local(out.at[slot], block_out.at[block(c, CHUNK)], store_sem.at[slot])

    def arrive(c, slot):
        store(c, slot).start()

    def leave(c, slot):
        store(c, slot).wait()

    line_sum(
        "mp", chunks, held * GROUP, part, inbox, out, sems, before, root, arrive, leave
    )

    @pl.loop(chunks + out.shape[0], max(begin, chunks + out.shape[0]))
    def _(k):
        run(k)

    stage_store(weights - 2).wait()
    stage_store(weights - 1).wait()
    gates_store(0).wait()
    gates_store(1).wait()


def backward_call(span, *args):
    block_part = args[0]
    low, w_out, branch, hidden, pre, padded, normed, mixed, carry, sums, taps = args[2:13]
    rows, model = block_part.shape
    seqs, width = carry.shape
    devices = lax.axis_size("seq")
    ring = ring_size("mp")
    held = 3 * GROUP * CHUNK
    dma = pltpu.SemaphoreType.DMA
    columns = pltpu.VMEM((width // LANES, rows, LANES), F32)
    return pl.pallas_call(
        functools.partial(backward_kernel, span),
        out_shape=(
            shape((rows, model)),
            shape((3, model, width)),
            shape((2, width, width)),
            shape((rows, width), BF16),
            shape((rows, width), BF16),
            shape((4 + taps.shape[0], TILE, width)),
        ),
        in_specs=[HBM] * 10 + [VMEM] * 5,
        out_specs=(HBM,) * 3 + (VMEM,) * 3,
        scratch_shapes=line_scratch("mp", held, model)
        + [
            pltpu.VMEM((rows // 2, model), F32),
            pltpu.VMEM((rows, model), BF16),
            pltpu.VMEM((width, model), BF16),
            pltpu.VMEM((rows, width), F32),
            pltpu.VMEM(hidden.shape, F32),
            pltpu.VMEM(pre.shape, F32),
            pltpu.VMEM(padded.shape, F32),
            pltpu.VMEM((rows, model), BF16),
            pltpu.VMEM((rows, width), BF16),
            columns,
            columns,
            pltpu.VMEM((span, width), F32),
            pltpu.VMEM((span, width), F32),
            pltpu.VMEM((seqs, span + TILE, width), F32),
            pltpu.VMEM((rows, width), BF16),
            pltpu.VMEM((rows, 2 * width), BF16),
            pltpu.VMEM((2, width, width), F32),
            pltpu.VMEM((2, model // WEIGHT_STEPS, width), F32),
            pltpu.VMEM((seqs, width), F32),
            pltpu.VMEM((devices, seqs, width), F32),
            pltpu.VMEM((seqs, TILE, width), F32),
            pltpu.VMEM((seqs, TILE, width), F32),
            dma((9,)),
            dma((3,)),
            dma((ring,)),
            dma((2,)),
            dma((2,)),
            dma((devices - 1,)),
            dma((devices - 1,)),
            dma((1,)),
            dma((1,)),
        ],
        compiler_params=params(1, 63),
        cost_estimate=cost(200),
        name="backward",
    )(*args)


def line_sum(axis, total, period, part, inbox, out, sems, before, root, arrive, leave):
    send_up, send_down, recv_up, recv_down = sems
    n, z = lax.axis_size(axis), lax.axis_index(axis)
    depth = n // 2
    ring = out.shape[0]

    def root_of(c):
        return depth - 1 + lax.rem(c, 2)

    def up(c, step, side):
        slot = lax.rem(c, ring)
        return pltpu.make_async_remote_copy(
            src_ref=part.at[block(lax.rem(c, period), CHUNK)],
            dst_ref=inbox.at[side, slot],
            send_sem=send_up.at[slot],
            recv_sem=recv_up.at[side, slot],
            device_id={axis: z + step},
            device_id_type=MESH,
        )

    def down(c, step, side):
        slot = lax.rem(c, ring)
        return pltpu.make_async_remote_copy(
            src_ref=out.at[slot],
            dst_ref=out.at[slot],
            send_sem=send_down.at[side, slot],
            recv_sem=recv_down.at[slot],
            device_id={axis: z + step},
            device_id_type=MESH,
        )

    inner = jnp.logical_and(z > 0, z < n - 1)

    @pl.loop(0, total + ring)
    def _(k):
        @pl.when(k >= ring)
        def _():
            c = k - ring
            r = root_of(c)
            step = jnp.where(z < r, 1, -1)
            side = jnp.where(z < r, 0, 1)

            @pl.when(z == r)
            def _():
                down(c, -1, 0).wait_send()
                down(c, 1, 1).wait_send()

            @pl.when(z != r)
            def _():
                up(c, step, side).wait_send()

            @pl.when(jnp.logical_and(z != r, inner))
            def _():
                down(c, -step, side).wait_send()

            leave(c, lax.rem(c, ring))

        before(k)

        for i in reversed(range(n + 1)):
            c = k - SKEW * i
            valid = jnp.logical_and(c >= 0, c < total)
            c = jnp.clip(c, 0, total - 1)
            at = block(lax.rem(c, period), CHUNK)
            slot = lax.rem(c, ring)
            r = root_of(c)
            step = jnp.where(z < r, 1, -1)
            side = jnp.where(z < r, 0, 1)
            if i > depth:
                here = jnp.logical_and(z != r, jnp.abs(z - r) == i - depth)

                @pl.when(jnp.logical_and(valid, here))
                def _():
                    down(c, -step, side).wait_recv()

                    @pl.when(inner)
                    def _():
                        down(c, -step, side).start()

                    arrive(c, slot)
            elif i == depth:

                @pl.when(jnp.logical_and(valid, z == r))
                def _():
                    up(c, 1, 0).wait_recv()
                    up(c, -1, 1).wait_recv()
                    root(c, slot, part[at, :] + inbox[0, slot] + inbox[1, slot])
                    down(c, -1, 0).start()
                    down(c, 1, 1).start()
                    arrive(c, slot)
            else:
                here = jnp.where(z < r, z, n - 1 - z) == i

                @pl.when(jnp.logical_and(valid, jnp.logical_and(z != r, here)))
                def _():
                    if i > 0:
                        up(c, step, side).wait_recv()
                        part[at, :] += inbox[side, slot]
                    up(c, step, side).start()


def ring_size(axis):
    return SKEW * lax.axis_size(axis) + 4


def line_scratch(axis, rows, model):
    dma = pltpu.SemaphoreType.DMA
    ring = ring_size(axis)
    return [
        pltpu.VMEM((rows, model), F32),
        pltpu.VMEM((2, ring, CHUNK, model), F32),
        pltpu.VMEM((ring, CHUNK, model), F32),
        dma((ring,)),
        dma((2, ring)),
        dma((2, ring)),
        dma((ring,)),
    ]


def mean_square(x):
    return lax.rsqrt(jnp.mean(x * x, axis=-1, keepdims=True) + EPS)


def nothing(*_):
    pass


def fold(value):
    total = value[0:TILE]
    for i in range(1, value.shape[0] // TILE):
        total = total + value[i * TILE : (i + 1) * TILE]
    return total


def norm_grad(value, gain, grad, acc_ref):
    q = mean_square(value)
    e = gain * grad
    acc_ref[...] += fold(grad * value * q)
    return q * e - value * (q * q * q) * jnp.mean(e * value, axis=-1, keepdims=True)


def middle_kernel(
    mixed_in,
    w_out_in,
    x_in,
    og_in,
    gain_ref,
    w_gate_in,
    w_up_in,
    w_down_in,
    normed_out,
    hidden_out,
    gate_out,
    up_out,
    glow_out,
    block_out,
    low_out,
    own_grad_out,
    own_ref,
    acc_ref,
    part,
    inbox,
    out,
    send_up,
    send_down,
    recv_up,
    recv_down,
    mixed,
    w_out,
    w_gate,
    w_up,
    w_down,
    normed,
    rows_ref,
    og_ref,
    glow,
    gate_val,
    up_val,
    grad_hidden,
    hidden,
    grad_gate,
    grad_up,
    block_part,
    low,
    weight_sem,
    row_sem,
    og_sem,
    act_sem,
    low_sem,
    own_sem,
):
    n, z = lax.axis_size("mp"), lax.axis_index("mp")
    count = part.shape[0] // CHUNK
    size = GROUP * CHUNK
    groups = count // GROUP
    ring = out.shape[0]
    sems = (send_up, send_down, recv_up, recv_down)
    local = pltpu.make_async_copy

    loads = [
        local(source, target, weight_sem.at[i])
        for i, (source, target) in enumerate(
            (
                (mixed_in, mixed),
                (w_out_in, w_out),
                (w_gate_in, w_gate),
                (w_up_in, w_up),
                (w_down_in, w_down),
            )
        )
    ]
    for copy in loads:
        copy.start()

    def og_load(g):
        return local(og_in.at[block(g, size)], og_ref, og_sem.at[0])

    og_load(0).start()
    enter_all(("mp",))
    acc_ref[...] = jnp.zeros_like(acc_ref)
    loads[0].wait()
    loads[1].wait()

    def is_root(c):
        return z == n // 2 - 1 + lax.rem(c, 2)

    def row_load(source, c):
        slot = lax.rem(c, ring)
        at = block(lax.rem(c, count), CHUNK)
        return local(source.at[at], rows_ref.at[slot], row_sem.at[slot])

    acts = (
        (normed, normed_out),
        (glow, glow_out),
        (hidden, hidden_out),
        (grad_gate, gate_out),
        (grad_up, up_out),
        (block_part, block_out),
    )

    def act_store(i, g):
        source, target = acts[i]
        source = source.at[lax.rem(g, 2)] if i == 0 else source
        return local(source, target.at[block(g, size)], act_sem.at[i])

    def at_tick(k, first, work):
        g = (k - first) // GROUP

        @pl.when(
            jnp.logical_and(
                jnp.logical_and(k >= first, k < first + GROUP * groups),
                lax.rem(k - first, GROUP) == 0,
            )
        )
        def _():
            work(g)

    def project(g):
        part[block(g, size), :] = dot(mixed[block(g, size), :], w_out[...])

    def piece_gate(g):
        @pl.when(g == 0)
        def _():
            for copy in loads[2:]:
                copy.wait()

        gate_val[...] = dot(normed[lax.rem(g, 2)], w_gate[...])
        act_store(0, g).start()

    def piece_up(g):
        up_val[...] = dot(normed[lax.rem(g, 2)], w_up[...])

        @pl.when(g > 0)
        def _():
            for i in range(1, 6):
                act_store(i, g - 1).wait()

    def piece_low(g):
        og_load(g).wait()

        @pl.loop(0, size // ROWS)
        def _(q):
            glow[block(q, ROWS), :] = og_ref[block(q, ROWS), :].astype(BF16)

        @pl.when(g + 1 < groups)
        def _():
            og_load(g + 1).start()

        act_store(1, g).start()
        act_store(0, g).wait()

    def piece_hidden(g):
        grad_hidden[...] = matmul_back(glow[...], w_down[...])

    def piece_act(g):
        @pl.loop(0, size // CHUNK)
        def _(q):
            at = block(q, CHUNK)
            up = up_val[at, :]
            grad = grad_hidden[at, :]
            act, slope = gelu_both(gate_val[at, :])
            hidden[at, :] = (act * up).astype(BF16)
            grad_gate[at, :] = (grad * up * slope).astype(BF16)
            grad_up[at, :] = (grad * act).astype(BF16)

        for i in range(2, 5):
            act_store(i, g).start()

    def piece_down(g):
        block_part[...] = dot(hidden[...], w_down[...])
        act_store(5, g).start()

    def piece_back_gate(g):
        part[block(g, size), :] = matmul_back(grad_gate[...], w_gate[...])

    def piece_back_up(g):
        part[block(g, size), :] += matmul_back(grad_up[...], w_up[...])

    first = GROUP + SKEW * n

    def before(k):
        @pl.when(jnp.logical_and(k < count, is_root(k)))
        def _():
            row_load(x_in, k).start()

        @pl.when(
            jnp.logical_and(jnp.logical_and(k >= count, k < 2 * count), is_root(k))
        )
        def _():
            row_load(og_in, k).start()

        at_tick(k, 0, project)
        at_tick(k, first, piece_gate)
        at_tick(k, first + 1, piece_up)
        at_tick(k, first + 2, piece_low)
        at_tick(k, first + 3, piece_hidden)
        at_tick(k, first + 4, piece_act)
        at_tick(k, first + 6, piece_down)
        at_tick(k, GROUP + ring, piece_back_gate)
        at_tick(k, GROUP + ring + 2, piece_back_up)

    def root(c, slot, total):
        j = lax.rem(c, count)
        mine = block(j // 2, CHUNK)
        row_load(x_in, c).wait()

        @pl.when(c < count)
        def _():
            value = rows_ref[slot] + total
            own_ref[mine, :] = value
            out[slot] = (value * mean_square(value) * gain_ref[...]).astype(BF16).astype(F32)

        @pl.when(c >= count)
        def _():
            back = norm_grad(own_ref[mine, :], gain_ref[...], total, acc_ref)
            out[slot] = rows_ref[slot] + back

    def low_store(c, slot):
        at = block(lax.rem(c, count), CHUNK)
        return local(low.at[slot], low_out.at[at], low_sem.at[slot])

    def own_store(c, slot):
        at = block(lax.rem(c, count) // 2, CHUNK)
        return local(out.at[slot], own_grad_out.at[at], own_sem.at[slot])

    def arrive(c, slot):
        @pl.when(c < count)
        def _():
            normed[lax.rem(c // GROUP, 2), block(lax.rem(c, GROUP), CHUNK), :] = out[slot].astype(BF16)

        @pl.when(c >= count)
        def _():
            low[slot] = out[slot].astype(BF16)
            low_store(c, slot).start()

            @pl.when(is_root(c))
            def _():
                own_store(c, slot).start()

    def leave(c, slot):
        @pl.when(c >= count)
        def _():
            low_store(c, slot).wait()

            @pl.when(is_root(c))
            def _():
                own_store(c, slot).wait()

    line_sum("mp", 2 * count, count, part, inbox, out, sems, before, root, arrive, leave)

    for i in range(1, 6):
        act_store(i, groups - 1).wait()


def middle_call(*args):
    mixed, w_out, x, og, gain, w_gate, w_up, w_down = args
    rows, model = x.shape
    width, hidden = mixed.shape[1], w_gate.shape[1]
    size = GROUP * CHUNK
    dma = pltpu.SemaphoreType.DMA
    ring = ring_size("mp")
    act = shape((rows, hidden), BF16)
    tall = shape((rows, model), BF16)
    return pl.pallas_call(
        middle_kernel,
        out_shape=(
            tall,
            act,
            act,
            act,
            tall,
            shape((rows, model)),
            tall,
            shape((rows // 2, model)),
            shape((rows // 2, model)),
            shape((TILE, model)),
        ),
        in_specs=[HBM] * 4 + [VMEM] + [HBM] * 3,
        out_specs=(HBM,) * 8 + (VMEM,) * 2,
        scratch_shapes=line_scratch("mp", rows, model)
        + [
            pltpu.VMEM((rows, width), BF16),
            pltpu.VMEM((width, model), BF16),
            pltpu.VMEM((model, hidden), BF16),
            pltpu.VMEM((model, hidden), BF16),
            pltpu.VMEM((hidden, model), BF16),
            pltpu.VMEM((2, size, model), BF16),
            pltpu.VMEM((ring, CHUNK, model), F32),
            pltpu.VMEM((size, model), F32),
            pltpu.VMEM((size, model), BF16),
            pltpu.VMEM((size, hidden), F32),
            pltpu.VMEM((size, hidden), F32),
            pltpu.VMEM((size, hidden), F32),
            pltpu.VMEM((size, hidden), BF16),
            pltpu.VMEM((size, hidden), BF16),
            pltpu.VMEM((size, hidden), BF16),
            pltpu.VMEM((size, model), F32),
            pltpu.VMEM((ring, CHUNK, model), BF16),
            dma((5,)),
            dma((ring,)),
            dma((1,)),
            dma((6,)),
            dma((ring,)),
            dma((ring,)),
        ],
        compiler_params=params(2, 63),
        cost_estimate=cost(400),
        name="middle",
    )(*args)


def last_kernel(
    own_grad_in,
    x_in,
    grad_branch_in,
    input_in,
    w_branch_in,
    w_input_in,
    gain_ref,
    other_acc,
    grad_out,
    norm_ref,
    part,
    inbox,
    out,
    send_up,
    send_down,
    recv_up,
    recv_down,
    own_grad_ref,
    x_ref,
    grad_branch,
    input_low,
    w_branch,
    w_input,
    load_sem,
    store_sem,
    acc_ref,
    mine_ref,
    seq_in,
    mp_in,
    send_s,
    recv_s,
    send_m,
    recv_m,
):
    count = part.shape[0] // CHUNK
    size = GROUP * CHUNK
    sems = (send_up, send_down, recv_up, recv_down)
    local = pltpu.make_async_copy

    loads = [
        local(source, target, load_sem.at[i])
        for i, (source, target) in enumerate(
            (
                (grad_branch_in, grad_branch),
                (w_branch_in, w_branch),
                (input_in, input_low),
                (w_input_in, w_input),
                (own_grad_in, own_grad_ref),
                (x_in, x_ref),
            )
        )
    ]
    for copy in loads:
        copy.start()
    acc_ref[...] = jnp.zeros_like(acc_ref)
    mine_ref[...] = jnp.zeros_like(mine_ref)
    enter_all(("seq", "mp"))
    for copy in loads[:4]:
        copy.wait()

    def before(k):
        @pl.when(jnp.logical_and(lax.rem(k, 4) == 0, k // 4 < count // GROUP))
        def _():
            at = block(k // 4, size)
            part[at, :] = matmul_back(grad_branch[at, :], w_branch[...])
            part[at, :] += matmul_back(input_low[at, :], w_input[...])

        @pl.when(k == 1)
        def _():
            for copy in loads[4:]:
                copy.wait()

    def root(c, slot, total):
        back = norm_grad(x_ref[block(c, CHUNK), :], gain_ref[...], total, acc_ref)
        out[slot] = own_grad_ref[block(c // 2, CHUNK), :] + back

    def store(c, slot):
        return local(out.at[slot], grad_out.at[block(c, CHUNK)], store_sem.at[slot])

    def arrive(c, slot):
        store(c, slot).start()

    def leave(c, slot):
        store(c, slot).wait()

    line_sum("mp", count, count, part, inbox, out, sems, before, root, arrive, leave)

    mine_ref[0, 0:1, :] = jnp.sum(acc_ref[...], axis=0, keepdims=True)
    mine_ref[0, 1:2, :] = jnp.sum(other_acc[...], axis=0, keepdims=True)
    for i, (axis, place, send, recv) in enumerate(
        (("seq", seq_in, send_s, recv_s), ("mp", mp_in, send_m, recv_m))
    ):
        if i == 1:
            mine_ref[1] = jnp.sum(seq_in[...], axis=0)
        place[lax.axis_index(axis)] = mine_ref[i]
        copies = to_all(axis, mine_ref.at[i], place, send, recv)
        for copy in copies:
            copy.start()
        for copy in copies:
            copy.wait()
    norm_ref[...] = jnp.sum(mp_in[...], axis=0)


def enter_all(axes):
    barrier = pltpu.get_barrier_semaphore()
    count = 0
    for axis in axes:
        size, me = lax.axis_size(axis), lax.axis_index(axis)
        for d in range(1, size):
            pl.semaphore_signal(
                barrier, 1, device_id={axis: lax.rem(me + d, size)}, device_id_type=MESH
            )
        count += size - 1
    pl.semaphore_wait(barrier, count)


def cost(micros):
    return pl.CostEstimate(flops=int(micros * 1e9), bytes_accessed=1 << 20, transcendentals=0)


def last_call(*args):
    x, grad_branch = args[1:3]
    rows, model = x.shape
    width = grad_branch.shape[1]
    dma = pltpu.SemaphoreType.DMA
    nseq, nmp = lax.axis_size("seq"), lax.axis_size("mp")
    return pl.pallas_call(
        last_kernel,
        out_shape=(shape((rows, model)), shape((TILE, model))),
        in_specs=[HBM] * 6 + [VMEM] * 2,
        out_specs=(HBM, VMEM),
        scratch_shapes=line_scratch("mp", rows, model)
        + [
            pltpu.VMEM((rows // 2, model), F32),
            pltpu.VMEM((rows, model), F32),
            pltpu.VMEM((rows, width), BF16),
            pltpu.VMEM((rows, width), BF16),
            pltpu.VMEM((model, width), BF16),
            pltpu.VMEM((model, width), BF16),
            dma((6,)),
            dma((ring_size("mp"),)),
            pltpu.VMEM((TILE, model), F32),
            pltpu.VMEM((2, TILE, model), F32),
            pltpu.VMEM((nseq, TILE, model), F32),
            pltpu.VMEM((nmp, TILE, model), F32),
            dma((nseq - 1,)),
            dma((nseq - 1,)),
            dma((nmp - 1,)),
            dma((nmp - 1,)),
        ],
        compiler_params=params(4, 62),
        cost_estimate=cost(200),
        name="last_sums",
    )(*args)


def weight_kernel(plan, lefts, *refs):
    left_refs, right_refs = refs[:lefts], refs[lefts:-2]
    out_ref, turned = refs[-2:]
    j = pl.program_id(0)
    begin = 0
    held = None
    for (left, blocks), right in zip(plan, right_refs):
        if left != held:
            held = left

            @pl.when(j == begin)
            def _():
                rows = left_refs[left].shape[0]
                for i in range(left_refs[left].shape[1] // TURN):
                    at = slice(i * TURN, (i + 1) * TURN)
                    turned[at, :] = left_refs[left][:, at].T

        @pl.when(jnp.logical_and(j >= begin, j < begin + blocks))
        def _():
            size = turned.shape[0] // 4

            @pl.loop(0, 4)
            def _(i):
                out_ref[block(i, size), :] = dot(turned[block(i, size), :], right[...])

        begin += blocks


def weight_grads(lefts, pairs, width):
    rows, model = lefts[0].shape
    plan = tuple((left, right.shape[1] // width) for left, right in pairs)
    steps = sum(blocks for _, blocks in plan)
    whole = pl.BlockSpec((rows, model), lambda j: (0, 0))
    specs = [whole] * len(lefts)
    begin = 0
    for _, blocks in plan:
        specs.append(
            pl.BlockSpec(
                (rows, width),
                lambda j, first=begin, n=blocks: (0, jnp.clip(j - first, 0, n - 1)),
            )
        )
        begin += blocks
    return pl.pallas_call(
        functools.partial(weight_kernel, plan, len(lefts)),
        out_shape=shape((model, steps * width)),
        grid=(steps,),
        in_specs=specs,
        out_specs=pl.BlockSpec((model, width), lambda j: (0, j)),
        scratch_shapes=[pltpu.VMEM((model, rows), BF16)],
        compiler_params=pltpu.CompilerParams(vmem_limit_bytes=60 << 20),
        cost_estimate=cost(30),
        name="weight_grads",
    )(*lefts, *(right for _, right in pairs))


def params(collective, megabytes=60):
    return pltpu.CompilerParams(
        collective_id=collective, has_side_effects=True, vmem_limit_bytes=megabytes << 20
    )


def shape(dims, dtype=F32):
    return jax.ShapeDtypeStruct(dims, dtype)


def recurrence_forward(span, *args):
    x, _, w_branch = args[:3]
    rows, model = x.shape
    seqs, width = rows // span, w_branch.shape[1]
    devices = lax.axis_size("seq")
    dma = pltpu.SemaphoreType.DMA
    return pl.pallas_call(
        functools.partial(forward_kernel, span),
        out_shape=(
            shape((rows, model), BF16),
            shape((rows, width)),
            shape((seqs, span + TILE, width)),
            shape((rows, 2 * width)),
            shape((width // LANES, rows, LANES)),
            shape((rows, width), BF16),
            shape((seqs, width)),
            shape((devices, 2, seqs, width)),
            shape((width, 2 * width), BF16),
            shape((TILE, width)),
        ),
        in_specs=[VMEM] * len(args),
        out_specs=(VMEM,) * 10,
        scratch_shapes=[
            pltpu.VMEM((width // LANES, rows, LANES), F32),
            pltpu.VMEM((width // LANES, rows, LANES), F32),
            pltpu.VMEM((span, width), F32),
            pltpu.VMEM((seqs, TILE, width), F32),
            pltpu.VMEM((seqs, TILE, width), F32),
            pltpu.VMEM((2, seqs, width), F32),
            dma((devices - 1,)),
            dma((devices - 1,)),
            dma((1,)),
            dma((1,)),
        ],
        compiler_params=params(0),
        cost_estimate=cost(50),
        name="recurrence_forward",
    )(*args)


def widen(array, width):
    short = width - array.shape[-1]
    if short == 0:
        return array
    return jnp.pad(array, [(0, 0)] * (array.ndim - 1) + [(0, short)])


def per_device(
    stream,
    norm_in,
    w_branch,
    w_input,
    conv_kernel,
    conv_bias,
    gate_r,
    bias_r,
    gate_i,
    bias_i,
    decay_param,
    w_out,
    norm_mlp,
    w_gate,
    w_up,
    w_down,
    state_init,
    conv_init,
    fresh_rows,
    out_grad,
):
    seqs, span, model = stream.shape
    channels = w_branch.shape[1]
    mlp_dev = w_gate.shape[1]
    heads, head_width = gate_r.shape[:2]
    taps = conv_kernel.shape[0]
    edge = taps - 1
    rows = seqs * span
    devices = lax.axis_size("seq")
    position = lax.axis_index("seq")
    width = -(-channels // 128) * 128

    flat_in = stream.reshape(rows, model)
    flat_grad = out_grad.reshape(rows, model)
    w_branch_p = widen(w_branch, width)
    w_input_p = widen(w_input, width)
    w_out_p = jnp.pad(w_out, ((0, width - channels), (0, 0))) if width > channels else w_out
    taps_p = widen(conv_kernel, width)
    vec = jnp.stack([widen(v, width) for v in (conv_bias, decay_param, bias_r, bias_i)])

    normed, branch, padded, pre, hidden, mixed, carry, sums, gates, rates = recurrence_forward(
        span,
        flat_in,
        norm_in[None],
        w_branch_p,
        w_input_p,
        taps_p,
        vec,
        gate_r,
        gate_i,
        fresh_rows[:, None],
        widen(state_init, width),
        widen(conv_init, width),
    )
    (
        normed_mlp,
        hidden_mlp,
        grad_gate,
        grad_up,
        grad_low,
        block_part,
        resid_low,
        own_grad,
        own,
        norm_mlp_acc,
    ) = middle_call(mixed, w_out_p, flat_in, flat_grad, norm_mlp[None], w_gate, w_up, w_down)
    mlp_grads = weight_grads(
        (normed_mlp, grad_low), ((0, grad_gate), (0, grad_up), (1, hidden_mlp)), mlp_dev // 3
    )
    mlp_grads, resid_low = lax.optimization_barrier((mlp_grads, resid_low))
    mlp_grads = lax.psum_scatter(mlp_grads, "seq", scatter_dimension=0, tiled=True)
    block_out, rec_grads, gates_grad, grad_branch, input_low, acc = backward_call(
        span,
        block_part,
        own,
        resid_low,
        w_out_p,
        branch,
        hidden,
        pre,
        padded,
        normed,
        mixed,
        carry,
        sums,
        taps_p,
        rates,
        gates,
    )

    def blocks(array):
        return jnp.stack(
            [
                array[h * head_width : (h + 1) * head_width, h * head_width : (h + 1) * head_width]
                for h in range(heads)
            ]
        )

    def place(array):
        flat = array.reshape(-1)
        return jnp.pad(flat, (0, -flat.size % 1024)).reshape(-1, LANES)

    last = position == devices - 1
    last_hidden = hidden.reshape(-1, seqs, span, LANES)[:, :, -1]
    last_hidden = jnp.swapaxes(last_hidden, 0, 1).reshape(seqs, width)[:, :channels]
    final_state = jnp.where(last, last_hidden, 0.0)
    final_conv = jnp.where(last, padded[:, span + TILE - edge :, :channels], 0.0)
    pieces = (
        jnp.sum(acc, axis=1)[:, :channels],
        blocks(gates_grad[0]),
        blocks(gates_grad[1]),
        final_state,
        final_conv,
    )
    small = jnp.concatenate([place(piece) for piece in pieces], axis=0)
    small, rec_grads, grad_branch, mlp_grads = lax.optimization_barrier(
        (small, rec_grads, grad_branch, mlp_grads)
    )
    rec_grads = lax.psum_scatter(rec_grads, "seq", scatter_dimension=1, tiled=True)
    small = lax.psum(small, "seq")

    stream_grad, norm_grads = last_call(
        own_grad,
        flat_in,
        grad_branch,
        input_low,
        w_branch_p,
        w_input_p,
        norm_in[None],
        norm_mlp_acc,
    )
    summed = []
    begin = 0
    for piece in pieces:
        lines = -(-piece.size // 1024) * 8
        flat = small[begin : begin + lines].reshape(-1)
        summed.append(flat[: piece.size].reshape(piece.shape))
        begin += lines
    acc, gate_r_grad, gate_i_grad, final_state, final_conv = summed
    norm_in_grad = norm_grads[0]
    norm_mlp_grad = norm_grads[1]
    decay_grad = acc[0] * (RATE_SCALE * jax.nn.sigmoid(-decay_param))
    w_gate_grad = mlp_grads[:, :mlp_dev]
    w_up_grad = mlp_grads[:, mlp_dev : 2 * mlp_dev]
    w_down_grad = mlp_grads[:, 2 * mlp_dev :]
    w_out_grad, w_branch_grad, w_input_grad = rec_grads
    return (
        block_out.reshape(stream.shape),
        stream_grad.reshape(stream.shape),
        norm_in_grad,
        w_branch_grad[:, :channels],
        w_input_grad[:, :channels],
        acc[4:],
        acc[3],
        gate_r_grad,
        acc[1],
        gate_i_grad,
        acc[2],
        decay_grad,
        w_out_grad[:, :channels].T,
        norm_mlp_grad,
        w_gate_grad,
        w_up_grad,
        w_down_grad.T,
        final_state,
        final_conv,
    )


def solution(mesh):
    seq_rows = P(None, "seq", None)
    columns = P(None, "mp")
    channel = P("mp")
    return jax.shard_map(
        per_device,
        mesh=mesh,
        in_specs=(
            seq_rows,
            P(),
            columns,
            columns,
            columns,
            channel,
            P("mp", None, None),
            channel,
            P("mp", None, None),
            channel,
            channel,
            P("mp", None),
            P(),
            columns,
            columns,
            P("mp", None),
            columns,
            P(None, None, "mp"),
            P(),
            seq_rows,
        ),
        out_specs=(
            seq_rows,
            seq_rows,
            P(),
            P("seq", "mp"),
            P("seq", "mp"),
            columns,
            channel,
            P("mp", None, None),
            channel,
            P("mp", None, None),
            channel,
            channel,
            P("mp", "seq"),
            P(),
            P("seq", "mp"),
            P("seq", "mp"),
            P("mp", "seq"),
            columns,
            P(None, None, "mp"),
        ),
        check_vma=False,
    )
```

```python
import functools

import jax
import jax.numpy as jnp
from jax import lax
from jax.experimental import pallas as pl
from jax.experimental.pallas import tpu as pltpu
from jax.sharding import PartitionSpec as P

MESH = pl.DeviceIdType.MESH
RATE_SCALE = 8.0
EPS = 1e-06
GELU_C = 0.7978845608028654
GELU_K = 0.044715
CONTRACT_ROWS = (((0,), (0,)), ((), ()))
CONTRACT_LAST = (((1,), (1,)), ((), ()))
TILE = 8
LANES = 128
ROWS = 32
CHUNK = 16
SKEW = 2
GROUP = 16
WEIGHT_STEPS = 8
COPIES = 4
F32 = jnp.float32
BF16 = jnp.bfloat16
VMEM = pl.BlockSpec(memory_space=pltpu.VMEM)
HBM = pl.BlockSpec(memory_space=pl.ANY)


def dot(a, b):
    return jnp.dot(a, b, preferred_element_type=F32)


def matmul_back(a, b):
    return lax.dot_general(a, b, CONTRACT_LAST, preferred_element_type=F32)


def block(i, size):
    return pl.ds(pl.multiple_of(i * size, size), size)


def gelu(x):
    t = jnp.tanh(GELU_C * (x + GELU_K * (x * x * x)))
    return 0.5 * x * (1.0 + t)


def gelu_both(x):
    x2 = x * x
    t = jnp.tanh(GELU_C * (x + GELU_K * (x2 * x)))
    half = 0.5 * (1.0 + t)
    slope = half + 0.5 * x * (1.0 - t * t) * (GELU_C * (1.0 + (3.0 * GELU_K) * x2))
    return x * half, slope


def one_minus_square(log_a, a):
    y = 2.0 * log_a
    s = 1.0 + y * (1.0 / 8.0)
    for k in (7, 6, 5, 4, 3, 2):
        s = 1.0 + (y * (1.0 / k)) * s
    return jnp.where(y > -0.35, -y * s, 1.0 - a * a)


def get(ref, at):
    return jnp.concatenate([ref[j, at, :] for j in range(ref.shape[0])], axis=-1)


def put(ref, at, value):
    for j in range(ref.shape[0]):
        ref[j, at, :] = value[:, j * LANES : (j + 1) * LANES]


def to_all(axis, src, slots, send, recv):
    size, me = lax.axis_size(axis), lax.axis_index(axis)
    return [
        pltpu.make_async_remote_copy(
            src_ref=src,
            dst_ref=slots.at[me],
            send_sem=send.at[d - 1],
            recv_sem=recv.at[d - 1],
            device_id={axis: lax.rem(me + d, size)},
            device_id_type=MESH,
        )
        for d in range(1, size)
    ]


def to_one(axis, distance, src, dst, send, recv):
    size, me = lax.axis_size(axis), lax.axis_index(axis)
    return pltpu.make_async_remote_copy(
        src_ref=src,
        dst_ref=dst,
        send_sem=send,
        recv_sem=recv,
        device_id={axis: lax.rem(me + distance + size, size)},
        device_id_type=MESH,
    )


def spread_gates(blocks_ref, out_ref, start, width):
    heads, size = blocks_ref.shape[:2]
    for h in range(heads):
        block_h = blocks_ref[h].astype(F32)
        parts = [block_h]
        if h > 0:
            parts.insert(0, jnp.zeros((size, h * size), F32))
        if width > (h + 1) * size:
            parts.append(jnp.zeros((size, width - (h + 1) * size), F32))
        row = jnp.concatenate(parts, axis=1).astype(BF16)
        out_ref[h * size : (h + 1) * size, start : start + width] = row
    if width > heads * size:
        rest = jnp.zeros((width - heads * size, width), BF16)
        out_ref[heads * size : width, start : start + width] = rest


def forward_kernel(
    span,
    x_ref,
    gain_ref,
    w_branch_ref,
    w_input_ref,
    taps_ref,
    vec_in,
    gate_r_ref,
    gate_i_ref,
    fresh_ref,
    state_ref,
    conv_init_ref,
    normed_ref,
    branch_ref,
    pad_ref,
    pre_ref,
    hidden_ref,
    mixed_ref,
    carry_ref,
    sums_ref,
    gates_ref,
    vec_ref,
    ends_ref,
    a_ref,
    b_ref,
    conv_ref,
    tail_ref,
    tail_in,
    mine_ref,
    send1,
    recv1,
    send_t,
    recv_t,
):
    seqs = state_ref.shape[0]
    width = taps_ref.shape[1]
    taps = taps_ref.shape[0]
    rows = seqs * span
    devices, me = lax.axis_size("seq"), lax.axis_index("seq")
    enter_all(("seq",))
    spread_gates(gate_r_ref, gates_ref, 0, width)
    spread_gates(gate_i_ref, gates_ref, width, width)
    vec_ref[0:1, :] = vec_in[0:1, :]
    vec_ref[1:2, :] = jax.nn.softplus(-vec_in[1:2, :])
    gate_bias = jnp.concatenate([vec_in[2:3, :], vec_in[3:4, :]], axis=1)
    keep = 1.0 - fresh_ref[...].astype(F32)

    group = 2 * span

    @pl.loop(0, rows // group)
    def _(g):
        @pl.loop(0, group // ROWS)
        def _(q):
            at = block(g * (group // ROWS) + q, ROWS)
            x = x_ref[at, :]
            scale = lax.rsqrt(jnp.mean(x * x, axis=-1, keepdims=True) + EPS)
            normed_ref[at, :] = (x * scale * gain_ref[...]).astype(BF16)

        conv = dot(normed_ref[block(g, group), :], w_input_ref[...])
        for j in range(group // span):
            pad_ref[g * (group // span) + j, pl.ds(TILE, span), :] = conv[
                j * span : (j + 1) * span
            ]

    for s in range(seqs):
        tail_ref[s] = pad_ref[s, pl.ds(span, TILE), :]
    tail_copy = to_one("seq", 1, tail_ref, tail_in, send_t.at[0], recv_t.at[0])
    tail_copy.start()

    @pl.loop(0, rows // group)
    def _(g):
        branch_ref[block(g, group), :] = dot(normed_ref[block(g, group), :], w_branch_ref[...])

    tail_copy.wait()
    lead = jnp.zeros((TILE - taps + 1, width), F32)
    for s in range(seqs):
        initial = jnp.concatenate([lead, conv_init_ref[s] * keep[s : s + 1, :]], axis=0)
        pad_ref[s, pl.ds(0, TILE), :] = jnp.where(me == 0, initial, tail_in[s])

    def conv_rows(s, q):
        part = pad_ref[s, pl.ds(pl.multiple_of(q * ROWS, ROWS), ROWS + TILE), :]
        total = vec_ref[0:1, :]
        for k in range(taps):
            first = TILE - (taps - 1) + k
            total = total + taps_ref[k : k + 1, :] * part[first : first + ROWS]
        return total

    @pl.loop(0, seqs)
    def _(s):
        @pl.loop(0, span // ROWS)
        def _(q):
            conv_ref[block(q, ROWS), :] = conv_rows(s, q)

        pre_ref[block(s, span), :] = (
            dot(conv_ref[...].astype(BF16), gates_ref[...]) + gate_bias
        )

        @pl.loop(0, span // ROWS)
        def _(q):
            at = block(s * (span // ROWS) + q, ROWS)
            conv = conv_ref[block(q, ROWS), :]
            recall = jax.nn.sigmoid(pre_ref[at, :width])
            gate = jax.nn.sigmoid(pre_ref[at, width:])
            log_a = (-RATE_SCALE * vec_ref[1:2, :]) * recall
            a = jnp.exp(log_a)
            put(a_ref, at, a)
            put(b_ref, at, jnp.sqrt(one_minus_square(log_a, a)) * gate * conv)

    def at_time(ref, t):
        return get(ref, pl.ds(t, seqs, stride=span))

    def local(t, value):
        prod, state = value
        a = at_time(a_ref, t)
        return prod * a, a * state + at_time(b_ref, t)

    ones = jnp.ones((seqs, width), F32)
    prod, state = lax.fori_loop(0, span, local, (ones, jnp.zeros_like(ones)), unroll=8)
    mine_ref[0] = prod
    mine_ref[1] = state
    sums_ref[me] = mine_ref[...]
    copies = to_all("seq", mine_ref, sums_ref, send1, recv1)
    for copy in copies:
        copy.start()
    for copy in copies:
        copy.wait()

    def carry_step(j, carry):
        both = sums_ref[j]
        return jnp.where(j < me, both[0] * carry + both[1], carry)

    carry = lax.fori_loop(0, devices - 1, carry_step, state_ref[...] * keep)
    carry_ref[...] = carry

    def final(t, state):
        state = at_time(a_ref, t) * state + at_time(b_ref, t)
        put(hidden_ref, pl.ds(t, seqs, stride=span), state)
        return state

    last = lax.fori_loop(0, span, final, carry, unroll=8)
    ends_ref[0:seqs, :] = jnp.where(me == devices - 1, last, 0.0)
    for s in range(seqs):
        ends_ref[(s + 1) * TILE : (s + 2) * TILE, :] = jnp.where(
            me == devices - 1, pad_ref[s, pl.ds(span, TILE), :], 0.0
        )

    @pl.loop(0, rows // ROWS)
    def _(q):
        at = block(q, ROWS)
        mixed_ref[at, :] = (get(hidden_ref, at) * gelu(branch_ref[at, :])).astype(BF16)


def backward_kernel(
    span,
    block_part_in,
    own_in,
    low_in,
    w_out_in,
    branch_in,
    hidden_in,
    pre_in,
    pad_in,
    normed_in,
    mixed_in,
    carry_ref,
    sums_ref,
    taps_ref,
    vec_ref,
    gates_ref,
    block_out,
    rec_out,
    grad_branch_ref,
    input_ref,
    acc_ref,
    blocks_ref,
    part,
    inbox,
    out,
    send_up,
    send_down,
    recv_up,
    recv_down,
    own_ref,
    resid_low,
    w_out_ref,
    branch_ref,
    hidden_ref,
    pre_ref,
    pad_ref,
    normed_ref,
    mixed_ref,
    a_ref,
    gd_ref,
    grad_ref,
    direct_ref,
    gpad_ref,
    heads_ref,
    low_ref,
    gates_grad,
    stage_ref,
    mine_ref,
    entries_ref,
    head_ref,
    head_in,
    load_sem,
    part_sem,
    store_sem,
    stage_sem,
    send1,
    recv1,
    send_t,
    recv_t,
):
    seqs, width = carry_ref.shape
    taps = taps_ref.shape[0]
    rows = seqs * span
    devices, me = lax.axis_size("seq"), lax.axis_index("seq")
    n, z = lax.axis_size("mp"), lax.axis_index("mp")
    chunks = rows // CHUNK
    size = GROUP * CHUNK
    held = part.shape[0] // size
    groups = chunks // GROUP
    sems = (send_up, send_down, recv_up, recv_down)
    local = pltpu.make_async_copy

    def part_load(g):
        slot = lax.rem(g, held)
        return local(block_part_in.at[block(g, size)], part.at[block(slot, size)], part_sem.at[slot])

    loads = [
        local(source, target, load_sem.at[i])
        for i, (source, target) in enumerate(
            (
                (own_in, own_ref),
                (low_in, resid_low),
                (w_out_in, w_out_ref),
                (pre_in, pre_ref),
                (branch_in, branch_ref),
                (hidden_in, hidden_ref),
                (pad_in, pad_ref),
                (mixed_in, mixed_ref),
                (normed_in, normed_ref),
            )
        )
    ]
    part_load(0).start()
    for copy in loads[:6]:
        copy.start()
    for g in range(1, held):
        part_load(g).start()
    for copy in loads[6:]:
        copy.start()
    acc_ref[...] = jnp.zeros_like(acc_ref)
    enter_all(("seq", "mp"))

    def decay(at):
        recall = jax.nn.sigmoid(pre_ref[at, :width])
        log_a = (-RATE_SCALE * vec_ref[1:2, :]) * recall
        return recall, log_a, jnp.exp(log_a)

    def piece_direct(s):
        @pl.when(s == 0)
        def _():
            for copy in loads[1:6]:
                copy.wait()

        grad_ref[...] = matmul_back(resid_low[block(s, span), :], w_out_ref[...])

        @pl.loop(0, span // ROWS)
        def _(q):
            at = block(s * (span // ROWS) + q, ROWS)
            put(a_ref, at, decay(at)[2])
            act, slope = gelu_both(branch_ref[at, :])
            grad = grad_ref[block(q, ROWS), :]
            put(gd_ref, at, grad * act)
            grad_branch_ref[at, :] = (grad * get(hidden_ref, at) * slope).astype(BF16)

    def at_time(ref, t):
        return get(ref, pl.ds(t, seqs, stride=span))

    zero = jnp.zeros((seqs, width), F32)
    entry_copies = to_all("seq", mine_ref, entries_ref, send1, recv1)

    def piece_entry(_):
        def step(k, through):
            t = span - 1 - k
            return at_time(a_ref, t) * (at_time(gd_ref, t) + through)

        mine_ref[...] = lax.fori_loop(0, span, step, zero, unroll=8)
        entries_ref[me] = mine_ref[...]
        for copy in entry_copies:
            copy.start()

    def piece_state(_):
        for copy in entry_copies:
            copy.wait()

        def back_step(k, through):
            j = devices - 1 - k
            return jnp.where(j > me, entries_ref[j] + sums_ref[j, 0] * through, through)

        incoming = lax.fori_loop(0, devices - 1, back_step, zero)

        def final(k, through):
            t = span - 1 - k
            grad = at_time(gd_ref, t) + through
            put(gd_ref, pl.ds(t, seqs, stride=span), grad)
            return at_time(a_ref, t) * grad

        lax.fori_loop(0, span, final, incoming, unroll=8)

    def add(k, value):
        acc_ref[k] += fold(value)

    def piece_gates(s):
        @pl.when(s == 0)
        def _():
            loads[6].wait()

        @pl.loop(0, span // ROWS)
        def _(q):
            at = block(s * (span // ROWS) + q, ROWS)
            part_rows = pad_ref[s, pl.ds(pl.multiple_of(q * ROWS, ROWS), ROWS + TILE), :]
            conv = vec_ref[0:1, :]
            for k in range(taps):
                first = TILE - (taps - 1) + k
                conv = conv + taps_ref[k : k + 1, :] * part_rows[first : first + ROWS]
            heads_ref[at, :] = conv.astype(BF16)
            recall, log_a, a = decay(at)
            gate = jax.nn.sigmoid(pre_ref[at, width:])
            square = one_minus_square(log_a, a)
            inverse = lax.rsqrt(square)
            root = jnp.sqrt(square)
            grad = get(gd_ref, at)
            hidden = get(hidden_ref, at)
            before_at = pl.multiple_of(jnp.maximum(s * span + q * ROWS - TILE, 0), TILE)
            earlier = get(hidden_ref, pl.ds(before_at, TILE))
            first_row = jnp.where(q == 0, carry_ref[pl.ds(s, 1), :], earlier[TILE - 1 :])
            place = lax.broadcasted_iota(jnp.int32, (ROWS, width), 0)
            prev = jnp.where(place == 0, first_row, pltpu.roll(hidden, 1, 0))
            grad_log = grad * a * (prev - gate * conv * a * inverse)
            through = grad_log * recall
            pre_r = through * (1.0 - recall) * (-RATE_SCALE * vec_ref[1:2, :])
            direct = grad * root * gate
            pre_i = direct * conv * (1.0 - gate)
            low_ref[at, :width] = pre_r.astype(BF16)
            low_ref[at, width:] = pre_i.astype(BF16)
            direct_ref[block(q, ROWS), :] = direct
            add(0, through)
            add(1, pre_r)
            add(2, pre_i)

        whole = direct_ref[...] + matmul_back(low_ref[block(s, span), :], gates_ref[...])
        gpad_ref[s, pl.ds(0, span), :] = whole
        head_ref[s] = whole[:TILE]

    head_copy = to_one("seq", -1, head_ref, head_in, send_t.at[0], recv_t.at[0])

    def piece_head(_):
        head_copy.start()

    def piece_taps(s):
        @pl.loop(0, span // ROWS)
        def _(q):
            at = pl.multiple_of(q * ROWS, ROWS)
            part_rows = pad_ref[s, pl.ds(at, ROWS + TILE), :]
            grad = gpad_ref[s, pl.ds(at, ROWS), :]
            add(3, grad)
            for k in range(taps):
                first = TILE - (taps - 1) + k
                add(4 + k, grad * part_rows[first : first + ROWS])

    def piece_tail(_):
        head_copy.wait()
        for s in range(seqs):
            gpad_ref[s, pl.ds(span, TILE), :] = jnp.where(me == devices - 1, 0.0, head_in[s])

    def piece_input(s):
        @pl.loop(0, span // ROWS)
        def _(q):
            part_rows = gpad_ref[s, pl.ds(pl.multiple_of(q * ROWS, ROWS), ROWS + TILE), :]
            total = taps_ref[taps - 1 : taps, :] * part_rows[0:ROWS]
            for k in range(taps - 1):
                first = taps - 1 - k
                total = total + taps_ref[k : k + 1, :] * part_rows[first : first + ROWS]
            input_ref[block(s * (span // ROWS) + q, ROWS), :] = total.astype(BF16)

    def contract(left, right):
        return lax.dot_general(left, right, CONTRACT_ROWS, preferred_element_type=F32)

    heads, head = blocks_ref.shape[1:3]

    def piece_gates_grad(i):
        @pl.when(i == 0)
        def _():
            gates_grad[...] = contract(heads_ref[...], low_ref[:, :width])

        @pl.when(i == 1)
        def _():
            gates_grad[...] = contract(heads_ref[...], low_ref[:, width:])

        for h in range(heads):
            row = gates_grad[h * head : (h + 1) * head, :]
            row = row if h == 0 else pltpu.roll(row, width - h * head, 1)
            blocks_ref[i, h] = row[:, :head]

    tall = resid_low.shape[1] // WEIGHT_STEPS

    def stage_store(i):
        at = block(lax.rem(i, WEIGHT_STEPS), tall)
        slot = lax.rem(i, 2)
        return local(stage_ref.at[slot], rec_out.at[i // WEIGHT_STEPS, at], stage_sem.at[slot])

    def piece_weight(i):
        @pl.when(i == 0)
        def _():
            loads[7].wait()
            loads[8].wait()

        @pl.when(i >= 2)
        def _():
            stage_store(i - 2).wait()

        at = block(lax.rem(i, WEIGHT_STEPS), tall)
        slot = lax.rem(i, 2)
        for which, (left, right) in enumerate(
            ((resid_low, mixed_ref), (normed_ref, grad_branch_ref), (normed_ref, input_ref))
        ):
            @pl.when(i // WEIGHT_STEPS == which)
            def _():
                stage_ref[slot] = contract(left[:, at], right[...])

        stage_store(i).start()

    weights = 3 * WEIGHT_STEPS
    plan = []
    begin = 3
    for work, times, gap in (
        (piece_direct, seqs, 0),
        (piece_entry, 1, 1),
        (piece_state, 1, 0),
        (piece_gates, seqs, 0),
        (piece_head, 1, 0),
        (piece_taps, seqs, 0),
        (piece_tail, 1, 0),
        (piece_input, seqs, 0),
        (piece_gates_grad, 2, 0),
        (piece_weight, weights, 0),
    ):
        plan.append((work, begin, times))
        begin += times + gap

    def run(step):
        for work, first, times in plan:
            @pl.when(jnp.logical_and(step >= first, step < first + times))
            def _():
                work(step - first)

    def before(k):
        @pl.when(k == 0)
        def _():
            loads[0].wait()

        @pl.when(jnp.logical_and(lax.rem(k, GROUP) == 0, k < chunks))
        def _():
            part_load(k // GROUP).wait()

        g = (k - out.shape[0]) // GROUP - 1 + held

        @pl.when(
            jnp.logical_and(
                jnp.logical_and(k >= out.shape[0] + GROUP, lax.rem(k - out.shape[0], GROUP) == 0),
                g < groups,
            )
        )
        def _():
            part_load(g).start()

        run(k)

    def root(c, slot, total):
        out[slot] = own_ref[block(c // 2, CHUNK), :] + total

    def store(c, slot):
        return local(out.at[slot], block_out.at[block(c, CHUNK)], store_sem.at[slot])

    def arrive(c, slot):
        store(c, slot).start()

    def leave(c, slot):
        store(c, slot).wait()

    line_sum(
        "mp", chunks, held * GROUP, part, inbox, out, sems, before, root, arrive, leave
    )

    @pl.loop(chunks + out.shape[0], max(begin, chunks + out.shape[0]))
    def _(k):
        run(k)

    stage_store(weights - 2).wait()
    stage_store(weights - 1).wait()


def backward_call(span, heads, head, *args):
    block_part = args[0]
    low, w_out, branch, hidden, pre, padded, normed, mixed, carry, sums, taps = args[2:13]
    rows, model = block_part.shape
    seqs, width = carry.shape
    devices = lax.axis_size("seq")
    ring = ring_size("mp")
    held = 3 * GROUP * CHUNK
    dma = pltpu.SemaphoreType.DMA
    columns = pltpu.VMEM((width // LANES, rows, LANES), F32)
    return pl.pallas_call(
        functools.partial(backward_kernel, span),
        out_shape=(
            shape((rows, model)),
            shape((3, model, width)),
            shape((rows, width), BF16),
            shape((rows, width), BF16),
            shape((4 + taps.shape[0], TILE, width)),
            shape((2, heads, head, head)),
        ),
        in_specs=[HBM] * 10 + [VMEM] * 5,
        out_specs=(HBM,) * 2 + (VMEM,) * 4,
        scratch_shapes=line_scratch("mp", held, model)
        + [
            pltpu.VMEM((rows // 2, model), F32),
            pltpu.VMEM((rows, model), BF16),
            pltpu.VMEM((width, model), BF16),
            pltpu.VMEM((rows, width), F32),
            pltpu.VMEM(hidden.shape, F32),
            pltpu.VMEM(pre.shape, F32),
            pltpu.VMEM(padded.shape, F32),
            pltpu.VMEM((rows, model), BF16),
            pltpu.VMEM((rows, width), BF16),
            columns,
            columns,
            pltpu.VMEM((span, width), F32),
            pltpu.VMEM((span, width), F32),
            pltpu.VMEM((seqs, span + TILE, width), F32),
            pltpu.VMEM((rows, width), BF16),
            pltpu.VMEM((rows, 2 * width), BF16),
            pltpu.VMEM((width, width), F32),
            pltpu.VMEM((2, model // WEIGHT_STEPS, width), F32),
            pltpu.VMEM((seqs, width), F32),
            pltpu.VMEM((devices, seqs, width), F32),
            pltpu.VMEM((seqs, TILE, width), F32),
            pltpu.VMEM((seqs, TILE, width), F32),
            dma((9,)),
            dma((3,)),
            dma((ring,)),
            dma((2,)),
            dma((devices - 1,)),
            dma((devices - 1,)),
            dma((1,)),
            dma((1,)),
        ],
        compiler_params=params(1, 63),
        cost_estimate=cost(200),
        name="backward",
    )(*args)


def line_sum(axis, total, period, part, inbox, out, sems, before, root, arrive, leave):
    send_up, send_down, recv_up, recv_down = sems
    n, z = lax.axis_size(axis), lax.axis_index(axis)
    depth = n // 2
    ring = out.shape[0]

    def root_of(c):
        return depth - 1 + lax.rem(c, 2)

    def up(c, step, side):
        slot = lax.rem(c, ring)
        return pltpu.make_async_remote_copy(
            src_ref=part.at[block(lax.rem(c, period), CHUNK)],
            dst_ref=inbox.at[side, slot],
            send_sem=send_up.at[slot],
            recv_sem=recv_up.at[side, slot],
            device_id={axis: z + step},
            device_id_type=MESH,
        )

    def down(c, step, side):
        slot = lax.rem(c, ring)
        return pltpu.make_async_remote_copy(
            src_ref=out.at[slot],
            dst_ref=out.at[slot],
            send_sem=send_down.at[side, slot],
            recv_sem=recv_down.at[slot],
            device_id={axis: z + step},
            device_id_type=MESH,
        )

    inner = jnp.logical_and(z > 0, z < n - 1)

    @pl.loop(0, total + ring)
    def _(k):
        @pl.when(k >= ring)
        def _():
            c = k - ring
            r = root_of(c)
            step = jnp.where(z < r, 1, -1)
            side = jnp.where(z < r, 0, 1)

            @pl.when(z == r)
            def _():
                down(c, -1, 0).wait_send()
                down(c, 1, 1).wait_send()

            @pl.when(z != r)
            def _():
                up(c, step, side).wait_send()

            @pl.when(jnp.logical_and(z != r, inner))
            def _():
                down(c, -step, side).wait_send()

            leave(c, lax.rem(c, ring))

        before(k)

        for i in reversed(range(n + 1)):
            c = k - SKEW * i
            valid = jnp.logical_and(c >= 0, c < total)
            c = jnp.clip(c, 0, total - 1)
            at = block(lax.rem(c, period), CHUNK)
            slot = lax.rem(c, ring)
            r = root_of(c)
            step = jnp.where(z < r, 1, -1)
            side = jnp.where(z < r, 0, 1)
            if i > depth:
                here = jnp.logical_and(z != r, jnp.abs(z - r) == i - depth)

                @pl.when(jnp.logical_and(valid, here))
                def _():
                    down(c, -step, side).wait_recv()

                    @pl.when(inner)
                    def _():
                        down(c, -step, side).start()

                    arrive(c, slot)
            elif i == depth:

                @pl.when(jnp.logical_and(valid, z == r))
                def _():
                    up(c, 1, 0).wait_recv()
                    up(c, -1, 1).wait_recv()
                    root(c, slot, part[at, :] + inbox[0, slot] + inbox[1, slot])
                    down(c, -1, 0).start()
                    down(c, 1, 1).start()
                    arrive(c, slot)
            else:
                here = jnp.where(z < r, z, n - 1 - z) == i

                @pl.when(jnp.logical_and(valid, jnp.logical_and(z != r, here)))
                def _():
                    if i > 0:
                        up(c, step, side).wait_recv()
                        part[at, :] += inbox[side, slot]
                    up(c, step, side).start()


def ring_size(axis):
    return SKEW * lax.axis_size(axis) + 4


def line_scratch(axis, rows, model):
    dma = pltpu.SemaphoreType.DMA
    ring = ring_size(axis)
    return [
        pltpu.VMEM((rows, model), F32),
        pltpu.VMEM((2, ring, CHUNK, model), F32),
        pltpu.VMEM((ring, CHUNK, model), F32),
        dma((ring,)),
        dma((2, ring)),
        dma((2, ring)),
        dma((ring,)),
    ]


def mean_square(x):
    return lax.rsqrt(jnp.mean(x * x, axis=-1, keepdims=True) + EPS)


def nothing(*_):
    pass


def fold(value):
    total = value[0:TILE]
    for i in range(1, value.shape[0] // TILE):
        total = total + value[i * TILE : (i + 1) * TILE]
    return total


def norm_grad(value, gain, grad, acc_ref):
    q = mean_square(value)
    e = gain * grad
    acc_ref[...] += fold(grad * value * q)
    return q * e - value * (q * q * q) * jnp.mean(e * value, axis=-1, keepdims=True)


def middle_kernel(
    mixed_in,
    w_out_in,
    x_in,
    og_in,
    gain_ref,
    w_gate_in,
    w_up_in,
    w_down_in,
    normed_out,
    hidden_out,
    gate_out,
    up_out,
    glow_out,
    block_out,
    low_out,
    own_grad_out,
    weight_out,
    own_ref,
    acc_ref,
    part,
    inbox,
    out,
    send_up,
    send_down,
    recv_up,
    recv_down,
    mixed,
    w_out,
    w_gate,
    w_up,
    w_down,
    normed,
    rows_ref,
    og_ref,
    glow,
    gate_val,
    up_val,
    grad_hidden,
    hidden,
    grad_gate,
    grad_up,
    block_part,
    low,
    weight_sem,
    row_sem,
    og_sem,
    act_sem,
    low_sem,
    own_sem,
    again_sem,
    stage_sem,
):
    n, z = lax.axis_size("mp"), lax.axis_index("mp")
    count = part.shape[0] // CHUNK
    size = GROUP * CHUNK
    groups = count // GROUP
    ring = out.shape[0]
    sems = (send_up, send_down, recv_up, recv_down)
    local = pltpu.make_async_copy

    loads = [
        local(source, target, weight_sem.at[i])
        for i, (source, target) in enumerate(
            (
                (mixed_in, mixed),
                (w_out_in, w_out),
                (w_gate_in, w_gate),
                (w_up_in, w_up),
                (w_down_in, w_down.at[slice(0, w_down_in.shape[0])]),
            )
        )
    ]
    for copy in loads:
        copy.start()
    deep = w_down_in.shape[0]

    def og_load(g):
        return local(og_in.at[block(g, size)], og_ref, og_sem.at[0])

    og_load(0).start()
    enter_all(("mp",))
    acc_ref[...] = jnp.zeros_like(acc_ref)
    loads[0].wait()
    loads[1].wait()

    def is_root(c):
        return z == n // 2 - 1 + lax.rem(c, 2)

    def row_load(source, c):
        slot = lax.rem(c, ring)
        at = block(lax.rem(c, count), CHUNK)
        return local(source.at[at], rows_ref.at[slot], row_sem.at[slot])

    acts = (
        (normed, normed_out),
        (glow, glow_out),
        (hidden, hidden_out),
        (grad_gate, gate_out),
        (grad_up, up_out),
        (block_part, block_out),
    )

    def act_store(i, g):
        source, target = acts[i]
        source = source.at[lax.rem(g, 2)] if i == 0 else source
        return local(source, target.at[block(g, size)], act_sem.at[i])

    def at_tick(k, first, work):
        g = (k - first) // GROUP

        @pl.when(
            jnp.logical_and(
                jnp.logical_and(k >= first, k < first + GROUP * groups),
                lax.rem(k - first, GROUP) == 0,
            )
        )
        def _():
            work(g)

    def project(g):
        part[block(g, size), :] = dot(mixed[block(g, size), :], w_out[...])

    def piece_gate(g):
        @pl.when(g == 0)
        def _():
            for copy in loads[2:]:
                copy.wait()

        gate_val[...] = dot(normed[lax.rem(g, 2)], w_gate[...])
        act_store(0, g).start()

    def piece_up(g):
        up_val[...] = dot(normed[lax.rem(g, 2)], w_up[...])

        @pl.when(g > 0)
        def _():
            for i in range(1, 6):
                act_store(i, g - 1).wait()

    def piece_low(g):
        og_load(g).wait()

        @pl.loop(0, size // ROWS)
        def _(q):
            glow[block(q, ROWS), :] = og_ref[block(q, ROWS), :].astype(BF16)

        @pl.when(g + 1 < groups)
        def _():
            og_load(g + 1).start()

        act_store(1, g).start()
        act_store(0, g).wait()

    def piece_hidden(g):
        grad_hidden[...] = matmul_back(glow[...], w_down[:deep, :])

    def piece_act(g):
        @pl.loop(0, size // CHUNK)
        def _(q):
            at = block(q, CHUNK)
            up = up_val[at, :]
            grad = grad_hidden[at, :]
            act, slope = gelu_both(gate_val[at, :])
            hidden[at, :] = (act * up).astype(BF16)
            grad_gate[at, :] = (grad * up * slope).astype(BF16)
            grad_up[at, :] = (grad * act).astype(BF16)

        for i in range(2, 5):
            act_store(i, g).start()

    def piece_down(g):
        block_part[...] = dot(hidden[...], w_down[:deep, :])
        act_store(5, g).start()

    def piece_back_gate(g):
        part[block(g, size), :] = matmul_back(grad_gate[...], w_gate[...])

    def piece_back_up(g):
        part[block(g, size), :] += matmul_back(grad_up[...], w_up[...])

    tokens = count * CHUNK
    half = tokens // 2
    quarter = half // 2
    again = [
        local(source, target, again_sem.at[i])
        for i, (source, target) in enumerate(
            (
                (normed_out, w_down.at[slice(0, tokens)]),
                (gate_out, w_gate.at[slice(0, tokens)]),
                (up_out, w_up.at[slice(0, tokens)]),
                (hidden_out, w_gate.at[slice(tokens, 2 * tokens)]),
                (glow_out.at[slice(0, half)], w_down.at[slice(tokens, tokens + half)]),
                (glow_out.at[slice(half, half + quarter)], normed.at[0]),
                (glow_out.at[slice(half + quarter, tokens)], normed.at[1]),
            )
        )
    ]
    tall = w_gate.shape[0] // WEIGHT_STEPS
    stages = (gate_val, up_val, grad_hidden)

    def stage_store(which, i):
        return local(stages[which], weight_out.at[which, block(i, tall)], stage_sem.at[which])

    def piece_reload():
        for i in range(1, 6):
            act_store(i, groups - 1).wait()
        for copy in again:
            copy.start()

    def piece_ready():
        for copy in again:
            copy.wait()

    def contract(left, right):
        return lax.dot_general(left, right, CONTRACT_ROWS, preferred_element_type=F32)

    def piece_weight(step):
        i = step // 3
        at = block(i, tall)
        for which in range(3):

            @pl.when(lax.rem(step, 3) == which)
            def _():
                @pl.when(i > 0)
                def _():
                    stage_store(which, i - 1).wait()

                stage = stages[which]
                if which == 0:
                    stage[...] = contract(w_down[:tokens, at], w_gate[:tokens, :])
                elif which == 1:
                    stage[...] = contract(w_down[:tokens, at], w_up[:tokens, :])
                else:
                    stage[...] = contract(
                        w_down[tokens : tokens + half, at], w_gate[tokens : tokens + half, :]
                    )
                    middle = tokens + half + quarter
                    stage[...] += contract(normed[0, :, at], w_gate[tokens + half : middle, :])
                    stage[...] += contract(normed[1, :, at], w_gate[middle : 2 * tokens, :])
                stage_store(which, i).start()

    first = GROUP + SKEW * n
    spare = GROUP * groups + ring + 3
    first_weight = spare + 3
    weights = 3 * WEIGHT_STEPS

    def before(k):
        @pl.when(k == spare)
        def _():
            piece_reload()

        @pl.when(k == first_weight - 1)
        def _():
            piece_ready()

        @pl.when(jnp.logical_and(k >= first_weight, k < first_weight + weights))
        def _():
            piece_weight(k - first_weight)

        @pl.when(jnp.logical_and(k < count, is_root(k)))
        def _():
            row_load(x_in, k).start()

        @pl.when(
            jnp.logical_and(jnp.logical_and(k >= count, k < 2 * count), is_root(k))
        )
        def _():
            row_load(og_in, k).start()

        at_tick(k, 0, project)
        at_tick(k, first, piece_gate)
        at_tick(k, first + 1, piece_up)
        at_tick(k, first + 2, piece_low)
        at_tick(k, first + 3, piece_hidden)
        at_tick(k, first + 4, piece_act)
        at_tick(k, first + 6, piece_down)
        at_tick(k, GROUP + ring, piece_back_gate)
        at_tick(k, GROUP + ring + 2, piece_back_up)

    def root(c, slot, total):
        j = lax.rem(c, count)
        mine = block(j // 2, CHUNK)
        row_load(x_in, c).wait()

        @pl.when(c < count)
        def _():
            value = rows_ref[slot] + total
            own_ref[mine, :] = value
            out[slot] = (value * mean_square(value) * gain_ref[...]).astype(BF16).astype(F32)

        @pl.when(c >= count)
        def _():
            back = norm_grad(own_ref[mine, :], gain_ref[...], total, acc_ref)
            out[slot] = rows_ref[slot] + back

    def low_store(c, slot):
        at = block(lax.rem(c, count), CHUNK)
        return local(low.at[slot], low_out.at[at], low_sem.at[slot])

    def own_store(c, slot):
        at = block(lax.rem(c, count) // 2, CHUNK)
        return local(out.at[slot], own_grad_out.at[at], own_sem.at[slot])

    def arrive(c, slot):
        @pl.when(c < count)
        def _():
            normed[lax.rem(c // GROUP, 2), block(lax.rem(c, GROUP), CHUNK), :] = out[slot].astype(BF16)

        @pl.when(c >= count)
        def _():
            low[slot] = out[slot].astype(BF16)
            low_store(c, slot).start()

            @pl.when(is_root(c))
            def _():
                own_store(c, slot).start()

    def leave(c, slot):
        @pl.when(c >= count)
        def _():
            low_store(c, slot).wait()

            @pl.when(is_root(c))
            def _():
                own_store(c, slot).wait()

    line_sum("mp", 2 * count, count, part, inbox, out, sems, before, root, arrive, leave)

    for which in range(3):
        stage_store(which, WEIGHT_STEPS - 1).wait()


def middle_call(*args):
    mixed, w_out, x, og, gain, w_gate, w_up, w_down = args
    rows, model = x.shape
    width, hidden = mixed.shape[1], w_gate.shape[1]
    size = GROUP * CHUNK
    dma = pltpu.SemaphoreType.DMA
    ring = ring_size("mp")
    act = shape((rows, hidden), BF16)
    tall = shape((rows, model), BF16)
    return pl.pallas_call(
        middle_kernel,
        out_shape=(
            tall,
            act,
            act,
            act,
            tall,
            shape((rows, model)),
            tall,
            shape((rows // 2, model)),
            shape((3, model, hidden)),
            shape((rows // 2, model)),
            shape((TILE, model)),
        ),
        in_specs=[HBM] * 4 + [VMEM] + [HBM] * 3,
        out_specs=(HBM,) * 9 + (VMEM,) * 2,
        scratch_shapes=line_scratch("mp", rows, model)
        + [
            pltpu.VMEM((rows, width), BF16),
            pltpu.VMEM((width, model), BF16),
            pltpu.VMEM((model, hidden), BF16),
            pltpu.VMEM((model, hidden), BF16),
            pltpu.VMEM((max(hidden, rows * 3 // 2), model), BF16),
            pltpu.VMEM((2, size, model), BF16),
            pltpu.VMEM((ring, CHUNK, model), F32),
            pltpu.VMEM((size, model), F32),
            pltpu.VMEM((size, model), BF16),
            pltpu.VMEM((size, hidden), F32),
            pltpu.VMEM((size, hidden), F32),
            pltpu.VMEM((size, hidden), F32),
            pltpu.VMEM((size, hidden), BF16),
            pltpu.VMEM((size, hidden), BF16),
            pltpu.VMEM((size, hidden), BF16),
            pltpu.VMEM((size, model), F32),
            pltpu.VMEM((ring, CHUNK, model), BF16),
            dma((5,)),
            dma((ring,)),
            dma((1,)),
            dma((6,)),
            dma((ring,)),
            dma((ring,)),
            dma((7,)),
            dma((3,)),
        ],
        compiler_params=params(2, 63),
        cost_estimate=cost(400),
        name="middle",
    )(*args)


def last_kernel(
    own_grad_in,
    x_in,
    grad_branch_in,
    input_in,
    w_branch_in,
    w_input_in,
    gain_ref,
    other_acc,
    sums_in,
    ends_in,
    blocks_in,
    grad_out,
    norm_ref,
    vector_out,
    blocks_out,
    part,
    inbox,
    out,
    send_up,
    send_down,
    recv_up,
    recv_down,
    own_grad_ref,
    x_ref,
    grad_branch,
    input_low,
    w_branch,
    w_input,
    load_sem,
    store_sem,
    acc_ref,
    mine_ref,
    seq_in,
    mp_in,
    send_s,
    recv_s,
    send_m,
    recv_m,
    vector,
    vector_in,
    block_slots,
    send_v,
    recv_v,
    send_b,
    recv_b,
):
    count = part.shape[0] // CHUNK
    size = GROUP * CHUNK
    sems = (send_up, send_down, recv_up, recv_down)
    local = pltpu.make_async_copy

    loads = [
        local(source, target, load_sem.at[i])
        for i, (source, target) in enumerate(
            (
                (grad_branch_in, grad_branch),
                (w_branch_in, w_branch),
                (input_in, input_low),
                (w_input_in, w_input),
                (own_grad_in, own_grad_ref),
                (x_in, x_ref),
            )
        )
    ]
    for copy in loads:
        copy.start()
    acc_ref[...] = jnp.zeros_like(acc_ref)
    mine_ref[...] = jnp.zeros_like(mine_ref)
    enter_all(("seq", "mp"))
    for copy in loads[:4]:
        copy.wait()

    kinds = sums_in.shape[0]
    me = lax.axis_index("seq")
    for i in range(kinds):
        vector[i : i + 1, :] = jnp.sum(sums_in[i], axis=0, keepdims=True)
    vector[kinds:, :] = ends_in[...]
    vector_copies = to_all("seq", vector, vector_in, send_v, recv_v)
    block_copies = to_all("seq", blocks_in, block_slots, send_b, recv_b)
    seq_copies = to_all("seq", mine_ref.at[0], seq_in, send_s, recv_s)
    mp_copies = to_all("mp", mine_ref.at[1], mp_in, send_m, recv_m)
    settled = count + SKEW * (lax.axis_size("mp") // 2)

    def before(k):
        @pl.when(k == 3)
        def _():
            vector_in[me] = vector[...]
            block_slots[me] = blocks_in[...]
            for copy in vector_copies + block_copies:
                copy.start()

        @pl.when(k == count - 6)
        def _():
            for copy in vector_copies + block_copies:
                copy.wait()
            vector_out[...] = jnp.sum(vector_in[...], axis=0)

        @pl.when(jnp.logical_and(k >= count - 5, k < count - 3))
        def _():
            i = k - (count - 5)
            for h in range(blocks_in.shape[1]):
                total = block_slots[0, i, h]
                for j in range(1, block_slots.shape[0]):
                    total = total + block_slots[j, i, h]
                blocks_out[i, h] = total

        @pl.when(k == settled)
        def _():
            mine_ref[0, 0:1, :] = jnp.sum(acc_ref[...], axis=0, keepdims=True)
            mine_ref[0, 1:2, :] = jnp.sum(other_acc[...], axis=0, keepdims=True)
            seq_in[me] = mine_ref[0]
            for copy in seq_copies:
                copy.start()

        @pl.when(k == settled + 2)
        def _():
            for copy in seq_copies:
                copy.wait()
            mine_ref[1] = jnp.sum(seq_in[...], axis=0)
            mp_in[lax.axis_index("mp")] = mine_ref[1]
            for copy in mp_copies:
                copy.start()

        @pl.when(jnp.logical_and(lax.rem(k, 4) == 0, k // 4 < count // GROUP))
        def _():
            at = block(k // 4, size)
            part[at, :] = matmul_back(grad_branch[at, :], w_branch[...])
            part[at, :] += matmul_back(input_low[at, :], w_input[...])

        @pl.when(k == 1)
        def _():
            for copy in loads[4:]:
                copy.wait()

    def root(c, slot, total):
        back = norm_grad(x_ref[block(c, CHUNK), :], gain_ref[...], total, acc_ref)
        out[slot] = own_grad_ref[block(c // 2, CHUNK), :] + back

    def store(c, slot):
        return local(out.at[slot], grad_out.at[block(c, CHUNK)], store_sem.at[slot])

    def arrive(c, slot):
        store(c, slot).start()

    def leave(c, slot):
        store(c, slot).wait()

    line_sum("mp", count, count, part, inbox, out, sems, before, root, arrive, leave)

    for copy in mp_copies:
        copy.wait()
    norm_ref[...] = jnp.sum(mp_in[...], axis=0)


def enter_all(axes):
    barrier = pltpu.get_barrier_semaphore()
    count = 0
    for axis in axes:
        size, me = lax.axis_size(axis), lax.axis_index(axis)
        for d in range(1, size):
            pl.semaphore_signal(
                barrier, 1, device_id={axis: lax.rem(me + d, size)}, device_id_type=MESH
            )
        count += size - 1
    pl.semaphore_wait(barrier, count)


def cost(micros):
    return pl.CostEstimate(flops=int(micros * 1e9), bytes_accessed=1 << 20, transcendentals=0)


def last_call(*args):
    x, grad_branch = args[1:3]
    rows, model = x.shape
    width = grad_branch.shape[1]
    vectors = args[8].shape[0] + args[9].shape[0]
    blocks = args[10].shape
    dma = pltpu.SemaphoreType.DMA
    nseq, nmp = lax.axis_size("seq"), lax.axis_size("mp")
    return pl.pallas_call(
        last_kernel,
        out_shape=(shape((rows, model)), shape((TILE, model)), shape((vectors, width)), shape(blocks)),
        in_specs=[HBM] * 6 + [VMEM] * 5,
        out_specs=(HBM,) + (VMEM,) * 3,
        scratch_shapes=line_scratch("mp", rows, model)
        + [
            pltpu.VMEM((rows // 2, model), F32),
            pltpu.VMEM((rows, model), F32),
            pltpu.VMEM((rows, width), BF16),
            pltpu.VMEM((rows, width), BF16),
            pltpu.VMEM((model, width), BF16),
            pltpu.VMEM((model, width), BF16),
            dma((6,)),
            dma((ring_size("mp"),)),
            pltpu.VMEM((TILE, model), F32),
            pltpu.VMEM((2, TILE, model), F32),
            pltpu.VMEM((nseq, TILE, model), F32),
            pltpu.VMEM((nmp, TILE, model), F32),
            dma((nseq - 1,)),
            dma((nseq - 1,)),
            dma((nmp - 1,)),
            dma((nmp - 1,)),
            pltpu.VMEM((vectors, width), F32),
            pltpu.VMEM((nseq, vectors, width), F32),
            pltpu.VMEM((nseq,) + blocks, F32),
            dma((nseq - 1,)),
            dma((nseq - 1,)),
            dma((nseq - 1,)),
            dma((nseq - 1,)),
        ],
        compiler_params=params(4, 62),
        cost_estimate=cost(200),
        name="last_sums",
    )(*args)


def finish_kernel(
    block_in,
    grad_in,
    mlp_in,
    rec_in,
    blocks_in,
    vector_in,
    norm_in,
    raw_ref,
    block_out,
    grad_out,
    w_gate_out,
    w_up_out,
    w_branch_out,
    w_input_out,
    w_down_out,
    w_out_out,
    gate_r_out,
    gate_i_out,
    taps_out,
    conv_bias_out,
    bias_r_out,
    bias_i_out,
    decay_out,
    norm_in_out,
    norm_mlp_out,
    state_out,
    conv_out,
    down,
    rec,
    sem,
):
    local = pltpu.make_async_copy
    loads = [local(mlp_in.at[2], down, sem.at[0]), local(rec_in.at[0], rec, sem.at[1])]
    pairs = [
        (mlp_in.at[0], w_gate_out),
        (mlp_in.at[1], w_up_out),
        (rec_in.at[1], w_branch_out),
        (rec_in.at[2], w_input_out),
    ]
    for source, target in ((block_in, block_out), (grad_in, grad_out)):
        size = source.shape[0] // COPIES
        for i in range(COPIES):
            at = slice(i * size, (i + 1) * size)
            pairs.append((source.at[at], target.at[at]))
    copies = [local(source, target, sem.at[2 + i]) for i, (source, target) in enumerate(pairs)]
    for copy in loads + copies:
        copy.start()
    gate_r_out[...] = blocks_in[0]
    gate_i_out[...] = blocks_in[1]
    taps, seqs, edge = taps_out.shape[0], state_out.shape[0], conv_out.shape[1]
    decay_out[...] = vector_in[0:1, :] * (RATE_SCALE * jax.nn.sigmoid(-raw_ref[1:2, :]))
    bias_r_out[...] = vector_in[1:2, :]
    bias_i_out[...] = vector_in[2:3, :]
    conv_bias_out[...] = vector_in[3:4, :]
    taps_out[...] = vector_in[4 : 4 + taps, :]
    begin = 4 + taps
    state_out[...] = vector_in[begin : begin + seqs, :]
    for s in range(seqs):
        end = begin + seqs + (s + 1) * TILE
        conv_out[s] = vector_in[end - edge : end, :]
    norm_in_out[...] = norm_in[0:1, :]
    norm_mlp_out[...] = norm_in[1:2, :]
    for copy in loads:
        copy.wait()
    w_down_out[...] = down[...].T
    w_out_out[...] = rec[...].T
    for copy in copies:
        copy.wait()


def finish_call(seqs, heads, head, edge, *args):
    block_out, stream_grad, mlp_grads, rec_grads, _, _, norms, raw = args
    rows, model = block_out.shape
    own, hidden = mlp_grads.shape[1:]
    width = rec_grads.shape[2]
    taps = edge + 1
    line = shape((1, width))
    tall = shape((rows, model))
    return pl.pallas_call(
        finish_kernel,
        out_shape=(
            tall,
            tall,
            shape((own, hidden)),
            shape((own, hidden)),
            shape((own, width)),
            shape((own, width)),
            shape((hidden, own)),
            shape((width, own)),
            shape((heads, head, head)),
            shape((heads, head, head)),
            shape((taps, width)),
            line,
            line,
            line,
            line,
            shape((1, model)),
            shape((1, model)),
            shape((seqs, width)),
            shape((seqs, edge, width)),
        ),
        in_specs=[HBM] * 4 + [VMEM] * 4,
        out_specs=(HBM,) * 6 + (VMEM,) * 13,
        scratch_shapes=[
            pltpu.VMEM((own, hidden), F32),
            pltpu.VMEM((own, width), F32),
            pltpu.SemaphoreType.DMA((6 + 2 * COPIES,)),
        ],
        compiler_params=pltpu.CompilerParams(vmem_limit_bytes=48 << 20),
        cost_estimate=cost(15),
        name="finish",
    )(*args)


def params(collective, megabytes=60):
    return pltpu.CompilerParams(
        collective_id=collective, has_side_effects=True, vmem_limit_bytes=megabytes << 20
    )


def shape(dims, dtype=F32):
    return jax.ShapeDtypeStruct(dims, dtype)


def recurrence_forward(span, *args):
    x, _, w_branch = args[:3]
    rows, model = x.shape
    seqs, width = rows // span, w_branch.shape[1]
    devices = lax.axis_size("seq")
    dma = pltpu.SemaphoreType.DMA
    return pl.pallas_call(
        functools.partial(forward_kernel, span),
        out_shape=(
            shape((rows, model), BF16),
            shape((rows, width)),
            shape((seqs, span + TILE, width)),
            shape((rows, 2 * width)),
            shape((width // LANES, rows, LANES)),
            shape((rows, width), BF16),
            shape((seqs, width)),
            shape((devices, 2, seqs, width)),
            shape((width, 2 * width), BF16),
            shape((TILE, width)),
            shape(((seqs + 1) * TILE, width)),
        ),
        in_specs=[VMEM] * len(args),
        out_specs=(VMEM,) * 11,
        scratch_shapes=[
            pltpu.VMEM((width // LANES, rows, LANES), F32),
            pltpu.VMEM((width // LANES, rows, LANES), F32),
            pltpu.VMEM((span, width), F32),
            pltpu.VMEM((seqs, TILE, width), F32),
            pltpu.VMEM((seqs, TILE, width), F32),
            pltpu.VMEM((2, seqs, width), F32),
            dma((devices - 1,)),
            dma((devices - 1,)),
            dma((1,)),
            dma((1,)),
        ],
        compiler_params=params(0),
        cost_estimate=cost(50),
        name="recurrence_forward",
    )(*args)


def widen(array, width):
    short = width - array.shape[-1]
    if short == 0:
        return array
    return jnp.pad(array, [(0, 0)] * (array.ndim - 1) + [(0, short)])


def per_device(
    stream,
    norm_in,
    w_branch,
    w_input,
    conv_kernel,
    conv_bias,
    gate_r,
    bias_r,
    gate_i,
    bias_i,
    decay_param,
    w_out,
    norm_mlp,
    w_gate,
    w_up,
    w_down,
    state_init,
    conv_init,
    fresh_rows,
    out_grad,
):
    seqs, span, model = stream.shape
    channels = w_branch.shape[1]
    mlp_dev = w_gate.shape[1]
    heads, head_width = gate_r.shape[:2]
    taps = conv_kernel.shape[0]
    edge = taps - 1
    rows = seqs * span
    devices = lax.axis_size("seq")
    position = lax.axis_index("seq")
    width = -(-channels // 128) * 128

    flat_in = stream.reshape(rows, model)
    flat_grad = out_grad.reshape(rows, model)
    w_branch_p = widen(w_branch, width)
    w_input_p = widen(w_input, width)
    w_out_p = jnp.pad(w_out, ((0, width - channels), (0, 0))) if width > channels else w_out
    taps_p = widen(conv_kernel, width)
    vec = jnp.stack([widen(v, width) for v in (conv_bias, decay_param, bias_r, bias_i)])

    (
        normed,
        branch,
        padded,
        pre,
        hidden,
        mixed,
        carry,
        sums,
        gates,
        rates,
        ends,
    ) = recurrence_forward(
        span,
        flat_in,
        norm_in[None],
        w_branch_p,
        w_input_p,
        taps_p,
        vec,
        gate_r,
        gate_i,
        fresh_rows[:, None],
        widen(state_init, width),
        widen(conv_init, width),
    )
    _, _, _, _, _, block_part, resid_low, own_grad, mlp_grads, own, norm_mlp_acc = middle_call(
        mixed, w_out_p, flat_in, flat_grad, norm_mlp[None], w_gate, w_up, w_down
    )
    mlp_grads = lax.psum_scatter(mlp_grads, "seq", scatter_dimension=1, tiled=True)
    block_out, rec_grads, grad_branch, input_low, acc, blocks = backward_call(
        span,
        heads,
        head_width,
        block_part,
        own,
        resid_low,
        w_out_p,
        branch,
        hidden,
        pre,
        padded,
        normed,
        mixed,
        carry,
        sums,
        taps_p,
        rates,
        gates,
    )

    rec_grads, grad_branch, mlp_grads = lax.optimization_barrier(
        (rec_grads, grad_branch, mlp_grads)
    )
    rec_grads = lax.psum_scatter(rec_grads, "seq", scatter_dimension=1, tiled=True)

    stream_grad, norm_grads, vectors, blocks = last_call(
        own_grad,
        flat_in,
        grad_branch,
        input_low,
        w_branch_p,
        w_input_p,
        norm_in[None],
        norm_mlp_acc,
        acc,
        ends,
        blocks,
    )
    (
        block_out,
        stream_grad,
        w_gate_grad,
        w_up_grad,
        w_branch_grad,
        w_input_grad,
        w_down_grad,
        w_out_grad,
        gate_r_grad,
        gate_i_grad,
        taps_grad,
        conv_bias_grad,
        bias_r_grad,
        bias_i_grad,
        decay_grad,
        norm_in_grad,
        norm_mlp_grad,
        final_state,
        final_conv,
    ) = finish_call(
        seqs,
        heads,
        head_width,
        edge,
        block_out,
        stream_grad,
        mlp_grads,
        rec_grads,
        blocks,
        vectors,
        norm_grads,
        vec,
    )
    return (
        block_out.reshape(stream.shape),
        stream_grad.reshape(stream.shape),
        norm_in_grad[0],
        w_branch_grad[:, :channels],
        w_input_grad[:, :channels],
        taps_grad[:, :channels],
        conv_bias_grad[0, :channels],
        gate_r_grad,
        bias_r_grad[0, :channels],
        gate_i_grad,
        bias_i_grad[0, :channels],
        decay_grad[0, :channels],
        w_out_grad[:channels],
        norm_mlp_grad[0],
        w_gate_grad,
        w_up_grad,
        w_down_grad,
        final_state[:, :channels],
        final_conv[:, :, :channels],
    )


def solution(mesh):
    seq_rows = P(None, "seq", None)
    columns = P(None, "mp")
    channel = P("mp")
    return jax.shard_map(
        per_device,
        mesh=mesh,
        in_specs=(
            seq_rows,
            P(),
            columns,
            columns,
            columns,
            channel,
            P("mp", None, None),
            channel,
            P("mp", None, None),
            channel,
            channel,
            P("mp", None),
            P(),
            columns,
            columns,
            P("mp", None),
            columns,
            P(None, None, "mp"),
            P(),
            seq_rows,
        ),
        out_specs=(
            seq_rows,
            seq_rows,
            P(),
            P("seq", "mp"),
            P("seq", "mp"),
            columns,
            channel,
            P("mp", None, None),
            channel,
            P("mp", None, None),
            channel,
            channel,
            P("mp", "seq"),
            P(),
            P("seq", "mp"),
            P("seq", "mp"),
            P("mp", "seq"),
            columns,
            P(None, None, "mp"),
        ),
        check_vma=False,
    )
```

```python
import functools

import jax
import jax.numpy as jnp
from jax import lax
from jax.experimental import pallas as pl
from jax.experimental.pallas import tpu as pltpu
from jax.sharding import PartitionSpec as P

MESH = pl.DeviceIdType.MESH
RATE_SCALE = 8.0
EPS = 1e-06
GELU_C = 0.7978845608028654
GELU_K = 0.044715
CONTRACT_ROWS = (((0,), (0,)), ((), ()))
CONTRACT_LAST = (((1,), (1,)), ((), ()))
TILE = 8
LANES = 128
ROWS = 32
CHUNK = 16
SKEW = 2
GROUP = 16
WEIGHT_STEPS = 8
COPIES = 8
F32 = jnp.float32
BF16 = jnp.bfloat16
VMEM = pl.BlockSpec(memory_space=pltpu.VMEM)
HBM = pl.BlockSpec(memory_space=pl.ANY)


def dot(a, b):
    return jnp.dot(a, b, preferred_element_type=F32)


def matmul_back(a, b):
    return lax.dot_general(a, b, CONTRACT_LAST, preferred_element_type=F32)


def block(i, size):
    return pl.ds(pl.multiple_of(i * size, size), size)


def gelu(x):
    t = jnp.tanh(GELU_C * (x + GELU_K * (x * x * x)))
    return 0.5 * x * (1.0 + t)


def gelu_both(x):
    x2 = x * x
    t = jnp.tanh(GELU_C * (x + GELU_K * (x2 * x)))
    half = 0.5 * (1.0 + t)
    slope = half + 0.5 * x * (1.0 - t * t) * (GELU_C * (1.0 + (3.0 * GELU_K) * x2))
    return x * half, slope


def one_minus_square(log_a, a):
    y = 2.0 * log_a
    s = 1.0 + y * (1.0 / 8.0)
    for k in (7, 6, 5, 4, 3, 2):
        s = 1.0 + (y * (1.0 / k)) * s
    return jnp.where(y > -0.35, -y * s, 1.0 - a * a)


def get(ref, at):
    return jnp.concatenate([ref[j, at, :] for j in range(ref.shape[0])], axis=-1)


def put(ref, at, value):
    for j in range(ref.shape[0]):
        ref[j, at, :] = value[:, j * LANES : (j + 1) * LANES]


def to_all(axis, src, slots, send, recv):
    size, me = lax.axis_size(axis), lax.axis_index(axis)
    return [
        pltpu.make_async_remote_copy(
            src_ref=src,
            dst_ref=slots.at[me],
            send_sem=send.at[d - 1],
            recv_sem=recv.at[d - 1],
            device_id={axis: lax.rem(me + d, size)},
            device_id_type=MESH,
        )
        for d in range(1, size)
    ]


def to_one(axis, distance, src, dst, send, recv):
    size, me = lax.axis_size(axis), lax.axis_index(axis)
    return pltpu.make_async_remote_copy(
        src_ref=src,
        dst_ref=dst,
        send_sem=send,
        recv_sem=recv,
        device_id={axis: lax.rem(me + distance + size, size)},
        device_id_type=MESH,
    )


def spread_gates(blocks_ref, out_ref, start, width):
    heads, size = blocks_ref.shape[:2]
    for h in range(heads):
        block_h = blocks_ref[h].astype(F32)
        parts = [block_h]
        if h > 0:
            parts.insert(0, jnp.zeros((size, h * size), F32))
        if width > (h + 1) * size:
            parts.append(jnp.zeros((size, width - (h + 1) * size), F32))
        row = jnp.concatenate(parts, axis=1).astype(BF16)
        out_ref[h * size : (h + 1) * size, start : start + width] = row
    if width > heads * size:
        rest = jnp.zeros((width - heads * size, width), BF16)
        out_ref[heads * size : width, start : start + width] = rest


def forward_kernel(
    span,
    x_in,
    w_input_in,
    w_branch_in,
    gain_ref,
    taps_ref,
    conv_bias_ref,
    decay_ref,
    bias_r_ref,
    bias_i_ref,
    gate_r_ref,
    gate_i_ref,
    fresh_ref,
    state_ref,
    conv_init_ref,
    normed_out,
    branch_out,
    pad_out,
    pre_out,
    hidden_out,
    mixed_ref,
    carry_ref,
    sums_ref,
    gates_ref,
    vec_ref,
    ends_ref,
    x_ref,
    w_input_ref,
    w_branch_ref,
    normed_ref,
    branch_ref,
    pad_ref,
    pre_ref,
    hidden_ref,
    act_ref,
    a_ref,
    b_ref,
    conv_ref,
    tail_ref,
    tail_in,
    mine_ref,
    load_sem,
    store_sem,
    normed_sem,
    send1,
    recv1,
    send_t,
    recv_t,
):
    seqs = state_ref.shape[0]
    width = taps_ref.shape[1]
    taps = taps_ref.shape[0]
    rows = seqs * span
    devices, me = lax.axis_size("seq"), lax.axis_index("seq")
    local = pltpu.make_async_copy
    group = 2 * span
    groups = rows // group

    def x_load(g):
        at = block(g, group)
        return local(x_in.at[at], x_ref.at[at], load_sem.at[g])

    weight_loads = [
        local(w_input_in, w_input_ref, load_sem.at[groups]),
        local(w_branch_in, w_branch_ref, load_sem.at[groups + 1]),
    ]
    x_load(0).start()
    weight_loads[0].start()
    for g in range(1, groups):
        x_load(g).start()
    weight_loads[1].start()

    enter_all(("seq",))
    spread_gates(gate_r_ref, gates_ref, 0, width)
    spread_gates(gate_i_ref, gates_ref, width, width)
    vec_ref[0:1, :] = conv_bias_ref[...]
    vec_ref[1:2, :] = jax.nn.softplus(-decay_ref[...])
    keep = [1.0 - fresh_ref[s].astype(F32) for s in range(seqs)]

    def normed_store(g):
        at = block(g, group)
        return local(normed_ref.at[at], normed_out.at[at], normed_sem.at[g])

    @pl.loop(0, groups)
    def _(g):
        x_load(g).wait()

        @pl.loop(0, group // CHUNK)
        def _(q):
            at = block(g * (group // CHUNK) + q, CHUNK)
            x = x_ref[at, :]
            normed_ref[at, :] = (x * mean_square(x) * gain_ref[...]).astype(BF16)

        normed_store(g).start()

        @pl.when(g == 0)
        def _():
            weight_loads[0].wait()

        conv = dot(normed_ref[block(g, group), :], w_input_ref[...])
        for j in range(group // span):
            pad_ref[g * (group // span) + j, pl.ds(TILE, span), :] = conv[
                j * span : (j + 1) * span
            ]

    for s in range(seqs):
        tail_ref[s] = pad_ref[s, pl.ds(span, TILE), :]
    tail_copy = to_one("seq", 1, tail_ref, tail_in, send_t.at[0], recv_t.at[0])
    tail_copy.start()
    weight_loads[1].wait()

    @pl.loop(0, groups)
    def _(g):
        branch_ref[block(g, group), :] = dot(normed_ref[block(g, group), :], w_branch_ref[...])

    stores = [
        local(source, target, store_sem.at[i])
        for i, (source, target) in enumerate(
            (
                (branch_ref, branch_out),
                (pad_ref, pad_out),
                (pre_ref, pre_out),
                (hidden_ref, hidden_out),
            )
        )
    ]
    stores[0].start()
    tail_copy.wait()
    lead = jnp.zeros((TILE - taps + 1, width), F32)
    for s in range(seqs):
        initial = jnp.concatenate(
            [lead] + [conv_init_ref[k, s : s + 1, :] * keep[s] for k in range(taps - 1)], axis=0
        )
        pad_ref[s, pl.ds(0, TILE), :] = jnp.where(me == 0, initial, tail_in[s])
    stores[1].start()

    @pl.loop(0, seqs)
    def _(s):
        @pl.loop(0, span // ROWS)
        def _(q):
            part = pad_ref[s, pl.ds(pl.multiple_of(q * ROWS, ROWS), ROWS + TILE), :]
            total = vec_ref[0:1, :]
            for k in range(taps):
                first = TILE - (taps - 1) + k
                total = total + taps_ref[k : k + 1, :] * part[first : first + ROWS]
            conv_ref[block(q, ROWS), :] = total

        pre = dot(conv_ref[...].astype(BF16), gates_ref[...])
        pre_ref[block(s, span), :width] = pre[:, :width] + bias_r_ref[...]
        pre_ref[block(s, span), width:] = pre[:, width:] + bias_i_ref[...]

        @pl.loop(0, span // ROWS)
        def _(q):
            at = block(s * (span // ROWS) + q, ROWS)
            conv = conv_ref[block(q, ROWS), :]
            recall = jax.nn.sigmoid(pre_ref[at, :width])
            gate = jax.nn.sigmoid(pre_ref[at, width:])
            log_a = (-RATE_SCALE * vec_ref[1:2, :]) * recall
            a = jnp.exp(log_a)
            put(a_ref, at, a)
            put(b_ref, at, jnp.sqrt(one_minus_square(log_a, a)) * gate * conv)

    stores[2].start()

    def at_time(ref, t):
        return get(ref, pl.ds(t, seqs, stride=span))

    def step(t, value):
        prod, state = value
        a = at_time(a_ref, t)
        return prod * a, a * state + at_time(b_ref, t)

    ones = jnp.ones((seqs, width), F32)
    prod, state = lax.fori_loop(0, span, step, (ones, jnp.zeros_like(ones)), unroll=8)
    mine_ref[0] = prod
    mine_ref[1] = state
    sums_ref[me] = mine_ref[...]
    copies = to_all("seq", mine_ref, sums_ref, send1, recv1)
    for copy in copies:
        copy.start()

    @pl.loop(0, rows // ROWS)
    def _(q):
        at = block(q, ROWS)
        act_ref[at, :] = gelu(branch_ref[at, :])

    for copy in copies:
        copy.wait()

    def carry_step(j, carry):
        both = sums_ref[j]
        return jnp.where(j < me, both[0] * carry + both[1], carry)

    start = jnp.concatenate([state_ref[s : s + 1, :] * keep[s] for s in range(seqs)], axis=0)
    carry = lax.fori_loop(0, devices - 1, carry_step, start)
    carry_ref[...] = carry

    def final(t, state):
        state = at_time(a_ref, t) * state + at_time(b_ref, t)
        put(hidden_ref, pl.ds(t, seqs, stride=span), state)
        return state

    last = lax.fori_loop(0, span, final, carry, unroll=8)
    stores[3].start()
    ends_ref[0:seqs, :] = jnp.where(me == devices - 1, last, 0.0)
    for s in range(seqs):
        ends_ref[(s + 1) * TILE : (s + 2) * TILE, :] = jnp.where(
            me == devices - 1, pad_ref[s, pl.ds(span, TILE), :], 0.0
        )

    @pl.loop(0, rows // ROWS)
    def _(q):
        at = block(q, ROWS)
        mixed_ref[at, :] = (get(hidden_ref, at) * act_ref[at, :]).astype(BF16)

    for copy in stores:
        copy.wait()
    for g in range(groups):
        normed_store(g).wait()


def backward_kernel(
    span,
    heads,
    block_part_in,
    own_in,
    low_in,
    w_out_in,
    branch_in,
    hidden_in,
    pre_in,
    pad_in,
    normed_in,
    mixed_in,
    carry_ref,
    sums_ref,
    taps_ref,
    vec_ref,
    gates_ref,
    block_out,
    rec_out,
    grad_branch_ref,
    input_ref,
    acc_ref,
    blocks_ref,
    part,
    inbox,
    out,
    send_up,
    send_down,
    recv_up,
    recv_down,
    own_ref,
    resid_low,
    w_out_ref,
    branch_ref,
    hidden_ref,
    pre_ref,
    pad_ref,
    normed_ref,
    mixed_ref,
    a_ref,
    gd_ref,
    grad_ref,
    direct_ref,
    gpad_ref,
    heads_ref,
    low_ref,
    gates_grad,
    stage_ref,
    mine_ref,
    entries_ref,
    head_ref,
    head_in,
    load_sem,
    part_sem,
    store_sem,
    stage_sem,
    send1,
    recv1,
    send_t,
    recv_t,
):
    seqs, width = carry_ref.shape
    taps = taps_ref.shape[0]
    rows = seqs * span
    devices, me = lax.axis_size("seq"), lax.axis_index("seq")
    n, z = lax.axis_size("mp"), lax.axis_index("mp")
    chunks = rows // CHUNK
    size = GROUP * CHUNK
    held = part.shape[0] // size
    groups = chunks // GROUP
    sems = (send_up, send_down, recv_up, recv_down)
    local = pltpu.make_async_copy

    def part_load(g):
        slot = lax.rem(g, held)
        return local(block_part_in.at[block(g, size)], part.at[block(slot, size)], part_sem.at[slot])

    loads = [
        local(source, target, load_sem.at[i])
        for i, (source, target) in enumerate(
            (
                (own_in, own_ref),
                (low_in, resid_low),
                (w_out_in, w_out_ref),
                (pre_in, pre_ref),
                (branch_in, branch_ref),
                (hidden_in, hidden_ref),
                (pad_in, pad_ref),
                (mixed_in, mixed_ref),
                (normed_in, normed_ref),
            )
        )
    ]
    part_load(0).start()
    for copy in loads[:6]:
        copy.start()
    for g in range(1, held):
        part_load(g).start()
    for copy in loads[6:]:
        copy.start()
    acc_ref[...] = jnp.zeros_like(acc_ref)
    enter_all(("seq", "mp"))

    def decay(at):
        recall = jax.nn.sigmoid(pre_ref[at, :width])
        log_a = (-RATE_SCALE * vec_ref[1:2, :]) * recall
        return recall, log_a, jnp.exp(log_a)

    def piece_direct(s):
        @pl.when(s == 0)
        def _():
            for copy in loads[1:6]:
                copy.wait()

        grad_ref[...] = matmul_back(resid_low[block(s, span), :], w_out_ref[...])

        @pl.loop(0, span // ROWS)
        def _(q):
            at = block(s * (span // ROWS) + q, ROWS)
            put(a_ref, at, decay(at)[2])
            act, slope = gelu_both(branch_ref[at, :])
            grad = grad_ref[block(q, ROWS), :]
            put(gd_ref, at, grad * act)
            grad_branch_ref[at, :] = (grad * get(hidden_ref, at) * slope).astype(BF16)

    def at_time(ref, t):
        return get(ref, pl.ds(t, seqs, stride=span))

    zero = jnp.zeros((seqs, width), F32)
    entry_copies = to_all("seq", mine_ref, entries_ref, send1, recv1)

    def piece_entry(_):
        def step(k, through):
            t = span - 1 - k
            return at_time(a_ref, t) * (at_time(gd_ref, t) + through)

        mine_ref[...] = lax.fori_loop(0, span, step, zero, unroll=8)
        entries_ref[me] = mine_ref[...]
        for copy in entry_copies:
            copy.start()

    def piece_state(_):
        for copy in entry_copies:
            copy.wait()

        def back_step(k, through):
            j = devices - 1 - k
            return jnp.where(j > me, entries_ref[j] + sums_ref[j, 0] * through, through)

        incoming = lax.fori_loop(0, devices - 1, back_step, zero)

        def final(k, through):
            t = span - 1 - k
            grad = at_time(gd_ref, t) + through
            put(gd_ref, pl.ds(t, seqs, stride=span), grad)
            return at_time(a_ref, t) * grad

        lax.fori_loop(0, span, final, incoming, unroll=8)

    def add(k, value):
        acc_ref[k] += fold(value)

    parts = 2

    def piece_gates(i):
        s = i // parts
        quarters = span // ROWS // parts

        @pl.when(i == 0)
        def _():
            loads[6].wait()

        @pl.loop(lax.rem(i, parts) * quarters, (lax.rem(i, parts) + 1) * quarters)
        def _(q):
            at = block(s * (span // ROWS) + q, ROWS)
            part_rows = pad_ref[s, pl.ds(pl.multiple_of(q * ROWS, ROWS), ROWS + TILE), :]
            conv = vec_ref[0:1, :]
            for k in range(taps):
                first = TILE - (taps - 1) + k
                conv = conv + taps_ref[k : k + 1, :] * part_rows[first : first + ROWS]
            heads_ref[at, :] = conv.astype(BF16)
            recall, log_a, a = decay(at)
            gate = jax.nn.sigmoid(pre_ref[at, width:])
            square = one_minus_square(log_a, a)
            inverse = lax.rsqrt(square)
            root = jnp.sqrt(square)
            grad = get(gd_ref, at)
            hidden = get(hidden_ref, at)
            before_at = pl.multiple_of(jnp.maximum(s * span + q * ROWS - TILE, 0), TILE)
            earlier = get(hidden_ref, pl.ds(before_at, TILE))
            first_row = jnp.where(q == 0, carry_ref[pl.ds(s, 1), :], earlier[TILE - 1 :])
            place = lax.broadcasted_iota(jnp.int32, (ROWS, width), 0)
            prev = jnp.where(place == 0, first_row, pltpu.roll(hidden, 1, 0))
            grad_log = grad * a * (prev - gate * conv * a * inverse)
            through = grad_log * recall
            pre_r = through * (1.0 - recall) * (-RATE_SCALE * vec_ref[1:2, :])
            direct = grad * root * gate
            pre_i = direct * conv * (1.0 - gate)
            low_ref[at, :width] = pre_r.astype(BF16)
            low_ref[at, width:] = pre_i.astype(BF16)
            direct_ref[block(q, ROWS), :] = direct
            add(0, through)
            add(1, pre_r)
            add(2, pre_i)

        @pl.when(lax.rem(i, parts) == parts - 1)
        def _():
            whole = direct_ref[...] + matmul_back(low_ref[block(s, span), :], gates_ref[...])
            gpad_ref[s, pl.ds(0, span), :] = whole
            head_ref[s] = whole[:TILE]

    head_copy = to_one("seq", -1, head_ref, head_in, send_t.at[0], recv_t.at[0])

    def piece_head(_):
        head_copy.start()

    def piece_taps(i):
        for j in range(2):
            taps_of(2 * i + j)

    def taps_of(s):
        @pl.loop(0, span // ROWS)
        def _(q):
            at = pl.multiple_of(q * ROWS, ROWS)
            part_rows = pad_ref[s, pl.ds(at, ROWS + TILE), :]
            grad = gpad_ref[s, pl.ds(at, ROWS), :]
            add(3, grad)
            for k in range(taps):
                first = TILE - (taps - 1) + k
                add(4 + k, grad * part_rows[first : first + ROWS])

    def piece_tail(_):
        head_copy.wait()
        for s in range(seqs):
            gpad_ref[s, pl.ds(span, TILE), :] = jnp.where(me == devices - 1, 0.0, head_in[s])

    def piece_input(i):
        for j in range(2):
            input_of(2 * i + j)

    def input_of(s):
        @pl.loop(0, span // ROWS)
        def _(q):
            part_rows = gpad_ref[s, pl.ds(pl.multiple_of(q * ROWS, ROWS), ROWS + TILE), :]
            total = taps_ref[taps - 1 : taps, :] * part_rows[0:ROWS]
            for k in range(taps - 1):
                first = taps - 1 - k
                total = total + taps_ref[k : k + 1, :] * part_rows[first : first + ROWS]
            input_ref[block(s * (span // ROWS) + q, ROWS), :] = total.astype(BF16)

    def contract(left, right):
        return lax.dot_general(left, right, CONTRACT_ROWS, preferred_element_type=F32)

    head = blocks_ref.shape[0]

    def piece_gates_grad(i):
        @pl.when(i == 0)
        def _():
            gates_grad[...] = contract(heads_ref[...], low_ref[:, :width])

        @pl.when(i == 1)
        def _():
            gates_grad[...] = contract(heads_ref[...], low_ref[:, width:])

        place = lax.broadcasted_iota(jnp.int32, (head, width), 1)
        line = jnp.zeros((head, width), F32)
        for h in range(heads):
            row = gates_grad[h * head : (h + 1) * head, :]
            inside = jnp.logical_and(place >= h * head, place < (h + 1) * head)
            line = jnp.where(inside, row, line)

        for j in range(2):

            @pl.when(i == j)
            def _():
                blocks_ref[:, j * width : (j + 1) * width] = line

    tall = resid_low.shape[1] // WEIGHT_STEPS

    def stage_store(i):
        at = block(lax.rem(i, WEIGHT_STEPS), tall)
        slot = lax.rem(i, 2)
        return local(stage_ref.at[slot], rec_out.at[i // WEIGHT_STEPS, at], stage_sem.at[slot])

    def piece_weights(i):
        @pl.when(i == 0)
        def _():
            loads[7].wait()
            loads[8].wait()

        @pl.loop(2 * i, 2 * i + 2)
        def _(j):
            weight_of(j)

    def weight_of(i):
        @pl.when(i >= 2)
        def _():
            stage_store(i - 2).wait()

        at = block(lax.rem(i, WEIGHT_STEPS), tall)
        slot = lax.rem(i, 2)
        for which, (left, right) in enumerate(
            ((resid_low, mixed_ref), (normed_ref, grad_branch_ref), (normed_ref, input_ref))
        ):
            @pl.when(i // WEIGHT_STEPS == which)
            def _():
                stage_ref[slot] = contract(left[:, at], right[...])

        stage_store(i).start()

    weights = 3 * WEIGHT_STEPS
    plan = []
    begin = 3
    for work, times, gap in (
        (piece_direct, seqs, 0),
        (piece_entry, 1, 1),
        (piece_state, 1, 0),
        (piece_gates, parts * seqs, 0),
        (piece_head, 1, 0),
        (piece_taps, seqs // 2, 0),
        (piece_tail, 1, 0),
        (piece_input, seqs // 2, 0),
        (piece_gates_grad, 2, 0),
        (piece_weights, weights // 2, 0),
    ):
        plan.append((work, begin, times))
        begin += times + gap

    def run(step):
        for work, first, times in plan:
            @pl.when(jnp.logical_and(step >= first, step < first + times))
            def _():
                work(step - first)

    def before(k):
        @pl.when(k == 0)
        def _():
            loads[0].wait()

        @pl.when(jnp.logical_and(lax.rem(k, GROUP) == 0, k < chunks))
        def _():
            part_load(k // GROUP).wait()

        g = (k - out.shape[0]) // GROUP - 1 + held

        @pl.when(
            jnp.logical_and(
                jnp.logical_and(k >= out.shape[0] + GROUP, lax.rem(k - out.shape[0], GROUP) == 0),
                g < groups,
            )
        )
        def _():
            part_load(g).start()

        run(k)

    def root(c, slot, total):
        out[slot] = own_ref[block(c // 2, CHUNK), :] + total

    def store(c, slot):
        return local(out.at[slot], block_out.at[block(c, CHUNK)], store_sem.at[slot])

    def arrive(c, slot):
        store(c, slot).start()

    def leave(c, slot):
        store(c, slot).wait()

    line_sum(
        "mp", chunks, held * GROUP, part, inbox, out, sems, before, root, arrive, leave
    )

    @pl.loop(chunks + out.shape[0], max(begin, chunks + out.shape[0]))
    def _(k):
        run(k)

    stage_store(weights - 2).wait()
    stage_store(weights - 1).wait()


def backward_call(span, heads, head, *args):
    block_part = args[0]
    low, w_out, branch, hidden, pre, padded, normed, mixed, carry, sums, taps = args[2:13]
    rows, model = block_part.shape
    seqs, width = carry.shape
    devices = lax.axis_size("seq")
    ring = ring_size("mp")
    held = 3 * GROUP * CHUNK
    dma = pltpu.SemaphoreType.DMA
    columns = pltpu.VMEM((width // LANES, rows, LANES), F32)
    return pl.pallas_call(
        functools.partial(backward_kernel, span, heads),
        out_shape=(
            shape((rows, model)),
            shape((3, model, width)),
            shape((rows, width), BF16),
            shape((rows, width), BF16),
            shape((4 + taps.shape[0], TILE, width)),
            shape((head, 2 * width)),
        ),
        in_specs=[HBM] * 10 + [VMEM] * 5,
        out_specs=(HBM,) * 2 + (VMEM,) * 4,
        scratch_shapes=line_scratch("mp", held, model)
        + [
            pltpu.VMEM((rows // 2, model), F32),
            pltpu.VMEM((rows, model), BF16),
            pltpu.VMEM((width, model), BF16),
            pltpu.VMEM((rows, width), F32),
            pltpu.VMEM(hidden.shape, F32),
            pltpu.VMEM(pre.shape, F32),
            pltpu.VMEM(padded.shape, F32),
            pltpu.VMEM((rows, model), BF16),
            pltpu.VMEM((rows, width), BF16),
            columns,
            columns,
            pltpu.VMEM((span, width), F32),
            pltpu.VMEM((span, width), F32),
            pltpu.VMEM((seqs, span + TILE, width), F32),
            pltpu.VMEM((rows, width), BF16),
            pltpu.VMEM((rows, 2 * width), BF16),
            pltpu.VMEM((width, width), F32),
            pltpu.VMEM((2, model // WEIGHT_STEPS, width), F32),
            pltpu.VMEM((seqs, width), F32),
            pltpu.VMEM((devices, seqs, width), F32),
            pltpu.VMEM((seqs, TILE, width), F32),
            pltpu.VMEM((seqs, TILE, width), F32),
            dma((9,)),
            dma((3,)),
            dma((ring,)),
            dma((2,)),
            dma((devices - 1,)),
            dma((devices - 1,)),
            dma((1,)),
            dma((1,)),
        ],
        compiler_params=params(1, 63),
        cost_estimate=cost(200),
        name="backward",
    )(*args)


def line_sum(axis, total, period, part, inbox, out, sems, before, root, arrive, leave):
    send_up, send_down, recv_up, recv_down = sems
    n, z = lax.axis_size(axis), lax.axis_index(axis)
    depth = n // 2
    ring = out.shape[0]

    def root_of(c):
        return depth - 1 + lax.rem(c, 2)

    def up(c, step, side):
        slot = lax.rem(c, ring)
        return pltpu.make_async_remote_copy(
            src_ref=part.at[block(lax.rem(c, period), CHUNK)],
            dst_ref=inbox.at[side, slot],
            send_sem=send_up.at[slot],
            recv_sem=recv_up.at[side, slot],
            device_id={axis: z + step},
            device_id_type=MESH,
        )

    def down(c, step, side):
        slot = lax.rem(c, ring)
        return pltpu.make_async_remote_copy(
            src_ref=out.at[slot],
            dst_ref=out.at[slot],
            send_sem=send_down.at[side, slot],
            recv_sem=recv_down.at[slot],
            device_id={axis: z + step},
            device_id_type=MESH,
        )

    inner = jnp.logical_and(z > 0, z < n - 1)

    @pl.loop(0, total + ring)
    def _(k):
        @pl.when(k >= ring)
        def _():
            c = k - ring
            r = root_of(c)
            step = jnp.where(z < r, 1, -1)
            side = jnp.where(z < r, 0, 1)

            @pl.when(z == r)
            def _():
                down(c, -1, 0).wait_send()
                down(c, 1, 1).wait_send()

            @pl.when(z != r)
            def _():
                up(c, step, side).wait_send()

            @pl.when(jnp.logical_and(z != r, inner))
            def _():
                down(c, -step, side).wait_send()

            leave(c, lax.rem(c, ring))

        before(k)

        for i in reversed(range(n + 1)):
            c = k - SKEW * i
            valid = jnp.logical_and(c >= 0, c < total)
            c = jnp.clip(c, 0, total - 1)
            at = block(lax.rem(c, period), CHUNK)
            slot = lax.rem(c, ring)
            r = root_of(c)
            step = jnp.where(z < r, 1, -1)
            side = jnp.where(z < r, 0, 1)
            if i > depth:
                here = jnp.logical_and(z != r, jnp.abs(z - r) == i - depth)

                @pl.when(jnp.logical_and(valid, here))
                def _():
                    down(c, -step, side).wait_recv()

                    @pl.when(inner)
                    def _():
                        down(c, -step, side).start()

                    arrive(c, slot)
            elif i == depth:

                @pl.when(jnp.logical_and(valid, z == r))
                def _():
                    up(c, 1, 0).wait_recv()
                    up(c, -1, 1).wait_recv()
                    root(c, slot, part[at, :] + inbox[0, slot] + inbox[1, slot])
                    down(c, -1, 0).start()
                    down(c, 1, 1).start()
                    arrive(c, slot)
            else:
                here = jnp.where(z < r, z, n - 1 - z) == i

                @pl.when(jnp.logical_and(valid, jnp.logical_and(z != r, here)))
                def _():
                    if i > 0:
                        up(c, step, side).wait_recv()
                        part[at, :] += inbox[side, slot]
                    up(c, step, side).start()


def ring_size(axis):
    return SKEW * lax.axis_size(axis) + 4


def line_scratch(axis, rows, model):
    dma = pltpu.SemaphoreType.DMA
    ring = ring_size(axis)
    return [
        pltpu.VMEM((rows, model), F32),
        pltpu.VMEM((2, ring, CHUNK, model), F32),
        pltpu.VMEM((ring, CHUNK, model), F32),
        dma((ring,)),
        dma((2, ring)),
        dma((2, ring)),
        dma((ring,)),
    ]


def mean_square(x):
    return lax.rsqrt(jnp.mean(x * x, axis=-1, keepdims=True) + EPS)


def nothing(*_):
    pass


def fold(value):
    total = value[0:TILE]
    for i in range(1, value.shape[0] // TILE):
        total = total + value[i * TILE : (i + 1) * TILE]
    return total


def norm_grad(value, gain, grad, acc_ref):
    q = mean_square(value)
    e = gain * grad
    acc_ref[...] += fold(grad * value * q)
    return q * e - value * (q * q * q) * jnp.mean(e * value, axis=-1, keepdims=True)


def middle_kernel(
    mixed_in,
    w_out_in,
    x_in,
    og_in,
    gain_ref,
    w_gate_in,
    w_up_in,
    w_down_in,
    normed_out,
    hidden_out,
    gate_out,
    up_out,
    glow_out,
    block_out,
    low_out,
    own_grad_out,
    weight_out,
    own_ref,
    acc_ref,
    part,
    inbox,
    out,
    send_up,
    send_down,
    recv_up,
    recv_down,
    mixed,
    w_out,
    w_gate,
    w_up,
    w_down,
    normed,
    rows_ref,
    og_ref,
    glow,
    gate_val,
    up_val,
    grad_hidden,
    hidden,
    grad_gate,
    grad_up,
    block_part,
    low,
    weight_sem,
    row_sem,
    og_sem,
    act_sem,
    low_sem,
    own_sem,
    again_sem,
    stage_sem,
):
    n, z = lax.axis_size("mp"), lax.axis_index("mp")
    count = part.shape[0] // CHUNK
    size = GROUP * CHUNK
    groups = count // GROUP
    ring = out.shape[0]
    sems = (send_up, send_down, recv_up, recv_down)
    local = pltpu.make_async_copy

    loads = [
        local(source, target, weight_sem.at[i])
        for i, (source, target) in enumerate(
            (
                (mixed_in, mixed),
                (w_out_in, w_out),
                (w_gate_in, w_gate),
                (w_up_in, w_up),
                (w_down_in, w_down.at[slice(0, w_down_in.shape[0])]),
            )
        )
    ]
    for copy in loads:
        copy.start()
    deep = w_down_in.shape[0]

    def og_load(g):
        return local(og_in.at[block(g, size)], og_ref, og_sem.at[0])

    og_load(0).start()
    enter_all(("mp",))
    acc_ref[...] = jnp.zeros_like(acc_ref)
    loads[0].wait()
    loads[1].wait()

    def is_root(c):
        return z == n // 2 - 1 + lax.rem(c, 2)

    def row_load(source, c):
        slot = lax.rem(c, ring)
        at = block(lax.rem(c, count), CHUNK)
        return local(source.at[at], rows_ref.at[slot], row_sem.at[slot])

    acts = (
        (normed, normed_out),
        (glow, glow_out),
        (hidden, hidden_out),
        (grad_gate, gate_out),
        (grad_up, up_out),
        (block_part, block_out),
    )

    def act_store(i, g):
        source, target = acts[i]
        source = source.at[lax.rem(g, 2)] if i == 0 else source
        return local(source, target.at[block(g, size)], act_sem.at[i])

    def at_tick(k, first, work):
        g = (k - first) // GROUP

        @pl.when(
            jnp.logical_and(
                jnp.logical_and(k >= first, k < first + GROUP * groups),
                lax.rem(k - first, GROUP) == 0,
            )
        )
        def _():
            work(g)

    def project(g):
        part[block(g, size), :] = dot(mixed[block(g, size), :], w_out[...])

    def piece_gate(g):
        @pl.when(g == 0)
        def _():
            for copy in loads[2:]:
                copy.wait()

        gate_val[...] = dot(normed[lax.rem(g, 2)], w_gate[...])
        act_store(0, g).start()

    def piece_up(g):
        up_val[...] = dot(normed[lax.rem(g, 2)], w_up[...])

        @pl.when(g > 0)
        def _():
            for i in range(1, 6):
                act_store(i, g - 1).wait()

    def piece_low(g):
        og_load(g).wait()

        @pl.loop(0, size // ROWS)
        def _(q):
            glow[block(q, ROWS), :] = og_ref[block(q, ROWS), :].astype(BF16)

        @pl.when(g + 1 < groups)
        def _():
            og_load(g + 1).start()

        act_store(1, g).start()
        act_store(0, g).wait()

    def piece_hidden(g):
        grad_hidden[...] = matmul_back(glow[...], w_down[:deep, :])

    def piece_act(g):
        @pl.loop(0, size // CHUNK)
        def _(q):
            at = block(q, CHUNK)
            up = up_val[at, :]
            grad = grad_hidden[at, :]
            act, slope = gelu_both(gate_val[at, :])
            hidden[at, :] = (act * up).astype(BF16)
            grad_gate[at, :] = (grad * up * slope).astype(BF16)
            grad_up[at, :] = (grad * act).astype(BF16)

        for i in range(2, 5):
            act_store(i, g).start()

    def piece_down(g):
        block_part[...] = dot(hidden[...], w_down[:deep, :])
        act_store(5, g).start()

    def piece_back_gate(g):
        part[block(g, size), :] = matmul_back(grad_gate[...], w_gate[...])

    def piece_back_up(g):
        part[block(g, size), :] += matmul_back(grad_up[...], w_up[...])

    tokens = count * CHUNK
    half = tokens // 2
    quarter = half // 2
    again = [
        local(source, target, again_sem.at[i])
        for i, (source, target) in enumerate(
            (
                (normed_out, w_down.at[slice(0, tokens)]),
                (gate_out, w_gate.at[slice(0, tokens)]),
                (up_out, w_up.at[slice(0, tokens)]),
                (hidden_out, w_gate.at[slice(tokens, 2 * tokens)]),
                (glow_out.at[slice(0, half)], w_down.at[slice(tokens, tokens + half)]),
                (glow_out.at[slice(half, half + quarter)], normed.at[0]),
                (glow_out.at[slice(half + quarter, tokens)], normed.at[1]),
            )
        )
    ]
    tall = w_gate.shape[0] // WEIGHT_STEPS
    stages = (gate_val, up_val, grad_hidden)

    def stage_store(which, i):
        return local(stages[which], weight_out.at[which, block(i, tall)], stage_sem.at[which])

    def piece_reload():
        for i in range(1, 6):
            act_store(i, groups - 1).wait()
        for copy in again:
            copy.start()

    def piece_ready():
        for copy in again:
            copy.wait()

    def contract(left, right):
        return lax.dot_general(left, right, CONTRACT_ROWS, preferred_element_type=F32)

    def piece_weight(step):
        i = step // 3
        at = block(i, tall)
        for which in range(3):

            @pl.when(lax.rem(step, 3) == which)
            def _():
                @pl.when(i > 0)
                def _():
                    stage_store(which, i - 1).wait()

                stage = stages[which]
                if which == 0:
                    stage[...] = contract(w_down[:tokens, at], w_gate[:tokens, :])
                elif which == 1:
                    stage[...] = contract(w_down[:tokens, at], w_up[:tokens, :])
                else:
                    stage[...] = contract(
                        w_down[tokens : tokens + half, at], w_gate[tokens : tokens + half, :]
                    )
                    middle = tokens + half + quarter
                    stage[...] += contract(normed[0, :, at], w_gate[tokens + half : middle, :])
                    stage[...] += contract(normed[1, :, at], w_gate[middle : 2 * tokens, :])
                stage_store(which, i).start()

    first = GROUP + SKEW * n
    spare = GROUP * groups + ring + 3
    first_weight = spare + 3
    weights = 3 * WEIGHT_STEPS

    def before(k):
        @pl.when(k == spare)
        def _():
            piece_reload()

        @pl.when(k == first_weight - 1)
        def _():
            piece_ready()

        @pl.when(jnp.logical_and(k >= first_weight, k < first_weight + weights))
        def _():
            piece_weight(k - first_weight)

        @pl.when(jnp.logical_and(k < count, is_root(k)))
        def _():
            row_load(x_in, k).start()

        @pl.when(
            jnp.logical_and(jnp.logical_and(k >= count, k < 2 * count), is_root(k))
        )
        def _():
            row_load(og_in, k).start()

        at_tick(k, 0, project)
        at_tick(k, first, piece_gate)
        at_tick(k, first + 1, piece_up)
        at_tick(k, first + 2, piece_low)
        at_tick(k, first + 3, piece_hidden)
        at_tick(k, first + 4, piece_act)
        at_tick(k, first + 6, piece_down)
        at_tick(k, GROUP + ring, piece_back_gate)
        at_tick(k, GROUP + ring + 2, piece_back_up)

    def root(c, slot, total):
        j = lax.rem(c, count)
        mine = block(j // 2, CHUNK)
        row_load(x_in, c).wait()

        @pl.when(c < count)
        def _():
            value = rows_ref[slot] + total
            own_ref[mine, :] = value
            out[slot] = (value * mean_square(value) * gain_ref[...]).astype(BF16).astype(F32)

        @pl.when(c >= count)
        def _():
            back = norm_grad(own_ref[mine, :], gain_ref[...], total, acc_ref)
            out[slot] = rows_ref[slot] + back

    def low_store(c, slot):
        at = block(lax.rem(c, count), CHUNK)
        return local(low.at[slot], low_out.at[at], low_sem.at[slot])

    def own_store(c, slot):
        at = block(lax.rem(c, count) // 2, CHUNK)
        return local(out.at[slot], own_grad_out.at[at], own_sem.at[slot])

    def arrive(c, slot):
        @pl.when(c < count)
        def _():
            normed[lax.rem(c // GROUP, 2), block(lax.rem(c, GROUP), CHUNK), :] = out[slot].astype(BF16)

        @pl.when(c >= count)
        def _():
            low[slot] = out[slot].astype(BF16)
            low_store(c, slot).start()

            @pl.when(is_root(c))
            def _():
                own_store(c, slot).start()

    def leave(c, slot):
        @pl.when(c >= count)
        def _():
            low_store(c, slot).wait()

            @pl.when(is_root(c))
            def _():
                own_store(c, slot).wait()

    line_sum("mp", 2 * count, count, part, inbox, out, sems, before, root, arrive, leave)

    for which in range(3):
        stage_store(which, WEIGHT_STEPS - 1).wait()


def middle_call(*args):
    mixed, w_out, x, og, gain, w_gate, w_up, w_down = args
    rows, model = x.shape
    width, hidden = mixed.shape[1], w_gate.shape[1]
    size = GROUP * CHUNK
    dma = pltpu.SemaphoreType.DMA
    ring = ring_size("mp")
    act = shape((rows, hidden), BF16)
    tall = shape((rows, model), BF16)
    return pl.pallas_call(
        middle_kernel,
        out_shape=(
            tall,
            act,
            act,
            act,
            tall,
            shape((rows, model)),
            tall,
            shape((rows // 2, model)),
            shape((3, model, hidden)),
            shape((rows // 2, model)),
            shape((TILE, model)),
        ),
        in_specs=[HBM] * 4 + [VMEM] + [HBM] * 3,
        out_specs=(HBM,) * 9 + (VMEM,) * 2,
        scratch_shapes=line_scratch("mp", rows, model)
        + [
            pltpu.VMEM((rows, width), BF16),
            pltpu.VMEM((width, model), BF16),
            pltpu.VMEM((model, hidden), BF16),
            pltpu.VMEM((model, hidden), BF16),
            pltpu.VMEM((max(hidden, rows * 3 // 2), model), BF16),
            pltpu.VMEM((2, size, model), BF16),
            pltpu.VMEM((ring, CHUNK, model), F32),
            pltpu.VMEM((size, model), F32),
            pltpu.VMEM((size, model), BF16),
            pltpu.VMEM((size, hidden), F32),
            pltpu.VMEM((size, hidden), F32),
            pltpu.VMEM((size, hidden), F32),
            pltpu.VMEM((size, hidden), BF16),
            pltpu.VMEM((size, hidden), BF16),
            pltpu.VMEM((size, hidden), BF16),
            pltpu.VMEM((size, model), F32),
            pltpu.VMEM((ring, CHUNK, model), BF16),
            dma((5,)),
            dma((ring,)),
            dma((1,)),
            dma((6,)),
            dma((ring,)),
            dma((ring,)),
            dma((7,)),
            dma((3,)),
        ],
        compiler_params=params(2, 63),
        cost_estimate=cost(400),
        name="middle",
    )(*args)


def last_kernel(
    own_grad_in,
    x_in,
    grad_branch_in,
    input_in,
    w_branch_in,
    w_input_in,
    gain_ref,
    other_acc,
    sums_in,
    ends_in,
    blocks_in,
    grad_out,
    norm_ref,
    small_out,
    part,
    inbox,
    out,
    send_up,
    send_down,
    recv_up,
    recv_down,
    own_grad_ref,
    x_ref,
    grad_branch,
    input_low,
    w_branch,
    w_input,
    load_sem,
    store_sem,
    acc_ref,
    mine_ref,
    seq_in,
    mp_in,
    send_s,
    recv_s,
    send_m,
    recv_m,
    small,
    small_in,
    send_v,
    recv_v,
):
    count = part.shape[0] // CHUNK
    size = GROUP * CHUNK
    sems = (send_up, send_down, recv_up, recv_down)
    local = pltpu.make_async_copy

    loads = [
        local(source, target, load_sem.at[i])
        for i, (source, target) in enumerate(
            (
                (grad_branch_in, grad_branch),
                (w_branch_in, w_branch),
                (input_in, input_low),
                (w_input_in, w_input),
                (own_grad_in, own_grad_ref),
                (x_in, x_ref),
            )
        )
    ]
    for copy in loads:
        copy.start()
    acc_ref[...] = jnp.zeros_like(acc_ref)
    mine_ref[...] = jnp.zeros_like(mine_ref)
    enter_all(("seq", "mp"))
    for copy in loads[:4]:
        copy.wait()

    kinds = sums_in.shape[0]
    me = lax.axis_index("seq")
    width = sums_in.shape[2]
    height = kinds + ends_in.shape[0]
    head = blocks_in.shape[0]
    for i in range(kinds):
        small[0, i : i + 1, :] = jnp.sum(sums_in[i], axis=0, keepdims=True)
    small[0, kinds:height, :] = ends_in[...]
    small[0, height : height + head, :] = blocks_in[:, :width]
    small[0, height + head :, :] = blocks_in[:, width:]
    levels = small_in.shape[0]

    def exchange(level):
        bit = 1 << level
        partner = me + bit - 2 * bit * lax.rem(me // bit, 2)
        return pltpu.make_async_remote_copy(
            src_ref=small.at[level],
            dst_ref=small_in.at[level],
            send_sem=send_v.at[level],
            recv_sem=recv_v.at[level],
            device_id={"seq": partner},
            device_id_type=MESH,
        )

    spacing = (count - 4) // (levels + 1)
    seq_copies = to_all("seq", mine_ref.at[0], seq_in, send_s, recv_s)
    mp_copies = to_all("mp", mine_ref.at[1], mp_in, send_m, recv_m)
    settled = count + SKEW * (lax.axis_size("mp") // 2)

    def before(k):
        for level in range(levels + 1):

            @pl.when(k == 3 + level * spacing)
            def _():
                if level > 0:
                    exchange(level - 1).wait()
                    total = small[level - 1] + small_in[level - 1]
                    if level < levels:
                        small[level] = total
                    else:
                        small_out[...] = total
                if level < levels:
                    exchange(level).start()

        @pl.when(k == settled)
        def _():
            mine_ref[0, 0:1, :] = jnp.sum(acc_ref[...], axis=0, keepdims=True)
            mine_ref[0, 1:2, :] = jnp.sum(other_acc[...], axis=0, keepdims=True)
            seq_in[me] = mine_ref[0]
            for copy in seq_copies:
                copy.start()

        @pl.when(k == settled + 2)
        def _():
            for copy in seq_copies:
                copy.wait()
            mine_ref[1] = jnp.sum(seq_in[...], axis=0)
            mp_in[lax.axis_index("mp")] = mine_ref[1]
            for copy in mp_copies:
                copy.start()

        @pl.when(jnp.logical_and(lax.rem(k, 4) == 0, k // 4 < count // GROUP))
        def _():
            at = block(k // 4, size)
            part[at, :] = matmul_back(grad_branch[at, :], w_branch[...])
            part[at, :] += matmul_back(input_low[at, :], w_input[...])

        @pl.when(k == 1)
        def _():
            for copy in loads[4:]:
                copy.wait()

    def root(c, slot, total):
        back = norm_grad(x_ref[block(c, CHUNK), :], gain_ref[...], total, acc_ref)
        out[slot] = own_grad_ref[block(c // 2, CHUNK), :] + back

    def store(c, slot):
        return local(out.at[slot], grad_out.at[block(c, CHUNK)], store_sem.at[slot])

    def arrive(c, slot):
        store(c, slot).start()

    def leave(c, slot):
        store(c, slot).wait()

    line_sum("mp", count, count, part, inbox, out, sems, before, root, arrive, leave)

    for copy in mp_copies:
        copy.wait()
    norm_ref[...] = jnp.sum(mp_in[...], axis=0)


def enter_all(axes):
    barrier = pltpu.get_barrier_semaphore()
    count = 0
    for axis in axes:
        size, me = lax.axis_size(axis), lax.axis_index(axis)
        for d in range(1, size):
            pl.semaphore_signal(
                barrier, 1, device_id={axis: lax.rem(me + d, size)}, device_id_type=MESH
            )
        count += size - 1
    pl.semaphore_wait(barrier, count)


def cost(micros):
    return pl.CostEstimate(flops=int(micros * 1e9), bytes_accessed=1 << 20, transcendentals=0)


def nseq_levels():
    return (lax.axis_size("seq") - 1).bit_length()


def last_call(*args):
    x, grad_branch = args[1:3]
    rows, model = x.shape
    width = grad_branch.shape[1]
    lines = args[8].shape[0] + args[9].shape[0] + 2 * args[10].shape[0]
    levels = nseq_levels()
    dma = pltpu.SemaphoreType.DMA
    nseq, nmp = lax.axis_size("seq"), lax.axis_size("mp")
    return pl.pallas_call(
        last_kernel,
        out_shape=(shape((rows, model)), shape((TILE, model)), shape((lines, width))),
        in_specs=[HBM] * 6 + [VMEM] * 5,
        out_specs=(HBM,) + (VMEM,) * 2,
        scratch_shapes=line_scratch("mp", rows, model)
        + [
            pltpu.VMEM((rows // 2, model), F32),
            pltpu.VMEM((rows, model), F32),
            pltpu.VMEM((rows, width), BF16),
            pltpu.VMEM((rows, width), BF16),
            pltpu.VMEM((model, width), BF16),
            pltpu.VMEM((model, width), BF16),
            dma((6,)),
            dma((ring_size("mp"),)),
            pltpu.VMEM((TILE, model), F32),
            pltpu.VMEM((2, TILE, model), F32),
            pltpu.VMEM((nseq, TILE, model), F32),
            pltpu.VMEM((nmp, TILE, model), F32),
            dma((nseq - 1,)),
            dma((nseq - 1,)),
            dma((nmp - 1,)),
            dma((nmp - 1,)),
            pltpu.VMEM((levels, lines, width), F32),
            pltpu.VMEM((levels, lines, width), F32),
            dma((levels,)),
            dma((levels,)),
        ],
        compiler_params=params(4, 62),
        cost_estimate=cost(200),
        name="last_sums",
    )(*args)


def finish_kernel(
    heads,
    grad_in,
    mlp_in,
    rec_in,
    small_hbm,
    norm_hbm,
    decay_hbm,
    grad_out,
    w_gate_out,
    w_up_out,
    w_branch_out,
    w_input_out,
    w_down_out,
    w_out_out,
    gate_r_out,
    gate_i_out,
    taps_out,
    conv_bias_out,
    bias_r_out,
    bias_i_out,
    decay_out,
    norm_in_out,
    norm_mlp_out,
    state_out,
    conv_out,
    tall,
    mlp,
    rec,
    small_in,
    norm_in,
    raw_ref,
    load_sem,
    store_sem,
    extra_sem,
):
    local = pltpu.make_async_copy
    size = grad_in.shape[0] // COPIES
    extra = [
        local(source, target, extra_sem.at[i])
        for i, (source, target) in enumerate(
            ((small_hbm, small_in), (norm_hbm, norm_in), (decay_hbm, raw_ref))
        )
    ]
    for copy in extra:
        copy.start()
    jobs = [(mlp_in, mlp, None), (rec_in, rec, None)]
    for i in range(COPIES):
        at = slice(i * size, (i + 1) * size)
        jobs.append((grad_in.at[at], tall.at[at], grad_out.at[at]))
    loads = [local(source, held, load_sem.at[i]) for i, (source, held, _) in enumerate(jobs)]
    stores = [
        local(held, target, store_sem.at[i])
        for i, (held, target) in enumerate(
            [(held, target) for _, held, target in jobs[2:]]
            + [
                (mlp.at[0], w_gate_out),
                (mlp.at[1], w_up_out),
                (rec.at[1], w_branch_out),
                (rec.at[2], w_input_out),
            ]
        )
    ]
    for copy in loads:
        copy.start()
    for copy in extra:
        copy.wait()
    taps, seqs, edge = taps_out.shape[0], state_out.shape[0], conv_out.shape[0]
    head = gate_r_out.shape[1]
    width = small_in.shape[1]
    decay_out[...] = small_in[0:1, :] * (RATE_SCALE * jax.nn.sigmoid(-raw_ref[...]))
    bias_r_out[...] = small_in[1:2, :]
    bias_i_out[...] = small_in[2:3, :]
    conv_bias_out[...] = small_in[3:4, :]
    taps_out[...] = small_in[4 : 4 + taps, :]
    begin = 4 + taps
    state_out[...] = small_in[begin : begin + seqs, :]
    for s in range(seqs):
        end = begin + seqs + (s + 1) * TILE
        for k in range(edge):
            conv_out[k, s : s + 1, :] = small_in[end - edge + k : end - edge + k + 1, :]
    begin += seqs + seqs * TILE
    for i, target in enumerate((gate_r_out, gate_i_out)):
        line = small_in[begin + i * head : begin + (i + 1) * head, :]
        for h in range(heads):
            turned = line if h == 0 else pltpu.roll(line, width - h * head, 1)
            target[h] = turned[:, :head]
    norm_in_out[...] = norm_in[0:1, :]
    norm_mlp_out[...] = norm_in[1:2, :]
    loads[0].wait()
    loads[1].wait()
    for copy in stores[COPIES:]:
        copy.start()
    w_down_out[...] = mlp[2].T
    w_out_out[...] = rec[0].T
    for i in range(COPIES):
        loads[2 + i].wait()
        stores[i].start()
    for copy in stores:
        copy.wait()


def finish_call(seqs, heads, head, edge, *args):
    stream_grad, mlp_grads, rec_grads, small, norms, decay = args
    rows, model = stream_grad.shape
    own, hidden = mlp_grads.shape[1:]
    width = rec_grads.shape[2]
    taps = edge + 1
    line = shape((1, width))
    tall = shape((rows, model))
    return pl.pallas_call(
        functools.partial(finish_kernel, heads),
        out_shape=(
            tall,
            shape((own, hidden)),
            shape((own, hidden)),
            shape((own, width)),
            shape((own, width)),
            shape((hidden, own)),
            shape((width, own)),
            shape((heads, head, head)),
            shape((heads, head, head)),
            shape((taps, width)),
            line,
            line,
            line,
            line,
            shape((1, model)),
            shape((1, model)),
            shape((seqs, width)),
            shape((edge, seqs, width)),
        ),
        in_specs=[HBM] * 6,
        out_specs=(HBM,) * 5 + (VMEM,) * 13,
        scratch_shapes=[
            pltpu.VMEM((rows, model), F32),
            pltpu.VMEM((3, own, hidden), F32),
            pltpu.VMEM((3, own, width), F32),
            pltpu.VMEM(small.shape, F32),
            pltpu.VMEM(norms.shape, F32),
            pltpu.VMEM(decay.shape, F32),
            pltpu.SemaphoreType.DMA((2 + COPIES,)),
            pltpu.SemaphoreType.DMA((4 + COPIES,)),
            pltpu.SemaphoreType.DMA((3,)),
        ],
        compiler_params=pltpu.CompilerParams(vmem_limit_bytes=48 << 20),
        cost_estimate=cost(15),
        name="finish",
    )(*args)


def copy_kernel(source, target, held, load_sem, store_sem):
    size = source.shape[0] // COPIES
    pieces = [slice(i * size, (i + 1) * size) for i in range(COPIES)]
    local = pltpu.make_async_copy
    loads = [local(source.at[p], held.at[p], load_sem.at[i]) for i, p in enumerate(pieces)]
    stores = [local(held.at[p], target.at[p], store_sem.at[i]) for i, p in enumerate(pieces)]
    for copy in loads:
        copy.start()
    for load, store in zip(loads, stores):
        load.wait()
        store.start()
    for copy in stores:
        copy.wait()


def copy_call(array):
    return pl.pallas_call(
        copy_kernel,
        out_shape=shape(array.shape),
        in_specs=[HBM],
        out_specs=HBM,
        scratch_shapes=[
            pltpu.VMEM(array.shape, F32),
            pltpu.SemaphoreType.DMA((COPIES,)),
            pltpu.SemaphoreType.DMA((COPIES,)),
        ],
        compiler_params=pltpu.CompilerParams(vmem_limit_bytes=48 << 20),
        cost_estimate=cost(6),
        name="copy_out",
    )(array)


def params(collective, megabytes=60):
    return pltpu.CompilerParams(
        collective_id=collective, has_side_effects=True, vmem_limit_bytes=megabytes << 20
    )


def shape(dims, dtype=F32):
    return jax.ShapeDtypeStruct(dims, dtype)


def recurrence_forward(span, *args):
    x, w_input = args[:2]
    rows, model = x.shape
    seqs, width = rows // span, w_input.shape[1]
    devices = lax.axis_size("seq")
    dma = pltpu.SemaphoreType.DMA
    groups = seqs // 2
    columns = (width // LANES, rows, LANES)
    padded = (seqs, span + TILE, width)
    return pl.pallas_call(
        functools.partial(forward_kernel, span),
        out_shape=(
            shape((rows, model), BF16),
            shape((rows, width)),
            shape(padded),
            shape((rows, 2 * width)),
            shape(columns),
            shape((rows, width), BF16),
            shape((seqs, width)),
            shape((devices, 2, seqs, width)),
            shape((width, 2 * width), BF16),
            shape((TILE, width)),
            shape(((seqs + 1) * TILE, width)),
        ),
        in_specs=[HBM] * 3 + [VMEM] * 8 + [pl.BlockSpec(memory_space=pltpu.SMEM)] + [VMEM] * 2,
        out_specs=(HBM,) * 5 + (VMEM,) * 6,
        scratch_shapes=[
            pltpu.VMEM((rows, model), F32),
            pltpu.VMEM((model, width), BF16),
            pltpu.VMEM((model, width), BF16),
            pltpu.VMEM((rows, model), BF16),
            pltpu.VMEM((rows, width), F32),
            pltpu.VMEM(padded, F32),
            pltpu.VMEM((rows, 2 * width), F32),
            pltpu.VMEM(columns, F32),
            pltpu.VMEM((rows, width), F32),
            pltpu.VMEM(columns, F32),
            pltpu.VMEM(columns, F32),
            pltpu.VMEM((span, width), F32),
            pltpu.VMEM((seqs, TILE, width), F32),
            pltpu.VMEM((seqs, TILE, width), F32),
            pltpu.VMEM((2, seqs, width), F32),
            dma((groups + 2,)),
            dma((4,)),
            dma((groups,)),
            dma((devices - 1,)),
            dma((devices - 1,)),
            dma((1,)),
            dma((1,)),
        ],
        compiler_params=params(0),
        cost_estimate=cost(50),
        name="recurrence_forward",
    )(*args)


def widen(array, width):
    short = width - array.shape[-1]
    if short == 0:
        return array
    return jnp.pad(array, [(0, 0)] * (array.ndim - 1) + [(0, short)])


def per_device(
    stream,
    norm_in,
    w_branch,
    w_input,
    conv_kernel,
    conv_bias,
    gate_r,
    bias_r,
    gate_i,
    bias_i,
    decay_param,
    w_out,
    norm_mlp,
    w_gate,
    w_up,
    w_down,
    state_init,
    conv_init,
    fresh_rows,
    out_grad,
):
    seqs, span, model = stream.shape
    channels = w_branch.shape[1]
    mlp_dev = w_gate.shape[1]
    heads, head_width = gate_r.shape[:2]
    taps = conv_kernel.shape[0]
    edge = taps - 1
    rows = seqs * span
    devices = lax.axis_size("seq")
    position = lax.axis_index("seq")
    width = -(-channels // 128) * 128

    flat_in = stream.reshape(rows, model)
    flat_grad = out_grad.reshape(rows, model)
    w_branch_p = widen(w_branch, width)
    w_input_p = widen(w_input, width)
    w_out_p = jnp.pad(w_out, ((0, width - channels), (0, 0))) if width > channels else w_out
    taps_p = widen(conv_kernel, width)
    def line(value):
        return widen(value[None], width)

    (
        normed,
        branch,
        padded,
        pre,
        hidden,
        mixed,
        carry,
        sums,
        gates,
        rates,
        ends,
    ) = recurrence_forward(
        span,
        flat_in,
        w_input_p,
        w_branch_p,
        norm_in[None],
        taps_p,
        line(conv_bias),
        line(decay_param),
        line(bias_r),
        line(bias_i),
        gate_r,
        gate_i,
        fresh_rows,
        widen(state_init, width),
        widen(jnp.swapaxes(conv_init, 0, 1), width),
    )
    _, _, _, _, _, block_part, resid_low, own_grad, mlp_grads, own, norm_mlp_acc = middle_call(
        mixed, w_out_p, flat_in, flat_grad, norm_mlp[None], w_gate, w_up, w_down
    )
    mlp_grads = lax.psum_scatter(mlp_grads, "seq", scatter_dimension=1, tiled=True)
    block_out, rec_grads, grad_branch, input_low, acc, blocks = backward_call(
        span,
        heads,
        head_width,
        block_part,
        own,
        resid_low,
        w_out_p,
        branch,
        hidden,
        pre,
        padded,
        normed,
        mixed,
        carry,
        sums,
        taps_p,
        rates,
        gates,
    )

    block_out = copy_call(block_out)
    rec_grads, grad_branch, mlp_grads, block_out = lax.optimization_barrier(
        (rec_grads, grad_branch, mlp_grads, block_out)
    )
    rec_grads = lax.psum_scatter(rec_grads, "seq", scatter_dimension=1, tiled=True)

    stream_grad, norm_grads, small = last_call(
        own_grad,
        flat_in,
        grad_branch,
        input_low,
        w_branch_p,
        w_input_p,
        norm_in[None],
        norm_mlp_acc,
        acc,
        ends,
        blocks,
    )
    (
        stream_grad,
        w_gate_grad,
        w_up_grad,
        w_branch_grad,
        w_input_grad,
        w_down_grad,
        w_out_grad,
        gate_r_grad,
        gate_i_grad,
        taps_grad,
        conv_bias_grad,
        bias_r_grad,
        bias_i_grad,
        decay_grad,
        norm_in_grad,
        norm_mlp_grad,
        final_state,
        final_conv,
    ) = finish_call(
        seqs,
        heads,
        head_width,
        edge,
        stream_grad,
        mlp_grads,
        rec_grads,
        small,
        norm_grads,
        line(decay_param),
    )
    return (
        block_out.reshape(stream.shape),
        stream_grad.reshape(stream.shape),
        norm_in_grad.reshape(-1),
        w_branch_grad[:, :channels],
        w_input_grad[:, :channels],
        taps_grad[:, :channels],
        conv_bias_grad.reshape(-1)[:channels],
        gate_r_grad,
        bias_r_grad.reshape(-1)[:channels],
        gate_i_grad,
        bias_i_grad.reshape(-1)[:channels],
        decay_grad.reshape(-1)[:channels],
        w_out_grad[:channels],
        norm_mlp_grad.reshape(-1),
        w_gate_grad,
        w_up_grad,
        w_down_grad,
        final_state[:, :channels],
        jnp.swapaxes(final_conv, 0, 1)[:, :, :channels],
    )


def solution(mesh):
    seq_rows = P(None, "seq", None)
    columns = P(None, "mp")
    channel = P("mp")
    return jax.shard_map(
        per_device,
        mesh=mesh,
        in_specs=(
            seq_rows,
            P(),
            columns,
            columns,
            columns,
            channel,
            P("mp", None, None),
            channel,
            P("mp", None, None),
            channel,
            channel,
            P("mp", None),
            P(),
            columns,
            columns,
            P("mp", None),
            columns,
            P(None, None, "mp"),
            P(),
            seq_rows,
        ),
        out_specs=(
            seq_rows,
            seq_rows,
            P(),
            P("seq", "mp"),
            P("seq", "mp"),
            columns,
            channel,
            P("mp", None, None),
            channel,
            P("mp", None, None),
            channel,
            channel,
            P("mp", "seq"),
            P(),
            P("seq", "mp"),
            P("seq", "mp"),
            P("mp", "seq"),
            columns,
            P(None, None, "mp"),
        ),
        check_vma=False,
    )
```

```python
import functools

import jax
import jax.numpy as jnp
from jax import lax
from jax.experimental import pallas as pl
from jax.experimental.pallas import tpu as pltpu
from jax.sharding import PartitionSpec as P

MESH = pl.DeviceIdType.MESH
RATE_SCALE = 8.0
EPS = 1e-06
GELU_C = 0.7978845608028654
GELU_K = 0.044715
CONTRACT_ROWS = (((0,), (0,)), ((), ()))
CONTRACT_LAST = (((1,), (1,)), ((), ()))
TILE = 8
LANES = 128
ROWS = 32
CHUNK = 16
SKEW = 2
GROUP = 16
WEIGHT_STEPS = 8
COPIES = 8
F32 = jnp.float32
BF16 = jnp.bfloat16
VMEM = pl.BlockSpec(memory_space=pltpu.VMEM)
HBM = pl.BlockSpec(memory_space=pl.ANY)
PINNED = pl.BlockSpec(memory_space=pltpu.HBM)


def dot(a, b):
    return jnp.dot(a, b, preferred_element_type=F32)


def matmul_back(a, b):
    return lax.dot_general(a, b, CONTRACT_LAST, preferred_element_type=F32)


def by_columns(width, work):
    tile = next(t for t in (512, 384, 256, 128) if width % t == 0)

    @pl.loop(0, width // tile)
    def _(j):
        work(block(j, tile))


def block(i, size):
    return pl.ds(pl.multiple_of(i * size, size), size)


def gelu(x):
    t = jnp.tanh(GELU_C * (x + GELU_K * (x * x * x)))
    return 0.5 * x * (1.0 + t)


def gelu_both(x):
    x2 = x * x
    t = jnp.tanh(GELU_C * (x + GELU_K * (x2 * x)))
    half = 0.5 * (1.0 + t)
    slope = half + 0.5 * x * (1.0 - t * t) * (GELU_C * (1.0 + (3.0 * GELU_K) * x2))
    return x * half, slope


def one_minus_square(log_a, a):
    y = 2.0 * log_a
    s = 1.0 + y * (1.0 / 8.0)
    for k in (7, 6, 5, 4, 3, 2):
        s = 1.0 + (y * (1.0 / k)) * s
    return jnp.where(y > -0.35, -y * s, 1.0 - a * a)


def get(ref, at):
    return jnp.concatenate([ref[j, at, :] for j in range(ref.shape[0])], axis=-1)


def put(ref, at, value):
    for j in range(ref.shape[0]):
        ref[j, at, :] = value[:, j * LANES : (j + 1) * LANES]


def to_all(axis, src, slots, send, recv):
    size, me = lax.axis_size(axis), lax.axis_index(axis)
    return [
        pltpu.make_async_remote_copy(
            src_ref=src,
            dst_ref=slots.at[me],
            send_sem=send.at[d - 1],
            recv_sem=recv.at[d - 1],
            device_id={axis: lax.rem(me + d, size)},
            device_id_type=MESH,
        )
        for d in range(1, size)
    ]


def to_one(axis, distance, src, dst, send, recv):
    size, me = lax.axis_size(axis), lax.axis_index(axis)
    return pltpu.make_async_remote_copy(
        src_ref=src,
        dst_ref=dst,
        send_sem=send,
        recv_sem=recv,
        device_id={axis: lax.rem(me + distance + size, size)},
        device_id_type=MESH,
    )


def spread_gates(blocks_ref, out_ref, start, width):
    heads, size = blocks_ref.shape[:2]
    for h in range(heads):
        block_h = blocks_ref[h].astype(F32)
        parts = [block_h]
        if h > 0:
            parts.insert(0, jnp.zeros((size, h * size), F32))
        if width > (h + 1) * size:
            parts.append(jnp.zeros((size, width - (h + 1) * size), F32))
        row = jnp.concatenate(parts, axis=1).astype(BF16)
        out_ref[h * size : (h + 1) * size, start : start + width] = row
    if width > heads * size:
        rest = jnp.zeros((width - heads * size, width), BF16)
        out_ref[heads * size : width, start : start + width] = rest


def forward_kernel(
    span,
    x_in,
    w_input_in,
    w_branch_in,
    gain_ref,
    taps_ref,
    conv_bias_ref,
    decay_ref,
    bias_r_ref,
    bias_i_ref,
    gate_r_ref,
    gate_i_ref,
    fresh_ref,
    state_ref,
    conv_init_ref,
    normed_out,
    branch_out,
    pad_out,
    pre_out,
    hidden_out,
    mixed_ref,
    carry_ref,
    sums_ref,
    gates_ref,
    vec_ref,
    ends_ref,
    x_ref,
    w_input_ref,
    w_branch_ref,
    normed_ref,
    branch_ref,
    pad_ref,
    pre_ref,
    hidden_ref,
    act_ref,
    a_ref,
    b_ref,
    conv_ref,
    tail_ref,
    tail_in,
    mine_ref,
    load_sem,
    store_sem,
    normed_sem,
    send1,
    recv1,
    send_t,
    recv_t,
):
    seqs = state_ref.shape[0]
    width = taps_ref.shape[1]
    taps = taps_ref.shape[0]
    rows = seqs * span
    devices, me = lax.axis_size("seq"), lax.axis_index("seq")
    local = pltpu.make_async_copy
    pitch = a_ref.shape[1] // seqs
    group = 2 * span
    groups = rows // group

    def x_load(g):
        at = block(g, group)
        return local(x_in.at[at], x_ref.at[at], load_sem.at[g])

    weight_loads = [
        local(w_input_in, w_input_ref, load_sem.at[groups]),
        local(w_branch_in, w_branch_ref, load_sem.at[groups + 1]),
    ]
    x_load(0).start()
    weight_loads[0].start()
    for g in range(1, groups):
        x_load(g).start()
    weight_loads[1].start()

    enter_all(("seq",))
    spread_gates(gate_r_ref, gates_ref, 0, width)
    spread_gates(gate_i_ref, gates_ref, width, width)
    vec_ref[0:1, :] = conv_bias_ref[...].reshape(1, width)
    vec_ref[1:2, :] = jax.nn.softplus(-decay_ref[...].reshape(1, width))
    bias_r = bias_r_ref[...].reshape(1, width)
    bias_i = bias_i_ref[...].reshape(1, width)
    keep = [1.0 - fresh_ref[s].astype(F32) for s in range(seqs)]

    def normed_store(g):
        at = block(g, group)
        return local(normed_ref.at[at], normed_out.at[at], normed_sem.at[g])

    @pl.loop(0, groups)
    def _(g):
        x_load(g).wait()

        @pl.loop(0, group // CHUNK, unroll=4)
        def _(q):
            at = block(g * (group // CHUNK) + q, CHUNK)
            x = x_ref[at, :]
            normed_ref[at, :] = (x * mean_square(x) * gain_ref[...]).astype(BF16)

        normed_store(g).start()

        @pl.when(g == 0)
        def _():
            weight_loads[0].wait()

        conv = dot(normed_ref[block(g, group), :], w_input_ref[...])
        for j in range(group // span):
            pad_ref[g * (group // span) + j, pl.ds(TILE, span), :] = conv[
                j * span : (j + 1) * span
            ]

    for s in range(seqs):
        tail_ref[s] = pad_ref[s, pl.ds(span, TILE), :]
    tail_copy = to_one("seq", 1, tail_ref, tail_in, send_t.at[0], recv_t.at[0])
    tail_copy.start()
    weight_loads[1].wait()

    @pl.loop(0, groups)
    def _(g):
        branch_ref[block(g, group), :] = dot(normed_ref[block(g, group), :], w_branch_ref[...])

    stores = [
        local(source, target, store_sem.at[i])
        for i, (source, target) in enumerate(
            (
                (branch_ref, branch_out),
                (pad_ref, pad_out),
                (pre_ref, pre_out),
                (hidden_ref, hidden_out),
            )
        )
    ]
    stores[0].start()
    tail_copy.wait()
    lead = jnp.zeros((TILE - taps + 1, width), F32)
    for s in range(seqs):
        initial = jnp.concatenate(
            [lead] + [conv_init_ref[k, s : s + 1, :] * keep[s] for k in range(taps - 1)], axis=0
        )
        pad_ref[s, pl.ds(0, TILE), :] = jnp.where(me == 0, initial, tail_in[s])
    stores[1].start()

    @pl.loop(0, seqs)
    def _(s):
        @pl.loop(0, span // ROWS)
        def _(q):
            part = pad_ref[s, pl.ds(pl.multiple_of(q * ROWS, ROWS), ROWS + TILE), :]
            total = vec_ref[0:1, :]
            for k in range(taps):
                first = TILE - (taps - 1) + k
                total = total + taps_ref[k : k + 1, :] * part[first : first + ROWS]
            conv_ref[block(q, ROWS), :] = total

        pre = dot(conv_ref[...].astype(BF16), gates_ref[...])
        pre_ref[block(s, span), :width] = pre[:, :width] + bias_r
        pre_ref[block(s, span), width:] = pre[:, width:] + bias_i

        @pl.loop(0, span // ROWS)
        def _(q):
            at = block(s * (span // ROWS) + q, ROWS)
            conv = conv_ref[block(q, ROWS), :]
            recall = jax.nn.sigmoid(pre_ref[at, :width])
            gate = jax.nn.sigmoid(pre_ref[at, width:])
            log_a = (-RATE_SCALE * vec_ref[1:2, :]) * recall
            a = jnp.exp(log_a)
            spaced = pl.ds(pl.multiple_of(s * pitch + q * ROWS, TILE), ROWS)
            put(a_ref, spaced, a)
            put(b_ref, spaced, jnp.sqrt(one_minus_square(log_a, a)) * gate * conv)

    stores[2].start()

    def at_time(ref, t):
        return get(ref, pl.ds(t, seqs, stride=pitch))

    def step(t, value):
        prod, state = value
        a = at_time(a_ref, t)
        return prod * a, a * state + at_time(b_ref, t)

    ones = jnp.ones((seqs, width), F32)
    prod, state = lax.fori_loop(0, span, step, (ones, jnp.zeros_like(ones)), unroll=8)
    mine_ref[0] = prod
    mine_ref[1] = state
    sums_ref[me] = mine_ref[...]
    copies = to_all("seq", mine_ref, sums_ref, send1, recv1)
    for copy in copies:
        copy.start()

    @pl.loop(0, rows // ROWS, unroll=2)
    def _(q):
        at = block(q, ROWS)
        act_ref[at, :] = gelu(branch_ref[at, :])

    for copy in copies:
        copy.wait()

    def carry_step(j, carry):
        both = sums_ref[j]
        return jnp.where(j < me, both[0] * carry + both[1], carry)

    start = jnp.concatenate([state_ref[s : s + 1, :] * keep[s] for s in range(seqs)], axis=0)
    carry = lax.fori_loop(0, devices - 1, carry_step, start)
    carry_ref[...] = carry

    def final(t, state):
        state = at_time(a_ref, t) * state + at_time(b_ref, t)
        put(hidden_ref, pl.ds(t, seqs, stride=span), state)
        return state

    last = lax.fori_loop(0, span, final, carry, unroll=8)
    stores[3].start()
    ends_ref[0:seqs, :] = jnp.where(me == devices - 1, last, 0.0)
    for s in range(seqs):
        ends_ref[(s + 1) * TILE : (s + 2) * TILE, :] = jnp.where(
            me == devices - 1, pad_ref[s, pl.ds(span, TILE), :], 0.0
        )

    @pl.loop(0, rows // ROWS)
    def _(q):
        at = block(q, ROWS)
        mixed_ref[at, :] = (get(hidden_ref, at) * act_ref[at, :]).astype(BF16)

    for copy in stores:
        copy.wait()
    for g in range(groups):
        normed_store(g).wait()


def backward_kernel(
    span,
    heads,
    block_part_in,
    own_in,
    low_in,
    w_out_in,
    branch_in,
    hidden_in,
    pre_in,
    pad_in,
    normed_in,
    mixed_in,
    carry_ref,
    sums_ref,
    taps_ref,
    vec_ref,
    gates_ref,
    block_out,
    rec_out,
    grad_branch_ref,
    input_ref,
    acc_ref,
    blocks_ref,
    part,
    inbox,
    out,
    send_up,
    send_down,
    recv_up,
    recv_down,
    own_ref,
    resid_low,
    w_out_ref,
    branch_ref,
    hidden_ref,
    pre_ref,
    pad_ref,
    normed_ref,
    mixed_ref,
    a_ref,
    gd_ref,
    grad_ref,
    direct_ref,
    gpad_ref,
    heads_ref,
    low_ref,
    gates_grad,
    stage_ref,
    mine_ref,
    entries_ref,
    head_ref,
    head_in,
    load_sem,
    part_sem,
    store_sem,
    stage_sem,
    send1,
    recv1,
    send_t,
    recv_t,
):
    seqs, width = carry_ref.shape
    taps = taps_ref.shape[0]
    rows = seqs * span
    devices, me = lax.axis_size("seq"), lax.axis_index("seq")
    n, z = lax.axis_size("mp"), lax.axis_index("mp")
    chunks = rows // CHUNK
    size = GROUP * CHUNK
    held = part.shape[0] // size
    groups = chunks // GROUP
    sems = (send_up, send_down, recv_up, recv_down)
    local = pltpu.make_async_copy

    def part_load(g):
        slot = lax.rem(g, held)
        return local(block_part_in.at[block(g, size)], part.at[block(slot, size)], part_sem.at[slot])

    loads = [
        local(source, target, load_sem.at[i])
        for i, (source, target) in enumerate(
            (
                (own_in, own_ref),
                (low_in, resid_low),
                (w_out_in, w_out_ref),
                (pre_in, pre_ref),
                (branch_in, branch_ref),
                (hidden_in, hidden_ref),
                (pad_in, pad_ref),
                (mixed_in, mixed_ref),
                (normed_in, normed_ref),
            )
        )
    ]
    part_load(0).start()
    for copy in loads[:6]:
        copy.start()
    for g in range(1, held):
        part_load(g).start()
    for copy in loads[6:]:
        copy.start()
    acc_ref[...] = jnp.zeros_like(acc_ref)
    enter_all(("seq", "mp"))

    def decay(at):
        recall = jax.nn.sigmoid(pre_ref[at, :width])
        log_a = (-RATE_SCALE * vec_ref[1:2, :]) * recall
        return recall, log_a, jnp.exp(log_a)

    def piece_direct(s):
        @pl.when(s == 0)
        def _():
            for copy in loads[1:6]:
                copy.wait()

        grad_ref[...] = matmul_back(resid_low[block(s, span), :], w_out_ref[...])

        @pl.loop(0, span // ROWS)
        def _(q):
            at = block(s * (span // ROWS) + q, ROWS)
            put(a_ref, at, decay(at)[2])
            act, slope = gelu_both(branch_ref[at, :])
            grad = grad_ref[block(q, ROWS), :]
            put(gd_ref, at, grad * act)
            grad_branch_ref[at, :] = (grad * get(hidden_ref, at) * slope).astype(BF16)

    def at_time(ref, t):
        return get(ref, pl.ds(t, seqs, stride=span))

    zero = jnp.zeros((seqs, width), F32)
    entry_copies = to_all("seq", mine_ref, entries_ref, send1, recv1)

    def piece_entry(_):
        def step(k, through):
            t = span - 1 - k
            return at_time(a_ref, t) * (at_time(gd_ref, t) + through)

        mine_ref[...] = lax.fori_loop(0, span, step, zero, unroll=8)
        entries_ref[me] = mine_ref[...]
        for copy in entry_copies:
            copy.start()

    def piece_state(_):
        for copy in entry_copies:
            copy.wait()

        def back_step(k, through):
            j = devices - 1 - k
            return jnp.where(j > me, entries_ref[j] + sums_ref[j, 0] * through, through)

        incoming = lax.fori_loop(0, devices - 1, back_step, zero)

        def final(k, through):
            t = span - 1 - k
            grad = at_time(gd_ref, t) + through
            put(gd_ref, pl.ds(t, seqs, stride=span), grad)
            return at_time(a_ref, t) * grad

        lax.fori_loop(0, span, final, incoming, unroll=8)

    def add(k, value):
        acc_ref[k] += fold(value)

    parts = 2

    def piece_gates(i):
        s = i // parts
        quarters = span // ROWS // parts

        @pl.when(i == 0)
        def _():
            loads[6].wait()

        @pl.loop(lax.rem(i, parts) * quarters, (lax.rem(i, parts) + 1) * quarters)
        def _(q):
            at = block(s * (span // ROWS) + q, ROWS)
            part_rows = pad_ref[s, pl.ds(pl.multiple_of(q * ROWS, ROWS), ROWS + TILE), :]
            conv = vec_ref[0:1, :]
            for k in range(taps):
                first = TILE - (taps - 1) + k
                conv = conv + taps_ref[k : k + 1, :] * part_rows[first : first + ROWS]
            heads_ref[at, :] = conv.astype(BF16)
            recall, log_a, a = decay(at)
            gate = jax.nn.sigmoid(pre_ref[at, width:])
            square = one_minus_square(log_a, a)
            inverse = lax.rsqrt(square)
            root = jnp.sqrt(square)
            grad = get(gd_ref, at)
            hidden = get(hidden_ref, at)
            before_at = pl.multiple_of(jnp.maximum(s * span + q * ROWS - TILE, 0), TILE)
            earlier = get(hidden_ref, pl.ds(before_at, TILE))
            first_row = jnp.where(q == 0, carry_ref[pl.ds(s, 1), :], earlier[TILE - 1 :])
            place = lax.broadcasted_iota(jnp.int32, (ROWS, width), 0)
            prev = jnp.where(place == 0, first_row, pltpu.roll(hidden, 1, 0))
            grad_log = grad * a * (prev - gate * conv * a * inverse)
            through = grad_log * recall
            pre_r = through * (1.0 - recall) * (-RATE_SCALE * vec_ref[1:2, :])
            direct = grad * root * gate
            pre_i = direct * conv * (1.0 - gate)
            low_ref[at, :width] = pre_r.astype(BF16)
            low_ref[at, width:] = pre_i.astype(BF16)
            direct_ref[block(q, ROWS), :] = direct
            add(0, through)
            add(1, pre_r)
            add(2, pre_i)

        @pl.when(lax.rem(i, parts) == parts - 1)
        def _():
            whole = direct_ref[...] + matmul_back(low_ref[block(s, span), :], gates_ref[...])
            gpad_ref[s, pl.ds(0, span), :] = whole
            head_ref[s] = whole[:TILE]

    head_copy = to_one("seq", -1, head_ref, head_in, send_t.at[0], recv_t.at[0])

    def piece_head(_):
        head_copy.start()

    def piece_taps(i):
        for j in range(2):
            taps_of(2 * i + j)

    def taps_of(s):
        @pl.loop(0, span // ROWS)
        def _(q):
            at = pl.multiple_of(q * ROWS, ROWS)
            part_rows = pad_ref[s, pl.ds(at, ROWS + TILE), :]
            grad = gpad_ref[s, pl.ds(at, ROWS), :]
            add(3, grad)
            for k in range(taps):
                first = TILE - (taps - 1) + k
                add(4 + k, grad * part_rows[first : first + ROWS])

    def piece_tail(_):
        head_copy.wait()
        for s in range(seqs):
            gpad_ref[s, pl.ds(span, TILE), :] = jnp.where(me == devices - 1, 0.0, head_in[s])

    def piece_input(i):
        for j in range(2):
            input_of(2 * i + j)

    def input_of(s):
        @pl.loop(0, span // ROWS)
        def _(q):
            part_rows = gpad_ref[s, pl.ds(pl.multiple_of(q * ROWS, ROWS), ROWS + TILE), :]
            total = taps_ref[taps - 1 : taps, :] * part_rows[0:ROWS]
            for k in range(taps - 1):
                first = taps - 1 - k
                total = total + taps_ref[k : k + 1, :] * part_rows[first : first + ROWS]
            input_ref[block(s * (span // ROWS) + q, ROWS), :] = total.astype(BF16)

    def contract(left, right):
        return lax.dot_general(left, right, CONTRACT_ROWS, preferred_element_type=F32)

    head = blocks_ref.shape[0]

    def piece_gates_grad(i):
        @pl.when(i == 0)
        def _():
            gates_grad[...] = contract(heads_ref[...], low_ref[:, :width])

        @pl.when(i == 1)
        def _():
            gates_grad[...] = contract(heads_ref[...], low_ref[:, width:])

        place = lax.broadcasted_iota(jnp.int32, (head, width), 1)
        line = jnp.zeros((head, width), F32)
        for h in range(heads):
            row = gates_grad[h * head : (h + 1) * head, :]
            inside = jnp.logical_and(place >= h * head, place < (h + 1) * head)
            line = jnp.where(inside, row, line)

        for j in range(2):

            @pl.when(i == j)
            def _():
                blocks_ref[:, j * width : (j + 1) * width] = line

    tall = resid_low.shape[1] // WEIGHT_STEPS

    def stage_store(i):
        at = block(lax.rem(i, WEIGHT_STEPS), tall)
        slot = lax.rem(i, 2)
        return local(stage_ref.at[slot], rec_out.at[i // WEIGHT_STEPS, at], stage_sem.at[slot])

    def piece_weights(i):
        @pl.when(i == 0)
        def _():
            loads[7].wait()
            loads[8].wait()

        @pl.loop(2 * i, 2 * i + 2)
        def _(j):
            weight_of(j)

    def weight_of(i):
        @pl.when(i >= 2)
        def _():
            stage_store(i - 2).wait()

        at = block(lax.rem(i, WEIGHT_STEPS), tall)
        slot = lax.rem(i, 2)
        for which, (left, right) in enumerate(
            ((resid_low, mixed_ref), (normed_ref, grad_branch_ref), (normed_ref, input_ref))
        ):
            @pl.when(i // WEIGHT_STEPS == which)
            def _():
                stage_ref[slot] = contract(left[:, at], right[...])

        stage_store(i).start()

    weights = 3 * WEIGHT_STEPS
    plan = []
    begin = 3
    for work, times, gap in (
        (piece_direct, seqs, 0),
        (piece_entry, 1, 1),
        (piece_state, 1, 0),
        (piece_gates, parts * seqs, 0),
        (piece_head, 1, 0),
        (piece_taps, seqs // 2, 0),
        (piece_tail, 1, 0),
        (piece_input, seqs // 2, 0),
        (piece_gates_grad, 2, 0),
        (piece_weights, weights // 2, 0),
    ):
        plan.append((work, begin, times))
        begin += times + gap

    def run(step):
        for work, first, times in plan:
            @pl.when(jnp.logical_and(step >= first, step < first + times))
            def _():
                work(step - first)

    def before(k):
        @pl.when(k == 0)
        def _():
            loads[0].wait()

        @pl.when(jnp.logical_and(lax.rem(k, GROUP) == 0, k < chunks))
        def _():
            part_load(k // GROUP).wait()

        g = (k - out.shape[0]) // GROUP - 1 + held

        @pl.when(
            jnp.logical_and(
                jnp.logical_and(k >= out.shape[0] + GROUP, lax.rem(k - out.shape[0], GROUP) == 0),
                g < groups,
            )
        )
        def _():
            part_load(g).start()

        run(k)

    def root(c, slot, total):
        out[slot] = own_ref[block(c // 2, CHUNK), :] + total

    def store(c, slot):
        return local(out.at[slot], block_out.at[block(c, CHUNK)], store_sem.at[slot])

    def arrive(c, slot):
        store(c, slot).start()

    def leave(c, slot):
        store(c, slot).wait()

    line_sum(
        "mp", chunks, held * GROUP, part, inbox, out, sems, before, root, arrive, leave
    )

    @pl.loop(chunks + out.shape[0], max(begin, chunks + out.shape[0]))
    def _(k):
        run(k)

    stage_store(weights - 2).wait()
    stage_store(weights - 1).wait()


def backward_call(span, heads, head, *args):
    block_part = args[0]
    low, w_out, branch, hidden, pre, padded, normed, mixed, carry, sums, taps = args[2:13]
    rows, model = block_part.shape
    seqs, width = carry.shape
    devices = lax.axis_size("seq")
    ring = ring_size("mp")
    held = 3 * GROUP * CHUNK
    dma = pltpu.SemaphoreType.DMA
    columns = pltpu.VMEM((width // LANES, rows, LANES), F32)
    return pl.pallas_call(
        functools.partial(backward_kernel, span, heads),
        out_shape=(
            shape((rows, model)),
            shape((3, model, width)),
            shape((rows, width), BF16),
            shape((rows, width), BF16),
            shape((4 + taps.shape[0], TILE, width)),
            shape((head, 2 * width)),
        ),
        in_specs=[HBM] * 10 + [VMEM] * 5,
        out_specs=(HBM,) * 2 + (VMEM,) * 4,
        scratch_shapes=line_scratch("mp", held, model)
        + [
            pltpu.VMEM((rows // 2, model), F32),
            pltpu.VMEM((rows, model), BF16),
            pltpu.VMEM((width, model), BF16),
            pltpu.VMEM((rows, width), F32),
            pltpu.VMEM(hidden.shape, F32),
            pltpu.VMEM(pre.shape, F32),
            pltpu.VMEM(padded.shape, F32),
            pltpu.VMEM((rows, model), BF16),
            pltpu.VMEM((rows, width), BF16),
            columns,
            columns,
            pltpu.VMEM((span, width), F32),
            pltpu.VMEM((span, width), F32),
            pltpu.VMEM((seqs, span + TILE, width), F32),
            pltpu.VMEM((rows, width), BF16),
            pltpu.VMEM((rows, 2 * width), BF16),
            pltpu.VMEM((width, width), F32),
            pltpu.VMEM((2, model // WEIGHT_STEPS, width), F32),
            pltpu.VMEM((seqs, width), F32),
            pltpu.VMEM((devices, seqs, width), F32),
            pltpu.VMEM((seqs, TILE, width), F32),
            pltpu.VMEM((seqs, TILE, width), F32),
            dma((9,)),
            dma((3,)),
            dma((ring,)),
            dma((2,)),
            dma((devices - 1,)),
            dma((devices - 1,)),
            dma((1,)),
            dma((1,)),
        ],
        compiler_params=params(1, 63),
        cost_estimate=cost(200),
        name="backward",
    )(*args)


def line_sum(axis, total, period, part, inbox, out, sems, before, root, arrive, leave):
    send_up, send_down, recv_up, recv_down = sems
    n, z = lax.axis_size(axis), lax.axis_index(axis)
    depth = n // 2
    ring = out.shape[0]

    def root_of(c):
        return depth - 1 + lax.rem(c, 2)

    def up(c, step, side):
        slot = lax.rem(c, ring)
        return pltpu.make_async_remote_copy(
            src_ref=part.at[block(lax.rem(c, period), CHUNK)],
            dst_ref=inbox.at[side, slot],
            send_sem=send_up.at[slot],
            recv_sem=recv_up.at[side, slot],
            device_id={axis: z + step},
            device_id_type=MESH,
        )

    def down(c, step, side):
        slot = lax.rem(c, ring)
        return pltpu.make_async_remote_copy(
            src_ref=out.at[slot],
            dst_ref=out.at[slot],
            send_sem=send_down.at[side, slot],
            recv_sem=recv_down.at[slot],
            device_id={axis: z + step},
            device_id_type=MESH,
        )

    inner = jnp.logical_and(z > 0, z < n - 1)

    @pl.loop(0, total + ring)
    def _(k):
        @pl.when(k >= ring)
        def _():
            c = k - ring
            r = root_of(c)
            step = jnp.where(z < r, 1, -1)
            side = jnp.where(z < r, 0, 1)

            @pl.when(z == r)
            def _():
                down(c, -1, 0).wait_send()
                down(c, 1, 1).wait_send()

            @pl.when(z != r)
            def _():
                up(c, step, side).wait_send()

            @pl.when(jnp.logical_and(z != r, inner))
            def _():
                down(c, -step, side).wait_send()

            leave(c, lax.rem(c, ring))

        before(k)

        for i in reversed(range(n + 1)):
            c = k - SKEW * i
            valid = jnp.logical_and(c >= 0, c < total)
            c = jnp.clip(c, 0, total - 1)
            at = block(lax.rem(c, period), CHUNK)
            slot = lax.rem(c, ring)
            r = root_of(c)
            step = jnp.where(z < r, 1, -1)
            side = jnp.where(z < r, 0, 1)
            if i > depth:
                here = jnp.logical_and(z != r, jnp.abs(z - r) == i - depth)

                @pl.when(jnp.logical_and(valid, here))
                def _():
                    down(c, -step, side).wait_recv()

                    @pl.when(inner)
                    def _():
                        down(c, -step, side).start()

                    arrive(c, slot)
            elif i == depth:

                @pl.when(jnp.logical_and(valid, z == r))
                def _():
                    up(c, 1, 0).wait_recv()
                    up(c, -1, 1).wait_recv()
                    root(c, slot, part[at, :] + inbox[0, slot] + inbox[1, slot])
                    down(c, -1, 0).start()
                    down(c, 1, 1).start()
                    arrive(c, slot)
            else:
                here = jnp.where(z < r, z, n - 1 - z) == i

                @pl.when(jnp.logical_and(valid, jnp.logical_and(z != r, here)))
                def _():
                    if i > 0:
                        up(c, step, side).wait_recv()
                        part[at, :] += inbox[side, slot]
                    up(c, step, side).start()


def ring_size(axis):
    return SKEW * lax.axis_size(axis) + 4


def line_scratch(axis, rows, model):
    dma = pltpu.SemaphoreType.DMA
    ring = ring_size(axis)
    return [
        pltpu.VMEM((rows, model), F32),
        pltpu.VMEM((2, ring, CHUNK, model), F32),
        pltpu.VMEM((ring, CHUNK, model), F32),
        dma((ring,)),
        dma((2, ring)),
        dma((2, ring)),
        dma((ring,)),
    ]


def mean_square(x):
    return lax.rsqrt(jnp.mean(x * x, axis=-1, keepdims=True) + EPS)


def nothing(*_):
    pass


def fold(value):
    total = value[0:TILE]
    for i in range(1, value.shape[0] // TILE):
        total = total + value[i * TILE : (i + 1) * TILE]
    return total


def norm_grad(value, gain, grad, acc_ref):
    q = mean_square(value)
    e = gain * grad
    acc_ref[...] += fold(grad * value * q)
    return q * e - value * (q * q * q) * jnp.mean(e * value, axis=-1, keepdims=True)


def middle_kernel(
    mixed_in,
    w_out_in,
    x_in,
    og_in,
    gain_ref,
    w_gate_in,
    w_up_in,
    w_down_in,
    normed_out,
    hidden_out,
    gate_out,
    up_out,
    glow_out,
    block_out,
    low_out,
    own_grad_out,
    weight_out,
    own_ref,
    acc_ref,
    part,
    inbox,
    out,
    send_up,
    send_down,
    recv_up,
    recv_down,
    mixed,
    w_out,
    w_gate,
    w_up,
    w_down,
    normed,
    rows_ref,
    og_ref,
    glow,
    gate_val,
    up_val,
    grad_hidden,
    hidden,
    grad_gate,
    grad_up,
    block_part,
    low,
    weight_sem,
    row_sem,
    og_sem,
    act_sem,
    low_sem,
    own_sem,
    again_sem,
    stage_sem,
):
    n, z = lax.axis_size("mp"), lax.axis_index("mp")
    count = part.shape[0] // CHUNK
    size = GROUP * CHUNK
    groups = count // GROUP
    ring = out.shape[0]
    sems = (send_up, send_down, recv_up, recv_down)
    local = pltpu.make_async_copy

    loads = [
        local(source, target, weight_sem.at[i])
        for i, (source, target) in enumerate(
            (
                (mixed_in, mixed),
                (w_out_in, w_out),
                (w_gate_in, w_gate),
                (w_up_in, w_up),
                (w_down_in, w_down.at[slice(0, w_down_in.shape[0])]),
            )
        )
    ]
    for copy in loads:
        copy.start()
    deep = w_down_in.shape[0]

    def og_load(g):
        return local(og_in.at[block(g, size)], og_ref, og_sem.at[0])

    og_load(0).start()
    enter_all(("mp",))
    acc_ref[...] = jnp.zeros_like(acc_ref)
    loads[0].wait()
    loads[1].wait()

    def is_root(c):
        return z == n // 2 - 1 + lax.rem(c, 2)

    def row_load(source, c):
        slot = lax.rem(c, ring)
        at = block(lax.rem(c, count), CHUNK)
        return local(source.at[at], rows_ref.at[slot], row_sem.at[slot])

    acts = (
        (normed, normed_out),
        (glow, glow_out),
        (hidden, hidden_out),
        (grad_gate, gate_out),
        (grad_up, up_out),
        (block_part, block_out),
    )

    def act_store(i, g):
        source, target = acts[i]
        source = source.at[lax.rem(g, 2)] if i == 0 else source
        return local(source, target.at[block(g, size)], act_sem.at[i])

    def at_tick(k, first, work):
        g = (k - first) // GROUP

        @pl.when(
            jnp.logical_and(
                jnp.logical_and(k >= first, k < first + GROUP * groups),
                lax.rem(k - first, GROUP) == 0,
            )
        )
        def _():
            work(g)

    def project(g):
        def work(cols):
            part[block(g, size), cols] = dot(mixed[block(g, size), :], w_out[:, cols])

        by_columns(part.shape[1], work)

    def piece_gate(g):
        @pl.when(g == 0)
        def _():
            for copy in loads[2:]:
                copy.wait()

        def work(cols):
            gate_val[:, cols] = dot(normed[lax.rem(g, 2)], w_gate[:, cols])

        by_columns(deep, work)
        act_store(0, g).start()

    def piece_up(g):
        def work(cols):
            up_val[:, cols] = dot(normed[lax.rem(g, 2)], w_up[:, cols])

        by_columns(deep, work)

        @pl.when(g > 0)
        def _():
            for i in range(1, 6):
                act_store(i, g - 1).wait()

    def piece_low(g):
        og_load(g).wait()

        @pl.loop(0, size // ROWS)
        def _(q):
            glow[block(q, ROWS), :] = og_ref[block(q, ROWS), :].astype(BF16)

        @pl.when(g + 1 < groups)
        def _():
            og_load(g + 1).start()

        act_store(1, g).start()
        act_store(0, g).wait()

    def piece_hidden(g):
        def work(cols):
            grad_hidden[:, cols] = matmul_back(glow[...], w_down[cols, :])

        by_columns(deep, work)

    def piece_act(g):
        @pl.loop(0, size // CHUNK)
        def _(q):
            at = block(q, CHUNK)
            up = up_val[at, :]
            grad = grad_hidden[at, :]
            act, slope = gelu_both(gate_val[at, :])
            hidden[at, :] = (act * up).astype(BF16)
            grad_gate[at, :] = (grad * up * slope).astype(BF16)
            grad_up[at, :] = (grad * act).astype(BF16)

        for i in range(2, 5):
            act_store(i, g).start()

    def piece_down(g):
        def work(cols):
            block_part[:, cols] = dot(hidden[...], w_down[:deep, cols])

        by_columns(block_part.shape[1], work)
        act_store(5, g).start()

    def piece_back_gate(g):
        def work(cols):
            part[block(g, size), cols] = matmul_back(grad_gate[...], w_gate[cols, :])

        by_columns(part.shape[1], work)

    def piece_back_up(g):
        def work(cols):
            part[block(g, size), cols] += matmul_back(grad_up[...], w_up[cols, :])

        by_columns(part.shape[1], work)

    tokens = count * CHUNK
    half = tokens // 2
    quarter = half // 2
    again = [
        local(source, target, again_sem.at[i])
        for i, (source, target) in enumerate(
            (
                (normed_out, w_down.at[slice(0, tokens)]),
                (gate_out, w_gate.at[slice(0, tokens)]),
                (up_out, w_up.at[slice(0, tokens)]),
                (hidden_out, w_gate.at[slice(tokens, 2 * tokens)]),
                (glow_out.at[slice(0, half)], w_down.at[slice(tokens, tokens + half)]),
                (glow_out.at[slice(half, half + quarter)], normed.at[0]),
                (glow_out.at[slice(half + quarter, tokens)], normed.at[1]),
            )
        )
    ]
    tall = w_gate.shape[0] // WEIGHT_STEPS
    stages = (gate_val, up_val, grad_hidden)

    def stage_store(which, i):
        return local(stages[which], weight_out.at[which, block(i, tall)], stage_sem.at[which])

    def piece_reload():
        for i in range(1, 6):
            act_store(i, groups - 1).wait()
        for copy in again:
            copy.start()

    def piece_ready():
        for copy in again:
            copy.wait()

    def contract(left, right):
        return lax.dot_general(left, right, CONTRACT_ROWS, preferred_element_type=F32)

    def piece_weight(step):
        i = step // 3
        at = block(i, tall)
        for which in range(3):

            @pl.when(lax.rem(step, 3) == which)
            def _():
                @pl.when(i > 0)
                def _():
                    stage_store(which, i - 1).wait()

                stage = stages[which]

                def work(cols):
                    if which == 0:
                        stage[:, cols] = contract(w_down[:tokens, at], w_gate[:tokens, cols])
                    elif which == 1:
                        stage[:, cols] = contract(w_down[:tokens, at], w_up[:tokens, cols])
                    else:
                        middle = tokens + half + quarter
                        stage[:, cols] = (
                            contract(
                                w_down[tokens : tokens + half, at],
                                w_gate[tokens : tokens + half, cols],
                            )
                            + contract(normed[0, :, at], w_gate[tokens + half : middle, cols])
                            + contract(normed[1, :, at], w_gate[middle : 2 * tokens, cols])
                        )

                by_columns(deep, work)
                stage_store(which, i).start()

    first = GROUP + SKEW * n
    spare = GROUP * groups + ring + 3
    first_weight = spare + 3
    weights = 3 * WEIGHT_STEPS

    def before(k):
        @pl.when(k == spare)
        def _():
            piece_reload()

        @pl.when(k == first_weight - 1)
        def _():
            piece_ready()

        @pl.when(jnp.logical_and(k >= first_weight, k < first_weight + weights))
        def _():
            piece_weight(k - first_weight)

        @pl.when(jnp.logical_and(k < count, is_root(k)))
        def _():
            row_load(x_in, k).start()

        @pl.when(
            jnp.logical_and(jnp.logical_and(k >= count, k < 2 * count), is_root(k))
        )
        def _():
            row_load(og_in, k).start()

        at_tick(k, 0, project)
        at_tick(k, first, piece_gate)
        at_tick(k, first + 1, piece_up)
        at_tick(k, first + 2, piece_low)
        at_tick(k, first + 3, piece_hidden)
        at_tick(k, first + 4, piece_act)
        at_tick(k, first + 6, piece_down)
        at_tick(k, GROUP + ring, piece_back_gate)
        at_tick(k, GROUP + ring + 2, piece_back_up)

    def root(c, slot, total):
        j = lax.rem(c, count)
        mine = block(j // 2, CHUNK)
        row_load(x_in, c).wait()

        @pl.when(c < count)
        def _():
            value = rows_ref[slot] + total
            own_ref[mine, :] = value
            out[slot] = (value * mean_square(value) * gain_ref[...]).astype(BF16).astype(F32)

        @pl.when(c >= count)
        def _():
            back = norm_grad(own_ref[mine, :], gain_ref[...], total, acc_ref)
            out[slot] = rows_ref[slot] + back

    def low_store(c, slot):
        at = block(lax.rem(c, count), CHUNK)
        return local(low.at[slot], low_out.at[at], low_sem.at[slot])

    def own_store(c, slot):
        at = block(lax.rem(c, count) // 2, CHUNK)
        return local(out.at[slot], own_grad_out.at[at], own_sem.at[slot])

    def arrive(c, slot):
        @pl.when(c < count)
        def _():
            normed[lax.rem(c // GROUP, 2), block(lax.rem(c, GROUP), CHUNK), :] = out[slot].astype(BF16)

        @pl.when(c >= count)
        def _():
            low[slot] = out[slot].astype(BF16)
            low_store(c, slot).start()

            @pl.when(is_root(c))
            def _():
                own_store(c, slot).start()

    def leave(c, slot):
        @pl.when(c >= count)
        def _():
            low_store(c, slot).wait()

            @pl.when(is_root(c))
            def _():
                own_store(c, slot).wait()

    line_sum("mp", 2 * count, count, part, inbox, out, sems, before, root, arrive, leave)

    for which in range(3):
        stage_store(which, WEIGHT_STEPS - 1).wait()


def middle_call(*args):
    mixed, w_out, x, og, gain, w_gate, w_up, w_down = args
    rows, model = x.shape
    width, hidden = mixed.shape[1], w_gate.shape[1]
    size = GROUP * CHUNK
    dma = pltpu.SemaphoreType.DMA
    ring = ring_size("mp")
    act = shape((rows, hidden), BF16)
    tall = shape((rows, model), BF16)
    return pl.pallas_call(
        middle_kernel,
        out_shape=(
            tall,
            act,
            act,
            act,
            tall,
            shape((rows, model)),
            tall,
            shape((rows // 2, model)),
            shape((3, model, hidden)),
            shape((rows // 2, model)),
            shape((TILE, model)),
        ),
        in_specs=[HBM] * 4 + [VMEM] + [HBM] * 3,
        out_specs=(HBM,) * 9 + (VMEM,) * 2,
        scratch_shapes=line_scratch("mp", rows, model)
        + [
            pltpu.VMEM((rows, width), BF16),
            pltpu.VMEM((width, model), BF16),
            pltpu.VMEM((model, hidden), BF16),
            pltpu.VMEM((model, hidden), BF16),
            pltpu.VMEM((max(hidden, rows * 3 // 2), model), BF16),
            pltpu.VMEM((2, size, model), BF16),
            pltpu.VMEM((ring, CHUNK, model), F32),
            pltpu.VMEM((size, model), F32),
            pltpu.VMEM((size, model), BF16),
            pltpu.VMEM((size, hidden), F32),
            pltpu.VMEM((size, hidden), F32),
            pltpu.VMEM((size, hidden), F32),
            pltpu.VMEM((size, hidden), BF16),
            pltpu.VMEM((size, hidden), BF16),
            pltpu.VMEM((size, hidden), BF16),
            pltpu.VMEM((size, model), F32),
            pltpu.VMEM((ring, CHUNK, model), BF16),
            dma((5,)),
            dma((ring,)),
            dma((1,)),
            dma((6,)),
            dma((ring,)),
            dma((ring,)),
            dma((7,)),
            dma((3,)),
        ],
        compiler_params=params(2, 63),
        cost_estimate=cost(400),
        name="middle",
    )(*args)


def last_kernel(
    own_grad_in,
    x_in,
    grad_branch_in,
    input_in,
    w_branch_in,
    w_input_in,
    gain_ref,
    other_acc,
    sums_in,
    ends_in,
    blocks_in,
    grad_out,
    norm_ref,
    small_out,
    part,
    inbox,
    out,
    send_up,
    send_down,
    recv_up,
    recv_down,
    own_grad_ref,
    x_ref,
    grad_branch,
    input_low,
    w_branch,
    w_input,
    load_sem,
    store_sem,
    acc_ref,
    mine_ref,
    seq_in,
    mp_in,
    send_s,
    recv_s,
    send_m,
    recv_m,
    small,
    small_in,
    send_v,
    recv_v,
):
    count = part.shape[0] // CHUNK
    size = GROUP * CHUNK
    sems = (send_up, send_down, recv_up, recv_down)
    local = pltpu.make_async_copy

    loads = [
        local(source, target, load_sem.at[i])
        for i, (source, target) in enumerate(
            (
                (grad_branch_in, grad_branch),
                (w_branch_in, w_branch),
                (input_in, input_low),
                (w_input_in, w_input),
                (own_grad_in, own_grad_ref),
                (x_in, x_ref),
            )
        )
    ]
    for copy in loads:
        copy.start()
    acc_ref[...] = jnp.zeros_like(acc_ref)
    mine_ref[...] = jnp.zeros_like(mine_ref)
    enter_all(("seq", "mp"))
    for copy in loads[:4]:
        copy.wait()

    kinds = sums_in.shape[0]
    me = lax.axis_index("seq")
    width = sums_in.shape[2]
    height = kinds + ends_in.shape[0]
    head = blocks_in.shape[0]
    for i in range(kinds):
        small[0, i : i + 1, :] = jnp.sum(sums_in[i], axis=0, keepdims=True)
    small[0, kinds:height, :] = ends_in[...]
    small[0, height : height + head, :] = blocks_in[:, :width]
    small[0, height + head :, :] = blocks_in[:, width:]
    levels = small_in.shape[0]

    def exchange(level):
        bit = 1 << level
        partner = me + bit - 2 * bit * lax.rem(me // bit, 2)
        return pltpu.make_async_remote_copy(
            src_ref=small.at[level],
            dst_ref=small_in.at[level],
            send_sem=send_v.at[level],
            recv_sem=recv_v.at[level],
            device_id={"seq": partner},
            device_id_type=MESH,
        )

    spacing = (count - 4) // (levels + 1)
    seq_copies = to_all("seq", mine_ref.at[0], seq_in, send_s, recv_s)
    mp_copies = to_all("mp", mine_ref.at[1], mp_in, send_m, recv_m)
    settled = count + SKEW * (lax.axis_size("mp") // 2)

    def before(k):
        for level in range(levels + 1):

            @pl.when(k == 3 + level * spacing)
            def _():
                if level > 0:
                    exchange(level - 1).wait()
                    total = small[level - 1] + small_in[level - 1]
                    if level < levels:
                        small[level] = total
                    else:
                        small_out[...] = total
                if level < levels:
                    exchange(level).start()

        @pl.when(k == settled)
        def _():
            mine_ref[0, 0:1, :] = jnp.sum(acc_ref[...], axis=0, keepdims=True)
            mine_ref[0, 1:2, :] = jnp.sum(other_acc[...], axis=0, keepdims=True)
            seq_in[me] = mine_ref[0]
            for copy in seq_copies:
                copy.start()

        @pl.when(k == settled + 2)
        def _():
            for copy in seq_copies:
                copy.wait()
            mine_ref[1] = jnp.sum(seq_in[...], axis=0)
            mp_in[lax.axis_index("mp")] = mine_ref[1]
            for copy in mp_copies:
                copy.start()

        @pl.when(jnp.logical_and(lax.rem(k, 4) == 0, k // 4 < count // GROUP))
        def _():
            at = block(k // 4, size)

            def work(cols):
                part[at, cols] = matmul_back(grad_branch[at, :], w_branch[cols, :]) + matmul_back(
                    input_low[at, :], w_input[cols, :]
                )

            by_columns(part.shape[1], work)

        @pl.when(k == 1)
        def _():
            for copy in loads[4:]:
                copy.wait()

    def root(c, slot, total):
        back = norm_grad(x_ref[block(c, CHUNK), :], gain_ref[...], total, acc_ref)
        out[slot] = own_grad_ref[block(c // 2, CHUNK), :] + back

    def store(c, slot):
        return local(out.at[slot], grad_out.at[block(c, CHUNK)], store_sem.at[slot])

    def arrive(c, slot):
        store(c, slot).start()

    def leave(c, slot):
        store(c, slot).wait()

    line_sum("mp", count, count, part, inbox, out, sems, before, root, arrive, leave)

    for copy in mp_copies:
        copy.wait()
    norm_ref[...] = jnp.sum(mp_in[...], axis=0)


def enter_all(axes):
    barrier = pltpu.get_barrier_semaphore()
    count = 0
    for axis in axes:
        size, me = lax.axis_size(axis), lax.axis_index(axis)
        for d in range(1, size):
            pl.semaphore_signal(
                barrier, 1, device_id={axis: lax.rem(me + d, size)}, device_id_type=MESH
            )
        count += size - 1
    pl.semaphore_wait(barrier, count)


def cost(micros):
    return pl.CostEstimate(flops=int(micros * 1e9), bytes_accessed=1 << 20, transcendentals=0)


def nseq_levels():
    return (lax.axis_size("seq") - 1).bit_length()


def last_call(*args):
    x, grad_branch = args[1:3]
    rows, model = x.shape
    width = grad_branch.shape[1]
    lines = args[8].shape[0] + args[9].shape[0] + 2 * args[10].shape[0]
    levels = nseq_levels()
    dma = pltpu.SemaphoreType.DMA
    nseq, nmp = lax.axis_size("seq"), lax.axis_size("mp")
    return pl.pallas_call(
        last_kernel,
        out_shape=(shape((rows, model)), shape((TILE, model)), shape((lines, width))),
        in_specs=[HBM] * 6 + [VMEM] * 5,
        out_specs=(HBM,) + (VMEM,) * 2,
        scratch_shapes=line_scratch("mp", rows, model)
        + [
            pltpu.VMEM((rows // 2, model), F32),
            pltpu.VMEM((rows, model), F32),
            pltpu.VMEM((rows, width), BF16),
            pltpu.VMEM((rows, width), BF16),
            pltpu.VMEM((model, width), BF16),
            pltpu.VMEM((model, width), BF16),
            dma((6,)),
            dma((ring_size("mp"),)),
            pltpu.VMEM((TILE, model), F32),
            pltpu.VMEM((2, TILE, model), F32),
            pltpu.VMEM((nseq, TILE, model), F32),
            pltpu.VMEM((nmp, TILE, model), F32),
            dma((nseq - 1,)),
            dma((nseq - 1,)),
            dma((nmp - 1,)),
            dma((nmp - 1,)),
            pltpu.VMEM((levels, lines, width), F32),
            pltpu.VMEM((levels, lines, width), F32),
            dma((levels,)),
            dma((levels,)),
        ],
        compiler_params=params(4, 62),
        cost_estimate=cost(200),
        name="last_sums",
    )(*args)


def finish_kernel(
    heads,
    grad_in,
    mlp_in,
    rec_in,
    small_hbm,
    norm_hbm,
    decay_hbm,
    grad_out,
    w_gate_out,
    w_up_out,
    w_branch_out,
    w_input_out,
    w_down_out,
    w_out_out,
    gate_r_out,
    gate_i_out,
    taps_out,
    conv_bias_out,
    bias_r_out,
    bias_i_out,
    decay_out,
    norm_in_out,
    norm_mlp_out,
    state_out,
    conv_out,
    tall,
    mlp,
    rec,
    small_in,
    norm_in,
    raw_ref,
    load_sem,
    store_sem,
    extra_sem,
):
    local = pltpu.make_async_copy
    size = grad_in.shape[0] // COPIES
    extra = [
        local(source, target, extra_sem.at[i])
        for i, (source, target) in enumerate(
            ((small_hbm, small_in), (norm_hbm, norm_in), (decay_hbm, raw_ref))
        )
    ]
    for copy in extra:
        copy.start()
    jobs = [(mlp_in, mlp, None), (rec_in, rec, None)]
    for i in range(COPIES):
        at = slice(i * size, (i + 1) * size)
        jobs.append((grad_in.at[at], tall.at[at], grad_out.at[at]))
    loads = [local(source, held, load_sem.at[i]) for i, (source, held, _) in enumerate(jobs)]
    stores = [
        local(held, target, store_sem.at[i])
        for i, (held, target) in enumerate(
            [(held, target) for _, held, target in jobs[2:]]
            + [
                (mlp.at[0], w_gate_out),
                (mlp.at[1], w_up_out),
                (rec.at[1], w_branch_out),
                (rec.at[2], w_input_out),
            ]
        )
    ]
    for copy in loads:
        copy.start()
    for copy in extra:
        copy.wait()
    taps, seqs, edge = taps_out.shape[0], state_out.shape[0], conv_out.shape[0]
    head = gate_r_out.shape[1]
    width = small_in.shape[1]
    decay = small_in[0:1, :].reshape(width) * (RATE_SCALE * jax.nn.sigmoid(-raw_ref[...]))
    decay_out[...] = decay
    bias_r_out[...] = small_in[1:2, :].reshape(width)
    bias_i_out[...] = small_in[2:3, :].reshape(width)
    conv_bias_out[...] = small_in[3:4, :].reshape(width)
    taps_out[...] = small_in[4 : 4 + taps, :]
    begin = 4 + taps
    state_out[...] = small_in[begin : begin + seqs, :]
    for s in range(seqs):
        end = begin + seqs + (s + 1) * TILE
        for k in range(edge):
            conv_out[k, s : s + 1, :] = small_in[end - edge + k : end - edge + k + 1, :]
    begin += seqs + seqs * TILE
    for i, target in enumerate((gate_r_out, gate_i_out)):
        line = small_in[begin + i * head : begin + (i + 1) * head, :]
        for h in range(heads):
            turned = line if h == 0 else pltpu.roll(line, width - h * head, 1)
            target[h] = turned[:, :head]
    norm_in_out[...] = norm_in[0:1, :].reshape(norm_in.shape[1])
    norm_mlp_out[...] = norm_in[1:2, :].reshape(norm_in.shape[1])
    loads[0].wait()
    loads[1].wait()
    for copy in stores[COPIES:]:
        copy.start()
    w_down_out[...] = mlp[2].T
    w_out_out[...] = rec[0].T
    for i in range(COPIES):
        loads[2 + i].wait()
        stores[i].start()
    for copy in stores:
        copy.wait()


def finish_call(seqs, heads, head, edge, *args):
    stream_grad, mlp_grads, rec_grads, small, norms, decay = args
    rows, model = stream_grad.shape
    own, hidden = mlp_grads.shape[1:]
    width = rec_grads.shape[2]
    taps = edge + 1
    line = shape((width,))
    tall = shape((rows, model))
    return pl.pallas_call(
        functools.partial(finish_kernel, heads),
        out_shape=(
            tall,
            shape((own, hidden)),
            shape((own, hidden)),
            shape((own, width)),
            shape((own, width)),
            shape((hidden, own)),
            shape((width, own)),
            shape((heads, head, head)),
            shape((heads, head, head)),
            shape((taps, width)),
            line,
            line,
            line,
            line,
            shape((model,)),
            shape((model,)),
            shape((seqs, width)),
            shape((edge, seqs, width)),
        ),
        in_specs=[HBM] * 3 + [PINNED] * 3,
        out_specs=(HBM,) * 5 + (VMEM,) * 13,
        scratch_shapes=[
            pltpu.VMEM((rows, model), F32),
            pltpu.VMEM((3, own, hidden), F32),
            pltpu.VMEM((3, own, width), F32),
            pltpu.VMEM(small.shape, F32),
            pltpu.VMEM(norms.shape, F32),
            pltpu.VMEM(decay.shape, F32),
            pltpu.SemaphoreType.DMA((2 + COPIES,)),
            pltpu.SemaphoreType.DMA((4 + COPIES,)),
            pltpu.SemaphoreType.DMA((3,)),
        ],
        compiler_params=pltpu.CompilerParams(vmem_limit_bytes=48 << 20),
        cost_estimate=cost(15),
        name="finish",
    )(*args)


def copy_kernel(source, target, held, load_sem, store_sem):
    size = source.shape[0] // COPIES
    pieces = [slice(i * size, (i + 1) * size) for i in range(COPIES)]
    local = pltpu.make_async_copy
    loads = [local(source.at[p], held.at[p], load_sem.at[i]) for i, p in enumerate(pieces)]
    stores = [local(held.at[p], target.at[p], store_sem.at[i]) for i, p in enumerate(pieces)]
    for copy in loads:
        copy.start()
    for load, store in zip(loads, stores):
        load.wait()
        store.start()
    for copy in stores:
        copy.wait()


def copy_call(array):
    return pl.pallas_call(
        copy_kernel,
        out_shape=shape(array.shape),
        in_specs=[HBM],
        out_specs=HBM,
        scratch_shapes=[
            pltpu.VMEM(array.shape, F32),
            pltpu.SemaphoreType.DMA((COPIES,)),
            pltpu.SemaphoreType.DMA((COPIES,)),
        ],
        compiler_params=pltpu.CompilerParams(vmem_limit_bytes=48 << 20),
        cost_estimate=cost(6),
        name="copy_out",
    )(array)


def params(collective, megabytes=60):
    return pltpu.CompilerParams(
        collective_id=collective, has_side_effects=True, vmem_limit_bytes=megabytes << 20
    )


def shape(dims, dtype=F32):
    return jax.ShapeDtypeStruct(dims, dtype)


def recurrence_forward(span, *args):
    x, w_input = args[:2]
    rows, model = x.shape
    seqs, width = rows // span, w_input.shape[1]
    devices = lax.axis_size("seq")
    dma = pltpu.SemaphoreType.DMA
    groups = seqs // 2
    columns = (width // LANES, rows, LANES)
    spaced = (width // LANES, seqs * (span + TILE), LANES)
    padded = (seqs, span + TILE, width)
    return pl.pallas_call(
        functools.partial(forward_kernel, span),
        out_shape=(
            shape((rows, model), BF16),
            shape((rows, width)),
            shape(padded),
            shape((rows, 2 * width)),
            shape(columns),
            shape((rows, width), BF16),
            shape((seqs, width)),
            shape((devices, 2, seqs, width)),
            shape((width, 2 * width), BF16),
            shape((TILE, width)),
            shape(((seqs + 1) * TILE, width)),
        ),
        in_specs=[HBM] * 3 + [VMEM] * 8 + [pl.BlockSpec(memory_space=pltpu.SMEM)] + [VMEM] * 2,
        out_specs=(HBM,) * 5 + (VMEM,) * 6,
        scratch_shapes=[
            pltpu.VMEM((rows, model), F32),
            pltpu.VMEM((model, width), BF16),
            pltpu.VMEM((model, width), BF16),
            pltpu.VMEM((rows, model), BF16),
            pltpu.VMEM((rows, width), F32),
            pltpu.VMEM(padded, F32),
            pltpu.VMEM((rows, 2 * width), F32),
            pltpu.VMEM(columns, F32),
            pltpu.VMEM((rows, width), F32),
            pltpu.VMEM(spaced, F32),
            pltpu.VMEM(spaced, F32),
            pltpu.VMEM((span, width), F32),
            pltpu.VMEM((seqs, TILE, width), F32),
            pltpu.VMEM((seqs, TILE, width), F32),
            pltpu.VMEM((2, seqs, width), F32),
            dma((groups + 2,)),
            dma((4,)),
            dma((groups,)),
            dma((devices - 1,)),
            dma((devices - 1,)),
            dma((1,)),
            dma((1,)),
        ],
        compiler_params=params(0),
        cost_estimate=cost(50),
        name="recurrence_forward",
    )(*args)


def widen(array, width):
    short = width - array.shape[-1]
    if short == 0:
        return array
    return jnp.pad(array, [(0, 0)] * (array.ndim - 1) + [(0, short)])


def per_device(
    stream,
    norm_in,
    w_branch,
    w_input,
    conv_kernel,
    conv_bias,
    gate_r,
    bias_r,
    gate_i,
    bias_i,
    decay_param,
    w_out,
    norm_mlp,
    w_gate,
    w_up,
    w_down,
    state_init,
    conv_init,
    fresh_rows,
    out_grad,
):
    seqs, span, model = stream.shape
    channels = w_branch.shape[1]
    mlp_dev = w_gate.shape[1]
    heads, head_width = gate_r.shape[:2]
    taps = conv_kernel.shape[0]
    edge = taps - 1
    rows = seqs * span
    devices = lax.axis_size("seq")
    position = lax.axis_index("seq")
    width = -(-channels // 128) * 128

    flat_in = stream.reshape(rows, model)
    flat_grad = out_grad.reshape(rows, model)
    w_branch_p = widen(w_branch, width)
    w_input_p = widen(w_input, width)
    w_out_p = jnp.pad(w_out, ((0, width - channels), (0, 0))) if width > channels else w_out
    taps_p = widen(conv_kernel, width)
    def line(value):
        return widen(value, width)

    (
        normed,
        branch,
        padded,
        pre,
        hidden,
        mixed,
        carry,
        sums,
        gates,
        rates,
        ends,
    ) = recurrence_forward(
        span,
        flat_in,
        w_input_p,
        w_branch_p,
        norm_in[None],
        taps_p,
        line(conv_bias),
        line(decay_param),
        line(bias_r),
        line(bias_i),
        gate_r,
        gate_i,
        fresh_rows,
        widen(state_init, width),
        widen(jnp.swapaxes(conv_init, 0, 1), width),
    )
    _, _, _, _, _, block_part, resid_low, own_grad, mlp_grads, own, norm_mlp_acc = middle_call(
        mixed, w_out_p, flat_in, flat_grad, norm_mlp[None], w_gate, w_up, w_down
    )
    mlp_grads = lax.psum_scatter(mlp_grads, "seq", scatter_dimension=1, tiled=True)
    block_out, rec_grads, grad_branch, input_low, acc, blocks = backward_call(
        span,
        heads,
        head_width,
        block_part,
        own,
        resid_low,
        w_out_p,
        branch,
        hidden,
        pre,
        padded,
        normed,
        mixed,
        carry,
        sums,
        taps_p,
        rates,
        gates,
    )

    block_out = copy_call(block_out)
    rec_grads, grad_branch, mlp_grads, block_out = lax.optimization_barrier(
        (rec_grads, grad_branch, mlp_grads, block_out)
    )
    rec_grads = lax.psum_scatter(rec_grads, "seq", scatter_dimension=1, tiled=True)

    stream_grad, norm_grads, small = last_call(
        own_grad,
        flat_in,
        grad_branch,
        input_low,
        w_branch_p,
        w_input_p,
        norm_in[None],
        norm_mlp_acc,
        acc,
        ends,
        blocks,
    )
    (
        stream_grad,
        w_gate_grad,
        w_up_grad,
        w_branch_grad,
        w_input_grad,
        w_down_grad,
        w_out_grad,
        gate_r_grad,
        gate_i_grad,
        taps_grad,
        conv_bias_grad,
        bias_r_grad,
        bias_i_grad,
        decay_grad,
        norm_in_grad,
        norm_mlp_grad,
        final_state,
        final_conv,
    ) = finish_call(
        seqs,
        heads,
        head_width,
        edge,
        stream_grad,
        mlp_grads,
        rec_grads,
        small,
        norm_grads,
        line(decay_param),
    )
    return (
        block_out.reshape(stream.shape),
        stream_grad.reshape(stream.shape),
        norm_in_grad,
        w_branch_grad[:, :channels],
        w_input_grad[:, :channels],
        taps_grad[:, :channels],
        conv_bias_grad[:channels],
        gate_r_grad,
        bias_r_grad[:channels],
        gate_i_grad,
        bias_i_grad[:channels],
        decay_grad[:channels],
        w_out_grad[:channels],
        norm_mlp_grad,
        w_gate_grad,
        w_up_grad,
        w_down_grad,
        final_state[:, :channels],
        jnp.swapaxes(final_conv, 0, 1)[:, :, :channels],
    )


def solution(mesh):
    seq_rows = P(None, "seq", None)
    columns = P(None, "mp")
    channel = P("mp")
    return jax.shard_map(
        per_device,
        mesh=mesh,
        in_specs=(
            seq_rows,
            P(),
            columns,
            columns,
            columns,
            channel,
            P("mp", None, None),
            channel,
            P("mp", None, None),
            channel,
            channel,
            P("mp", None),
            P(),
            columns,
            columns,
            P("mp", None),
            columns,
            P(None, None, "mp"),
            P(),
            seq_rows,
        ),
        out_specs=(
            seq_rows,
            seq_rows,
            P(),
            P("seq", "mp"),
            P("seq", "mp"),
            columns,
            channel,
            P("mp", None, None),
            channel,
            P("mp", None, None),
            channel,
            channel,
            P("mp", "seq"),
            P(),
            P("seq", "mp"),
            P("seq", "mp"),
            P("mp", "seq"),
            columns,
            P(None, None, "mp"),
        ),
        check_vma=False,
    )
```

```python
import functools

import jax
import jax.numpy as jnp
from jax import lax
from jax.experimental import pallas as pl
from jax.experimental.pallas import tpu as pltpu
from jax.sharding import PartitionSpec as P

MESH = pl.DeviceIdType.MESH
RATE_SCALE = 8.0
EPS = 1e-06
GELU_C = 0.7978845608028654
GELU_K = 0.044715
CONTRACT_ROWS = (((0,), (0,)), ((), ()))
CONTRACT_LAST = (((1,), (1,)), ((), ()))
TILE = 8
LANES = 128
ROWS = 32
CHUNK = 16
SKEW = 2
GROUP = 16
WEIGHT_STEPS = 8
COPIES = 8
F32 = jnp.float32
BF16 = jnp.bfloat16
VMEM = pl.BlockSpec(memory_space=pltpu.VMEM)
HBM = pl.BlockSpec(memory_space=pl.ANY)
PINNED = pl.BlockSpec(memory_space=pltpu.HBM)


def dot(a, b):
    return jnp.dot(a, b, preferred_element_type=F32)


def matmul_back(a, b):
    return lax.dot_general(a, b, CONTRACT_LAST, preferred_element_type=F32)


def block(i, size):
    return pl.ds(pl.multiple_of(i * size, size), size)


def gelu(x):
    t = jnp.tanh(GELU_C * (x + GELU_K * (x * x * x)))
    return 0.5 * x * (1.0 + t)


def gelu_both(x):
    x2 = x * x
    t = jnp.tanh(GELU_C * (x + GELU_K * (x2 * x)))
    half = 0.5 * (1.0 + t)
    slope = half + 0.5 * x * (1.0 - t * t) * (GELU_C * (1.0 + (3.0 * GELU_K) * x2))
    return x * half, slope


def one_minus_square(log_a, a):
    y = 2.0 * log_a
    s = 1.0 + y * (1.0 / 8.0)
    for k in (7, 6, 5, 4, 3, 2):
        s = 1.0 + (y * (1.0 / k)) * s
    return jnp.where(y > -0.35, -y * s, 1.0 - a * a)


def get(ref, at):
    return jnp.concatenate([ref[j, at, :] for j in range(ref.shape[0])], axis=-1)


def put(ref, at, value):
    for j in range(ref.shape[0]):
        ref[j, at, :] = value[:, j * LANES : (j + 1) * LANES]


def to_all(axis, src, slots, send, recv):
    size, me = lax.axis_size(axis), lax.axis_index(axis)
    return [
        pltpu.make_async_remote_copy(
            src_ref=src,
            dst_ref=slots.at[me],
            send_sem=send.at[d - 1],
            recv_sem=recv.at[d - 1],
            device_id={axis: lax.rem(me + d, size)},
            device_id_type=MESH,
        )
        for d in range(1, size)
    ]


def to_one(axis, distance, src, dst, send, recv):
    size, me = lax.axis_size(axis), lax.axis_index(axis)
    return pltpu.make_async_remote_copy(
        src_ref=src,
        dst_ref=dst,
        send_sem=send,
        recv_sem=recv,
        device_id={axis: lax.rem(me + distance + size, size)},
        device_id_type=MESH,
    )


def spread_gates(blocks_ref, out_ref, start, width):
    heads, size = blocks_ref.shape[:2]
    for h in range(heads):
        block_h = blocks_ref[h].astype(F32)
        parts = [block_h]
        if h > 0:
            parts.insert(0, jnp.zeros((size, h * size), F32))
        if width > (h + 1) * size:
            parts.append(jnp.zeros((size, width - (h + 1) * size), F32))
        row = jnp.concatenate(parts, axis=1).astype(BF16)
        out_ref[h * size : (h + 1) * size, start : start + width] = row
    if width > heads * size:
        rest = jnp.zeros((width - heads * size, width), BF16)
        out_ref[heads * size : width, start : start + width] = rest


def forward_kernel(
    span,
    x_in,
    w_input_in,
    w_branch_in,
    gain_ref,
    taps_ref,
    conv_bias_ref,
    decay_ref,
    bias_r_ref,
    bias_i_ref,
    gate_r_ref,
    gate_i_ref,
    fresh_ref,
    state_ref,
    conv_init_ref,
    normed_out,
    branch_out,
    pad_out,
    pre_out,
    hidden_out,
    mixed_ref,
    carry_ref,
    sums_ref,
    gates_ref,
    vec_ref,
    ends_ref,
    x_ref,
    w_input_ref,
    w_branch_ref,
    normed_ref,
    branch_ref,
    pad_ref,
    pre_ref,
    hidden_ref,
    act_ref,
    a_ref,
    b_ref,
    conv_ref,
    tail_ref,
    tail_in,
    mine_ref,
    load_sem,
    store_sem,
    normed_sem,
    send1,
    recv1,
    send_t,
    recv_t,
):
    seqs = state_ref.shape[0]
    width = taps_ref.shape[1]
    taps = taps_ref.shape[0]
    rows = seqs * span
    devices, me = lax.axis_size("seq"), lax.axis_index("seq")
    local = pltpu.make_async_copy
    pitch = a_ref.shape[1] // seqs
    group = 2 * span
    groups = rows // group

    def x_load(g):
        at = block(g, group)
        return local(x_in.at[at], x_ref.at[at], load_sem.at[g])

    weight_loads = [
        local(w_input_in, w_input_ref, load_sem.at[groups]),
        local(w_branch_in, w_branch_ref, load_sem.at[groups + 1]),
    ]
    x_load(0).start()
    weight_loads[0].start()
    for g in range(1, groups):
        x_load(g).start()
    weight_loads[1].start()

    enter_all(("seq",))
    spread_gates(gate_r_ref, gates_ref, 0, width)
    spread_gates(gate_i_ref, gates_ref, width, width)
    vec_ref[0:1, :] = conv_bias_ref[...].reshape(1, width)
    vec_ref[1:2, :] = jax.nn.softplus(-decay_ref[...].reshape(1, width))
    bias_r = bias_r_ref[...].reshape(1, width)
    bias_i = bias_i_ref[...].reshape(1, width)
    keep = [1.0 - fresh_ref[s].astype(F32) for s in range(seqs)]

    def normed_store(g):
        at = block(g, group)
        return local(normed_ref.at[at], normed_out.at[at], normed_sem.at[g])

    def norm(g):
        x_load(g).wait()
        for q in range(group // CHUNK):
            at = slice(g * group + q * CHUNK, g * group + (q + 1) * CHUNK)
            x = x_ref[at, :]
            normed_ref[at, :] = (x * mean_square(x) * gain_ref[...]).astype(BF16)

    norm(0)
    weight_loads[0].wait()
    for g in range(groups):
        if g + 1 < groups:
            norm(g + 1)
        conv = dot(normed_ref[slice(g * group, (g + 1) * group), :], w_input_ref[...])
        for j in range(group // span):
            pad_ref[g * (group // span) + j, pl.ds(TILE, span), :] = conv[
                j * span : (j + 1) * span
            ]
    for g in range(groups):
        normed_store(g).start()

    for s in range(seqs):
        tail_ref[s] = pad_ref[s, pl.ds(span, TILE), :]
    tail_copy = to_one("seq", 1, tail_ref, tail_in, send_t.at[0], recv_t.at[0])
    tail_copy.start()
    weight_loads[1].wait()

    def branch(g):
        branch_ref[block(g, group), :] = dot(normed_ref[block(g, group), :], w_branch_ref[...])

    @pl.loop(0, groups // 2)
    def _(g):
        branch(g)

    stores = [
        local(source, target, store_sem.at[i])
        for i, (source, target) in enumerate(
            (
                (branch_ref, branch_out),
                (pad_ref, pad_out),
                (pre_ref, pre_out),
                (hidden_ref, hidden_out),
            )
        )
    ]
    tail_copy.wait()
    lead = jnp.zeros((TILE - taps + 1, width), F32)
    for s in range(seqs):
        initial = jnp.concatenate(
            [lead] + [conv_init_ref[k, s : s + 1, :] * keep[s] for k in range(taps - 1)], axis=0
        )
        pad_ref[s, pl.ds(0, TILE), :] = jnp.where(me == 0, initial, tail_in[s])
    stores[1].start()

    def gates(s, slot):
        for q in range(span // ROWS):
            part = pad_ref[s, pl.ds(q * ROWS, ROWS + TILE), :]
            total = vec_ref[0:1, :]
            for k in range(taps):
                first = TILE - (taps - 1) + k
                total = total + taps_ref[k : k + 1, :] * part[first : first + ROWS]
            conv_ref[slot, pl.ds(q * ROWS, ROWS), :] = total

        pre = dot(conv_ref[slot].astype(BF16), gates_ref[...])
        pre_ref[block(s, span), :width] = pre[:, :width] + bias_r
        pre_ref[block(s, span), width:] = pre[:, width:] + bias_i
        for q in range(span // ROWS):
            rows_q = slice(q * ROWS, (q + 1) * ROWS)
            conv = conv_ref[slot, pl.ds(q * ROWS, ROWS), :]
            recall = jax.nn.sigmoid(pre[rows_q, :width] + bias_r)
            gate = jax.nn.sigmoid(pre[rows_q, width:] + bias_i)
            log_a = (-RATE_SCALE * vec_ref[1:2, :]) * recall
            a = jnp.exp(log_a)
            spaced = pl.ds(pl.multiple_of(s * pitch + q * ROWS, TILE), ROWS)
            put(a_ref, spaced, a)
            put(b_ref, spaced, jnp.sqrt(one_minus_square(log_a, a)) * gate * conv)

    per = seqs // (groups - groups // 2)

    @pl.loop(0, groups - groups // 2)
    def _(i):
        branch(groups // 2 + i)
        for j in range(per):
            gates(i * per + j, j % 2)

    stores[0].start()
    stores[2].start()

    def at_time(ref, t):
        return get(ref, pl.ds(t, seqs, stride=pitch))

    def step(t, value):
        prod, state = value
        a = at_time(a_ref, t)
        return prod * a, a * state + at_time(b_ref, t)

    ones = jnp.ones((seqs, width), F32)
    prod, state = lax.fori_loop(0, span, step, (ones, jnp.zeros_like(ones)), unroll=8)
    mine_ref[0] = prod
    mine_ref[1] = state
    sums_ref[me] = mine_ref[...]
    copies = to_all("seq", mine_ref, sums_ref, send1, recv1)
    for copy in copies:
        copy.start()

    @pl.loop(0, rows // ROWS, unroll=2)
    def _(q):
        at = block(q, ROWS)
        act_ref[at, :] = gelu(branch_ref[at, :])

    for copy in copies:
        copy.wait()

    def carry_step(j, carry):
        both = sums_ref[j]
        return jnp.where(j < me, both[0] * carry + both[1], carry)

    start = jnp.concatenate([state_ref[s : s + 1, :] * keep[s] for s in range(seqs)], axis=0)
    carry = lax.fori_loop(0, devices - 1, carry_step, start)
    carry_ref[...] = carry

    def final(t, state):
        state = at_time(a_ref, t) * state + at_time(b_ref, t)
        put(hidden_ref, pl.ds(t, seqs, stride=span), state)
        return state

    last = lax.fori_loop(0, span, final, carry, unroll=8)
    stores[3].start()
    ends_ref[0:seqs, :] = jnp.where(me == devices - 1, last, 0.0)
    for s in range(seqs):
        ends_ref[(s + 1) * TILE : (s + 2) * TILE, :] = jnp.where(
            me == devices - 1, pad_ref[s, pl.ds(span, TILE), :], 0.0
        )

    @pl.loop(0, rows // ROWS, unroll=2)
    def _(q):
        at = block(q, ROWS)
        mixed_ref[at, :] = (get(hidden_ref, at) * act_ref[at, :]).astype(BF16)

    for copy in stores:
        copy.wait()
    for g in range(groups):
        normed_store(g).wait()


def backward_kernel(
    span,
    heads,
    block_part_in,
    own_in,
    low_in,
    w_out_in,
    branch_in,
    hidden_in,
    pre_in,
    pad_in,
    normed_in,
    mixed_in,
    carry_ref,
    sums_ref,
    taps_ref,
    vec_ref,
    gates_ref,
    block_out,
    rec_out,
    grad_branch_ref,
    input_ref,
    acc_ref,
    blocks_ref,
    part,
    inbox,
    out,
    send_up,
    send_down,
    recv_up,
    recv_down,
    own_ref,
    resid_low,
    w_out_ref,
    branch_ref,
    hidden_ref,
    pre_ref,
    pad_ref,
    normed_ref,
    mixed_ref,
    a_ref,
    gd_ref,
    grad_ref,
    direct_ref,
    gpad_ref,
    heads_ref,
    low_ref,
    gates_grad,
    stage_ref,
    mine_ref,
    entries_ref,
    head_ref,
    head_in,
    load_sem,
    part_sem,
    store_sem,
    stage_sem,
    send1,
    recv1,
    send_t,
    recv_t,
):
    seqs, width = carry_ref.shape
    taps = taps_ref.shape[0]
    rows = seqs * span
    devices, me = lax.axis_size("seq"), lax.axis_index("seq")
    n, z = lax.axis_size("mp"), lax.axis_index("mp")
    chunks = rows // CHUNK
    size = GROUP * CHUNK
    held = part.shape[0] // size
    groups = chunks // GROUP
    sems = (send_up, send_down, recv_up, recv_down)
    local = pltpu.make_async_copy

    def part_load(g):
        slot = lax.rem(g, held)
        return local(block_part_in.at[block(g, size)], part.at[block(slot, size)], part_sem.at[slot])

    loads = [
        local(source, target, load_sem.at[i])
        for i, (source, target) in enumerate(
            (
                (own_in, own_ref),
                (low_in, resid_low),
                (w_out_in, w_out_ref),
                (pre_in, pre_ref),
                (branch_in, branch_ref),
                (hidden_in, hidden_ref),
                (pad_in, pad_ref),
                (mixed_in, mixed_ref),
                (normed_in, normed_ref),
            )
        )
    ]
    part_load(0).start()
    for copy in loads[:6]:
        copy.start(priority=1)
    for g in range(1, held):
        part_load(g).start()
    for copy in loads[6:]:
        copy.start(priority=1)
    acc_ref[...] = jnp.zeros_like(acc_ref)
    enter_all(("seq", "mp"))

    pitch = a_ref.shape[1] // seqs

    def spaced(s, q):
        return pl.ds(pl.multiple_of(s * pitch + q * ROWS, TILE), ROWS)

    def decay(at):
        recall = jax.nn.sigmoid(pre_ref[at, :width])
        log_a = (-RATE_SCALE * vec_ref[1:2, :]) * recall
        return recall, log_a, jnp.exp(log_a)

    def piece_direct(s):
        @pl.when(s == 0)
        def _():
            for copy in loads[1:6]:
                copy.wait()

        grad_ref[...] = matmul_back(resid_low[block(s, span), :], w_out_ref[...])

        @pl.loop(0, span // ROWS)
        def _(q):
            at = block(s * (span // ROWS) + q, ROWS)
            put(a_ref, spaced(s, q), decay(at)[2])
            act, slope = gelu_both(branch_ref[at, :])
            grad = grad_ref[block(q, ROWS), :]
            put(gd_ref, spaced(s, q), grad * act)
            grad_branch_ref[at, :] = (grad * get(hidden_ref, at) * slope).astype(BF16)

    def at_time(ref, t):
        return get(ref, pl.ds(t, seqs, stride=pitch))

    zero = jnp.zeros((seqs, width), F32)
    entry_copies = to_all("seq", mine_ref, entries_ref, send1, recv1)

    def piece_entry(_):
        def step(k, through):
            t = span - 1 - k
            return at_time(a_ref, t) * (at_time(gd_ref, t) + through)

        mine_ref[...] = lax.fori_loop(0, span, step, zero, unroll=8)
        entries_ref[me] = mine_ref[...]
        for copy in entry_copies:
            copy.start()

    def piece_state(_):
        for copy in entry_copies:
            copy.wait()

        def back_step(k, through):
            j = devices - 1 - k
            return jnp.where(j > me, entries_ref[j] + sums_ref[j, 0] * through, through)

        incoming = lax.fori_loop(0, devices - 1, back_step, zero)

        def final(k, through):
            t = span - 1 - k
            grad = at_time(gd_ref, t) + through
            put(gd_ref, pl.ds(t, seqs, stride=pitch), grad)
            return at_time(a_ref, t) * grad

        lax.fori_loop(0, span, final, incoming, unroll=8)

    def add(k, value):
        acc_ref[k] += fold(value)

    parts = 2

    def piece_gates(i):
        s = i // parts
        quarters = span // ROWS // parts

        @pl.when(i == 0)
        def _():
            loads[6].wait()

        @pl.loop(lax.rem(i, parts) * quarters, (lax.rem(i, parts) + 1) * quarters)
        def _(q):
            at = block(s * (span // ROWS) + q, ROWS)
            part_rows = pad_ref[s, pl.ds(pl.multiple_of(q * ROWS, ROWS), ROWS + TILE), :]
            conv = vec_ref[0:1, :]
            for k in range(taps):
                first = TILE - (taps - 1) + k
                conv = conv + taps_ref[k : k + 1, :] * part_rows[first : first + ROWS]
            heads_ref[at, :] = conv.astype(BF16)
            recall, log_a, a = decay(at)
            gate = jax.nn.sigmoid(pre_ref[at, width:])
            square = one_minus_square(log_a, a)
            inverse = lax.rsqrt(square)
            root = jnp.sqrt(square)
            grad = get(gd_ref, spaced(s, q))
            hidden = get(hidden_ref, at)
            before_at = pl.multiple_of(jnp.maximum(s * span + q * ROWS - TILE, 0), TILE)
            earlier = get(hidden_ref, pl.ds(before_at, TILE))
            first_row = jnp.where(q == 0, carry_ref[pl.ds(s, 1), :], earlier[TILE - 1 :])
            place = lax.broadcasted_iota(jnp.int32, (ROWS, width), 0)
            prev = jnp.where(place == 0, first_row, pltpu.roll(hidden, 1, 0))
            grad_log = grad * a * (prev - gate * conv * a * inverse)
            through = grad_log * recall
            pre_r = through * (1.0 - recall) * (-RATE_SCALE * vec_ref[1:2, :])
            direct = grad * root * gate
            pre_i = direct * conv * (1.0 - gate)
            low_ref[at, :width] = pre_r.astype(BF16)
            low_ref[at, width:] = pre_i.astype(BF16)
            direct_ref[block(q, ROWS), :] = direct
            add(0, through)
            add(1, pre_r)
            add(2, pre_i)

        @pl.when(lax.rem(i, parts) == parts - 1)
        def _():
            whole = direct_ref[...] + matmul_back(low_ref[block(s, span), :], gates_ref[...])
            gpad_ref[s, pl.ds(0, span), :] = whole
            head_ref[s] = whole[:TILE]

    head_copy = to_one("seq", -1, head_ref, head_in, send_t.at[0], recv_t.at[0])

    def piece_head(_):
        head_copy.start()

    def piece_taps(i):
        for j in range(2):
            taps_of(2 * i + j)

    def taps_of(s):
        @pl.loop(0, span // ROWS)
        def _(q):
            at = pl.multiple_of(q * ROWS, ROWS)
            part_rows = pad_ref[s, pl.ds(at, ROWS + TILE), :]
            grad = gpad_ref[s, pl.ds(at, ROWS), :]
            add(3, grad)
            for k in range(taps):
                first = TILE - (taps - 1) + k
                add(4 + k, grad * part_rows[first : first + ROWS])

    def piece_tail(_):
        head_copy.wait()
        for s in range(seqs):
            gpad_ref[s, pl.ds(span, TILE), :] = jnp.where(me == devices - 1, 0.0, head_in[s])

    def piece_input(i):
        for j in range(2):
            input_of(2 * i + j)

    def input_of(s):
        @pl.loop(0, span // ROWS)
        def _(q):
            part_rows = gpad_ref[s, pl.ds(pl.multiple_of(q * ROWS, ROWS), ROWS + TILE), :]
            total = taps_ref[taps - 1 : taps, :] * part_rows[0:ROWS]
            for k in range(taps - 1):
                first = taps - 1 - k
                total = total + taps_ref[k : k + 1, :] * part_rows[first : first + ROWS]
            input_ref[block(s * (span // ROWS) + q, ROWS), :] = total.astype(BF16)

    def contract(left, right):
        return lax.dot_general(left, right, CONTRACT_ROWS, preferred_element_type=F32)

    head = blocks_ref.shape[0]

    def piece_gates_grad(i):
        @pl.when(i == 0)
        def _():
            gates_grad[...] = contract(heads_ref[...], low_ref[:, :width])

        @pl.when(i == 1)
        def _():
            gates_grad[...] = contract(heads_ref[...], low_ref[:, width:])

        place = lax.broadcasted_iota(jnp.int32, (head, width), 1)
        line = jnp.zeros((head, width), F32)
        for h in range(heads):
            row = gates_grad[h * head : (h + 1) * head, :]
            inside = jnp.logical_and(place >= h * head, place < (h + 1) * head)
            line = jnp.where(inside, row, line)

        for j in range(2):

            @pl.when(i == j)
            def _():
                blocks_ref[:, j * width : (j + 1) * width] = line

    tall = resid_low.shape[1] // WEIGHT_STEPS

    def stage_store(i):
        at = block(lax.rem(i, WEIGHT_STEPS), tall)
        slot = lax.rem(i, 2)
        return local(stage_ref.at[slot], rec_out.at[i // WEIGHT_STEPS, at], stage_sem.at[slot])

    def piece_weights(i):
        @pl.when(i == 0)
        def _():
            loads[7].wait()
            loads[8].wait()

        @pl.loop(2 * i, 2 * i + 2)
        def _(j):
            weight_of(j)

    def weight_of(i):
        @pl.when(i >= 2)
        def _():
            stage_store(i - 2).wait()

        at = block(lax.rem(i, WEIGHT_STEPS), tall)
        slot = lax.rem(i, 2)
        for which, (left, right) in enumerate(
            ((resid_low, mixed_ref), (normed_ref, grad_branch_ref), (normed_ref, input_ref))
        ):
            @pl.when(i // WEIGHT_STEPS == which)
            def _():
                stage_ref[slot] = contract(left[:, at], right[...])

        stage_store(i).start(priority=1)

    weights = 3 * WEIGHT_STEPS
    plan = []
    begin = 3
    for work, times, gap in (
        (piece_direct, seqs, 0),
        (piece_entry, 1, 1),
        (piece_state, 1, 0),
        (piece_gates, parts * seqs, 0),
        (piece_head, 1, 0),
        (piece_taps, seqs // 2, 0),
        (piece_tail, 1, 0),
        (piece_input, seqs // 2, 0),
        (piece_gates_grad, 2, 0),
        (piece_weights, weights // 2, 0),
    ):
        plan.append((work, begin, times))
        begin += times + gap

    def run(step):
        for work, first, times in plan:
            @pl.when(jnp.logical_and(step >= first, step < first + times))
            def _():
                work(step - first)

    def before(k):
        @pl.when(k == SKEW * (n // 2))
        def _():
            loads[0].wait()

        @pl.when(jnp.logical_and(lax.rem(k, GROUP) == 0, k < chunks))
        def _():
            part_load(k // GROUP).wait()

        g = (k - out.shape[0]) // GROUP - 1 + held

        @pl.when(
            jnp.logical_and(
                jnp.logical_and(k >= out.shape[0] + GROUP, lax.rem(k - out.shape[0], GROUP) == 0),
                g < groups,
            )
        )
        def _():
            part_load(g).start()

        run(k)

    def root(c, slot, total):
        out[slot] = own_ref[block(c // 2, CHUNK), :] + total

    def store(c, slot):
        return local(out.at[slot], block_out.at[block(c, CHUNK)], store_sem.at[slot])

    def arrive(c, slot):
        store(c, slot).start()

    def leave(c, slot):
        store(c, slot).wait()

    line_sum(
        "mp", chunks, held * GROUP, part, inbox, out, sems, before, root, arrive, leave
    )

    @pl.loop(chunks + out.shape[0], max(begin, chunks + out.shape[0]))
    def _(k):
        run(k)

    stage_store(weights - 2).wait()
    stage_store(weights - 1).wait()


def backward_call(span, heads, head, *args):
    block_part = args[0]
    low, w_out, branch, hidden, pre, padded, normed, mixed, carry, sums, taps = args[2:13]
    rows, model = block_part.shape
    seqs, width = carry.shape
    devices = lax.axis_size("seq")
    ring = ring_size("mp")
    held = 3 * GROUP * CHUNK
    dma = pltpu.SemaphoreType.DMA
    columns = pltpu.VMEM((width // LANES, seqs * (span + TILE), LANES), F32)
    return pl.pallas_call(
        functools.partial(backward_kernel, span, heads),
        out_shape=(
            shape((rows, model)),
            shape((3, model, width)),
            shape((rows, width), BF16),
            shape((rows, width), BF16),
            shape((4 + taps.shape[0], TILE, width)),
            shape((head, 2 * width)),
        ),
        in_specs=[HBM] * 10 + [VMEM] * 5,
        out_specs=(HBM,) * 2 + (VMEM,) * 4,
        scratch_shapes=line_scratch("mp", held, model)
        + [
            pltpu.VMEM((rows // 2, model), F32),
            pltpu.VMEM((rows, model), BF16),
            pltpu.VMEM((width, model), BF16),
            pltpu.VMEM((rows, width), F32),
            pltpu.VMEM(hidden.shape, F32),
            pltpu.VMEM(pre.shape, F32),
            pltpu.VMEM(padded.shape, F32),
            pltpu.VMEM((rows, model), BF16),
            pltpu.VMEM((rows, width), BF16),
            columns,
            columns,
            pltpu.VMEM((span, width), F32),
            pltpu.VMEM((span, width), F32),
            pltpu.VMEM((seqs, span + TILE, width), F32),
            pltpu.VMEM((rows, width), BF16),
            pltpu.VMEM((rows, 2 * width), BF16),
            pltpu.VMEM((width, width), F32),
            pltpu.VMEM((2, model // WEIGHT_STEPS, width), F32),
            pltpu.VMEM((seqs, width), F32),
            pltpu.VMEM((devices, seqs, width), F32),
            pltpu.VMEM((seqs, TILE, width), F32),
            pltpu.VMEM((seqs, TILE, width), F32),
            dma((9,)),
            dma((3,)),
            dma((ring,)),
            dma((2,)),
            dma((devices - 1,)),
            dma((devices - 1,)),
            dma((1,)),
            dma((1,)),
        ],
        compiler_params=params(1, 63),
        cost_estimate=cost(200),
        name="backward",
    )(*args)


def line_sum(axis, total, period, part, inbox, out, sems, before, root, arrive, leave):
    send_up, send_down, recv_up, recv_down = sems
    n, z = lax.axis_size(axis), lax.axis_index(axis)
    depth = n // 2
    ring = out.shape[0]

    def root_of(c):
        return depth - 1 + lax.rem(c, 2)

    def up(c, step, side):
        slot = lax.rem(c, ring)
        return pltpu.make_async_remote_copy(
            src_ref=part.at[block(lax.rem(c, period), CHUNK)],
            dst_ref=inbox.at[side, slot],
            send_sem=send_up.at[slot],
            recv_sem=recv_up.at[side, slot],
            device_id={axis: z + step},
            device_id_type=MESH,
        )

    def down(c, step, side):
        slot = lax.rem(c, ring)
        return pltpu.make_async_remote_copy(
            src_ref=out.at[slot],
            dst_ref=out.at[slot],
            send_sem=send_down.at[side, slot],
            recv_sem=recv_down.at[slot],
            device_id={axis: z + step},
            device_id_type=MESH,
        )

    inner = jnp.logical_and(z > 0, z < n - 1)

    @pl.loop(0, total + ring)
    def _(k):
        @pl.when(k >= ring)
        def _():
            c = k - ring
            r = root_of(c)
            step = jnp.where(z < r, 1, -1)
            side = jnp.where(z < r, 0, 1)

            @pl.when(z == r)
            def _():
                down(c, -1, 0).wait_send()
                down(c, 1, 1).wait_send()

            @pl.when(z != r)
            def _():
                up(c, step, side).wait_send()

            @pl.when(jnp.logical_and(z != r, inner))
            def _():
                down(c, -step, side).wait_send()

            leave(c, lax.rem(c, ring))

        before(k)

        for i in reversed(range(n + 1)):
            c = k - SKEW * i
            valid = jnp.logical_and(c >= 0, c < total)
            c = jnp.clip(c, 0, total - 1)
            at = block(lax.rem(c, period), CHUNK)
            slot = lax.rem(c, ring)
            r = root_of(c)
            step = jnp.where(z < r, 1, -1)
            side = jnp.where(z < r, 0, 1)
            if i > depth:
                here = jnp.logical_and(z != r, jnp.abs(z - r) == i - depth)

                @pl.when(jnp.logical_and(valid, here))
                def _():
                    down(c, -step, side).wait_recv()

                    @pl.when(inner)
                    def _():
                        down(c, -step, side).start()

                    arrive(c, slot)
            elif i == depth:

                @pl.when(jnp.logical_and(valid, z == r))
                def _():
                    up(c, 1, 0).wait_recv()
                    up(c, -1, 1).wait_recv()
                    root(c, slot, part[at, :] + inbox[0, slot] + inbox[1, slot])
                    down(c, -1, 0).start()
                    down(c, 1, 1).start()
                    arrive(c, slot)
            else:
                here = jnp.where(z < r, z, n - 1 - z) == i

                @pl.when(jnp.logical_and(valid, jnp.logical_and(z != r, here)))
                def _():
                    if i > 0:
                        up(c, step, side).wait_recv()
                        part[at, :] += inbox[side, slot]
                    up(c, step, side).start()


def ring_size(axis):
    return SKEW * lax.axis_size(axis) + 4


def line_scratch(axis, rows, model):
    dma = pltpu.SemaphoreType.DMA
    ring = ring_size(axis)
    return [
        pltpu.VMEM((rows, model), F32),
        pltpu.VMEM((2, ring, CHUNK, model), F32),
        pltpu.VMEM((ring, CHUNK, model), F32),
        dma((ring,)),
        dma((2, ring)),
        dma((2, ring)),
        dma((ring,)),
    ]


def mean_square(x):
    return lax.rsqrt(jnp.mean(x * x, axis=-1, keepdims=True) + EPS)


def nothing(*_):
    pass


def fold(value):
    total = value[0:TILE]
    for i in range(1, value.shape[0] // TILE):
        total = total + value[i * TILE : (i + 1) * TILE]
    return total


def norm_grad(value, gain, grad, acc_ref):
    q = mean_square(value)
    e = gain * grad
    acc_ref[...] += fold(grad * value * q)
    return q * e - value * (q * q * q) * jnp.mean(e * value, axis=-1, keepdims=True)


def middle_kernel(
    mixed_in,
    w_out_in,
    x_in,
    og_in,
    gain_ref,
    w_gate_in,
    w_up_in,
    w_down_in,
    normed_out,
    hidden_out,
    gate_out,
    up_out,
    glow_out,
    block_out,
    low_out,
    own_grad_out,
    weight_out,
    own_ref,
    acc_ref,
    part,
    inbox,
    out,
    send_up,
    send_down,
    recv_up,
    recv_down,
    mixed,
    w_out,
    w_gate,
    w_up,
    w_down,
    normed,
    rows_ref,
    og_ref,
    glow,
    gate_val,
    up_val,
    grad_hidden,
    hidden,
    grad_gate,
    grad_up,
    block_part,
    low,
    weight_sem,
    row_sem,
    og_sem,
    act_sem,
    low_sem,
    own_sem,
    again_sem,
    stage_sem,
):
    n, z = lax.axis_size("mp"), lax.axis_index("mp")
    count = part.shape[0] // CHUNK
    size = GROUP * CHUNK
    groups = count // GROUP
    ring = out.shape[0]
    sems = (send_up, send_down, recv_up, recv_down)
    local = pltpu.make_async_copy

    loads = [
        local(source, target, weight_sem.at[i])
        for i, (source, target) in enumerate(
            (
                (mixed_in, mixed),
                (w_out_in, w_out),
                (w_gate_in, w_gate),
                (w_up_in, w_up),
                (w_down_in, w_down.at[slice(0, w_down_in.shape[0])]),
            )
        )
    ]
    for copy in loads:
        copy.start(priority=1)
    deep = w_down_in.shape[0]

    def og_load(g):
        return local(og_in.at[block(g, size)], og_ref, og_sem.at[0])

    og_load(0).start(priority=1)
    enter_all(("mp",))
    acc_ref[...] = jnp.zeros_like(acc_ref)
    loads[0].wait()
    loads[1].wait()

    def is_root(c):
        return z == n // 2 - 1 + lax.rem(c, 2)

    def row_load(source, c):
        slot = lax.rem(c, ring)
        at = block(lax.rem(c, count), CHUNK)
        return local(source.at[at], rows_ref.at[slot], row_sem.at[slot])

    acts = (
        (normed, normed_out),
        (glow, glow_out),
        (hidden, hidden_out),
        (grad_gate, gate_out),
        (grad_up, up_out),
        (block_part, block_out),
    )

    def act_store(i, g):
        source, target = acts[i]
        source = source.at[lax.rem(g, 2)] if i == 0 else source
        return local(source, target.at[block(g, size)], act_sem.at[i])

    def at_tick(k, first, work):
        g = (k - first) // GROUP

        @pl.when(
            jnp.logical_and(
                jnp.logical_and(k >= first, k < first + GROUP * groups),
                lax.rem(k - first, GROUP) == 0,
            )
        )
        def _():
            work(g)

    def project(g):
        def work(cols):
            part[block(g, size), cols] = dot(mixed[block(g, size), :], w_out[:, cols])

        work(slice(None))

    def piece_gate(g):
        @pl.when(g == 0)
        def _():
            for copy in loads[2:]:
                copy.wait()

        def work(cols):
            gate_val[:, cols] = dot(normed[lax.rem(g, 2)], w_gate[:, cols])

        work(slice(None))
        act_store(0, g).start(priority=1)

    def piece_up(g):
        def work(cols):
            up_val[:, cols] = dot(normed[lax.rem(g, 2)], w_up[:, cols])

        work(slice(None))

        @pl.when(g > 0)
        def _():
            for i in range(1, 6):
                act_store(i, g - 1).wait()

    def piece_low(g):
        og_load(g).wait()

        @pl.loop(0, size // ROWS)
        def _(q):
            glow[block(q, ROWS), :] = og_ref[block(q, ROWS), :].astype(BF16)

        @pl.when(g + 1 < groups)
        def _():
            og_load(g + 1).start(priority=1)

        act_store(1, g).start(priority=1)
        act_store(0, g).wait()

    def piece_hidden(g):
        def work(cols):
            grad_hidden[...] = matmul_back(glow[...], w_down[:deep, :])

        work(slice(None))

    def piece_act(g):
        @pl.loop(0, size // CHUNK)
        def _(q):
            at = block(q, CHUNK)
            up = up_val[at, :]
            grad = grad_hidden[at, :]
            act, slope = gelu_both(gate_val[at, :])
            hidden[at, :] = (act * up).astype(BF16)
            grad_gate[at, :] = (grad * up * slope).astype(BF16)
            grad_up[at, :] = (grad * act).astype(BF16)

        for i in range(2, 5):
            act_store(i, g).start(priority=1)

    def piece_down(g):
        def work(cols):
            block_part[:, cols] = dot(hidden[...], w_down[:deep, cols])

        work(slice(None))
        act_store(5, g).start(priority=1)

    def piece_back_gate(g):
        def work(cols):
            part[block(g, size), cols] = matmul_back(grad_gate[...], w_gate[cols, :])

        work(slice(None))

    def piece_back_up(g):
        def work(cols):
            part[block(g, size), cols] += matmul_back(grad_up[...], w_up[cols, :])

        work(slice(None))

    tokens = count * CHUNK
    half = tokens // 2
    quarter = half // 2
    again = [
        local(source, target, again_sem.at[i])
        for i, (source, target) in enumerate(
            (
                (normed_out, w_down.at[slice(0, tokens)]),
                (gate_out, w_gate.at[slice(0, tokens)]),
                (up_out, w_up.at[slice(0, tokens)]),
                (hidden_out, w_gate.at[slice(tokens, 2 * tokens)]),
                (glow_out.at[slice(0, half)], w_down.at[slice(tokens, tokens + half)]),
                (glow_out.at[slice(half, half + quarter)], normed.at[0]),
                (glow_out.at[slice(half + quarter, tokens)], normed.at[1]),
            )
        )
    ]
    tall = w_gate.shape[0] // WEIGHT_STEPS
    stages = (gate_val, up_val, grad_hidden)

    def stage_store(which, i):
        return local(stages[which], weight_out.at[which, block(i, tall)], stage_sem.at[which])

    def piece_reload():
        for i in range(1, 6):
            act_store(i, groups - 1).wait()
        for copy in again:
            copy.start(priority=1)

    def piece_ready():
        for copy in again:
            copy.wait()

    def contract(left, right):
        return lax.dot_general(left, right, CONTRACT_ROWS, preferred_element_type=F32)

    def piece_weight(step):
        i = step // 3
        at = block(i, tall)
        for which in range(3):

            @pl.when(lax.rem(step, 3) == which)
            def _():
                @pl.when(i > 0)
                def _():
                    stage_store(which, i - 1).wait()

                stage = stages[which]

                def work(cols):
                    if which == 0:
                        stage[:, cols] = contract(w_down[:tokens, at], w_gate[:tokens, cols])
                    elif which == 1:
                        stage[:, cols] = contract(w_down[:tokens, at], w_up[:tokens, cols])
                    else:
                        middle = tokens + half + quarter
                        stage[:, cols] = (
                            contract(
                                w_down[tokens : tokens + half, at],
                                w_gate[tokens : tokens + half, cols],
                            )
                            + contract(normed[0, :, at], w_gate[tokens + half : middle, cols])
                            + contract(normed[1, :, at], w_gate[middle : 2 * tokens, cols])
                        )

                work(slice(None))
                stage_store(which, i).start(priority=1)

    first = GROUP + SKEW * n
    spare = GROUP * groups + ring + 3
    first_weight = spare + 3
    weights = 3 * WEIGHT_STEPS

    def before(k):
        @pl.when(k == spare)
        def _():
            piece_reload()

        @pl.when(k == first_weight - 1)
        def _():
            piece_ready()

        @pl.when(jnp.logical_and(k >= first_weight, k < first_weight + weights))
        def _():
            piece_weight(k - first_weight)

        @pl.when(jnp.logical_and(k < count, is_root(k)))
        def _():
            row_load(x_in, k).start(priority=1)

        @pl.when(
            jnp.logical_and(jnp.logical_and(k >= count, k < 2 * count), is_root(k))
        )
        def _():
            row_load(og_in, k).start(priority=1)

        at_tick(k, 0, project)
        at_tick(k, first, piece_gate)
        at_tick(k, first + 1, piece_up)
        at_tick(k, first + 2, piece_low)
        at_tick(k, first + 3, piece_hidden)
        at_tick(k, first + 4, piece_act)
        at_tick(k, first + 6, piece_down)
        at_tick(k, GROUP + ring, piece_back_gate)
        at_tick(k, GROUP + ring + 2, piece_back_up)

    def root(c, slot, total):
        j = lax.rem(c, count)
        mine = block(j // 2, CHUNK)
        row_load(x_in, c).wait()

        @pl.when(c < count)
        def _():
            value = rows_ref[slot] + total
            own_ref[mine, :] = value
            out[slot] = (value * mean_square(value) * gain_ref[...]).astype(BF16).astype(F32)

        @pl.when(c >= count)
        def _():
            back = norm_grad(own_ref[mine, :], gain_ref[...], total, acc_ref)
            out[slot] = rows_ref[slot] + back

    def low_store(c, slot):
        at = block(lax.rem(c, count), CHUNK)
        return local(low.at[slot], low_out.at[at], low_sem.at[slot])

    def own_store(c, slot):
        at = block(lax.rem(c, count) // 2, CHUNK)
        return local(out.at[slot], own_grad_out.at[at], own_sem.at[slot])

    def arrive(c, slot):
        @pl.when(c < count)
        def _():
            normed[lax.rem(c // GROUP, 2), block(lax.rem(c, GROUP), CHUNK), :] = out[slot].astype(BF16)

        @pl.when(c >= count)
        def _():
            low[slot] = out[slot].astype(BF16)
            low_store(c, slot).start(priority=1)

            @pl.when(is_root(c))
            def _():
                own_store(c, slot).start(priority=1)

    def leave(c, slot):
        @pl.when(c >= count)
        def _():
            low_store(c, slot).wait()

            @pl.when(is_root(c))
            def _():
                own_store(c, slot).wait()

    line_sum("mp", 2 * count, count, part, inbox, out, sems, before, root, arrive, leave)

    for which in range(3):
        stage_store(which, WEIGHT_STEPS - 1).wait()


def middle_call(*args):
    mixed, w_out, x, og, gain, w_gate, w_up, w_down = args
    rows, model = x.shape
    width, hidden = mixed.shape[1], w_gate.shape[1]
    size = GROUP * CHUNK
    dma = pltpu.SemaphoreType.DMA
    ring = ring_size("mp")
    act = shape((rows, hidden), BF16)
    tall = shape((rows, model), BF16)
    return pl.pallas_call(
        middle_kernel,
        out_shape=(
            tall,
            act,
            act,
            act,
            tall,
            shape((rows, model)),
            tall,
            shape((rows // 2, model)),
            shape((3, model, hidden)),
            shape((rows // 2, model)),
            shape((TILE, model)),
        ),
        in_specs=[HBM] * 4 + [VMEM] + [HBM] * 3,
        out_specs=(HBM,) * 9 + (VMEM,) * 2,
        scratch_shapes=line_scratch("mp", rows, model)
        + [
            pltpu.VMEM((rows, width), BF16),
            pltpu.VMEM((width, model), BF16),
            pltpu.VMEM((model, hidden), BF16),
            pltpu.VMEM((model, hidden), BF16),
            pltpu.VMEM((max(hidden, rows * 3 // 2), model), BF16),
            pltpu.VMEM((2, size, model), BF16),
            pltpu.VMEM((ring, CHUNK, model), F32),
            pltpu.VMEM((size, model), F32),
            pltpu.VMEM((size, model), BF16),
            pltpu.VMEM((size, hidden), F32),
            pltpu.VMEM((size, hidden), F32),
            pltpu.VMEM((size, hidden), F32),
            pltpu.VMEM((size, hidden), BF16),
            pltpu.VMEM((size, hidden), BF16),
            pltpu.VMEM((size, hidden), BF16),
            pltpu.VMEM((size, model), F32),
            pltpu.VMEM((ring, CHUNK, model), BF16),
            dma((5,)),
            dma((ring,)),
            dma((1,)),
            dma((6,)),
            dma((ring,)),
            dma((ring,)),
            dma((7,)),
            dma((3,)),
        ],
        compiler_params=params(2, 63),
        cost_estimate=cost(400),
        name="middle",
    )(*args)


def last_kernel(
    own_grad_in,
    x_in,
    grad_branch_in,
    input_in,
    w_branch_in,
    w_input_in,
    gain_ref,
    other_acc,
    sums_in,
    ends_in,
    blocks_in,
    grad_out,
    norm_ref,
    small_out,
    part,
    inbox,
    out,
    send_up,
    send_down,
    recv_up,
    recv_down,
    own_grad_ref,
    x_ref,
    grad_branch,
    input_low,
    w_branch,
    w_input,
    load_sem,
    store_sem,
    acc_ref,
    mine_ref,
    seq_in,
    mp_in,
    send_s,
    recv_s,
    send_m,
    recv_m,
    small,
    small_in,
    send_v,
    recv_v,
):
    count = part.shape[0] // CHUNK
    size = GROUP * CHUNK
    sems = (send_up, send_down, recv_up, recv_down)
    local = pltpu.make_async_copy

    loads = [
        local(source, target, load_sem.at[i])
        for i, (source, target) in enumerate(
            (
                (grad_branch_in, grad_branch),
                (w_branch_in, w_branch),
                (input_in, input_low),
                (w_input_in, w_input),
                (own_grad_in, own_grad_ref),
                (x_in, x_ref),
            )
        )
    ]
    for copy in loads:
        copy.start()
    acc_ref[...] = jnp.zeros_like(acc_ref)
    mine_ref[...] = jnp.zeros_like(mine_ref)
    enter_all(("seq", "mp"))
    for copy in loads[:4]:
        copy.wait()

    kinds = sums_in.shape[0]
    me = lax.axis_index("seq")
    width = sums_in.shape[2]
    height = kinds + ends_in.shape[0]
    head = blocks_in.shape[0]
    for i in range(kinds):
        small[0, i : i + 1, :] = jnp.sum(sums_in[i], axis=0, keepdims=True)
    small[0, kinds:height, :] = ends_in[...]
    small[0, height : height + head, :] = blocks_in[:, :width]
    small[0, height + head :, :] = blocks_in[:, width:]
    levels = small_in.shape[0]

    def exchange(level):
        bit = 1 << level
        partner = me + bit - 2 * bit * lax.rem(me // bit, 2)
        return pltpu.make_async_remote_copy(
            src_ref=small.at[level],
            dst_ref=small_in.at[level],
            send_sem=send_v.at[level],
            recv_sem=recv_v.at[level],
            device_id={"seq": partner},
            device_id_type=MESH,
        )

    spacing = (count - 4) // (levels + 1)
    seq_copies = to_all("seq", mine_ref.at[0], seq_in, send_s, recv_s)
    mp_copies = to_all("mp", mine_ref.at[1], mp_in, send_m, recv_m)
    settled = count + SKEW * (lax.axis_size("mp") // 2)

    def before(k):
        for level in range(levels + 1):

            @pl.when(k == 3 + level * spacing)
            def _():
                if level > 0:
                    exchange(level - 1).wait()
                    total = small[level - 1] + small_in[level - 1]
                    if level < levels:
                        small[level] = total
                    else:
                        small_out[...] = total
                if level < levels:
                    exchange(level).start()

        @pl.when(k == settled)
        def _():
            mine_ref[0, 0:1, :] = jnp.sum(acc_ref[...], axis=0, keepdims=True)
            mine_ref[0, 1:2, :] = jnp.sum(other_acc[...], axis=0, keepdims=True)
            seq_in[me] = mine_ref[0]
            for copy in seq_copies:
                copy.start()

        @pl.when(k == settled + 2)
        def _():
            for copy in seq_copies:
                copy.wait()
            mine_ref[1] = jnp.sum(seq_in[...], axis=0)
            mp_in[lax.axis_index("mp")] = mine_ref[1]
            for copy in mp_copies:
                copy.start()

        @pl.when(jnp.logical_and(lax.rem(k, 4) == 0, k // 4 < count // GROUP))
        def _():
            at = block(k // 4, size)

            def work(cols):
                part[at, cols] = matmul_back(grad_branch[at, :], w_branch[cols, :]) + matmul_back(
                    input_low[at, :], w_input[cols, :]
                )

            work(slice(None))

        @pl.when(k == 1)
        def _():
            for copy in loads[4:]:
                copy.wait()

    def root(c, slot, total):
        back = norm_grad(x_ref[block(c, CHUNK), :], gain_ref[...], total, acc_ref)
        out[slot] = own_grad_ref[block(c // 2, CHUNK), :] + back

    def store(c, slot):
        return local(out.at[slot], grad_out.at[block(c, CHUNK)], store_sem.at[slot])

    def arrive(c, slot):
        store(c, slot).start()

    def leave(c, slot):
        store(c, slot).wait()

    line_sum("mp", count, count, part, inbox, out, sems, before, root, arrive, leave)

    for copy in mp_copies:
        copy.wait()
    norm_ref[...] = jnp.sum(mp_in[...], axis=0)


def enter_all(axes):
    barrier = pltpu.get_barrier_semaphore()
    count = 0
    for axis in axes:
        size, me = lax.axis_size(axis), lax.axis_index(axis)
        for d in range(1, size):
            pl.semaphore_signal(
                barrier, 1, device_id={axis: lax.rem(me + d, size)}, device_id_type=MESH
            )
        count += size - 1
    pl.semaphore_wait(barrier, count)


def cost(micros):
    return pl.CostEstimate(flops=int(micros * 1e9), bytes_accessed=1 << 20, transcendentals=0)


def nseq_levels():
    return (lax.axis_size("seq") - 1).bit_length()


def last_call(*args):
    x, grad_branch = args[1:3]
    rows, model = x.shape
    width = grad_branch.shape[1]
    lines = args[8].shape[0] + args[9].shape[0] + 2 * args[10].shape[0]
    levels = nseq_levels()
    dma = pltpu.SemaphoreType.DMA
    nseq, nmp = lax.axis_size("seq"), lax.axis_size("mp")
    return pl.pallas_call(
        last_kernel,
        out_shape=(shape((rows, model)), shape((TILE, model)), shape((lines, width))),
        in_specs=[HBM] * 6 + [VMEM] * 5,
        out_specs=(HBM,) + (VMEM,) * 2,
        scratch_shapes=line_scratch("mp", rows, model)
        + [
            pltpu.VMEM((rows // 2, model), F32),
            pltpu.VMEM((rows, model), F32),
            pltpu.VMEM((rows, width), BF16),
            pltpu.VMEM((rows, width), BF16),
            pltpu.VMEM((model, width), BF16),
            pltpu.VMEM((model, width), BF16),
            dma((6,)),
            dma((ring_size("mp"),)),
            pltpu.VMEM((TILE, model), F32),
            pltpu.VMEM((2, TILE, model), F32),
            pltpu.VMEM((nseq, TILE, model), F32),
            pltpu.VMEM((nmp, TILE, model), F32),
            dma((nseq - 1,)),
            dma((nseq - 1,)),
            dma((nmp - 1,)),
            dma((nmp - 1,)),
            pltpu.VMEM((levels, lines, width), F32),
            pltpu.VMEM((levels, lines, width), F32),
            dma((levels,)),
            dma((levels,)),
        ],
        compiler_params=params(4, 62),
        cost_estimate=cost(200),
        name="last_sums",
    )(*args)


def finish_kernel(
    heads,
    grad_in,
    mlp_in,
    rec_in,
    small_hbm,
    norm_hbm,
    decay_hbm,
    grad_out,
    w_gate_out,
    w_up_out,
    w_branch_out,
    w_input_out,
    w_down_out,
    w_out_out,
    gate_r_out,
    gate_i_out,
    taps_out,
    conv_bias_out,
    bias_r_out,
    bias_i_out,
    decay_out,
    norm_in_out,
    norm_mlp_out,
    state_out,
    conv_out,
    tall,
    mlp,
    rec,
    small_in,
    norm_in,
    raw_ref,
    load_sem,
    store_sem,
    extra_sem,
):
    local = pltpu.make_async_copy
    size = grad_in.shape[0] // COPIES
    extra = [
        local(source, target, extra_sem.at[i])
        for i, (source, target) in enumerate(
            ((small_hbm, small_in), (norm_hbm, norm_in), (decay_hbm, raw_ref))
        )
    ]
    for copy in extra:
        copy.start()
    jobs = [(mlp_in, mlp, None), (rec_in, rec, None)]
    for i in range(COPIES):
        at = slice(i * size, (i + 1) * size)
        jobs.append((grad_in.at[at], tall.at[at], grad_out.at[at]))
    loads = [local(source, held, load_sem.at[i]) for i, (source, held, _) in enumerate(jobs)]
    stores = [
        local(held, target, store_sem.at[i])
        for i, (held, target) in enumerate(
            [(held, target) for _, held, target in jobs[2:]]
            + [
                (mlp.at[0], w_gate_out),
                (mlp.at[1], w_up_out),
                (rec.at[1], w_branch_out),
                (rec.at[2], w_input_out),
            ]
        )
    ]
    for copy in loads:
        copy.start()
    for copy in extra:
        copy.wait()
    taps, seqs, edge = taps_out.shape[0], state_out.shape[0], conv_out.shape[0]
    head = gate_r_out.shape[1]
    width = small_in.shape[1]
    decay = small_in[0:1, :].reshape(width) * (RATE_SCALE * jax.nn.sigmoid(-raw_ref[...]))
    decay_out[...] = decay
    bias_r_out[...] = small_in[1:2, :].reshape(width)
    bias_i_out[...] = small_in[2:3, :].reshape(width)
    conv_bias_out[...] = small_in[3:4, :].reshape(width)
    taps_out[...] = small_in[4 : 4 + taps, :]
    begin = 4 + taps
    state_out[...] = small_in[begin : begin + seqs, :]
    for s in range(seqs):
        end = begin + seqs + (s + 1) * TILE
        for k in range(edge):
            conv_out[k, s : s + 1, :] = small_in[end - edge + k : end - edge + k + 1, :]
    begin += seqs + seqs * TILE
    for i, target in enumerate((gate_r_out, gate_i_out)):
        line = small_in[begin + i * head : begin + (i + 1) * head, :]
        for h in range(heads):
            turned = line if h == 0 else pltpu.roll(line, width - h * head, 1)
            target[h] = turned[:, :head]
    norm_in_out[...] = norm_in[0:1, :].reshape(norm_in.shape[1])
    norm_mlp_out[...] = norm_in[1:2, :].reshape(norm_in.shape[1])
    loads[0].wait()
    loads[1].wait()
    for copy in stores[COPIES:]:
        copy.start()
    w_down_out[...] = mlp[2].T
    w_out_out[...] = rec[0].T
    for i in range(COPIES):
        loads[2 + i].wait()
        stores[i].start()
    for copy in stores:
        copy.wait()


def finish_call(seqs, heads, head, edge, *args):
    stream_grad, mlp_grads, rec_grads, small, norms, decay = args
    rows, model = stream_grad.shape
    own, hidden = mlp_grads.shape[1:]
    width = rec_grads.shape[2]
    taps = edge + 1
    line = shape((width,))
    tall = shape((rows, model))
    return pl.pallas_call(
        functools.partial(finish_kernel, heads),
        out_shape=(
            tall,
            shape((own, hidden)),
            shape((own, hidden)),
            shape((own, width)),
            shape((own, width)),
            shape((hidden, own)),
            shape((width, own)),
            shape((heads, head, head)),
            shape((heads, head, head)),
            shape((taps, width)),
            line,
            line,
            line,
            line,
            shape((model,)),
            shape((model,)),
            shape((seqs, width)),
            shape((edge, seqs, width)),
        ),
        in_specs=[HBM] * 3 + [PINNED] * 3,
        out_specs=(HBM,) * 5 + (VMEM,) * 13,
        scratch_shapes=[
            pltpu.VMEM((rows, model), F32),
            pltpu.VMEM((3, own, hidden), F32),
            pltpu.VMEM((3, own, width), F32),
            pltpu.VMEM(small.shape, F32),
            pltpu.VMEM(norms.shape, F32),
            pltpu.VMEM(decay.shape, F32),
            pltpu.SemaphoreType.DMA((2 + COPIES,)),
            pltpu.SemaphoreType.DMA((4 + COPIES,)),
            pltpu.SemaphoreType.DMA((3,)),
        ],
        compiler_params=pltpu.CompilerParams(vmem_limit_bytes=63 << 20),
        cost_estimate=cost(15),
        name="finish",
    )(*args)


def copy_kernel(source, target, held, load_sem, store_sem):
    size = source.shape[0] // COPIES
    pieces = [slice(i * size, (i + 1) * size) for i in range(COPIES)]
    local = pltpu.make_async_copy
    loads = [local(source.at[p], held.at[p], load_sem.at[i]) for i, p in enumerate(pieces)]
    stores = [local(held.at[p], target.at[p], store_sem.at[i]) for i, p in enumerate(pieces)]
    for copy in loads:
        copy.start()
    for load, store in zip(loads, stores):
        load.wait()
        store.start()
    for copy in stores:
        copy.wait()


def copy_call(array):
    return pl.pallas_call(
        copy_kernel,
        out_shape=shape(array.shape),
        in_specs=[HBM],
        out_specs=HBM,
        scratch_shapes=[
            pltpu.VMEM(array.shape, F32),
            pltpu.SemaphoreType.DMA((COPIES,)),
            pltpu.SemaphoreType.DMA((COPIES,)),
        ],
        compiler_params=pltpu.CompilerParams(vmem_limit_bytes=63 << 20),
        cost_estimate=cost(6),
        name="copy_out",
    )(array)


def params(collective, megabytes=60):
    return pltpu.CompilerParams(
        collective_id=collective, has_side_effects=True, vmem_limit_bytes=megabytes << 20
    )


def shape(dims, dtype=F32):
    return jax.ShapeDtypeStruct(dims, dtype)


def recurrence_forward(span, *args):
    x, w_input = args[:2]
    rows, model = x.shape
    seqs, width = rows // span, w_input.shape[1]
    devices = lax.axis_size("seq")
    dma = pltpu.SemaphoreType.DMA
    groups = seqs // 2
    columns = (width // LANES, rows, LANES)
    spaced = (width // LANES, seqs * (span + TILE), LANES)
    padded = (seqs, span + TILE, width)
    return pl.pallas_call(
        functools.partial(forward_kernel, span),
        out_shape=(
            shape((rows, model), BF16),
            shape((rows, width)),
            shape(padded),
            shape((rows, 2 * width)),
            shape(columns),
            shape((rows, width), BF16),
            shape((seqs, width)),
            shape((devices, 2, seqs, width)),
            shape((width, 2 * width), BF16),
            shape((TILE, width)),
            shape(((seqs + 1) * TILE, width)),
        ),
        in_specs=[HBM] * 3 + [VMEM] * 8 + [pl.BlockSpec(memory_space=pltpu.SMEM)] + [VMEM] * 2,
        out_specs=(HBM,) * 5 + (VMEM,) * 6,
        scratch_shapes=[
            pltpu.VMEM((rows, model), F32),
            pltpu.VMEM((model, width), BF16),
            pltpu.VMEM((model, width), BF16),
            pltpu.VMEM((rows, model), BF16),
            pltpu.VMEM((rows, width), F32),
            pltpu.VMEM(padded, F32),
            pltpu.VMEM((rows, 2 * width), F32),
            pltpu.VMEM(columns, F32),
            pltpu.VMEM((rows, width), F32),
            pltpu.VMEM(spaced, F32),
            pltpu.VMEM(spaced, F32),
            pltpu.VMEM((2, span, width), F32),
            pltpu.VMEM((seqs, TILE, width), F32),
            pltpu.VMEM((seqs, TILE, width), F32),
            pltpu.VMEM((2, seqs, width), F32),
            dma((groups + 2,)),
            dma((4,)),
            dma((groups,)),
            dma((devices - 1,)),
            dma((devices - 1,)),
            dma((1,)),
            dma((1,)),
        ],
        compiler_params=params(0),
        cost_estimate=cost(50),
        name="recurrence_forward",
    )(*args)


def widen(array, width):
    short = width - array.shape[-1]
    if short == 0:
        return array
    return jnp.pad(array, [(0, 0)] * (array.ndim - 1) + [(0, short)])


def per_device(
    stream,
    norm_in,
    w_branch,
    w_input,
    conv_kernel,
    conv_bias,
    gate_r,
    bias_r,
    gate_i,
    bias_i,
    decay_param,
    w_out,
    norm_mlp,
    w_gate,
    w_up,
    w_down,
    state_init,
    conv_init,
    fresh_rows,
    out_grad,
):
    seqs, span, model = stream.shape
    channels = w_branch.shape[1]
    mlp_dev = w_gate.shape[1]
    heads, head_width = gate_r.shape[:2]
    taps = conv_kernel.shape[0]
    edge = taps - 1
    rows = seqs * span
    devices = lax.axis_size("seq")
    position = lax.axis_index("seq")
    width = -(-channels // 128) * 128

    flat_in = stream.reshape(rows, model)
    flat_grad = out_grad.reshape(rows, model)
    w_branch_p = widen(w_branch, width)
    w_input_p = widen(w_input, width)
    w_out_p = jnp.pad(w_out, ((0, width - channels), (0, 0))) if width > channels else w_out
    taps_p = widen(conv_kernel, width)
    def line(value):
        return widen(value, width)

    (
        normed,
        branch,
        padded,
        pre,
        hidden,
        mixed,
        carry,
        sums,
        gates,
        rates,
        ends,
    ) = recurrence_forward(
        span,
        flat_in,
        w_input_p,
        w_branch_p,
        norm_in[None],
        taps_p,
        line(conv_bias),
        line(decay_param),
        line(bias_r),
        line(bias_i),
        gate_r,
        gate_i,
        fresh_rows,
        widen(state_init, width),
        widen(jnp.swapaxes(conv_init, 0, 1), width),
    )
    _, _, _, _, _, block_part, resid_low, own_grad, mlp_grads, own, norm_mlp_acc = middle_call(
        mixed, w_out_p, flat_in, flat_grad, norm_mlp[None], w_gate, w_up, w_down
    )
    mlp_grads = lax.psum_scatter(mlp_grads, "seq", scatter_dimension=1, tiled=True)
    block_out, rec_grads, grad_branch, input_low, acc, blocks = backward_call(
        span,
        heads,
        head_width,
        block_part,
        own,
        resid_low,
        w_out_p,
        branch,
        hidden,
        pre,
        padded,
        normed,
        mixed,
        carry,
        sums,
        taps_p,
        rates,
        gates,
    )

    block_out = copy_call(block_out)
    rec_grads, grad_branch, mlp_grads, block_out = lax.optimization_barrier(
        (rec_grads, grad_branch, mlp_grads, block_out)
    )
    rec_grads = lax.psum_scatter(rec_grads, "seq", scatter_dimension=1, tiled=True)

    stream_grad, norm_grads, small = last_call(
        own_grad,
        flat_in,
        grad_branch,
        input_low,
        w_branch_p,
        w_input_p,
        norm_in[None],
        norm_mlp_acc,
        acc,
        ends,
        blocks,
    )
    (
        stream_grad,
        w_gate_grad,
        w_up_grad,
        w_branch_grad,
        w_input_grad,
        w_down_grad,
        w_out_grad,
        gate_r_grad,
        gate_i_grad,
        taps_grad,
        conv_bias_grad,
        bias_r_grad,
        bias_i_grad,
        decay_grad,
        norm_in_grad,
        norm_mlp_grad,
        final_state,
        final_conv,
    ) = finish_call(
        seqs,
        heads,
        head_width,
        edge,
        stream_grad,
        mlp_grads,
        rec_grads,
        small,
        norm_grads,
        line(decay_param),
    )
    return (
        block_out.reshape(stream.shape),
        stream_grad.reshape(stream.shape),
        norm_in_grad,
        w_branch_grad[:, :channels],
        w_input_grad[:, :channels],
        taps_grad[:, :channels],
        conv_bias_grad[:channels],
        gate_r_grad,
        bias_r_grad[:channels],
        gate_i_grad,
        bias_i_grad[:channels],
        decay_grad[:channels],
        w_out_grad[:channels],
        norm_mlp_grad,
        w_gate_grad,
        w_up_grad,
        w_down_grad,
        final_state[:, :channels],
        jnp.swapaxes(final_conv, 0, 1)[:, :, :channels],
    )


def solution(mesh):
    seq_rows = P(None, "seq", None)
    columns = P(None, "mp")
    channel = P("mp")
    return jax.shard_map(
        per_device,
        mesh=mesh,
        in_specs=(
            seq_rows,
            P(),
            columns,
            columns,
            columns,
            channel,
            P("mp", None, None),
            channel,
            P("mp", None, None),
            channel,
            channel,
            P("mp", None),
            P(),
            columns,
            columns,
            P("mp", None),
            columns,
            P(None, None, "mp"),
            P(),
            seq_rows,
        ),
        out_specs=(
            seq_rows,
            seq_rows,
            P(),
            P("seq", "mp"),
            P("seq", "mp"),
            columns,
            channel,
            P("mp", None, None),
            channel,
            P("mp", None, None),
            channel,
            channel,
            P("mp", "seq"),
            P(),
            P("seq", "mp"),
            P("seq", "mp"),
            P("mp", "seq"),
            columns,
            P(None, None, "mp"),
        ),
        check_vma=False,
    )
```

```python
import functools

import jax
import jax.numpy as jnp
from jax import lax
from jax.experimental import pallas as pl
from jax.experimental.pallas import tpu as pltpu
from jax.sharding import PartitionSpec as P

MESH = pl.DeviceIdType.MESH
RATE_SCALE = 8.0
EPS = 1e-06
GELU_C = 0.7978845608028654
GELU_K = 0.044715
CONTRACT_ROWS = (((0,), (0,)), ((), ()))
CONTRACT_LAST = (((1,), (1,)), ((), ()))
TILE = 8
LANES = 128
ROWS = 32
CHUNK = 16
SKEW = 2
GROUP = 16
WEIGHT_STEPS = 8
COPIES = 8
LATER = 6
F32 = jnp.float32
BF16 = jnp.bfloat16
VMEM = pl.BlockSpec(memory_space=pltpu.VMEM)
HBM = pl.BlockSpec(memory_space=pl.ANY)
PINNED = pl.BlockSpec(memory_space=pltpu.HBM)


def dot(a, b):
    return jnp.dot(a, b, preferred_element_type=F32)


def matmul_back(a, b):
    return lax.dot_general(a, b, CONTRACT_LAST, preferred_element_type=F32)


def block(i, size):
    return pl.ds(pl.multiple_of(i * size, size), size)


def gelu(x):
    t = jnp.tanh(GELU_C * (x + GELU_K * (x * x * x)))
    return 0.5 * x * (1.0 + t)


def gelu_both(x):
    x2 = x * x
    t = jnp.tanh(GELU_C * (x + GELU_K * (x2 * x)))
    half = 0.5 * (1.0 + t)
    slope = half + 0.5 * x * (1.0 - t * t) * (GELU_C * (1.0 + (3.0 * GELU_K) * x2))
    return x * half, slope


def one_minus_square(log_a, a):
    y = 2.0 * log_a
    s = 1.0 + y * (1.0 / 8.0)
    for k in (7, 6, 5, 4, 3, 2):
        s = 1.0 + (y * (1.0 / k)) * s
    return jnp.where(y > -0.35, -y * s, 1.0 - a * a)


def get(ref, at):
    return jnp.concatenate([ref[j, at, :] for j in range(ref.shape[0])], axis=-1)


def put(ref, at, value):
    for j in range(ref.shape[0]):
        ref[j, at, :] = value[:, j * LANES : (j + 1) * LANES]


def to_all(axis, src, slots, send, recv):
    size, me = lax.axis_size(axis), lax.axis_index(axis)
    return [
        pltpu.make_async_remote_copy(
            src_ref=src,
            dst_ref=slots.at[me],
            send_sem=send.at[d - 1],
            recv_sem=recv.at[d - 1],
            device_id={axis: lax.rem(me + d, size)},
            device_id_type=MESH,
        )
        for d in range(1, size)
    ]


def to_one(axis, distance, src, dst, send, recv):
    size, me = lax.axis_size(axis), lax.axis_index(axis)
    return pltpu.make_async_remote_copy(
        src_ref=src,
        dst_ref=dst,
        send_sem=send,
        recv_sem=recv,
        device_id={axis: lax.rem(me + distance + size, size)},
        device_id_type=MESH,
    )


def spread_gates(blocks_ref, out_ref, start, width):
    heads, size = blocks_ref.shape[:2]
    for h in range(heads):
        block_h = blocks_ref[h].astype(F32)
        parts = [block_h]
        if h > 0:
            parts.insert(0, jnp.zeros((size, h * size), F32))
        if width > (h + 1) * size:
            parts.append(jnp.zeros((size, width - (h + 1) * size), F32))
        row = jnp.concatenate(parts, axis=1).astype(BF16)
        out_ref[h * size : (h + 1) * size, start : start + width] = row
    if width > heads * size:
        rest = jnp.zeros((width - heads * size, width), BF16)
        out_ref[heads * size : width, start : start + width] = rest


def forward_kernel(
    span,
    x_in,
    w_input_in,
    w_branch_in,
    gain_ref,
    taps_ref,
    conv_bias_ref,
    decay_ref,
    bias_r_ref,
    bias_i_ref,
    gate_r_ref,
    gate_i_ref,
    fresh_ref,
    state_ref,
    conv_init_ref,
    normed_out,
    branch_out,
    pad_out,
    pre_out,
    hidden_out,
    mixed_ref,
    carry_ref,
    sums_ref,
    gates_ref,
    vec_ref,
    ends_ref,
    x_ref,
    w_input_ref,
    w_branch_ref,
    normed_ref,
    branch_ref,
    pad_ref,
    pre_ref,
    hidden_ref,
    act_ref,
    a_ref,
    b_ref,
    conv_ref,
    tail_ref,
    tail_in,
    mine_ref,
    load_sem,
    store_sem,
    normed_sem,
    send1,
    recv1,
    send_t,
    recv_t,
):
    seqs = state_ref.shape[0]
    width = taps_ref.shape[1]
    taps = taps_ref.shape[0]
    rows = seqs * span
    devices, me = lax.axis_size("seq"), lax.axis_index("seq")
    local = pltpu.make_async_copy
    pitch = a_ref.shape[1] // seqs
    group = 2 * span
    groups = rows // group

    def x_load(g):
        at = block(g, group)
        return local(x_in.at[at], x_ref.at[at], load_sem.at[g])

    weight_loads = [
        local(w_input_in, w_input_ref, load_sem.at[groups]),
        local(w_branch_in, w_branch_ref, load_sem.at[groups + 1]),
    ]
    x_load(0).start()
    weight_loads[0].start()
    for g in range(1, groups):
        x_load(g).start()
    weight_loads[1].start()

    enter_all(("seq",))
    spread_gates(gate_r_ref, gates_ref, 0, width)
    spread_gates(gate_i_ref, gates_ref, width, width)
    vec_ref[0:1, :] = conv_bias_ref[...].reshape(1, width)
    vec_ref[1:2, :] = jax.nn.softplus(-decay_ref[...].reshape(1, width))
    bias_r = bias_r_ref[...].reshape(1, width)
    bias_i = bias_i_ref[...].reshape(1, width)
    keep = [1.0 - fresh_ref[s].astype(F32) for s in range(seqs)]

    def normed_store(g):
        at = block(g, group)
        return local(normed_ref.at[at], normed_out.at[at], normed_sem.at[g])

    def norm(g):
        x_load(g).wait()
        for q in range(group // CHUNK):
            at = slice(g * group + q * CHUNK, g * group + (q + 1) * CHUNK)
            x = x_ref[at, :]
            normed_ref[at, :] = (x * mean_square(x) * gain_ref[...]).astype(BF16)

    norm(0)
    weight_loads[0].wait()
    for g in range(groups):
        if g + 1 < groups:
            norm(g + 1)
        conv = dot(normed_ref[slice(g * group, (g + 1) * group), :], w_input_ref[...])
        for j in range(group // span):
            pad_ref[g * (group // span) + j, pl.ds(TILE, span), :] = conv[
                j * span : (j + 1) * span
            ]
    for g in range(groups):
        normed_store(g).start()

    for s in range(seqs):
        tail_ref[s] = pad_ref[s, pl.ds(span, TILE), :]
    tail_copy = to_one("seq", 1, tail_ref, tail_in, send_t.at[0], recv_t.at[0])
    tail_copy.start()
    weight_loads[1].wait()

    def branch(g):
        branch_ref[block(g, group), :] = dot(normed_ref[block(g, group), :], w_branch_ref[...])

    @pl.loop(0, groups // 2)
    def _(g):
        branch(g)

    stores = [
        local(source, target, store_sem.at[i])
        for i, (source, target) in enumerate(
            (
                (branch_ref, branch_out),
                (pad_ref, pad_out),
                (pre_ref, pre_out),
                (hidden_ref, hidden_out),
            )
        )
    ]
    tail_copy.wait()
    lead = jnp.zeros((TILE - taps + 1, width), F32)
    for s in range(seqs):
        initial = jnp.concatenate(
            [lead] + [conv_init_ref[k, s : s + 1, :] * keep[s] for k in range(taps - 1)], axis=0
        )
        pad_ref[s, pl.ds(0, TILE), :] = jnp.where(me == 0, initial, tail_in[s])
    stores[1].start()

    def gates(s, slot):
        for q in range(span // ROWS):
            part = pad_ref[s, pl.ds(q * ROWS, ROWS + TILE), :]
            total = vec_ref[0:1, :]
            for k in range(taps):
                first = TILE - (taps - 1) + k
                total = total + taps_ref[k : k + 1, :] * part[first : first + ROWS]
            conv_ref[slot, pl.ds(q * ROWS, ROWS), :] = total

        pre = dot(conv_ref[slot].astype(BF16), gates_ref[...])
        pre_ref[block(s, span), :width] = pre[:, :width] + bias_r
        pre_ref[block(s, span), width:] = pre[:, width:] + bias_i
        for q in range(span // ROWS):
            rows_q = slice(q * ROWS, (q + 1) * ROWS)
            conv = conv_ref[slot, pl.ds(q * ROWS, ROWS), :]
            recall = jax.nn.sigmoid(pre[rows_q, :width] + bias_r)
            gate = jax.nn.sigmoid(pre[rows_q, width:] + bias_i)
            log_a = (-RATE_SCALE * vec_ref[1:2, :]) * recall
            a = jnp.exp(log_a)
            spaced = pl.ds(pl.multiple_of(s * pitch + q * ROWS, TILE), ROWS)
            put(a_ref, spaced, a)
            put(b_ref, spaced, jnp.sqrt(one_minus_square(log_a, a)) * gate * conv)

    per = seqs // (groups - groups // 2)

    @pl.loop(0, groups - groups // 2)
    def _(i):
        branch(groups // 2 + i)
        for j in range(per):
            gates(i * per + j, j % 2)

    stores[0].start()
    stores[2].start()

    def at_time(ref, t):
        return get(ref, pl.ds(t, seqs, stride=pitch))

    def step(t, value):
        prod, state = value
        a = at_time(a_ref, t)
        return prod * a, a * state + at_time(b_ref, t)

    ones = jnp.ones((seqs, width), F32)
    prod, state = lax.fori_loop(0, span, step, (ones, jnp.zeros_like(ones)), unroll=8)
    mine_ref[0] = prod
    mine_ref[1] = state
    sums_ref[me] = mine_ref[...]
    copies = to_all("seq", mine_ref, sums_ref, send1, recv1)
    for copy in copies:
        copy.start()

    @pl.loop(0, rows // ROWS, unroll=2)
    def _(q):
        at = block(q, ROWS)
        act_ref[at, :] = gelu(branch_ref[at, :])

    for copy in copies:
        copy.wait()

    def carry_step(j, carry):
        both = sums_ref[j]
        return jnp.where(j < me, both[0] * carry + both[1], carry)

    start = jnp.concatenate([state_ref[s : s + 1, :] * keep[s] for s in range(seqs)], axis=0)
    carry = lax.fori_loop(0, devices - 1, carry_step, start)
    carry_ref[...] = carry

    def final(t, state):
        state = at_time(a_ref, t) * state + at_time(b_ref, t)
        put(hidden_ref, pl.ds(t, seqs, stride=span), state)
        return state

    last = lax.fori_loop(0, span, final, carry, unroll=8)
    stores[3].start()
    ends_ref[0:seqs, :] = jnp.where(me == devices - 1, last, 0.0)
    for s in range(seqs):
        ends_ref[(s + 1) * TILE : (s + 2) * TILE, :] = jnp.where(
            me == devices - 1, pad_ref[s, pl.ds(span, TILE), :], 0.0
        )

    @pl.loop(0, rows // ROWS, unroll=2)
    def _(q):
        at = block(q, ROWS)
        mixed_ref[at, :] = (get(hidden_ref, at) * act_ref[at, :]).astype(BF16)

    for copy in stores:
        copy.wait()
    for g in range(groups):
        normed_store(g).wait()


def backward_kernel(
    span,
    heads,
    block_part_in,
    own_in,
    low_in,
    w_out_in,
    branch_in,
    hidden_in,
    pre_in,
    pad_in,
    normed_in,
    mixed_in,
    rest_in,
    carry_ref,
    sums_ref,
    taps_ref,
    vec_ref,
    gates_ref,
    block_out,
    rec_out,
    grad_branch_ref,
    input_ref,
    acc_ref,
    blocks_ref,
    part,
    inbox,
    out,
    send_up,
    send_down,
    recv_up,
    recv_down,
    own_ref,
    resid_low,
    w_out_ref,
    branch_ref,
    hidden_ref,
    pre_ref,
    pad_ref,
    normed_ref,
    mixed_ref,
    a_ref,
    gd_ref,
    grad_ref,
    direct_ref,
    gpad_ref,
    heads_ref,
    low_ref,
    gates_grad,
    stage_ref,
    mine_ref,
    entries_ref,
    head_ref,
    head_in,
    load_sem,
    part_sem,
    store_sem,
    stage_sem,
    send1,
    recv1,
    send_t,
    recv_t,
):
    seqs, width = carry_ref.shape
    taps = taps_ref.shape[0]
    rows = seqs * span
    devices, me = lax.axis_size("seq"), lax.axis_index("seq")
    n, z = lax.axis_size("mp"), lax.axis_index("mp")
    chunks = rows // CHUNK
    size = GROUP * CHUNK
    held = part.shape[0] // size
    groups = chunks // GROUP
    sems = (send_up, send_down, recv_up, recv_down)
    local = pltpu.make_async_copy

    def part_load(g):
        slot = lax.rem(g, held)
        return local(block_part_in.at[block(g, size)], part.at[block(slot, size)], part_sem.at[slot])

    loads = [
        local(source, target, load_sem.at[i])
        for i, (source, target) in enumerate(
            (
                (own_in, own_ref),
                (low_in, resid_low),
                (w_out_in, w_out_ref),
                (pre_in, pre_ref),
                (branch_in, branch_ref),
                (hidden_in, hidden_ref),
                (pad_in, pad_ref),
                (mixed_in, mixed_ref),
                (normed_in, normed_ref),
            )
        )
    ]
    part_load(0).start()
    for copy in loads[:6]:
        copy.start(priority=1)
    for g in range(1, held):
        part_load(g).start()
    for copy in loads[6:]:
        copy.start(priority=1)
    acc_ref[...] = jnp.zeros_like(acc_ref)
    enter_all(("seq", "mp"))

    pitch = a_ref.shape[1] // seqs

    def spaced(s, q):
        return pl.ds(pl.multiple_of(s * pitch + q * ROWS, TILE), ROWS)

    def decay(at):
        recall = jax.nn.sigmoid(pre_ref[at, :width])
        log_a = (-RATE_SCALE * vec_ref[1:2, :]) * recall
        return recall, log_a, jnp.exp(log_a)

    def piece_direct(s):
        @pl.when(s == 0)
        def _():
            for copy in loads[1:6]:
                copy.wait()

        grad_ref[...] = matmul_back(resid_low[block(s, span), :], w_out_ref[...])

        @pl.loop(0, span // ROWS)
        def _(q):
            at = block(s * (span // ROWS) + q, ROWS)
            put(a_ref, spaced(s, q), decay(at)[2])
            act, slope = gelu_both(branch_ref[at, :])
            grad = grad_ref[block(q, ROWS), :]
            put(gd_ref, spaced(s, q), grad * act)
            grad_branch_ref[at, :] = (grad * get(hidden_ref, at) * slope).astype(BF16)

    def at_time(ref, t):
        return get(ref, pl.ds(t, seqs, stride=pitch))

    zero = jnp.zeros((seqs, width), F32)
    entry_copies = to_all("seq", mine_ref, entries_ref, send1, recv1)

    def piece_entry(_):
        def step(k, through):
            t = span - 1 - k
            return at_time(a_ref, t) * (at_time(gd_ref, t) + through)

        mine_ref[...] = lax.fori_loop(0, span, step, zero, unroll=8)
        entries_ref[me] = mine_ref[...]
        for copy in entry_copies:
            copy.start()

    def piece_state(_):
        for copy in entry_copies:
            copy.wait()

        def back_step(k, through):
            j = devices - 1 - k
            return jnp.where(j > me, entries_ref[j] + sums_ref[j, 0] * through, through)

        incoming = lax.fori_loop(0, devices - 1, back_step, zero)

        def final(k, through):
            t = span - 1 - k
            grad = at_time(gd_ref, t) + through
            put(gd_ref, pl.ds(t, seqs, stride=pitch), grad)
            return at_time(a_ref, t) * grad

        lax.fori_loop(0, span, final, incoming, unroll=8)

    def add(k, value):
        acc_ref[k] += fold(value)

    parts = 2

    def piece_gates(i):
        s = i // parts
        quarters = span // ROWS // parts

        @pl.when(i == 0)
        def _():
            loads[6].wait()

        @pl.loop(lax.rem(i, parts) * quarters, (lax.rem(i, parts) + 1) * quarters)
        def _(q):
            at = block(s * (span // ROWS) + q, ROWS)
            part_rows = pad_ref[s, pl.ds(pl.multiple_of(q * ROWS, ROWS), ROWS + TILE), :]
            conv = vec_ref[0:1, :]
            for k in range(taps):
                first = TILE - (taps - 1) + k
                conv = conv + taps_ref[k : k + 1, :] * part_rows[first : first + ROWS]
            heads_ref[at, :] = conv.astype(BF16)
            recall, log_a, a = decay(at)
            gate = jax.nn.sigmoid(pre_ref[at, width:])
            square = one_minus_square(log_a, a)
            inverse = lax.rsqrt(square)
            root = jnp.sqrt(square)
            grad = get(gd_ref, spaced(s, q))
            hidden = get(hidden_ref, at)
            before_at = pl.multiple_of(jnp.maximum(s * span + q * ROWS - TILE, 0), TILE)
            earlier = get(hidden_ref, pl.ds(before_at, TILE))
            first_row = jnp.where(q == 0, carry_ref[pl.ds(s, 1), :], earlier[TILE - 1 :])
            place = lax.broadcasted_iota(jnp.int32, (ROWS, width), 0)
            prev = jnp.where(place == 0, first_row, pltpu.roll(hidden, 1, 0))
            grad_log = grad * a * (prev - gate * conv * a * inverse)
            through = grad_log * recall
            pre_r = through * (1.0 - recall) * (-RATE_SCALE * vec_ref[1:2, :])
            direct = grad * root * gate
            pre_i = direct * conv * (1.0 - gate)
            low_ref[at, :width] = pre_r.astype(BF16)
            low_ref[at, width:] = pre_i.astype(BF16)
            direct_ref[block(q, ROWS), :] = direct
            add(0, through)
            add(1, pre_r)
            add(2, pre_i)

        @pl.when(lax.rem(i, parts) == parts - 1)
        def _():
            whole = direct_ref[...] + matmul_back(low_ref[block(s, span), :], gates_ref[...])
            gpad_ref[s, pl.ds(0, span), :] = whole
            head_ref[s] = whole[:TILE]

    head_copy = to_one("seq", -1, head_ref, head_in, send_t.at[0], recv_t.at[0])

    def piece_head(_):
        head_copy.start()

    def piece_taps(i):
        for j in range(2):
            taps_of(2 * i + j)

    def taps_of(s):
        @pl.loop(0, span // ROWS)
        def _(q):
            at = pl.multiple_of(q * ROWS, ROWS)
            part_rows = pad_ref[s, pl.ds(at, ROWS + TILE), :]
            grad = gpad_ref[s, pl.ds(at, ROWS), :]
            add(3, grad)
            for k in range(taps):
                first = TILE - (taps - 1) + k
                add(4 + k, grad * part_rows[first : first + ROWS])

    def piece_tail(_):
        head_copy.wait()
        for s in range(seqs):
            gpad_ref[s, pl.ds(span, TILE), :] = jnp.where(me == devices - 1, 0.0, head_in[s])

    def piece_input(i):
        for j in range(2):
            input_of(2 * i + j)

    def input_of(s):
        @pl.loop(0, span // ROWS)
        def _(q):
            part_rows = gpad_ref[s, pl.ds(pl.multiple_of(q * ROWS, ROWS), ROWS + TILE), :]
            total = taps_ref[taps - 1 : taps, :] * part_rows[0:ROWS]
            for k in range(taps - 1):
                first = taps - 1 - k
                total = total + taps_ref[k : k + 1, :] * part_rows[first : first + ROWS]
            input_ref[block(s * (span // ROWS) + q, ROWS), :] = total.astype(BF16)

    def contract(left, right):
        return lax.dot_general(left, right, CONTRACT_ROWS, preferred_element_type=F32)

    head = blocks_ref.shape[0]

    def piece_gates_grad(i):
        @pl.when(i == 0)
        def _():
            gates_grad[...] = contract(heads_ref[...], low_ref[:, :width])

        @pl.when(i == 1)
        def _():
            gates_grad[...] = contract(heads_ref[...], low_ref[:, width:])

        place = lax.broadcasted_iota(jnp.int32, (head, width), 1)
        line = jnp.zeros((head, width), F32)
        for h in range(heads):
            row = gates_grad[h * head : (h + 1) * head, :]
            inside = jnp.logical_and(place >= h * head, place < (h + 1) * head)
            line = jnp.where(inside, row, line)

        for j in range(2):

            @pl.when(i == j)
            def _():
                blocks_ref[:, j * width : (j + 1) * width] = line

    tall = resid_low.shape[1] // WEIGHT_STEPS

    def stage_store(i):
        at = block(lax.rem(i, WEIGHT_STEPS), tall)
        slot = lax.rem(i, 2)
        return local(
            stage_ref.at[slot],
            rec_out.at[i // WEIGHT_STEPS, at, pl.ds(0, width)],
            stage_sem.at[slot],
        )

    def piece_weights(i):
        @pl.when(i == 0)
        def _():
            loads[7].wait()
            loads[8].wait()

        @pl.loop(2 * i, 2 * i + 2)
        def _(j):
            weight_of(j)

    def weight_of(i):
        @pl.when(i >= 2)
        def _():
            stage_store(i - 2).wait()

        at = block(lax.rem(i, WEIGHT_STEPS), tall)
        slot = lax.rem(i, 2)
        for which, (left, right) in enumerate(
            ((resid_low, mixed_ref), (normed_ref, grad_branch_ref), (normed_ref, input_ref))
        ):
            @pl.when(i // WEIGHT_STEPS == which)
            def _():
                stage_ref[slot] = contract(left[:, at], right[...])

        stage_store(i).start(priority=1)

    weights = 3 * WEIGHT_STEPS
    plan = []
    begin = 3
    for work, times, gap in (
        (piece_direct, seqs, 0),
        (piece_entry, 1, 1),
        (piece_state, 1, 0),
        (piece_gates, parts * seqs, 0),
        (piece_head, 1, 0),
        (piece_taps, seqs // 2, 0),
        (piece_tail, 1, 0),
        (piece_input, seqs // 2, 0),
        (piece_gates_grad, 2, 0),
        (piece_weights, weights // 2, 0),
    ):
        plan.append((work, begin, times))
        begin += times + gap

    def run(step):
        for work, first, times in plan:
            @pl.when(jnp.logical_and(step >= first, step < first + times))
            def _():
                work(step - first)

    def before(k):
        @pl.when(k == SKEW * (n // 2))
        def _():
            loads[0].wait()

        @pl.when(jnp.logical_and(lax.rem(k, GROUP) == 0, k < chunks))
        def _():
            part_load(k // GROUP).wait()

        g = (k - out.shape[0]) // GROUP - 1 + held

        @pl.when(
            jnp.logical_and(
                jnp.logical_and(k >= out.shape[0] + GROUP, lax.rem(k - out.shape[0], GROUP) == 0),
                g < groups,
            )
        )
        def _():
            part_load(g).start(priority=1)

        run(k)

    def root(c, slot, total):
        out[slot] = own_ref[block(c // 2, CHUNK), :] + total

    def store(c, slot):
        return local(out.at[slot], block_out.at[block(c, CHUNK)], store_sem.at[slot])

    def arrive(c, slot):
        store(c, slot).start(priority=1)

    def leave(c, slot):
        store(c, slot).wait()

    line_sum(
        "mp", chunks, held * GROUP, part, inbox, out, sems, before, root, arrive, leave
    )

    @pl.loop(chunks + out.shape[0], max(begin, chunks + out.shape[0]))
    def _(k):
        run(k)

    stage_store(weights - 2).wait()
    stage_store(weights - 1).wait()


def backward_call(span, heads, head, *args):
    block_part = args[0]
    low, w_out, branch, hidden, pre, padded, normed, mixed, rest, carry, sums, taps = args[2:14]
    rows, model = block_part.shape
    seqs, width = carry.shape
    devices = lax.axis_size("seq")
    ring = ring_size("mp")
    held = 3 * GROUP * CHUNK
    dma = pltpu.SemaphoreType.DMA
    columns = pltpu.VMEM((width // LANES, seqs * (span + TILE), LANES), F32)
    return pl.pallas_call(
        functools.partial(backward_kernel, span, heads),
        out_shape=(
            shape((rows, model)),
            shape(rest.shape),
            shape((rows, width), BF16),
            shape((rows, width), BF16),
            shape((4 + taps.shape[0], TILE, width)),
            shape((head, 2 * width)),
        ),
        in_specs=[HBM] * 11 + [VMEM] * 5,
        input_output_aliases={10: 1},
        out_specs=(HBM,) * 2 + (VMEM,) * 4,
        scratch_shapes=line_scratch("mp", held, model)
        + [
            pltpu.VMEM((rows // 2, model), F32),
            pltpu.VMEM((rows, model), BF16),
            pltpu.VMEM((width, model), BF16),
            pltpu.VMEM((rows, width), F32),
            pltpu.VMEM(hidden.shape, F32),
            pltpu.VMEM(pre.shape, F32),
            pltpu.VMEM(padded.shape, F32),
            pltpu.VMEM((rows, model), BF16),
            pltpu.VMEM((rows, width), BF16),
            columns,
            columns,
            pltpu.VMEM((span, width), F32),
            pltpu.VMEM((span, width), F32),
            pltpu.VMEM((seqs, span + TILE, width), F32),
            pltpu.VMEM((rows, width), BF16),
            pltpu.VMEM((rows, 2 * width), BF16),
            pltpu.VMEM((width, width), F32),
            pltpu.VMEM((2, model // WEIGHT_STEPS, width), F32),
            pltpu.VMEM((seqs, width), F32),
            pltpu.VMEM((devices, seqs, width), F32),
            pltpu.VMEM((seqs, TILE, width), F32),
            pltpu.VMEM((seqs, TILE, width), F32),
            dma((9,)),
            dma((3,)),
            dma((ring,)),
            dma((2,)),
            dma((devices - 1,)),
            dma((devices - 1,)),
            dma((1,)),
            dma((1,)),
        ],
        compiler_params=params(1, 63),
        cost_estimate=cost(200),
        name="backward",
    )(*args)


def line_sum(axis, total, period, part, inbox, out, sems, before, root, arrive, leave):
    send_up, send_down, recv_up, recv_down = sems
    n, z = lax.axis_size(axis), lax.axis_index(axis)
    depth = n // 2
    ring = out.shape[0]

    def root_of(c):
        return depth - 1 + lax.rem(c, 2)

    def up(c, step, side):
        slot = lax.rem(c, ring)
        return pltpu.make_async_remote_copy(
            src_ref=part.at[block(lax.rem(c, period), CHUNK)],
            dst_ref=inbox.at[side, slot],
            send_sem=send_up.at[slot],
            recv_sem=recv_up.at[side, slot],
            device_id={axis: z + step},
            device_id_type=MESH,
        )

    def down(c, step, side):
        slot = lax.rem(c, ring)
        return pltpu.make_async_remote_copy(
            src_ref=out.at[slot],
            dst_ref=out.at[slot],
            send_sem=send_down.at[side, slot],
            recv_sem=recv_down.at[slot],
            device_id={axis: z + step},
            device_id_type=MESH,
        )

    inner = jnp.logical_and(z > 0, z < n - 1)

    @pl.loop(0, total + ring)
    def _(k):
        @pl.when(k >= ring)
        def _():
            c = k - ring
            r = root_of(c)
            step = jnp.where(z < r, 1, -1)
            side = jnp.where(z < r, 0, 1)

            @pl.when(z == r)
            def _():
                down(c, -1, 0).wait_send()
                down(c, 1, 1).wait_send()

            @pl.when(z != r)
            def _():
                up(c, step, side).wait_send()

            @pl.when(jnp.logical_and(z != r, inner))
            def _():
                down(c, -step, side).wait_send()

            leave(c, lax.rem(c, ring))

        before(k)

        for i in reversed(range(n + 1)):
            c = k - SKEW * i
            valid = jnp.logical_and(c >= 0, c < total)
            c = jnp.clip(c, 0, total - 1)
            at = block(lax.rem(c, period), CHUNK)
            slot = lax.rem(c, ring)
            r = root_of(c)
            step = jnp.where(z < r, 1, -1)
            side = jnp.where(z < r, 0, 1)
            if i > depth:
                here = jnp.logical_and(z != r, jnp.abs(z - r) == i - depth)

                @pl.when(jnp.logical_and(valid, here))
                def _():
                    down(c, -step, side).wait_recv()

                    @pl.when(inner)
                    def _():
                        down(c, -step, side).start()

                    arrive(c, slot)
            elif i == depth:

                @pl.when(jnp.logical_and(valid, z == r))
                def _():
                    up(c, 1, 0).wait_recv()
                    up(c, -1, 1).wait_recv()
                    root(c, slot, part[at, :] + inbox[0, slot] + inbox[1, slot])
                    down(c, -1, 0).start()
                    down(c, 1, 1).start()
                    arrive(c, slot)
            else:
                here = jnp.where(z < r, z, n - 1 - z) == i

                @pl.when(jnp.logical_and(valid, jnp.logical_and(z != r, here)))
                def _():
                    if i > 0:
                        up(c, step, side).wait_recv()
                        part[at, :] += inbox[side, slot]
                    up(c, step, side).start()


def ring_size(axis):
    return SKEW * lax.axis_size(axis) + 4


def line_scratch(axis, rows, model):
    dma = pltpu.SemaphoreType.DMA
    ring = ring_size(axis)
    return [
        pltpu.VMEM((rows, model), F32),
        pltpu.VMEM((2, ring, CHUNK, model), F32),
        pltpu.VMEM((ring, CHUNK, model), F32),
        dma((ring,)),
        dma((2, ring)),
        dma((2, ring)),
        dma((ring,)),
    ]


def mean_square(x):
    return lax.rsqrt(jnp.mean(x * x, axis=-1, keepdims=True) + EPS)


def nothing(*_):
    pass


def fold(value):
    total = value[0:TILE]
    for i in range(1, value.shape[0] // TILE):
        total = total + value[i * TILE : (i + 1) * TILE]
    return total


def norm_grad(value, gain, grad, acc_ref):
    q = mean_square(value)
    e = gain * grad
    acc_ref[...] += fold(grad * value * q)
    return q * e - value * (q * q * q) * jnp.mean(e * value, axis=-1, keepdims=True)


def middle_kernel(
    mixed_in,
    w_out_in,
    x_in,
    og_in,
    gain_ref,
    w_gate_in,
    w_up_in,
    w_down_in,
    normed_out,
    hidden_out,
    gate_out,
    up_out,
    glow_out,
    block_out,
    low_out,
    own_grad_out,
    weight_out,
    rest_out,
    own_ref,
    acc_ref,
    part,
    inbox,
    out,
    send_up,
    send_down,
    recv_up,
    recv_down,
    mixed,
    w_out,
    w_gate,
    w_up,
    w_down,
    normed,
    rows_ref,
    og_ref,
    glow,
    gate_val,
    up_val,
    grad_hidden,
    hidden,
    grad_gate,
    grad_up,
    block_part,
    low,
    weight_sem,
    row_sem,
    og_sem,
    act_sem,
    low_sem,
    own_sem,
    again_sem,
    stage_sem,
    rest_sem,
):
    n, z = lax.axis_size("mp"), lax.axis_index("mp")
    count = part.shape[0] // CHUNK
    size = GROUP * CHUNK
    groups = count // GROUP
    ring = out.shape[0]
    sems = (send_up, send_down, recv_up, recv_down)
    local = pltpu.make_async_copy

    loads = [
        local(source, target, weight_sem.at[i])
        for i, (source, target) in enumerate(
            (
                (mixed_in, mixed),
                (w_out_in, w_out),
                (w_gate_in, w_gate),
                (w_up_in, w_up),
                (w_down_in, w_down.at[slice(0, w_down_in.shape[0])]),
            )
        )
    ]
    for copy in loads:
        copy.start(priority=1)
    deep = w_down_in.shape[0]

    def og_load(g):
        return local(og_in.at[block(g, size)], og_ref, og_sem.at[0])

    og_load(0).start(priority=1)
    enter_all(("mp",))
    acc_ref[...] = jnp.zeros_like(acc_ref)
    loads[0].wait()
    loads[1].wait()

    def is_root(c):
        return z == n // 2 - 1 + lax.rem(c, 2)

    def row_load(source, c):
        slot = lax.rem(c, ring)
        at = block(lax.rem(c, count), CHUNK)
        return local(source.at[at], rows_ref.at[slot], row_sem.at[slot])

    acts = (
        (normed, normed_out),
        (glow, glow_out),
        (hidden, hidden_out),
        (grad_gate, gate_out),
        (grad_up, up_out),
        (block_part, block_out),
    )

    def act_store(i, g):
        source, target = acts[i]
        source = source.at[lax.rem(g, 2)] if i == 0 else source
        return local(source, target.at[block(g, size)], act_sem.at[i])

    def at_tick(k, first, work):
        g = (k - first) // GROUP

        @pl.when(
            jnp.logical_and(
                jnp.logical_and(k >= first, k < first + GROUP * groups),
                lax.rem(k - first, GROUP) == 0,
            )
        )
        def _():
            work(g)

    def project(g):
        def work(cols):
            part[block(g, size), cols] = dot(mixed[block(g, size), :], w_out[:, cols])

        work(slice(None))

    def piece_gate(g):
        @pl.when(g == 0)
        def _():
            for copy in loads[2:]:
                copy.wait()

        def work(cols):
            gate_val[:, cols] = dot(normed[lax.rem(g, 2)], w_gate[:, cols])

        work(slice(None))
        act_store(0, g).start(priority=1)

    def piece_up(g):
        def work(cols):
            up_val[:, cols] = dot(normed[lax.rem(g, 2)], w_up[:, cols])

        work(slice(None))

        @pl.when(g > 0)
        def _():
            for i in range(1, 6):
                act_store(i, g - 1).wait()

    def piece_low(g):
        og_load(g).wait()

        @pl.loop(0, size // ROWS)
        def _(q):
            glow[block(q, ROWS), :] = og_ref[block(q, ROWS), :].astype(BF16)

        @pl.when(g + 1 < groups)
        def _():
            og_load(g + 1).start(priority=1)

        act_store(1, g).start(priority=1)
        act_store(0, g).wait()

    def piece_hidden(g):
        def work(cols):
            grad_hidden[...] = matmul_back(glow[...], w_down[:deep, :])

        work(slice(None))

    def piece_act(g):
        @pl.loop(0, size // CHUNK)
        def _(q):
            at = block(q, CHUNK)
            up = up_val[at, :]
            grad = grad_hidden[at, :]
            act, slope = gelu_both(gate_val[at, :])
            hidden[at, :] = (act * up).astype(BF16)
            grad_gate[at, :] = (grad * up * slope).astype(BF16)
            grad_up[at, :] = (grad * act).astype(BF16)

        for i in range(2, 5):
            act_store(i, g).start(priority=1)

    def piece_down(g):
        def work(cols):
            block_part[:, cols] = dot(hidden[...], w_down[:deep, cols])

        work(slice(None))
        act_store(5, g).start(priority=1)

    def piece_back_gate(g):
        def work(cols):
            part[block(g, size), cols] = matmul_back(grad_gate[...], w_gate[cols, :])

        work(slice(None))

    def piece_back_up(g):
        def work(cols):
            part[block(g, size), cols] += matmul_back(grad_up[...], w_up[cols, :])

        work(slice(None))

    tokens = count * CHUNK
    half = tokens // 2
    quarter = half // 2
    again = [
        local(source, target, again_sem.at[i])
        for i, (source, target) in enumerate(
            (
                (normed_out, w_down.at[slice(0, tokens)]),
                (gate_out, w_gate.at[slice(0, tokens)]),
                (up_out, w_up.at[slice(0, tokens)]),
                (hidden_out, w_gate.at[slice(tokens, 2 * tokens)]),
                (glow_out.at[slice(0, half)], w_down.at[slice(tokens, tokens + half)]),
                (glow_out.at[slice(half, half + quarter)], normed.at[0]),
                (glow_out.at[slice(half + quarter, tokens)], normed.at[1]),
            )
        )
    ]
    tall = w_gate.shape[0] // WEIGHT_STEPS
    stages = (gate_val, up_val, grad_hidden)

    kept = weight_out.shape[2]
    before_rest = rest_out.shape[2] - (deep - kept)

    def stage_stores(which, i):
        at = block(i, tall)
        return (
            local(
                stages[which].at[:, pl.ds(0, kept)],
                weight_out.at[which, at],
                stage_sem.at[which],
            ),
            local(
                stages[which].at[:, pl.ds(kept, deep - kept)],
                rest_out.at[which, at, pl.ds(before_rest, deep - kept)],
                rest_sem.at[which],
            ),
        )

    def piece_reload():
        for i in range(1, 6):
            act_store(i, groups - 1).wait()
        for copy in again:
            copy.start(priority=1)

    def piece_ready():
        for copy in again:
            copy.wait()

    def contract(left, right):
        return lax.dot_general(left, right, CONTRACT_ROWS, preferred_element_type=F32)

    def piece_weight(step):
        i = step // 3
        at = block(i, tall)
        for which in range(3):

            @pl.when(lax.rem(step, 3) == which)
            def _():
                @pl.when(i > 0)
                def _():
                    for copy in stage_stores(which, i - 1):
                        copy.wait()

                stage = stages[which]

                def work(cols):
                    if which == 0:
                        stage[:, cols] = contract(w_down[:tokens, at], w_gate[:tokens, cols])
                    elif which == 1:
                        stage[:, cols] = contract(w_down[:tokens, at], w_up[:tokens, cols])
                    else:
                        middle = tokens + half + quarter
                        stage[:, cols] = (
                            contract(
                                w_down[tokens : tokens + half, at],
                                w_gate[tokens : tokens + half, cols],
                            )
                            + contract(normed[0, :, at], w_gate[tokens + half : middle, cols])
                            + contract(normed[1, :, at], w_gate[middle : 2 * tokens, cols])
                        )

                work(slice(None))
                for copy in stage_stores(which, i):
                    copy.start(priority=1)

    first = GROUP + SKEW * n
    spare = GROUP * groups + ring + 3
    first_weight = spare + 3
    weights = 3 * WEIGHT_STEPS

    def before(k):
        @pl.when(k == spare)
        def _():
            piece_reload()

        @pl.when(k == first_weight - 1)
        def _():
            piece_ready()

        @pl.when(jnp.logical_and(k >= first_weight, k < first_weight + weights))
        def _():
            piece_weight(k - first_weight)

        @pl.when(jnp.logical_and(k < count, is_root(k)))
        def _():
            row_load(x_in, k).start(priority=1)

        @pl.when(
            jnp.logical_and(jnp.logical_and(k >= count, k < 2 * count), is_root(k))
        )
        def _():
            row_load(og_in, k).start(priority=1)

        at_tick(k, 0, project)
        at_tick(k, first, piece_gate)
        at_tick(k, first + 1, piece_up)
        at_tick(k, first + 2, piece_low)
        at_tick(k, first + 3, piece_hidden)
        at_tick(k, first + 4, piece_act)
        at_tick(k, first + 6, piece_down)
        at_tick(k, GROUP + ring, piece_back_gate)
        at_tick(k, GROUP + ring + 2, piece_back_up)

    def root(c, slot, total):
        j = lax.rem(c, count)
        mine = block(j // 2, CHUNK)
        row_load(x_in, c).wait()

        @pl.when(c < count)
        def _():
            value = rows_ref[slot] + total
            own_ref[mine, :] = value
            out[slot] = (value * mean_square(value) * gain_ref[...]).astype(BF16).astype(F32)

        @pl.when(c >= count)
        def _():
            back = norm_grad(own_ref[mine, :], gain_ref[...], total, acc_ref)
            out[slot] = rows_ref[slot] + back

    def low_store(c, slot):
        at = block(lax.rem(c, count), CHUNK)
        return local(low.at[slot], low_out.at[at], low_sem.at[slot])

    def own_store(c, slot):
        at = block(lax.rem(c, count) // 2, CHUNK)
        return local(out.at[slot], own_grad_out.at[at], own_sem.at[slot])

    def arrive(c, slot):
        @pl.when(c < count)
        def _():
            normed[lax.rem(c // GROUP, 2), block(lax.rem(c, GROUP), CHUNK), :] = out[slot].astype(BF16)

        @pl.when(c >= count)
        def _():
            low[slot] = out[slot].astype(BF16)
            low_store(c, slot).start(priority=1)

            @pl.when(is_root(c))
            def _():
                own_store(c, slot).start(priority=1)

    def leave(c, slot):
        @pl.when(c >= count)
        def _():
            low_store(c, slot).wait()

            @pl.when(is_root(c))
            def _():
                own_store(c, slot).wait()

    line_sum("mp", 2 * count, count, part, inbox, out, sems, before, root, arrive, leave)

    for which in range(3):
        for copy in stage_stores(which, WEIGHT_STEPS - 1):
            copy.wait()


def middle_call(*args):
    mixed, w_out, x, og, gain, w_gate, w_up, w_down = args
    rows, model = x.shape
    width, hidden = mixed.shape[1], w_gate.shape[1]
    size = GROUP * CHUNK
    dma = pltpu.SemaphoreType.DMA
    ring = ring_size("mp")
    act = shape((rows, hidden), BF16)
    tall = shape((rows, model), BF16)
    return pl.pallas_call(
        middle_kernel,
        out_shape=(
            tall,
            act,
            act,
            act,
            tall,
            shape((rows, model)),
            tall,
            shape((rows // 2, model)),
            shape((3, model, hidden - hidden // LATER)),
            shape((3, model, width + hidden // LATER)),
            shape((rows // 2, model)),
            shape((TILE, model)),
        ),
        in_specs=[HBM] * 4 + [VMEM] + [HBM] * 3,
        out_specs=(HBM,) * 10 + (VMEM,) * 2,
        scratch_shapes=line_scratch("mp", rows, model)
        + [
            pltpu.VMEM((rows, width), BF16),
            pltpu.VMEM((width, model), BF16),
            pltpu.VMEM((model, hidden), BF16),
            pltpu.VMEM((model, hidden), BF16),
            pltpu.VMEM((max(hidden, rows * 3 // 2), model), BF16),
            pltpu.VMEM((2, size, model), BF16),
            pltpu.VMEM((ring, CHUNK, model), F32),
            pltpu.VMEM((size, model), F32),
            pltpu.VMEM((size, model), BF16),
            pltpu.VMEM((size, hidden), F32),
            pltpu.VMEM((size, hidden), F32),
            pltpu.VMEM((size, hidden), F32),
            pltpu.VMEM((size, hidden), BF16),
            pltpu.VMEM((size, hidden), BF16),
            pltpu.VMEM((size, hidden), BF16),
            pltpu.VMEM((size, model), F32),
            pltpu.VMEM((ring, CHUNK, model), BF16),
            dma((5,)),
            dma((ring,)),
            dma((1,)),
            dma((6,)),
            dma((ring,)),
            dma((ring,)),
            dma((7,)),
            dma((3,)),
            dma((3,)),
        ],
        compiler_params=params(2, 63),
        cost_estimate=cost(400),
        name="middle",
    )(*args)


def last_kernel(
    own_grad_in,
    x_in,
    grad_branch_in,
    input_in,
    w_branch_in,
    w_input_in,
    gain_ref,
    other_acc,
    sums_in,
    ends_in,
    blocks_in,
    grad_out,
    norm_ref,
    small_out,
    part,
    inbox,
    out,
    send_up,
    send_down,
    recv_up,
    recv_down,
    own_grad_ref,
    x_ref,
    grad_branch,
    input_low,
    w_branch,
    w_input,
    load_sem,
    store_sem,
    acc_ref,
    mine_ref,
    seq_in,
    mp_in,
    send_s,
    recv_s,
    send_m,
    recv_m,
    small,
    small_in,
    send_v,
    recv_v,
):
    count = part.shape[0] // CHUNK
    size = GROUP * CHUNK
    sems = (send_up, send_down, recv_up, recv_down)
    local = pltpu.make_async_copy

    loads = [
        local(source, target, load_sem.at[i])
        for i, (source, target) in enumerate(
            (
                (grad_branch_in, grad_branch),
                (w_branch_in, w_branch),
                (input_in, input_low),
                (w_input_in, w_input),
                (own_grad_in, own_grad_ref),
                (x_in, x_ref),
            )
        )
    ]
    for copy in loads:
        copy.start(priority=1)
    acc_ref[...] = jnp.zeros_like(acc_ref)
    mine_ref[...] = jnp.zeros_like(mine_ref)
    enter_all(("seq", "mp"))
    for copy in loads[:4]:
        copy.wait()

    kinds = sums_in.shape[0]
    me = lax.axis_index("seq")
    width = sums_in.shape[2]
    height = kinds + ends_in.shape[0]
    head = blocks_in.shape[0]
    for i in range(kinds):
        small[0, i : i + 1, :] = jnp.sum(sums_in[i], axis=0, keepdims=True)
    small[0, kinds:height, :] = ends_in[...]
    small[0, height : height + head, :] = blocks_in[:, :width]
    small[0, height + head :, :] = blocks_in[:, width:]
    levels = small_in.shape[0]

    def exchange(level):
        bit = 1 << level
        partner = me + bit - 2 * bit * lax.rem(me // bit, 2)
        return pltpu.make_async_remote_copy(
            src_ref=small.at[level],
            dst_ref=small_in.at[level],
            send_sem=send_v.at[level],
            recv_sem=recv_v.at[level],
            device_id={"seq": partner},
            device_id_type=MESH,
        )

    spacing = (count - 4) // (levels + 1)
    seq_copies = to_all("seq", mine_ref.at[0], seq_in, send_s, recv_s)
    mp_copies = to_all("mp", mine_ref.at[1], mp_in, send_m, recv_m)
    settled = count + SKEW * (lax.axis_size("mp") // 2)

    def before(k):
        for level in range(levels + 1):

            @pl.when(k == 3 + level * spacing)
            def _():
                if level > 0:
                    exchange(level - 1).wait()
                    total = small[level - 1] + small_in[level - 1]
                    if level < levels:
                        small[level] = total
                    else:
                        small_out[...] = total
                if level < levels:
                    exchange(level).start()

        @pl.when(k == settled)
        def _():
            mine_ref[0, 0:1, :] = jnp.sum(acc_ref[...], axis=0, keepdims=True)
            mine_ref[0, 1:2, :] = jnp.sum(other_acc[...], axis=0, keepdims=True)
            seq_in[me] = mine_ref[0]
            for copy in seq_copies:
                copy.start()

        @pl.when(k == settled + 2)
        def _():
            for copy in seq_copies:
                copy.wait()
            mine_ref[1] = jnp.sum(seq_in[...], axis=0)
            mp_in[lax.axis_index("mp")] = mine_ref[1]
            for copy in mp_copies:
                copy.start()

        @pl.when(jnp.logical_and(lax.rem(k, 4) == 0, k // 4 < count // GROUP))
        def _():
            at = block(k // 4, size)

            def work(cols):
                part[at, cols] = matmul_back(grad_branch[at, :], w_branch[cols, :]) + matmul_back(
                    input_low[at, :], w_input[cols, :]
                )

            work(slice(None))

        @pl.when(k == SKEW * (lax.axis_size("mp") // 2))
        def _():
            for copy in loads[4:]:
                copy.wait()

    def root(c, slot, total):
        back = norm_grad(x_ref[block(c, CHUNK), :], gain_ref[...], total, acc_ref)
        out[slot] = own_grad_ref[block(c // 2, CHUNK), :] + back

    def store(c, slot):
        return local(out.at[slot], grad_out.at[block(c, CHUNK)], store_sem.at[slot])

    def arrive(c, slot):
        store(c, slot).start(priority=1)

    def leave(c, slot):
        store(c, slot).wait()

    line_sum("mp", count, count, part, inbox, out, sems, before, root, arrive, leave)

    for copy in mp_copies:
        copy.wait()
    norm_ref[...] = jnp.sum(mp_in[...], axis=0)


def enter_all(axes):
    barrier = pltpu.get_barrier_semaphore()
    count = 0
    for axis in axes:
        size, me = lax.axis_size(axis), lax.axis_index(axis)
        for d in range(1, size):
            pl.semaphore_signal(
                barrier, 1, device_id={axis: lax.rem(me + d, size)}, device_id_type=MESH
            )
        count += size - 1
    pl.semaphore_wait(barrier, count)


def cost(micros):
    return pl.CostEstimate(flops=int(micros * 1e9), bytes_accessed=1 << 20, transcendentals=0)


def nseq_levels():
    return (lax.axis_size("seq") - 1).bit_length()


def last_call(*args):
    x, grad_branch = args[1:3]
    rows, model = x.shape
    width = grad_branch.shape[1]
    lines = args[8].shape[0] + args[9].shape[0] + 2 * args[10].shape[0]
    levels = nseq_levels()
    dma = pltpu.SemaphoreType.DMA
    nseq, nmp = lax.axis_size("seq"), lax.axis_size("mp")
    return pl.pallas_call(
        last_kernel,
        out_shape=(shape((rows, model)), shape((TILE, model)), shape((lines, width))),
        in_specs=[HBM] * 6 + [VMEM] * 5,
        out_specs=(HBM,) + (VMEM,) * 2,
        scratch_shapes=line_scratch("mp", rows, model)
        + [
            pltpu.VMEM((rows // 2, model), F32),
            pltpu.VMEM((rows, model), F32),
            pltpu.VMEM((rows, width), BF16),
            pltpu.VMEM((rows, width), BF16),
            pltpu.VMEM((model, width), BF16),
            pltpu.VMEM((model, width), BF16),
            dma((6,)),
            dma((ring_size("mp"),)),
            pltpu.VMEM((TILE, model), F32),
            pltpu.VMEM((2, TILE, model), F32),
            pltpu.VMEM((nseq, TILE, model), F32),
            pltpu.VMEM((nmp, TILE, model), F32),
            dma((nseq - 1,)),
            dma((nseq - 1,)),
            dma((nmp - 1,)),
            dma((nmp - 1,)),
            pltpu.VMEM((levels, lines, width), F32),
            pltpu.VMEM((levels, lines, width), F32),
            dma((levels,)),
            dma((levels,)),
        ],
        compiler_params=params(4, 62),
        cost_estimate=cost(200),
        name="last_sums",
    )(*args)


def finish_kernel(
    heads,
    grad_in,
    mlp_in,
    rec_in,
    small_hbm,
    norm_hbm,
    decay_hbm,
    grad_out,
    w_gate_out,
    w_up_out,
    w_branch_out,
    w_input_out,
    w_down_out,
    w_out_out,
    gate_r_out,
    gate_i_out,
    taps_out,
    conv_bias_out,
    bias_r_out,
    bias_i_out,
    decay_out,
    norm_in_out,
    norm_mlp_out,
    state_out,
    conv_out,
    tall,
    mlp,
    rec,
    small_in,
    norm_in,
    raw_ref,
    load_sem,
    store_sem,
    extra_sem,
):
    local = pltpu.make_async_copy
    width = small_in.shape[1]
    kept = mlp.shape[2]
    late = rec.shape[2] - width
    size = grad_in.shape[0] // COPIES
    extra = [
        local(source, target, extra_sem.at[i])
        for i, (source, target) in enumerate(
            ((small_hbm, small_in), (norm_hbm, norm_in), (decay_hbm, raw_ref))
        )
    ]
    for copy in extra:
        copy.start()
    jobs = [(mlp_in, mlp, None), (rec_in, rec, None)]
    for i in range(COPIES):
        at = slice(i * size, (i + 1) * size)
        jobs.append((grad_in.at[at], tall.at[at], grad_out.at[at]))
    loads = [local(source, held, load_sem.at[i]) for i, (source, held, _) in enumerate(jobs)]
    stores = [
        local(held, target, store_sem.at[i])
        for i, (held, target) in enumerate(
            [(held, target) for _, held, target in jobs[2:]]
            + [
                (mlp.at[0], w_gate_out.at[:, pl.ds(0, kept)]),
                (mlp.at[1], w_up_out.at[:, pl.ds(0, kept)]),
                (rec.at[0, :, pl.ds(width, late)], w_gate_out.at[:, pl.ds(kept, late)]),
                (rec.at[1, :, pl.ds(width, late)], w_up_out.at[:, pl.ds(kept, late)]),
                (rec.at[1, :, pl.ds(0, width)], w_branch_out),
                (rec.at[2, :, pl.ds(0, width)], w_input_out),
            ]
        )
    ]
    for copy in loads:
        copy.start()
    for copy in extra:
        copy.wait()
    taps, seqs, edge = taps_out.shape[0], state_out.shape[0], conv_out.shape[0]
    head = gate_r_out.shape[1]
    decay = small_in[0:1, :].reshape(width) * (RATE_SCALE * jax.nn.sigmoid(-raw_ref[...]))
    decay_out[...] = decay
    bias_r_out[...] = small_in[1:2, :].reshape(width)
    bias_i_out[...] = small_in[2:3, :].reshape(width)
    conv_bias_out[...] = small_in[3:4, :].reshape(width)
    taps_out[...] = small_in[4 : 4 + taps, :]
    begin = 4 + taps
    state_out[...] = small_in[begin : begin + seqs, :]
    for s in range(seqs):
        end = begin + seqs + (s + 1) * TILE
        for k in range(edge):
            conv_out[k, s : s + 1, :] = small_in[end - edge + k : end - edge + k + 1, :]
    begin += seqs + seqs * TILE
    for i, target in enumerate((gate_r_out, gate_i_out)):
        line = small_in[begin + i * head : begin + (i + 1) * head, :]
        for h in range(heads):
            turned = line if h == 0 else pltpu.roll(line, width - h * head, 1)
            target[h] = turned[:, :head]
    norm_in_out[...] = norm_in[0:1, :].reshape(norm_in.shape[1])
    norm_mlp_out[...] = norm_in[1:2, :].reshape(norm_in.shape[1])
    loads[0].wait()
    loads[1].wait()
    for copy in stores[COPIES:]:
        copy.start()
    w_down_out[:kept, :] = mlp[2].T
    w_down_out[kept:, :] = rec[2, :, width:].T
    w_out_out[...] = rec[0, :, :width].T
    for i in range(COPIES):
        loads[2 + i].wait()
        stores[i].start()
    for copy in stores:
        copy.wait()


def finish_call(seqs, heads, head, edge, *args):
    stream_grad, mlp_grads, rec_grads, small, norms, decay = args
    rows, model = stream_grad.shape
    own, kept = mlp_grads.shape[1:]
    width = small.shape[1]
    hidden = kept + rec_grads.shape[2] - width
    taps = edge + 1
    line = shape((width,))
    tall = shape((rows, model))
    return pl.pallas_call(
        functools.partial(finish_kernel, heads),
        out_shape=(
            tall,
            shape((own, hidden)),
            shape((own, hidden)),
            shape((own, width)),
            shape((own, width)),
            shape((hidden, own)),
            shape((width, own)),
            shape((heads, head, head)),
            shape((heads, head, head)),
            shape((taps, width)),
            line,
            line,
            line,
            line,
            shape((model,)),
            shape((model,)),
            shape((seqs, width)),
            shape((edge, seqs, width)),
        ),
        in_specs=[HBM] * 3 + [PINNED] * 3,
        out_specs=(HBM,) * 5 + (VMEM,) * 13,
        scratch_shapes=[
            pltpu.VMEM((rows, model), F32),
            pltpu.VMEM(mlp_grads.shape, F32),
            pltpu.VMEM(rec_grads.shape, F32),
            pltpu.VMEM(small.shape, F32),
            pltpu.VMEM(norms.shape, F32),
            pltpu.VMEM(decay.shape, F32),
            pltpu.SemaphoreType.DMA((2 + COPIES,)),
            pltpu.SemaphoreType.DMA((6 + COPIES,)),
            pltpu.SemaphoreType.DMA((3,)),
        ],
        compiler_params=pltpu.CompilerParams(vmem_limit_bytes=63 << 20),
        cost_estimate=cost(15),
        name="finish",
    )(*args)


def copy_kernel(source, target, held, load_sem, store_sem):
    size = source.shape[0] // COPIES
    pieces = [slice(i * size, (i + 1) * size) for i in range(COPIES)]
    local = pltpu.make_async_copy
    loads = [local(source.at[p], held.at[p], load_sem.at[i]) for i, p in enumerate(pieces)]
    stores = [local(held.at[p], target.at[p], store_sem.at[i]) for i, p in enumerate(pieces)]
    for copy in loads:
        copy.start()
    for load, store in zip(loads, stores):
        load.wait()
        store.start()
    for copy in stores:
        copy.wait()


def copy_call(array):
    return pl.pallas_call(
        copy_kernel,
        out_shape=shape(array.shape),
        in_specs=[HBM],
        out_specs=HBM,
        scratch_shapes=[
            pltpu.VMEM(array.shape, F32),
            pltpu.SemaphoreType.DMA((COPIES,)),
            pltpu.SemaphoreType.DMA((COPIES,)),
        ],
        compiler_params=pltpu.CompilerParams(vmem_limit_bytes=63 << 20),
        cost_estimate=cost(6),
        name="copy_out",
    )(array)


def params(collective, megabytes=60):
    return pltpu.CompilerParams(
        collective_id=collective, has_side_effects=True, vmem_limit_bytes=megabytes << 20
    )


def shape(dims, dtype=F32):
    return jax.ShapeDtypeStruct(dims, dtype)


def recurrence_forward(span, *args):
    x, w_input = args[:2]
    rows, model = x.shape
    seqs, width = rows // span, w_input.shape[1]
    devices = lax.axis_size("seq")
    dma = pltpu.SemaphoreType.DMA
    groups = seqs // 2
    columns = (width // LANES, rows, LANES)
    spaced = (width // LANES, seqs * (span + TILE), LANES)
    padded = (seqs, span + TILE, width)
    return pl.pallas_call(
        functools.partial(forward_kernel, span),
        out_shape=(
            shape((rows, model), BF16),
            shape((rows, width)),
            shape(padded),
            shape((rows, 2 * width)),
            shape(columns),
            shape((rows, width), BF16),
            shape((seqs, width)),
            shape((devices, 2, seqs, width)),
            shape((width, 2 * width), BF16),
            shape((TILE, width)),
            shape(((seqs + 1) * TILE, width)),
        ),
        in_specs=[HBM] * 3 + [VMEM] * 8 + [pl.BlockSpec(memory_space=pltpu.SMEM)] + [VMEM] * 2,
        out_specs=(HBM,) * 5 + (VMEM,) * 6,
        scratch_shapes=[
            pltpu.VMEM((rows, model), F32),
            pltpu.VMEM((model, width), BF16),
            pltpu.VMEM((model, width), BF16),
            pltpu.VMEM((rows, model), BF16),
            pltpu.VMEM((rows, width), F32),
            pltpu.VMEM(padded, F32),
            pltpu.VMEM((rows, 2 * width), F32),
            pltpu.VMEM(columns, F32),
            pltpu.VMEM((rows, width), F32),
            pltpu.VMEM(spaced, F32),
            pltpu.VMEM(spaced, F32),
            pltpu.VMEM((2, span, width), F32),
            pltpu.VMEM((seqs, TILE, width), F32),
            pltpu.VMEM((seqs, TILE, width), F32),
            pltpu.VMEM((2, seqs, width), F32),
            dma((groups + 2,)),
            dma((4,)),
            dma((groups,)),
            dma((devices - 1,)),
            dma((devices - 1,)),
            dma((1,)),
            dma((1,)),
        ],
        compiler_params=params(0),
        cost_estimate=cost(50),
        name="recurrence_forward",
    )(*args)


def widen(array, width):
    short = width - array.shape[-1]
    if short == 0:
        return array
    return jnp.pad(array, [(0, 0)] * (array.ndim - 1) + [(0, short)])


def per_device(
    stream,
    norm_in,
    w_branch,
    w_input,
    conv_kernel,
    conv_bias,
    gate_r,
    bias_r,
    gate_i,
    bias_i,
    decay_param,
    w_out,
    norm_mlp,
    w_gate,
    w_up,
    w_down,
    state_init,
    conv_init,
    fresh_rows,
    out_grad,
):
    seqs, span, model = stream.shape
    channels = w_branch.shape[1]
    mlp_dev = w_gate.shape[1]
    heads, head_width = gate_r.shape[:2]
    taps = conv_kernel.shape[0]
    edge = taps - 1
    rows = seqs * span
    devices = lax.axis_size("seq")
    position = lax.axis_index("seq")
    width = -(-channels // 128) * 128

    flat_in = stream.reshape(rows, model)
    flat_grad = out_grad.reshape(rows, model)
    w_branch_p = widen(w_branch, width)
    w_input_p = widen(w_input, width)
    w_out_p = jnp.pad(w_out, ((0, width - channels), (0, 0))) if width > channels else w_out
    taps_p = widen(conv_kernel, width)
    def line(value):
        return widen(value, width)

    (
        normed,
        branch,
        padded,
        pre,
        hidden,
        mixed,
        carry,
        sums,
        gates,
        rates,
        ends,
    ) = recurrence_forward(
        span,
        flat_in,
        w_input_p,
        w_branch_p,
        norm_in[None],
        taps_p,
        line(conv_bias),
        line(decay_param),
        line(bias_r),
        line(bias_i),
        gate_r,
        gate_i,
        fresh_rows,
        widen(state_init, width),
        widen(jnp.swapaxes(conv_init, 0, 1), width),
    )
    made = middle_call(mixed, w_out_p, flat_in, flat_grad, norm_mlp[None], w_gate, w_up, w_down)
    block_part, resid_low, own_grad, mlp_grads, rest, own, norm_mlp_acc = made[5:]
    mlp_grads = lax.psum_scatter(mlp_grads, "seq", scatter_dimension=1, tiled=True)
    block_out, rec_grads, grad_branch, input_low, acc, blocks = backward_call(
        span,
        heads,
        head_width,
        block_part,
        own,
        resid_low,
        w_out_p,
        branch,
        hidden,
        pre,
        padded,
        normed,
        mixed,
        rest,
        carry,
        sums,
        taps_p,
        rates,
        gates,
    )

    block_out = copy_call(block_out)
    rec_grads, grad_branch, mlp_grads, block_out = lax.optimization_barrier(
        (rec_grads, grad_branch, mlp_grads, block_out)
    )
    rec_grads = lax.psum_scatter(rec_grads, "seq", scatter_dimension=1, tiled=True)

    stream_grad, norm_grads, small = last_call(
        own_grad,
        flat_in,
        grad_branch,
        input_low,
        w_branch_p,
        w_input_p,
        norm_in[None],
        norm_mlp_acc,
        acc,
        ends,
        blocks,
    )
    (
        stream_grad,
        w_gate_grad,
        w_up_grad,
        w_branch_grad,
        w_input_grad,
        w_down_grad,
        w_out_grad,
        gate_r_grad,
        gate_i_grad,
        taps_grad,
        conv_bias_grad,
        bias_r_grad,
        bias_i_grad,
        decay_grad,
        norm_in_grad,
        norm_mlp_grad,
        final_state,
        final_conv,
    ) = finish_call(
        seqs,
        heads,
        head_width,
        edge,
        stream_grad,
        mlp_grads,
        rec_grads,
        small,
        norm_grads,
        line(decay_param),
    )
    return (
        block_out.reshape(stream.shape),
        stream_grad.reshape(stream.shape),
        norm_in_grad,
        w_branch_grad[:, :channels],
        w_input_grad[:, :channels],
        taps_grad[:, :channels],
        conv_bias_grad[:channels],
        gate_r_grad,
        bias_r_grad[:channels],
        gate_i_grad,
        bias_i_grad[:channels],
        decay_grad[:channels],
        w_out_grad[:channels],
        norm_mlp_grad,
        w_gate_grad,
        w_up_grad,
        w_down_grad,
        final_state[:, :channels],
        jnp.swapaxes(final_conv, 0, 1)[:, :, :channels],
    )


def solution(mesh):
    seq_rows = P(None, "seq", None)
    columns = P(None, "mp")
    channel = P("mp")
    return jax.shard_map(
        per_device,
        mesh=mesh,
        in_specs=(
            seq_rows,
            P(),
            columns,
            columns,
            columns,
            channel,
            P("mp", None, None),
            channel,
            P("mp", None, None),
            channel,
            channel,
            P("mp", None),
            P(),
            columns,
            columns,
            P("mp", None),
            columns,
            P(None, None, "mp"),
            P(),
            seq_rows,
        ),
        out_specs=(
            seq_rows,
            seq_rows,
            P(),
            P("seq", "mp"),
            P("seq", "mp"),
            columns,
            channel,
            P("mp", None, None),
            channel,
            P("mp", None, None),
            channel,
            channel,
            P("mp", "seq"),
            P(),
            P("seq", "mp"),
            P("seq", "mp"),
            P("mp", "seq"),
            columns,
            P(None, None, "mp"),
        ),
        check_vma=False,
    )
```

```python
import functools

import jax
import jax.numpy as jnp
from jax import lax
from jax.experimental import pallas as pl
from jax.experimental.pallas import tpu as pltpu
from jax.sharding import PartitionSpec as P

MESH = pl.DeviceIdType.MESH
RATE_SCALE = 8.0
EPS = 1e-06
GELU_C = 0.7978845608028654
GELU_K = 0.044715
CONTRACT_ROWS = (((0,), (0,)), ((), ()))
CONTRACT_LAST = (((1,), (1,)), ((), ()))
TILE = 8
LANES = 128
ROWS = 32
CHUNK = 16
SKEW = 2
GROUP = 16
WEIGHT_STEPS = 8
COPIES = 8
LATER = 6
F32 = jnp.float32
BF16 = jnp.bfloat16
VMEM = pl.BlockSpec(memory_space=pltpu.VMEM)
HBM = pl.BlockSpec(memory_space=pl.ANY)
PINNED = pl.BlockSpec(memory_space=pltpu.HBM)


def dot(a, b):
    return jnp.dot(a, b, preferred_element_type=F32)


def matmul_back(a, b):
    return lax.dot_general(a, b, CONTRACT_LAST, preferred_element_type=F32)


def block(i, size):
    return pl.ds(pl.multiple_of(i * size, size), size)


def gelu(x):
    t = jnp.tanh(GELU_C * (x + GELU_K * (x * x * x)))
    return 0.5 * x * (1.0 + t)


def gelu_both(x):
    x2 = x * x
    t = jnp.tanh(GELU_C * (x + GELU_K * (x2 * x)))
    half = 0.5 * (1.0 + t)
    slope = half + 0.5 * x * (1.0 - t * t) * (GELU_C * (1.0 + (3.0 * GELU_K) * x2))
    return x * half, slope


def one_minus_square(log_a, a):
    y = 2.0 * log_a
    s = 1.0 + y * (1.0 / 8.0)
    for k in (7, 6, 5, 4, 3, 2):
        s = 1.0 + (y * (1.0 / k)) * s
    return jnp.where(y > -0.35, -y * s, 1.0 - a * a)


def get(ref, at):
    return jnp.concatenate([ref[j, at, :] for j in range(ref.shape[0])], axis=-1)


def put(ref, at, value):
    for j in range(ref.shape[0]):
        ref[j, at, :] = value[:, j * LANES : (j + 1) * LANES]


def to_all(axis, src, slots, send, recv):
    size, me = lax.axis_size(axis), lax.axis_index(axis)
    return [
        pltpu.make_async_remote_copy(
            src_ref=src,
            dst_ref=slots.at[me],
            send_sem=send.at[d - 1],
            recv_sem=recv.at[d - 1],
            device_id={axis: lax.rem(me + d, size)},
            device_id_type=MESH,
        )
        for d in range(1, size)
    ]


def to_one(axis, distance, src, dst, send, recv):
    size, me = lax.axis_size(axis), lax.axis_index(axis)
    return pltpu.make_async_remote_copy(
        src_ref=src,
        dst_ref=dst,
        send_sem=send,
        recv_sem=recv,
        device_id={axis: lax.rem(me + distance + size, size)},
        device_id_type=MESH,
    )


def spread_gates(blocks_ref, out_ref, start, width):
    heads, size = blocks_ref.shape[:2]
    for h in range(heads):
        block_h = blocks_ref[h].astype(F32)
        parts = [block_h]
        if h > 0:
            parts.insert(0, jnp.zeros((size, h * size), F32))
        if width > (h + 1) * size:
            parts.append(jnp.zeros((size, width - (h + 1) * size), F32))
        row = jnp.concatenate(parts, axis=1).astype(BF16)
        out_ref[h * size : (h + 1) * size, start : start + width] = row
    if width > heads * size:
        rest = jnp.zeros((width - heads * size, width), BF16)
        out_ref[heads * size : width, start : start + width] = rest


def forward_kernel(
    span,
    x_in,
    w_input_in,
    w_branch_in,
    gain_ref,
    taps_ref,
    conv_bias_ref,
    decay_ref,
    bias_r_ref,
    bias_i_ref,
    gate_r_ref,
    gate_i_ref,
    fresh_ref,
    state_ref,
    conv_init_ref,
    normed_out,
    branch_out,
    pad_out,
    pre_out,
    hidden_out,
    mixed_ref,
    carry_ref,
    sums_ref,
    gates_ref,
    vec_ref,
    ends_ref,
    x_ref,
    w_input_ref,
    w_branch_ref,
    normed_ref,
    branch_ref,
    pad_ref,
    pre_ref,
    hidden_ref,
    act_ref,
    a_ref,
    b_ref,
    conv_ref,
    tail_ref,
    tail_in,
    mine_ref,
    load_sem,
    store_sem,
    normed_sem,
    send1,
    recv1,
    send_t,
    recv_t,
):
    seqs = state_ref.shape[0]
    width = taps_ref.shape[1]
    taps = taps_ref.shape[0]
    rows = seqs * span
    devices, me = lax.axis_size("seq"), lax.axis_index("seq")
    local = pltpu.make_async_copy
    pitch = a_ref.shape[1] // seqs
    group = 2 * span
    groups = rows // group

    def x_load(g):
        at = block(g, group)
        return local(x_in.at[at], x_ref.at[at], load_sem.at[g])

    weight_loads = [
        local(w_input_in, w_input_ref, load_sem.at[groups]),
        local(w_branch_in, w_branch_ref, load_sem.at[groups + 1]),
    ]
    x_load(0).start()
    weight_loads[0].start()
    for g in range(1, groups):
        x_load(g).start()
    weight_loads[1].start()

    enter_all(("seq",))
    spread_gates(gate_r_ref, gates_ref, 0, width)
    spread_gates(gate_i_ref, gates_ref, width, width)
    vec_ref[0:1, :] = conv_bias_ref[...].reshape(1, width)
    vec_ref[1:2, :] = jax.nn.softplus(-decay_ref[...].reshape(1, width))
    bias_r = bias_r_ref[...].reshape(1, width)
    bias_i = bias_i_ref[...].reshape(1, width)
    keep = [1.0 - fresh_ref[s].astype(F32) for s in range(seqs)]

    def normed_store(g):
        at = block(g, group)
        return local(normed_ref.at[at], normed_out.at[at], normed_sem.at[g])

    def norm(g):
        x_load(g).wait()
        for q in range(group // CHUNK):
            at = slice(g * group + q * CHUNK, g * group + (q + 1) * CHUNK)
            x = x_ref[at, :]
            normed_ref[at, :] = (x * mean_square(x) * gain_ref[...]).astype(BF16)

    norm(0)
    weight_loads[0].wait()
    for g in range(groups):
        if g + 1 < groups:
            norm(g + 1)
        conv = dot(normed_ref[slice(g * group, (g + 1) * group), :], w_input_ref[...])
        for j in range(group // span):
            pad_ref[g * (group // span) + j, pl.ds(TILE, span), :] = conv[
                j * span : (j + 1) * span
            ]
    for g in range(groups):
        normed_store(g).start()

    for s in range(seqs):
        tail_ref[s] = pad_ref[s, pl.ds(span, TILE), :]
    tail_copy = to_one("seq", 1, tail_ref, tail_in, send_t.at[0], recv_t.at[0])
    tail_copy.start()
    weight_loads[1].wait()

    def branch(g):
        branch_ref[block(g, group), :] = dot(normed_ref[block(g, group), :], w_branch_ref[...])

    @pl.loop(0, groups // 2)
    def _(g):
        branch(g)

    stores = [
        local(source, target, store_sem.at[i])
        for i, (source, target) in enumerate(
            (
                (branch_ref, branch_out),
                (pad_ref, pad_out),
                (pre_ref, pre_out),
                (hidden_ref, hidden_out),
            )
        )
    ]
    tail_copy.wait()
    lead = jnp.zeros((TILE - taps + 1, width), F32)
    for s in range(seqs):
        initial = jnp.concatenate(
            [lead] + [conv_init_ref[k, s : s + 1, :] * keep[s] for k in range(taps - 1)], axis=0
        )
        pad_ref[s, pl.ds(0, TILE), :] = jnp.where(me == 0, initial, tail_in[s])
    stores[1].start()

    def gates(s, slot):
        for q in range(span // ROWS):
            part = pad_ref[s, pl.ds(q * ROWS, ROWS + TILE), :]
            total = vec_ref[0:1, :]
            for k in range(taps):
                first = TILE - (taps - 1) + k
                total = total + taps_ref[k : k + 1, :] * part[first : first + ROWS]
            conv_ref[slot, pl.ds(q * ROWS, ROWS), :] = total

        pre = dot(conv_ref[slot].astype(BF16), gates_ref[...])
        pre_ref[block(s, span), :width] = pre[:, :width] + bias_r
        pre_ref[block(s, span), width:] = pre[:, width:] + bias_i
        for q in range(span // ROWS):
            rows_q = slice(q * ROWS, (q + 1) * ROWS)
            conv = conv_ref[slot, pl.ds(q * ROWS, ROWS), :]
            recall = jax.nn.sigmoid(pre[rows_q, :width] + bias_r)
            gate = jax.nn.sigmoid(pre[rows_q, width:] + bias_i)
            log_a = (-RATE_SCALE * vec_ref[1:2, :]) * recall
            a = jnp.exp(log_a)
            spaced = pl.ds(pl.multiple_of(s * pitch + q * ROWS, TILE), ROWS)
            put(a_ref, spaced, a)
            put(b_ref, spaced, jnp.sqrt(one_minus_square(log_a, a)) * gate * conv)

    per = seqs // (groups - groups // 2)

    @pl.loop(0, groups - groups // 2)
    def _(i):
        branch(groups // 2 + i)
        for j in range(per):
            gates(i * per + j, j % 2)

    stores[0].start()
    stores[2].start()

    def at_time(ref, t):
        return get(ref, pl.ds(t, seqs, stride=pitch))

    def step(t, value):
        prod, state = value
        a = at_time(a_ref, t)
        return prod * a, a * state + at_time(b_ref, t)

    ones = jnp.ones((seqs, width), F32)
    prod, state = lax.fori_loop(0, span, step, (ones, jnp.zeros_like(ones)), unroll=8)
    mine_ref[0] = prod
    mine_ref[1] = state
    sums_ref[me] = mine_ref[...]
    copies = to_all("seq", mine_ref, sums_ref, send1, recv1)
    for copy in copies:
        copy.start()

    @pl.loop(0, rows // ROWS, unroll=2)
    def _(q):
        at = block(q, ROWS)
        act_ref[at, :] = gelu(branch_ref[at, :])

    for copy in copies:
        copy.wait()

    def carry_step(j, carry):
        both = sums_ref[j]
        return jnp.where(j < me, both[0] * carry + both[1], carry)

    start = jnp.concatenate([state_ref[s : s + 1, :] * keep[s] for s in range(seqs)], axis=0)
    carry = lax.fori_loop(0, devices - 1, carry_step, start)
    carry_ref[...] = carry

    def final(t, state):
        state = at_time(a_ref, t) * state + at_time(b_ref, t)
        put(hidden_ref, pl.ds(t, seqs, stride=span), state)
        return state

    last = lax.fori_loop(0, span, final, carry, unroll=8)
    stores[3].start()
    ends_ref[0:seqs, :] = jnp.where(me == devices - 1, last, 0.0)
    for s in range(seqs):
        ends_ref[(s + 1) * TILE : (s + 2) * TILE, :] = jnp.where(
            me == devices - 1, pad_ref[s, pl.ds(span, TILE), :], 0.0
        )

    @pl.loop(0, rows // ROWS, unroll=2)
    def _(q):
        at = block(q, ROWS)
        mixed_ref[at, :] = (get(hidden_ref, at) * act_ref[at, :]).astype(BF16)

    for copy in stores:
        copy.wait()
    for g in range(groups):
        normed_store(g).wait()


def backward_kernel(
    span,
    heads,
    block_part_in,
    own_in,
    low_in,
    w_out_in,
    branch_in,
    hidden_in,
    pre_in,
    pad_in,
    normed_in,
    mixed_in,
    rest_in,
    gates_in,
    carry_ref,
    sums_ref,
    taps_ref,
    vec_ref,
    block_out,
    rec_out,
    grad_branch_out,
    input_out,
    acc_ref,
    blocks_ref,
    part,
    inbox,
    out,
    send_up,
    send_down,
    recv_up,
    recv_down,
    own_ref,
    resid_low,
    w_out_ref,
    branch_ref,
    hidden_ref,
    pre_ref,
    pad_ref,
    normed_ref,
    mixed_ref,
    a_ref,
    gd_ref,
    grad_ref,
    direct_ref,
    gpad_ref,
    heads_ref,
    low_ref,
    gates_grad,
    stage_ref,
    mine_ref,
    entries_ref,
    head_ref,
    head_in,
    load_sem,
    part_sem,
    store_sem,
    stage_sem,
    send1,
    recv1,
    send_t,
    recv_t,
    gates_ref,
    grad_branch_ref,
    input_ref,
    give_sem,
):
    seqs, width = carry_ref.shape
    taps = taps_ref.shape[0]
    rows = seqs * span
    devices, me = lax.axis_size("seq"), lax.axis_index("seq")
    n, z = lax.axis_size("mp"), lax.axis_index("mp")
    chunks = rows // CHUNK
    size = GROUP * CHUNK
    held = part.shape[0] // size
    groups = chunks // GROUP
    sems = (send_up, send_down, recv_up, recv_down)
    local = pltpu.make_async_copy

    def part_load(g):
        slot = lax.rem(g, held)
        return local(block_part_in.at[block(g, size)], part.at[block(slot, size)], part_sem.at[slot])

    loads = [
        local(source, target, load_sem.at[i])
        for i, (source, target) in enumerate(
            (
                (own_in, own_ref),
                (low_in, resid_low),
                (w_out_in, w_out_ref),
                (pre_in, pre_ref),
                (branch_in, branch_ref),
                (hidden_in, hidden_ref),
                (pad_in, pad_ref),
                (mixed_in, mixed_ref),
                (normed_in, normed_ref),
                (gates_in, gates_ref),
            )
        )
    ]
    part_load(0).start()
    for copy in loads[:6]:
        copy.start(priority=1)
    for g in range(1, held):
        part_load(g).start()
    for copy in loads[6:]:
        copy.start(priority=1)
    acc_ref[...] = jnp.zeros_like(acc_ref)
    enter_all(("seq", "mp"))

    pitch = a_ref.shape[1] // seqs

    def spaced(s, q):
        return pl.ds(pl.multiple_of(s * pitch + q * ROWS, TILE), ROWS)

    def decay(at):
        recall = jax.nn.sigmoid(pre_ref[at, :width])
        log_a = (-RATE_SCALE * vec_ref[1:2, :]) * recall
        return recall, log_a, jnp.exp(log_a)

    def piece_direct(s):
        @pl.when(s == 0)
        def _():
            for copy in loads[1:6]:
                copy.wait()

        grad_ref[...] = matmul_back(resid_low[block(s, span), :], w_out_ref[...])

        @pl.loop(0, span // ROWS)
        def _(q):
            at = block(s * (span // ROWS) + q, ROWS)
            put(a_ref, spaced(s, q), decay(at)[2])
            act, slope = gelu_both(branch_ref[at, :])
            grad = grad_ref[block(q, ROWS), :]
            put(gd_ref, spaced(s, q), grad * act)
            grad_branch_ref[at, :] = (grad * get(hidden_ref, at) * slope).astype(BF16)

    def at_time(ref, t):
        return get(ref, pl.ds(t, seqs, stride=pitch))

    zero = jnp.zeros((seqs, width), F32)
    entry_copies = to_all("seq", mine_ref, entries_ref, send1, recv1)

    def piece_entry(_):
        def step(k, through):
            t = span - 1 - k
            return at_time(a_ref, t) * (at_time(gd_ref, t) + through)

        mine_ref[...] = lax.fori_loop(0, span, step, zero, unroll=8)
        entries_ref[me] = mine_ref[...]
        for copy in entry_copies:
            copy.start()

    def piece_state(_):
        for copy in entry_copies:
            copy.wait()

        def back_step(k, through):
            j = devices - 1 - k
            return jnp.where(j > me, entries_ref[j] + sums_ref[j, 0] * through, through)

        incoming = lax.fori_loop(0, devices - 1, back_step, zero)

        def final(k, through):
            t = span - 1 - k
            grad = at_time(gd_ref, t) + through
            put(gd_ref, pl.ds(t, seqs, stride=pitch), grad)
            return at_time(a_ref, t) * grad

        lax.fori_loop(0, span, final, incoming, unroll=8)

    def add(k, value):
        acc_ref[k] += fold(value)

    parts = 2

    def piece_gates(i):
        s = i // parts
        quarters = span // ROWS // parts

        @pl.when(i == 0)
        def _():
            loads[6].wait()
            loads[9].wait()

        @pl.loop(lax.rem(i, parts) * quarters, (lax.rem(i, parts) + 1) * quarters)
        def _(q):
            at = block(s * (span // ROWS) + q, ROWS)
            part_rows = pad_ref[s, pl.ds(pl.multiple_of(q * ROWS, ROWS), ROWS + TILE), :]
            conv = vec_ref[0:1, :]
            for k in range(taps):
                first = TILE - (taps - 1) + k
                conv = conv + taps_ref[k : k + 1, :] * part_rows[first : first + ROWS]
            heads_ref[at, :] = conv.astype(BF16)
            recall, log_a, a = decay(at)
            gate = jax.nn.sigmoid(pre_ref[at, width:])
            square = one_minus_square(log_a, a)
            inverse = lax.rsqrt(square)
            root = jnp.sqrt(square)
            grad = get(gd_ref, spaced(s, q))
            hidden = get(hidden_ref, at)
            before_at = pl.multiple_of(jnp.maximum(s * span + q * ROWS - TILE, 0), TILE)
            earlier = get(hidden_ref, pl.ds(before_at, TILE))
            first_row = jnp.where(q == 0, carry_ref[pl.ds(s, 1), :], earlier[TILE - 1 :])
            place = lax.broadcasted_iota(jnp.int32, (ROWS, width), 0)
            prev = jnp.where(place == 0, first_row, pltpu.roll(hidden, 1, 0))
            grad_log = grad * a * (prev - gate * conv * a * inverse)
            through = grad_log * recall
            pre_r = through * (1.0 - recall) * (-RATE_SCALE * vec_ref[1:2, :])
            direct = grad * root * gate
            pre_i = direct * conv * (1.0 - gate)
            low_ref[at, :width] = pre_r.astype(BF16)
            low_ref[at, width:] = pre_i.astype(BF16)
            direct_ref[block(q, ROWS), :] = direct
            add(0, through)
            add(1, pre_r)
            add(2, pre_i)

        @pl.when(lax.rem(i, parts) == parts - 1)
        def _():
            whole = direct_ref[...] + matmul_back(low_ref[block(s, span), :], gates_ref[...])
            gpad_ref[s, pl.ds(0, span), :] = whole
            head_ref[s] = whole[:TILE]

    head_copy = to_one("seq", -1, head_ref, head_in, send_t.at[0], recv_t.at[0])

    def piece_head(_):
        head_copy.start()

    def piece_taps(i):
        for j in range(2):
            taps_of(2 * i + j)

    def taps_of(s):
        @pl.loop(0, span // ROWS)
        def _(q):
            at = pl.multiple_of(q * ROWS, ROWS)
            part_rows = pad_ref[s, pl.ds(at, ROWS + TILE), :]
            grad = gpad_ref[s, pl.ds(at, ROWS), :]
            add(3, grad)
            for k in range(taps):
                first = TILE - (taps - 1) + k
                add(4 + k, grad * part_rows[first : first + ROWS])

    def piece_tail(_):
        head_copy.wait()
        for s in range(seqs):
            gpad_ref[s, pl.ds(span, TILE), :] = jnp.where(me == devices - 1, 0.0, head_in[s])

    def piece_input(i):
        for j in range(2):
            input_of(2 * i + j)

    def input_of(s):
        @pl.loop(0, span // ROWS)
        def _(q):
            part_rows = gpad_ref[s, pl.ds(pl.multiple_of(q * ROWS, ROWS), ROWS + TILE), :]
            total = taps_ref[taps - 1 : taps, :] * part_rows[0:ROWS]
            for k in range(taps - 1):
                first = taps - 1 - k
                total = total + taps_ref[k : k + 1, :] * part_rows[first : first + ROWS]
            input_ref[block(s * (span // ROWS) + q, ROWS), :] = total.astype(BF16)

    def contract(left, right):
        return lax.dot_general(left, right, CONTRACT_ROWS, preferred_element_type=F32)

    head = blocks_ref.shape[0]

    gives = [
        local(grad_branch_ref, grad_branch_out, give_sem.at[0]),
        local(input_ref, input_out, give_sem.at[1]),
    ]

    def piece_gates_grad(i):
        @pl.when(i == 0)
        def _():
            for copy in gives:
                copy.start(priority=1)

        @pl.when(i == 0)
        def _():
            gates_grad[...] = contract(heads_ref[...], low_ref[:, :width])

        @pl.when(i == 1)
        def _():
            gates_grad[...] = contract(heads_ref[...], low_ref[:, width:])

        place = lax.broadcasted_iota(jnp.int32, (head, width), 1)
        line = jnp.zeros((head, width), F32)
        for h in range(heads):
            row = gates_grad[h * head : (h + 1) * head, :]
            inside = jnp.logical_and(place >= h * head, place < (h + 1) * head)
            line = jnp.where(inside, row, line)

        for j in range(2):

            @pl.when(i == j)
            def _():
                blocks_ref[:, j * width : (j + 1) * width] = line

    tall = resid_low.shape[1] // WEIGHT_STEPS

    def stage_store(i):
        at = block(lax.rem(i, WEIGHT_STEPS), tall)
        slot = lax.rem(i, 2)
        return local(
            stage_ref.at[slot],
            rec_out.at[i // WEIGHT_STEPS, at, pl.ds(0, width)],
            stage_sem.at[slot],
        )

    def piece_weights(i):
        @pl.when(i == 0)
        def _():
            loads[7].wait()
            loads[8].wait()

        @pl.loop(2 * i, 2 * i + 2)
        def _(j):
            weight_of(j)

    def weight_of(i):
        @pl.when(i >= 2)
        def _():
            stage_store(i - 2).wait()

        at = block(lax.rem(i, WEIGHT_STEPS), tall)
        slot = lax.rem(i, 2)
        for which, (left, right) in enumerate(
            ((resid_low, mixed_ref), (normed_ref, grad_branch_ref), (normed_ref, input_ref))
        ):
            @pl.when(i // WEIGHT_STEPS == which)
            def _():
                stage_ref[slot] = contract(left[:, at], right[...])

        stage_store(i).start(priority=1)

    weights = 3 * WEIGHT_STEPS
    plan = []
    begin = 3
    for work, times, gap in (
        (piece_direct, seqs, 0),
        (piece_entry, 1, 1),
        (piece_state, 1, 0),
        (piece_gates, parts * seqs, 0),
        (piece_head, 1, 0),
        (piece_taps, seqs // 2, 0),
        (piece_tail, 1, 0),
        (piece_input, seqs // 2, 0),
        (piece_gates_grad, 2, 0),
        (piece_weights, weights // 2, 0),
    ):
        plan.append((work, begin, times))
        begin += times + gap

    def run(step):
        for work, first, times in plan:
            @pl.when(jnp.logical_and(step >= first, step < first + times))
            def _():
                work(step - first)

    def before(k):
        @pl.when(k == SKEW * (n // 2))
        def _():
            loads[0].wait()

        @pl.when(jnp.logical_and(lax.rem(k, GROUP) == 0, k < chunks))
        def _():
            part_load(k // GROUP).wait()

        g = (k - out.shape[0]) // GROUP - 1 + held

        @pl.when(
            jnp.logical_and(
                jnp.logical_and(k >= out.shape[0] + GROUP, lax.rem(k - out.shape[0], GROUP) == 0),
                g < groups,
            )
        )
        def _():
            part_load(g).start(priority=1)

        run(k)

    def root(c, slot, total):
        out[slot] = own_ref[block(c // 2, CHUNK), :] + total

    def store(c, slot):
        return local(out.at[slot], block_out.at[block(c, CHUNK)], store_sem.at[slot])

    def arrive(c, slot):
        store(c, slot).start(priority=1)

    def leave(c, slot):
        store(c, slot).wait()

    line_sum(
        "mp", chunks, held * GROUP, part, inbox, out, sems, before, root, arrive, leave
    )

    @pl.loop(chunks + out.shape[0], max(begin, chunks + out.shape[0]))
    def _(k):
        run(k)

    for copy in gives:
        copy.wait()
    stage_store(weights - 2).wait()
    stage_store(weights - 1).wait()


def backward_call(span, heads, head, *args):
    block_part = args[0]
    low, w_out, branch, hidden, pre, padded, normed, mixed, rest, gates = args[2:12]
    carry, sums, taps = args[12:15]
    rows, model = block_part.shape
    seqs, width = carry.shape
    devices = lax.axis_size("seq")
    ring = ring_size("mp")
    held = 3 * GROUP * CHUNK
    dma = pltpu.SemaphoreType.DMA
    columns = pltpu.VMEM((width // LANES, seqs * (span + TILE), LANES), F32)
    return pl.pallas_call(
        functools.partial(backward_kernel, span, heads),
        out_shape=(
            shape((rows, model)),
            shape(rest.shape),
            shape((rows, width), BF16),
            shape((rows, width), BF16),
            shape((4 + taps.shape[0], TILE, width)),
            shape((head, 2 * width)),
        ),
        in_specs=[HBM] * 12 + [VMEM] * 4,
        input_output_aliases={10: 1},
        out_specs=(HBM,) * 4 + (VMEM,) * 2,
        scratch_shapes=line_scratch("mp", held, model)
        + [
            pltpu.VMEM((rows // 2, model), F32),
            pltpu.VMEM((rows, model), BF16),
            pltpu.VMEM((width, model), BF16),
            pltpu.VMEM((rows, width), F32),
            pltpu.VMEM(hidden.shape, F32),
            pltpu.VMEM(pre.shape, F32),
            pltpu.VMEM(padded.shape, F32),
            pltpu.VMEM((rows, model), BF16),
            pltpu.VMEM((rows, width), BF16),
            columns,
            columns,
            pltpu.VMEM((span, width), F32),
            pltpu.VMEM((span, width), F32),
            pltpu.VMEM((seqs, span + TILE, width), F32),
            pltpu.VMEM((rows, width), BF16),
            pltpu.VMEM((rows, 2 * width), BF16),
            pltpu.VMEM((width, width), F32),
            pltpu.VMEM((2, model // WEIGHT_STEPS, width), F32),
            pltpu.VMEM((seqs, width), F32),
            pltpu.VMEM((devices, seqs, width), F32),
            pltpu.VMEM((seqs, TILE, width), F32),
            pltpu.VMEM((seqs, TILE, width), F32),
            dma((10,)),
            dma((3,)),
            dma((ring,)),
            dma((2,)),
            dma((devices - 1,)),
            dma((devices - 1,)),
            dma((1,)),
            dma((1,)),
            pltpu.VMEM(gates.shape, BF16),
            pltpu.VMEM((rows, width), BF16),
            pltpu.VMEM((rows, width), BF16),
            dma((2,)),
        ],
        compiler_params=params(1, 63),
        cost_estimate=cost(200),
        name="backward",
    )(*args)


def line_sum(axis, total, period, part, inbox, out, sems, before, root, arrive, leave):
    send_up, send_down, recv_up, recv_down = sems
    parts = send_up.shape[0]
    columns = out.shape[2] // parts
    n, z = lax.axis_size(axis), lax.axis_index(axis)
    depth = n // 2
    ring = out.shape[0]

    def cols(p):
        return pl.ds(p * columns, columns)

    def root_of(c):
        return depth - 1 + lax.rem(c, 2)

    def up(c, step, side, p):
        slot = lax.rem(c, ring)
        return pltpu.make_async_remote_copy(
            src_ref=part.at[block(lax.rem(c, period), CHUNK), cols(p)],
            dst_ref=inbox.at[side, slot, :, cols(p)],
            send_sem=send_up.at[p, slot],
            recv_sem=recv_up.at[p, side, slot],
            device_id={axis: z + step},
            device_id_type=MESH,
        )

    def down(c, step, side, p):
        slot = lax.rem(c, ring)
        return pltpu.make_async_remote_copy(
            src_ref=out.at[slot, :, cols(p)],
            dst_ref=out.at[slot, :, cols(p)],
            send_sem=send_down.at[p, side, slot],
            recv_sem=recv_down.at[p, slot],
            device_id={axis: z + step},
            device_id_type=MESH,
        )

    inner = jnp.logical_and(z > 0, z < n - 1)

    @pl.loop(0, total + ring)
    def _(k):
        @pl.when(k >= ring)
        def _():
            c = k - ring
            r = root_of(c)
            step = jnp.where(z < r, 1, -1)
            side = jnp.where(z < r, 0, 1)

            @pl.when(z == r)
            def _():
                for p in range(parts):
                    down(c, -1, 0, p).wait_send()
                    down(c, 1, 1, p).wait_send()

            @pl.when(z != r)
            def _():
                for p in range(parts):
                    up(c, step, side, p).wait_send()

            @pl.when(jnp.logical_and(z != r, inner))
            def _():
                for p in range(parts):
                    down(c, -step, side, p).wait_send()

            leave(c, lax.rem(c, ring))

        before(k)

        for i in reversed(range(n + 1)):
            c = k - SKEW * i
            valid = jnp.logical_and(c >= 0, c < total)
            c = jnp.clip(c, 0, total - 1)
            at = block(lax.rem(c, period), CHUNK)
            slot = lax.rem(c, ring)
            r = root_of(c)
            step = jnp.where(z < r, 1, -1)
            side = jnp.where(z < r, 0, 1)
            if i > depth:
                here = jnp.logical_and(z != r, jnp.abs(z - r) == i - depth)

                @pl.when(jnp.logical_and(valid, here))
                def _():
                    for p in range(parts):
                        down(c, -step, side, p).wait_recv()

                        @pl.when(inner)
                        def _():
                            down(c, -step, side, p).start()

                    arrive(c, slot)
            elif i == depth:

                @pl.when(jnp.logical_and(valid, z == r))
                def _():
                    for p in range(parts):
                        up(c, 1, 0, p).wait_recv()
                        up(c, -1, 1, p).wait_recv()
                    root(c, slot, part[at, :] + inbox[0, slot] + inbox[1, slot])
                    for p in range(parts):
                        down(c, -1, 0, p).start()
                        down(c, 1, 1, p).start()
                    arrive(c, slot)
            else:
                here = jnp.where(z < r, z, n - 1 - z) == i

                @pl.when(jnp.logical_and(valid, jnp.logical_and(z != r, here)))
                def _():
                    for p in range(parts):
                        if i > 0:
                            up(c, step, side, p).wait_recv()
                            part[at, cols(p)] += inbox[side, slot, :, cols(p)]
                        up(c, step, side, p).start()


def ring_size(axis):
    return SKEW * lax.axis_size(axis) + 4


def line_scratch(axis, rows, model, parts=2):
    dma = pltpu.SemaphoreType.DMA
    ring = ring_size(axis)
    return [
        pltpu.VMEM((rows, model), F32),
        pltpu.VMEM((2, ring, CHUNK, model), F32),
        pltpu.VMEM((ring, CHUNK, model), F32),
        dma((parts, ring)),
        dma((parts, 2, ring)),
        dma((parts, 2, ring)),
        dma((parts, ring)),
    ]


def mean_square(x):
    return lax.rsqrt(jnp.mean(x * x, axis=-1, keepdims=True) + EPS)


def nothing(*_):
    pass


def fold(value):
    total = value[0:TILE]
    for i in range(1, value.shape[0] // TILE):
        total = total + value[i * TILE : (i + 1) * TILE]
    return total


def norm_grad(value, gain, grad, acc_ref):
    q = mean_square(value)
    e = gain * grad
    acc_ref[...] += fold(grad * value * q)
    return q * e - value * (q * q * q) * jnp.mean(e * value, axis=-1, keepdims=True)


def middle_kernel(
    mixed_in,
    w_out_in,
    x_in,
    og_in,
    gain_ref,
    w_gate_in,
    w_up_in,
    w_down_in,
    normed_out,
    hidden_out,
    gate_out,
    up_out,
    glow_out,
    block_out,
    low_out,
    own_grad_out,
    weight_out,
    rest_out,
    own_out,
    acc_ref,
    part,
    inbox,
    out,
    send_up,
    send_down,
    recv_up,
    recv_down,
    mixed,
    w_out,
    w_gate,
    w_up,
    w_down,
    normed,
    rows_ref,
    og_ref,
    glow,
    gate_val,
    up_val,
    grad_hidden,
    hidden,
    grad_gate,
    grad_up,
    block_part,
    low,
    weight_sem,
    row_sem,
    og_sem,
    act_sem,
    low_sem,
    own_sem,
    again_sem,
    stage_sem,
    rest_sem,
    own_ref,
):
    n, z = lax.axis_size("mp"), lax.axis_index("mp")
    count = part.shape[0] // CHUNK
    size = GROUP * CHUNK
    groups = count // GROUP
    ring = out.shape[0]
    sems = (send_up, send_down, recv_up, recv_down)
    local = pltpu.make_async_copy

    loads = [
        local(source, target, weight_sem.at[i])
        for i, (source, target) in enumerate(
            (
                (mixed_in, mixed),
                (w_out_in, w_out),
                (w_gate_in, w_gate),
                (w_up_in, w_up),
                (w_down_in, w_down.at[slice(0, w_down_in.shape[0])]),
            )
        )
    ]
    for copy in loads:
        copy.start(priority=1)
    deep = w_down_in.shape[0]

    def og_load(g):
        return local(og_in.at[block(g, size)], og_ref, og_sem.at[0])

    og_load(0).start(priority=1)
    enter_all(("mp",))
    acc_ref[...] = jnp.zeros_like(acc_ref)
    loads[0].wait()
    loads[1].wait()

    def is_root(c):
        return z == n // 2 - 1 + lax.rem(c, 2)

    def row_load(source, c):
        slot = lax.rem(c, ring)
        at = block(lax.rem(c, count), CHUNK)
        return local(source.at[at], rows_ref.at[slot], row_sem.at[slot])

    acts = (
        (normed, normed_out),
        (glow, glow_out),
        (hidden, hidden_out),
        (grad_gate, gate_out),
        (grad_up, up_out),
        (block_part, block_out),
    )

    def act_store(i, g):
        source, target = acts[i]
        source = source.at[lax.rem(g, 2)] if i == 0 else source
        return local(source, target.at[block(g, size)], act_sem.at[i])

    def at_tick(k, first, work):
        g = (k - first) // GROUP

        @pl.when(
            jnp.logical_and(
                jnp.logical_and(k >= first, k < first + GROUP * groups),
                lax.rem(k - first, GROUP) == 0,
            )
        )
        def _():
            work(g)

    def project(g):
        def work(cols):
            part[block(g, size), cols] = dot(mixed[block(g, size), :], w_out[:, cols])

        work(slice(None))

    def piece_gate(g):
        @pl.when(g == 0)
        def _():
            for copy in loads[2:]:
                copy.wait()

        def work(cols):
            gate_val[:, cols] = dot(normed[lax.rem(g, 2)], w_gate[:, cols])

        work(slice(None))
        act_store(0, g).start(priority=1)

    def piece_up(g):
        def work(cols):
            up_val[:, cols] = dot(normed[lax.rem(g, 2)], w_up[:, cols])

        work(slice(None))

        @pl.when(g > 0)
        def _():
            for i in range(1, 6):
                act_store(i, g - 1).wait()

    def piece_low(g):
        og_load(g).wait()

        @pl.loop(0, size // ROWS)
        def _(q):
            glow[block(q, ROWS), :] = og_ref[block(q, ROWS), :].astype(BF16)

        @pl.when(g + 1 < groups)
        def _():
            og_load(g + 1).start(priority=1)

        act_store(1, g).start(priority=1)
        act_store(0, g).wait()

    def piece_hidden(g):
        def work(cols):
            grad_hidden[...] = matmul_back(glow[...], w_down[:deep, :])

        work(slice(None))

    def piece_act(g):
        @pl.loop(0, size // CHUNK)
        def _(q):
            at = block(q, CHUNK)
            up = up_val[at, :]
            grad = grad_hidden[at, :]
            act, slope = gelu_both(gate_val[at, :])
            hidden[at, :] = (act * up).astype(BF16)
            grad_gate[at, :] = (grad * up * slope).astype(BF16)
            grad_up[at, :] = (grad * act).astype(BF16)

        for i in range(2, 5):
            act_store(i, g).start(priority=1)

    def piece_down(g):
        def work(cols):
            block_part[:, cols] = dot(hidden[...], w_down[:deep, cols])

        work(slice(None))
        act_store(5, g).start(priority=1)

    def piece_back_gate(g):
        def work(cols):
            part[block(g, size), cols] = matmul_back(grad_gate[...], w_gate[cols, :])

        work(slice(None))

    def piece_back_up(g):
        def work(cols):
            part[block(g, size), cols] += matmul_back(grad_up[...], w_up[cols, :])

        work(slice(None))

    tokens = count * CHUNK
    half = tokens // 2
    quarter = half // 2
    again = [
        local(source, target, again_sem.at[i])
        for i, (source, target) in enumerate(
            (
                (normed_out, w_down.at[slice(0, tokens)]),
                (gate_out, w_gate.at[slice(0, tokens)]),
                (up_out, w_up.at[slice(0, tokens)]),
                (hidden_out, w_gate.at[slice(tokens, 2 * tokens)]),
                (glow_out.at[slice(0, half)], w_down.at[slice(tokens, tokens + half)]),
                (glow_out.at[slice(half, half + quarter)], normed.at[0]),
                (glow_out.at[slice(half + quarter, tokens)], normed.at[1]),
            )
        )
    ]
    tall = w_gate.shape[0] // WEIGHT_STEPS
    stages = (gate_val, up_val, grad_hidden)

    kept = weight_out.shape[2]
    before_rest = rest_out.shape[2] - (deep - kept)

    def stage_stores(which, i):
        at = block(i, tall)
        return (
            local(
                stages[which].at[:, pl.ds(0, kept)],
                weight_out.at[which, at],
                stage_sem.at[which],
            ),
            local(
                stages[which].at[:, pl.ds(kept, deep - kept)],
                rest_out.at[which, at, pl.ds(before_rest, deep - kept)],
                rest_sem.at[which],
            ),
        )

    own_copy = local(own_ref, own_out, rest_sem.at[3])

    def piece_reload():
        own_copy.start(priority=1)
        for i in range(1, 6):
            act_store(i, groups - 1).wait()
        for copy in again:
            copy.start(priority=1)

    def piece_ready():
        for copy in again:
            copy.wait()

    def contract(left, right):
        return lax.dot_general(left, right, CONTRACT_ROWS, preferred_element_type=F32)

    def piece_weight(step):
        i = step // 3
        at = block(i, tall)
        for which in range(3):

            @pl.when(lax.rem(step, 3) == which)
            def _():
                @pl.when(i > 0)
                def _():
                    for copy in stage_stores(which, i - 1):
                        copy.wait()

                stage = stages[which]

                def work(cols):
                    if which == 0:
                        stage[:, cols] = contract(w_down[:tokens, at], w_gate[:tokens, cols])
                    elif which == 1:
                        stage[:, cols] = contract(w_down[:tokens, at], w_up[:tokens, cols])
                    else:
                        middle = tokens + half + quarter
                        stage[:, cols] = (
                            contract(
                                w_down[tokens : tokens + half, at],
                                w_gate[tokens : tokens + half, cols],
                            )
                            + contract(normed[0, :, at], w_gate[tokens + half : middle, cols])
                            + contract(normed[1, :, at], w_gate[middle : 2 * tokens, cols])
                        )

                work(slice(None))
                for copy in stage_stores(which, i):
                    copy.start(priority=1)

    first = GROUP + SKEW * n
    spare = GROUP * groups + ring + 3
    first_weight = spare + 3
    weights = 3 * WEIGHT_STEPS

    def before(k):
        @pl.when(k == spare)
        def _():
            piece_reload()

        @pl.when(k == first_weight - 1)
        def _():
            piece_ready()

        @pl.when(jnp.logical_and(k >= first_weight, k < first_weight + weights))
        def _():
            piece_weight(k - first_weight)

        @pl.when(jnp.logical_and(k < count, is_root(k)))
        def _():
            row_load(x_in, k).start(priority=1)

        @pl.when(
            jnp.logical_and(jnp.logical_and(k >= count, k < 2 * count), is_root(k))
        )
        def _():
            row_load(og_in, k).start(priority=1)

        at_tick(k, 0, project)
        at_tick(k, first, piece_gate)
        at_tick(k, first + 1, piece_up)
        at_tick(k, first + 2, piece_low)
        at_tick(k, first + 3, piece_hidden)
        at_tick(k, first + 4, piece_act)
        at_tick(k, first + 6, piece_down)
        at_tick(k, GROUP + ring, piece_back_gate)
        at_tick(k, GROUP + ring + 2, piece_back_up)

    def root(c, slot, total):
        j = lax.rem(c, count)
        mine = block(j // 2, CHUNK)
        row_load(x_in, c).wait()

        @pl.when(c < count)
        def _():
            value = rows_ref[slot] + total
            own_ref[mine, :] = value
            out[slot] = (value * mean_square(value) * gain_ref[...]).astype(BF16).astype(F32)

        @pl.when(c >= count)
        def _():
            back = norm_grad(own_ref[mine, :], gain_ref[...], total, acc_ref)
            out[slot] = rows_ref[slot] + back

    def low_store(c, slot):
        at = block(lax.rem(c, count), CHUNK)
        return local(low.at[slot], low_out.at[at], low_sem.at[slot])

    def own_store(c, slot):
        at = block(lax.rem(c, count) // 2, CHUNK)
        return local(out.at[slot], own_grad_out.at[at], own_sem.at[slot])

    def arrive(c, slot):
        @pl.when(c < count)
        def _():
            normed[lax.rem(c // GROUP, 2), block(lax.rem(c, GROUP), CHUNK), :] = out[slot].astype(BF16)

        @pl.when(c >= count)
        def _():
            low[slot] = out[slot].astype(BF16)
            low_store(c, slot).start(priority=1)

            @pl.when(is_root(c))
            def _():
                own_store(c, slot).start(priority=1)

    def leave(c, slot):
        @pl.when(c >= count)
        def _():
            low_store(c, slot).wait()

            @pl.when(is_root(c))
            def _():
                own_store(c, slot).wait()

    line_sum("mp", 2 * count, count, part, inbox, out, sems, before, root, arrive, leave)

    own_copy.wait()
    for which in range(3):
        for copy in stage_stores(which, WEIGHT_STEPS - 1):
            copy.wait()


def middle_call(*args):
    mixed, w_out, x, og, gain, w_gate, w_up, w_down = args
    rows, model = x.shape
    width, hidden = mixed.shape[1], w_gate.shape[1]
    size = GROUP * CHUNK
    dma = pltpu.SemaphoreType.DMA
    ring = ring_size("mp")
    act = shape((rows, hidden), BF16)
    tall = shape((rows, model), BF16)
    return pl.pallas_call(
        middle_kernel,
        out_shape=(
            tall,
            act,
            act,
            act,
            tall,
            shape((rows, model)),
            tall,
            shape((rows // 2, model)),
            shape((3, model, hidden - hidden // LATER)),
            shape((3, model, width + hidden // LATER)),
            shape((rows // 2, model)),
            shape((TILE, model)),
        ),
        in_specs=[HBM] * 4 + [VMEM] + [HBM] * 3,
        out_specs=(HBM,) * 11 + (VMEM,),
        scratch_shapes=line_scratch("mp", rows, model)
        + [
            pltpu.VMEM((rows, width), BF16),
            pltpu.VMEM((width, model), BF16),
            pltpu.VMEM((model, hidden), BF16),
            pltpu.VMEM((model, hidden), BF16),
            pltpu.VMEM((max(hidden, rows * 3 // 2), model), BF16),
            pltpu.VMEM((2, size, model), BF16),
            pltpu.VMEM((ring, CHUNK, model), F32),
            pltpu.VMEM((size, model), F32),
            pltpu.VMEM((size, model), BF16),
            pltpu.VMEM((size, hidden), F32),
            pltpu.VMEM((size, hidden), F32),
            pltpu.VMEM((size, hidden), F32),
            pltpu.VMEM((size, hidden), BF16),
            pltpu.VMEM((size, hidden), BF16),
            pltpu.VMEM((size, hidden), BF16),
            pltpu.VMEM((size, model), F32),
            pltpu.VMEM((ring, CHUNK, model), BF16),
            dma((5,)),
            dma((ring,)),
            dma((1,)),
            dma((6,)),
            dma((ring,)),
            dma((ring,)),
            dma((7,)),
            dma((3,)),
            dma((4,)),
            pltpu.VMEM((rows // 2, model), F32),
        ],
        compiler_params=params(2, 63),
        cost_estimate=cost(400),
        name="middle",
    )(*args)


def last_kernel(
    own_grad_in,
    x_in,
    grad_branch_in,
    input_in,
    w_branch_in,
    w_input_in,
    gain_ref,
    other_acc,
    sums_in,
    ends_in,
    blocks_in,
    grad_out,
    norm_ref,
    small_out,
    part,
    inbox,
    out,
    send_up,
    send_down,
    recv_up,
    recv_down,
    own_grad_ref,
    x_ref,
    grad_branch,
    input_low,
    w_branch,
    w_input,
    load_sem,
    store_sem,
    acc_ref,
    mine_ref,
    seq_in,
    mp_in,
    send_s,
    recv_s,
    send_m,
    recv_m,
    small,
    small_in,
    send_v,
    recv_v,
):
    count = part.shape[0] // CHUNK
    size = GROUP * CHUNK
    sems = (send_up, send_down, recv_up, recv_down)
    local = pltpu.make_async_copy

    loads = [
        local(source, target, load_sem.at[i])
        for i, (source, target) in enumerate(
            (
                (grad_branch_in, grad_branch),
                (w_branch_in, w_branch),
                (input_in, input_low),
                (w_input_in, w_input),
                (own_grad_in, own_grad_ref),
                (x_in, x_ref),
            )
        )
    ]
    for copy in loads:
        copy.start(priority=1)
    acc_ref[...] = jnp.zeros_like(acc_ref)
    mine_ref[...] = jnp.zeros_like(mine_ref)
    enter_all(("seq", "mp"))
    for copy in loads[:4]:
        copy.wait()

    kinds = sums_in.shape[0]
    me = lax.axis_index("seq")
    width = sums_in.shape[2]
    height = kinds + ends_in.shape[0]
    head = blocks_in.shape[0]
    for i in range(kinds):
        small[0, i : i + 1, :] = jnp.sum(sums_in[i], axis=0, keepdims=True)
    small[0, kinds:height, :] = ends_in[...]
    small[0, height : height + head, :] = blocks_in[:, :width]
    small[0, height + head :, :] = blocks_in[:, width:]
    levels = small_in.shape[0]

    def exchange(level):
        bit = 1 << level
        partner = me + bit - 2 * bit * lax.rem(me // bit, 2)
        return pltpu.make_async_remote_copy(
            src_ref=small.at[level],
            dst_ref=small_in.at[level],
            send_sem=send_v.at[level],
            recv_sem=recv_v.at[level],
            device_id={"seq": partner},
            device_id_type=MESH,
        )

    spacing = (count - 4) // (levels + 1)
    seq_copies = to_all("seq", mine_ref.at[0], seq_in, send_s, recv_s)
    mp_copies = to_all("mp", mine_ref.at[1], mp_in, send_m, recv_m)
    settled = count + SKEW * (lax.axis_size("mp") // 2)

    def before(k):
        for level in range(levels + 1):

            @pl.when(k == 3 + level * spacing)
            def _():
                if level > 0:
                    exchange(level - 1).wait()
                    total = small[level - 1] + small_in[level - 1]
                    if level < levels:
                        small[level] = total
                    else:
                        small_out[...] = total
                if level < levels:
                    exchange(level).start()

        @pl.when(k == settled)
        def _():
            mine_ref[0, 0:1, :] = jnp.sum(acc_ref[...], axis=0, keepdims=True)
            mine_ref[0, 1:2, :] = jnp.sum(other_acc[...], axis=0, keepdims=True)
            seq_in[me] = mine_ref[0]
            for copy in seq_copies:
                copy.start()

        @pl.when(k == settled + 2)
        def _():
            for copy in seq_copies:
                copy.wait()
            mine_ref[1] = jnp.sum(seq_in[...], axis=0)
            mp_in[lax.axis_index("mp")] = mine_ref[1]
            for copy in mp_copies:
                copy.start()

        @pl.when(jnp.logical_and(lax.rem(k, 4) == 0, k // 4 < count // GROUP))
        def _():
            at = block(k // 4, size)

            def work(cols):
                part[at, cols] = matmul_back(grad_branch[at, :], w_branch[cols, :]) + matmul_back(
                    input_low[at, :], w_input[cols, :]
                )

            work(slice(None))

        @pl.when(k == SKEW * (lax.axis_size("mp") // 2))
        def _():
            for copy in loads[4:]:
                copy.wait()

    def root(c, slot, total):
        back = norm_grad(x_ref[block(c, CHUNK), :], gain_ref[...], total, acc_ref)
        out[slot] = own_grad_ref[block(c // 2, CHUNK), :] + back

    def store(c, slot):
        return local(out.at[slot], grad_out.at[block(c, CHUNK)], store_sem.at[slot])

    def arrive(c, slot):
        store(c, slot).start(priority=1)

    def leave(c, slot):
        store(c, slot).wait()

    line_sum("mp", count, count, part, inbox, out, sems, before, root, arrive, leave)

    for copy in mp_copies:
        copy.wait()
    norm_ref[...] = jnp.sum(mp_in[...], axis=0)


def enter_all(axes):
    barrier = pltpu.get_barrier_semaphore()
    count = 0
    for axis in axes:
        size, me = lax.axis_size(axis), lax.axis_index(axis)
        for d in range(1, size):
            pl.semaphore_signal(
                barrier, 1, device_id={axis: lax.rem(me + d, size)}, device_id_type=MESH
            )
        count += size - 1
    pl.semaphore_wait(barrier, count)


def cost(micros):
    return pl.CostEstimate(flops=int(micros * 1e9), bytes_accessed=1 << 20, transcendentals=0)


def nseq_levels():
    return (lax.axis_size("seq") - 1).bit_length()


def last_call(*args):
    x, grad_branch = args[1:3]
    rows, model = x.shape
    width = grad_branch.shape[1]
    lines = args[8].shape[0] + args[9].shape[0] + 2 * args[10].shape[0]
    levels = nseq_levels()
    dma = pltpu.SemaphoreType.DMA
    nseq, nmp = lax.axis_size("seq"), lax.axis_size("mp")
    return pl.pallas_call(
        last_kernel,
        out_shape=(shape((rows, model)), shape((TILE, model)), shape((lines, width))),
        in_specs=[HBM] * 6 + [VMEM] * 5,
        out_specs=(HBM,) + (VMEM,) * 2,
        scratch_shapes=line_scratch("mp", rows, model)
        + [
            pltpu.VMEM((rows // 2, model), F32),
            pltpu.VMEM((rows, model), F32),
            pltpu.VMEM((rows, width), BF16),
            pltpu.VMEM((rows, width), BF16),
            pltpu.VMEM((model, width), BF16),
            pltpu.VMEM((model, width), BF16),
            dma((6,)),
            dma((ring_size("mp"),)),
            pltpu.VMEM((TILE, model), F32),
            pltpu.VMEM((2, TILE, model), F32),
            pltpu.VMEM((nseq, TILE, model), F32),
            pltpu.VMEM((nmp, TILE, model), F32),
            dma((nseq - 1,)),
            dma((nseq - 1,)),
            dma((nmp - 1,)),
            dma((nmp - 1,)),
            pltpu.VMEM((levels, lines, width), F32),
            pltpu.VMEM((levels, lines, width), F32),
            dma((levels,)),
            dma((levels,)),
        ],
        compiler_params=params(4, 62),
        cost_estimate=cost(200),
        name="last_sums",
    )(*args)


def finish_kernel(
    heads,
    block_in,
    grad_in,
    mlp_in,
    rec_in,
    small_hbm,
    norm_hbm,
    decay_hbm,
    block_out,
    grad_out,
    w_gate_out,
    w_up_out,
    w_branch_out,
    w_input_out,
    w_down_out,
    w_out_out,
    gate_r_out,
    gate_i_out,
    taps_out,
    conv_bias_out,
    bias_r_out,
    bias_i_out,
    decay_out,
    norm_in_out,
    norm_mlp_out,
    state_out,
    conv_out,
    tall,
    mlp,
    rec,
    small_in,
    norm_in,
    raw_ref,
    load_sem,
    store_sem,
    extra_sem,
):
    local = pltpu.make_async_copy
    width = small_in.shape[1]
    kept = mlp.shape[2]
    late = rec.shape[2] - width
    size = grad_in.shape[0] // COPIES
    extra = [
        local(source, target, extra_sem.at[i])
        for i, (source, target) in enumerate(
            ((small_hbm, small_in), (norm_hbm, norm_in), (decay_hbm, raw_ref))
        )
    ]
    for copy in extra:
        copy.start()
    jobs = [(mlp_in, mlp, None), (rec_in, rec, None)]
    for j, (source, target) in enumerate(((block_in, block_out), (grad_in, grad_out))):
        for i in range(COPIES):
            at = slice(i * size, (i + 1) * size)
            jobs.append((source.at[at], tall.at[j, at], target.at[at]))
    loads = [local(source, held, load_sem.at[i]) for i, (source, held, _) in enumerate(jobs)]
    stores = [
        local(held, target, store_sem.at[i])
        for i, (held, target) in enumerate(
            [(held, target) for _, held, target in jobs[2:]]
            + [
                (mlp.at[0], w_gate_out.at[:, pl.ds(0, kept)]),
                (mlp.at[1], w_up_out.at[:, pl.ds(0, kept)]),
                (rec.at[0, :, pl.ds(width, late)], w_gate_out.at[:, pl.ds(kept, late)]),
                (rec.at[1, :, pl.ds(width, late)], w_up_out.at[:, pl.ds(kept, late)]),
                (rec.at[1, :, pl.ds(0, width)], w_branch_out),
                (rec.at[2, :, pl.ds(0, width)], w_input_out),
            ]
        )
    ]
    for copy in loads:
        copy.start()
    for copy in extra:
        copy.wait()
    taps, seqs, edge = taps_out.shape[0], state_out.shape[0], conv_out.shape[0]
    head = gate_r_out.shape[1]
    decay = small_in[0:1, :].reshape(width) * (RATE_SCALE * jax.nn.sigmoid(-raw_ref[...]))
    decay_out[...] = decay
    bias_r_out[...] = small_in[1:2, :].reshape(width)
    bias_i_out[...] = small_in[2:3, :].reshape(width)
    conv_bias_out[...] = small_in[3:4, :].reshape(width)
    taps_out[...] = small_in[4 : 4 + taps, :]
    begin = 4 + taps
    state_out[...] = small_in[begin : begin + seqs, :]
    for s in range(seqs):
        end = begin + seqs + (s + 1) * TILE
        for k in range(edge):
            conv_out[k, s : s + 1, :] = small_in[end - edge + k : end - edge + k + 1, :]
    begin += seqs + seqs * TILE
    for i, target in enumerate((gate_r_out, gate_i_out)):
        line = small_in[begin + i * head : begin + (i + 1) * head, :]
        for h in range(heads):
            turned = line if h == 0 else pltpu.roll(line, width - h * head, 1)
            target[h] = turned[:, :head]
    norm_in_out[...] = norm_in[0:1, :].reshape(norm_in.shape[1])
    norm_mlp_out[...] = norm_in[1:2, :].reshape(norm_in.shape[1])
    loads[0].wait()
    loads[1].wait()
    for copy in stores[2 * COPIES :]:
        copy.start()
    w_down_out[:kept, :] = mlp[2].T
    w_down_out[kept:, :] = rec[2, :, width:].T
    w_out_out[...] = rec[0, :, :width].T
    for i in range(2 * COPIES):
        loads[2 + i].wait()
        stores[i].start()
    for copy in stores:
        copy.wait()


def finish_call(seqs, heads, head, edge, *args):
    _, stream_grad, mlp_grads, rec_grads, small, norms, decay = args
    rows, model = stream_grad.shape
    own, kept = mlp_grads.shape[1:]
    width = small.shape[1]
    hidden = kept + rec_grads.shape[2] - width
    taps = edge + 1
    line = shape((width,))
    tall = shape((rows, model))
    return pl.pallas_call(
        functools.partial(finish_kernel, heads),
        out_shape=(
            tall,
            tall,
            shape((own, hidden)),
            shape((own, hidden)),
            shape((own, width)),
            shape((own, width)),
            shape((hidden, own)),
            shape((width, own)),
            shape((heads, head, head)),
            shape((heads, head, head)),
            shape((taps, width)),
            line,
            line,
            line,
            line,
            shape((model,)),
            shape((model,)),
            shape((seqs, width)),
            shape((edge, seqs, width)),
        ),
        in_specs=[HBM] * 4 + [PINNED] * 3,
        out_specs=(HBM,) * 6 + (VMEM,) * 13,
        scratch_shapes=[
            pltpu.VMEM((2, rows, model), F32),
            pltpu.VMEM(mlp_grads.shape, F32),
            pltpu.VMEM(rec_grads.shape, F32),
            pltpu.VMEM(small.shape, F32),
            pltpu.VMEM(norms.shape, F32),
            pltpu.VMEM(decay.shape, F32),
            pltpu.SemaphoreType.DMA((2 + 2 * COPIES,)),
            pltpu.SemaphoreType.DMA((6 + 2 * COPIES,)),
            pltpu.SemaphoreType.DMA((3,)),
        ],
        compiler_params=pltpu.CompilerParams(vmem_limit_bytes=63 << 20),
        cost_estimate=cost(15),
        name="finish",
    )(*args)


def params(collective, megabytes=60):
    return pltpu.CompilerParams(
        collective_id=collective, has_side_effects=True, vmem_limit_bytes=megabytes << 20
    )


def shape(dims, dtype=F32):
    return jax.ShapeDtypeStruct(dims, dtype)


def recurrence_forward(span, *args):
    x, w_input = args[:2]
    rows, model = x.shape
    seqs, width = rows // span, w_input.shape[1]
    devices = lax.axis_size("seq")
    dma = pltpu.SemaphoreType.DMA
    groups = seqs // 2
    columns = (width // LANES, rows, LANES)
    spaced = (width // LANES, seqs * (span + TILE), LANES)
    padded = (seqs, span + TILE, width)
    return pl.pallas_call(
        functools.partial(forward_kernel, span),
        out_shape=(
            shape((rows, model), BF16),
            shape((rows, width)),
            shape(padded),
            shape((rows, 2 * width)),
            shape(columns),
            shape((rows, width), BF16),
            shape((seqs, width)),
            shape((devices, 2, seqs, width)),
            shape((width, 2 * width), BF16),
            shape((TILE, width)),
            shape(((seqs + 1) * TILE, width)),
        ),
        in_specs=[HBM] * 3 + [VMEM] * 8 + [pl.BlockSpec(memory_space=pltpu.SMEM)] + [VMEM] * 2,
        out_specs=(HBM,) * 5 + (VMEM,) * 6,
        scratch_shapes=[
            pltpu.VMEM((rows, model), F32),
            pltpu.VMEM((model, width), BF16),
            pltpu.VMEM((model, width), BF16),
            pltpu.VMEM((rows, model), BF16),
            pltpu.VMEM((rows, width), F32),
            pltpu.VMEM(padded, F32),
            pltpu.VMEM((rows, 2 * width), F32),
            pltpu.VMEM(columns, F32),
            pltpu.VMEM((rows, width), F32),
            pltpu.VMEM(spaced, F32),
            pltpu.VMEM(spaced, F32),
            pltpu.VMEM((2, span, width), F32),
            pltpu.VMEM((seqs, TILE, width), F32),
            pltpu.VMEM((seqs, TILE, width), F32),
            pltpu.VMEM((2, seqs, width), F32),
            dma((groups + 2,)),
            dma((4,)),
            dma((groups,)),
            dma((devices - 1,)),
            dma((devices - 1,)),
            dma((1,)),
            dma((1,)),
        ],
        compiler_params=params(0),
        cost_estimate=cost(50),
        name="recurrence_forward",
    )(*args)


def widen(array, width):
    short = width - array.shape[-1]
    if short == 0:
        return array
    return jnp.pad(array, [(0, 0)] * (array.ndim - 1) + [(0, short)])


def per_device(
    stream,
    norm_in,
    w_branch,
    w_input,
    conv_kernel,
    conv_bias,
    gate_r,
    bias_r,
    gate_i,
    bias_i,
    decay_param,
    w_out,
    norm_mlp,
    w_gate,
    w_up,
    w_down,
    state_init,
    conv_init,
    fresh_rows,
    out_grad,
):
    seqs, span, model = stream.shape
    channels = w_branch.shape[1]
    mlp_dev = w_gate.shape[1]
    heads, head_width = gate_r.shape[:2]
    taps = conv_kernel.shape[0]
    edge = taps - 1
    rows = seqs * span
    devices = lax.axis_size("seq")
    position = lax.axis_index("seq")
    width = -(-channels // 128) * 128

    flat_in = stream.reshape(rows, model)
    flat_grad = out_grad.reshape(rows, model)
    w_branch_p = widen(w_branch, width)
    w_input_p = widen(w_input, width)
    w_out_p = jnp.pad(w_out, ((0, width - channels), (0, 0))) if width > channels else w_out
    taps_p = widen(conv_kernel, width)
    def line(value):
        return widen(value, width)

    (
        normed,
        branch,
        padded,
        pre,
        hidden,
        mixed,
        carry,
        sums,
        gates,
        rates,
        ends,
    ) = recurrence_forward(
        span,
        flat_in,
        w_input_p,
        w_branch_p,
        norm_in[None],
        taps_p,
        line(conv_bias),
        line(decay_param),
        line(bias_r),
        line(bias_i),
        gate_r,
        gate_i,
        fresh_rows,
        widen(state_init, width),
        widen(jnp.swapaxes(conv_init, 0, 1), width),
    )
    made = middle_call(mixed, w_out_p, flat_in, flat_grad, norm_mlp[None], w_gate, w_up, w_down)
    block_part, resid_low, own_grad, mlp_grads, rest, own, norm_mlp_acc = made[5:]
    mlp_grads = lax.psum_scatter(mlp_grads, "seq", scatter_dimension=1, tiled=True)
    block_out, rec_grads, grad_branch, input_low, acc, blocks = backward_call(
        span,
        heads,
        head_width,
        block_part,
        own,
        resid_low,
        w_out_p,
        branch,
        hidden,
        pre,
        padded,
        normed,
        mixed,
        rest,
        gates,
        carry,
        sums,
        taps_p,
        rates,
    )

    rec_grads, grad_branch, mlp_grads = lax.optimization_barrier(
        (rec_grads, grad_branch, mlp_grads)
    )
    rec_grads = lax.psum_scatter(rec_grads, "seq", scatter_dimension=1, tiled=True)

    stream_grad, norm_grads, small = last_call(
        own_grad,
        flat_in,
        grad_branch,
        input_low,
        w_branch_p,
        w_input_p,
        norm_in[None],
        norm_mlp_acc,
        acc,
        ends,
        blocks,
    )
    (
        block_out,
        stream_grad,
        w_gate_grad,
        w_up_grad,
        w_branch_grad,
        w_input_grad,
        w_down_grad,
        w_out_grad,
        gate_r_grad,
        gate_i_grad,
        taps_grad,
        conv_bias_grad,
        bias_r_grad,
        bias_i_grad,
        decay_grad,
        norm_in_grad,
        norm_mlp_grad,
        final_state,
        final_conv,
    ) = finish_call(
        seqs,
        heads,
        head_width,
        edge,
        block_out,
        stream_grad,
        mlp_grads,
        rec_grads,
        small,
        norm_grads,
        line(decay_param),
    )
    return (
        block_out.reshape(stream.shape),
        stream_grad.reshape(stream.shape),
        norm_in_grad,
        w_branch_grad[:, :channels],
        w_input_grad[:, :channels],
        taps_grad[:, :channels],
        conv_bias_grad[:channels],
        gate_r_grad,
        bias_r_grad[:channels],
        gate_i_grad,
        bias_i_grad[:channels],
        decay_grad[:channels],
        w_out_grad[:channels],
        norm_mlp_grad,
        w_gate_grad,
        w_up_grad,
        w_down_grad,
        final_state[:, :channels],
        jnp.swapaxes(final_conv, 0, 1)[:, :, :channels],
    )


def solution(mesh):
    seq_rows = P(None, "seq", None)
    columns = P(None, "mp")
    channel = P("mp")
    return jax.shard_map(
        per_device,
        mesh=mesh,
        in_specs=(
            seq_rows,
            P(),
            columns,
            columns,
            columns,
            channel,
            P("mp", None, None),
            channel,
            P("mp", None, None),
            channel,
            channel,
            P("mp", None),
            P(),
            columns,
            columns,
            P("mp", None),
            columns,
            P(None, None, "mp"),
            P(),
            seq_rows,
        ),
        out_specs=(
            seq_rows,
            seq_rows,
            P(),
            P("seq", "mp"),
            P("seq", "mp"),
            columns,
            channel,
            P("mp", None, None),
            channel,
            P("mp", None, None),
            channel,
            channel,
            P("mp", "seq"),
            P(),
            P("seq", "mp"),
            P("seq", "mp"),
            P("mp", "seq"),
            columns,
            P(None, None, "mp"),
        ),
        check_vma=False,
    )
```

```python
import functools

import jax
import jax.numpy as jnp
from jax import lax
from jax.experimental import pallas as pl
from jax.experimental.pallas import tpu as pltpu
from jax.sharding import PartitionSpec as P

MESH = pl.DeviceIdType.MESH
RATE_SCALE = 8.0
EPS = 1e-06
GELU_C = 0.7978845608028654
GELU_K = 0.044715
CONTRACT_ROWS = (((0,), (0,)), ((), ()))
CONTRACT_LAST = (((1,), (1,)), ((), ()))
TILE = 8
LANES = 128
ROWS = 32
CHUNK = 16
SKEW = 2
GROUP = 16
WEIGHT_STEPS = 8
COPIES = 8
LATER = 6
F32 = jnp.float32
BF16 = jnp.bfloat16
VMEM = pl.BlockSpec(memory_space=pltpu.VMEM)
HBM = pl.BlockSpec(memory_space=pl.ANY)
PINNED = pl.BlockSpec(memory_space=pltpu.HBM)


def dot(a, b):
    return jnp.dot(a, b, preferred_element_type=F32)


def matmul_back(a, b):
    return lax.dot_general(a, b, CONTRACT_LAST, preferred_element_type=F32)


def block(i, size):
    return pl.ds(pl.multiple_of(i * size, size), size)


def gelu(x):
    t = jnp.tanh(GELU_C * (x + GELU_K * (x * x * x)))
    return 0.5 * x * (1.0 + t)


def gelu_both(x):
    x2 = x * x
    t = jnp.tanh(GELU_C * (x + GELU_K * (x2 * x)))
    half = 0.5 * (1.0 + t)
    slope = half + 0.5 * x * (1.0 - t * t) * (GELU_C * (1.0 + (3.0 * GELU_K) * x2))
    return x * half, slope


def one_minus_square(log_a, a):
    y = 2.0 * log_a
    s = 1.0 + y * (1.0 / 8.0)
    for k in (7, 6, 5, 4, 3, 2):
        s = 1.0 + (y * (1.0 / k)) * s
    return jnp.where(y > -0.35, -y * s, 1.0 - a * a)


def get(ref, at):
    return jnp.concatenate([ref[j, at, :] for j in range(ref.shape[0])], axis=-1)


def put(ref, at, value):
    for j in range(ref.shape[0]):
        ref[j, at, :] = value[:, j * LANES : (j + 1) * LANES]


def to_all(axis, src, slots, send, recv):
    size, me = lax.axis_size(axis), lax.axis_index(axis)
    return [
        pltpu.make_async_remote_copy(
            src_ref=src,
            dst_ref=slots.at[me],
            send_sem=send.at[d - 1],
            recv_sem=recv.at[d - 1],
            device_id={axis: lax.rem(me + d, size)},
            device_id_type=MESH,
        )
        for d in range(1, size)
    ]


def to_one(axis, distance, src, dst, send, recv):
    size, me = lax.axis_size(axis), lax.axis_index(axis)
    return pltpu.make_async_remote_copy(
        src_ref=src,
        dst_ref=dst,
        send_sem=send,
        recv_sem=recv,
        device_id={axis: lax.rem(me + distance + size, size)},
        device_id_type=MESH,
    )


def spread_gates(blocks_ref, out_ref, start, width):
    heads, size = blocks_ref.shape[:2]
    for h in range(heads):
        block_h = blocks_ref[h].astype(F32)
        parts = [block_h]
        if h > 0:
            parts.insert(0, jnp.zeros((size, h * size), F32))
        if width > (h + 1) * size:
            parts.append(jnp.zeros((size, width - (h + 1) * size), F32))
        row = jnp.concatenate(parts, axis=1).astype(BF16)
        out_ref[h * size : (h + 1) * size, start : start + width] = row
    if width > heads * size:
        rest = jnp.zeros((width - heads * size, width), BF16)
        out_ref[heads * size : width, start : start + width] = rest


def forward_kernel(
    span,
    x_in,
    w_input_in,
    w_branch_in,
    gain_ref,
    taps_ref,
    conv_bias_ref,
    decay_ref,
    bias_r_ref,
    bias_i_ref,
    gate_r_ref,
    gate_i_ref,
    fresh_ref,
    state_ref,
    conv_init_ref,
    normed_out,
    branch_out,
    pad_out,
    pre_out,
    hidden_out,
    mixed_ref,
    carry_ref,
    sums_ref,
    gates_ref,
    vec_ref,
    ends_ref,
    x_ref,
    w_input_ref,
    w_branch_ref,
    normed_ref,
    branch_ref,
    pad_ref,
    pre_ref,
    hidden_ref,
    act_ref,
    a_ref,
    b_ref,
    conv_ref,
    tail_ref,
    tail_in,
    mine_ref,
    load_sem,
    store_sem,
    normed_sem,
    send1,
    recv1,
    send_t,
    recv_t,
):
    seqs = state_ref.shape[0]
    width = taps_ref.shape[1]
    taps = taps_ref.shape[0]
    rows = seqs * span
    devices, me = lax.axis_size("seq"), lax.axis_index("seq")
    local = pltpu.make_async_copy
    pitch = a_ref.shape[1] // seqs
    group = 2 * span
    groups = rows // group

    def x_load(g):
        at = block(g, group)
        return local(x_in.at[at], x_ref.at[at], load_sem.at[g])

    weight_loads = [
        local(w_input_in, w_input_ref, load_sem.at[groups]),
        local(w_branch_in, w_branch_ref, load_sem.at[groups + 1]),
    ]
    x_load(0).start()
    weight_loads[0].start()
    for g in range(1, groups):
        x_load(g).start()
    weight_loads[1].start()

    enter_all(("seq",))
    spread_gates(gate_r_ref, gates_ref, 0, width)
    spread_gates(gate_i_ref, gates_ref, width, width)
    vec_ref[0:1, :] = conv_bias_ref[...].reshape(1, width)
    vec_ref[1:2, :] = jax.nn.softplus(-decay_ref[...].reshape(1, width))
    bias_r = bias_r_ref[...].reshape(1, width)
    bias_i = bias_i_ref[...].reshape(1, width)
    keep = [1.0 - fresh_ref[s].astype(F32) for s in range(seqs)]

    def normed_store(g):
        at = block(g, group)
        return local(normed_ref.at[at], normed_out.at[at], normed_sem.at[g])

    def norm(g):
        x_load(g).wait()
        for q in range(group // CHUNK):
            at = slice(g * group + q * CHUNK, g * group + (q + 1) * CHUNK)
            x = x_ref[at, :]
            normed_ref[at, :] = (x * mean_square(x) * gain_ref[...]).astype(BF16)

    norm(0)
    weight_loads[0].wait()
    for g in range(groups):
        if g + 1 < groups:
            norm(g + 1)
        conv = dot(normed_ref[slice(g * group, (g + 1) * group), :], w_input_ref[...])
        for j in range(group // span):
            pad_ref[g * (group // span) + j, pl.ds(TILE, span), :] = conv[
                j * span : (j + 1) * span
            ]
    for g in range(groups):
        normed_store(g).start()

    for s in range(seqs):
        tail_ref[s] = pad_ref[s, pl.ds(span, TILE), :]
    tail_copy = to_one("seq", 1, tail_ref, tail_in, send_t.at[0], recv_t.at[0])
    tail_copy.start()
    weight_loads[1].wait()

    def branch(g):
        branch_ref[block(g, group), :] = dot(normed_ref[block(g, group), :], w_branch_ref[...])

    @pl.loop(0, groups // 2)
    def _(g):
        branch(g)

    stores = [
        local(source, target, store_sem.at[i])
        for i, (source, target) in enumerate(
            (
                (branch_ref, branch_out),
                (pad_ref, pad_out),
                (pre_ref, pre_out),
                (hidden_ref, hidden_out),
            )
        )
    ]
    tail_copy.wait()
    lead = jnp.zeros((TILE - taps + 1, width), F32)
    for s in range(seqs):
        initial = jnp.concatenate(
            [lead] + [conv_init_ref[k, s : s + 1, :] * keep[s] for k in range(taps - 1)], axis=0
        )
        pad_ref[s, pl.ds(0, TILE), :] = jnp.where(me == 0, initial, tail_in[s])
    stores[1].start()

    def gates(s, slot):
        for q in range(span // ROWS):
            part = pad_ref[s, pl.ds(q * ROWS, ROWS + TILE), :]
            total = vec_ref[0:1, :]
            for k in range(taps):
                first = TILE - (taps - 1) + k
                total = total + taps_ref[k : k + 1, :] * part[first : first + ROWS]
            conv_ref[slot, pl.ds(q * ROWS, ROWS), :] = total

        pre = dot(conv_ref[slot].astype(BF16), gates_ref[...])
        pre_ref[block(s, span), :width] = pre[:, :width] + bias_r
        pre_ref[block(s, span), width:] = pre[:, width:] + bias_i
        for q in range(span // ROWS):
            rows_q = slice(q * ROWS, (q + 1) * ROWS)
            conv = conv_ref[slot, pl.ds(q * ROWS, ROWS), :]
            recall = jax.nn.sigmoid(pre[rows_q, :width] + bias_r)
            gate = jax.nn.sigmoid(pre[rows_q, width:] + bias_i)
            log_a = (-RATE_SCALE * vec_ref[1:2, :]) * recall
            a = jnp.exp(log_a)
            spaced = pl.ds(pl.multiple_of(s * pitch + q * ROWS, TILE), ROWS)
            put(a_ref, spaced, a)
            put(b_ref, spaced, jnp.sqrt(one_minus_square(log_a, a)) * gate * conv)

    per = seqs // (groups - groups // 2)

    @pl.loop(0, groups - groups // 2)
    def _(i):
        branch(groups // 2 + i)
        for j in range(per):
            gates(i * per + j, j % 2)

    stores[0].start()
    stores[2].start()

    def at_time(ref, t):
        return get(ref, pl.ds(t, seqs, stride=pitch))

    def step(t, value):
        prod, state = value
        a = at_time(a_ref, t)
        return prod * a, a * state + at_time(b_ref, t)

    ones = jnp.ones((seqs, width), F32)
    prod, state = lax.fori_loop(0, span, step, (ones, jnp.zeros_like(ones)), unroll=8)
    mine_ref[0] = prod
    mine_ref[1] = state
    sums_ref[me] = mine_ref[...]
    copies = to_all("seq", mine_ref, sums_ref, send1, recv1)
    for copy in copies:
        copy.start()

    @pl.loop(0, rows // ROWS, unroll=2)
    def _(q):
        at = block(q, ROWS)
        act_ref[at, :] = gelu(branch_ref[at, :])

    for copy in copies:
        copy.wait()

    def carry_step(j, carry):
        both = sums_ref[j]
        return jnp.where(j < me, both[0] * carry + both[1], carry)

    start = jnp.concatenate([state_ref[s : s + 1, :] * keep[s] for s in range(seqs)], axis=0)
    carry = lax.fori_loop(0, devices - 1, carry_step, start)
    carry_ref[...] = carry

    def final(t, state):
        state = at_time(a_ref, t) * state + at_time(b_ref, t)
        put(hidden_ref, pl.ds(t, seqs, stride=span), state)
        return state

    last = lax.fori_loop(0, span, final, carry, unroll=8)
    stores[3].start()
    ends_ref[0:seqs, :] = jnp.where(me == devices - 1, last, 0.0)
    for s in range(seqs):
        ends_ref[(s + 1) * TILE : (s + 2) * TILE, :] = jnp.where(
            me == devices - 1, pad_ref[s, pl.ds(span, TILE), :], 0.0
        )

    @pl.loop(0, rows // ROWS, unroll=2)
    def _(q):
        at = block(q, ROWS)
        mixed_ref[at, :] = (get(hidden_ref, at) * act_ref[at, :]).astype(BF16)

    for copy in stores:
        copy.wait()
    for g in range(groups):
        normed_store(g).wait()


def backward_kernel(
    span,
    heads,
    block_part_in,
    own_in,
    low_in,
    w_out_in,
    branch_in,
    hidden_in,
    pre_in,
    pad_in,
    normed_in,
    mixed_in,
    rest_in,
    gates_in,
    carry_ref,
    sums_ref,
    taps_ref,
    vec_ref,
    block_out,
    rec_out,
    grad_branch_out,
    input_out,
    acc_ref,
    blocks_ref,
    part,
    inbox,
    out,
    send_up,
    send_down,
    recv_up,
    recv_down,
    own_ref,
    resid_low,
    w_out_ref,
    branch_ref,
    hidden_ref,
    pre_ref,
    pad_ref,
    normed_ref,
    mixed_ref,
    a_ref,
    gd_ref,
    grad_ref,
    direct_ref,
    gpad_ref,
    heads_ref,
    low_ref,
    gates_grad,
    stage_ref,
    mine_ref,
    entries_ref,
    head_ref,
    head_in,
    load_sem,
    part_sem,
    store_sem,
    stage_sem,
    send1,
    recv1,
    send_t,
    recv_t,
    gates_ref,
    grad_branch_ref,
    input_ref,
    give_sem,
):
    seqs, width = carry_ref.shape
    taps = taps_ref.shape[0]
    rows = seqs * span
    devices, me = lax.axis_size("seq"), lax.axis_index("seq")
    n, z = lax.axis_size("mp"), lax.axis_index("mp")
    chunks = rows // CHUNK
    size = GROUP * CHUNK
    held = part.shape[0] // size
    groups = chunks // GROUP
    sems = (send_up, send_down, recv_up, recv_down)
    local = pltpu.make_async_copy

    def part_load(g):
        slot = lax.rem(g, held)
        return local(block_part_in.at[block(g, size)], part.at[block(slot, size)], part_sem.at[slot])

    loads = [
        local(source, target, load_sem.at[i])
        for i, (source, target) in enumerate(
            (
                (own_in, own_ref),
                (low_in, resid_low),
                (w_out_in, w_out_ref),
                (pre_in, pre_ref),
                (branch_in, branch_ref),
                (hidden_in, hidden_ref),
                (pad_in, pad_ref),
                (mixed_in, mixed_ref),
                (normed_in, normed_ref),
                (gates_in, gates_ref),
            )
        )
    ]
    part_load(0).start()
    for copy in loads[:6]:
        copy.start(priority=1)
    for g in range(1, held):
        part_load(g).start()
    for copy in loads[6:]:
        copy.start(priority=1)
    acc_ref[...] = jnp.zeros_like(acc_ref)
    enter_all(("seq", "mp"))

    pitch = a_ref.shape[1] // seqs

    def spaced(s, q):
        return pl.ds(pl.multiple_of(s * pitch + q * ROWS, TILE), ROWS)

    def decay(at):
        recall = jax.nn.sigmoid(pre_ref[at, :width])
        log_a = (-RATE_SCALE * vec_ref[1:2, :]) * recall
        return recall, log_a, jnp.exp(log_a)

    def piece_direct(s):
        @pl.when(s == 0)
        def _():
            for copy in loads[1:6]:
                copy.wait()

        grad_ref[...] = matmul_back(resid_low[block(s, span), :], w_out_ref[...])

        @pl.loop(0, span // ROWS)
        def _(q):
            at = block(s * (span // ROWS) + q, ROWS)
            put(a_ref, spaced(s, q), decay(at)[2])
            act, slope = gelu_both(branch_ref[at, :])
            grad = grad_ref[block(q, ROWS), :]
            put(gd_ref, spaced(s, q), grad * act)
            grad_branch_ref[at, :] = (grad * get(hidden_ref, at) * slope).astype(BF16)

    def at_time(ref, t):
        return get(ref, pl.ds(t, seqs, stride=pitch))

    zero = jnp.zeros((seqs, width), F32)
    entry_copies = to_all("seq", mine_ref, entries_ref, send1, recv1)

    def piece_entry(_):
        def step(k, through):
            t = span - 1 - k
            return at_time(a_ref, t) * (at_time(gd_ref, t) + through)

        mine_ref[...] = lax.fori_loop(0, span, step, zero, unroll=8)
        entries_ref[me] = mine_ref[...]
        for copy in entry_copies:
            copy.start()

    def piece_state(_):
        for copy in entry_copies:
            copy.wait()

        def back_step(k, through):
            j = devices - 1 - k
            return jnp.where(j > me, entries_ref[j] + sums_ref[j, 0] * through, through)

        incoming = lax.fori_loop(0, devices - 1, back_step, zero)

        def final(k, through):
            t = span - 1 - k
            grad = at_time(gd_ref, t) + through
            put(gd_ref, pl.ds(t, seqs, stride=pitch), grad)
            return at_time(a_ref, t) * grad

        lax.fori_loop(0, span, final, incoming, unroll=8)

    def add(k, value):
        acc_ref[k] += fold(value)

    parts = 2

    def piece_gates(i):
        s = i // parts
        quarters = span // ROWS // parts

        @pl.when(i == 0)
        def _():
            loads[6].wait()
            loads[9].wait()

        @pl.loop(lax.rem(i, parts) * quarters, (lax.rem(i, parts) + 1) * quarters)
        def _(q):
            at = block(s * (span // ROWS) + q, ROWS)
            part_rows = pad_ref[s, pl.ds(pl.multiple_of(q * ROWS, ROWS), ROWS + TILE), :]
            conv = vec_ref[0:1, :]
            for k in range(taps):
                first = TILE - (taps - 1) + k
                conv = conv + taps_ref[k : k + 1, :] * part_rows[first : first + ROWS]
            heads_ref[at, :] = conv.astype(BF16)
            recall, log_a, a = decay(at)
            gate = jax.nn.sigmoid(pre_ref[at, width:])
            square = one_minus_square(log_a, a)
            inverse = lax.rsqrt(square)
            root = jnp.sqrt(square)
            grad = get(gd_ref, spaced(s, q))
            hidden = get(hidden_ref, at)
            before_at = pl.multiple_of(jnp.maximum(s * span + q * ROWS - TILE, 0), TILE)
            earlier = get(hidden_ref, pl.ds(before_at, TILE))
            first_row = jnp.where(q == 0, carry_ref[pl.ds(s, 1), :], earlier[TILE - 1 :])
            place = lax.broadcasted_iota(jnp.int32, (ROWS, width), 0)
            prev = jnp.where(place == 0, first_row, pltpu.roll(hidden, 1, 0))
            grad_log = grad * a * (prev - gate * conv * a * inverse)
            through = grad_log * recall
            pre_r = through * (1.0 - recall) * (-RATE_SCALE * vec_ref[1:2, :])
            direct = grad * root * gate
            pre_i = direct * conv * (1.0 - gate)
            low_ref[at, :width] = pre_r.astype(BF16)
            low_ref[at, width:] = pre_i.astype(BF16)
            direct_ref[block(q, ROWS), :] = direct
            add(0, through)
            add(1, pre_r)
            add(2, pre_i)

        @pl.when(lax.rem(i, parts) == parts - 1)
        def _():
            whole = direct_ref[...] + matmul_back(low_ref[block(s, span), :], gates_ref[...])
            gpad_ref[s, pl.ds(0, span), :] = whole
            head_ref[s] = whole[:TILE]

    head_copy = to_one("seq", -1, head_ref, head_in, send_t.at[0], recv_t.at[0])

    def piece_head(_):
        head_copy.start()

    def piece_taps(i):
        for j in range(2):
            taps_of(2 * i + j)

    def taps_of(s):
        @pl.loop(0, span // ROWS)
        def _(q):
            at = pl.multiple_of(q * ROWS, ROWS)
            part_rows = pad_ref[s, pl.ds(at, ROWS + TILE), :]
            grad = gpad_ref[s, pl.ds(at, ROWS), :]
            add(3, grad)
            for k in range(taps):
                first = TILE - (taps - 1) + k
                add(4 + k, grad * part_rows[first : first + ROWS])

    def piece_tail(_):
        head_copy.wait()
        for s in range(seqs):
            gpad_ref[s, pl.ds(span, TILE), :] = jnp.where(me == devices - 1, 0.0, head_in[s])

    def piece_input(i):
        for j in range(2):
            input_of(2 * i + j)

    def input_of(s):
        @pl.loop(0, span // ROWS)
        def _(q):
            part_rows = gpad_ref[s, pl.ds(pl.multiple_of(q * ROWS, ROWS), ROWS + TILE), :]
            total = taps_ref[taps - 1 : taps, :] * part_rows[0:ROWS]
            for k in range(taps - 1):
                first = taps - 1 - k
                total = total + taps_ref[k : k + 1, :] * part_rows[first : first + ROWS]
            input_ref[block(s * (span // ROWS) + q, ROWS), :] = total.astype(BF16)

    def contract(left, right):
        return lax.dot_general(left, right, CONTRACT_ROWS, preferred_element_type=F32)

    head = blocks_ref.shape[0]

    gives = [
        local(grad_branch_ref, grad_branch_out, give_sem.at[0]),
        local(input_ref, input_out, give_sem.at[1]),
    ]

    def piece_gates_grad(i):
        @pl.when(i == 0)
        def _():
            for copy in gives:
                copy.start(priority=1)

        @pl.when(i == 0)
        def _():
            gates_grad[...] = contract(heads_ref[...], low_ref[:, :width])

        @pl.when(i == 1)
        def _():
            gates_grad[...] = contract(heads_ref[...], low_ref[:, width:])

        place = lax.broadcasted_iota(jnp.int32, (head, width), 1)
        line = jnp.zeros((head, width), F32)
        for h in range(heads):
            row = gates_grad[h * head : (h + 1) * head, :]
            inside = jnp.logical_and(place >= h * head, place < (h + 1) * head)
            line = jnp.where(inside, row, line)

        for j in range(2):

            @pl.when(i == j)
            def _():
                blocks_ref[:, j * width : (j + 1) * width] = line

    tall = resid_low.shape[1] // WEIGHT_STEPS

    def stage_store(i):
        at = block(lax.rem(i, WEIGHT_STEPS), tall)
        slot = lax.rem(i, 2)
        return local(
            stage_ref.at[slot],
            rec_out.at[i // WEIGHT_STEPS, at, pl.ds(0, width)],
            stage_sem.at[slot],
        )

    def piece_weights(i):
        @pl.when(i == 0)
        def _():
            loads[7].wait()
            loads[8].wait()

        @pl.loop(2 * i, 2 * i + 2)
        def _(j):
            weight_of(j)

    def weight_of(i):
        @pl.when(i >= 2)
        def _():
            stage_store(i - 2).wait()

        at = block(lax.rem(i, WEIGHT_STEPS), tall)
        slot = lax.rem(i, 2)
        for which, (left, right) in enumerate(
            ((resid_low, mixed_ref), (normed_ref, grad_branch_ref), (normed_ref, input_ref))
        ):
            @pl.when(i // WEIGHT_STEPS == which)
            def _():
                stage_ref[slot] = contract(left[:, at], right[...])

        stage_store(i).start(priority=1)

    weights = 3 * WEIGHT_STEPS
    plan = []
    begin = 3
    for work, times, gap in (
        (piece_direct, seqs, 0),
        (piece_entry, 1, 1),
        (piece_state, 1, 0),
        (piece_gates, parts * seqs, 0),
        (piece_head, 1, 0),
        (piece_taps, seqs // 2, 0),
        (piece_tail, 1, 0),
        (piece_input, seqs // 2, 0),
        (piece_gates_grad, 2, 0),
        (piece_weights, weights // 2, 0),
    ):
        plan.append((work, begin, times))
        begin += times + gap

    def run(step):
        for work, first, times in plan:
            @pl.when(jnp.logical_and(step >= first, step < first + times))
            def _():
                work(step - first)

    def before(k):
        @pl.when(k == SKEW * (n // 2))
        def _():
            loads[0].wait()

        @pl.when(jnp.logical_and(lax.rem(k, GROUP) == 0, k < chunks))
        def _():
            part_load(k // GROUP).wait()

        g = (k - out.shape[0]) // GROUP - 1 + held

        @pl.when(
            jnp.logical_and(
                jnp.logical_and(k >= out.shape[0] + GROUP, lax.rem(k - out.shape[0], GROUP) == 0),
                g < groups,
            )
        )
        def _():
            part_load(g).start(priority=1)

        run(k)

    def root(c, slot, total):
        out[slot] = own_ref[block(c // 2, CHUNK), :] + total

    def store(c, slot):
        return local(out.at[slot], block_out.at[block(c, CHUNK)], store_sem.at[slot])

    def arrive(c, slot):
        store(c, slot).start(priority=1)

    def leave(c, slot):
        store(c, slot).wait()

    line_sum(
        "mp", chunks, held * GROUP, part, inbox, out, sems, before, root, arrive, leave
    )

    @pl.loop(chunks + out.shape[0], max(begin, chunks + out.shape[0]))
    def _(k):
        run(k)

    for copy in gives:
        copy.wait()
    stage_store(weights - 2).wait()
    stage_store(weights - 1).wait()


def backward_call(span, heads, head, *args):
    block_part = args[0]
    low, w_out, branch, hidden, pre, padded, normed, mixed, rest, gates = args[2:12]
    carry, sums, taps = args[12:15]
    rows, model = block_part.shape
    seqs, width = carry.shape
    devices = lax.axis_size("seq")
    ring = ring_size("mp")
    held = 3 * GROUP * CHUNK
    dma = pltpu.SemaphoreType.DMA
    columns = pltpu.VMEM((width // LANES, seqs * (span + TILE), LANES), F32)
    return pl.pallas_call(
        functools.partial(backward_kernel, span, heads),
        out_shape=(
            shape((rows, model)),
            shape(rest.shape),
            shape((rows, width), BF16),
            shape((rows, width), BF16),
            shape((4 + taps.shape[0], TILE, width)),
            shape((head, 2 * width)),
        ),
        in_specs=[HBM] * 12 + [VMEM] * 4,
        input_output_aliases={10: 1},
        out_specs=(HBM,) * 4 + (VMEM,) * 2,
        scratch_shapes=line_scratch("mp", held, model)
        + [
            pltpu.VMEM((rows // 2, model), F32),
            pltpu.VMEM((rows, model), BF16),
            pltpu.VMEM((width, model), BF16),
            pltpu.VMEM((rows, width), F32),
            pltpu.VMEM(hidden.shape, F32),
            pltpu.VMEM(pre.shape, F32),
            pltpu.VMEM(padded.shape, F32),
            pltpu.VMEM((rows, model), BF16),
            pltpu.VMEM((rows, width), BF16),
            columns,
            columns,
            pltpu.VMEM((span, width), F32),
            pltpu.VMEM((span, width), F32),
            pltpu.VMEM((seqs, span + TILE, width), F32),
            pltpu.VMEM((rows, width), BF16),
            pltpu.VMEM((rows, 2 * width), BF16),
            pltpu.VMEM((width, width), F32),
            pltpu.VMEM((2, model // WEIGHT_STEPS, width), F32),
            pltpu.VMEM((seqs, width), F32),
            pltpu.VMEM((devices, seqs, width), F32),
            pltpu.VMEM((seqs, TILE, width), F32),
            pltpu.VMEM((seqs, TILE, width), F32),
            dma((10,)),
            dma((3,)),
            dma((ring,)),
            dma((2,)),
            dma((devices - 1,)),
            dma((devices - 1,)),
            dma((1,)),
            dma((1,)),
            pltpu.VMEM(gates.shape, BF16),
            pltpu.VMEM((rows, width), BF16),
            pltpu.VMEM((rows, width), BF16),
            dma((2,)),
        ],
        compiler_params=params(1, 63),
        cost_estimate=cost(200),
        name="backward",
    )(*args)


def line_sum(axis, total, period, part, inbox, out, sems, before, root, arrive, leave):
    send_up, send_down, recv_up, recv_down = sems
    parts = send_up.shape[0]
    columns = out.shape[2] // parts
    n, z = lax.axis_size(axis), lax.axis_index(axis)
    depth = n // 2
    ring = out.shape[0]

    def cols(p):
        return pl.ds(p * columns, columns)

    def root_of(c):
        return depth - 1 + lax.rem(c, 2)

    def up(c, step, side, p):
        slot = lax.rem(c, ring)
        return pltpu.make_async_remote_copy(
            src_ref=part.at[block(lax.rem(c, period), CHUNK), cols(p)],
            dst_ref=inbox.at[side, slot, :, cols(p)],
            send_sem=send_up.at[p, slot],
            recv_sem=recv_up.at[p, side, slot],
            device_id={axis: z + step},
            device_id_type=MESH,
        )

    def down(c, step, side, p):
        slot = lax.rem(c, ring)
        return pltpu.make_async_remote_copy(
            src_ref=out.at[slot, :, cols(p)],
            dst_ref=out.at[slot, :, cols(p)],
            send_sem=send_down.at[p, side, slot],
            recv_sem=recv_down.at[p, slot],
            device_id={axis: z + step},
            device_id_type=MESH,
        )

    inner = jnp.logical_and(z > 0, z < n - 1)

    @pl.loop(0, total + ring)
    def _(k):
        @pl.when(k >= ring)
        def _():
            c = k - ring
            r = root_of(c)
            step = jnp.where(z < r, 1, -1)
            side = jnp.where(z < r, 0, 1)

            @pl.when(z == r)
            def _():
                for p in range(parts):
                    down(c, -1, 0, p).wait_send()
                    down(c, 1, 1, p).wait_send()

            @pl.when(z != r)
            def _():
                for p in range(parts):
                    up(c, step, side, p).wait_send()

            @pl.when(jnp.logical_and(z != r, inner))
            def _():
                for p in range(parts):
                    down(c, -step, side, p).wait_send()

            leave(c, lax.rem(c, ring))

        before(k)

        for i in reversed(range(n + 1)):
            c = k - SKEW * i
            valid = jnp.logical_and(c >= 0, c < total)
            c = jnp.clip(c, 0, total - 1)
            at = block(lax.rem(c, period), CHUNK)
            slot = lax.rem(c, ring)
            r = root_of(c)
            step = jnp.where(z < r, 1, -1)
            side = jnp.where(z < r, 0, 1)
            if i > depth:
                here = jnp.logical_and(z != r, jnp.abs(z - r) == i - depth)

                @pl.when(jnp.logical_and(valid, here))
                def _():
                    for p in range(parts):
                        down(c, step, side, p).wait_recv()

                        @pl.when(inner)
                        def _():
                            down(c, -step, side, p).start()

                    arrive(c, slot)
            elif i == depth:

                @pl.when(jnp.logical_and(valid, z == r))
                def _():
                    for p in range(parts):
                        up(c, 1, 0, p).wait_recv()
                        up(c, -1, 1, p).wait_recv()
                    root(c, slot, part[at, :] + inbox[0, slot] + inbox[1, slot])
                    for p in range(parts):
                        down(c, -1, 0, p).start()
                        down(c, 1, 1, p).start()
                    arrive(c, slot)
            else:
                here = jnp.where(z < r, z, n - 1 - z) == i

                @pl.when(jnp.logical_and(valid, jnp.logical_and(z != r, here)))
                def _():
                    for p in range(parts):
                        if i > 0:
                            up(c, step, side, p).wait_recv()
                            part[at, cols(p)] += inbox[side, slot, :, cols(p)]
                        up(c, step, side, p).start()


def ring_size(axis):
    return SKEW * lax.axis_size(axis) + 4


def line_scratch(axis, rows, model, parts=2):
    dma = pltpu.SemaphoreType.DMA
    ring = ring_size(axis)
    return [
        pltpu.VMEM((rows, model), F32),
        pltpu.VMEM((2, ring, CHUNK, model), F32),
        pltpu.VMEM((ring, CHUNK, model), F32),
        dma((parts, ring)),
        dma((parts, 2, ring)),
        dma((parts, 2, ring)),
        dma((parts, ring)),
    ]


def mean_square(x):
    return lax.rsqrt(jnp.mean(x * x, axis=-1, keepdims=True) + EPS)


def nothing(*_):
    pass


def fold(value):
    total = value[0:TILE]
    for i in range(1, value.shape[0] // TILE):
        total = total + value[i * TILE : (i + 1) * TILE]
    return total


def norm_grad(value, gain, grad, acc_ref):
    q = mean_square(value)
    e = gain * grad
    acc_ref[...] += fold(grad * value * q)
    return q * e - value * (q * q * q) * jnp.mean(e * value, axis=-1, keepdims=True)


def middle_kernel(
    mixed_in,
    w_out_in,
    x_in,
    og_in,
    gain_ref,
    w_gate_in,
    w_up_in,
    w_down_in,
    normed_out,
    hidden_out,
    gate_out,
    up_out,
    glow_out,
    block_out,
    low_out,
    own_grad_out,
    weight_out,
    rest_out,
    own_out,
    acc_ref,
    part,
    inbox,
    out,
    send_up,
    send_down,
    recv_up,
    recv_down,
    mixed,
    w_out,
    w_gate,
    w_up,
    w_down,
    normed,
    rows_ref,
    og_ref,
    glow,
    gate_val,
    up_val,
    grad_hidden,
    hidden,
    grad_gate,
    grad_up,
    block_part,
    low,
    weight_sem,
    row_sem,
    og_sem,
    act_sem,
    low_sem,
    own_sem,
    again_sem,
    stage_sem,
    rest_sem,
    own_ref,
):
    n, z = lax.axis_size("mp"), lax.axis_index("mp")
    count = part.shape[0] // CHUNK
    size = GROUP * CHUNK
    groups = count // GROUP
    ring = out.shape[0]
    sems = (send_up, send_down, recv_up, recv_down)
    local = pltpu.make_async_copy

    loads = [
        local(source, target, weight_sem.at[i])
        for i, (source, target) in enumerate(
            (
                (mixed_in, mixed),
                (w_out_in, w_out),
                (w_gate_in, w_gate),
                (w_up_in, w_up),
                (w_down_in, w_down.at[slice(0, w_down_in.shape[0])]),
            )
        )
    ]
    for copy in loads:
        copy.start(priority=1)
    deep = w_down_in.shape[0]

    def og_load(g):
        return local(og_in.at[block(g, size)], og_ref, og_sem.at[0])

    og_load(0).start(priority=1)
    enter_all(("mp",))
    acc_ref[...] = jnp.zeros_like(acc_ref)
    loads[0].wait()
    loads[1].wait()

    def is_root(c):
        return z == n // 2 - 1 + lax.rem(c, 2)

    def row_load(source, c):
        slot = lax.rem(c, ring)
        at = block(lax.rem(c, count), CHUNK)
        return local(source.at[at], rows_ref.at[slot], row_sem.at[slot])

    acts = (
        (normed, normed_out),
        (glow, glow_out),
        (hidden, hidden_out),
        (grad_gate, gate_out),
        (grad_up, up_out),
        (block_part, block_out),
    )

    def act_store(i, g):
        source, target = acts[i]
        source = source.at[lax.rem(g, 2)] if i == 0 else source
        return local(source, target.at[block(g, size)], act_sem.at[i])

    def at_tick(k, first, work):
        g = (k - first) // GROUP

        @pl.when(
            jnp.logical_and(
                jnp.logical_and(k >= first, k < first + GROUP * groups),
                lax.rem(k - first, GROUP) == 0,
            )
        )
        def _():
            work(g)

    def project(g):
        def work(cols):
            part[block(g, size), cols] = dot(mixed[block(g, size), :], w_out[:, cols])

        work(slice(None))

    def piece_gate(g):
        @pl.when(g == 0)
        def _():
            for copy in loads[2:]:
                copy.wait()

        def work(cols):
            gate_val[:, cols] = dot(normed[lax.rem(g, 2)], w_gate[:, cols])

        work(slice(None))
        act_store(0, g).start(priority=1)

    def piece_up(g):
        def work(cols):
            up_val[:, cols] = dot(normed[lax.rem(g, 2)], w_up[:, cols])

        work(slice(None))

        @pl.when(g > 0)
        def _():
            for i in range(1, 6):
                act_store(i, g - 1).wait()

    def piece_low(g):
        og_load(g).wait()

        @pl.loop(0, size // ROWS)
        def _(q):
            glow[block(q, ROWS), :] = og_ref[block(q, ROWS), :].astype(BF16)

        @pl.when(g + 1 < groups)
        def _():
            og_load(g + 1).start(priority=1)

        act_store(1, g).start(priority=1)
        act_store(0, g).wait()

    def piece_hidden(g):
        def work(cols):
            grad_hidden[...] = matmul_back(glow[...], w_down[:deep, :])

        work(slice(None))

    def piece_act(g):
        @pl.loop(0, size // CHUNK)
        def _(q):
            at = block(q, CHUNK)
            up = up_val[at, :]
            grad = grad_hidden[at, :]
            act, slope = gelu_both(gate_val[at, :])
            hidden[at, :] = (act * up).astype(BF16)
            grad_gate[at, :] = (grad * up * slope).astype(BF16)
            grad_up[at, :] = (grad * act).astype(BF16)

        for i in range(2, 5):
            act_store(i, g).start(priority=1)

    def piece_down(g):
        def work(cols):
            block_part[:, cols] = dot(hidden[...], w_down[:deep, cols])

        work(slice(None))
        act_store(5, g).start(priority=1)

    def piece_back_gate(g):
        def work(cols):
            part[block(g, size), cols] = matmul_back(grad_gate[...], w_gate[cols, :])

        work(slice(None))

    def piece_back_up(g):
        def work(cols):
            part[block(g, size), cols] += matmul_back(grad_up[...], w_up[cols, :])

        work(slice(None))

    tokens = count * CHUNK
    half = tokens // 2
    quarter = half // 2
    again = [
        local(source, target, again_sem.at[i])
        for i, (source, target) in enumerate(
            (
                (normed_out, w_down.at[slice(0, tokens)]),
                (gate_out, w_gate.at[slice(0, tokens)]),
                (up_out, w_up.at[slice(0, tokens)]),
                (hidden_out, w_gate.at[slice(tokens, 2 * tokens)]),
                (glow_out.at[slice(0, half)], w_down.at[slice(tokens, tokens + half)]),
                (glow_out.at[slice(half, half + quarter)], normed.at[0]),
                (glow_out.at[slice(half + quarter, tokens)], normed.at[1]),
            )
        )
    ]
    tall = w_gate.shape[0] // WEIGHT_STEPS
    stages = (gate_val, up_val, grad_hidden)

    kept = weight_out.shape[2]
    before_rest = rest_out.shape[2] - (deep - kept)

    def stage_stores(which, i):
        at = block(i, tall)
        return (
            local(
                stages[which].at[:, pl.ds(0, kept)],
                weight_out.at[which, at],
                stage_sem.at[which],
            ),
            local(
                stages[which].at[:, pl.ds(kept, deep - kept)],
                rest_out.at[which, at, pl.ds(before_rest, deep - kept)],
                rest_sem.at[which],
            ),
        )

    own_copy = local(own_ref, own_out, rest_sem.at[3])

    def piece_reload():
        own_copy.start(priority=1)
        for i in range(1, 6):
            act_store(i, groups - 1).wait()
        for copy in again:
            copy.start(priority=1)

    def piece_ready():
        for copy in again:
            copy.wait()

    def contract(left, right):
        return lax.dot_general(left, right, CONTRACT_ROWS, preferred_element_type=F32)

    def piece_weight(step):
        i = step // 3
        at = block(i, tall)
        for which in range(3):

            @pl.when(lax.rem(step, 3) == which)
            def _():
                @pl.when(i > 0)
                def _():
                    for copy in stage_stores(which, i - 1):
                        copy.wait()

                stage = stages[which]

                def work(cols):
                    if which == 0:
                        stage[:, cols] = contract(w_down[:tokens, at], w_gate[:tokens, cols])
                    elif which == 1:
                        stage[:, cols] = contract(w_down[:tokens, at], w_up[:tokens, cols])
                    else:
                        middle = tokens + half + quarter
                        stage[:, cols] = (
                            contract(
                                w_down[tokens : tokens + half, at],
                                w_gate[tokens : tokens + half, cols],
                            )
                            + contract(normed[0, :, at], w_gate[tokens + half : middle, cols])
                            + contract(normed[1, :, at], w_gate[middle : 2 * tokens, cols])
                        )

                work(slice(None))
                for copy in stage_stores(which, i):
                    copy.start(priority=1)

    first = GROUP + SKEW * n
    spare = GROUP * groups + ring + 3
    first_weight = spare + 3
    weights = 3 * WEIGHT_STEPS

    def before(k):
        @pl.when(k == spare)
        def _():
            piece_reload()

        @pl.when(k == first_weight - 1)
        def _():
            piece_ready()

        @pl.when(jnp.logical_and(k >= first_weight, k < first_weight + weights))
        def _():
            piece_weight(k - first_weight)

        @pl.when(jnp.logical_and(k < count, is_root(k)))
        def _():
            row_load(x_in, k).start(priority=1)

        @pl.when(
            jnp.logical_and(jnp.logical_and(k >= count, k < 2 * count), is_root(k))
        )
        def _():
            row_load(og_in, k).start(priority=1)

        at_tick(k, 0, project)
        at_tick(k, first, piece_gate)
        at_tick(k, first + 1, piece_up)
        at_tick(k, first + 2, piece_low)
        at_tick(k, first + 3, piece_hidden)
        at_tick(k, first + 4, piece_act)
        at_tick(k, first + 6, piece_down)
        at_tick(k, GROUP + ring, piece_back_gate)
        at_tick(k, GROUP + ring + 2, piece_back_up)

    def root(c, slot, total):
        j = lax.rem(c, count)
        mine = block(j // 2, CHUNK)
        row_load(x_in, c).wait()

        @pl.when(c < count)
        def _():
            value = rows_ref[slot] + total
            own_ref[mine, :] = value
            out[slot] = (value * mean_square(value) * gain_ref[...]).astype(BF16).astype(F32)

        @pl.when(c >= count)
        def _():
            back = norm_grad(own_ref[mine, :], gain_ref[...], total, acc_ref)
            out[slot] = rows_ref[slot] + back

    def low_store(c, slot):
        at = block(lax.rem(c, count), CHUNK)
        return local(low.at[slot], low_out.at[at], low_sem.at[slot])

    def own_store(c, slot):
        at = block(lax.rem(c, count) // 2, CHUNK)
        return local(out.at[slot], own_grad_out.at[at], own_sem.at[slot])

    def arrive(c, slot):
        @pl.when(c < count)
        def _():
            normed[lax.rem(c // GROUP, 2), block(lax.rem(c, GROUP), CHUNK), :] = out[slot].astype(BF16)

        @pl.when(c >= count)
        def _():
            low[slot] = out[slot].astype(BF16)
            low_store(c, slot).start(priority=1)

            @pl.when(is_root(c))
            def _():
                own_store(c, slot).start(priority=1)

    def leave(c, slot):
        @pl.when(c >= count)
        def _():
            low_store(c, slot).wait()

            @pl.when(is_root(c))
            def _():
                own_store(c, slot).wait()

    line_sum("mp", 2 * count, count, part, inbox, out, sems, before, root, arrive, leave)

    own_copy.wait()
    for which in range(3):
        for copy in stage_stores(which, WEIGHT_STEPS - 1):
            copy.wait()


def middle_call(*args):
    mixed, w_out, x, og, gain, w_gate, w_up, w_down = args
    rows, model = x.shape
    width, hidden = mixed.shape[1], w_gate.shape[1]
    size = GROUP * CHUNK
    dma = pltpu.SemaphoreType.DMA
    ring = ring_size("mp")
    act = shape((rows, hidden), BF16)
    tall = shape((rows, model), BF16)
    return pl.pallas_call(
        middle_kernel,
        out_shape=(
            tall,
            act,
            act,
            act,
            tall,
            shape((rows, model)),
            tall,
            shape((rows // 2, model)),
            shape((3, model, hidden - hidden // LATER)),
            shape((3, model, width + hidden // LATER)),
            shape((rows // 2, model)),
            shape((TILE, model)),
        ),
        in_specs=[HBM] * 4 + [VMEM] + [HBM] * 3,
        out_specs=(HBM,) * 11 + (VMEM,),
        scratch_shapes=line_scratch("mp", rows, model)
        + [
            pltpu.VMEM((rows, width), BF16),
            pltpu.VMEM((width, model), BF16),
            pltpu.VMEM((model, hidden), BF16),
            pltpu.VMEM((model, hidden), BF16),
            pltpu.VMEM((max(hidden, rows * 3 // 2), model), BF16),
            pltpu.VMEM((2, size, model), BF16),
            pltpu.VMEM((ring, CHUNK, model), F32),
            pltpu.VMEM((size, model), F32),
            pltpu.VMEM((size, model), BF16),
            pltpu.VMEM((size, hidden), F32),
            pltpu.VMEM((size, hidden), F32),
            pltpu.VMEM((size, hidden), F32),
            pltpu.VMEM((size, hidden), BF16),
            pltpu.VMEM((size, hidden), BF16),
            pltpu.VMEM((size, hidden), BF16),
            pltpu.VMEM((size, model), F32),
            pltpu.VMEM((ring, CHUNK, model), BF16),
            dma((5,)),
            dma((ring,)),
            dma((1,)),
            dma((6,)),
            dma((ring,)),
            dma((ring,)),
            dma((7,)),
            dma((3,)),
            dma((4,)),
            pltpu.VMEM((rows // 2, model), F32),
        ],
        compiler_params=params(2, 63),
        cost_estimate=cost(400),
        name="middle",
    )(*args)


def last_kernel(
    own_grad_in,
    x_in,
    grad_branch_in,
    input_in,
    w_branch_in,
    w_input_in,
    gain_ref,
    other_acc,
    sums_in,
    ends_in,
    blocks_in,
    grad_out,
    norm_ref,
    small_out,
    part,
    inbox,
    out,
    send_up,
    send_down,
    recv_up,
    recv_down,
    own_grad_ref,
    x_ref,
    grad_branch,
    input_low,
    w_branch,
    w_input,
    load_sem,
    store_sem,
    acc_ref,
    mine_ref,
    seq_in,
    mp_in,
    send_s,
    recv_s,
    send_m,
    recv_m,
    small,
    small_in,
    send_v,
    recv_v,
):
    count = part.shape[0] // CHUNK
    size = GROUP * CHUNK
    sems = (send_up, send_down, recv_up, recv_down)
    local = pltpu.make_async_copy

    loads = [
        local(source, target, load_sem.at[i])
        for i, (source, target) in enumerate(
            (
                (grad_branch_in, grad_branch),
                (w_branch_in, w_branch),
                (input_in, input_low),
                (w_input_in, w_input),
                (own_grad_in, own_grad_ref),
                (x_in, x_ref),
            )
        )
    ]
    for copy in loads:
        copy.start(priority=1)
    acc_ref[...] = jnp.zeros_like(acc_ref)
    norm_ref[...] = jnp.zeros_like(norm_ref)
    enter_all(("seq", "mp"))
    for copy in loads[:4]:
        copy.wait()

    kinds = sums_in.shape[0]
    me = lax.axis_index("seq")
    width = sums_in.shape[2]
    height = kinds + ends_in.shape[0]
    head = blocks_in.shape[0]
    levels = small_in.shape[0]

    def exchange(level):
        bit = 1 << level
        partner = me + bit - 2 * bit * lax.rem(me // bit, 2)
        return pltpu.make_async_remote_copy(
            src_ref=small.at[level],
            dst_ref=small_in.at[level],
            send_sem=send_v.at[level],
            recv_sem=recv_v.at[level],
            device_id={"seq": partner},
            device_id_type=MESH,
        )

    spacing = (count - 4) // (levels + 1)
    plane = lax.axis_index("mp")

    def norm_sum(i, k, first, source):
        seq_copies = to_all("seq", mine_ref.at[i, 0], seq_in.at[i], send_s.at[i], recv_s.at[i])
        mp_copies = to_all("mp", mine_ref.at[i, 1], mp_in.at[i], send_m.at[i], recv_m.at[i])

        @pl.when(k == first)
        def _():
            mine_ref[i, 0] = jnp.sum(source[...], axis=0, keepdims=True)
            seq_in[i, me] = mine_ref[i, 0]
            for copy in seq_copies:
                copy.start()

        @pl.when(k == first + 2)
        def _():
            for copy in seq_copies:
                copy.wait()
            mine_ref[i, 1] = jnp.sum(seq_in[i], axis=0)
            mp_in[i, plane] = mine_ref[i, 1]
            for copy in mp_copies:
                copy.start()

        @pl.when(k == first + 5)
        def _():
            for copy in mp_copies:
                copy.wait()
            norm_ref[i : i + 1, :] = jnp.sum(mp_in[i], axis=0)

    settled = count + SKEW * (lax.axis_size("mp") // 2)

    def before(k):
        @pl.when(k == 2)
        def _():
            for i in range(kinds):
                small[0, i : i + 1, :] = jnp.sum(sums_in[i], axis=0, keepdims=True)
            small[0, kinds:height, :] = ends_in[...]
            small[0, height : height + head, :] = blocks_in[:, :width]
            small[0, height + head :, :] = blocks_in[:, width:]

        for level in range(levels + 1):

            @pl.when(k == 3 + level * spacing)
            def _():
                if level > 0:
                    exchange(level - 1).wait()
                    total = small[level - 1] + small_in[level - 1]
                    if level < levels:
                        small[level] = total
                    else:
                        small_out[...] = total
                if level < levels:
                    exchange(level).start()

        norm_sum(0, k, settled, acc_ref)
        norm_sum(1, k, GROUP + 8, other_acc)

        @pl.when(jnp.logical_and(lax.rem(k, 4) == 0, k // 4 < count // GROUP))
        def _():
            at = block(k // 4, size)

            def work(cols):
                part[at, cols] = matmul_back(grad_branch[at, :], w_branch[cols, :]) + matmul_back(
                    input_low[at, :], w_input[cols, :]
                )

            work(slice(None))

        @pl.when(k == SKEW * (lax.axis_size("mp") // 2))
        def _():
            for copy in loads[4:]:
                copy.wait()

    def root(c, slot, total):
        back = norm_grad(x_ref[block(c, CHUNK), :], gain_ref[...], total, acc_ref)
        out[slot] = own_grad_ref[block(c // 2, CHUNK), :] + back

    def store(c, slot):
        return local(out.at[slot], grad_out.at[block(c, CHUNK)], store_sem.at[slot])

    def arrive(c, slot):
        store(c, slot).start(priority=1)

    def leave(c, slot):
        store(c, slot).wait()

    line_sum("mp", count, count, part, inbox, out, sems, before, root, arrive, leave)


def enter_all(axes):
    barrier = pltpu.get_barrier_semaphore()
    count = 0
    for axis in axes:
        size, me = lax.axis_size(axis), lax.axis_index(axis)
        for d in range(1, size):
            pl.semaphore_signal(
                barrier, 1, device_id={axis: lax.rem(me + d, size)}, device_id_type=MESH
            )
        count += size - 1
    pl.semaphore_wait(barrier, count)


def cost(micros):
    return pl.CostEstimate(flops=int(micros * 1e9), bytes_accessed=1 << 20, transcendentals=0)


def nseq_levels():
    return (lax.axis_size("seq") - 1).bit_length()


def last_call(*args):
    x, grad_branch = args[1:3]
    rows, model = x.shape
    width = grad_branch.shape[1]
    lines = args[8].shape[0] + args[9].shape[0] + 2 * args[10].shape[0]
    levels = nseq_levels()
    dma = pltpu.SemaphoreType.DMA
    nseq, nmp = lax.axis_size("seq"), lax.axis_size("mp")
    return pl.pallas_call(
        last_kernel,
        out_shape=(shape((rows, model)), shape((TILE, model)), shape((lines, width))),
        in_specs=[HBM] * 6 + [VMEM] * 5,
        out_specs=(HBM,) + (VMEM,) * 2,
        scratch_shapes=line_scratch("mp", rows, model)
        + [
            pltpu.VMEM((rows // 2, model), F32),
            pltpu.VMEM((rows, model), F32),
            pltpu.VMEM((rows, width), BF16),
            pltpu.VMEM((rows, width), BF16),
            pltpu.VMEM((model, width), BF16),
            pltpu.VMEM((model, width), BF16),
            dma((6,)),
            dma((ring_size("mp"),)),
            pltpu.VMEM((TILE, model), F32),
            pltpu.VMEM((2, 2, 1, model), F32),
            pltpu.VMEM((2, nseq, 1, model), F32),
            pltpu.VMEM((2, nmp, 1, model), F32),
            dma((2, nseq - 1)),
            dma((2, nseq - 1)),
            dma((2, nmp - 1)),
            dma((2, nmp - 1)),
            pltpu.VMEM((levels, lines, width), F32),
            pltpu.VMEM((levels, lines, width), F32),
            dma((levels,)),
            dma((levels,)),
        ],
        compiler_params=params(4, 62),
        cost_estimate=cost(200),
        name="last_sums",
    )(*args)


def finish_kernel(
    heads,
    block_in,
    grad_in,
    mlp_in,
    rec_in,
    small_hbm,
    norm_hbm,
    decay_hbm,
    block_out,
    grad_out,
    w_gate_out,
    w_up_out,
    w_branch_out,
    w_input_out,
    w_down_out,
    w_out_out,
    gate_r_out,
    gate_i_out,
    taps_out,
    conv_bias_out,
    bias_r_out,
    bias_i_out,
    decay_out,
    norm_in_out,
    norm_mlp_out,
    state_out,
    conv_out,
    tall,
    mlp,
    rec,
    small_in,
    norm_in,
    raw_ref,
    load_sem,
    store_sem,
    extra_sem,
):
    local = pltpu.make_async_copy
    width = small_in.shape[1]
    kept = mlp.shape[2]
    late = rec.shape[2] - width
    size = grad_in.shape[0] // COPIES
    extra = [
        local(source, target, extra_sem.at[i])
        for i, (source, target) in enumerate(
            ((small_hbm, small_in), (norm_hbm, norm_in), (decay_hbm, raw_ref))
        )
    ]
    for copy in extra:
        copy.start()
    jobs = [(mlp_in, mlp, None), (rec_in, rec, None)]
    for j, (source, target) in enumerate(((block_in, block_out), (grad_in, grad_out))):
        for i in range(COPIES):
            at = slice(i * size, (i + 1) * size)
            jobs.append((source.at[at], tall.at[j, at], target.at[at]))
    loads = [local(source, held, load_sem.at[i]) for i, (source, held, _) in enumerate(jobs)]
    stores = [
        local(held, target, store_sem.at[i])
        for i, (held, target) in enumerate(
            [(held, target) for _, held, target in jobs[2:]]
            + [
                (mlp.at[0], w_gate_out.at[:, pl.ds(0, kept)]),
                (mlp.at[1], w_up_out.at[:, pl.ds(0, kept)]),
                (rec.at[0, :, pl.ds(width, late)], w_gate_out.at[:, pl.ds(kept, late)]),
                (rec.at[1, :, pl.ds(width, late)], w_up_out.at[:, pl.ds(kept, late)]),
                (rec.at[1, :, pl.ds(0, width)], w_branch_out),
                (rec.at[2, :, pl.ds(0, width)], w_input_out),
            ]
        )
    ]
    for copy in loads:
        copy.start()
    for copy in extra:
        copy.wait()
    taps, seqs, edge = taps_out.shape[0], state_out.shape[0], conv_out.shape[0]
    head = gate_r_out.shape[1]
    decay = small_in[0:1, :].reshape(width) * (RATE_SCALE * jax.nn.sigmoid(-raw_ref[...]))
    decay_out[...] = decay
    bias_r_out[...] = small_in[1:2, :].reshape(width)
    bias_i_out[...] = small_in[2:3, :].reshape(width)
    conv_bias_out[...] = small_in[3:4, :].reshape(width)
    taps_out[...] = small_in[4 : 4 + taps, :]
    begin = 4 + taps
    state_out[...] = small_in[begin : begin + seqs, :]
    for s in range(seqs):
        end = begin + seqs + (s + 1) * TILE
        for k in range(edge):
            conv_out[k, s : s + 1, :] = small_in[end - edge + k : end - edge + k + 1, :]
    begin += seqs + seqs * TILE
    for i, target in enumerate((gate_r_out, gate_i_out)):
        line = small_in[begin + i * head : begin + (i + 1) * head, :]
        for h in range(heads):
            turned = line if h == 0 else pltpu.roll(line, width - h * head, 1)
            target[h] = turned[:, :head]
    norm_in_out[...] = norm_in[0:1, :].reshape(norm_in.shape[1])
    norm_mlp_out[...] = norm_in[1:2, :].reshape(norm_in.shape[1])
    loads[0].wait()
    loads[1].wait()
    for copy in stores[2 * COPIES :]:
        copy.start()
    w_down_out[:kept, :] = mlp[2].T
    w_down_out[kept:, :] = rec[2, :, width:].T
    w_out_out[...] = rec[0, :, :width].T
    for i in range(2 * COPIES):
        loads[2 + i].wait()
        stores[i].start()
    for copy in stores:
        copy.wait()


def finish_call(seqs, heads, head, edge, *args):
    _, stream_grad, mlp_grads, rec_grads, small, norms, decay = args
    rows, model = stream_grad.shape
    own, kept = mlp_grads.shape[1:]
    width = small.shape[1]
    hidden = kept + rec_grads.shape[2] - width
    taps = edge + 1
    line = shape((width,))
    tall = shape((rows, model))
    return pl.pallas_call(
        functools.partial(finish_kernel, heads),
        out_shape=(
            tall,
            tall,
            shape((own, hidden)),
            shape((own, hidden)),
            shape((own, width)),
            shape((own, width)),
            shape((hidden, own)),
            shape((width, own)),
            shape((heads, head, head)),
            shape((heads, head, head)),
            shape((taps, width)),
            line,
            line,
            line,
            line,
            shape((model,)),
            shape((model,)),
            shape((seqs, width)),
            shape((edge, seqs, width)),
        ),
        in_specs=[HBM] * 4 + [PINNED] * 3,
        out_specs=(HBM,) * 6 + (VMEM,) * 13,
        scratch_shapes=[
            pltpu.VMEM((2, rows, model), F32),
            pltpu.VMEM(mlp_grads.shape, F32),
            pltpu.VMEM(rec_grads.shape, F32),
            pltpu.VMEM(small.shape, F32),
            pltpu.VMEM(norms.shape, F32),
            pltpu.VMEM(decay.shape, F32),
            pltpu.SemaphoreType.DMA((2 + 2 * COPIES,)),
            pltpu.SemaphoreType.DMA((6 + 2 * COPIES,)),
            pltpu.SemaphoreType.DMA((3,)),
        ],
        compiler_params=pltpu.CompilerParams(vmem_limit_bytes=63 << 20),
        cost_estimate=cost(15),
        name="finish",
    )(*args)


def params(collective, megabytes=60):
    return pltpu.CompilerParams(
        collective_id=collective, has_side_effects=True, vmem_limit_bytes=megabytes << 20
    )


def shape(dims, dtype=F32):
    return jax.ShapeDtypeStruct(dims, dtype)


def recurrence_forward(span, *args):
    x, w_input = args[:2]
    rows, model = x.shape
    seqs, width = rows // span, w_input.shape[1]
    devices = lax.axis_size("seq")
    dma = pltpu.SemaphoreType.DMA
    groups = seqs // 2
    columns = (width // LANES, rows, LANES)
    spaced = (width // LANES, seqs * (span + TILE), LANES)
    padded = (seqs, span + TILE, width)
    return pl.pallas_call(
        functools.partial(forward_kernel, span),
        out_shape=(
            shape((rows, model), BF16),
            shape((rows, width)),
            shape(padded),
            shape((rows, 2 * width)),
            shape(columns),
            shape((rows, width), BF16),
            shape((seqs, width)),
            shape((devices, 2, seqs, width)),
            shape((width, 2 * width), BF16),
            shape((TILE, width)),
            shape(((seqs + 1) * TILE, width)),
        ),
        in_specs=[HBM] * 3 + [VMEM] * 8 + [pl.BlockSpec(memory_space=pltpu.SMEM)] + [VMEM] * 2,
        out_specs=(HBM,) * 5 + (VMEM,) * 6,
        scratch_shapes=[
            pltpu.VMEM((rows, model), F32),
            pltpu.VMEM((model, width), BF16),
            pltpu.VMEM((model, width), BF16),
            pltpu.VMEM((rows, model), BF16),
            pltpu.VMEM((rows, width), F32),
            pltpu.VMEM(padded, F32),
            pltpu.VMEM((rows, 2 * width), F32),
            pltpu.VMEM(columns, F32),
            pltpu.VMEM((rows, width), F32),
            pltpu.VMEM(spaced, F32),
            pltpu.VMEM(spaced, F32),
            pltpu.VMEM((2, span, width), F32),
            pltpu.VMEM((seqs, TILE, width), F32),
            pltpu.VMEM((seqs, TILE, width), F32),
            pltpu.VMEM((2, seqs, width), F32),
            dma((groups + 2,)),
            dma((4,)),
            dma((groups,)),
            dma((devices - 1,)),
            dma((devices - 1,)),
            dma((1,)),
            dma((1,)),
        ],
        compiler_params=params(0),
        cost_estimate=cost(50),
        name="recurrence_forward",
    )(*args)


def widen(array, width):
    short = width - array.shape[-1]
    if short == 0:
        return array
    return jnp.pad(array, [(0, 0)] * (array.ndim - 1) + [(0, short)])


def per_device(
    stream,
    norm_in,
    w_branch,
    w_input,
    conv_kernel,
    conv_bias,
    gate_r,
    bias_r,
    gate_i,
    bias_i,
    decay_param,
    w_out,
    norm_mlp,
    w_gate,
    w_up,
    w_down,
    state_init,
    conv_init,
    fresh_rows,
    out_grad,
):
    seqs, span, model = stream.shape
    channels = w_branch.shape[1]
    mlp_dev = w_gate.shape[1]
    heads, head_width = gate_r.shape[:2]
    taps = conv_kernel.shape[0]
    edge = taps - 1
    rows = seqs * span
    devices = lax.axis_size("seq")
    position = lax.axis_index("seq")
    width = -(-channels // 128) * 128

    flat_in = stream.reshape(rows, model)
    flat_grad = out_grad.reshape(rows, model)
    w_branch_p = widen(w_branch, width)
    w_input_p = widen(w_input, width)
    w_out_p = jnp.pad(w_out, ((0, width - channels), (0, 0))) if width > channels else w_out
    taps_p = widen(conv_kernel, width)
    def line(value):
        return widen(value, width)

    (
        normed,
        branch,
        padded,
        pre,
        hidden,
        mixed,
        carry,
        sums,
        gates,
        rates,
        ends,
    ) = recurrence_forward(
        span,
        flat_in,
        w_input_p,
        w_branch_p,
        norm_in[None],
        taps_p,
        line(conv_bias),
        line(decay_param),
        line(bias_r),
        line(bias_i),
        gate_r,
        gate_i,
        fresh_rows,
        widen(state_init, width),
        widen(jnp.swapaxes(conv_init, 0, 1), width),
    )
    made = middle_call(mixed, w_out_p, flat_in, flat_grad, norm_mlp[None], w_gate, w_up, w_down)
    block_part, resid_low, own_grad, mlp_grads, rest, own, norm_mlp_acc = made[5:]
    mlp_grads = lax.psum_scatter(mlp_grads, "seq", scatter_dimension=1, tiled=True)
    block_out, rec_grads, grad_branch, input_low, acc, blocks = backward_call(
        span,
        heads,
        head_width,
        block_part,
        own,
        resid_low,
        w_out_p,
        branch,
        hidden,
        pre,
        padded,
        normed,
        mixed,
        rest,
        gates,
        carry,
        sums,
        taps_p,
        rates,
    )

    rec_grads, grad_branch, mlp_grads = lax.optimization_barrier(
        (rec_grads, grad_branch, mlp_grads)
    )
    rec_grads = lax.psum_scatter(rec_grads, "seq", scatter_dimension=1, tiled=True)

    stream_grad, norm_grads, small = last_call(
        own_grad,
        flat_in,
        grad_branch,
        input_low,
        w_branch_p,
        w_input_p,
        norm_in[None],
        norm_mlp_acc,
        acc,
        ends,
        blocks,
    )
    (
        block_out,
        stream_grad,
        w_gate_grad,
        w_up_grad,
        w_branch_grad,
        w_input_grad,
        w_down_grad,
        w_out_grad,
        gate_r_grad,
        gate_i_grad,
        taps_grad,
        conv_bias_grad,
        bias_r_grad,
        bias_i_grad,
        decay_grad,
        norm_in_grad,
        norm_mlp_grad,
        final_state,
        final_conv,
    ) = finish_call(
        seqs,
        heads,
        head_width,
        edge,
        block_out,
        stream_grad,
        mlp_grads,
        rec_grads,
        small,
        norm_grads,
        line(decay_param),
    )
    return (
        block_out.reshape(stream.shape),
        stream_grad.reshape(stream.shape),
        norm_in_grad,
        w_branch_grad[:, :channels],
        w_input_grad[:, :channels],
        taps_grad[:, :channels],
        conv_bias_grad[:channels],
        gate_r_grad,
        bias_r_grad[:channels],
        gate_i_grad,
        bias_i_grad[:channels],
        decay_grad[:channels],
        w_out_grad[:channels],
        norm_mlp_grad,
        w_gate_grad,
        w_up_grad,
        w_down_grad,
        final_state[:, :channels],
        jnp.swapaxes(final_conv, 0, 1)[:, :, :channels],
    )


def solution(mesh):
    seq_rows = P(None, "seq", None)
    columns = P(None, "mp")
    channel = P("mp")
    return jax.shard_map(
        per_device,
        mesh=mesh,
        in_specs=(
            seq_rows,
            P(),
            columns,
            columns,
            columns,
            channel,
            P("mp", None, None),
            channel,
            P("mp", None, None),
            channel,
            channel,
            P("mp", None),
            P(),
            columns,
            columns,
            P("mp", None),
            columns,
            P(None, None, "mp"),
            P(),
            seq_rows,
        ),
        out_specs=(
            seq_rows,
            seq_rows,
            P(),
            P("seq", "mp"),
            P("seq", "mp"),
            columns,
            channel,
            P("mp", None, None),
            channel,
            P("mp", None, None),
            channel,
            channel,
            P("mp", "seq"),
            P(),
            P("seq", "mp"),
            P("seq", "mp"),
            P("mp", "seq"),
            columns,
            P(None, None, "mp"),
        ),
        check_vma=False,
    )
```

```python
import functools

import jax
import jax.numpy as jnp
from jax import lax
from jax.experimental import pallas as pl
from jax.experimental.pallas import tpu as pltpu
from jax.sharding import PartitionSpec as P

MESH = pl.DeviceIdType.MESH
RATE_SCALE = 8.0
EPS = 1e-06
GELU_C = 0.7978845608028654
GELU_K = 0.044715
CONTRACT_ROWS = (((0,), (0,)), ((), ()))
CONTRACT_LAST = (((1,), (1,)), ((), ()))
TILE = 8
LANES = 128
ROWS = 32
CHUNK = 16
SKEW = 2
GROUP = 16
WEIGHT_STEPS = 8
COPIES = 8
LATER = 6
F32 = jnp.float32
BF16 = jnp.bfloat16
VMEM = pl.BlockSpec(memory_space=pltpu.VMEM)
HBM = pl.BlockSpec(memory_space=pl.ANY)
PINNED = pl.BlockSpec(memory_space=pltpu.HBM)


def dot(a, b):
    return jnp.dot(a, b, preferred_element_type=F32)


def matmul_back(a, b):
    return lax.dot_general(a, b, CONTRACT_LAST, preferred_element_type=F32)


def block(i, size):
    return pl.ds(pl.multiple_of(i * size, size), size)


def gelu(x):
    t = jnp.tanh(GELU_C * (x + GELU_K * (x * x * x)))
    return 0.5 * x * (1.0 + t)


def gelu_both(x):
    x2 = x * x
    t = jnp.tanh(GELU_C * (x + GELU_K * (x2 * x)))
    half = 0.5 * (1.0 + t)
    slope = half + 0.5 * x * (1.0 - t * t) * (GELU_C * (1.0 + (3.0 * GELU_K) * x2))
    return x * half, slope


def one_minus_square(log_a, a):
    y = 2.0 * log_a
    s = 1.0 + y * (1.0 / 8.0)
    for k in (7, 6, 5, 4, 3, 2):
        s = 1.0 + (y * (1.0 / k)) * s
    return jnp.where(y > -0.35, -y * s, 1.0 - a * a)


def get(ref, at):
    return jnp.concatenate([ref[j, at, :] for j in range(ref.shape[0])], axis=-1)


def put(ref, at, value):
    for j in range(ref.shape[0]):
        ref[j, at, :] = value[:, j * LANES : (j + 1) * LANES]


def to_all(axis, src, slots, send, recv):
    size, me = lax.axis_size(axis), lax.axis_index(axis)
    return [
        pltpu.make_async_remote_copy(
            src_ref=src,
            dst_ref=slots.at[me],
            send_sem=send.at[d - 1],
            recv_sem=recv.at[d - 1],
            device_id={axis: lax.rem(me + d, size)},
            device_id_type=MESH,
        )
        for d in range(1, size)
    ]


def to_one(axis, distance, src, dst, send, recv):
    size, me = lax.axis_size(axis), lax.axis_index(axis)
    return pltpu.make_async_remote_copy(
        src_ref=src,
        dst_ref=dst,
        send_sem=send,
        recv_sem=recv,
        device_id={axis: lax.rem(me + distance + size, size)},
        device_id_type=MESH,
    )


def spread_gates(blocks_ref, out_ref, start, width):
    heads, size = blocks_ref.shape[:2]
    for h in range(heads):
        block_h = blocks_ref[h].astype(F32)
        parts = [block_h]
        if h > 0:
            parts.insert(0, jnp.zeros((size, h * size), F32))
        if width > (h + 1) * size:
            parts.append(jnp.zeros((size, width - (h + 1) * size), F32))
        row = jnp.concatenate(parts, axis=1).astype(BF16)
        out_ref[h * size : (h + 1) * size, start : start + width] = row
    if width > heads * size:
        rest = jnp.zeros((width - heads * size, width), BF16)
        out_ref[heads * size : width, start : start + width] = rest


def forward_kernel(
    span,
    x_in,
    w_input_in,
    w_branch_in,
    gain_ref,
    taps_ref,
    conv_bias_ref,
    decay_ref,
    bias_r_ref,
    bias_i_ref,
    gate_r_ref,
    gate_i_ref,
    fresh_ref,
    state_ref,
    conv_init_ref,
    normed_out,
    branch_out,
    pad_out,
    pre_out,
    hidden_out,
    mixed_ref,
    carry_ref,
    sums_ref,
    gates_ref,
    vec_ref,
    ends_ref,
    x_ref,
    w_input_ref,
    w_branch_ref,
    normed_ref,
    branch_ref,
    pad_ref,
    pre_ref,
    hidden_ref,
    act_ref,
    a_ref,
    b_ref,
    conv_ref,
    tail_ref,
    tail_in,
    mine_ref,
    load_sem,
    store_sem,
    normed_sem,
    send1,
    recv1,
    send_t,
    recv_t,
):
    seqs = state_ref.shape[0]
    width = taps_ref.shape[1]
    taps = taps_ref.shape[0]
    rows = seqs * span
    devices, me = lax.axis_size("seq"), lax.axis_index("seq")
    local = pltpu.make_async_copy
    pitch = a_ref.shape[1] // seqs
    group = 2 * span
    groups = rows // group

    def x_load(g):
        at = block(g, group)
        return local(x_in.at[at], x_ref.at[at], load_sem.at[g])

    weight_loads = [
        local(w_input_in, w_input_ref, load_sem.at[groups]),
        local(w_branch_in, w_branch_ref, load_sem.at[groups + 1]),
    ]
    x_load(0).start()
    weight_loads[0].start()
    for g in range(1, groups):
        x_load(g).start()
    weight_loads[1].start()

    enter_all(("seq",))
    spread_gates(gate_r_ref, gates_ref, 0, width)
    spread_gates(gate_i_ref, gates_ref, width, width)
    vec_ref[0:1, :] = conv_bias_ref[...].reshape(1, width)
    vec_ref[1:2, :] = jax.nn.softplus(-decay_ref[...].reshape(1, width))
    bias_r = bias_r_ref[...].reshape(1, width)
    bias_i = bias_i_ref[...].reshape(1, width)
    keep = [1.0 - fresh_ref[s].astype(F32) for s in range(seqs)]

    def normed_store(g):
        at = block(g, group)
        return local(normed_ref.at[at], normed_out.at[at], normed_sem.at[g])

    def norm(g):
        x_load(g).wait()
        for q in range(group // CHUNK):
            at = slice(g * group + q * CHUNK, g * group + (q + 1) * CHUNK)
            x = x_ref[at, :]
            normed_ref[at, :] = (x * mean_square(x) * gain_ref[...]).astype(BF16)

    norm(0)
    weight_loads[0].wait()
    for g in range(groups):
        if g + 1 < groups:
            norm(g + 1)
        conv = dot(normed_ref[slice(g * group, (g + 1) * group), :], w_input_ref[...])
        for j in range(group // span):
            pad_ref[g * (group // span) + j, pl.ds(TILE, span), :] = conv[
                j * span : (j + 1) * span
            ]
    for g in range(groups):
        normed_store(g).start()

    for s in range(seqs):
        tail_ref[s] = pad_ref[s, pl.ds(span, TILE), :]
    tail_copy = to_one("seq", 1, tail_ref, tail_in, send_t.at[0], recv_t.at[0])
    tail_copy.start()
    weight_loads[1].wait()

    def branch(g):
        branch_ref[block(g, group), :] = dot(normed_ref[block(g, group), :], w_branch_ref[...])

    @pl.loop(0, groups // 2)
    def _(g):
        branch(g)

    stores = [
        local(source, target, store_sem.at[i])
        for i, (source, target) in enumerate(
            (
                (branch_ref, branch_out),
                (pad_ref, pad_out),
                (pre_ref, pre_out),
                (hidden_ref, hidden_out),
            )
        )
    ]
    tail_copy.wait()
    lead = jnp.zeros((TILE - taps + 1, width), F32)
    for s in range(seqs):
        initial = jnp.concatenate(
            [lead] + [conv_init_ref[k, s : s + 1, :] * keep[s] for k in range(taps - 1)], axis=0
        )
        pad_ref[s, pl.ds(0, TILE), :] = jnp.where(me == 0, initial, tail_in[s])
    stores[1].start()

    def gates(s, slot):
        for q in range(span // ROWS):
            part = pad_ref[s, pl.ds(q * ROWS, ROWS + TILE), :]
            total = vec_ref[0:1, :]
            for k in range(taps):
                first = TILE - (taps - 1) + k
                total = total + taps_ref[k : k + 1, :] * part[first : first + ROWS]
            conv_ref[slot, pl.ds(q * ROWS, ROWS), :] = total

        pre = dot(conv_ref[slot].astype(BF16), gates_ref[...])
        pre_ref[block(s, span), :width] = pre[:, :width] + bias_r
        pre_ref[block(s, span), width:] = pre[:, width:] + bias_i
        for q in range(span // ROWS):
            rows_q = slice(q * ROWS, (q + 1) * ROWS)
            conv = conv_ref[slot, pl.ds(q * ROWS, ROWS), :]
            recall = jax.nn.sigmoid(pre[rows_q, :width] + bias_r)
            gate = jax.nn.sigmoid(pre[rows_q, width:] + bias_i)
            log_a = (-RATE_SCALE * vec_ref[1:2, :]) * recall
            a = jnp.exp(log_a)
            spaced = pl.ds(pl.multiple_of(s * pitch + q * ROWS, TILE), ROWS)
            put(a_ref, spaced, a)
            put(b_ref, spaced, jnp.sqrt(one_minus_square(log_a, a)) * gate * conv)

    per = seqs // (groups - groups // 2)

    @pl.loop(0, groups - groups // 2)
    def _(i):
        branch(groups // 2 + i)
        for j in range(per):
            gates(i * per + j, j % 2)

    stores[0].start()
    stores[2].start()

    def at_time(ref, t):
        return get(ref, pl.ds(t, seqs, stride=pitch))

    def step(t, value):
        prod, state = value
        a = at_time(a_ref, t)
        return prod * a, a * state + at_time(b_ref, t)

    ones = jnp.ones((seqs, width), F32)
    prod, state = lax.fori_loop(0, span, step, (ones, jnp.zeros_like(ones)), unroll=8)
    mine_ref[0] = prod
    mine_ref[1] = state
    sums_ref[me] = mine_ref[...]
    copies = to_all("seq", mine_ref, sums_ref, send1, recv1)
    for copy in copies:
        copy.start()

    @pl.loop(0, rows // ROWS, unroll=2)
    def _(q):
        at = block(q, ROWS)
        act_ref[at, :] = gelu(branch_ref[at, :])

    for copy in copies:
        copy.wait()

    def carry_step(j, carry):
        both = sums_ref[j]
        return jnp.where(j < me, both[0] * carry + both[1], carry)

    start = jnp.concatenate([state_ref[s : s + 1, :] * keep[s] for s in range(seqs)], axis=0)
    carry = lax.fori_loop(0, devices - 1, carry_step, start)
    carry_ref[...] = carry

    def final(t, state):
        state = at_time(a_ref, t) * state + at_time(b_ref, t)
        put(hidden_ref, pl.ds(t, seqs, stride=span), state)
        return state

    last = lax.fori_loop(0, span, final, carry, unroll=8)
    stores[3].start()
    ends_ref[0:seqs, :] = jnp.where(me == devices - 1, last, 0.0)
    for s in range(seqs):
        ends_ref[(s + 1) * TILE : (s + 2) * TILE, :] = jnp.where(
            me == devices - 1, pad_ref[s, pl.ds(span, TILE), :], 0.0
        )

    @pl.loop(0, rows // ROWS, unroll=2)
    def _(q):
        at = block(q, ROWS)
        mixed_ref[at, :] = (get(hidden_ref, at) * act_ref[at, :]).astype(BF16)

    for copy in stores:
        copy.wait()
    for g in range(groups):
        normed_store(g).wait()


def backward_kernel(
    span,
    heads,
    block_part_in,
    own_in,
    low_in,
    w_out_in,
    branch_in,
    hidden_in,
    pre_in,
    pad_in,
    normed_in,
    mixed_in,
    rest_in,
    gates_in,
    carry_ref,
    sums_ref,
    taps_ref,
    vec_ref,
    block_out,
    rec_out,
    grad_branch_out,
    input_out,
    acc_ref,
    blocks_ref,
    part,
    inbox,
    out,
    send_up,
    send_down,
    recv_up,
    recv_down,
    own_ref,
    resid_low,
    w_out_ref,
    branch_ref,
    hidden_ref,
    pre_ref,
    pad_ref,
    normed_ref,
    mixed_ref,
    a_ref,
    gd_ref,
    grad_ref,
    direct_ref,
    gpad_ref,
    heads_ref,
    low_ref,
    gates_grad,
    stage_ref,
    mine_ref,
    entries_ref,
    head_ref,
    head_in,
    load_sem,
    part_sem,
    store_sem,
    stage_sem,
    send1,
    recv1,
    send_t,
    recv_t,
    gates_ref,
    grad_branch_ref,
    input_ref,
    give_sem,
):
    seqs, width = carry_ref.shape
    taps = taps_ref.shape[0]
    rows = seqs * span
    devices, me = lax.axis_size("seq"), lax.axis_index("seq")
    n, z = lax.axis_size("mp"), lax.axis_index("mp")
    chunks = rows // CHUNK
    size = GROUP * CHUNK
    held = part.shape[0] // size
    groups = chunks // GROUP
    sems = (send_up, send_down, recv_up, recv_down)
    local = pltpu.make_async_copy

    def part_load(g):
        slot = lax.rem(g, held)
        return local(block_part_in.at[block(g, size)], part.at[block(slot, size)], part_sem.at[slot])

    loads = [
        local(source, target, load_sem.at[i])
        for i, (source, target) in enumerate(
            (
                (own_in, own_ref),
                (low_in, resid_low),
                (w_out_in, w_out_ref),
                (pre_in, pre_ref),
                (branch_in, branch_ref),
                (hidden_in, hidden_ref),
                (pad_in, pad_ref),
                (mixed_in, mixed_ref),
                (normed_in, normed_ref),
                (gates_in, gates_ref),
            )
        )
    ]
    part_load(0).start()
    for copy in loads[:6]:
        copy.start(priority=1)
    for g in range(1, held):
        part_load(g).start()
    for copy in loads[6:]:
        copy.start(priority=1)
    acc_ref[...] = jnp.zeros_like(acc_ref)
    enter_all(("seq", "mp"))

    pitch = a_ref.shape[1] // seqs

    def spaced(s, q):
        return pl.ds(pl.multiple_of(s * pitch + q * ROWS, TILE), ROWS)

    def decay(at):
        recall = jax.nn.sigmoid(pre_ref[at, :width])
        log_a = (-RATE_SCALE * vec_ref[1:2, :]) * recall
        return recall, log_a, jnp.exp(log_a)

    def piece_direct(s):
        @pl.when(s == 0)
        def _():
            for copy in loads[1:6]:
                copy.wait()

        grad_ref[...] = matmul_back(resid_low[block(s, span), :], w_out_ref[...])

        @pl.loop(0, span // ROWS)
        def _(q):
            at = block(s * (span // ROWS) + q, ROWS)
            put(a_ref, spaced(s, q), decay(at)[2])
            act, slope = gelu_both(branch_ref[at, :])
            grad = grad_ref[block(q, ROWS), :]
            put(gd_ref, spaced(s, q), grad * act)
            grad_branch_ref[at, :] = (grad * get(hidden_ref, at) * slope).astype(BF16)

    def at_time(ref, t):
        return get(ref, pl.ds(t, seqs, stride=pitch))

    zero = jnp.zeros((seqs, width), F32)
    entry_copies = to_all("seq", mine_ref, entries_ref, send1, recv1)

    def piece_entry(_):
        def step(k, through):
            t = span - 1 - k
            return at_time(a_ref, t) * (at_time(gd_ref, t) + through)

        mine_ref[...] = lax.fori_loop(0, span, step, zero, unroll=8)
        entries_ref[me] = mine_ref[...]
        for copy in entry_copies:
            copy.start()

    def piece_state(_):
        for copy in entry_copies:
            copy.wait()

        def back_step(k, through):
            j = devices - 1 - k
            return jnp.where(j > me, entries_ref[j] + sums_ref[j, 0] * through, through)

        incoming = lax.fori_loop(0, devices - 1, back_step, zero)

        def final(k, through):
            t = span - 1 - k
            grad = at_time(gd_ref, t) + through
            put(gd_ref, pl.ds(t, seqs, stride=pitch), grad)
            return at_time(a_ref, t) * grad

        lax.fori_loop(0, span, final, incoming, unroll=8)

    def add(k, value):
        acc_ref[k] += fold(value)

    parts = 2

    def piece_gates(i):
        s = i // parts
        quarters = span // ROWS // parts

        @pl.when(i == 0)
        def _():
            loads[6].wait()
            loads[9].wait()

        @pl.loop(lax.rem(i, parts) * quarters, (lax.rem(i, parts) + 1) * quarters)
        def _(q):
            at = block(s * (span // ROWS) + q, ROWS)
            part_rows = pad_ref[s, pl.ds(pl.multiple_of(q * ROWS, ROWS), ROWS + TILE), :]
            conv = vec_ref[0:1, :]
            for k in range(taps):
                first = TILE - (taps - 1) + k
                conv = conv + taps_ref[k : k + 1, :] * part_rows[first : first + ROWS]
            heads_ref[at, :] = conv.astype(BF16)
            recall, log_a, a = decay(at)
            gate = jax.nn.sigmoid(pre_ref[at, width:])
            square = one_minus_square(log_a, a)
            inverse = lax.rsqrt(square)
            root = jnp.sqrt(square)
            grad = get(gd_ref, spaced(s, q))
            hidden = get(hidden_ref, at)
            before_at = pl.multiple_of(jnp.maximum(s * span + q * ROWS - TILE, 0), TILE)
            earlier = get(hidden_ref, pl.ds(before_at, TILE))
            first_row = jnp.where(q == 0, carry_ref[pl.ds(s, 1), :], earlier[TILE - 1 :])
            place = lax.broadcasted_iota(jnp.int32, (ROWS, width), 0)
            prev = jnp.where(place == 0, first_row, pltpu.roll(hidden, 1, 0))
            grad_log = grad * a * (prev - gate * conv * a * inverse)
            through = grad_log * recall
            pre_r = through * (1.0 - recall) * (-RATE_SCALE * vec_ref[1:2, :])
            direct = grad * root * gate
            pre_i = direct * conv * (1.0 - gate)
            low_ref[at, :width] = pre_r.astype(BF16)
            low_ref[at, width:] = pre_i.astype(BF16)
            direct_ref[block(q, ROWS), :] = direct
            add(0, through)
            add(1, pre_r)
            add(2, pre_i)

        @pl.when(lax.rem(i, parts) == parts - 1)
        def _():
            whole = direct_ref[...] + matmul_back(low_ref[block(s, span), :], gates_ref[...])
            gpad_ref[s, pl.ds(0, span), :] = whole
            head_ref[s] = whole[:TILE]

    head_copy = to_one("seq", -1, head_ref, head_in, send_t.at[0], recv_t.at[0])

    def piece_head(_):
        head_copy.start()

    def piece_taps(i):
        for j in range(2):
            taps_of(2 * i + j)

    def taps_of(s):
        @pl.loop(0, span // ROWS)
        def _(q):
            at = pl.multiple_of(q * ROWS, ROWS)
            part_rows = pad_ref[s, pl.ds(at, ROWS + TILE), :]
            grad = gpad_ref[s, pl.ds(at, ROWS), :]
            add(3, grad)
            for k in range(taps):
                first = TILE - (taps - 1) + k
                add(4 + k, grad * part_rows[first : first + ROWS])

    def piece_tail(_):
        head_copy.wait()
        for s in range(seqs):
            gpad_ref[s, pl.ds(span, TILE), :] = jnp.where(me == devices - 1, 0.0, head_in[s])

    def piece_input(i):
        for j in range(2):
            input_of(2 * i + j)

    def input_of(s):
        @pl.loop(0, span // ROWS)
        def _(q):
            part_rows = gpad_ref[s, pl.ds(pl.multiple_of(q * ROWS, ROWS), ROWS + TILE), :]
            total = taps_ref[taps - 1 : taps, :] * part_rows[0:ROWS]
            for k in range(taps - 1):
                first = taps - 1 - k
                total = total + taps_ref[k : k + 1, :] * part_rows[first : first + ROWS]
            input_ref[block(s * (span // ROWS) + q, ROWS), :] = total.astype(BF16)

    def contract(left, right):
        return lax.dot_general(left, right, CONTRACT_ROWS, preferred_element_type=F32)

    head = blocks_ref.shape[0]

    gives = [
        local(grad_branch_ref, grad_branch_out, give_sem.at[0]),
        local(input_ref, input_out, give_sem.at[1]),
    ]

    def piece_give(_):
        for copy in gives:
            copy.start(priority=1)

    def piece_gates_grad(i):
        @pl.when(i == 0)
        def _():
            gates_grad[...] = contract(heads_ref[...], low_ref[:, :width])

        @pl.when(i == 1)
        def _():
            gates_grad[...] = contract(heads_ref[...], low_ref[:, width:])

        place = lax.broadcasted_iota(jnp.int32, (head, width), 1)
        line = jnp.zeros((head, width), F32)
        for h in range(heads):
            row = gates_grad[h * head : (h + 1) * head, :]
            inside = jnp.logical_and(place >= h * head, place < (h + 1) * head)
            line = jnp.where(inside, row, line)

        for j in range(2):

            @pl.when(i == j)
            def _():
                blocks_ref[:, j * width : (j + 1) * width] = line

    tall = resid_low.shape[1] // WEIGHT_STEPS

    def stage_store(i):
        at = block(lax.rem(i, WEIGHT_STEPS), tall)
        slot = lax.rem(i, 2)
        return local(
            stage_ref.at[slot],
            rec_out.at[i // WEIGHT_STEPS, at, pl.ds(0, width)],
            stage_sem.at[slot],
        )

    def piece_weights(i):
        @pl.when(i == 0)
        def _():
            loads[7].wait()
            loads[8].wait()

        @pl.loop(2 * i, 2 * i + 2)
        def _(j):
            weight_of(j)

    def weight_of(i):
        @pl.when(i >= 2)
        def _():
            stage_store(i - 2).wait()

        at = block(lax.rem(i, WEIGHT_STEPS), tall)
        slot = lax.rem(i, 2)
        for which, (left, right) in enumerate(
            ((resid_low, mixed_ref), (normed_ref, grad_branch_ref), (normed_ref, input_ref))
        ):
            @pl.when(i // WEIGHT_STEPS == which)
            def _():
                stage_ref[slot] = contract(left[:, at], right[...])

        stage_store(i).start(priority=1)

    weights = 3 * WEIGHT_STEPS
    plan = []
    begin = 3
    early = WEIGHT_STEPS // 2

    def piece_weights_later(i):
        piece_weights(i + early)

    for work, times, gap in (
        (piece_direct, seqs, 0),
        (piece_entry, 1, 0),
        (piece_weights, early, 5),
        (piece_state, 1, 0),
        (piece_gates, parts * seqs, 0),
        (piece_head, 1, 0),
        (piece_taps, seqs // 2, 0),
        (piece_gates_grad, 2, 3),
        (piece_tail, 1, 0),
        (piece_input, seqs // 2, 0),
        (piece_give, 1, 0),
        (piece_weights_later, weights // 2 - early, 0),
    ):
        plan.append((work, begin, times))
        begin += times + gap

    def run(step):
        for work, first, times in plan:
            @pl.when(jnp.logical_and(step >= first, step < first + times))
            def _():
                work(step - first)

    def before(k):
        @pl.when(k == SKEW * (n // 2))
        def _():
            loads[0].wait()

        @pl.when(jnp.logical_and(lax.rem(k, GROUP) == 0, k < chunks))
        def _():
            part_load(k // GROUP).wait()

        g = (k - out.shape[0]) // GROUP - 1 + held

        @pl.when(
            jnp.logical_and(
                jnp.logical_and(k >= out.shape[0] + GROUP, lax.rem(k - out.shape[0], GROUP) == 0),
                g < groups,
            )
        )
        def _():
            part_load(g).start(priority=1)

        run(k)

    def root(c, slot, total):
        out[slot] = own_ref[block(c // 2, CHUNK), :] + total

    def store(c, slot):
        return local(out.at[slot], block_out.at[block(c, CHUNK)], store_sem.at[slot])

    def arrive(c, slot):
        store(c, slot).start(priority=1)

    def leave(c, slot):
        store(c, slot).wait()

    line_sum(
        "mp", chunks, held * GROUP, part, inbox, out, sems, before, root, arrive, leave
    )

    @pl.loop(chunks + out.shape[0], max(begin, chunks + out.shape[0]))
    def _(k):
        run(k)

    for copy in gives:
        copy.wait()
    stage_store(weights - 2).wait()
    stage_store(weights - 1).wait()


def backward_call(span, heads, head, *args):
    block_part = args[0]
    low, w_out, branch, hidden, pre, padded, normed, mixed, rest, gates = args[2:12]
    carry, sums, taps = args[12:15]
    rows, model = block_part.shape
    seqs, width = carry.shape
    devices = lax.axis_size("seq")
    ring = ring_size("mp")
    held = 3 * GROUP * CHUNK
    dma = pltpu.SemaphoreType.DMA
    columns = pltpu.VMEM((width // LANES, seqs * (span + TILE), LANES), F32)
    return pl.pallas_call(
        functools.partial(backward_kernel, span, heads),
        out_shape=(
            shape((rows, model)),
            shape(rest.shape),
            shape((rows, width), BF16),
            shape((rows, width), BF16),
            shape((4 + taps.shape[0], TILE, width)),
            shape((head, 2 * width)),
        ),
        in_specs=[HBM] * 12 + [VMEM] * 4,
        input_output_aliases={10: 1},
        out_specs=(HBM,) * 4 + (VMEM,) * 2,
        scratch_shapes=line_scratch("mp", held, model)
        + [
            pltpu.VMEM((rows // 2, model), F32),
            pltpu.VMEM((rows, model), BF16),
            pltpu.VMEM((width, model), BF16),
            pltpu.VMEM((rows, width), F32),
            pltpu.VMEM(hidden.shape, F32),
            pltpu.VMEM(pre.shape, F32),
            pltpu.VMEM(padded.shape, F32),
            pltpu.VMEM((rows, model), BF16),
            pltpu.VMEM((rows, width), BF16),
            columns,
            columns,
            pltpu.VMEM((span, width), F32),
            pltpu.VMEM((span, width), F32),
            pltpu.VMEM((seqs, span + TILE, width), F32),
            pltpu.VMEM((rows, width), BF16),
            pltpu.VMEM((rows, 2 * width), BF16),
            pltpu.VMEM((width, width), F32),
            pltpu.VMEM((2, model // WEIGHT_STEPS, width), F32),
            pltpu.VMEM((seqs, width), F32),
            pltpu.VMEM((devices, seqs, width), F32),
            pltpu.VMEM((seqs, TILE, width), F32),
            pltpu.VMEM((seqs, TILE, width), F32),
            dma((10,)),
            dma((3,)),
            dma((ring,)),
            dma((2,)),
            dma((devices - 1,)),
            dma((devices - 1,)),
            dma((1,)),
            dma((1,)),
            pltpu.VMEM(gates.shape, BF16),
            pltpu.VMEM((rows, width), BF16),
            pltpu.VMEM((rows, width), BF16),
            dma((2,)),
        ],
        compiler_params=params(1, 63),
        cost_estimate=cost(200),
        name="backward",
    )(*args)


def line_sum(axis, total, period, part, inbox, out, sems, before, root, arrive, leave):
    send_up, send_down, recv_up, recv_down = sems
    parts = send_up.shape[0]
    columns = out.shape[2] // parts
    n, z = lax.axis_size(axis), lax.axis_index(axis)
    depth = n // 2
    ring = out.shape[0]

    def cols(p):
        return pl.ds(p * columns, columns)

    def root_of(c):
        return depth - 1 + lax.rem(c, 2)

    def up(c, step, side, p):
        slot = lax.rem(c, ring)
        return pltpu.make_async_remote_copy(
            src_ref=part.at[block(lax.rem(c, period), CHUNK), cols(p)],
            dst_ref=inbox.at[side, slot, :, cols(p)],
            send_sem=send_up.at[p, slot],
            recv_sem=recv_up.at[p, side, slot],
            device_id={axis: z + step},
            device_id_type=MESH,
        )

    def down(c, step, side, p):
        slot = lax.rem(c, ring)
        return pltpu.make_async_remote_copy(
            src_ref=out.at[slot, :, cols(p)],
            dst_ref=out.at[slot, :, cols(p)],
            send_sem=send_down.at[p, side, slot],
            recv_sem=recv_down.at[p, slot],
            device_id={axis: z + step},
            device_id_type=MESH,
        )

    inner = jnp.logical_and(z > 0, z < n - 1)

    @pl.loop(0, total + ring)
    def _(k):
        @pl.when(k >= ring)
        def _():
            c = k - ring
            r = root_of(c)
            step = jnp.where(z < r, 1, -1)
            side = jnp.where(z < r, 0, 1)

            @pl.when(z == r)
            def _():
                for p in range(parts):
                    down(c, -1, 0, p).wait_send()
                    down(c, 1, 1, p).wait_send()

            @pl.when(z != r)
            def _():
                for p in range(parts):
                    up(c, step, side, p).wait_send()

            @pl.when(jnp.logical_and(z != r, inner))
            def _():
                for p in range(parts):
                    down(c, -step, side, p).wait_send()

            leave(c, lax.rem(c, ring))

        before(k)

        for i in reversed(range(n + 1)):
            c = k - SKEW * i
            valid = jnp.logical_and(c >= 0, c < total)
            c = jnp.clip(c, 0, total - 1)
            at = block(lax.rem(c, period), CHUNK)
            slot = lax.rem(c, ring)
            r = root_of(c)
            step = jnp.where(z < r, 1, -1)
            side = jnp.where(z < r, 0, 1)
            if i > depth:
                here = jnp.logical_and(z != r, jnp.abs(z - r) == i - depth)

                @pl.when(jnp.logical_and(valid, here))
                def _():
                    for p in range(parts):
                        down(c, step, side, p).wait_recv()

                        @pl.when(inner)
                        def _():
                            down(c, -step, side, p).start()

                    arrive(c, slot)
            elif i == depth:

                @pl.when(jnp.logical_and(valid, z == r))
                def _():
                    for p in range(parts):
                        up(c, 1, 0, p).wait_recv()
                        up(c, -1, 1, p).wait_recv()
                    root(c, slot, part[at, :] + inbox[0, slot] + inbox[1, slot])
                    for p in range(parts):
                        down(c, -1, 0, p).start()
                        down(c, 1, 1, p).start()
                    arrive(c, slot)
            else:
                here = jnp.where(z < r, z, n - 1 - z) == i

                @pl.when(jnp.logical_and(valid, jnp.logical_and(z != r, here)))
                def _():
                    for p in range(parts):
                        if i > 0:
                            up(c, step, side, p).wait_recv()
                            part[at, cols(p)] += inbox[side, slot, :, cols(p)]
                        up(c, step, side, p).start()


def ring_size(axis):
    return SKEW * lax.axis_size(axis) + 4


def line_scratch(axis, rows, model, parts=2):
    dma = pltpu.SemaphoreType.DMA
    ring = ring_size(axis)
    return [
        pltpu.VMEM((rows, model), F32),
        pltpu.VMEM((2, ring, CHUNK, model), F32),
        pltpu.VMEM((ring, CHUNK, model), F32),
        dma((parts, ring)),
        dma((parts, 2, ring)),
        dma((parts, 2, ring)),
        dma((parts, ring)),
    ]


def mean_square(x):
    return lax.rsqrt(jnp.mean(x * x, axis=-1, keepdims=True) + EPS)


def nothing(*_):
    pass


def fold(value):
    total = value[0:TILE]
    for i in range(1, value.shape[0] // TILE):
        total = total + value[i * TILE : (i + 1) * TILE]
    return total


def norm_grad(value, gain, grad, acc_ref):
    q = mean_square(value)
    e = gain * grad
    acc_ref[...] += fold(grad * value * q)
    return q * e - value * (q * q * q) * jnp.mean(e * value, axis=-1, keepdims=True)


def middle_kernel(
    mixed_in,
    w_out_in,
    x_in,
    og_in,
    gain_ref,
    w_gate_in,
    w_up_in,
    w_down_in,
    normed_out,
    hidden_out,
    gate_out,
    up_out,
    glow_out,
    block_out,
    low_out,
    own_grad_out,
    weight_out,
    rest_out,
    own_out,
    acc_ref,
    part,
    inbox,
    out,
    send_up,
    send_down,
    recv_up,
    recv_down,
    mixed,
    w_out,
    w_gate,
    w_up,
    w_down,
    normed,
    rows_ref,
    og_ref,
    glow,
    gate_val,
    up_val,
    grad_hidden,
    hidden,
    grad_gate,
    grad_up,
    block_part,
    low,
    weight_sem,
    row_sem,
    og_sem,
    act_sem,
    low_sem,
    own_sem,
    again_sem,
    stage_sem,
    rest_sem,
    own_ref,
):
    n, z = lax.axis_size("mp"), lax.axis_index("mp")
    count = part.shape[0] // CHUNK
    size = GROUP * CHUNK
    groups = count // GROUP
    ring = out.shape[0]
    sems = (send_up, send_down, recv_up, recv_down)
    local = pltpu.make_async_copy

    loads = [
        local(source, target, weight_sem.at[i])
        for i, (source, target) in enumerate(
            (
                (mixed_in, mixed),
                (w_out_in, w_out),
                (w_gate_in, w_gate),
                (w_up_in, w_up),
                (w_down_in, w_down.at[slice(0, w_down_in.shape[0])]),
            )
        )
    ]
    for copy in loads:
        copy.start(priority=1)
    deep = w_down_in.shape[0]

    def og_load(g):
        return local(og_in.at[block(g, size)], og_ref, og_sem.at[0])

    og_load(0).start(priority=1)
    enter_all(("mp",))
    acc_ref[...] = jnp.zeros_like(acc_ref)
    loads[0].wait()
    loads[1].wait()

    def is_root(c):
        return z == n // 2 - 1 + lax.rem(c, 2)

    def row_load(source, c):
        slot = lax.rem(c, ring)
        at = block(lax.rem(c, count), CHUNK)
        return local(source.at[at], rows_ref.at[slot], row_sem.at[slot])

    acts = (
        (normed, normed_out),
        (glow, glow_out),
        (hidden, hidden_out),
        (grad_gate, gate_out),
        (grad_up, up_out),
        (block_part, block_out),
    )

    def act_store(i, g):
        source, target = acts[i]
        source = source.at[lax.rem(g, 2)] if i == 0 else source
        return local(source, target.at[block(g, size)], act_sem.at[i])

    def at_tick(k, first, work):
        g = (k - first) // GROUP

        @pl.when(
            jnp.logical_and(
                jnp.logical_and(k >= first, k < first + GROUP * groups),
                lax.rem(k - first, GROUP) == 0,
            )
        )
        def _():
            work(g)

    def project(g):
        def work(cols):
            part[block(g, size), cols] = dot(mixed[block(g, size), :], w_out[:, cols])

        work(slice(None))

    def piece_gate(g):
        @pl.when(g == 0)
        def _():
            for copy in loads[2:]:
                copy.wait()

        def work(cols):
            gate_val[:, cols] = dot(normed[lax.rem(g, 2)], w_gate[:, cols])

        work(slice(None))
        act_store(0, g).start(priority=1)

    def piece_up(g):
        def work(cols):
            up_val[:, cols] = dot(normed[lax.rem(g, 2)], w_up[:, cols])

        work(slice(None))

        @pl.when(g > 0)
        def _():
            for i in range(1, 6):
                act_store(i, g - 1).wait()

    def piece_low(g):
        og_load(g).wait()

        @pl.loop(0, size // ROWS)
        def _(q):
            glow[block(q, ROWS), :] = og_ref[block(q, ROWS), :].astype(BF16)

        @pl.when(g + 1 < groups)
        def _():
            og_load(g + 1).start(priority=1)

        act_store(1, g).start(priority=1)
        act_store(0, g).wait()

    def piece_hidden(g):
        def work(cols):
            grad_hidden[...] = matmul_back(glow[...], w_down[:deep, :])

        work(slice(None))

    def piece_act(g):
        @pl.loop(0, size // CHUNK)
        def _(q):
            at = block(q, CHUNK)
            up = up_val[at, :]
            grad = grad_hidden[at, :]
            act, slope = gelu_both(gate_val[at, :])
            hidden[at, :] = (act * up).astype(BF16)
            grad_gate[at, :] = (grad * up * slope).astype(BF16)
            grad_up[at, :] = (grad * act).astype(BF16)

        for i in range(2, 5):
            act_store(i, g).start(priority=1)

    def piece_down(g):
        def work(cols):
            block_part[:, cols] = dot(hidden[...], w_down[:deep, cols])

        work(slice(None))
        act_store(5, g).start(priority=1)

    def piece_back_gate(g):
        def work(cols):
            part[block(g, size), cols] = matmul_back(grad_gate[...], w_gate[cols, :])

        work(slice(None))

    def piece_back_up(g):
        def work(cols):
            part[block(g, size), cols] += matmul_back(grad_up[...], w_up[cols, :])

        work(slice(None))

    tokens = count * CHUNK
    half = tokens // 2
    quarter = half // 2
    again = [
        local(source, target, again_sem.at[i])
        for i, (source, target) in enumerate(
            (
                (normed_out, w_down.at[slice(0, tokens)]),
                (gate_out, w_gate.at[slice(0, tokens)]),
                (up_out, w_up.at[slice(0, tokens)]),
                (hidden_out, w_gate.at[slice(tokens, 2 * tokens)]),
                (glow_out.at[slice(0, half)], w_down.at[slice(tokens, tokens + half)]),
                (glow_out.at[slice(half, half + quarter)], normed.at[0]),
                (glow_out.at[slice(half + quarter, tokens)], normed.at[1]),
            )
        )
    ]
    tall = w_gate.shape[0] // WEIGHT_STEPS
    stages = (gate_val, up_val, grad_hidden)

    kept = weight_out.shape[2]
    before_rest = rest_out.shape[2] - (deep - kept)

    def stage_stores(which, i):
        at = block(i, tall)
        return (
            local(
                stages[which].at[:, pl.ds(0, kept)],
                weight_out.at[which, at],
                stage_sem.at[which],
            ),
            local(
                stages[which].at[:, pl.ds(kept, deep - kept)],
                rest_out.at[which, at, pl.ds(before_rest, deep - kept)],
                rest_sem.at[which],
            ),
        )

    own_copy = local(own_ref, own_out, rest_sem.at[3])

    def piece_reload():
        own_copy.start(priority=1)
        for i in range(1, 6):
            act_store(i, groups - 1).wait()
        for copy in again:
            copy.start(priority=1)

    def piece_ready():
        for copy in again:
            copy.wait()

    def contract(left, right):
        return lax.dot_general(left, right, CONTRACT_ROWS, preferred_element_type=F32)

    def piece_weight(step):
        i = step // 3
        at = block(i, tall)
        for which in range(3):

            @pl.when(lax.rem(step, 3) == which)
            def _():
                @pl.when(i > 0)
                def _():
                    for copy in stage_stores(which, i - 1):
                        copy.wait()

                stage = stages[which]

                def work(cols):
                    if which == 0:
                        stage[:, cols] = contract(w_down[:tokens, at], w_gate[:tokens, cols])
                    elif which == 1:
                        stage[:, cols] = contract(w_down[:tokens, at], w_up[:tokens, cols])
                    else:
                        middle = tokens + half + quarter
                        stage[:, cols] = (
                            contract(
                                w_down[tokens : tokens + half, at],
                                w_gate[tokens : tokens + half, cols],
                            )
                            + contract(normed[0, :, at], w_gate[tokens + half : middle, cols])
                            + contract(normed[1, :, at], w_gate[middle : 2 * tokens, cols])
                        )

                work(slice(None))
                for copy in stage_stores(which, i):
                    copy.start(priority=1)

    first = GROUP + SKEW * n
    spare = GROUP * groups + ring + 3
    first_weight = spare + 3
    weights = 3 * WEIGHT_STEPS

    def before(k):
        @pl.when(k == spare)
        def _():
            piece_reload()

        @pl.when(k == first_weight - 1)
        def _():
            piece_ready()

        @pl.when(jnp.logical_and(k >= first_weight, k < first_weight + weights))
        def _():
            piece_weight(k - first_weight)

        @pl.when(jnp.logical_and(k < count, is_root(k)))
        def _():
            row_load(x_in, k).start(priority=1)

        @pl.when(
            jnp.logical_and(jnp.logical_and(k >= count, k < 2 * count), is_root(k))
        )
        def _():
            row_load(og_in, k).start(priority=1)

        at_tick(k, 0, project)
        at_tick(k, first, piece_gate)
        at_tick(k, first + 1, piece_up)
        at_tick(k, first + 2, piece_low)
        at_tick(k, first + 3, piece_hidden)
        at_tick(k, first + 4, piece_act)
        at_tick(k, first + 6, piece_down)
        at_tick(k, GROUP + ring, piece_back_gate)
        at_tick(k, GROUP + ring + 2, piece_back_up)

    def root(c, slot, total):
        j = lax.rem(c, count)
        mine = block(j // 2, CHUNK)
        row_load(x_in, c).wait()

        @pl.when(c < count)
        def _():
            value = rows_ref[slot] + total
            own_ref[mine, :] = value
            out[slot] = (value * mean_square(value) * gain_ref[...]).astype(BF16).astype(F32)

        @pl.when(c >= count)
        def _():
            back = norm_grad(own_ref[mine, :], gain_ref[...], total, acc_ref)
            out[slot] = rows_ref[slot] + back

    def low_store(c, slot):
        at = block(lax.rem(c, count), CHUNK)
        return local(low.at[slot], low_out.at[at], low_sem.at[slot])

    def own_store(c, slot):
        at = block(lax.rem(c, count) // 2, CHUNK)
        return local(out.at[slot], own_grad_out.at[at], own_sem.at[slot])

    def arrive(c, slot):
        @pl.when(c < count)
        def _():
            normed[lax.rem(c // GROUP, 2), block(lax.rem(c, GROUP), CHUNK), :] = out[slot].astype(BF16)

        @pl.when(c >= count)
        def _():
            low[slot] = out[slot].astype(BF16)
            low_store(c, slot).start(priority=1)

            @pl.when(is_root(c))
            def _():
                own_store(c, slot).start(priority=1)

    def leave(c, slot):
        @pl.when(c >= count)
        def _():
            low_store(c, slot).wait()

            @pl.when(is_root(c))
            def _():
                own_store(c, slot).wait()

    line_sum("mp", 2 * count, count, part, inbox, out, sems, before, root, arrive, leave)

    own_copy.wait()
    for which in range(3):
        for copy in stage_stores(which, WEIGHT_STEPS - 1):
            copy.wait()


def middle_call(*args):
    mixed, w_out, x, og, gain, w_gate, w_up, w_down = args
    rows, model = x.shape
    width, hidden = mixed.shape[1], w_gate.shape[1]
    size = GROUP * CHUNK
    dma = pltpu.SemaphoreType.DMA
    ring = ring_size("mp")
    act = shape((rows, hidden), BF16)
    tall = shape((rows, model), BF16)
    return pl.pallas_call(
        middle_kernel,
        out_shape=(
            tall,
            act,
            act,
            act,
            tall,
            shape((rows, model)),
            tall,
            shape((rows // 2, model)),
            shape((3, model, hidden - hidden // LATER)),
            shape((3, model, width + hidden // LATER)),
            shape((rows // 2, model)),
            shape((TILE, model)),
        ),
        in_specs=[HBM] * 4 + [VMEM] + [HBM] * 3,
        out_specs=(HBM,) * 11 + (VMEM,),
        scratch_shapes=line_scratch("mp", rows, model)
        + [
            pltpu.VMEM((rows, width), BF16),
            pltpu.VMEM((width, model), BF16),
            pltpu.VMEM((model, hidden), BF16),
            pltpu.VMEM((model, hidden), BF16),
            pltpu.VMEM((max(hidden, rows * 3 // 2), model), BF16),
            pltpu.VMEM((2, size, model), BF16),
            pltpu.VMEM((ring, CHUNK, model), F32),
            pltpu.VMEM((size, model), F32),
            pltpu.VMEM((size, model), BF16),
            pltpu.VMEM((size, hidden), F32),
            pltpu.VMEM((size, hidden), F32),
            pltpu.VMEM((size, hidden), F32),
            pltpu.VMEM((size, hidden), BF16),
            pltpu.VMEM((size, hidden), BF16),
            pltpu.VMEM((size, hidden), BF16),
            pltpu.VMEM((size, model), F32),
            pltpu.VMEM((ring, CHUNK, model), BF16),
            dma((5,)),
            dma((ring,)),
            dma((1,)),
            dma((6,)),
            dma((ring,)),
            dma((ring,)),
            dma((7,)),
            dma((3,)),
            dma((4,)),
            pltpu.VMEM((rows // 2, model), F32),
        ],
        compiler_params=params(2, 63),
        cost_estimate=cost(400),
        name="middle",
    )(*args)


def last_kernel(
    own_grad_in,
    x_in,
    grad_branch_in,
    input_in,
    w_branch_in,
    w_input_in,
    gain_ref,
    other_acc,
    sums_in,
    ends_in,
    blocks_in,
    grad_out,
    norm_ref,
    small_out,
    part,
    inbox,
    out,
    send_up,
    send_down,
    recv_up,
    recv_down,
    own_grad_ref,
    x_ref,
    grad_branch,
    input_low,
    w_branch,
    w_input,
    load_sem,
    store_sem,
    acc_ref,
    mine_ref,
    seq_in,
    mp_in,
    send_s,
    recv_s,
    send_m,
    recv_m,
    small,
    small_in,
    send_v,
    recv_v,
):
    count = part.shape[0] // CHUNK
    size = GROUP * CHUNK
    sems = (send_up, send_down, recv_up, recv_down)
    local = pltpu.make_async_copy

    loads = [
        local(source, target, load_sem.at[i])
        for i, (source, target) in enumerate(
            (
                (grad_branch_in, grad_branch),
                (w_branch_in, w_branch),
                (input_in, input_low),
                (w_input_in, w_input),
                (own_grad_in, own_grad_ref),
                (x_in, x_ref),
            )
        )
    ]
    for copy in loads:
        copy.start(priority=1)
    acc_ref[...] = jnp.zeros_like(acc_ref)
    norm_ref[...] = jnp.zeros_like(norm_ref)
    enter_all(("seq", "mp"))
    for copy in loads[:4]:
        copy.wait()

    kinds = sums_in.shape[0]
    me = lax.axis_index("seq")
    width = sums_in.shape[2]
    height = kinds + ends_in.shape[0]
    head = blocks_in.shape[0]
    levels = small_in.shape[0]

    def exchange(level):
        bit = 1 << level
        partner = me + bit - 2 * bit * lax.rem(me // bit, 2)
        return pltpu.make_async_remote_copy(
            src_ref=small.at[level],
            dst_ref=small_in.at[level],
            send_sem=send_v.at[level],
            recv_sem=recv_v.at[level],
            device_id={"seq": partner},
            device_id_type=MESH,
        )

    spacing = (count - 4) // (levels + 1)
    plane = lax.axis_index("mp")

    def norm_sum(i, k, first, gaps, source):
        seq_copies = to_all("seq", mine_ref.at[i, 0], seq_in.at[i], send_s.at[i], recv_s.at[i])
        mp_copies = to_all("mp", mine_ref.at[i, 1], mp_in.at[i], send_m.at[i], recv_m.at[i])

        @pl.when(k == first)
        def _():
            mine_ref[i, 0] = jnp.sum(source[...], axis=0, keepdims=True)
            seq_in[i, me] = mine_ref[i, 0]
            for copy in seq_copies:
                copy.start()

        @pl.when(k == first + gaps[0])
        def _():
            for copy in seq_copies:
                copy.wait()
            mine_ref[i, 1] = jnp.sum(seq_in[i], axis=0)
            mp_in[i, plane] = mine_ref[i, 1]
            for copy in mp_copies:
                copy.start()

        @pl.when(k == first + gaps[0] + gaps[1])
        def _():
            for copy in mp_copies:
                copy.wait()
            norm_ref[i : i + 1, :] = jnp.sum(mp_in[i], axis=0)

    settled = count + SKEW * (lax.axis_size("mp") // 2)

    def before(k):
        @pl.when(k == 2)
        def _():
            for i in range(kinds):
                small[0, i : i + 1, :] = jnp.sum(sums_in[i], axis=0, keepdims=True)
            small[0, kinds:height, :] = ends_in[...]
            small[0, height : height + head, :] = blocks_in[:, :width]
            small[0, height + head :, :] = blocks_in[:, width:]

        for level in range(levels + 1):

            @pl.when(k == 3 + level * spacing)
            def _():
                if level > 0:
                    exchange(level - 1).wait()
                    total = small[level - 1] + small_in[level - 1]
                    if level < levels:
                        small[level] = total
                    else:
                        small_out[...] = total
                if level < levels:
                    exchange(level).start()

        norm_sum(0, k, settled, (2, 3), acc_ref)
        norm_sum(1, k, 10, (20, 20), other_acc)

        @pl.when(jnp.logical_and(lax.rem(k, 4) == 0, k // 4 < count // GROUP))
        def _():
            at = block(k // 4, size)

            def work(cols):
                part[at, cols] = matmul_back(grad_branch[at, :], w_branch[cols, :]) + matmul_back(
                    input_low[at, :], w_input[cols, :]
                )

            work(slice(None))

        @pl.when(k == SKEW * (lax.axis_size("mp") // 2))
        def _():
            for copy in loads[4:]:
                copy.wait()

    def root(c, slot, total):
        back = norm_grad(x_ref[block(c, CHUNK), :], gain_ref[...], total, acc_ref)
        out[slot] = own_grad_ref[block(c // 2, CHUNK), :] + back

    def store(c, slot):
        return local(out.at[slot], grad_out.at[block(c, CHUNK)], store_sem.at[slot])

    def arrive(c, slot):
        store(c, slot).start(priority=1)

    def leave(c, slot):
        store(c, slot).wait()

    line_sum("mp", count, count, part, inbox, out, sems, before, root, arrive, leave)


def enter_all(axes):
    barrier = pltpu.get_barrier_semaphore()
    count = 0
    for axis in axes:
        size, me = lax.axis_size(axis), lax.axis_index(axis)
        for d in range(1, size):
            pl.semaphore_signal(
                barrier, 1, device_id={axis: lax.rem(me + d, size)}, device_id_type=MESH
            )
        count += size - 1
    pl.semaphore_wait(barrier, count)


def cost(micros):
    return pl.CostEstimate(flops=int(micros * 1e9), bytes_accessed=1 << 20, transcendentals=0)


def nseq_levels():
    return (lax.axis_size("seq") - 1).bit_length()


def last_call(*args):
    x, grad_branch = args[1:3]
    rows, model = x.shape
    width = grad_branch.shape[1]
    lines = args[8].shape[0] + args[9].shape[0] + 2 * args[10].shape[0]
    levels = nseq_levels()
    dma = pltpu.SemaphoreType.DMA
    nseq, nmp = lax.axis_size("seq"), lax.axis_size("mp")
    return pl.pallas_call(
        last_kernel,
        out_shape=(shape((rows, model)), shape((TILE, model)), shape((lines, width))),
        in_specs=[HBM] * 6 + [VMEM] * 5,
        out_specs=(HBM,) + (VMEM,) * 2,
        scratch_shapes=line_scratch("mp", rows, model)
        + [
            pltpu.VMEM((rows // 2, model), F32),
            pltpu.VMEM((rows, model), F32),
            pltpu.VMEM((rows, width), BF16),
            pltpu.VMEM((rows, width), BF16),
            pltpu.VMEM((model, width), BF16),
            pltpu.VMEM((model, width), BF16),
            dma((6,)),
            dma((ring_size("mp"),)),
            pltpu.VMEM((TILE, model), F32),
            pltpu.VMEM((2, 2, 1, model), F32),
            pltpu.VMEM((2, nseq, 1, model), F32),
            pltpu.VMEM((2, nmp, 1, model), F32),
            dma((2, nseq - 1)),
            dma((2, nseq - 1)),
            dma((2, nmp - 1)),
            dma((2, nmp - 1)),
            pltpu.VMEM((levels, lines, width), F32),
            pltpu.VMEM((levels, lines, width), F32),
            dma((levels,)),
            dma((levels,)),
        ],
        compiler_params=params(4, 62),
        cost_estimate=cost(200),
        name="last_sums",
    )(*args)


def finish_kernel(
    heads,
    block_in,
    grad_in,
    mlp_in,
    rec_in,
    small_hbm,
    norm_hbm,
    decay_hbm,
    block_out,
    grad_out,
    w_gate_out,
    w_up_out,
    w_branch_out,
    w_input_out,
    w_down_out,
    w_out_out,
    gate_r_out,
    gate_i_out,
    taps_out,
    conv_bias_out,
    bias_r_out,
    bias_i_out,
    decay_out,
    norm_in_out,
    norm_mlp_out,
    state_out,
    conv_out,
    tall,
    mlp,
    rec,
    small_in,
    norm_in,
    raw_ref,
    load_sem,
    store_sem,
    extra_sem,
):
    local = pltpu.make_async_copy
    width = small_in.shape[1]
    kept = mlp.shape[2]
    late = rec.shape[2] - width
    size = grad_in.shape[0] // COPIES
    extra = [
        local(source, target, extra_sem.at[i])
        for i, (source, target) in enumerate(
            ((small_hbm, small_in), (norm_hbm, norm_in), (decay_hbm, raw_ref))
        )
    ]
    for copy in extra:
        copy.start()
    jobs = [(mlp_in, mlp, None), (rec_in, rec, None)]
    for j, (source, target) in enumerate(((block_in, block_out), (grad_in, grad_out))):
        for i in range(COPIES):
            at = slice(i * size, (i + 1) * size)
            jobs.append((source.at[at], tall.at[j, at], target.at[at]))
    loads = [local(source, held, load_sem.at[i]) for i, (source, held, _) in enumerate(jobs)]
    stores = [
        local(held, target, store_sem.at[i])
        for i, (held, target) in enumerate(
            [(held, target) for _, held, target in jobs[2:]]
            + [
                (mlp.at[0], w_gate_out.at[:, pl.ds(0, kept)]),
                (mlp.at[1], w_up_out.at[:, pl.ds(0, kept)]),
                (rec.at[0, :, pl.ds(width, late)], w_gate_out.at[:, pl.ds(kept, late)]),
                (rec.at[1, :, pl.ds(width, late)], w_up_out.at[:, pl.ds(kept, late)]),
                (rec.at[1, :, pl.ds(0, width)], w_branch_out),
                (rec.at[2, :, pl.ds(0, width)], w_input_out),
            ]
        )
    ]
    for copy in loads:
        copy.start()
    for copy in extra:
        copy.wait()
    taps, seqs, edge = taps_out.shape[0], state_out.shape[0], conv_out.shape[0]
    head = gate_r_out.shape[1]
    decay = small_in[0:1, :].reshape(width) * (RATE_SCALE * jax.nn.sigmoid(-raw_ref[...]))
    decay_out[...] = decay
    bias_r_out[...] = small_in[1:2, :].reshape(width)
    bias_i_out[...] = small_in[2:3, :].reshape(width)
    conv_bias_out[...] = small_in[3:4, :].reshape(width)
    taps_out[...] = small_in[4 : 4 + taps, :]
    begin = 4 + taps
    state_out[...] = small_in[begin : begin + seqs, :]
    for s in range(seqs):
        end = begin + seqs + (s + 1) * TILE
        for k in range(edge):
            conv_out[k, s : s + 1, :] = small_in[end - edge + k : end - edge + k + 1, :]
    begin += seqs + seqs * TILE
    for i, target in enumerate((gate_r_out, gate_i_out)):
        line = small_in[begin + i * head : begin + (i + 1) * head, :]
        for h in range(heads):
            turned = line if h == 0 else pltpu.roll(line, width - h * head, 1)
            target[h] = turned[:, :head]
    norm_in_out[...] = norm_in[0:1, :].reshape(norm_in.shape[1])
    norm_mlp_out[...] = norm_in[1:2, :].reshape(norm_in.shape[1])
    loads[0].wait()
    loads[1].wait()
    for copy in stores[2 * COPIES :]:
        copy.start()
    w_down_out[:kept, :] = mlp[2].T
    w_down_out[kept:, :] = rec[2, :, width:].T
    w_out_out[...] = rec[0, :, :width].T
    for i in range(2 * COPIES):
        loads[2 + i].wait()
        stores[i].start()
    for copy in stores:
        copy.wait()


def finish_call(seqs, heads, head, edge, *args):
    _, stream_grad, mlp_grads, rec_grads, small, norms, decay = args
    rows, model = stream_grad.shape
    own, kept = mlp_grads.shape[1:]
    width = small.shape[1]
    hidden = kept + rec_grads.shape[2] - width
    taps = edge + 1
    line = shape((width,))
    tall = shape((rows, model))
    return pl.pallas_call(
        functools.partial(finish_kernel, heads),
        out_shape=(
            tall,
            tall,
            shape((own, hidden)),
            shape((own, hidden)),
            shape((own, width)),
            shape((own, width)),
            shape((hidden, own)),
            shape((width, own)),
            shape((heads, head, head)),
            shape((heads, head, head)),
            shape((taps, width)),
            line,
            line,
            line,
            line,
            shape((model,)),
            shape((model,)),
            shape((seqs, width)),
            shape((edge, seqs, width)),
        ),
        in_specs=[HBM] * 4 + [PINNED] * 3,
        out_specs=(HBM,) * 6 + (VMEM,) * 13,
        scratch_shapes=[
            pltpu.VMEM((2, rows, model), F32),
            pltpu.VMEM(mlp_grads.shape, F32),
            pltpu.VMEM(rec_grads.shape, F32),
            pltpu.VMEM(small.shape, F32),
            pltpu.VMEM(norms.shape, F32),
            pltpu.VMEM(decay.shape, F32),
            pltpu.SemaphoreType.DMA((2 + 2 * COPIES,)),
            pltpu.SemaphoreType.DMA((6 + 2 * COPIES,)),
            pltpu.SemaphoreType.DMA((3,)),
        ],
        compiler_params=pltpu.CompilerParams(vmem_limit_bytes=63 << 20),
        cost_estimate=cost(15),
        name="finish",
    )(*args)


def params(collective, megabytes=60):
    return pltpu.CompilerParams(
        collective_id=collective, has_side_effects=True, vmem_limit_bytes=megabytes << 20
    )


def shape(dims, dtype=F32):
    return jax.ShapeDtypeStruct(dims, dtype)


def recurrence_forward(span, *args):
    x, w_input = args[:2]
    rows, model = x.shape
    seqs, width = rows // span, w_input.shape[1]
    devices = lax.axis_size("seq")
    dma = pltpu.SemaphoreType.DMA
    groups = seqs // 2
    columns = (width // LANES, rows, LANES)
    spaced = (width // LANES, seqs * (span + TILE), LANES)
    padded = (seqs, span + TILE, width)
    return pl.pallas_call(
        functools.partial(forward_kernel, span),
        out_shape=(
            shape((rows, model), BF16),
            shape((rows, width)),
            shape(padded),
            shape((rows, 2 * width)),
            shape(columns),
            shape((rows, width), BF16),
            shape((seqs, width)),
            shape((devices, 2, seqs, width)),
            shape((width, 2 * width), BF16),
            shape((TILE, width)),
            shape(((seqs + 1) * TILE, width)),
        ),
        in_specs=[HBM] * 3 + [VMEM] * 8 + [pl.BlockSpec(memory_space=pltpu.SMEM)] + [VMEM] * 2,
        out_specs=(HBM,) * 5 + (VMEM,) * 6,
        scratch_shapes=[
            pltpu.VMEM((rows, model), F32),
            pltpu.VMEM((model, width), BF16),
            pltpu.VMEM((model, width), BF16),
            pltpu.VMEM((rows, model), BF16),
            pltpu.VMEM((rows, width), F32),
            pltpu.VMEM(padded, F32),
            pltpu.VMEM((rows, 2 * width), F32),
            pltpu.VMEM(columns, F32),
            pltpu.VMEM((rows, width), F32),
            pltpu.VMEM(spaced, F32),
            pltpu.VMEM(spaced, F32),
            pltpu.VMEM((2, span, width), F32),
            pltpu.VMEM((seqs, TILE, width), F32),
            pltpu.VMEM((seqs, TILE, width), F32),
            pltpu.VMEM((2, seqs, width), F32),
            dma((groups + 2,)),
            dma((4,)),
            dma((groups,)),
            dma((devices - 1,)),
            dma((devices - 1,)),
            dma((1,)),
            dma((1,)),
        ],
        compiler_params=params(0),
        cost_estimate=cost(50),
        name="recurrence_forward",
    )(*args)


def widen(array, width):
    short = width - array.shape[-1]
    if short == 0:
        return array
    return jnp.pad(array, [(0, 0)] * (array.ndim - 1) + [(0, short)])


def per_device(
    stream,
    norm_in,
    w_branch,
    w_input,
    conv_kernel,
    conv_bias,
    gate_r,
    bias_r,
    gate_i,
    bias_i,
    decay_param,
    w_out,
    norm_mlp,
    w_gate,
    w_up,
    w_down,
    state_init,
    conv_init,
    fresh_rows,
    out_grad,
):
    seqs, span, model = stream.shape
    channels = w_branch.shape[1]
    mlp_dev = w_gate.shape[1]
    heads, head_width = gate_r.shape[:2]
    taps = conv_kernel.shape[0]
    edge = taps - 1
    rows = seqs * span
    devices = lax.axis_size("seq")
    position = lax.axis_index("seq")
    width = -(-channels // 128) * 128

    flat_in = stream.reshape(rows, model)
    flat_grad = out_grad.reshape(rows, model)
    w_branch_p = widen(w_branch, width)
    w_input_p = widen(w_input, width)
    w_out_p = jnp.pad(w_out, ((0, width - channels), (0, 0))) if width > channels else w_out
    taps_p = widen(conv_kernel, width)
    def line(value):
        return widen(value, width)

    (
        normed,
        branch,
        padded,
        pre,
        hidden,
        mixed,
        carry,
        sums,
        gates,
        rates,
        ends,
    ) = recurrence_forward(
        span,
        flat_in,
        w_input_p,
        w_branch_p,
        norm_in[None],
        taps_p,
        line(conv_bias),
        line(decay_param),
        line(bias_r),
        line(bias_i),
        gate_r,
        gate_i,
        fresh_rows,
        widen(state_init, width),
        widen(jnp.swapaxes(conv_init, 0, 1), width),
    )
    made = middle_call(mixed, w_out_p, flat_in, flat_grad, norm_mlp[None], w_gate, w_up, w_down)
    block_part, resid_low, own_grad, mlp_grads, rest, own, norm_mlp_acc = made[5:]
    mlp_grads = lax.psum_scatter(mlp_grads, "seq", scatter_dimension=1, tiled=True)
    block_out, rec_grads, grad_branch, input_low, acc, blocks = backward_call(
        span,
        heads,
        head_width,
        block_part,
        own,
        resid_low,
        w_out_p,
        branch,
        hidden,
        pre,
        padded,
        normed,
        mixed,
        rest,
        gates,
        carry,
        sums,
        taps_p,
        rates,
    )

    rec_grads, grad_branch, mlp_grads = lax.optimization_barrier(
        (rec_grads, grad_branch, mlp_grads)
    )
    rec_grads = lax.psum_scatter(rec_grads, "seq", scatter_dimension=1, tiled=True)

    stream_grad, norm_grads, small = last_call(
        own_grad,
        flat_in,
        grad_branch,
        input_low,
        w_branch_p,
        w_input_p,
        norm_in[None],
        norm_mlp_acc,
        acc,
        ends,
        blocks,
    )
    (
        block_out,
        stream_grad,
        w_gate_grad,
        w_up_grad,
        w_branch_grad,
        w_input_grad,
        w_down_grad,
        w_out_grad,
        gate_r_grad,
        gate_i_grad,
        taps_grad,
        conv_bias_grad,
        bias_r_grad,
        bias_i_grad,
        decay_grad,
        norm_in_grad,
        norm_mlp_grad,
        final_state,
        final_conv,
    ) = finish_call(
        seqs,
        heads,
        head_width,
        edge,
        block_out,
        stream_grad,
        mlp_grads,
        rec_grads,
        small,
        norm_grads,
        line(decay_param),
    )
    return (
        block_out.reshape(stream.shape),
        stream_grad.reshape(stream.shape),
        norm_in_grad,
        w_branch_grad[:, :channels],
        w_input_grad[:, :channels],
        taps_grad[:, :channels],
        conv_bias_grad[:channels],
        gate_r_grad,
        bias_r_grad[:channels],
        gate_i_grad,
        bias_i_grad[:channels],
        decay_grad[:channels],
        w_out_grad[:channels],
        norm_mlp_grad,
        w_gate_grad,
        w_up_grad,
        w_down_grad,
        final_state[:, :channels],
        jnp.swapaxes(final_conv, 0, 1)[:, :, :channels],
    )


def solution(mesh):
    seq_rows = P(None, "seq", None)
    columns = P(None, "mp")
    channel = P("mp")
    return jax.shard_map(
        per_device,
        mesh=mesh,
        in_specs=(
            seq_rows,
            P(),
            columns,
            columns,
            columns,
            channel,
            P("mp", None, None),
            channel,
            P("mp", None, None),
            channel,
            channel,
            P("mp", None),
            P(),
            columns,
            columns,
            P("mp", None),
            columns,
            P(None, None, "mp"),
            P(),
            seq_rows,
        ),
        out_specs=(
            seq_rows,
            seq_rows,
            P(),
            P("seq", "mp"),
            P("seq", "mp"),
            columns,
            channel,
            P("mp", None, None),
            channel,
            P("mp", None, None),
            channel,
            channel,
            P("mp", "seq"),
            P(),
            P("seq", "mp"),
            P("seq", "mp"),
            P("mp", "seq"),
            columns,
            P(None, None, "mp"),
        ),
        check_vma=False,
    )
```

```python
import functools

import jax
import jax.numpy as jnp
from jax import lax
from jax.experimental import pallas as pl
from jax.experimental.pallas import tpu as pltpu
from jax.sharding import PartitionSpec as P

MESH = pl.DeviceIdType.MESH
RATE_SCALE = 8.0
EPS = 1e-06
GELU_C = 0.7978845608028654
GELU_K = 0.044715
CONTRACT_ROWS = (((0,), (0,)), ((), ()))
CONTRACT_LAST = (((1,), (1,)), ((), ()))
TILE = 8
LANES = 128
ROWS = 32
CHUNK = 16
SKEW = 2
GROUP = 16
WEIGHT_STEPS = 8
COPIES = 8
LATER = 6
F32 = jnp.float32
BF16 = jnp.bfloat16
VMEM = pl.BlockSpec(memory_space=pltpu.VMEM)
HBM = pl.BlockSpec(memory_space=pl.ANY)
PINNED = pl.BlockSpec(memory_space=pltpu.HBM)


def dot(a, b):
    return jnp.dot(a, b, preferred_element_type=F32)


def matmul_back(a, b):
    return lax.dot_general(a, b, CONTRACT_LAST, preferred_element_type=F32)


def block(i, size):
    return pl.ds(pl.multiple_of(i * size, size), size)


def gelu(x):
    t = jnp.tanh(GELU_C * (x + GELU_K * (x * x * x)))
    return 0.5 * x * (1.0 + t)


def gelu_both(x):
    x2 = x * x
    t = jnp.tanh(GELU_C * (x + GELU_K * (x2 * x)))
    half = 0.5 * (1.0 + t)
    slope = half + 0.5 * x * (1.0 - t * t) * (GELU_C * (1.0 + (3.0 * GELU_K) * x2))
    return x * half, slope


def one_minus_square(log_a, a):
    y = 2.0 * log_a
    s = 1.0 + y * (1.0 / 8.0)
    for k in (7, 6, 5, 4, 3, 2):
        s = 1.0 + (y * (1.0 / k)) * s
    return jnp.where(y > -0.35, -y * s, 1.0 - a * a)


def get(ref, at):
    return jnp.concatenate([ref[j, at, :] for j in range(ref.shape[0])], axis=-1)


def put(ref, at, value):
    for j in range(ref.shape[0]):
        ref[j, at, :] = value[:, j * LANES : (j + 1) * LANES]


def to_all(axis, src, slots, send, recv):
    size, me = lax.axis_size(axis), lax.axis_index(axis)
    return [
        pltpu.make_async_remote_copy(
            src_ref=src,
            dst_ref=slots.at[me],
            send_sem=send.at[d - 1],
            recv_sem=recv.at[d - 1],
            device_id={axis: lax.rem(me + d, size)},
            device_id_type=MESH,
        )
        for d in range(1, size)
    ]


def to_one(axis, distance, src, dst, send, recv):
    size, me = lax.axis_size(axis), lax.axis_index(axis)
    return pltpu.make_async_remote_copy(
        src_ref=src,
        dst_ref=dst,
        send_sem=send,
        recv_sem=recv,
        device_id={axis: lax.rem(me + distance + size, size)},
        device_id_type=MESH,
    )


def spread_gates(blocks_ref, out_ref, start, width):
    heads, size = blocks_ref.shape[:2]
    for h in range(heads):
        block_h = blocks_ref[h].astype(F32)
        parts = [block_h]
        if h > 0:
            parts.insert(0, jnp.zeros((size, h * size), F32))
        if width > (h + 1) * size:
            parts.append(jnp.zeros((size, width - (h + 1) * size), F32))
        row = jnp.concatenate(parts, axis=1).astype(BF16)
        out_ref[h * size : (h + 1) * size, start : start + width] = row
    if width > heads * size:
        rest = jnp.zeros((width - heads * size, width), BF16)
        out_ref[heads * size : width, start : start + width] = rest


def forward_kernel(
    span,
    x_in,
    w_input_in,
    w_branch_in,
    gain_ref,
    taps_ref,
    conv_bias_ref,
    decay_ref,
    bias_r_ref,
    bias_i_ref,
    gate_r_ref,
    gate_i_ref,
    fresh_ref,
    state_ref,
    conv_init_ref,
    normed_out,
    branch_out,
    pad_out,
    pre_out,
    hidden_out,
    mixed_ref,
    carry_ref,
    sums_ref,
    gates_ref,
    vec_ref,
    ends_ref,
    x_ref,
    w_input_ref,
    w_branch_ref,
    normed_ref,
    branch_ref,
    pad_ref,
    pre_ref,
    hidden_ref,
    act_ref,
    a_ref,
    b_ref,
    conv_ref,
    tail_ref,
    tail_in,
    mine_ref,
    load_sem,
    store_sem,
    normed_sem,
    send1,
    recv1,
    send_t,
    recv_t,
):
    seqs = state_ref.shape[0]
    width = taps_ref.shape[1]
    taps = taps_ref.shape[0]
    rows = seqs * span
    devices, me = lax.axis_size("seq"), lax.axis_index("seq")
    local = pltpu.make_async_copy
    pitch = a_ref.shape[1] // seqs
    group = 2 * span
    groups = rows // group

    def x_load(g):
        at = block(g, group)
        return local(x_in.at[at], x_ref.at[at], load_sem.at[g])

    weight_loads = [
        local(w_input_in, w_input_ref, load_sem.at[groups]),
        local(w_branch_in, w_branch_ref, load_sem.at[groups + 1]),
    ]
    x_load(0).start()
    weight_loads[0].start()
    for g in range(1, groups):
        x_load(g).start()
    weight_loads[1].start()

    enter_all(("seq",))
    spread_gates(gate_r_ref, gates_ref, 0, width)
    spread_gates(gate_i_ref, gates_ref, width, width)
    vec_ref[0:1, :] = conv_bias_ref[...].reshape(1, width)
    vec_ref[1:2, :] = jax.nn.softplus(-decay_ref[...].reshape(1, width))
    bias_r = bias_r_ref[...].reshape(1, width)
    bias_i = bias_i_ref[...].reshape(1, width)
    keep = [1.0 - fresh_ref[s].astype(F32) for s in range(seqs)]

    def normed_store(g):
        at = block(g, group)
        return local(normed_ref.at[at], normed_out.at[at], normed_sem.at[g])

    def norm(g):
        x_load(g).wait()
        for q in range(group // CHUNK):
            at = slice(g * group + q * CHUNK, g * group + (q + 1) * CHUNK)
            x = x_ref[at, :]
            normed_ref[at, :] = (x * mean_square(x) * gain_ref[...]).astype(BF16)

    norm(0)
    weight_loads[0].wait()
    for g in range(groups):
        if g + 1 < groups:
            norm(g + 1)
        conv = dot(normed_ref[slice(g * group, (g + 1) * group), :], w_input_ref[...])
        for j in range(group // span):
            pad_ref[g * (group // span) + j, pl.ds(TILE, span), :] = conv[
                j * span : (j + 1) * span
            ]
    for g in range(groups):
        normed_store(g).start()

    for s in range(seqs):
        tail_ref[s] = pad_ref[s, pl.ds(span, TILE), :]
    tail_copy = to_one("seq", 1, tail_ref, tail_in, send_t.at[0], recv_t.at[0])
    tail_copy.start()
    weight_loads[1].wait()

    def branch(g):
        branch_ref[block(g, group), :] = dot(normed_ref[block(g, group), :], w_branch_ref[...])

    @pl.loop(0, groups // 2)
    def _(g):
        branch(g)

    stores = [
        local(source, target, store_sem.at[i])
        for i, (source, target) in enumerate(
            (
                (branch_ref, branch_out),
                (pad_ref, pad_out),
                (pre_ref, pre_out),
                (hidden_ref, hidden_out),
            )
        )
    ]
    tail_copy.wait()
    lead = jnp.zeros((TILE - taps + 1, width), F32)
    for s in range(seqs):
        initial = jnp.concatenate(
            [lead] + [conv_init_ref[k, s : s + 1, :] * keep[s] for k in range(taps - 1)], axis=0
        )
        pad_ref[s, pl.ds(0, TILE), :] = jnp.where(me == 0, initial, tail_in[s])
    stores[1].start()

    def gates(s, slot):
        for q in range(span // ROWS):
            part = pad_ref[s, pl.ds(q * ROWS, ROWS + TILE), :]
            total = vec_ref[0:1, :]
            for k in range(taps):
                first = TILE - (taps - 1) + k
                total = total + taps_ref[k : k + 1, :] * part[first : first + ROWS]
            conv_ref[slot, pl.ds(q * ROWS, ROWS), :] = total

        pre = dot(conv_ref[slot].astype(BF16), gates_ref[...])
        pre_ref[block(s, span), :width] = pre[:, :width] + bias_r
        pre_ref[block(s, span), width:] = pre[:, width:] + bias_i
        for q in range(span // ROWS):
            rows_q = slice(q * ROWS, (q + 1) * ROWS)
            conv = conv_ref[slot, pl.ds(q * ROWS, ROWS), :]
            recall = jax.nn.sigmoid(pre[rows_q, :width] + bias_r)
            gate = jax.nn.sigmoid(pre[rows_q, width:] + bias_i)
            log_a = (-RATE_SCALE * vec_ref[1:2, :]) * recall
            a = jnp.exp(log_a)
            spaced = pl.ds(pl.multiple_of(s * pitch + q * ROWS, TILE), ROWS)
            put(a_ref, spaced, a)
            put(b_ref, spaced, jnp.sqrt(one_minus_square(log_a, a)) * gate * conv)

    per = seqs // (groups - groups // 2)

    @pl.loop(0, groups - groups // 2)
    def _(i):
        branch(groups // 2 + i)
        for j in range(per):
            gates(i * per + j, j % 2)

    stores[0].start()
    stores[2].start()

    def at_time(ref, t):
        return get(ref, pl.ds(t, seqs, stride=pitch))

    def step(t, value):
        prod, state = value
        a = at_time(a_ref, t)
        return prod * a, a * state + at_time(b_ref, t)

    ones = jnp.ones((seqs, width), F32)
    prod, state = lax.fori_loop(0, span, step, (ones, jnp.zeros_like(ones)), unroll=8)
    mine_ref[0] = prod
    mine_ref[1] = state
    sums_ref[me] = mine_ref[...]
    copies = to_all("seq", mine_ref, sums_ref, send1, recv1)
    for copy in copies:
        copy.start()

    @pl.loop(0, rows // ROWS, unroll=2)
    def _(q):
        at = block(q, ROWS)
        act_ref[at, :] = gelu(branch_ref[at, :])

    for copy in copies:
        copy.wait()

    def carry_step(j, carry):
        both = sums_ref[j]
        return jnp.where(j < me, both[0] * carry + both[1], carry)

    start = jnp.concatenate([state_ref[s : s + 1, :] * keep[s] for s in range(seqs)], axis=0)
    carry = lax.fori_loop(0, devices - 1, carry_step, start)
    carry_ref[...] = carry

    def final(t, state):
        state = at_time(a_ref, t) * state + at_time(b_ref, t)
        put(hidden_ref, pl.ds(t, seqs, stride=span), state)
        return state

    last = lax.fori_loop(0, span, final, carry, unroll=8)
    stores[3].start()
    ends_ref[0:seqs, :] = jnp.where(me == devices - 1, last, 0.0)
    for s in range(seqs):
        ends_ref[(s + 1) * TILE : (s + 2) * TILE, :] = jnp.where(
            me == devices - 1, pad_ref[s, pl.ds(span, TILE), :], 0.0
        )

    @pl.loop(0, rows // ROWS, unroll=2)
    def _(q):
        at = block(q, ROWS)
        mixed_ref[at, :] = (get(hidden_ref, at) * act_ref[at, :]).astype(BF16)

    for copy in stores:
        copy.wait()
    for g in range(groups):
        normed_store(g).wait()


def backward_kernel(
    span,
    heads,
    block_part_in,
    own_in,
    low_in,
    w_out_in,
    branch_in,
    hidden_in,
    pre_in,
    pad_in,
    normed_in,
    mixed_in,
    rest_in,
    gates_in,
    w_branch_in,
    w_input_in,
    carry_ref,
    sums_ref,
    taps_ref,
    vec_ref,
    block_out,
    rec_out,
    grad_branch_out,
    input_out,
    first_out,
    acc_ref,
    blocks_ref,
    part,
    inbox,
    out,
    send_up,
    send_down,
    recv_up,
    recv_down,
    own_ref,
    resid_low,
    w_out_ref,
    branch_ref,
    hidden_ref,
    pre_ref,
    pad_ref,
    normed_ref,
    mixed_ref,
    a_ref,
    gd_ref,
    grad_ref,
    direct_ref,
    gpad_ref,
    heads_ref,
    low_ref,
    gates_grad,
    stage_ref,
    mine_ref,
    entries_ref,
    head_ref,
    head_in,
    load_sem,
    part_sem,
    store_sem,
    stage_sem,
    send1,
    recv1,
    send_t,
    recv_t,
    gates_ref,
    grad_branch_ref,
    input_ref,
    give_sem,
    late_sem,
):
    seqs, width = carry_ref.shape
    taps = taps_ref.shape[0]
    rows = seqs * span
    devices, me = lax.axis_size("seq"), lax.axis_index("seq")
    n, z = lax.axis_size("mp"), lax.axis_index("mp")
    chunks = rows // CHUNK
    size = GROUP * CHUNK
    held = part.shape[0] // size
    groups = chunks // GROUP
    sems = (send_up, send_down, recv_up, recv_down)
    local = pltpu.make_async_copy

    def part_load(g):
        slot = lax.rem(g, held)
        return local(block_part_in.at[block(g, size)], part.at[block(slot, size)], part_sem.at[slot])

    loads = [
        local(source, target, load_sem.at[i])
        for i, (source, target) in enumerate(
            (
                (own_in, own_ref),
                (low_in, resid_low),
                (w_out_in, w_out_ref),
                (pre_in, pre_ref),
                (branch_in, branch_ref),
                (hidden_in, hidden_ref),
                (pad_in, pad_ref),
                (mixed_in, mixed_ref),
                (normed_in, normed_ref),
                (gates_in, gates_ref),
            )
        )
    ]
    part_load(0).start()
    for copy in loads[:6]:
        copy.start(priority=1)
    for g in range(1, held):
        part_load(g).start()
    for copy in loads[6:]:
        copy.start(priority=1)
    acc_ref[...] = jnp.zeros_like(acc_ref)
    enter_all(("seq", "mp"))

    pitch = a_ref.shape[1] // seqs

    def spaced(s, q):
        return pl.ds(pl.multiple_of(s * pitch + q * ROWS, TILE), ROWS)

    def decay(at):
        recall = jax.nn.sigmoid(pre_ref[at, :width])
        log_a = (-RATE_SCALE * vec_ref[1:2, :]) * recall
        return recall, log_a, jnp.exp(log_a)

    def piece_direct(s):
        @pl.when(s == 0)
        def _():
            for copy in loads[1:6]:
                copy.wait()

        grad_ref[...] = matmul_back(resid_low[block(s, span), :], w_out_ref[...])

        @pl.loop(0, span // ROWS)
        def _(q):
            at = block(s * (span // ROWS) + q, ROWS)
            put(a_ref, spaced(s, q), decay(at)[2])
            act, slope = gelu_both(branch_ref[at, :])
            grad = grad_ref[block(q, ROWS), :]
            put(gd_ref, spaced(s, q), grad * act)
            grad_branch_ref[at, :] = (grad * get(hidden_ref, at) * slope).astype(BF16)

    def at_time(ref, t):
        return get(ref, pl.ds(t, seqs, stride=pitch))

    zero = jnp.zeros((seqs, width), F32)
    entry_copies = to_all("seq", mine_ref, entries_ref, send1, recv1)

    def piece_entry(_):
        def step(k, through):
            t = span - 1 - k
            return at_time(a_ref, t) * (at_time(gd_ref, t) + through)

        mine_ref[...] = lax.fori_loop(0, span, step, zero, unroll=8)
        entries_ref[me] = mine_ref[...]
        for copy in entry_copies:
            copy.start()

    def piece_state(_):
        for copy in entry_copies:
            copy.wait()

        def back_step(k, through):
            j = devices - 1 - k
            return jnp.where(j > me, entries_ref[j] + sums_ref[j, 0] * through, through)

        incoming = lax.fori_loop(0, devices - 1, back_step, zero)

        def final(k, through):
            t = span - 1 - k
            grad = at_time(gd_ref, t) + through
            put(gd_ref, pl.ds(t, seqs, stride=pitch), grad)
            return at_time(a_ref, t) * grad

        lax.fori_loop(0, span, final, incoming, unroll=8)

    def add(k, value):
        acc_ref[k] += fold(value)

    parts = 2

    def piece_gates(i):
        s = i // parts
        quarters = span // ROWS // parts

        @pl.when(i == 0)
        def _():
            loads[6].wait()
            loads[9].wait()

        @pl.loop(lax.rem(i, parts) * quarters, (lax.rem(i, parts) + 1) * quarters)
        def _(q):
            at = block(s * (span // ROWS) + q, ROWS)
            part_rows = pad_ref[s, pl.ds(pl.multiple_of(q * ROWS, ROWS), ROWS + TILE), :]
            conv = vec_ref[0:1, :]
            for k in range(taps):
                first = TILE - (taps - 1) + k
                conv = conv + taps_ref[k : k + 1, :] * part_rows[first : first + ROWS]
            heads_ref[at, :] = conv.astype(BF16)
            recall, log_a, a = decay(at)
            gate = jax.nn.sigmoid(pre_ref[at, width:])
            square = one_minus_square(log_a, a)
            inverse = lax.rsqrt(square)
            root = jnp.sqrt(square)
            grad = get(gd_ref, spaced(s, q))
            hidden = get(hidden_ref, at)
            before_at = pl.multiple_of(jnp.maximum(s * span + q * ROWS - TILE, 0), TILE)
            earlier = get(hidden_ref, pl.ds(before_at, TILE))
            first_row = jnp.where(q == 0, carry_ref[pl.ds(s, 1), :], earlier[TILE - 1 :])
            place = lax.broadcasted_iota(jnp.int32, (ROWS, width), 0)
            prev = jnp.where(place == 0, first_row, pltpu.roll(hidden, 1, 0))
            grad_log = grad * a * (prev - gate * conv * a * inverse)
            through = grad_log * recall
            pre_r = through * (1.0 - recall) * (-RATE_SCALE * vec_ref[1:2, :])
            direct = grad * root * gate
            pre_i = direct * conv * (1.0 - gate)
            low_ref[at, :width] = pre_r.astype(BF16)
            low_ref[at, width:] = pre_i.astype(BF16)
            direct_ref[block(q, ROWS), :] = direct
            add(0, through)
            add(1, pre_r)
            add(2, pre_i)

        @pl.when(lax.rem(i, parts) == parts - 1)
        def _():
            whole = direct_ref[...] + matmul_back(low_ref[block(s, span), :], gates_ref[...])
            gpad_ref[s, pl.ds(0, span), :] = whole
            head_ref[s] = whole[:TILE]

    head_copy = to_one("seq", -1, head_ref, head_in, send_t.at[0], recv_t.at[0])

    def piece_head(_):
        head_copy.start()

    def piece_taps(i):
        for j in range(2):
            taps_of(2 * i + j)

    def taps_of(s):
        @pl.loop(0, span // ROWS)
        def _(q):
            at = pl.multiple_of(q * ROWS, ROWS)
            part_rows = pad_ref[s, pl.ds(at, ROWS + TILE), :]
            grad = gpad_ref[s, pl.ds(at, ROWS), :]
            add(3, grad)
            for k in range(taps):
                first = TILE - (taps - 1) + k
                add(4 + k, grad * part_rows[first : first + ROWS])

    def piece_tail(_):
        head_copy.wait()
        for s in range(seqs):
            gpad_ref[s, pl.ds(span, TILE), :] = jnp.where(me == devices - 1, 0.0, head_in[s])

    def piece_input(i):
        for j in range(2):
            input_of(2 * i + j)

    def input_of(s):
        @pl.loop(0, span // ROWS)
        def _(q):
            part_rows = gpad_ref[s, pl.ds(pl.multiple_of(q * ROWS, ROWS), ROWS + TILE), :]
            total = taps_ref[taps - 1 : taps, :] * part_rows[0:ROWS]
            for k in range(taps - 1):
                first = taps - 1 - k
                total = total + taps_ref[k : k + 1, :] * part_rows[first : first + ROWS]
            input_ref[block(s * (span // ROWS) + q, ROWS), :] = total.astype(BF16)

    def contract(left, right):
        return lax.dot_general(left, right, CONTRACT_ROWS, preferred_element_type=F32)

    head = blocks_ref.shape[0]

    late_loads = [
        local(source.at[slice(i * rows, (i + 1) * rows)], target, late_sem.at[2 * j + i])
        for j, (source, targets) in enumerate(
            (
                (
                    w_branch_in,
                    (
                        resid_low.at[:, pl.ds(0, width)],
                        resid_low.at[:, pl.ds(width, width)],
                    ),
                ),
                (w_input_in, (resid_low.at[:, pl.ds(2 * width, width)], mixed_ref)),
            )
        )
        for i, target in enumerate(targets)
    ]
    first_copy = local(part.at[slice(size, 2 * size)], first_out, late_sem.at[4])

    def piece_projections(_):
        for copy in late_loads:
            copy.start(priority=1)

    def piece_first(i):
        branch_rows = grad_branch_ref[:size, :]
        input_rows = input_ref[:size, :]

        @pl.when(i == 0)
        def _():
            for copy in late_loads:
                copy.wait()

            part[size : 2 * size, :rows] = matmul_back(
                branch_rows, resid_low[:, :width]
            ) + matmul_back(input_rows, resid_low[:, 2 * width : 3 * width])

        @pl.when(i == 1)
        def _():
            part[size : 2 * size, rows:] = matmul_back(
                branch_rows, resid_low[:, width : 2 * width]
            ) + matmul_back(input_rows, mixed_ref[...])
            first_copy.start(priority=1)

    gives = [
        local(grad_branch_ref, grad_branch_out, give_sem.at[0]),
        local(input_ref, input_out, give_sem.at[1]),
    ]

    def piece_give(_):
        for copy in gives:
            copy.start(priority=1)

    def piece_gates_grad(i):
        @pl.when(i == 0)
        def _():
            gates_grad[...] = contract(heads_ref[...], low_ref[:, :width])

        @pl.when(i == 1)
        def _():
            gates_grad[...] = contract(heads_ref[...], low_ref[:, width:])

        place = lax.broadcasted_iota(jnp.int32, (head, width), 1)
        line = jnp.zeros((head, width), F32)
        for h in range(heads):
            row = gates_grad[h * head : (h + 1) * head, :]
            inside = jnp.logical_and(place >= h * head, place < (h + 1) * head)
            line = jnp.where(inside, row, line)

        for j in range(2):

            @pl.when(i == j)
            def _():
                blocks_ref[:, j * width : (j + 1) * width] = line

    tall = resid_low.shape[1] // WEIGHT_STEPS

    def stage_store(i):
        at = block(lax.rem(i, WEIGHT_STEPS), tall)
        slot = lax.rem(i, 2)
        return local(
            stage_ref.at[slot],
            rec_out.at[i // WEIGHT_STEPS, at, pl.ds(0, width)],
            stage_sem.at[slot],
        )

    def piece_weights(i):
        @pl.when(i == 0)
        def _():
            loads[7].wait()
            loads[8].wait()

        @pl.loop(2 * i, 2 * i + 2)
        def _(j):
            weight_of(j)

    def weight_of(i):
        @pl.when(i >= 2)
        def _():
            stage_store(i - 2).wait()

        at = block(lax.rem(i, WEIGHT_STEPS), tall)
        slot = lax.rem(i, 2)
        for which, (left, right) in enumerate(
            ((resid_low, mixed_ref), (normed_ref, grad_branch_ref), (normed_ref, input_ref))
        ):
            @pl.when(i // WEIGHT_STEPS == which)
            def _():
                stage_ref[slot] = contract(left[:, at], right[...])

        stage_store(i).start(priority=1)

    weights = 3 * WEIGHT_STEPS
    plan = []
    begin = 3
    early = WEIGHT_STEPS // 2

    def piece_weights_later(i):
        piece_weights(i + early)

    for work, times, gap in (
        (piece_direct, seqs, 0),
        (piece_entry, 1, 0),
        (piece_weights, early, 0),
        (piece_projections, 1, 4),
        (piece_state, 1, 0),
        (piece_gates, parts * seqs, 0),
        (piece_head, 1, 0),
        (piece_taps, seqs // 2, 0),
        (piece_gates_grad, 2, 3),
        (piece_tail, 1, 0),
        (piece_input, seqs // 2, 0),
        (piece_give, 1, 0),
        (piece_first, 2, 0),
        (piece_weights_later, weights // 2 - early, 0),
    ):
        plan.append((work, begin, times))
        begin += times + gap

    def run(step):
        for work, first, times in plan:
            @pl.when(jnp.logical_and(step >= first, step < first + times))
            def _():
                work(step - first)

    def before(k):
        @pl.when(k == SKEW * (n // 2))
        def _():
            loads[0].wait()

        @pl.when(jnp.logical_and(lax.rem(k, GROUP) == 0, k < chunks))
        def _():
            part_load(k // GROUP).wait()

        g = (k - out.shape[0]) // GROUP - 1 + held

        @pl.when(
            jnp.logical_and(
                jnp.logical_and(k >= out.shape[0] + GROUP, lax.rem(k - out.shape[0], GROUP) == 0),
                g < groups,
            )
        )
        def _():
            part_load(g).start(priority=1)

        run(k)

    def root(c, slot, total):
        out[slot] = own_ref[block(c // 2, CHUNK), :] + total

    def store(c, slot):
        return local(out.at[slot], block_out.at[block(c, CHUNK)], store_sem.at[slot])

    def arrive(c, slot):
        store(c, slot).start(priority=1)

    def leave(c, slot):
        store(c, slot).wait()

    line_sum(
        "mp", chunks, held * GROUP, part, inbox, out, sems, before, root, arrive, leave
    )

    @pl.loop(chunks + out.shape[0], max(begin, chunks + out.shape[0]))
    def _(k):
        run(k)

    for copy in gives:
        copy.wait()
    first_copy.wait()
    stage_store(weights - 2).wait()
    stage_store(weights - 1).wait()


def backward_call(span, heads, head, *args):
    block_part = args[0]
    low, w_out, branch, hidden, pre, padded, normed, mixed, rest, gates = args[2:12]
    carry, sums, taps = args[14:17]
    rows, model = block_part.shape
    seqs, width = carry.shape
    devices = lax.axis_size("seq")
    ring = ring_size("mp")
    held = 3 * GROUP * CHUNK
    dma = pltpu.SemaphoreType.DMA
    columns = pltpu.VMEM((width // LANES, seqs * (span + TILE), LANES), F32)
    return pl.pallas_call(
        functools.partial(backward_kernel, span, heads),
        out_shape=(
            shape((rows, model)),
            shape(rest.shape),
            shape((rows, width), BF16),
            shape((rows, width), BF16),
            shape((GROUP * CHUNK, model)),
            shape((4 + taps.shape[0], TILE, width)),
            shape((head, 2 * width)),
        ),
        in_specs=[HBM] * 14 + [VMEM] * 4,
        input_output_aliases={10: 1},
        out_specs=(HBM,) * 5 + (VMEM,) * 2,
        scratch_shapes=line_scratch("mp", held, model)
        + [
            pltpu.VMEM((rows // 2, model), F32),
            pltpu.VMEM((rows, model), BF16),
            pltpu.VMEM((width, model), BF16),
            pltpu.VMEM((rows, width), F32),
            pltpu.VMEM(hidden.shape, F32),
            pltpu.VMEM(pre.shape, F32),
            pltpu.VMEM(padded.shape, F32),
            pltpu.VMEM((rows, model), BF16),
            pltpu.VMEM((rows, width), BF16),
            columns,
            columns,
            pltpu.VMEM((span, width), F32),
            pltpu.VMEM((span, width), F32),
            pltpu.VMEM((seqs, span + TILE, width), F32),
            pltpu.VMEM((rows, width), BF16),
            pltpu.VMEM((rows, 2 * width), BF16),
            pltpu.VMEM((width, width), F32),
            pltpu.VMEM((2, model // WEIGHT_STEPS, width), F32),
            pltpu.VMEM((seqs, width), F32),
            pltpu.VMEM((devices, seqs, width), F32),
            pltpu.VMEM((seqs, TILE, width), F32),
            pltpu.VMEM((seqs, TILE, width), F32),
            dma((10,)),
            dma((3,)),
            dma((ring,)),
            dma((2,)),
            dma((devices - 1,)),
            dma((devices - 1,)),
            dma((1,)),
            dma((1,)),
            pltpu.VMEM(gates.shape, BF16),
            pltpu.VMEM((rows, width), BF16),
            pltpu.VMEM((rows, width), BF16),
            dma((2,)),
            dma((5,)),
        ],
        compiler_params=params(1, 63),
        cost_estimate=cost(200),
        name="backward",
    )(*args)


def line_sum(axis, total, period, part, inbox, out, sems, before, root, arrive, leave):
    send_up, send_down, recv_up, recv_down = sems
    parts = send_up.shape[0]
    columns = out.shape[2] // parts
    n, z = lax.axis_size(axis), lax.axis_index(axis)
    depth = n // 2
    ring = out.shape[0]

    def cols(p):
        return pl.ds(p * columns, columns)

    def root_of(c):
        return depth - 1 + lax.rem(c, 2)

    def up(c, step, side, p):
        slot = lax.rem(c, ring)
        return pltpu.make_async_remote_copy(
            src_ref=part.at[block(lax.rem(c, period), CHUNK), cols(p)],
            dst_ref=inbox.at[side, slot, :, cols(p)],
            send_sem=send_up.at[p, slot],
            recv_sem=recv_up.at[p, side, slot],
            device_id={axis: z + step},
            device_id_type=MESH,
        )

    def down(c, step, side, p):
        slot = lax.rem(c, ring)
        return pltpu.make_async_remote_copy(
            src_ref=out.at[slot, :, cols(p)],
            dst_ref=out.at[slot, :, cols(p)],
            send_sem=send_down.at[p, side, slot],
            recv_sem=recv_down.at[p, slot],
            device_id={axis: z + step},
            device_id_type=MESH,
        )

    inner = jnp.logical_and(z > 0, z < n - 1)

    @pl.loop(0, total + ring)
    def _(k):
        @pl.when(k >= ring)
        def _():
            c = k - ring
            r = root_of(c)
            step = jnp.where(z < r, 1, -1)
            side = jnp.where(z < r, 0, 1)

            @pl.when(z == r)
            def _():
                for p in range(parts):
                    down(c, -1, 0, p).wait_send()
                    down(c, 1, 1, p).wait_send()

            @pl.when(z != r)
            def _():
                for p in range(parts):
                    up(c, step, side, p).wait_send()

            @pl.when(jnp.logical_and(z != r, inner))
            def _():
                for p in range(parts):
                    down(c, -step, side, p).wait_send()

            leave(c, lax.rem(c, ring))

        before(k)

        for i in reversed(range(n + 1)):
            c = k - SKEW * i
            valid = jnp.logical_and(c >= 0, c < total)
            c = jnp.clip(c, 0, total - 1)
            at = block(lax.rem(c, period), CHUNK)
            slot = lax.rem(c, ring)
            r = root_of(c)
            step = jnp.where(z < r, 1, -1)
            side = jnp.where(z < r, 0, 1)
            if i > depth:
                here = jnp.logical_and(z != r, jnp.abs(z - r) == i - depth)

                @pl.when(jnp.logical_and(valid, here))
                def _():
                    for p in range(parts):
                        down(c, step, side, p).wait_recv()

                        @pl.when(inner)
                        def _():
                            down(c, -step, side, p).start()

                    arrive(c, slot)
            elif i == depth:

                @pl.when(jnp.logical_and(valid, z == r))
                def _():
                    for p in range(parts):
                        up(c, 1, 0, p).wait_recv()
                        up(c, -1, 1, p).wait_recv()
                    root(c, slot, part[at, :] + inbox[0, slot] + inbox[1, slot])
                    for p in range(parts):
                        down(c, -1, 0, p).start()
                        down(c, 1, 1, p).start()
                    arrive(c, slot)
            else:
                here = jnp.where(z < r, z, n - 1 - z) == i

                @pl.when(jnp.logical_and(valid, jnp.logical_and(z != r, here)))
                def _():
                    for p in range(parts):
                        if i > 0:
                            up(c, step, side, p).wait_recv()
                            part[at, cols(p)] += inbox[side, slot, :, cols(p)]
                        up(c, step, side, p).start()


def ring_size(axis):
    return SKEW * lax.axis_size(axis) + 4


def line_scratch(axis, rows, model, parts=2):
    dma = pltpu.SemaphoreType.DMA
    ring = ring_size(axis)
    return [
        pltpu.VMEM((rows, model), F32),
        pltpu.VMEM((2, ring, CHUNK, model), F32),
        pltpu.VMEM((ring, CHUNK, model), F32),
        dma((parts, ring)),
        dma((parts, 2, ring)),
        dma((parts, 2, ring)),
        dma((parts, ring)),
    ]


def mean_square(x):
    return lax.rsqrt(jnp.mean(x * x, axis=-1, keepdims=True) + EPS)


def nothing(*_):
    pass


def fold(value):
    total = value[0:TILE]
    for i in range(1, value.shape[0] // TILE):
        total = total + value[i * TILE : (i + 1) * TILE]
    return total


def norm_grad(value, gain, grad, acc_ref):
    q = mean_square(value)
    e = gain * grad
    acc_ref[...] += fold(grad * value * q)
    return q * e - value * (q * q * q) * jnp.mean(e * value, axis=-1, keepdims=True)


def middle_kernel(
    mixed_in,
    w_out_in,
    x_in,
    og_in,
    gain_ref,
    w_gate_in,
    w_up_in,
    w_down_in,
    normed_out,
    hidden_out,
    gate_out,
    up_out,
    glow_out,
    block_out,
    low_out,
    own_grad_out,
    weight_out,
    rest_out,
    own_out,
    acc_ref,
    part,
    inbox,
    out,
    send_up,
    send_down,
    recv_up,
    recv_down,
    mixed,
    w_out,
    w_gate,
    w_up,
    w_down,
    normed,
    rows_ref,
    og_ref,
    glow,
    gate_val,
    up_val,
    grad_hidden,
    hidden,
    grad_gate,
    grad_up,
    block_part,
    low,
    weight_sem,
    row_sem,
    og_sem,
    act_sem,
    low_sem,
    own_sem,
    again_sem,
    stage_sem,
    rest_sem,
    own_ref,
):
    n, z = lax.axis_size("mp"), lax.axis_index("mp")
    count = part.shape[0] // CHUNK
    size = GROUP * CHUNK
    groups = count // GROUP
    ring = out.shape[0]
    sems = (send_up, send_down, recv_up, recv_down)
    local = pltpu.make_async_copy

    loads = [
        local(source, target, weight_sem.at[i])
        for i, (source, target) in enumerate(
            (
                (mixed_in, mixed),
                (w_out_in, w_out),
                (w_gate_in, w_gate),
                (w_up_in, w_up),
                (w_down_in, w_down.at[slice(0, w_down_in.shape[0])]),
            )
        )
    ]
    for copy in loads:
        copy.start(priority=1)
    deep = w_down_in.shape[0]

    def og_load(g):
        return local(og_in.at[block(g, size)], og_ref, og_sem.at[0])

    og_load(0).start(priority=1)
    enter_all(("mp",))
    acc_ref[...] = jnp.zeros_like(acc_ref)
    loads[0].wait()
    loads[1].wait()

    def is_root(c):
        return z == n // 2 - 1 + lax.rem(c, 2)

    def row_load(source, c):
        slot = lax.rem(c, ring)
        at = block(lax.rem(c, count), CHUNK)
        return local(source.at[at], rows_ref.at[slot], row_sem.at[slot])

    acts = (
        (normed, normed_out),
        (glow, glow_out),
        (hidden, hidden_out),
        (grad_gate, gate_out),
        (grad_up, up_out),
        (block_part, block_out),
    )

    def act_store(i, g):
        source, target = acts[i]
        source = source.at[lax.rem(g, 2)] if i == 0 else source
        return local(source, target.at[block(g, size)], act_sem.at[i])

    def at_tick(k, first, work):
        g = (k - first) // GROUP

        @pl.when(
            jnp.logical_and(
                jnp.logical_and(k >= first, k < first + GROUP * groups),
                lax.rem(k - first, GROUP) == 0,
            )
        )
        def _():
            work(g)

    def project(g):
        def work(cols):
            part[block(g, size), cols] = dot(mixed[block(g, size), :], w_out[:, cols])

        work(slice(None))

    def piece_gate(g):
        @pl.when(g == 0)
        def _():
            for copy in loads[2:]:
                copy.wait()

        def work(cols):
            gate_val[:, cols] = dot(normed[lax.rem(g, 2)], w_gate[:, cols])

        work(slice(None))
        act_store(0, g).start(priority=1)

    def piece_up(g):
        def work(cols):
            up_val[:, cols] = dot(normed[lax.rem(g, 2)], w_up[:, cols])

        work(slice(None))

        @pl.when(g > 0)
        def _():
            for i in range(1, 6):
                act_store(i, g - 1).wait()

    def piece_low(g):
        og_load(g).wait()

        @pl.loop(0, size // ROWS)
        def _(q):
            glow[block(q, ROWS), :] = og_ref[block(q, ROWS), :].astype(BF16)

        @pl.when(g + 1 < groups)
        def _():
            og_load(g + 1).start(priority=1)

        act_store(1, g).start(priority=1)
        act_store(0, g).wait()

    def piece_hidden(g):
        def work(cols):
            grad_hidden[...] = matmul_back(glow[...], w_down[:deep, :])

        work(slice(None))

    def piece_act(g):
        @pl.loop(0, size // CHUNK)
        def _(q):
            at = block(q, CHUNK)
            up = up_val[at, :]
            grad = grad_hidden[at, :]
            act, slope = gelu_both(gate_val[at, :])
            hidden[at, :] = (act * up).astype(BF16)
            grad_gate[at, :] = (grad * up * slope).astype(BF16)
            grad_up[at, :] = (grad * act).astype(BF16)

        for i in range(2, 5):
            act_store(i, g).start(priority=1)

    def piece_down(g):
        def work(cols):
            block_part[:, cols] = dot(hidden[...], w_down[:deep, cols])

        work(slice(None))
        act_store(5, g).start(priority=1)

    def piece_back_gate(g):
        def work(cols):
            part[block(g, size), cols] = matmul_back(grad_gate[...], w_gate[cols, :])

        work(slice(None))

    def piece_back_up(g):
        def work(cols):
            part[block(g, size), cols] += matmul_back(grad_up[...], w_up[cols, :])

        work(slice(None))

    tokens = count * CHUNK
    half = tokens // 2
    quarter = half // 2
    again = [
        local(source, target, again_sem.at[i])
        for i, (source, target) in enumerate(
            (
                (normed_out, w_down.at[slice(0, tokens)]),
                (gate_out, w_gate.at[slice(0, tokens)]),
                (up_out, w_up.at[slice(0, tokens)]),
                (hidden_out, w_gate.at[slice(tokens, 2 * tokens)]),
                (glow_out.at[slice(0, half)], w_down.at[slice(tokens, tokens + half)]),
                (glow_out.at[slice(half, half + quarter)], normed.at[0]),
                (glow_out.at[slice(half + quarter, tokens)], normed.at[1]),
            )
        )
    ]
    tall = w_gate.shape[0] // WEIGHT_STEPS
    stages = (gate_val, up_val, grad_hidden)

    kept = weight_out.shape[2]
    before_rest = rest_out.shape[2] - (deep - kept)

    def stage_stores(which, i):
        at = block(i, tall)
        return (
            local(
                stages[which].at[:, pl.ds(0, kept)],
                weight_out.at[which, at],
                stage_sem.at[which],
            ),
            local(
                stages[which].at[:, pl.ds(kept, deep - kept)],
                rest_out.at[which, at, pl.ds(before_rest, deep - kept)],
                rest_sem.at[which],
            ),
        )

    own_copy = local(own_ref, own_out, rest_sem.at[3])

    def piece_reload():
        own_copy.start(priority=1)
        for i in range(1, 6):
            act_store(i, groups - 1).wait()
        for copy in again:
            copy.start(priority=1)

    def piece_ready():
        for copy in again:
            copy.wait()

    def contract(left, right):
        return lax.dot_general(left, right, CONTRACT_ROWS, preferred_element_type=F32)

    def piece_weight(step):
        i = step // 3
        at = block(i, tall)
        for which in range(3):

            @pl.when(lax.rem(step, 3) == which)
            def _():
                @pl.when(i > 0)
                def _():
                    for copy in stage_stores(which, i - 1):
                        copy.wait()

                stage = stages[which]

                def work(cols):
                    if which == 0:
                        stage[:, cols] = contract(w_down[:tokens, at], w_gate[:tokens, cols])
                    elif which == 1:
                        stage[:, cols] = contract(w_down[:tokens, at], w_up[:tokens, cols])
                    else:
                        middle = tokens + half + quarter
                        stage[:, cols] = (
                            contract(
                                w_down[tokens : tokens + half, at],
                                w_gate[tokens : tokens + half, cols],
                            )
                            + contract(normed[0, :, at], w_gate[tokens + half : middle, cols])
                            + contract(normed[1, :, at], w_gate[middle : 2 * tokens, cols])
                        )

                work(slice(None))
                for copy in stage_stores(which, i):
                    copy.start(priority=1)

    first = GROUP + SKEW * n
    spare = GROUP * groups + ring + 3
    first_weight = spare + 3
    weights = 3 * WEIGHT_STEPS

    def before(k):
        @pl.when(k == spare)
        def _():
            piece_reload()

        @pl.when(k == first_weight - 1)
        def _():
            piece_ready()

        @pl.when(jnp.logical_and(k >= first_weight, k < first_weight + weights))
        def _():
            piece_weight(k - first_weight)

        @pl.when(jnp.logical_and(k < count, is_root(k)))
        def _():
            row_load(x_in, k).start(priority=1)

        @pl.when(
            jnp.logical_and(jnp.logical_and(k >= count, k < 2 * count), is_root(k))
        )
        def _():
            row_load(og_in, k).start(priority=1)

        at_tick(k, 0, project)
        at_tick(k, first, piece_gate)
        at_tick(k, first + 1, piece_up)
        at_tick(k, first + 2, piece_low)
        at_tick(k, first + 3, piece_hidden)
        at_tick(k, first + 4, piece_act)
        at_tick(k, first + 6, piece_down)
        at_tick(k, GROUP + ring, piece_back_gate)
        at_tick(k, GROUP + ring + 2, piece_back_up)

    def root(c, slot, total):
        j = lax.rem(c, count)
        mine = block(j // 2, CHUNK)
        row_load(x_in, c).wait()

        @pl.when(c < count)
        def _():
            value = rows_ref[slot] + total
            own_ref[mine, :] = value
            out[slot] = (value * mean_square(value) * gain_ref[...]).astype(BF16).astype(F32)

        @pl.when(c >= count)
        def _():
            back = norm_grad(own_ref[mine, :], gain_ref[...], total, acc_ref)
            out[slot] = rows_ref[slot] + back

    def low_store(c, slot):
        at = block(lax.rem(c, count), CHUNK)
        return local(low.at[slot], low_out.at[at], low_sem.at[slot])

    def own_store(c, slot):
        at = block(lax.rem(c, count) // 2, CHUNK)
        return local(out.at[slot], own_grad_out.at[at], own_sem.at[slot])

    def arrive(c, slot):
        @pl.when(c < count)
        def _():
            normed[lax.rem(c // GROUP, 2), block(lax.rem(c, GROUP), CHUNK), :] = out[slot].astype(BF16)

        @pl.when(c >= count)
        def _():
            low[slot] = out[slot].astype(BF16)
            low_store(c, slot).start(priority=1)

            @pl.when(is_root(c))
            def _():
                own_store(c, slot).start(priority=1)

    def leave(c, slot):
        @pl.when(c >= count)
        def _():
            low_store(c, slot).wait()

            @pl.when(is_root(c))
            def _():
                own_store(c, slot).wait()

    line_sum("mp", 2 * count, count, part, inbox, out, sems, before, root, arrive, leave)

    own_copy.wait()
    for which in range(3):
        for copy in stage_stores(which, WEIGHT_STEPS - 1):
            copy.wait()


def middle_call(*args):
    mixed, w_out, x, og, gain, w_gate, w_up, w_down = args
    rows, model = x.shape
    width, hidden = mixed.shape[1], w_gate.shape[1]
    size = GROUP * CHUNK
    dma = pltpu.SemaphoreType.DMA
    ring = ring_size("mp")
    act = shape((rows, hidden), BF16)
    tall = shape((rows, model), BF16)
    return pl.pallas_call(
        middle_kernel,
        out_shape=(
            tall,
            act,
            act,
            act,
            tall,
            shape((rows, model)),
            tall,
            shape((rows // 2, model)),
            shape((3, model, hidden - hidden // LATER)),
            shape((3, model, width + hidden // LATER)),
            shape((rows // 2, model)),
            shape((TILE, model)),
        ),
        in_specs=[HBM] * 4 + [VMEM] + [HBM] * 3,
        out_specs=(HBM,) * 11 + (VMEM,),
        scratch_shapes=line_scratch("mp", rows, model, 4)
        + [
            pltpu.VMEM((rows, width), BF16),
            pltpu.VMEM((width, model), BF16),
            pltpu.VMEM((model, hidden), BF16),
            pltpu.VMEM((model, hidden), BF16),
            pltpu.VMEM((max(hidden, rows * 3 // 2), model), BF16),
            pltpu.VMEM((2, size, model), BF16),
            pltpu.VMEM((ring, CHUNK, model), F32),
            pltpu.VMEM((size, model), F32),
            pltpu.VMEM((size, model), BF16),
            pltpu.VMEM((size, hidden), F32),
            pltpu.VMEM((size, hidden), F32),
            pltpu.VMEM((size, hidden), F32),
            pltpu.VMEM((size, hidden), BF16),
            pltpu.VMEM((size, hidden), BF16),
            pltpu.VMEM((size, hidden), BF16),
            pltpu.VMEM((size, model), F32),
            pltpu.VMEM((ring, CHUNK, model), BF16),
            dma((5,)),
            dma((ring,)),
            dma((1,)),
            dma((6,)),
            dma((ring,)),
            dma((ring,)),
            dma((7,)),
            dma((3,)),
            dma((4,)),
            pltpu.VMEM((rows // 2, model), F32),
        ],
        compiler_params=params(2, 63),
        cost_estimate=cost(400),
        name="middle",
    )(*args)


def last_kernel(
    first_in,
    own_grad_in,
    x_in,
    grad_branch_in,
    input_in,
    w_branch_in,
    w_input_in,
    gain_ref,
    other_acc,
    sums_in,
    ends_in,
    blocks_in,
    grad_out,
    norm_ref,
    small_out,
    part,
    inbox,
    out,
    send_up,
    send_down,
    recv_up,
    recv_down,
    own_grad_ref,
    x_ref,
    grad_branch,
    input_low,
    w_branch,
    w_input,
    load_sem,
    store_sem,
    acc_ref,
    mine_ref,
    seq_in,
    mp_in,
    send_s,
    recv_s,
    send_m,
    recv_m,
    small,
    small_in,
    send_v,
    recv_v,
):
    count = part.shape[0] // CHUNK
    size = GROUP * CHUNK
    sems = (send_up, send_down, recv_up, recv_down)
    local = pltpu.make_async_copy

    loads = [
        local(source, target, load_sem.at[i])
        for i, (source, target) in enumerate(
            (
                (grad_branch_in, grad_branch),
                (w_branch_in, w_branch),
                (input_in, input_low),
                (w_input_in, w_input),
                (own_grad_in, own_grad_ref),
                (x_in, x_ref),
            )
        )
    ]
    first_load = local(first_in, part.at[slice(0, size)], load_sem.at[6])
    first_load.start()
    for copy in loads:
        copy.start(priority=1)
    acc_ref[...] = jnp.zeros_like(acc_ref)
    norm_ref[...] = jnp.zeros_like(norm_ref)
    enter_all(("seq", "mp"))
    first_load.wait()

    kinds = sums_in.shape[0]
    me = lax.axis_index("seq")
    width = sums_in.shape[2]
    height = kinds + ends_in.shape[0]
    head = blocks_in.shape[0]
    levels = small_in.shape[0]

    def exchange(level):
        bit = 1 << level
        partner = me + bit - 2 * bit * lax.rem(me // bit, 2)
        return pltpu.make_async_remote_copy(
            src_ref=small.at[level],
            dst_ref=small_in.at[level],
            send_sem=send_v.at[level],
            recv_sem=recv_v.at[level],
            device_id={"seq": partner},
            device_id_type=MESH,
        )

    spacing = (count - 4) // (levels + 1)
    plane = lax.axis_index("mp")

    def norm_sum(i, k, first, gaps, source):
        seq_copies = to_all("seq", mine_ref.at[i, 0], seq_in.at[i], send_s.at[i], recv_s.at[i])
        mp_copies = to_all("mp", mine_ref.at[i, 1], mp_in.at[i], send_m.at[i], recv_m.at[i])

        @pl.when(k == first)
        def _():
            mine_ref[i, 0] = jnp.sum(source[...], axis=0, keepdims=True)
            seq_in[i, me] = mine_ref[i, 0]
            for copy in seq_copies:
                copy.start()

        @pl.when(k == first + gaps[0])
        def _():
            for copy in seq_copies:
                copy.wait()
            mine_ref[i, 1] = jnp.sum(seq_in[i], axis=0)
            mp_in[i, plane] = mine_ref[i, 1]
            for copy in mp_copies:
                copy.start()

        @pl.when(k == first + gaps[0] + gaps[1])
        def _():
            for copy in mp_copies:
                copy.wait()
            norm_ref[i : i + 1, :] = jnp.sum(mp_in[i], axis=0)

    settled = count + SKEW * (lax.axis_size("mp") // 2)

    def before(k):
        @pl.when(k == 2)
        def _():
            for i in range(kinds):
                small[0, i : i + 1, :] = jnp.sum(sums_in[i], axis=0, keepdims=True)
            small[0, kinds:height, :] = ends_in[...]
            small[0, height : height + head, :] = blocks_in[:, :width]
            small[0, height + head :, :] = blocks_in[:, width:]

        for level in range(levels + 1):

            @pl.when(k == 3 + level * spacing)
            def _():
                if level > 0:
                    exchange(level - 1).wait()
                    total = small[level - 1] + small_in[level - 1]
                    if level < levels:
                        small[level] = total
                    else:
                        small_out[...] = total
                if level < levels:
                    exchange(level).start()

        norm_sum(0, k, settled, (2, 3), acc_ref)
        norm_sum(1, k, 10, (20, 20), other_acc)

        @pl.when(k == 4)
        def _():
            for copy in loads[:4]:
                copy.wait()

        @pl.when(
            jnp.logical_and(
                lax.rem(k, 4) == 0, jnp.logical_and(k > 0, k // 4 < count // GROUP)
            )
        )
        def _():
            at = block(k // 4, size)

            def work(cols):
                part[at, cols] = matmul_back(grad_branch[at, :], w_branch[cols, :]) + matmul_back(
                    input_low[at, :], w_input[cols, :]
                )

            work(slice(None))

        @pl.when(k == SKEW * (lax.axis_size("mp") // 2))
        def _():
            for copy in loads[4:]:
                copy.wait()

    def root(c, slot, total):
        back = norm_grad(x_ref[block(c, CHUNK), :], gain_ref[...], total, acc_ref)
        out[slot] = own_grad_ref[block(c // 2, CHUNK), :] + back

    def store(c, slot):
        return local(out.at[slot], grad_out.at[block(c, CHUNK)], store_sem.at[slot])

    def arrive(c, slot):
        store(c, slot).start(priority=1)

    def leave(c, slot):
        store(c, slot).wait()

    line_sum("mp", count, count, part, inbox, out, sems, before, root, arrive, leave)


def enter_all(axes):
    barrier = pltpu.get_barrier_semaphore()
    count = 0
    for axis in axes:
        size, me = lax.axis_size(axis), lax.axis_index(axis)
        for d in range(1, size):
            pl.semaphore_signal(
                barrier, 1, device_id={axis: lax.rem(me + d, size)}, device_id_type=MESH
            )
        count += size - 1
    pl.semaphore_wait(barrier, count)


def cost(micros):
    return pl.CostEstimate(flops=int(micros * 1e9), bytes_accessed=1 << 20, transcendentals=0)


def nseq_levels():
    return (lax.axis_size("seq") - 1).bit_length()


def last_call(*args):
    x, grad_branch = args[2:4]
    rows, model = x.shape
    width = grad_branch.shape[1]
    lines = args[9].shape[0] + args[10].shape[0] + 2 * args[11].shape[0]
    levels = nseq_levels()
    dma = pltpu.SemaphoreType.DMA
    nseq, nmp = lax.axis_size("seq"), lax.axis_size("mp")
    return pl.pallas_call(
        last_kernel,
        out_shape=(shape((rows, model)), shape((TILE, model)), shape((lines, width))),
        in_specs=[HBM] * 7 + [VMEM] * 5,
        out_specs=(HBM,) + (VMEM,) * 2,
        scratch_shapes=line_scratch("mp", rows, model)
        + [
            pltpu.VMEM((rows // 2, model), F32),
            pltpu.VMEM((rows, model), F32),
            pltpu.VMEM((rows, width), BF16),
            pltpu.VMEM((rows, width), BF16),
            pltpu.VMEM((model, width), BF16),
            pltpu.VMEM((model, width), BF16),
            dma((7,)),
            dma((ring_size("mp"),)),
            pltpu.VMEM((TILE, model), F32),
            pltpu.VMEM((2, 2, 1, model), F32),
            pltpu.VMEM((2, nseq, 1, model), F32),
            pltpu.VMEM((2, nmp, 1, model), F32),
            dma((2, nseq - 1)),
            dma((2, nseq - 1)),
            dma((2, nmp - 1)),
            dma((2, nmp - 1)),
            pltpu.VMEM((levels, lines, width), F32),
            pltpu.VMEM((levels, lines, width), F32),
            dma((levels,)),
            dma((levels,)),
        ],
        compiler_params=params(4, 62),
        cost_estimate=cost(200),
        name="last_sums",
    )(*args)


def finish_kernel(
    heads,
    block_in,
    grad_in,
    mlp_in,
    rec_in,
    small_hbm,
    norm_hbm,
    decay_hbm,
    block_out,
    grad_out,
    w_gate_out,
    w_up_out,
    w_branch_out,
    w_input_out,
    w_down_out,
    w_out_out,
    gate_r_out,
    gate_i_out,
    taps_out,
    conv_bias_out,
    bias_r_out,
    bias_i_out,
    decay_out,
    norm_in_out,
    norm_mlp_out,
    state_out,
    conv_out,
    tall,
    mlp,
    rec,
    small_in,
    norm_in,
    raw_ref,
    load_sem,
    store_sem,
    extra_sem,
):
    local = pltpu.make_async_copy
    width = small_in.shape[1]
    kept = mlp.shape[2]
    late = rec.shape[2] - width
    size = grad_in.shape[0] // COPIES
    extra = [
        local(source, target, extra_sem.at[i])
        for i, (source, target) in enumerate(
            ((small_hbm, small_in), (norm_hbm, norm_in), (decay_hbm, raw_ref))
        )
    ]
    for copy in extra:
        copy.start()
    jobs = [(mlp_in, mlp, None), (rec_in, rec, None)]
    for j, (source, target) in enumerate(((block_in, block_out), (grad_in, grad_out))):
        for i in range(COPIES):
            at = slice(i * size, (i + 1) * size)
            jobs.append((source.at[at], tall.at[j, at], target.at[at]))
    loads = [local(source, held, load_sem.at[i]) for i, (source, held, _) in enumerate(jobs)]
    stores = [
        local(held, target, store_sem.at[i])
        for i, (held, target) in enumerate(
            [(held, target) for _, held, target in jobs[2:]]
            + [
                (mlp.at[0], w_gate_out.at[:, pl.ds(0, kept)]),
                (mlp.at[1], w_up_out.at[:, pl.ds(0, kept)]),
                (rec.at[0, :, pl.ds(width, late)], w_gate_out.at[:, pl.ds(kept, late)]),
                (rec.at[1, :, pl.ds(width, late)], w_up_out.at[:, pl.ds(kept, late)]),
                (rec.at[1, :, pl.ds(0, width)], w_branch_out),
                (rec.at[2, :, pl.ds(0, width)], w_input_out),
            ]
        )
    ]
    for copy in loads:
        copy.start()
    for copy in extra:
        copy.wait()
    taps, seqs, edge = taps_out.shape[0], state_out.shape[0], conv_out.shape[0]
    head = gate_r_out.shape[1]
    decay = small_in[0:1, :].reshape(width) * (RATE_SCALE * jax.nn.sigmoid(-raw_ref[...]))
    decay_out[...] = decay
    bias_r_out[...] = small_in[1:2, :].reshape(width)
    bias_i_out[...] = small_in[2:3, :].reshape(width)
    conv_bias_out[...] = small_in[3:4, :].reshape(width)
    taps_out[...] = small_in[4 : 4 + taps, :]
    begin = 4 + taps
    state_out[...] = small_in[begin : begin + seqs, :]
    for s in range(seqs):
        end = begin + seqs + (s + 1) * TILE
        for k in range(edge):
            conv_out[k, s : s + 1, :] = small_in[end - edge + k : end - edge + k + 1, :]
    begin += seqs + seqs * TILE
    for i, target in enumerate((gate_r_out, gate_i_out)):
        line = small_in[begin + i * head : begin + (i + 1) * head, :]
        for h in range(heads):
            turned = line if h == 0 else pltpu.roll(line, width - h * head, 1)
            target[h] = turned[:, :head]
    norm_in_out[...] = norm_in[0:1, :].reshape(norm_in.shape[1])
    norm_mlp_out[...] = norm_in[1:2, :].reshape(norm_in.shape[1])
    loads[0].wait()
    loads[1].wait()
    for copy in stores[2 * COPIES :]:
        copy.start()
    w_down_out[:kept, :] = mlp[2].T
    w_down_out[kept:, :] = rec[2, :, width:].T
    w_out_out[...] = rec[0, :, :width].T
    for i in range(2 * COPIES):
        loads[2 + i].wait()
        stores[i].start()
    for copy in stores:
        copy.wait()


def finish_call(seqs, heads, head, edge, *args):
    _, stream_grad, mlp_grads, rec_grads, small, norms, decay = args
    rows, model = stream_grad.shape
    own, kept = mlp_grads.shape[1:]
    width = small.shape[1]
    hidden = kept + rec_grads.shape[2] - width
    taps = edge + 1
    line = shape((width,))
    tall = shape((rows, model))
    return pl.pallas_call(
        functools.partial(finish_kernel, heads),
        out_shape=(
            tall,
            tall,
            shape((own, hidden)),
            shape((own, hidden)),
            shape((own, width)),
            shape((own, width)),
            shape((hidden, own)),
            shape((width, own)),
            shape((heads, head, head)),
            shape((heads, head, head)),
            shape((taps, width)),
            line,
            line,
            line,
            line,
            shape((model,)),
            shape((model,)),
            shape((seqs, width)),
            shape((edge, seqs, width)),
        ),
        in_specs=[HBM] * 4 + [PINNED] * 3,
        out_specs=(HBM,) * 6 + (VMEM,) * 13,
        scratch_shapes=[
            pltpu.VMEM((2, rows, model), F32),
            pltpu.VMEM(mlp_grads.shape, F32),
            pltpu.VMEM(rec_grads.shape, F32),
            pltpu.VMEM(small.shape, F32),
            pltpu.VMEM(norms.shape, F32),
            pltpu.VMEM(decay.shape, F32),
            pltpu.SemaphoreType.DMA((2 + 2 * COPIES,)),
            pltpu.SemaphoreType.DMA((6 + 2 * COPIES,)),
            pltpu.SemaphoreType.DMA((3,)),
        ],
        compiler_params=pltpu.CompilerParams(vmem_limit_bytes=63 << 20),
        cost_estimate=cost(15),
        name="finish",
    )(*args)


def params(collective, megabytes=60):
    return pltpu.CompilerParams(
        collective_id=collective, has_side_effects=True, vmem_limit_bytes=megabytes << 20
    )


def shape(dims, dtype=F32):
    return jax.ShapeDtypeStruct(dims, dtype)


def recurrence_forward(span, *args):
    x, w_input = args[:2]
    rows, model = x.shape
    seqs, width = rows // span, w_input.shape[1]
    devices = lax.axis_size("seq")
    dma = pltpu.SemaphoreType.DMA
    groups = seqs // 2
    columns = (width // LANES, rows, LANES)
    spaced = (width // LANES, seqs * (span + TILE), LANES)
    padded = (seqs, span + TILE, width)
    return pl.pallas_call(
        functools.partial(forward_kernel, span),
        out_shape=(
            shape((rows, model), BF16),
            shape((rows, width)),
            shape(padded),
            shape((rows, 2 * width)),
            shape(columns),
            shape((rows, width), BF16),
            shape((seqs, width)),
            shape((devices, 2, seqs, width)),
            shape((width, 2 * width), BF16),
            shape((TILE, width)),
            shape(((seqs + 1) * TILE, width)),
        ),
        in_specs=[HBM] * 3 + [VMEM] * 8 + [pl.BlockSpec(memory_space=pltpu.SMEM)] + [VMEM] * 2,
        out_specs=(HBM,) * 5 + (VMEM,) * 6,
        scratch_shapes=[
            pltpu.VMEM((rows, model), F32),
            pltpu.VMEM((model, width), BF16),
            pltpu.VMEM((model, width), BF16),
            pltpu.VMEM((rows, model), BF16),
            pltpu.VMEM((rows, width), F32),
            pltpu.VMEM(padded, F32),
            pltpu.VMEM((rows, 2 * width), F32),
            pltpu.VMEM(columns, F32),
            pltpu.VMEM((rows, width), F32),
            pltpu.VMEM(spaced, F32),
            pltpu.VMEM(spaced, F32),
            pltpu.VMEM((2, span, width), F32),
            pltpu.VMEM((seqs, TILE, width), F32),
            pltpu.VMEM((seqs, TILE, width), F32),
            pltpu.VMEM((2, seqs, width), F32),
            dma((groups + 2,)),
            dma((4,)),
            dma((groups,)),
            dma((devices - 1,)),
            dma((devices - 1,)),
            dma((1,)),
            dma((1,)),
        ],
        compiler_params=params(0),
        cost_estimate=cost(50),
        name="recurrence_forward",
    )(*args)


def widen(array, width):
    short = width - array.shape[-1]
    if short == 0:
        return array
    return jnp.pad(array, [(0, 0)] * (array.ndim - 1) + [(0, short)])


def per_device(
    stream,
    norm_in,
    w_branch,
    w_input,
    conv_kernel,
    conv_bias,
    gate_r,
    bias_r,
    gate_i,
    bias_i,
    decay_param,
    w_out,
    norm_mlp,
    w_gate,
    w_up,
    w_down,
    state_init,
    conv_init,
    fresh_rows,
    out_grad,
):
    seqs, span, model = stream.shape
    channels = w_branch.shape[1]
    mlp_dev = w_gate.shape[1]
    heads, head_width = gate_r.shape[:2]
    taps = conv_kernel.shape[0]
    edge = taps - 1
    rows = seqs * span
    devices = lax.axis_size("seq")
    position = lax.axis_index("seq")
    width = -(-channels // 128) * 128

    flat_in = stream.reshape(rows, model)
    flat_grad = out_grad.reshape(rows, model)
    w_branch_p = widen(w_branch, width)
    w_input_p = widen(w_input, width)
    w_out_p = jnp.pad(w_out, ((0, width - channels), (0, 0))) if width > channels else w_out
    taps_p = widen(conv_kernel, width)
    def line(value):
        return widen(value, width)

    (
        normed,
        branch,
        padded,
        pre,
        hidden,
        mixed,
        carry,
        sums,
        gates,
        rates,
        ends,
    ) = recurrence_forward(
        span,
        flat_in,
        w_input_p,
        w_branch_p,
        norm_in[None],
        taps_p,
        line(conv_bias),
        line(decay_param),
        line(bias_r),
        line(bias_i),
        gate_r,
        gate_i,
        fresh_rows,
        widen(state_init, width),
        widen(jnp.swapaxes(conv_init, 0, 1), width),
    )
    made = middle_call(mixed, w_out_p, flat_in, flat_grad, norm_mlp[None], w_gate, w_up, w_down)
    block_part, resid_low, own_grad, mlp_grads, rest, own, norm_mlp_acc = made[5:]
    mlp_grads = lax.psum_scatter(mlp_grads, "seq", scatter_dimension=1, tiled=True)
    block_out, rec_grads, grad_branch, input_low, first_rows, acc, blocks = backward_call(
        span,
        heads,
        head_width,
        block_part,
        own,
        resid_low,
        w_out_p,
        branch,
        hidden,
        pre,
        padded,
        normed,
        mixed,
        rest,
        gates,
        w_branch_p,
        w_input_p,
        carry,
        sums,
        taps_p,
        rates,
    )

    rec_grads, grad_branch, mlp_grads = lax.optimization_barrier(
        (rec_grads, grad_branch, mlp_grads)
    )
    rec_grads = lax.psum_scatter(rec_grads, "seq", scatter_dimension=1, tiled=True)

    stream_grad, norm_grads, small = last_call(
        first_rows,
        own_grad,
        flat_in,
        grad_branch,
        input_low,
        w_branch_p,
        w_input_p,
        norm_in[None],
        norm_mlp_acc,
        acc,
        ends,
        blocks,
    )
    (
        block_out,
        stream_grad,
        w_gate_grad,
        w_up_grad,
        w_branch_grad,
        w_input_grad,
        w_down_grad,
        w_out_grad,
        gate_r_grad,
        gate_i_grad,
        taps_grad,
        conv_bias_grad,
        bias_r_grad,
        bias_i_grad,
        decay_grad,
        norm_in_grad,
        norm_mlp_grad,
        final_state,
        final_conv,
    ) = finish_call(
        seqs,
        heads,
        head_width,
        edge,
        block_out,
        stream_grad,
        mlp_grads,
        rec_grads,
        small,
        norm_grads,
        line(decay_param),
    )
    return (
        block_out.reshape(stream.shape),
        stream_grad.reshape(stream.shape),
        norm_in_grad,
        w_branch_grad[:, :channels],
        w_input_grad[:, :channels],
        taps_grad[:, :channels],
        conv_bias_grad[:channels],
        gate_r_grad,
        bias_r_grad[:channels],
        gate_i_grad,
        bias_i_grad[:channels],
        decay_grad[:channels],
        w_out_grad[:channels],
        norm_mlp_grad,
        w_gate_grad,
        w_up_grad,
        w_down_grad,
        final_state[:, :channels],
        jnp.swapaxes(final_conv, 0, 1)[:, :, :channels],
    )


def solution(mesh):
    seq_rows = P(None, "seq", None)
    columns = P(None, "mp")
    channel = P("mp")
    return jax.shard_map(
        per_device,
        mesh=mesh,
        in_specs=(
            seq_rows,
            P(),
            columns,
            columns,
            columns,
            channel,
            P("mp", None, None),
            channel,
            P("mp", None, None),
            channel,
            channel,
            P("mp", None),
            P(),
            columns,
            columns,
            P("mp", None),
            columns,
            P(None, None, "mp"),
            P(),
            seq_rows,
        ),
        out_specs=(
            seq_rows,
            seq_rows,
            P(),
            P("seq", "mp"),
            P("seq", "mp"),
            columns,
            channel,
            P("mp", None, None),
            channel,
            P("mp", None, None),
            channel,
            channel,
            P("mp", "seq"),
            P(),
            P("seq", "mp"),
            P("seq", "mp"),
            P("mp", "seq"),
            columns,
            P(None, None, "mp"),
        ),
        check_vma=False,
    )
```

```python
import functools

import jax
import jax.numpy as jnp
from jax import lax
from jax.experimental import pallas as pl
from jax.experimental.pallas import tpu as pltpu
from jax.sharding import PartitionSpec as P

MESH = pl.DeviceIdType.MESH
RATE_SCALE = 8.0
EPS = 1e-06
GELU_C = 0.7978845608028654
GELU_K = 0.044715
CONTRACT_ROWS = (((0,), (0,)), ((), ()))
CONTRACT_LAST = (((1,), (1,)), ((), ()))
TILE = 8
LANES = 128
ROWS = 32
CHUNK = 16
SKEW = 2
GROUP = 16
WEIGHT_STEPS = 8
COPIES = 8
LATER = 6
F32 = jnp.float32
BF16 = jnp.bfloat16
VMEM = pl.BlockSpec(memory_space=pltpu.VMEM)
HBM = pl.BlockSpec(memory_space=pl.ANY)
PINNED = pl.BlockSpec(memory_space=pltpu.HBM)


def dot(a, b):
    return jnp.dot(a, b, preferred_element_type=F32)


def matmul_back(a, b):
    return lax.dot_general(a, b, CONTRACT_LAST, preferred_element_type=F32)


def block(i, size):
    return pl.ds(pl.multiple_of(i * size, size), size)


def gelu(x):
    t = jnp.tanh(GELU_C * (x + GELU_K * (x * x * x)))
    return 0.5 * x * (1.0 + t)


def gelu_both(x):
    x2 = x * x
    t = jnp.tanh(GELU_C * (x + GELU_K * (x2 * x)))
    half = 0.5 * (1.0 + t)
    slope = half + 0.5 * x * (1.0 - t * t) * (GELU_C * (1.0 + (3.0 * GELU_K) * x2))
    return x * half, slope


def one_minus_square(log_a, a):
    y = 2.0 * log_a
    s = 1.0 + y * (1.0 / 8.0)
    for k in (7, 6, 5, 4, 3, 2):
        s = 1.0 + (y * (1.0 / k)) * s
    return jnp.where(y > -0.35, -y * s, 1.0 - a * a)


def get(ref, at):
    return jnp.concatenate([ref[j, at, :] for j in range(ref.shape[0])], axis=-1)


def put(ref, at, value):
    for j in range(ref.shape[0]):
        ref[j, at, :] = value[:, j * LANES : (j + 1) * LANES]


def to_all(axis, src, slots, send, recv):
    size, me = lax.axis_size(axis), lax.axis_index(axis)
    return [
        pltpu.make_async_remote_copy(
            src_ref=src,
            dst_ref=slots.at[me],
            send_sem=send.at[d - 1],
            recv_sem=recv.at[d - 1],
            device_id={axis: lax.rem(me + d, size)},
            device_id_type=MESH,
        )
        for d in range(1, size)
    ]


def to_one(axis, distance, src, dst, send, recv):
    size, me = lax.axis_size(axis), lax.axis_index(axis)
    return pltpu.make_async_remote_copy(
        src_ref=src,
        dst_ref=dst,
        send_sem=send,
        recv_sem=recv,
        device_id={axis: lax.rem(me + distance + size, size)},
        device_id_type=MESH,
    )


def spread_gates(blocks_ref, out_ref, start, width):
    heads, size = blocks_ref.shape[:2]
    for h in range(heads):
        block_h = blocks_ref[h].astype(F32)
        parts = [block_h]
        if h > 0:
            parts.insert(0, jnp.zeros((size, h * size), F32))
        if width > (h + 1) * size:
            parts.append(jnp.zeros((size, width - (h + 1) * size), F32))
        row = jnp.concatenate(parts, axis=1).astype(BF16)
        out_ref[h * size : (h + 1) * size, start : start + width] = row
    if width > heads * size:
        rest = jnp.zeros((width - heads * size, width), BF16)
        out_ref[heads * size : width, start : start + width] = rest


def forward_kernel(
    span,
    x_in,
    w_input_in,
    w_branch_in,
    gain_ref,
    taps_ref,
    conv_bias_ref,
    decay_ref,
    bias_r_ref,
    bias_i_ref,
    gate_r_ref,
    gate_i_ref,
    fresh_ref,
    state_ref,
    conv_init_ref,
    normed_out,
    branch_out,
    pad_out,
    pre_out,
    hidden_out,
    mixed_ref,
    carry_ref,
    sums_ref,
    gates_ref,
    vec_ref,
    ends_ref,
    x_ref,
    w_input_ref,
    w_branch_ref,
    normed_ref,
    branch_ref,
    pad_ref,
    pre_ref,
    hidden_ref,
    act_ref,
    a_ref,
    b_ref,
    conv_ref,
    tail_ref,
    tail_in,
    mine_ref,
    load_sem,
    store_sem,
    normed_sem,
    send1,
    recv1,
    send_t,
    recv_t,
):
    seqs = state_ref.shape[0]
    width = taps_ref.shape[1]
    taps = taps_ref.shape[0]
    rows = seqs * span
    devices, me = lax.axis_size("seq"), lax.axis_index("seq")
    local = pltpu.make_async_copy
    pitch = a_ref.shape[1] // seqs
    group = 2 * span
    groups = rows // group

    def x_load(g):
        at = block(g, group)
        return local(x_in.at[at], x_ref.at[at], load_sem.at[g])

    weight_loads = [
        local(w_input_in, w_input_ref, load_sem.at[groups]),
        local(w_branch_in, w_branch_ref, load_sem.at[groups + 1]),
    ]
    x_load(0).start()
    weight_loads[0].start()
    for g in range(1, groups):
        x_load(g).start()
    weight_loads[1].start()

    enter_all(("seq",))
    spread_gates(gate_r_ref, gates_ref, 0, width)
    spread_gates(gate_i_ref, gates_ref, width, width)
    vec_ref[0:1, :] = conv_bias_ref[...].reshape(1, width)
    vec_ref[1:2, :] = jax.nn.softplus(-decay_ref[...].reshape(1, width))
    bias_r = bias_r_ref[...].reshape(1, width)
    bias_i = bias_i_ref[...].reshape(1, width)
    keep = [1.0 - fresh_ref[s].astype(F32) for s in range(seqs)]

    def normed_store(g):
        at = block(g, group)
        return local(normed_ref.at[at], normed_out.at[at], normed_sem.at[g])

    def norm(g):
        x_load(g).wait()
        for q in range(group // CHUNK):
            at = slice(g * group + q * CHUNK, g * group + (q + 1) * CHUNK)
            x = x_ref[at, :]
            normed_ref[at, :] = (x * mean_square(x) * gain_ref[...]).astype(BF16)

    norm(0)
    weight_loads[0].wait()
    for g in range(groups):
        if g + 1 < groups:
            norm(g + 1)
        conv = dot(normed_ref[slice(g * group, (g + 1) * group), :], w_input_ref[...])
        for j in range(group // span):
            pad_ref[g * (group // span) + j, pl.ds(TILE, span), :] = conv[
                j * span : (j + 1) * span
            ]
    for g in range(groups):
        normed_store(g).start()

    for s in range(seqs):
        tail_ref[s] = pad_ref[s, pl.ds(span, TILE), :]
    tail_copy = to_one("seq", 1, tail_ref, tail_in, send_t.at[0], recv_t.at[0])
    tail_copy.start()
    weight_loads[1].wait()

    def branch(g):
        branch_ref[block(g, group), :] = dot(normed_ref[block(g, group), :], w_branch_ref[...])

    @pl.loop(0, groups // 2)
    def _(g):
        branch(g)

    stores = [
        local(source, target, store_sem.at[i])
        for i, (source, target) in enumerate(
            (
                (branch_ref, branch_out),
                (pad_ref, pad_out),
                (pre_ref, pre_out),
                (hidden_ref, hidden_out),
            )
        )
    ]
    tail_copy.wait()
    lead = jnp.zeros((TILE - taps + 1, width), F32)
    for s in range(seqs):
        initial = jnp.concatenate(
            [lead] + [conv_init_ref[k, s : s + 1, :] * keep[s] for k in range(taps - 1)], axis=0
        )
        pad_ref[s, pl.ds(0, TILE), :] = jnp.where(me == 0, initial, tail_in[s])
    stores[1].start()

    def gates(s, slot):
        for q in range(span // ROWS):
            part = pad_ref[s, pl.ds(q * ROWS, ROWS + TILE), :]
            total = vec_ref[0:1, :]
            for k in range(taps):
                first = TILE - (taps - 1) + k
                total = total + taps_ref[k : k + 1, :] * part[first : first + ROWS]
            conv_ref[slot, pl.ds(q * ROWS, ROWS), :] = total

        pre = dot(conv_ref[slot].astype(BF16), gates_ref[...])
        pre_ref[block(s, span), :width] = pre[:, :width] + bias_r
        pre_ref[block(s, span), width:] = pre[:, width:] + bias_i
        for q in range(span // ROWS):
            rows_q = slice(q * ROWS, (q + 1) * ROWS)
            conv = conv_ref[slot, pl.ds(q * ROWS, ROWS), :]
            recall = jax.nn.sigmoid(pre[rows_q, :width] + bias_r)
            gate = jax.nn.sigmoid(pre[rows_q, width:] + bias_i)
            log_a = (-RATE_SCALE * vec_ref[1:2, :]) * recall
            a = jnp.exp(log_a)
            spaced = pl.ds(pl.multiple_of(s * pitch + q * ROWS, TILE), ROWS)
            put(a_ref, spaced, a)
            put(b_ref, spaced, jnp.sqrt(one_minus_square(log_a, a)) * gate * conv)

    per = seqs // (groups - groups // 2)

    @pl.loop(0, groups - groups // 2)
    def _(i):
        branch(groups // 2 + i)
        for j in range(per):
            gates(i * per + j, j % 2)

    stores[0].start()
    stores[2].start()

    def at_time(ref, t):
        return get(ref, pl.ds(t, seqs, stride=pitch))

    def step(t, value):
        prod, state = value
        a = at_time(a_ref, t)
        return prod * a, a * state + at_time(b_ref, t)

    ones = jnp.ones((seqs, width), F32)
    prod, state = lax.fori_loop(0, span, step, (ones, jnp.zeros_like(ones)), unroll=8)
    mine_ref[0] = prod
    mine_ref[1] = state
    sums_ref[me] = mine_ref[...]
    copies = to_all("seq", mine_ref, sums_ref, send1, recv1)
    for copy in copies:
        copy.start()

    @pl.loop(0, rows // ROWS, unroll=2)
    def _(q):
        at = block(q, ROWS)
        act_ref[at, :] = gelu(branch_ref[at, :])

    for copy in copies:
        copy.wait()

    def carry_step(j, carry):
        both = sums_ref[j]
        return jnp.where(j < me, both[0] * carry + both[1], carry)

    start = jnp.concatenate([state_ref[s : s + 1, :] * keep[s] for s in range(seqs)], axis=0)
    carry = lax.fori_loop(0, devices - 1, carry_step, start)
    carry_ref[...] = carry

    def final(t, state):
        state = at_time(a_ref, t) * state + at_time(b_ref, t)
        put(hidden_ref, pl.ds(t, seqs, stride=span), state)
        return state

    last = lax.fori_loop(0, span, final, carry, unroll=8)
    stores[3].start()
    ends_ref[0:seqs, :] = jnp.where(me == devices - 1, last, 0.0)
    for s in range(seqs):
        ends_ref[(s + 1) * TILE : (s + 2) * TILE, :] = jnp.where(
            me == devices - 1, pad_ref[s, pl.ds(span, TILE), :], 0.0
        )

    @pl.loop(0, rows // ROWS, unroll=2)
    def _(q):
        at = block(q, ROWS)
        mixed_ref[at, :] = (get(hidden_ref, at) * act_ref[at, :]).astype(BF16)

    for copy in stores:
        copy.wait()
    for g in range(groups):
        normed_store(g).wait()


def backward_kernel(
    span,
    heads,
    block_part_in,
    own_in,
    low_in,
    w_out_in,
    branch_in,
    hidden_in,
    pre_in,
    pad_in,
    normed_in,
    mixed_in,
    rest_in,
    gates_in,
    w_branch_in,
    w_input_in,
    carry_ref,
    sums_ref,
    taps_ref,
    vec_ref,
    block_out,
    rec_out,
    grad_branch_out,
    input_out,
    first_out,
    acc_ref,
    blocks_ref,
    part,
    inbox,
    out,
    send_up,
    send_down,
    recv_up,
    recv_down,
    own_ref,
    resid_low,
    w_out_ref,
    branch_ref,
    hidden_ref,
    pre_ref,
    pad_ref,
    normed_ref,
    mixed_ref,
    a_ref,
    gd_ref,
    grad_ref,
    direct_ref,
    gpad_ref,
    heads_ref,
    low_ref,
    gates_grad,
    stage_ref,
    mine_ref,
    entries_ref,
    head_ref,
    head_in,
    load_sem,
    part_sem,
    store_sem,
    stage_sem,
    send1,
    recv1,
    send_t,
    recv_t,
    gates_ref,
    grad_branch_ref,
    input_ref,
    give_sem,
    late_sem,
):
    seqs, width = carry_ref.shape
    taps = taps_ref.shape[0]
    rows = seqs * span
    devices, me = lax.axis_size("seq"), lax.axis_index("seq")
    n, z = lax.axis_size("mp"), lax.axis_index("mp")
    chunks = rows // CHUNK
    size = GROUP * CHUNK
    held = part.shape[0] // size
    groups = chunks // GROUP
    sems = (send_up, send_down, recv_up, recv_down)
    local = pltpu.make_async_copy

    def part_load(g):
        slot = lax.rem(g, held)
        return local(block_part_in.at[block(g, size)], part.at[block(slot, size)], part_sem.at[slot])

    loads = [
        local(source, target, load_sem.at[i])
        for i, (source, target) in enumerate(
            (
                (own_in, own_ref),
                (low_in, resid_low),
                (w_out_in, w_out_ref),
                (pre_in, pre_ref),
                (branch_in, branch_ref),
                (hidden_in, hidden_ref),
                (pad_in, pad_ref),
                (mixed_in, mixed_ref),
                (normed_in, normed_ref),
                (gates_in, gates_ref),
            )
        )
    ]
    part_load(0).start()
    for copy in loads[:6]:
        copy.start(priority=1)
    for g in range(1, held):
        part_load(g).start()
    for copy in loads[6:]:
        copy.start(priority=1)
    acc_ref[...] = jnp.zeros_like(acc_ref)
    enter_all(("seq", "mp"))

    pitch = a_ref.shape[1] // seqs

    def spaced(s, q):
        return pl.ds(pl.multiple_of(s * pitch + q * ROWS, TILE), ROWS)

    def decay(at):
        recall = jax.nn.sigmoid(pre_ref[at, :width])
        log_a = (-RATE_SCALE * vec_ref[1:2, :]) * recall
        return recall, log_a, jnp.exp(log_a)

    def piece_direct(s):
        @pl.when(s == 0)
        def _():
            for copy in loads[1:6]:
                copy.wait()

        grad_ref[...] = matmul_back(resid_low[block(s, span), :], w_out_ref[...])

        @pl.loop(0, span // ROWS)
        def _(q):
            at = block(s * (span // ROWS) + q, ROWS)
            put(a_ref, spaced(s, q), decay(at)[2])
            act, slope = gelu_both(branch_ref[at, :])
            grad = grad_ref[block(q, ROWS), :]
            put(gd_ref, spaced(s, q), grad * act)
            grad_branch_ref[at, :] = (grad * get(hidden_ref, at) * slope).astype(BF16)

    def at_time(ref, t):
        return get(ref, pl.ds(t, seqs, stride=pitch))

    zero = jnp.zeros((seqs, width), F32)
    entry_copies = to_all("seq", mine_ref, entries_ref, send1, recv1)

    def piece_entry(_):
        def step(k, through):
            t = span - 1 - k
            return at_time(a_ref, t) * (at_time(gd_ref, t) + through)

        mine_ref[...] = lax.fori_loop(0, span, step, zero, unroll=8)
        entries_ref[me] = mine_ref[...]
        for copy in entry_copies:
            copy.start()

    def piece_state(_):
        for copy in entry_copies:
            copy.wait()

        def back_step(k, through):
            j = devices - 1 - k
            return jnp.where(j > me, entries_ref[j] + sums_ref[j, 0] * through, through)

        incoming = lax.fori_loop(0, devices - 1, back_step, zero)

        def final(k, through):
            t = span - 1 - k
            grad = at_time(gd_ref, t) + through
            put(gd_ref, pl.ds(t, seqs, stride=pitch), grad)
            return at_time(a_ref, t) * grad

        lax.fori_loop(0, span, final, incoming, unroll=8)

    def add(k, value):
        acc_ref[k] += fold(value)

    parts = 2

    def piece_gates(i):
        s = i // parts
        quarters = span // ROWS // parts

        @pl.when(i == 0)
        def _():
            loads[6].wait()
            loads[9].wait()

        @pl.loop(lax.rem(i, parts) * quarters, (lax.rem(i, parts) + 1) * quarters)
        def _(q):
            at = block(s * (span // ROWS) + q, ROWS)
            part_rows = pad_ref[s, pl.ds(pl.multiple_of(q * ROWS, ROWS), ROWS + TILE), :]
            conv = vec_ref[0:1, :]
            for k in range(taps):
                first = TILE - (taps - 1) + k
                conv = conv + taps_ref[k : k + 1, :] * part_rows[first : first + ROWS]
            heads_ref[at, :] = conv.astype(BF16)
            recall, log_a, a = decay(at)
            gate = jax.nn.sigmoid(pre_ref[at, width:])
            square = one_minus_square(log_a, a)
            inverse = lax.rsqrt(square)
            root = jnp.sqrt(square)
            grad = get(gd_ref, spaced(s, q))
            hidden = get(hidden_ref, at)
            before_at = pl.multiple_of(jnp.maximum(s * span + q * ROWS - TILE, 0), TILE)
            earlier = get(hidden_ref, pl.ds(before_at, TILE))
            first_row = jnp.where(q == 0, carry_ref[pl.ds(s, 1), :], earlier[TILE - 1 :])
            place = lax.broadcasted_iota(jnp.int32, (ROWS, width), 0)
            prev = jnp.where(place == 0, first_row, pltpu.roll(hidden, 1, 0))
            grad_log = grad * a * (prev - gate * conv * a * inverse)
            through = grad_log * recall
            pre_r = through * (1.0 - recall) * (-RATE_SCALE * vec_ref[1:2, :])
            direct = grad * root * gate
            pre_i = direct * conv * (1.0 - gate)
            low_ref[at, :width] = pre_r.astype(BF16)
            low_ref[at, width:] = pre_i.astype(BF16)
            direct_ref[block(q, ROWS), :] = direct
            add(0, through)
            add(1, pre_r)
            add(2, pre_i)

        @pl.when(lax.rem(i, parts) == parts - 1)
        def _():
            whole = direct_ref[...] + matmul_back(low_ref[block(s, span), :], gates_ref[...])
            gpad_ref[s, pl.ds(0, span), :] = whole
            head_ref[s] = whole[:TILE]

    head_copy = to_one("seq", -1, head_ref, head_in, send_t.at[0], recv_t.at[0])

    def piece_head(_):
        head_copy.start()

    def piece_taps(i):
        for j in range(2):
            taps_of(2 * i + j)

    def taps_of(s):
        @pl.loop(0, span // ROWS)
        def _(q):
            at = pl.multiple_of(q * ROWS, ROWS)
            part_rows = pad_ref[s, pl.ds(at, ROWS + TILE), :]
            grad = gpad_ref[s, pl.ds(at, ROWS), :]
            add(3, grad)
            for k in range(taps):
                first = TILE - (taps - 1) + k
                add(4 + k, grad * part_rows[first : first + ROWS])

    def piece_tail(_):
        head_copy.wait()
        for s in range(seqs):
            gpad_ref[s, pl.ds(span, TILE), :] = jnp.where(me == devices - 1, 0.0, head_in[s])

    def piece_input(i):
        for j in range(2):
            input_of(2 * i + j)

    def input_of(s):
        @pl.loop(0, span // ROWS)
        def _(q):
            part_rows = gpad_ref[s, pl.ds(pl.multiple_of(q * ROWS, ROWS), ROWS + TILE), :]
            total = taps_ref[taps - 1 : taps, :] * part_rows[0:ROWS]
            for k in range(taps - 1):
                first = taps - 1 - k
                total = total + taps_ref[k : k + 1, :] * part_rows[first : first + ROWS]
            input_ref[block(s * (span // ROWS) + q, ROWS), :] = total.astype(BF16)

    def contract(left, right):
        return lax.dot_general(left, right, CONTRACT_ROWS, preferred_element_type=F32)

    head = blocks_ref.shape[0]

    late_loads = [
        local(source.at[slice(i * rows, (i + 1) * rows)], target, late_sem.at[2 * j + i])
        for j, (source, targets) in enumerate(
            (
                (
                    w_branch_in,
                    (
                        resid_low.at[:, pl.ds(0, width)],
                        resid_low.at[:, pl.ds(width, width)],
                    ),
                ),
                (w_input_in, (resid_low.at[:, pl.ds(2 * width, width)], mixed_ref)),
            )
        )
        for i, target in enumerate(targets)
    ]
    first_copy = local(part.at[slice(size, 2 * size)], first_out, late_sem.at[4])

    def piece_projections(_):
        for copy in late_loads:
            copy.start(priority=1)

    def piece_first(i):
        branch_rows = grad_branch_ref[:size, :]
        input_rows = input_ref[:size, :]

        @pl.when(i == 0)
        def _():
            for copy in late_loads:
                copy.wait()

            part[size : 2 * size, :rows] = matmul_back(
                branch_rows, resid_low[:, :width]
            ) + matmul_back(input_rows, resid_low[:, 2 * width : 3 * width])

        @pl.when(i == 1)
        def _():
            part[size : 2 * size, rows:] = matmul_back(
                branch_rows, resid_low[:, width : 2 * width]
            ) + matmul_back(input_rows, mixed_ref[...])
            first_copy.start(priority=1)

    gives = [
        local(grad_branch_ref, grad_branch_out, give_sem.at[0]),
        local(input_ref, input_out, give_sem.at[1]),
    ]

    def piece_give(_):
        for copy in gives:
            copy.start(priority=1)

    def piece_gates_grad(i):
        @pl.when(i == 0)
        def _():
            gates_grad[...] = contract(heads_ref[...], low_ref[:, :width])

        @pl.when(i == 1)
        def _():
            gates_grad[...] = contract(heads_ref[...], low_ref[:, width:])

        place = lax.broadcasted_iota(jnp.int32, (head, width), 1)
        line = jnp.zeros((head, width), F32)
        for h in range(heads):
            row = gates_grad[h * head : (h + 1) * head, :]
            inside = jnp.logical_and(place >= h * head, place < (h + 1) * head)
            line = jnp.where(inside, row, line)

        for j in range(2):

            @pl.when(i == j)
            def _():
                blocks_ref[:, j * width : (j + 1) * width] = line

    tall = resid_low.shape[1] // WEIGHT_STEPS

    def stage_store(i):
        at = block(lax.rem(i, WEIGHT_STEPS), tall)
        slot = lax.rem(i, 2)
        return local(
            stage_ref.at[slot],
            rec_out.at[i // WEIGHT_STEPS, at, pl.ds(0, width)],
            stage_sem.at[slot],
        )

    def piece_weights(i):
        @pl.when(i == 0)
        def _():
            loads[7].wait()
            loads[8].wait()

        @pl.loop(2 * i, 2 * i + 2)
        def _(j):
            weight_of(j)

    def weight_of(i):
        @pl.when(i >= 2)
        def _():
            stage_store(i - 2).wait()

        at = block(lax.rem(i, WEIGHT_STEPS), tall)
        slot = lax.rem(i, 2)
        for which, (left, right) in enumerate(
            ((resid_low, mixed_ref), (normed_ref, grad_branch_ref), (normed_ref, input_ref))
        ):
            @pl.when(i // WEIGHT_STEPS == which)
            def _():
                stage_ref[slot] = contract(left[:, at], right[...])

        stage_store(i).start(priority=1)

    weights = 3 * WEIGHT_STEPS
    plan = []
    begin = 3
    early = WEIGHT_STEPS // 2

    def piece_weights_later(i):
        piece_weights(i + early)

    for work, times, gap in (
        (piece_direct, seqs, 0),
        (piece_entry, 1, 0),
        (piece_weights, early, 0),
        (piece_projections, 1, 4),
        (piece_state, 1, 0),
        (piece_gates, parts * seqs, 0),
        (piece_head, 1, 0),
        (piece_taps, seqs // 2, 0),
        (piece_gates_grad, 2, 3),
        (piece_tail, 1, 0),
        (piece_input, seqs // 2, 0),
        (piece_give, 1, 0),
        (piece_first, 2, 0),
        (piece_weights_later, weights // 2 - early, 0),
    ):
        plan.append((work, begin, times))
        begin += times + gap

    def run(step):
        for work, first, times in plan:
            @pl.when(jnp.logical_and(step >= first, step < first + times))
            def _():
                work(step - first)

    def before(k):
        @pl.when(k == SKEW * (n // 2))
        def _():
            loads[0].wait()

        @pl.when(jnp.logical_and(lax.rem(k, GROUP) == 0, k < chunks))
        def _():
            part_load(k // GROUP).wait()

        g = (k - out.shape[0]) // GROUP - 1 + held

        @pl.when(
            jnp.logical_and(
                jnp.logical_and(k >= out.shape[0] + GROUP, lax.rem(k - out.shape[0], GROUP) == 0),
                g < groups,
            )
        )
        def _():
            part_load(g).start(priority=1)

        run(k)

    def root(c, slot, total):
        out[slot] = own_ref[block(c // 2, CHUNK), :] + total

    def store(c, slot):
        return local(out.at[slot], block_out.at[block(c, CHUNK)], store_sem.at[slot])

    def arrive(c, slot):
        store(c, slot).start(priority=1)

    def leave(c, slot):
        store(c, slot).wait()

    line_sum(
        "mp", chunks, held * GROUP, part, inbox, out, sems, before, root, arrive, leave
    )

    @pl.loop(chunks + out.shape[0], max(begin, chunks + out.shape[0]))
    def _(k):
        run(k)

    for copy in gives:
        copy.wait()
    first_copy.wait()
    stage_store(weights - 2).wait()
    stage_store(weights - 1).wait()


def backward_call(span, heads, head, *args):
    block_part = args[0]
    low, w_out, branch, hidden, pre, padded, normed, mixed, rest, gates = args[2:12]
    carry, sums, taps = args[14:17]
    rows, model = block_part.shape
    seqs, width = carry.shape
    devices = lax.axis_size("seq")
    ring = ring_size("mp")
    held = 3 * GROUP * CHUNK
    dma = pltpu.SemaphoreType.DMA
    columns = pltpu.VMEM((width // LANES, seqs * (span + TILE), LANES), F32)
    return pl.pallas_call(
        functools.partial(backward_kernel, span, heads),
        out_shape=(
            shape((rows, model)),
            shape(rest.shape),
            shape((rows, width), BF16),
            shape((rows, width), BF16),
            shape((GROUP * CHUNK, model)),
            shape((4 + taps.shape[0], TILE, width)),
            shape((head, 2 * width)),
        ),
        in_specs=[HBM] * 14 + [VMEM] * 4,
        input_output_aliases={10: 1},
        out_specs=(HBM,) * 5 + (VMEM,) * 2,
        scratch_shapes=line_scratch("mp", held, model)
        + [
            pltpu.VMEM((rows // 2, model), F32),
            pltpu.VMEM((rows, model), BF16),
            pltpu.VMEM((width, model), BF16),
            pltpu.VMEM((rows, width), F32),
            pltpu.VMEM(hidden.shape, F32),
            pltpu.VMEM(pre.shape, F32),
            pltpu.VMEM(padded.shape, F32),
            pltpu.VMEM((rows, model), BF16),
            pltpu.VMEM((rows, width), BF16),
            columns,
            columns,
            pltpu.VMEM((span, width), F32),
            pltpu.VMEM((span, width), F32),
            pltpu.VMEM((seqs, span + TILE, width), F32),
            pltpu.VMEM((rows, width), BF16),
            pltpu.VMEM((rows, 2 * width), BF16),
            pltpu.VMEM((width, width), F32),
            pltpu.VMEM((2, model // WEIGHT_STEPS, width), F32),
            pltpu.VMEM((seqs, width), F32),
            pltpu.VMEM((devices, seqs, width), F32),
            pltpu.VMEM((seqs, TILE, width), F32),
            pltpu.VMEM((seqs, TILE, width), F32),
            dma((10,)),
            dma((3,)),
            dma((ring,)),
            dma((2,)),
            dma((devices - 1,)),
            dma((devices - 1,)),
            dma((1,)),
            dma((1,)),
            pltpu.VMEM(gates.shape, BF16),
            pltpu.VMEM((rows, width), BF16),
            pltpu.VMEM((rows, width), BF16),
            dma((2,)),
            dma((5,)),
        ],
        compiler_params=params(1, 63),
        cost_estimate=cost(200),
        name="backward",
    )(*args)


def line_sum(axis, total, period, part, inbox, out, sems, before, root, arrive, leave):
    send_up, send_down, recv_up, recv_down = sems
    parts = send_up.shape[0]
    columns = out.shape[2] // parts
    n, z = lax.axis_size(axis), lax.axis_index(axis)
    depth = n // 2
    ring = out.shape[0]

    def cols(p):
        return pl.ds(p * columns, columns)

    def root_of(c):
        return depth - 1 + lax.rem(c, 2)

    def up(c, step, side, p):
        slot = lax.rem(c, ring)
        return pltpu.make_async_remote_copy(
            src_ref=part.at[block(lax.rem(c, period), CHUNK), cols(p)],
            dst_ref=inbox.at[side, slot, :, cols(p)],
            send_sem=send_up.at[p, slot],
            recv_sem=recv_up.at[p, side, slot],
            device_id={axis: z + step},
            device_id_type=MESH,
        )

    def down(c, step, side, p):
        slot = lax.rem(c, ring)
        return pltpu.make_async_remote_copy(
            src_ref=out.at[slot, :, cols(p)],
            dst_ref=out.at[slot, :, cols(p)],
            send_sem=send_down.at[p, side, slot],
            recv_sem=recv_down.at[p, slot],
            device_id={axis: z + step},
            device_id_type=MESH,
        )

    inner = jnp.logical_and(z > 0, z < n - 1)

    @pl.loop(0, total + ring)
    def _(k):
        @pl.when(k >= ring)
        def _():
            c = k - ring
            r = root_of(c)
            step = jnp.where(z < r, 1, -1)
            side = jnp.where(z < r, 0, 1)

            @pl.when(z == r)
            def _():
                for p in range(parts):
                    down(c, -1, 0, p).wait_send()
                    down(c, 1, 1, p).wait_send()

            @pl.when(z != r)
            def _():
                for p in range(parts):
                    up(c, step, side, p).wait_send()

            @pl.when(jnp.logical_and(z != r, inner))
            def _():
                for p in range(parts):
                    down(c, -step, side, p).wait_send()

            leave(c, lax.rem(c, ring))

        before(k)

        for i in reversed(range(n + 1)):
            c = k - SKEW * i
            valid = jnp.logical_and(c >= 0, c < total)
            c = jnp.clip(c, 0, total - 1)
            at = block(lax.rem(c, period), CHUNK)
            slot = lax.rem(c, ring)
            r = root_of(c)
            step = jnp.where(z < r, 1, -1)
            side = jnp.where(z < r, 0, 1)
            if i > depth:
                here = jnp.logical_and(z != r, jnp.abs(z - r) == i - depth)

                @pl.when(jnp.logical_and(valid, here))
                def _():
                    for p in range(parts):
                        down(c, step, side, p).wait_recv()

                        @pl.when(inner)
                        def _():
                            down(c, -step, side, p).start()

                    arrive(c, slot)
            elif i == depth:

                @pl.when(jnp.logical_and(valid, z == r))
                def _():
                    for p in range(parts):
                        up(c, 1, 0, p).wait_recv()
                        up(c, -1, 1, p).wait_recv()
                    root(c, slot, part[at, :] + inbox[0, slot] + inbox[1, slot])
                    for p in range(parts):
                        down(c, -1, 0, p).start()
                        down(c, 1, 1, p).start()
                    arrive(c, slot)
            else:
                here = jnp.where(z < r, z, n - 1 - z) == i

                @pl.when(jnp.logical_and(valid, jnp.logical_and(z != r, here)))
                def _():
                    for p in range(parts):
                        if i > 0:
                            up(c, step, side, p).wait_recv()
                            part[at, cols(p)] += inbox[side, slot, :, cols(p)]
                        up(c, step, side, p).start()


def ring_size(axis):
    return SKEW * lax.axis_size(axis) + 4


def line_scratch(axis, rows, model, parts=2):
    dma = pltpu.SemaphoreType.DMA
    ring = ring_size(axis)
    return [
        pltpu.VMEM((rows, model), F32),
        pltpu.VMEM((2, ring, CHUNK, model), F32),
        pltpu.VMEM((ring, CHUNK, model), F32),
        dma((parts, ring)),
        dma((parts, 2, ring)),
        dma((parts, 2, ring)),
        dma((parts, ring)),
    ]


def mean_square(x):
    return lax.rsqrt(jnp.mean(x * x, axis=-1, keepdims=True) + EPS)


def nothing(*_):
    pass


def fold(value):
    total = value[0:TILE]
    for i in range(1, value.shape[0] // TILE):
        total = total + value[i * TILE : (i + 1) * TILE]
    return total


def norm_grad(value, gain, grad, acc_ref):
    q = mean_square(value)
    e = gain * grad
    acc_ref[...] += fold(grad * value * q)
    return q * e - value * (q * q * q) * jnp.mean(e * value, axis=-1, keepdims=True)


def middle_kernel(
    mixed_in,
    w_out_in,
    x_in,
    og_in,
    gain_ref,
    w_gate_in,
    w_up_in,
    w_down_in,
    normed_out,
    hidden_out,
    gate_out,
    up_out,
    glow_out,
    block_out,
    low_out,
    own_grad_out,
    weight_out,
    rest_out,
    own_out,
    acc_ref,
    part,
    inbox,
    out,
    send_up,
    send_down,
    recv_up,
    recv_down,
    mixed,
    w_out,
    w_gate,
    w_up,
    w_down,
    normed,
    rows_ref,
    og_ref,
    glow,
    gate_val,
    up_val,
    grad_hidden,
    hidden,
    grad_gate,
    grad_up,
    block_part,
    low,
    weight_sem,
    row_sem,
    og_sem,
    act_sem,
    low_sem,
    own_sem,
    again_sem,
    stage_sem,
    rest_sem,
    own_ref,
):
    n, z = lax.axis_size("mp"), lax.axis_index("mp")
    count = part.shape[0] // CHUNK
    size = GROUP * CHUNK
    groups = count // GROUP
    ring = out.shape[0]
    sems = (send_up, send_down, recv_up, recv_down)
    local = pltpu.make_async_copy

    loads = [
        local(source, target, weight_sem.at[i])
        for i, (source, target) in enumerate(
            (
                (mixed_in, mixed),
                (w_out_in, w_out),
                (w_gate_in, w_gate),
                (w_up_in, w_up),
                (w_down_in, w_down.at[slice(0, w_down_in.shape[0])]),
            )
        )
    ]
    for copy in loads:
        copy.start(priority=1)
    deep = w_down_in.shape[0]

    def og_load(g):
        return local(og_in.at[block(g, size)], og_ref, og_sem.at[0])

    og_load(0).start(priority=1)
    enter_all(("mp",))
    acc_ref[...] = jnp.zeros_like(acc_ref)
    loads[0].wait()
    loads[1].wait()

    def is_root(c):
        return z == n // 2 - 1 + lax.rem(c, 2)

    def row_load(source, c):
        slot = lax.rem(c, ring)
        at = block(lax.rem(c, count), CHUNK)
        return local(source.at[at], rows_ref.at[slot], row_sem.at[slot])

    acts = (
        (normed, normed_out),
        (glow, glow_out),
        (hidden, hidden_out),
        (grad_gate, gate_out),
        (grad_up, up_out),
        (block_part, block_out),
    )

    def act_store(i, g):
        source, target = acts[i]
        source = source.at[lax.rem(g, 2)] if i == 0 else source
        return local(source, target.at[block(g, size)], act_sem.at[i])

    def at_tick(k, first, work):
        g = (k - first) // GROUP

        @pl.when(
            jnp.logical_and(
                jnp.logical_and(k >= first, k < first + GROUP * groups),
                lax.rem(k - first, GROUP) == 0,
            )
        )
        def _():
            work(g)

    def project(g):
        part[block(g, size), :] = dot(mixed[block(g, size), :], w_out[...])

    def piece_gate(g):
        @pl.when(g == 0)
        def _():
            for copy in loads[2:]:
                copy.wait()

        def work(cols):
            gate_val[:, cols] = dot(normed[lax.rem(g, 2)], w_gate[:, cols])

        work(slice(None))
        act_store(0, g).start(priority=1)

    def piece_up(g):
        def work(cols):
            up_val[:, cols] = dot(normed[lax.rem(g, 2)], w_up[:, cols])

        work(slice(None))

        @pl.when(g > 0)
        def _():
            for i in range(1, 6):
                act_store(i, g - 1).wait()

    def piece_low(g):
        og_load(g).wait()

        @pl.loop(0, size // ROWS)
        def _(q):
            glow[block(q, ROWS), :] = og_ref[block(q, ROWS), :].astype(BF16)

        @pl.when(g + 1 < groups)
        def _():
            og_load(g + 1).start(priority=1)

        act_store(1, g).start(priority=1)
        act_store(0, g).wait()

    def piece_hidden(g):
        def work(cols):
            grad_hidden[...] = matmul_back(glow[...], w_down[:deep, :])

        work(slice(None))

    def piece_act(g):
        @pl.loop(0, size // CHUNK)
        def _(q):
            at = block(q, CHUNK)
            up = up_val[at, :]
            grad = grad_hidden[at, :]
            act, slope = gelu_both(gate_val[at, :])
            hidden[at, :] = (act * up).astype(BF16)
            grad_gate[at, :] = (grad * up * slope).astype(BF16)
            grad_up[at, :] = (grad * act).astype(BF16)

        for i in range(2, 5):
            act_store(i, g).start(priority=1)

    def piece_down(g):
        def work(cols):
            block_part[:, cols] = dot(hidden[...], w_down[:deep, cols])

        work(slice(None))
        act_store(5, g).start(priority=1)

    def piece_back_gate(g):
        def work(cols):
            part[block(g, size), cols] = matmul_back(grad_gate[...], w_gate[cols, :])

        work(slice(None))

    def piece_back_up(g):
        def work(cols):
            part[block(g, size), cols] += matmul_back(grad_up[...], w_up[cols, :])

        work(slice(None))

    tokens = count * CHUNK
    half = tokens // 2
    quarter = half // 2
    again = [
        local(source, target, again_sem.at[i])
        for i, (source, target) in enumerate(
            (
                (normed_out, w_down.at[slice(0, tokens)]),
                (gate_out, w_gate.at[slice(0, tokens)]),
                (up_out, w_up.at[slice(0, tokens)]),
                (hidden_out, w_gate.at[slice(tokens, 2 * tokens)]),
                (glow_out.at[slice(0, half)], w_down.at[slice(tokens, tokens + half)]),
                (glow_out.at[slice(half, half + quarter)], normed.at[0]),
                (glow_out.at[slice(half + quarter, tokens)], normed.at[1]),
            )
        )
    ]
    tall = w_gate.shape[0] // WEIGHT_STEPS
    stages = (gate_val, up_val, grad_hidden)

    kept = weight_out.shape[2]
    before_rest = rest_out.shape[2] - (deep - kept)

    def stage_stores(which, i):
        at = block(i, tall)
        return (
            local(
                stages[which].at[:, pl.ds(0, kept)],
                weight_out.at[which, at],
                stage_sem.at[which],
            ),
            local(
                stages[which].at[:, pl.ds(kept, deep - kept)],
                rest_out.at[which, at, pl.ds(before_rest, deep - kept)],
                rest_sem.at[which],
            ),
        )

    own_copy = local(own_ref, own_out, rest_sem.at[3])

    def piece_reload():
        own_copy.start(priority=1)
        for i in range(1, 6):
            act_store(i, groups - 1).wait()
        for copy in again:
            copy.start(priority=1)

    def piece_ready():
        for copy in again:
            copy.wait()

    def contract(left, right):
        return lax.dot_general(left, right, CONTRACT_ROWS, preferred_element_type=F32)

    def piece_weight(step):
        i = step // 3
        at = block(i, tall)
        for which in range(3):

            @pl.when(lax.rem(step, 3) == which)
            def _():
                @pl.when(i > 0)
                def _():
                    for copy in stage_stores(which, i - 1):
                        copy.wait()

                stage = stages[which]

                def work(cols):
                    if which == 0:
                        stage[:, cols] = contract(w_down[:tokens, at], w_gate[:tokens, cols])
                    elif which == 1:
                        stage[:, cols] = contract(w_down[:tokens, at], w_up[:tokens, cols])
                    else:
                        middle = tokens + half + quarter
                        stage[:, cols] = (
                            contract(
                                w_down[tokens : tokens + half, at],
                                w_gate[tokens : tokens + half, cols],
                            )
                            + contract(normed[0, :, at], w_gate[tokens + half : middle, cols])
                            + contract(normed[1, :, at], w_gate[middle : 2 * tokens, cols])
                        )

                work(slice(None))
                for copy in stage_stores(which, i):
                    copy.start(priority=1)

    first = GROUP + SKEW * n
    spare = GROUP * groups + ring + 3
    first_weight = spare + 3
    weights = 3 * WEIGHT_STEPS

    def before(k):
        @pl.when(k == spare)
        def _():
            piece_reload()

        @pl.when(k == first_weight - 1)
        def _():
            piece_ready()

        @pl.when(jnp.logical_and(k >= first_weight, k < first_weight + weights))
        def _():
            piece_weight(k - first_weight)

        @pl.when(jnp.logical_and(k < count, is_root(k)))
        def _():
            row_load(x_in, k).start(priority=1)

        @pl.when(
            jnp.logical_and(jnp.logical_and(k >= count, k < 2 * count), is_root(k))
        )
        def _():
            row_load(og_in, k).start(priority=1)

        @pl.when(k == 0)
        def _():
            project(0)

        @pl.when(jnp.logical_and(lax.rem(k, GROUP) == GROUP // 2, k < (groups - 1) * GROUP))
        def _():
            project(k // GROUP + 1)

        at_tick(k, first, piece_gate)
        at_tick(k, first + 1, piece_up)
        at_tick(k, first + 2, piece_low)
        at_tick(k, first + 3, piece_hidden)
        at_tick(k, first + 4, piece_act)
        at_tick(k, first + 6, piece_down)
        at_tick(k, GROUP + ring, piece_back_gate)
        at_tick(k, GROUP + ring + 2, piece_back_up)

    def root(c, slot, total):
        j = lax.rem(c, count)
        mine = block(j // 2, CHUNK)
        row_load(x_in, c).wait()

        @pl.when(c < count)
        def _():
            value = rows_ref[slot] + total
            own_ref[mine, :] = value
            out[slot] = (value * mean_square(value) * gain_ref[...]).astype(BF16).astype(F32)

        @pl.when(c >= count)
        def _():
            back = norm_grad(own_ref[mine, :], gain_ref[...], total, acc_ref)
            out[slot] = rows_ref[slot] + back

    def low_store(c, slot):
        at = block(lax.rem(c, count), CHUNK)
        return local(low.at[slot], low_out.at[at], low_sem.at[slot])

    def own_store(c, slot):
        at = block(lax.rem(c, count) // 2, CHUNK)
        return local(out.at[slot], own_grad_out.at[at], own_sem.at[slot])

    def arrive(c, slot):
        @pl.when(c < count)
        def _():
            normed[lax.rem(c // GROUP, 2), block(lax.rem(c, GROUP), CHUNK), :] = out[slot].astype(BF16)

        @pl.when(c >= count)
        def _():
            low[slot] = out[slot].astype(BF16)
            low_store(c, slot).start(priority=1)

            @pl.when(is_root(c))
            def _():
                own_store(c, slot).start(priority=1)

    def leave(c, slot):
        @pl.when(c >= count)
        def _():
            low_store(c, slot).wait()

            @pl.when(is_root(c))
            def _():
                own_store(c, slot).wait()

    line_sum("mp", 2 * count, count, part, inbox, out, sems, before, root, arrive, leave)

    own_copy.wait()
    for which in range(3):
        for copy in stage_stores(which, WEIGHT_STEPS - 1):
            copy.wait()


def middle_call(*args):
    mixed, w_out, x, og, gain, w_gate, w_up, w_down = args
    rows, model = x.shape
    width, hidden = mixed.shape[1], w_gate.shape[1]
    size = GROUP * CHUNK
    dma = pltpu.SemaphoreType.DMA
    ring = ring_size("mp")
    act = shape((rows, hidden), BF16)
    tall = shape((rows, model), BF16)
    return pl.pallas_call(
        middle_kernel,
        out_shape=(
            tall,
            act,
            act,
            act,
            tall,
            shape((rows, model)),
            tall,
            shape((rows // 2, model)),
            shape((3, model, hidden - hidden // LATER)),
            shape((3, model, width + hidden // LATER)),
            shape((rows // 2, model)),
            shape((TILE, model)),
        ),
        in_specs=[HBM] * 4 + [VMEM] + [HBM] * 3,
        out_specs=(HBM,) * 11 + (VMEM,),
        scratch_shapes=line_scratch("mp", rows, model)
        + [
            pltpu.VMEM((rows, width), BF16),
            pltpu.VMEM((width, model), BF16),
            pltpu.VMEM((model, hidden), BF16),
            pltpu.VMEM((model, hidden), BF16),
            pltpu.VMEM((max(hidden, rows * 3 // 2), model), BF16),
            pltpu.VMEM((2, size, model), BF16),
            pltpu.VMEM((ring, CHUNK, model), F32),
            pltpu.VMEM((size, model), F32),
            pltpu.VMEM((size, model), BF16),
            pltpu.VMEM((size, hidden), F32),
            pltpu.VMEM((size, hidden), F32),
            pltpu.VMEM((size, hidden), F32),
            pltpu.VMEM((size, hidden), BF16),
            pltpu.VMEM((size, hidden), BF16),
            pltpu.VMEM((size, hidden), BF16),
            pltpu.VMEM((size, model), F32),
            pltpu.VMEM((ring, CHUNK, model), BF16),
            dma((5,)),
            dma((ring,)),
            dma((1,)),
            dma((6,)),
            dma((ring,)),
            dma((ring,)),
            dma((7,)),
            dma((3,)),
            dma((4,)),
            pltpu.VMEM((rows // 2, model), F32),
        ],
        compiler_params=params(2, 63),
        cost_estimate=cost(400),
        name="middle",
    )(*args)


def last_kernel(
    first_in,
    own_grad_in,
    x_in,
    grad_branch_in,
    input_in,
    w_branch_in,
    w_input_in,
    gain_ref,
    other_acc,
    sums_in,
    ends_in,
    blocks_in,
    grad_out,
    norm_ref,
    small_out,
    part,
    inbox,
    out,
    send_up,
    send_down,
    recv_up,
    recv_down,
    own_grad_ref,
    x_ref,
    grad_branch,
    input_low,
    w_branch,
    w_input,
    load_sem,
    store_sem,
    acc_ref,
    mine_ref,
    seq_in,
    mp_in,
    send_s,
    recv_s,
    send_m,
    recv_m,
    small,
    small_in,
    send_v,
    recv_v,
):
    count = part.shape[0] // CHUNK
    size = GROUP * CHUNK
    sems = (send_up, send_down, recv_up, recv_down)
    local = pltpu.make_async_copy

    loads = [
        local(source, target, load_sem.at[i])
        for i, (source, target) in enumerate(
            (
                (grad_branch_in, grad_branch),
                (w_branch_in, w_branch),
                (input_in, input_low),
                (w_input_in, w_input),
                (own_grad_in, own_grad_ref),
                (x_in, x_ref),
            )
        )
    ]
    first_load = local(first_in, part.at[slice(0, size)], load_sem.at[6])
    first_load.start()
    for copy in loads:
        copy.start(priority=1)
    acc_ref[...] = jnp.zeros_like(acc_ref)
    norm_ref[...] = jnp.zeros_like(norm_ref)
    enter_all(("seq", "mp"))
    first_load.wait()

    kinds = sums_in.shape[0]
    me = lax.axis_index("seq")
    width = sums_in.shape[2]
    height = kinds + ends_in.shape[0]
    head = blocks_in.shape[0]
    levels = small_in.shape[0]

    def exchange(level):
        bit = 1 << level
        partner = me + bit - 2 * bit * lax.rem(me // bit, 2)
        return pltpu.make_async_remote_copy(
            src_ref=small.at[level],
            dst_ref=small_in.at[level],
            send_sem=send_v.at[level],
            recv_sem=recv_v.at[level],
            device_id={"seq": partner},
            device_id_type=MESH,
        )

    spacing = (count - 4) // (levels + 1)
    plane = lax.axis_index("mp")

    def norm_sum(i, k, first, gaps, source):
        seq_copies = to_all("seq", mine_ref.at[i, 0], seq_in.at[i], send_s.at[i], recv_s.at[i])
        mp_copies = to_all("mp", mine_ref.at[i, 1], mp_in.at[i], send_m.at[i], recv_m.at[i])

        @pl.when(k == first)
        def _():
            mine_ref[i, 0] = jnp.sum(source[...], axis=0, keepdims=True)
            seq_in[i, me] = mine_ref[i, 0]
            for copy in seq_copies:
                copy.start()

        @pl.when(k == first + gaps[0])
        def _():
            for copy in seq_copies:
                copy.wait()
            mine_ref[i, 1] = jnp.sum(seq_in[i], axis=0)
            mp_in[i, plane] = mine_ref[i, 1]
            for copy in mp_copies:
                copy.start()

        @pl.when(k == first + gaps[0] + gaps[1])
        def _():
            for copy in mp_copies:
                copy.wait()
            norm_ref[i : i + 1, :] = jnp.sum(mp_in[i], axis=0)

    settled = count + SKEW * (lax.axis_size("mp") // 2)

    def before(k):
        @pl.when(k == 2)
        def _():
            for i in range(kinds):
                small[0, i : i + 1, :] = jnp.sum(sums_in[i], axis=0, keepdims=True)
            small[0, kinds:height, :] = ends_in[...]
            small[0, height : height + head, :] = blocks_in[:, :width]
            small[0, height + head :, :] = blocks_in[:, width:]

        for level in range(levels + 1):

            @pl.when(k == 3 + level * spacing)
            def _():
                if level > 0:
                    exchange(level - 1).wait()
                    total = small[level - 1] + small_in[level - 1]
                    if level < levels:
                        small[level] = total
                    else:
                        small_out[...] = total
                if level < levels:
                    exchange(level).start()

        norm_sum(0, k, settled, (2, 3), acc_ref)
        norm_sum(1, k, 10, (20, 20), other_acc)

        @pl.when(k == 4)
        def _():
            for copy in loads[:4]:
                copy.wait()

        @pl.when(
            jnp.logical_and(
                lax.rem(k, 4) == 0, jnp.logical_and(k > 0, k // 4 < count // GROUP)
            )
        )
        def _():
            at = block(k // 4, size)

            def work(cols):
                part[at, cols] = matmul_back(grad_branch[at, :], w_branch[cols, :]) + matmul_back(
                    input_low[at, :], w_input[cols, :]
                )

            work(slice(None))

        @pl.when(k == SKEW * (lax.axis_size("mp") // 2))
        def _():
            for copy in loads[4:]:
                copy.wait()

    def root(c, slot, total):
        back = norm_grad(x_ref[block(c, CHUNK), :], gain_ref[...], total, acc_ref)
        out[slot] = own_grad_ref[block(c // 2, CHUNK), :] + back

    def store(c, slot):
        return local(out.at[slot], grad_out.at[block(c, CHUNK)], store_sem.at[slot])

    def arrive(c, slot):
        store(c, slot).start(priority=1)

    def leave(c, slot):
        store(c, slot).wait()

    line_sum("mp", count, count, part, inbox, out, sems, before, root, arrive, leave)


def enter_all(axes):
    barrier = pltpu.get_barrier_semaphore()
    count = 0
    for axis in axes:
        size, me = lax.axis_size(axis), lax.axis_index(axis)
        for d in range(1, size):
            pl.semaphore_signal(
                barrier, 1, device_id={axis: lax.rem(me + d, size)}, device_id_type=MESH
            )
        count += size - 1
    pl.semaphore_wait(barrier, count)


def cost(micros):
    return pl.CostEstimate(flops=int(micros * 1e9), bytes_accessed=1 << 20, transcendentals=0)


def nseq_levels():
    return (lax.axis_size("seq") - 1).bit_length()


def last_call(*args):
    x, grad_branch = args[2:4]
    rows, model = x.shape
    width = grad_branch.shape[1]
    lines = args[9].shape[0] + args[10].shape[0] + 2 * args[11].shape[0]
    levels = nseq_levels()
    dma = pltpu.SemaphoreType.DMA
    nseq, nmp = lax.axis_size("seq"), lax.axis_size("mp")
    return pl.pallas_call(
        last_kernel,
        out_shape=(shape((rows, model)), shape((TILE, model)), shape((lines, width))),
        in_specs=[HBM] * 7 + [VMEM] * 5,
        out_specs=(HBM,) + (VMEM,) * 2,
        scratch_shapes=line_scratch("mp", rows, model)
        + [
            pltpu.VMEM((rows // 2, model), F32),
            pltpu.VMEM((rows, model), F32),
            pltpu.VMEM((rows, width), BF16),
            pltpu.VMEM((rows, width), BF16),
            pltpu.VMEM((model, width), BF16),
            pltpu.VMEM((model, width), BF16),
            dma((7,)),
            dma((ring_size("mp"),)),
            pltpu.VMEM((TILE, model), F32),
            pltpu.VMEM((2, 2, 1, model), F32),
            pltpu.VMEM((2, nseq, 1, model), F32),
            pltpu.VMEM((2, nmp, 1, model), F32),
            dma((2, nseq - 1)),
            dma((2, nseq - 1)),
            dma((2, nmp - 1)),
            dma((2, nmp - 1)),
            pltpu.VMEM((levels, lines, width), F32),
            pltpu.VMEM((levels, lines, width), F32),
            dma((levels,)),
            dma((levels,)),
        ],
        compiler_params=params(4, 62),
        cost_estimate=cost(200),
        name="last_sums",
    )(*args)


def finish_kernel(
    heads,
    block_in,
    grad_in,
    mlp_in,
    rec_in,
    small_hbm,
    norm_hbm,
    decay_hbm,
    block_out,
    grad_out,
    w_gate_out,
    w_up_out,
    w_branch_out,
    w_input_out,
    w_down_out,
    w_out_out,
    gate_r_out,
    gate_i_out,
    taps_out,
    conv_bias_out,
    bias_r_out,
    bias_i_out,
    decay_out,
    norm_in_out,
    norm_mlp_out,
    state_out,
    conv_out,
    tall,
    mlp,
    rec,
    small_in,
    norm_in,
    raw_ref,
    load_sem,
    store_sem,
    extra_sem,
):
    local = pltpu.make_async_copy
    width = small_in.shape[1]
    kept = mlp.shape[2]
    late = rec.shape[2] - width
    size = grad_in.shape[0] // COPIES
    extra = [
        local(source, target, extra_sem.at[i])
        for i, (source, target) in enumerate(
            ((small_hbm, small_in), (norm_hbm, norm_in), (decay_hbm, raw_ref))
        )
    ]
    for copy in extra:
        copy.start()
    jobs = [(mlp_in, mlp, None), (rec_in, rec, None)]
    for j, (source, target) in enumerate(((block_in, block_out), (grad_in, grad_out))):
        for i in range(COPIES):
            at = slice(i * size, (i + 1) * size)
            jobs.append((source.at[at], tall.at[j, at], target.at[at]))
    loads = [local(source, held, load_sem.at[i]) for i, (source, held, _) in enumerate(jobs)]
    stores = [
        local(held, target, store_sem.at[i])
        for i, (held, target) in enumerate(
            [(held, target) for _, held, target in jobs[2:]]
            + [
                (mlp.at[0], w_gate_out.at[:, pl.ds(0, kept)]),
                (mlp.at[1], w_up_out.at[:, pl.ds(0, kept)]),
                (rec.at[0, :, pl.ds(width, late)], w_gate_out.at[:, pl.ds(kept, late)]),
                (rec.at[1, :, pl.ds(width, late)], w_up_out.at[:, pl.ds(kept, late)]),
                (rec.at[1, :, pl.ds(0, width)], w_branch_out),
                (rec.at[2, :, pl.ds(0, width)], w_input_out),
            ]
        )
    ]
    for copy in loads:
        copy.start()
    for copy in extra:
        copy.wait()
    taps, seqs, edge = taps_out.shape[0], state_out.shape[0], conv_out.shape[0]
    head = gate_r_out.shape[1]
    decay = small_in[0:1, :].reshape(width) * (RATE_SCALE * jax.nn.sigmoid(-raw_ref[...]))
    decay_out[...] = decay
    bias_r_out[...] = small_in[1:2, :].reshape(width)
    bias_i_out[...] = small_in[2:3, :].reshape(width)
    conv_bias_out[...] = small_in[3:4, :].reshape(width)
    taps_out[...] = small_in[4 : 4 + taps, :]
    begin = 4 + taps
    state_out[...] = small_in[begin : begin + seqs, :]
    for s in range(seqs):
        end = begin + seqs + (s + 1) * TILE
        for k in range(edge):
            conv_out[k, s : s + 1, :] = small_in[end - edge + k : end - edge + k + 1, :]
    begin += seqs + seqs * TILE
    for i, target in enumerate((gate_r_out, gate_i_out)):
        line = small_in[begin + i * head : begin + (i + 1) * head, :]
        for h in range(heads):
            turned = line if h == 0 else pltpu.roll(line, width - h * head, 1)
            target[h] = turned[:, :head]
    norm_in_out[...] = norm_in[0:1, :].reshape(norm_in.shape[1])
    norm_mlp_out[...] = norm_in[1:2, :].reshape(norm_in.shape[1])
    loads[0].wait()
    loads[1].wait()
    for copy in stores[2 * COPIES :]:
        copy.start()
    w_down_out[:kept, :] = mlp[2].T
    w_down_out[kept:, :] = rec[2, :, width:].T
    w_out_out[...] = rec[0, :, :width].T
    for i in range(2 * COPIES):
        loads[2 + i].wait()
        stores[i].start()
    for copy in stores:
        copy.wait()


def finish_call(seqs, heads, head, edge, *args):
    _, stream_grad, mlp_grads, rec_grads, small, norms, decay = args
    rows, model = stream_grad.shape
    own, kept = mlp_grads.shape[1:]
    width = small.shape[1]
    hidden = kept + rec_grads.shape[2] - width
    taps = edge + 1
    line = shape((width,))
    tall = shape((rows, model))
    return pl.pallas_call(
        functools.partial(finish_kernel, heads),
        out_shape=(
            tall,
            tall,
            shape((own, hidden)),
            shape((own, hidden)),
            shape((own, width)),
            shape((own, width)),
            shape((hidden, own)),
            shape((width, own)),
            shape((heads, head, head)),
            shape((heads, head, head)),
            shape((taps, width)),
            line,
            line,
            line,
            line,
            shape((model,)),
            shape((model,)),
            shape((seqs, width)),
            shape((edge, seqs, width)),
        ),
        in_specs=[HBM] * 4 + [PINNED] * 3,
        out_specs=(HBM,) * 6 + (VMEM,) * 13,
        scratch_shapes=[
            pltpu.VMEM((2, rows, model), F32),
            pltpu.VMEM(mlp_grads.shape, F32),
            pltpu.VMEM(rec_grads.shape, F32),
            pltpu.VMEM(small.shape, F32),
            pltpu.VMEM(norms.shape, F32),
            pltpu.VMEM(decay.shape, F32),
            pltpu.SemaphoreType.DMA((2 + 2 * COPIES,)),
            pltpu.SemaphoreType.DMA((6 + 2 * COPIES,)),
            pltpu.SemaphoreType.DMA((3,)),
        ],
        compiler_params=pltpu.CompilerParams(vmem_limit_bytes=63 << 20),
        cost_estimate=cost(15),
        name="finish",
    )(*args)


def params(collective, megabytes=60):
    return pltpu.CompilerParams(
        collective_id=collective, has_side_effects=True, vmem_limit_bytes=megabytes << 20
    )


def shape(dims, dtype=F32):
    return jax.ShapeDtypeStruct(dims, dtype)


def recurrence_forward(span, *args):
    x, w_input = args[:2]
    rows, model = x.shape
    seqs, width = rows // span, w_input.shape[1]
    devices = lax.axis_size("seq")
    dma = pltpu.SemaphoreType.DMA
    groups = seqs // 2
    columns = (width // LANES, rows, LANES)
    spaced = (width // LANES, seqs * (span + TILE), LANES)
    padded = (seqs, span + TILE, width)
    return pl.pallas_call(
        functools.partial(forward_kernel, span),
        out_shape=(
            shape((rows, model), BF16),
            shape((rows, width)),
            shape(padded),
            shape((rows, 2 * width)),
            shape(columns),
            shape((rows, width), BF16),
            shape((seqs, width)),
            shape((devices, 2, seqs, width)),
            shape((width, 2 * width), BF16),
            shape((TILE, width)),
            shape(((seqs + 1) * TILE, width)),
        ),
        in_specs=[HBM] * 3 + [VMEM] * 8 + [pl.BlockSpec(memory_space=pltpu.SMEM)] + [VMEM] * 2,
        out_specs=(HBM,) * 5 + (VMEM,) * 6,
        scratch_shapes=[
            pltpu.VMEM((rows, model), F32),
            pltpu.VMEM((model, width), BF16),
            pltpu.VMEM((model, width), BF16),
            pltpu.VMEM((rows, model), BF16),
            pltpu.VMEM((rows, width), F32),
            pltpu.VMEM(padded, F32),
            pltpu.VMEM((rows, 2 * width), F32),
            pltpu.VMEM(columns, F32),
            pltpu.VMEM((rows, width), F32),
            pltpu.VMEM(spaced, F32),
            pltpu.VMEM(spaced, F32),
            pltpu.VMEM((2, span, width), F32),
            pltpu.VMEM((seqs, TILE, width), F32),
            pltpu.VMEM((seqs, TILE, width), F32),
            pltpu.VMEM((2, seqs, width), F32),
            dma((groups + 2,)),
            dma((4,)),
            dma((groups,)),
            dma((devices - 1,)),
            dma((devices - 1,)),
            dma((1,)),
            dma((1,)),
        ],
        compiler_params=params(0),
        cost_estimate=cost(50),
        name="recurrence_forward",
    )(*args)


def widen(array, width):
    short = width - array.shape[-1]
    if short == 0:
        return array
    return jnp.pad(array, [(0, 0)] * (array.ndim - 1) + [(0, short)])


def per_device(
    stream,
    norm_in,
    w_branch,
    w_input,
    conv_kernel,
    conv_bias,
    gate_r,
    bias_r,
    gate_i,
    bias_i,
    decay_param,
    w_out,
    norm_mlp,
    w_gate,
    w_up,
    w_down,
    state_init,
    conv_init,
    fresh_rows,
    out_grad,
):
    seqs, span, model = stream.shape
    channels = w_branch.shape[1]
    mlp_dev = w_gate.shape[1]
    heads, head_width = gate_r.shape[:2]
    taps = conv_kernel.shape[0]
    edge = taps - 1
    rows = seqs * span
    devices = lax.axis_size("seq")
    position = lax.axis_index("seq")
    width = -(-channels // 128) * 128

    flat_in = stream.reshape(rows, model)
    flat_grad = out_grad.reshape(rows, model)
    w_branch_p = widen(w_branch, width)
    w_input_p = widen(w_input, width)
    w_out_p = jnp.pad(w_out, ((0, width - channels), (0, 0))) if width > channels else w_out
    taps_p = widen(conv_kernel, width)
    def line(value):
        return widen(value, width)

    (
        normed,
        branch,
        padded,
        pre,
        hidden,
        mixed,
        carry,
        sums,
        gates,
        rates,
        ends,
    ) = recurrence_forward(
        span,
        flat_in,
        w_input_p,
        w_branch_p,
        norm_in[None],
        taps_p,
        line(conv_bias),
        line(decay_param),
        line(bias_r),
        line(bias_i),
        gate_r,
        gate_i,
        fresh_rows,
        widen(state_init, width),
        widen(jnp.swapaxes(conv_init, 0, 1), width),
    )
    made = middle_call(mixed, w_out_p, flat_in, flat_grad, norm_mlp[None], w_gate, w_up, w_down)
    block_part, resid_low, own_grad, mlp_grads, rest, own, norm_mlp_acc = made[5:]
    mlp_grads = lax.psum_scatter(mlp_grads, "seq", scatter_dimension=1, tiled=True)
    block_out, rec_grads, grad_branch, input_low, first_rows, acc, blocks = backward_call(
        span,
        heads,
        head_width,
        block_part,
        own,
        resid_low,
        w_out_p,
        branch,
        hidden,
        pre,
        padded,
        normed,
        mixed,
        rest,
        gates,
        w_branch_p,
        w_input_p,
        carry,
        sums,
        taps_p,
        rates,
    )

    rec_grads, grad_branch, mlp_grads = lax.optimization_barrier(
        (rec_grads, grad_branch, mlp_grads)
    )
    rec_grads = lax.psum_scatter(rec_grads, "seq", scatter_dimension=1, tiled=True)

    stream_grad, norm_grads, small = last_call(
        first_rows,
        own_grad,
        flat_in,
        grad_branch,
        input_low,
        w_branch_p,
        w_input_p,
        norm_in[None],
        norm_mlp_acc,
        acc,
        ends,
        blocks,
    )
    (
        block_out,
        stream_grad,
        w_gate_grad,
        w_up_grad,
        w_branch_grad,
        w_input_grad,
        w_down_grad,
        w_out_grad,
        gate_r_grad,
        gate_i_grad,
        taps_grad,
        conv_bias_grad,
        bias_r_grad,
        bias_i_grad,
        decay_grad,
        norm_in_grad,
        norm_mlp_grad,
        final_state,
        final_conv,
    ) = finish_call(
        seqs,
        heads,
        head_width,
        edge,
        block_out,
        stream_grad,
        mlp_grads,
        rec_grads,
        small,
        norm_grads,
        line(decay_param),
    )
    return (
        block_out.reshape(stream.shape),
        stream_grad.reshape(stream.shape),
        norm_in_grad,
        w_branch_grad[:, :channels],
        w_input_grad[:, :channels],
        taps_grad[:, :channels],
        conv_bias_grad[:channels],
        gate_r_grad,
        bias_r_grad[:channels],
        gate_i_grad,
        bias_i_grad[:channels],
        decay_grad[:channels],
        w_out_grad[:channels],
        norm_mlp_grad,
        w_gate_grad,
        w_up_grad,
        w_down_grad,
        final_state[:, :channels],
        jnp.swapaxes(final_conv, 0, 1)[:, :, :channels],
    )


def solution(mesh):
    seq_rows = P(None, "seq", None)
    columns = P(None, "mp")
    channel = P("mp")
    return jax.shard_map(
        per_device,
        mesh=mesh,
        in_specs=(
            seq_rows,
            P(),
            columns,
            columns,
            columns,
            channel,
            P("mp", None, None),
            channel,
            P("mp", None, None),
            channel,
            channel,
            P("mp", None),
            P(),
            columns,
            columns,
            P("mp", None),
            columns,
            P(None, None, "mp"),
            P(),
            seq_rows,
        ),
        out_specs=(
            seq_rows,
            seq_rows,
            P(),
            P("seq", "mp"),
            P("seq", "mp"),
            columns,
            channel,
            P("mp", None, None),
            channel,
            P("mp", None, None),
            channel,
            channel,
            P("mp", "seq"),
            P(),
            P("seq", "mp"),
            P("seq", "mp"),
            P("mp", "seq"),
            columns,
            P(None, None, "mp"),
        ),
        check_vma=False,
    )
```

```python
import functools

import jax
import jax.numpy as jnp
from jax import lax
from jax.experimental import pallas as pl
from jax.experimental.pallas import tpu as pltpu
from jax.sharding import PartitionSpec as P

MESH = pl.DeviceIdType.MESH
RATE_SCALE = 8.0
EPS = 1e-06
GELU_C = 0.7978845608028654
GELU_K = 0.044715
CONTRACT_ROWS = (((0,), (0,)), ((), ()))
CONTRACT_LAST = (((1,), (1,)), ((), ()))
TILE = 8
LANES = 128
ROWS = 32
CHUNK = 16
SKEW = 2
GROUP = 16
WEIGHT_STEPS = 8
COPIES = 8
LATER = 6
F32 = jnp.float32
BF16 = jnp.bfloat16
VMEM = pl.BlockSpec(memory_space=pltpu.VMEM)
HBM = pl.BlockSpec(memory_space=pl.ANY)
PINNED = pl.BlockSpec(memory_space=pltpu.HBM)


def dot(a, b):
    return jnp.dot(a, b, preferred_element_type=F32)


def matmul_back(a, b):
    return lax.dot_general(a, b, CONTRACT_LAST, preferred_element_type=F32)


def block(i, size):
    return pl.ds(pl.multiple_of(i * size, size), size)


def gelu(x):
    t = jnp.tanh(GELU_C * (x + GELU_K * (x * x * x)))
    return 0.5 * x * (1.0 + t)


def gelu_both(x):
    x2 = x * x
    t = jnp.tanh(GELU_C * (x + GELU_K * (x2 * x)))
    half = 0.5 * (1.0 + t)
    slope = half + 0.5 * x * (1.0 - t * t) * (GELU_C * (1.0 + (3.0 * GELU_K) * x2))
    return x * half, slope


def one_minus_square(log_a, a):
    y = 2.0 * log_a
    s = 1.0 + y * (1.0 / 8.0)
    for k in (7, 6, 5, 4, 3, 2):
        s = 1.0 + (y * (1.0 / k)) * s
    return jnp.where(y > -0.35, -y * s, 1.0 - a * a)


def get(ref, at):
    return jnp.concatenate([ref[j, at, :] for j in range(ref.shape[0])], axis=-1)


def put(ref, at, value):
    for j in range(ref.shape[0]):
        ref[j, at, :] = value[:, j * LANES : (j + 1) * LANES]


def to_all(axis, src, slots, send, recv):
    size, me = lax.axis_size(axis), lax.axis_index(axis)
    return [
        pltpu.make_async_remote_copy(
            src_ref=src,
            dst_ref=slots.at[me],
            send_sem=send.at[d - 1],
            recv_sem=recv.at[d - 1],
            device_id={axis: lax.rem(me + d, size)},
            device_id_type=MESH,
        )
        for d in range(1, size)
    ]


def to_one(axis, distance, src, dst, send, recv):
    size, me = lax.axis_size(axis), lax.axis_index(axis)
    return pltpu.make_async_remote_copy(
        src_ref=src,
        dst_ref=dst,
        send_sem=send,
        recv_sem=recv,
        device_id={axis: lax.rem(me + distance + size, size)},
        device_id_type=MESH,
    )


def spread_gates(blocks_ref, out_ref, start, width):
    heads, size = blocks_ref.shape[:2]
    for h in range(heads):
        block_h = blocks_ref[h].astype(F32)
        parts = [block_h]
        if h > 0:
            parts.insert(0, jnp.zeros((size, h * size), F32))
        if width > (h + 1) * size:
            parts.append(jnp.zeros((size, width - (h + 1) * size), F32))
        row = jnp.concatenate(parts, axis=1).astype(BF16)
        out_ref[h * size : (h + 1) * size, start : start + width] = row
    if width > heads * size:
        rest = jnp.zeros((width - heads * size, width), BF16)
        out_ref[heads * size : width, start : start + width] = rest


def forward_kernel(
    span,
    x_in,
    w_input_in,
    w_branch_in,
    gain_ref,
    taps_ref,
    conv_bias_ref,
    decay_ref,
    bias_r_ref,
    bias_i_ref,
    gate_r_ref,
    gate_i_ref,
    fresh_ref,
    state_ref,
    conv_init_ref,
    normed_out,
    branch_out,
    pad_out,
    pre_out,
    hidden_out,
    mixed_ref,
    carry_ref,
    sums_ref,
    gates_ref,
    vec_ref,
    ends_ref,
    x_ref,
    w_input_ref,
    w_branch_ref,
    normed_ref,
    branch_ref,
    pad_ref,
    pre_ref,
    hidden_ref,
    act_ref,
    a_ref,
    b_ref,
    conv_ref,
    tail_ref,
    tail_in,
    mine_ref,
    load_sem,
    store_sem,
    normed_sem,
    send1,
    recv1,
    send_t,
    recv_t,
):
    seqs = state_ref.shape[0]
    width = taps_ref.shape[1]
    taps = taps_ref.shape[0]
    rows = seqs * span
    devices, me = lax.axis_size("seq"), lax.axis_index("seq")
    local = pltpu.make_async_copy
    pitch = a_ref.shape[1] // seqs
    group = 2 * span
    groups = rows // group

    def x_load(g):
        at = block(g, group)
        return local(x_in.at[at], x_ref.at[at], load_sem.at[g])

    weight_loads = [
        local(w_input_in, w_input_ref, load_sem.at[groups]),
        local(w_branch_in, w_branch_ref, load_sem.at[groups + 1]),
    ]
    x_load(0).start()
    weight_loads[0].start()
    for g in range(1, groups):
        x_load(g).start()
    weight_loads[1].start()

    enter_all(("seq",))
    spread_gates(gate_r_ref, gates_ref, 0, width)
    spread_gates(gate_i_ref, gates_ref, width, width)
    vec_ref[0:1, :] = conv_bias_ref[...].reshape(1, width)
    vec_ref[1:2, :] = jax.nn.softplus(-decay_ref[...].reshape(1, width))
    bias_r = bias_r_ref[...].reshape(1, width)
    bias_i = bias_i_ref[...].reshape(1, width)
    keep = [1.0 - fresh_ref[s].astype(F32) for s in range(seqs)]

    def normed_store(g):
        at = block(g, group)
        return local(normed_ref.at[at], normed_out.at[at], normed_sem.at[g])

    def norm(g):
        x_load(g).wait()
        for q in range(group // CHUNK):
            at = slice(g * group + q * CHUNK, g * group + (q + 1) * CHUNK)
            x = x_ref[at, :]
            normed_ref[at, :] = (x * mean_square(x) * gain_ref[...]).astype(BF16)

    norm(0)
    weight_loads[0].wait()
    for g in range(groups):
        if g + 1 < groups:
            norm(g + 1)
        conv = dot(normed_ref[slice(g * group, (g + 1) * group), :], w_input_ref[...])
        for j in range(group // span):
            pad_ref[g * (group // span) + j, pl.ds(TILE, span), :] = conv[
                j * span : (j + 1) * span
            ]
    for g in range(groups):
        normed_store(g).start(priority=1)

    for s in range(seqs):
        tail_ref[s] = pad_ref[s, pl.ds(span, TILE), :]
    tail_copy = to_one("seq", 1, tail_ref, tail_in, send_t.at[0], recv_t.at[0])
    tail_copy.start()
    weight_loads[1].wait()

    def branch(g):
        branch_ref[block(g, group), :] = dot(normed_ref[block(g, group), :], w_branch_ref[...])

    @pl.loop(0, groups // 2)
    def _(g):
        branch(g)

    stores = [
        local(source, target, store_sem.at[i])
        for i, (source, target) in enumerate(
            (
                (branch_ref, branch_out),
                (pad_ref, pad_out),
                (pre_ref, pre_out),
                (hidden_ref, hidden_out),
            )
        )
    ]
    tail_copy.wait()
    lead = jnp.zeros((TILE - taps + 1, width), F32)
    for s in range(seqs):
        initial = jnp.concatenate(
            [lead] + [conv_init_ref[k, s : s + 1, :] * keep[s] for k in range(taps - 1)], axis=0
        )
        pad_ref[s, pl.ds(0, TILE), :] = jnp.where(me == 0, initial, tail_in[s])
    stores[1].start(priority=1)

    def gates(s, slot):
        for q in range(span // ROWS):
            part = pad_ref[s, pl.ds(q * ROWS, ROWS + TILE), :]
            total = vec_ref[0:1, :]
            for k in range(taps):
                first = TILE - (taps - 1) + k
                total = total + taps_ref[k : k + 1, :] * part[first : first + ROWS]
            conv_ref[slot, pl.ds(q * ROWS, ROWS), :] = total

        pre = dot(conv_ref[slot].astype(BF16), gates_ref[...])
        pre_ref[block(s, span), :width] = pre[:, :width] + bias_r
        pre_ref[block(s, span), width:] = pre[:, width:] + bias_i
        for q in range(span // ROWS):
            rows_q = slice(q * ROWS, (q + 1) * ROWS)
            conv = conv_ref[slot, pl.ds(q * ROWS, ROWS), :]
            recall = jax.nn.sigmoid(pre[rows_q, :width] + bias_r)
            gate = jax.nn.sigmoid(pre[rows_q, width:] + bias_i)
            log_a = (-RATE_SCALE * vec_ref[1:2, :]) * recall
            a = jnp.exp(log_a)
            spaced = pl.ds(pl.multiple_of(s * pitch + q * ROWS, TILE), ROWS)
            put(a_ref, spaced, a)
            put(b_ref, spaced, jnp.sqrt(one_minus_square(log_a, a)) * gate * conv)

    per = seqs // (groups - groups // 2)

    @pl.loop(0, groups - groups // 2)
    def _(i):
        branch(groups // 2 + i)
        for j in range(per):
            gates(i * per + j, j % 2)

    stores[0].start(priority=1)
    stores[2].start(priority=1)

    def at_time(ref, t):
        return get(ref, pl.ds(t, seqs, stride=pitch))

    def step(t, value):
        prod, state = value
        a = at_time(a_ref, t)
        return prod * a, a * state + at_time(b_ref, t)

    ones = jnp.ones((seqs, width), F32)
    prod, state = lax.fori_loop(0, span, step, (ones, jnp.zeros_like(ones)), unroll=8)
    mine_ref[0] = prod
    mine_ref[1] = state
    sums_ref[me] = mine_ref[...]
    copies = to_all("seq", mine_ref, sums_ref, send1, recv1)
    for copy in copies:
        copy.start()

    @pl.loop(0, rows // ROWS, unroll=2)
    def _(q):
        at = block(q, ROWS)
        act_ref[at, :] = gelu(branch_ref[at, :])

    for copy in copies:
        copy.wait()

    def carry_step(j, carry):
        both = sums_ref[j]
        return jnp.where(j < me, both[0] * carry + both[1], carry)

    start = jnp.concatenate([state_ref[s : s + 1, :] * keep[s] for s in range(seqs)], axis=0)
    carry = lax.fori_loop(0, devices - 1, carry_step, start)
    carry_ref[...] = carry

    def final(t, state):
        state = at_time(a_ref, t) * state + at_time(b_ref, t)
        put(hidden_ref, pl.ds(t, seqs, stride=span), state)
        return state

    last = lax.fori_loop(0, span, final, carry, unroll=8)
    stores[3].start(priority=1)
    ends_ref[0:seqs, :] = jnp.where(me == devices - 1, last, 0.0)
    for s in range(seqs):
        ends_ref[(s + 1) * TILE : (s + 2) * TILE, :] = jnp.where(
            me == devices - 1, pad_ref[s, pl.ds(span, TILE), :], 0.0
        )

    @pl.loop(0, rows // ROWS, unroll=2)
    def _(q):
        at = block(q, ROWS)
        mixed_ref[at, :] = (get(hidden_ref, at) * act_ref[at, :]).astype(BF16)

    for copy in stores:
        copy.wait()
    for g in range(groups):
        normed_store(g).wait()


def backward_kernel(
    span,
    heads,
    block_part_in,
    own_in,
    low_in,
    w_out_in,
    branch_in,
    hidden_in,
    pre_in,
    pad_in,
    normed_in,
    mixed_in,
    rest_in,
    gates_in,
    w_branch_in,
    w_input_in,
    carry_ref,
    sums_ref,
    taps_ref,
    vec_ref,
    block_out,
    rec_out,
    grad_branch_out,
    input_out,
    first_out,
    acc_ref,
    blocks_ref,
    part,
    inbox,
    out,
    send_up,
    send_down,
    recv_up,
    recv_down,
    own_ref,
    resid_low,
    w_out_ref,
    branch_ref,
    hidden_ref,
    pre_ref,
    pad_ref,
    normed_ref,
    mixed_ref,
    a_ref,
    gd_ref,
    grad_ref,
    direct_ref,
    gpad_ref,
    heads_ref,
    low_ref,
    gates_grad,
    stage_ref,
    mine_ref,
    entries_ref,
    head_ref,
    head_in,
    load_sem,
    part_sem,
    store_sem,
    stage_sem,
    send1,
    recv1,
    send_t,
    recv_t,
    gates_ref,
    grad_branch_ref,
    input_ref,
    give_sem,
    late_sem,
):
    seqs, width = carry_ref.shape
    taps = taps_ref.shape[0]
    rows = seqs * span
    devices, me = lax.axis_size("seq"), lax.axis_index("seq")
    n, z = lax.axis_size("mp"), lax.axis_index("mp")
    chunks = rows // CHUNK
    size = GROUP * CHUNK
    held = part.shape[0] // size
    groups = chunks // GROUP
    sems = (send_up, send_down, recv_up, recv_down)
    local = pltpu.make_async_copy

    def part_load(g):
        slot = lax.rem(g, held)
        return local(block_part_in.at[block(g, size)], part.at[block(slot, size)], part_sem.at[slot])

    loads = [
        local(source, target, load_sem.at[i])
        for i, (source, target) in enumerate(
            (
                (own_in, own_ref),
                (low_in, resid_low),
                (w_out_in, w_out_ref),
                (pre_in, pre_ref),
                (branch_in, branch_ref),
                (hidden_in, hidden_ref),
                (pad_in, pad_ref),
                (mixed_in, mixed_ref),
                (normed_in, normed_ref),
                (gates_in, gates_ref),
            )
        )
    ]
    part_load(0).start()
    for copy in loads[:6]:
        copy.start(priority=1)
    for g in range(1, held):
        part_load(g).start()
    for copy in loads[6:]:
        copy.start(priority=1)
    acc_ref[...] = jnp.zeros_like(acc_ref)
    enter_all(("seq", "mp"))

    pitch = a_ref.shape[1] // seqs

    def spaced(s, q):
        return pl.ds(pl.multiple_of(s * pitch + q * ROWS, TILE), ROWS)

    def decay(at):
        recall = jax.nn.sigmoid(pre_ref[at, :width])
        log_a = (-RATE_SCALE * vec_ref[1:2, :]) * recall
        return recall, log_a, jnp.exp(log_a)

    def piece_direct(s):
        @pl.when(s == 0)
        def _():
            for copy in loads[1:6]:
                copy.wait()

        grad_ref[...] = matmul_back(resid_low[block(s, span), :], w_out_ref[...])

        @pl.loop(0, span // ROWS)
        def _(q):
            at = block(s * (span // ROWS) + q, ROWS)
            put(a_ref, spaced(s, q), decay(at)[2])
            act, slope = gelu_both(branch_ref[at, :])
            grad = grad_ref[block(q, ROWS), :]
            put(gd_ref, spaced(s, q), grad * act)
            grad_branch_ref[at, :] = (grad * get(hidden_ref, at) * slope).astype(BF16)

    def at_time(ref, t):
        return get(ref, pl.ds(t, seqs, stride=pitch))

    zero = jnp.zeros((seqs, width), F32)
    entry_copies = to_all("seq", mine_ref, entries_ref, send1, recv1)

    def piece_entry(_):
        def step(k, through):
            t = span - 1 - k
            return at_time(a_ref, t) * (at_time(gd_ref, t) + through)

        mine_ref[...] = lax.fori_loop(0, span, step, zero, unroll=8)
        entries_ref[me] = mine_ref[...]
        for copy in entry_copies:
            copy.start()

    def piece_state(_):
        for copy in entry_copies:
            copy.wait()

        def back_step(k, through):
            j = devices - 1 - k
            return jnp.where(j > me, entries_ref[j] + sums_ref[j, 0] * through, through)

        incoming = lax.fori_loop(0, devices - 1, back_step, zero)

        def final(k, through):
            t = span - 1 - k
            grad = at_time(gd_ref, t) + through
            put(gd_ref, pl.ds(t, seqs, stride=pitch), grad)
            return at_time(a_ref, t) * grad

        lax.fori_loop(0, span, final, incoming, unroll=8)

    def add(k, value):
        acc_ref[k] += fold(value)

    parts = 2

    def piece_gates(i):
        s = i // parts
        quarters = span // ROWS // parts

        @pl.when(i == 0)
        def _():
            loads[6].wait()
            loads[9].wait()

        @pl.loop(lax.rem(i, parts) * quarters, (lax.rem(i, parts) + 1) * quarters)
        def _(q):
            at = block(s * (span // ROWS) + q, ROWS)
            part_rows = pad_ref[s, pl.ds(pl.multiple_of(q * ROWS, ROWS), ROWS + TILE), :]
            conv = vec_ref[0:1, :]
            for k in range(taps):
                first = TILE - (taps - 1) + k
                conv = conv + taps_ref[k : k + 1, :] * part_rows[first : first + ROWS]
            heads_ref[at, :] = conv.astype(BF16)
            recall, log_a, a = decay(at)
            gate = jax.nn.sigmoid(pre_ref[at, width:])
            square = one_minus_square(log_a, a)
            inverse = lax.rsqrt(square)
            root = jnp.sqrt(square)
            grad = get(gd_ref, spaced(s, q))
            hidden = get(hidden_ref, at)
            before_at = pl.multiple_of(jnp.maximum(s * span + q * ROWS - TILE, 0), TILE)
            earlier = get(hidden_ref, pl.ds(before_at, TILE))
            first_row = jnp.where(q == 0, carry_ref[pl.ds(s, 1), :], earlier[TILE - 1 :])
            place = lax.broadcasted_iota(jnp.int32, (ROWS, width), 0)
            prev = jnp.where(place == 0, first_row, pltpu.roll(hidden, 1, 0))
            grad_log = grad * a * (prev - gate * conv * a * inverse)
            through = grad_log * recall
            pre_r = through * (1.0 - recall) * (-RATE_SCALE * vec_ref[1:2, :])
            direct = grad * root * gate
            pre_i = direct * conv * (1.0 - gate)
            low_ref[at, :width] = pre_r.astype(BF16)
            low_ref[at, width:] = pre_i.astype(BF16)
            direct_ref[block(q, ROWS), :] = direct
            add(0, through)
            add(1, pre_r)
            add(2, pre_i)

        @pl.when(lax.rem(i, parts) == parts - 1)
        def _():
            whole = direct_ref[...] + matmul_back(low_ref[block(s, span), :], gates_ref[...])
            gpad_ref[s, pl.ds(0, span), :] = whole
            head_ref[s] = whole[:TILE]

    head_copy = to_one("seq", -1, head_ref, head_in, send_t.at[0], recv_t.at[0])

    def piece_head(_):
        head_copy.start()

    def piece_taps(i):
        for j in range(2):
            taps_of(2 * i + j)

    def taps_of(s):
        @pl.loop(0, span // ROWS)
        def _(q):
            at = pl.multiple_of(q * ROWS, ROWS)
            part_rows = pad_ref[s, pl.ds(at, ROWS + TILE), :]
            grad = gpad_ref[s, pl.ds(at, ROWS), :]
            add(3, grad)
            for k in range(taps):
                first = TILE - (taps - 1) + k
                add(4 + k, grad * part_rows[first : first + ROWS])

    def piece_tail(_):
        head_copy.wait()
        for s in range(seqs):
            gpad_ref[s, pl.ds(span, TILE), :] = jnp.where(me == devices - 1, 0.0, head_in[s])

    def piece_input(i):
        for j in range(2):
            input_of(2 * i + j)

    def input_of(s):
        @pl.loop(0, span // ROWS)
        def _(q):
            part_rows = gpad_ref[s, pl.ds(pl.multiple_of(q * ROWS, ROWS), ROWS + TILE), :]
            total = taps_ref[taps - 1 : taps, :] * part_rows[0:ROWS]
            for k in range(taps - 1):
                first = taps - 1 - k
                total = total + taps_ref[k : k + 1, :] * part_rows[first : first + ROWS]
            input_ref[block(s * (span // ROWS) + q, ROWS), :] = total.astype(BF16)

    def contract(left, right):
        return lax.dot_general(left, right, CONTRACT_ROWS, preferred_element_type=F32)

    head = blocks_ref.shape[0]

    late_loads = [
        local(source.at[slice(i * rows, (i + 1) * rows)], target, late_sem.at[2 * j + i])
        for j, (source, targets) in enumerate(
            (
                (
                    w_branch_in,
                    (
                        resid_low.at[:, pl.ds(0, width)],
                        resid_low.at[:, pl.ds(width, width)],
                    ),
                ),
                (w_input_in, (resid_low.at[:, pl.ds(2 * width, width)], mixed_ref)),
            )
        )
        for i, target in enumerate(targets)
    ]
    first_copy = local(part.at[slice(size, 2 * size)], first_out, late_sem.at[4])

    def piece_projections(_):
        for copy in late_loads:
            copy.start(priority=1)

    def piece_first(i):
        branch_rows = grad_branch_ref[:size, :]
        input_rows = input_ref[:size, :]

        @pl.when(i == 0)
        def _():
            for copy in late_loads:
                copy.wait()

            part[size : 2 * size, :rows] = matmul_back(
                branch_rows, resid_low[:, :width]
            ) + matmul_back(input_rows, resid_low[:, 2 * width : 3 * width])

        @pl.when(i == 1)
        def _():
            part[size : 2 * size, rows:] = matmul_back(
                branch_rows, resid_low[:, width : 2 * width]
            ) + matmul_back(input_rows, mixed_ref[...])
            first_copy.start(priority=1)

    gives = [
        local(grad_branch_ref, grad_branch_out, give_sem.at[0]),
        local(input_ref, input_out, give_sem.at[1]),
    ]

    def piece_give(_):
        for copy in gives:
            copy.start(priority=1)

    def piece_gates_grad(i):
        @pl.when(i == 0)
        def _():
            gates_grad[...] = contract(heads_ref[...], low_ref[:, :width])

        @pl.when(i == 1)
        def _():
            gates_grad[...] = contract(heads_ref[...], low_ref[:, width:])

        place = lax.broadcasted_iota(jnp.int32, (head, width), 1)
        line = jnp.zeros((head, width), F32)
        for h in range(heads):
            row = gates_grad[h * head : (h + 1) * head, :]
            inside = jnp.logical_and(place >= h * head, place < (h + 1) * head)
            line = jnp.where(inside, row, line)

        for j in range(2):

            @pl.when(i == j)
            def _():
                blocks_ref[:, j * width : (j + 1) * width] = line

    tall = resid_low.shape[1] // WEIGHT_STEPS

    def stage_store(i):
        at = block(lax.rem(i, WEIGHT_STEPS), tall)
        slot = lax.rem(i, 2)
        return local(
            stage_ref.at[slot],
            rec_out.at[i // WEIGHT_STEPS, at, pl.ds(0, width)],
            stage_sem.at[slot],
        )

    def piece_weights(i):
        @pl.when(i == 0)
        def _():
            loads[7].wait()
            loads[8].wait()

        @pl.loop(2 * i, 2 * i + 2)
        def _(j):
            weight_of(j)

    def weight_of(i):
        @pl.when(i >= 2)
        def _():
            stage_store(i - 2).wait()

        at = block(lax.rem(i, WEIGHT_STEPS), tall)
        slot = lax.rem(i, 2)
        for which, (left, right) in enumerate(
            ((resid_low, mixed_ref), (normed_ref, grad_branch_ref), (normed_ref, input_ref))
        ):
            @pl.when(i // WEIGHT_STEPS == which)
            def _():
                stage_ref[slot] = contract(left[:, at], right[...])

        stage_store(i).start(priority=1)

    weights = 3 * WEIGHT_STEPS
    plan = []
    begin = 3
    early = WEIGHT_STEPS // 2

    def piece_weights_later(i):
        piece_weights(i + early)

    for work, times, gap in (
        (piece_direct, seqs, 0),
        (piece_entry, 1, 0),
        (piece_weights, early, 0),
        (piece_projections, 1, 4),
        (piece_state, 1, 0),
        (piece_gates, parts * seqs, 0),
        (piece_head, 1, 0),
        (piece_taps, seqs // 2, 0),
        (piece_gates_grad, 2, 3),
        (piece_tail, 1, 0),
        (piece_input, seqs // 2, 0),
        (piece_give, 1, 0),
        (piece_first, 2, 0),
        (piece_weights_later, weights // 2 - early, 0),
    ):
        plan.append((work, begin, times))
        begin += times + gap

    def run(step):
        for work, first, times in plan:
            @pl.when(jnp.logical_and(step >= first, step < first + times))
            def _():
                work(step - first)

    def before(k):
        @pl.when(k == SKEW * (n // 2))
        def _():
            loads[0].wait()

        @pl.when(jnp.logical_and(lax.rem(k, GROUP) == 0, k < chunks))
        def _():
            part_load(k // GROUP).wait()

        g = (k - out.shape[0]) // GROUP - 1 + held

        @pl.when(
            jnp.logical_and(
                jnp.logical_and(k >= out.shape[0] + GROUP, lax.rem(k - out.shape[0], GROUP) == 0),
                g < groups,
            )
        )
        def _():
            part_load(g).start(priority=1)

        run(k)

    def root(c, slot, total):
        out[slot] = own_ref[block(c // 2, CHUNK), :] + total

    def store(c, slot):
        return local(out.at[slot], block_out.at[block(c, CHUNK)], store_sem.at[slot])

    def arrive(c, slot):
        store(c, slot).start(priority=1)

    def leave(c, slot):
        store(c, slot).wait()

    line_sum(
        "mp", chunks, held * GROUP, part, inbox, out, sems, before, root, arrive, leave
    )

    @pl.loop(chunks + out.shape[0], max(begin, chunks + out.shape[0]))
    def _(k):
        run(k)

    for copy in gives:
        copy.wait()
    first_copy.wait()
    stage_store(weights - 2).wait()
    stage_store(weights - 1).wait()


def backward_call(span, heads, head, *args):
    block_part = args[0]
    low, w_out, branch, hidden, pre, padded, normed, mixed, rest, gates = args[2:12]
    carry, sums, taps = args[14:17]
    rows, model = block_part.shape
    seqs, width = carry.shape
    devices = lax.axis_size("seq")
    ring = ring_size("mp")
    held = 3 * GROUP * CHUNK
    dma = pltpu.SemaphoreType.DMA
    columns = pltpu.VMEM((width // LANES, seqs * (span + TILE), LANES), F32)
    return pl.pallas_call(
        functools.partial(backward_kernel, span, heads),
        out_shape=(
            shape((rows, model)),
            shape(rest.shape),
            shape((rows, width), BF16),
            shape((rows, width), BF16),
            shape((GROUP * CHUNK, model)),
            shape((4 + taps.shape[0], TILE, width)),
            shape((head, 2 * width)),
        ),
        in_specs=[HBM] * 14 + [VMEM] * 4,
        input_output_aliases={10: 1},
        out_specs=(HBM,) * 5 + (VMEM,) * 2,
        scratch_shapes=line_scratch("mp", held, model)
        + [
            pltpu.VMEM((rows // 2, model), F32),
            pltpu.VMEM((rows, model), BF16),
            pltpu.VMEM((width, model), BF16),
            pltpu.VMEM((rows, width), F32),
            pltpu.VMEM(hidden.shape, F32),
            pltpu.VMEM(pre.shape, F32),
            pltpu.VMEM(padded.shape, F32),
            pltpu.VMEM((rows, model), BF16),
            pltpu.VMEM((rows, width), BF16),
            columns,
            columns,
            pltpu.VMEM((span, width), F32),
            pltpu.VMEM((span, width), F32),
            pltpu.VMEM((seqs, span + TILE, width), F32),
            pltpu.VMEM((rows, width), BF16),
            pltpu.VMEM((rows, 2 * width), BF16),
            pltpu.VMEM((width, width), F32),
            pltpu.VMEM((2, model // WEIGHT_STEPS, width), F32),
            pltpu.VMEM((seqs, width), F32),
            pltpu.VMEM((devices, seqs, width), F32),
            pltpu.VMEM((seqs, TILE, width), F32),
            pltpu.VMEM((seqs, TILE, width), F32),
            dma((10,)),
            dma((3,)),
            dma((ring,)),
            dma((2,)),
            dma((devices - 1,)),
            dma((devices - 1,)),
            dma((1,)),
            dma((1,)),
            pltpu.VMEM(gates.shape, BF16),
            pltpu.VMEM((rows, width), BF16),
            pltpu.VMEM((rows, width), BF16),
            dma((2,)),
            dma((5,)),
        ],
        compiler_params=params(1, 63),
        cost_estimate=cost(200),
        name="backward",
    )(*args)


def line_sum(axis, total, period, part, inbox, out, sems, before, root, arrive, leave):
    send_up, send_down, recv_up, recv_down = sems
    parts = send_up.shape[0]
    columns = out.shape[2] // parts
    n, z = lax.axis_size(axis), lax.axis_index(axis)
    depth = n // 2
    ring = out.shape[0]

    def cols(p):
        return pl.ds(p * columns, columns)

    def root_of(c):
        return depth - 1 + lax.rem(c, 2)

    def up(c, step, side, p):
        slot = lax.rem(c, ring)
        return pltpu.make_async_remote_copy(
            src_ref=part.at[block(lax.rem(c, period), CHUNK), cols(p)],
            dst_ref=inbox.at[side, slot, :, cols(p)],
            send_sem=send_up.at[p, slot],
            recv_sem=recv_up.at[p, side, slot],
            device_id={axis: z + step},
            device_id_type=MESH,
        )

    def down(c, step, side, p):
        slot = lax.rem(c, ring)
        return pltpu.make_async_remote_copy(
            src_ref=out.at[slot, :, cols(p)],
            dst_ref=out.at[slot, :, cols(p)],
            send_sem=send_down.at[p, side, slot],
            recv_sem=recv_down.at[p, slot],
            device_id={axis: z + step},
            device_id_type=MESH,
        )

    inner = jnp.logical_and(z > 0, z < n - 1)

    @pl.loop(0, total + ring)
    def _(k):
        @pl.when(k >= ring)
        def _():
            c = k - ring
            r = root_of(c)
            step = jnp.where(z < r, 1, -1)
            side = jnp.where(z < r, 0, 1)

            @pl.when(z == r)
            def _():
                for p in range(parts):
                    down(c, -1, 0, p).wait_send()
                    down(c, 1, 1, p).wait_send()

            @pl.when(z != r)
            def _():
                for p in range(parts):
                    up(c, step, side, p).wait_send()

            @pl.when(jnp.logical_and(z != r, inner))
            def _():
                for p in range(parts):
                    down(c, -step, side, p).wait_send()

            leave(c, lax.rem(c, ring))

        before(k)

        for i in reversed(range(n + 1)):
            c = k - SKEW * i
            valid = jnp.logical_and(c >= 0, c < total)
            c = jnp.clip(c, 0, total - 1)
            at = block(lax.rem(c, period), CHUNK)
            slot = lax.rem(c, ring)
            r = root_of(c)
            step = jnp.where(z < r, 1, -1)
            side = jnp.where(z < r, 0, 1)
            if i > depth:
                here = jnp.logical_and(z != r, jnp.abs(z - r) == i - depth)

                @pl.when(jnp.logical_and(valid, here))
                def _():
                    for p in range(parts):
                        down(c, step, side, p).wait_recv()

                        @pl.when(inner)
                        def _():
                            down(c, -step, side, p).start()

                    arrive(c, slot)
            elif i == depth:

                @pl.when(jnp.logical_and(valid, z == r))
                def _():
                    for p in range(parts):
                        up(c, 1, 0, p).wait_recv()
                        up(c, -1, 1, p).wait_recv()
                    root(c, slot, part[at, :] + inbox[0, slot] + inbox[1, slot])
                    for p in range(parts):
                        down(c, -1, 0, p).start()
                        down(c, 1, 1, p).start()
                    arrive(c, slot)
            else:
                here = jnp.where(z < r, z, n - 1 - z) == i

                @pl.when(jnp.logical_and(valid, jnp.logical_and(z != r, here)))
                def _():
                    for p in range(parts):
                        if i > 0:
                            up(c, step, side, p).wait_recv()
                            part[at, cols(p)] += inbox[side, slot, :, cols(p)]
                        up(c, step, side, p).start()


def ring_size(axis):
    return SKEW * lax.axis_size(axis) + 4


def line_scratch(axis, rows, model, parts=2):
    dma = pltpu.SemaphoreType.DMA
    ring = ring_size(axis)
    return [
        pltpu.VMEM((rows, model), F32),
        pltpu.VMEM((2, ring, CHUNK, model), F32),
        pltpu.VMEM((ring, CHUNK, model), F32),
        dma((parts, ring)),
        dma((parts, 2, ring)),
        dma((parts, 2, ring)),
        dma((parts, ring)),
    ]


def mean_square(x):
    return lax.rsqrt(jnp.mean(x * x, axis=-1, keepdims=True) + EPS)


def nothing(*_):
    pass


def fold(value):
    total = value[0:TILE]
    for i in range(1, value.shape[0] // TILE):
        total = total + value[i * TILE : (i + 1) * TILE]
    return total


def norm_grad(value, gain, grad, acc_ref):
    q = mean_square(value)
    e = gain * grad
    acc_ref[...] += fold(grad * value * q)
    return q * e - value * (q * q * q) * jnp.mean(e * value, axis=-1, keepdims=True)


def middle_kernel(
    mixed_in,
    w_out_in,
    x_in,
    og_in,
    gain_ref,
    w_gate_in,
    w_up_in,
    w_down_in,
    normed_out,
    hidden_out,
    gate_out,
    up_out,
    glow_out,
    block_out,
    low_out,
    own_grad_out,
    weight_out,
    rest_out,
    own_out,
    acc_ref,
    part,
    inbox,
    out,
    send_up,
    send_down,
    recv_up,
    recv_down,
    mixed,
    w_out,
    w_gate,
    w_up,
    w_down,
    normed,
    rows_ref,
    og_ref,
    glow,
    gate_val,
    up_val,
    grad_hidden,
    hidden,
    grad_gate,
    grad_up,
    block_part,
    low,
    weight_sem,
    row_sem,
    og_sem,
    act_sem,
    low_sem,
    own_sem,
    again_sem,
    stage_sem,
    rest_sem,
    own_ref,
):
    n, z = lax.axis_size("mp"), lax.axis_index("mp")
    count = part.shape[0] // CHUNK
    size = GROUP * CHUNK
    groups = count // GROUP
    ring = out.shape[0]
    sems = (send_up, send_down, recv_up, recv_down)
    local = pltpu.make_async_copy

    loads = [
        local(source, target, weight_sem.at[i])
        for i, (source, target) in enumerate(
            (
                (mixed_in, mixed),
                (w_out_in, w_out),
                (w_gate_in, w_gate),
                (w_up_in, w_up),
                (w_down_in, w_down.at[slice(0, w_down_in.shape[0])]),
            )
        )
    ]
    for copy in loads:
        copy.start(priority=1)
    deep = w_down_in.shape[0]

    def og_load(g):
        return local(og_in.at[block(g, size)], og_ref, og_sem.at[0])

    og_load(0).start(priority=1)
    enter_all(("mp",))
    acc_ref[...] = jnp.zeros_like(acc_ref)
    loads[0].wait()
    loads[1].wait()

    def is_root(c):
        return z == n // 2 - 1 + lax.rem(c, 2)

    def row_load(source, c):
        slot = lax.rem(c, ring)
        at = block(lax.rem(c, count), CHUNK)
        return local(source.at[at], rows_ref.at[slot], row_sem.at[slot])

    acts = (
        (normed, normed_out),
        (glow, glow_out),
        (hidden, hidden_out),
        (grad_gate, gate_out),
        (grad_up, up_out),
        (block_part, block_out),
    )

    def act_store(i, g):
        source, target = acts[i]
        source = source.at[lax.rem(g, 2)] if i == 0 else source
        return local(source, target.at[block(g, size)], act_sem.at[i])

    def at_tick(k, first, work):
        g = (k - first) // GROUP

        @pl.when(
            jnp.logical_and(
                jnp.logical_and(k >= first, k < first + GROUP * groups),
                lax.rem(k - first, GROUP) == 0,
            )
        )
        def _():
            work(g)

    def project(g):
        part[block(g, size), :] = dot(mixed[block(g, size), :], w_out[...])

    def piece_gate(g):
        @pl.when(g == 0)
        def _():
            for copy in loads[2:]:
                copy.wait()

        def work(cols):
            gate_val[:, cols] = dot(normed[lax.rem(g, 2)], w_gate[:, cols])

        work(slice(None))
        act_store(0, g).start(priority=1)

    def piece_up(g):
        def work(cols):
            up_val[:, cols] = dot(normed[lax.rem(g, 2)], w_up[:, cols])

        work(slice(None))

        @pl.when(g > 0)
        def _():
            for i in range(1, 6):
                act_store(i, g - 1).wait()

    def piece_low(g):
        og_load(g).wait()

        @pl.loop(0, size // ROWS)
        def _(q):
            glow[block(q, ROWS), :] = og_ref[block(q, ROWS), :].astype(BF16)

        @pl.when(g + 1 < groups)
        def _():
            og_load(g + 1).start(priority=1)

        act_store(1, g).start(priority=1)
        act_store(0, g).wait()

    def piece_hidden(g):
        def work(cols):
            grad_hidden[...] = matmul_back(glow[...], w_down[:deep, :])

        work(slice(None))

    def piece_act(g):
        @pl.loop(0, size // CHUNK)
        def _(q):
            at = block(q, CHUNK)
            up = up_val[at, :]
            grad = grad_hidden[at, :]
            act, slope = gelu_both(gate_val[at, :])
            hidden[at, :] = (act * up).astype(BF16)
            grad_gate[at, :] = (grad * up * slope).astype(BF16)
            grad_up[at, :] = (grad * act).astype(BF16)

        for i in range(2, 5):
            act_store(i, g).start(priority=1)

    def piece_down(g):
        def work(cols):
            block_part[:, cols] = dot(hidden[...], w_down[:deep, cols])

        work(slice(None))
        act_store(5, g).start(priority=1)

    def piece_back_gate(g):
        def work(cols):
            part[block(g, size), cols] = matmul_back(grad_gate[...], w_gate[cols, :])

        work(slice(None))

    def piece_back_up(g):
        def work(cols):
            part[block(g, size), cols] += matmul_back(grad_up[...], w_up[cols, :])

        work(slice(None))

    tokens = count * CHUNK
    half = tokens // 2
    quarter = half // 2
    again = [
        local(source, target, again_sem.at[i])
        for i, (source, target) in enumerate(
            (
                (normed_out, w_down.at[slice(0, tokens)]),
                (gate_out, w_gate.at[slice(0, tokens)]),
                (up_out, w_up.at[slice(0, tokens)]),
                (hidden_out, w_gate.at[slice(tokens, 2 * tokens)]),
                (glow_out.at[slice(0, half)], w_down.at[slice(tokens, tokens + half)]),
                (glow_out.at[slice(half, half + quarter)], normed.at[0]),
                (glow_out.at[slice(half + quarter, tokens)], normed.at[1]),
            )
        )
    ]
    tall = w_gate.shape[0] // WEIGHT_STEPS
    stages = (gate_val, up_val, grad_hidden)

    kept = weight_out.shape[2]
    before_rest = rest_out.shape[2] - (deep - kept)

    def stage_stores(which, i):
        at = block(i, tall)
        return (
            local(
                stages[which].at[:, pl.ds(0, kept)],
                weight_out.at[which, at],
                stage_sem.at[which],
            ),
            local(
                stages[which].at[:, pl.ds(kept, deep - kept)],
                rest_out.at[which, at, pl.ds(before_rest, deep - kept)],
                rest_sem.at[which],
            ),
        )

    own_copy = local(own_ref, own_out, rest_sem.at[3])

    def piece_reload():
        own_copy.start(priority=1)
        for i in range(1, 6):
            act_store(i, groups - 1).wait()
        for copy in again:
            copy.start(priority=1)

    def piece_ready():
        for copy in again:
            copy.wait()

    def contract(left, right):
        return lax.dot_general(left, right, CONTRACT_ROWS, preferred_element_type=F32)

    def piece_weight(step):
        i = step // 3
        at = block(i, tall)
        for which in range(3):

            @pl.when(lax.rem(step, 3) == which)
            def _():
                @pl.when(i > 0)
                def _():
                    for copy in stage_stores(which, i - 1):
                        copy.wait()

                stage = stages[which]

                def work(cols):
                    if which == 0:
                        stage[:, cols] = contract(w_down[:tokens, at], w_gate[:tokens, cols])
                    elif which == 1:
                        stage[:, cols] = contract(w_down[:tokens, at], w_up[:tokens, cols])
                    else:
                        middle = tokens + half + quarter
                        stage[:, cols] = (
                            contract(
                                w_down[tokens : tokens + half, at],
                                w_gate[tokens : tokens + half, cols],
                            )
                            + contract(normed[0, :, at], w_gate[tokens + half : middle, cols])
                            + contract(normed[1, :, at], w_gate[middle : 2 * tokens, cols])
                        )

                work(slice(None))
                for copy in stage_stores(which, i):
                    copy.start(priority=1)

    first = GROUP + SKEW * n
    spare = GROUP * groups + ring + 3
    first_weight = spare + 3
    weights = 3 * WEIGHT_STEPS

    def before(k):
        @pl.when(k == spare)
        def _():
            piece_reload()

        @pl.when(k == first_weight - 1)
        def _():
            piece_ready()

        @pl.when(jnp.logical_and(k >= first_weight, k < first_weight + weights))
        def _():
            piece_weight(k - first_weight)

        @pl.when(jnp.logical_and(k < count, is_root(k)))
        def _():
            row_load(x_in, k).start(priority=1)

        @pl.when(
            jnp.logical_and(jnp.logical_and(k >= count, k < 2 * count), is_root(k))
        )
        def _():
            row_load(og_in, k).start(priority=1)

        @pl.when(k == 0)
        def _():
            project(0)

        @pl.when(jnp.logical_and(lax.rem(k, GROUP) == GROUP // 2, k < (groups - 1) * GROUP))
        def _():
            project(k // GROUP + 1)

        at_tick(k, first, piece_gate)
        at_tick(k, first + 1, piece_up)
        at_tick(k, first + 2, piece_low)
        at_tick(k, first + 3, piece_hidden)
        at_tick(k, first + 4, piece_act)
        at_tick(k, first + 6, piece_down)
        at_tick(k, GROUP + ring, piece_back_gate)
        at_tick(k, GROUP + ring + 2, piece_back_up)

    def root(c, slot, total):
        j = lax.rem(c, count)
        mine = block(j // 2, CHUNK)
        row_load(x_in, c).wait()

        @pl.when(c < count)
        def _():
            value = rows_ref[slot] + total
            own_ref[mine, :] = value
            out[slot] = (value * mean_square(value) * gain_ref[...]).astype(BF16).astype(F32)

        @pl.when(c >= count)
        def _():
            back = norm_grad(own_ref[mine, :], gain_ref[...], total, acc_ref)
            out[slot] = rows_ref[slot] + back

    def low_store(c, slot):
        at = block(lax.rem(c, count), CHUNK)
        return local(low.at[slot], low_out.at[at], low_sem.at[slot])

    def own_store(c, slot):
        at = block(lax.rem(c, count) // 2, CHUNK)
        return local(out.at[slot], own_grad_out.at[at], own_sem.at[slot])

    def arrive(c, slot):
        @pl.when(c < count)
        def _():
            normed[lax.rem(c // GROUP, 2), block(lax.rem(c, GROUP), CHUNK), :] = out[slot].astype(BF16)

        @pl.when(c >= count)
        def _():
            low[slot] = out[slot].astype(BF16)
            low_store(c, slot).start(priority=1)

            @pl.when(is_root(c))
            def _():
                own_store(c, slot).start(priority=1)

    def leave(c, slot):
        @pl.when(c >= count)
        def _():
            low_store(c, slot).wait()

            @pl.when(is_root(c))
            def _():
                own_store(c, slot).wait()

    line_sum("mp", 2 * count, count, part, inbox, out, sems, before, root, arrive, leave)

    own_copy.wait()
    for which in range(3):
        for copy in stage_stores(which, WEIGHT_STEPS - 1):
            copy.wait()


def middle_call(*args):
    mixed, w_out, x, og, gain, w_gate, w_up, w_down = args
    rows, model = x.shape
    width, hidden = mixed.shape[1], w_gate.shape[1]
    size = GROUP * CHUNK
    dma = pltpu.SemaphoreType.DMA
    ring = ring_size("mp")
    act = shape((rows, hidden), BF16)
    tall = shape((rows, model), BF16)
    return pl.pallas_call(
        middle_kernel,
        out_shape=(
            tall,
            act,
            act,
            act,
            tall,
            shape((rows, model)),
            tall,
            shape((rows // 2, model)),
            shape((3, model, hidden - hidden // LATER)),
            shape((3, model, width + hidden // LATER)),
            shape((rows // 2, model)),
            shape((TILE, model)),
        ),
        in_specs=[HBM] * 4 + [VMEM] + [HBM] * 3,
        out_specs=(HBM,) * 11 + (VMEM,),
        scratch_shapes=line_scratch("mp", rows, model)
        + [
            pltpu.VMEM((rows, width), BF16),
            pltpu.VMEM((width, model), BF16),
            pltpu.VMEM((model, hidden), BF16),
            pltpu.VMEM((model, hidden), BF16),
            pltpu.VMEM((max(hidden, rows * 3 // 2), model), BF16),
            pltpu.VMEM((2, size, model), BF16),
            pltpu.VMEM((ring, CHUNK, model), F32),
            pltpu.VMEM((size, model), F32),
            pltpu.VMEM((size, model), BF16),
            pltpu.VMEM((size, hidden), F32),
            pltpu.VMEM((size, hidden), F32),
            pltpu.VMEM((size, hidden), F32),
            pltpu.VMEM((size, hidden), BF16),
            pltpu.VMEM((size, hidden), BF16),
            pltpu.VMEM((size, hidden), BF16),
            pltpu.VMEM((size, model), F32),
            pltpu.VMEM((ring, CHUNK, model), BF16),
            dma((5,)),
            dma((ring,)),
            dma((1,)),
            dma((6,)),
            dma((ring,)),
            dma((ring,)),
            dma((7,)),
            dma((3,)),
            dma((4,)),
            pltpu.VMEM((rows // 2, model), F32),
        ],
        compiler_params=params(2, 63),
        cost_estimate=cost(400),
        name="middle",
    )(*args)


def last_kernel(
    first_in,
    own_grad_in,
    x_in,
    grad_branch_in,
    input_in,
    w_branch_in,
    w_input_in,
    gain_ref,
    other_acc,
    sums_in,
    ends_in,
    blocks_in,
    grad_out,
    norm_ref,
    small_out,
    part,
    inbox,
    out,
    send_up,
    send_down,
    recv_up,
    recv_down,
    own_grad_ref,
    x_ref,
    grad_branch,
    input_low,
    w_branch,
    w_input,
    load_sem,
    store_sem,
    acc_ref,
    mine_ref,
    seq_in,
    mp_in,
    send_s,
    recv_s,
    send_m,
    recv_m,
    small,
    small_in,
    send_v,
    recv_v,
):
    count = part.shape[0] // CHUNK
    size = GROUP * CHUNK
    sems = (send_up, send_down, recv_up, recv_down)
    local = pltpu.make_async_copy

    loads = [
        local(source, target, load_sem.at[i])
        for i, (source, target) in enumerate(
            (
                (grad_branch_in, grad_branch),
                (w_branch_in, w_branch),
                (input_in, input_low),
                (w_input_in, w_input),
                (own_grad_in, own_grad_ref),
                (x_in, x_ref),
            )
        )
    ]
    first_load = local(first_in, part.at[slice(0, size)], load_sem.at[6])
    first_load.start()
    for copy in loads:
        copy.start(priority=1)
    acc_ref[...] = jnp.zeros_like(acc_ref)
    norm_ref[...] = jnp.zeros_like(norm_ref)
    enter_all(("seq", "mp"))
    first_load.wait()

    kinds = sums_in.shape[0]
    me = lax.axis_index("seq")
    width = sums_in.shape[2]
    height = kinds + ends_in.shape[0]
    head = blocks_in.shape[0]
    levels = small_in.shape[0]

    def exchange(level):
        bit = 1 << level
        partner = me + bit - 2 * bit * lax.rem(me // bit, 2)
        return pltpu.make_async_remote_copy(
            src_ref=small.at[level],
            dst_ref=small_in.at[level],
            send_sem=send_v.at[level],
            recv_sem=recv_v.at[level],
            device_id={"seq": partner},
            device_id_type=MESH,
        )

    spacing = (count - 4) // (levels + 1)
    plane = lax.axis_index("mp")

    def norm_sum(i, k, first, gaps, source):
        seq_copies = to_all("seq", mine_ref.at[i, 0], seq_in.at[i], send_s.at[i], recv_s.at[i])
        mp_copies = to_all("mp", mine_ref.at[i, 1], mp_in.at[i], send_m.at[i], recv_m.at[i])

        @pl.when(k == first)
        def _():
            mine_ref[i, 0] = jnp.sum(source[...], axis=0, keepdims=True)
            seq_in[i, me] = mine_ref[i, 0]
            for copy in seq_copies:
                copy.start()

        @pl.when(k == first + gaps[0])
        def _():
            for copy in seq_copies:
                copy.wait()
            mine_ref[i, 1] = jnp.sum(seq_in[i], axis=0)
            mp_in[i, plane] = mine_ref[i, 1]
            for copy in mp_copies:
                copy.start()

        @pl.when(k == first + gaps[0] + gaps[1])
        def _():
            for copy in mp_copies:
                copy.wait()
            norm_ref[i : i + 1, :] = jnp.sum(mp_in[i], axis=0)

    settled = count + SKEW * (lax.axis_size("mp") // 2)

    def before(k):
        @pl.when(k == 2)
        def _():
            for i in range(kinds):
                small[0, i : i + 1, :] = jnp.sum(sums_in[i], axis=0, keepdims=True)
            small[0, kinds:height, :] = ends_in[...]
            small[0, height : height + head, :] = blocks_in[:, :width]
            small[0, height + head :, :] = blocks_in[:, width:]

        for level in range(levels + 1):

            @pl.when(k == 3 + level * spacing)
            def _():
                if level > 0:
                    exchange(level - 1).wait()
                    total = small[level - 1] + small_in[level - 1]
                    if level < levels:
                        small[level] = total
                    else:
                        small_out[...] = total
                if level < levels:
                    exchange(level).start()

        norm_sum(0, k, settled, (2, 3), acc_ref)
        norm_sum(1, k, 10, (20, 20), other_acc)

        @pl.when(k == 4)
        def _():
            for copy in loads[:4]:
                copy.wait()

        @pl.when(
            jnp.logical_and(
                lax.rem(k, 4) == 0, jnp.logical_and(k > 0, k // 4 < count // GROUP)
            )
        )
        def _():
            at = block(k // 4, size)

            def work(cols):
                part[at, cols] = matmul_back(grad_branch[at, :], w_branch[cols, :]) + matmul_back(
                    input_low[at, :], w_input[cols, :]
                )

            work(slice(None))

        @pl.when(k == SKEW * (lax.axis_size("mp") // 2))
        def _():
            for copy in loads[4:]:
                copy.wait()

    def root(c, slot, total):
        back = norm_grad(x_ref[block(c, CHUNK), :], gain_ref[...], total, acc_ref)
        out[slot] = own_grad_ref[block(c // 2, CHUNK), :] + back

    def store(c, slot):
        return local(out.at[slot], grad_out.at[block(c, CHUNK)], store_sem.at[slot])

    def arrive(c, slot):
        store(c, slot).start(priority=1)

    def leave(c, slot):
        store(c, slot).wait()

    line_sum("mp", count, count, part, inbox, out, sems, before, root, arrive, leave)


def enter_all(axes):
    barrier = pltpu.get_barrier_semaphore()
    count = 0
    for axis in axes:
        size, me = lax.axis_size(axis), lax.axis_index(axis)
        for d in range(1, size):
            pl.semaphore_signal(
                barrier, 1, device_id={axis: lax.rem(me + d, size)}, device_id_type=MESH
            )
        count += size - 1
    pl.semaphore_wait(barrier, count)


def cost(micros):
    return pl.CostEstimate(flops=int(micros * 1e9), bytes_accessed=1 << 20, transcendentals=0)


def nseq_levels():
    return (lax.axis_size("seq") - 1).bit_length()


def last_call(*args):
    x, grad_branch = args[2:4]
    rows, model = x.shape
    width = grad_branch.shape[1]
    lines = args[9].shape[0] + args[10].shape[0] + 2 * args[11].shape[0]
    levels = nseq_levels()
    dma = pltpu.SemaphoreType.DMA
    nseq, nmp = lax.axis_size("seq"), lax.axis_size("mp")
    return pl.pallas_call(
        last_kernel,
        out_shape=(shape((rows, model)), shape((TILE, model)), shape((lines, width))),
        in_specs=[HBM] * 7 + [VMEM] * 5,
        out_specs=(HBM,) + (VMEM,) * 2,
        scratch_shapes=line_scratch("mp", rows, model)
        + [
            pltpu.VMEM((rows // 2, model), F32),
            pltpu.VMEM((rows, model), F32),
            pltpu.VMEM((rows, width), BF16),
            pltpu.VMEM((rows, width), BF16),
            pltpu.VMEM((model, width), BF16),
            pltpu.VMEM((model, width), BF16),
            dma((7,)),
            dma((ring_size("mp"),)),
            pltpu.VMEM((TILE, model), F32),
            pltpu.VMEM((2, 2, 1, model), F32),
            pltpu.VMEM((2, nseq, 1, model), F32),
            pltpu.VMEM((2, nmp, 1, model), F32),
            dma((2, nseq - 1)),
            dma((2, nseq - 1)),
            dma((2, nmp - 1)),
            dma((2, nmp - 1)),
            pltpu.VMEM((levels, lines, width), F32),
            pltpu.VMEM((levels, lines, width), F32),
            dma((levels,)),
            dma((levels,)),
        ],
        compiler_params=params(4, 62),
        cost_estimate=cost(200),
        name="last_sums",
    )(*args)


def finish_kernel(
    heads,
    block_in,
    grad_in,
    mlp_in,
    rec_in,
    small_hbm,
    norm_hbm,
    decay_hbm,
    block_out,
    grad_out,
    w_gate_out,
    w_up_out,
    w_branch_out,
    w_input_out,
    w_down_out,
    w_out_out,
    gate_r_out,
    gate_i_out,
    taps_out,
    conv_bias_out,
    bias_r_out,
    bias_i_out,
    decay_out,
    norm_in_out,
    norm_mlp_out,
    state_out,
    conv_out,
    tall,
    mlp,
    rec,
    small_in,
    norm_in,
    raw_ref,
    load_sem,
    store_sem,
    extra_sem,
):
    local = pltpu.make_async_copy
    width = small_in.shape[1]
    kept = mlp.shape[2]
    late = rec.shape[2] - width
    size = grad_in.shape[0] // COPIES
    extra = [
        local(source, target, extra_sem.at[i])
        for i, (source, target) in enumerate(
            ((small_hbm, small_in), (norm_hbm, norm_in), (decay_hbm, raw_ref))
        )
    ]
    for copy in extra:
        copy.start()
    jobs = [(mlp_in, mlp, None), (rec_in, rec, None)]
    for j, (source, target) in enumerate(((block_in, block_out), (grad_in, grad_out))):
        for i in range(COPIES):
            at = slice(i * size, (i + 1) * size)
            jobs.append((source.at[at], tall.at[j, at], target.at[at]))
    loads = [local(source, held, load_sem.at[i]) for i, (source, held, _) in enumerate(jobs)]
    stores = [
        local(held, target, store_sem.at[i])
        for i, (held, target) in enumerate(
            [(held, target) for _, held, target in jobs[2:]]
            + [
                (mlp.at[0], w_gate_out.at[:, pl.ds(0, kept)]),
                (mlp.at[1], w_up_out.at[:, pl.ds(0, kept)]),
                (rec.at[0, :, pl.ds(width, late)], w_gate_out.at[:, pl.ds(kept, late)]),
                (rec.at[1, :, pl.ds(width, late)], w_up_out.at[:, pl.ds(kept, late)]),
                (rec.at[1, :, pl.ds(0, width)], w_branch_out),
                (rec.at[2, :, pl.ds(0, width)], w_input_out),
            ]
        )
    ]
    for copy in loads:
        copy.start()
    for copy in extra:
        copy.wait()
    taps, seqs, edge = taps_out.shape[0], state_out.shape[0], conv_out.shape[0]
    head = gate_r_out.shape[1]
    decay = small_in[0:1, :].reshape(width) * (RATE_SCALE * jax.nn.sigmoid(-raw_ref[...]))
    decay_out[...] = decay
    bias_r_out[...] = small_in[1:2, :].reshape(width)
    bias_i_out[...] = small_in[2:3, :].reshape(width)
    conv_bias_out[...] = small_in[3:4, :].reshape(width)
    taps_out[...] = small_in[4 : 4 + taps, :]
    begin = 4 + taps
    state_out[...] = small_in[begin : begin + seqs, :]
    for s in range(seqs):
        end = begin + seqs + (s + 1) * TILE
        for k in range(edge):
            conv_out[k, s : s + 1, :] = small_in[end - edge + k : end - edge + k + 1, :]
    begin += seqs + seqs * TILE
    for i, target in enumerate((gate_r_out, gate_i_out)):
        line = small_in[begin + i * head : begin + (i + 1) * head, :]
        for h in range(heads):
            turned = line if h == 0 else pltpu.roll(line, width - h * head, 1)
            target[h] = turned[:, :head]
    norm_in_out[...] = norm_in[0:1, :].reshape(norm_in.shape[1])
    norm_mlp_out[...] = norm_in[1:2, :].reshape(norm_in.shape[1])
    loads[0].wait()
    loads[1].wait()
    for copy in stores[2 * COPIES :]:
        copy.start(priority=1)
    w_down_out[:kept, :] = mlp[2].T
    w_down_out[kept:, :] = rec[2, :, width:].T
    w_out_out[...] = rec[0, :, :width].T
    for i in range(2 * COPIES):
        loads[2 + i].wait()
        stores[i].start(priority=1)
    for copy in stores:
        copy.wait()


def finish_call(seqs, heads, head, edge, *args):
    _, stream_grad, mlp_grads, rec_grads, small, norms, decay = args
    rows, model = stream_grad.shape
    own, kept = mlp_grads.shape[1:]
    width = small.shape[1]
    hidden = kept + rec_grads.shape[2] - width
    taps = edge + 1
    line = shape((width,))
    tall = shape((rows, model))
    return pl.pallas_call(
        functools.partial(finish_kernel, heads),
        out_shape=(
            tall,
            tall,
            shape((own, hidden)),
            shape((own, hidden)),
            shape((own, width)),
            shape((own, width)),
            shape((hidden, own)),
            shape((width, own)),
            shape((heads, head, head)),
            shape((heads, head, head)),
            shape((taps, width)),
            line,
            line,
            line,
            line,
            shape((model,)),
            shape((model,)),
            shape((seqs, width)),
            shape((edge, seqs, width)),
        ),
        in_specs=[HBM] * 4 + [PINNED] * 3,
        out_specs=(HBM,) * 6 + (VMEM,) * 13,
        scratch_shapes=[
            pltpu.VMEM((2, rows, model), F32),
            pltpu.VMEM(mlp_grads.shape, F32),
            pltpu.VMEM(rec_grads.shape, F32),
            pltpu.VMEM(small.shape, F32),
            pltpu.VMEM(norms.shape, F32),
            pltpu.VMEM(decay.shape, F32),
            pltpu.SemaphoreType.DMA((2 + 2 * COPIES,)),
            pltpu.SemaphoreType.DMA((6 + 2 * COPIES,)),
            pltpu.SemaphoreType.DMA((3,)),
        ],
        compiler_params=pltpu.CompilerParams(vmem_limit_bytes=63 << 20),
        cost_estimate=cost(15),
        name="finish",
    )(*args)


def params(collective, megabytes=60):
    return pltpu.CompilerParams(
        collective_id=collective, has_side_effects=True, vmem_limit_bytes=megabytes << 20
    )


def shape(dims, dtype=F32):
    return jax.ShapeDtypeStruct(dims, dtype)


def recurrence_forward(span, *args):
    x, w_input = args[:2]
    rows, model = x.shape
    seqs, width = rows // span, w_input.shape[1]
    devices = lax.axis_size("seq")
    dma = pltpu.SemaphoreType.DMA
    groups = seqs // 2
    columns = (width // LANES, rows, LANES)
    spaced = (width // LANES, seqs * (span + TILE), LANES)
    padded = (seqs, span + TILE, width)
    return pl.pallas_call(
        functools.partial(forward_kernel, span),
        out_shape=(
            shape((rows, model), BF16),
            shape((rows, width)),
            shape(padded),
            shape((rows, 2 * width)),
            shape(columns),
            shape((rows, width), BF16),
            shape((seqs, width)),
            shape((devices, 2, seqs, width)),
            shape((width, 2 * width), BF16),
            shape((TILE, width)),
            shape(((seqs + 1) * TILE, width)),
        ),
        in_specs=[HBM] * 3 + [VMEM] * 8 + [pl.BlockSpec(memory_space=pltpu.SMEM)] + [VMEM] * 2,
        out_specs=(HBM,) * 5 + (VMEM,) * 6,
        scratch_shapes=[
            pltpu.VMEM((rows, model), F32),
            pltpu.VMEM((model, width), BF16),
            pltpu.VMEM((model, width), BF16),
            pltpu.VMEM((rows, model), BF16),
            pltpu.VMEM((rows, width), F32),
            pltpu.VMEM(padded, F32),
            pltpu.VMEM((rows, 2 * width), F32),
            pltpu.VMEM(columns, F32),
            pltpu.VMEM((rows, width), F32),
            pltpu.VMEM(spaced, F32),
            pltpu.VMEM(spaced, F32),
            pltpu.VMEM((2, span, width), F32),
            pltpu.VMEM((seqs, TILE, width), F32),
            pltpu.VMEM((seqs, TILE, width), F32),
            pltpu.VMEM((2, seqs, width), F32),
            dma((groups + 2,)),
            dma((4,)),
            dma((groups,)),
            dma((devices - 1,)),
            dma((devices - 1,)),
            dma((1,)),
            dma((1,)),
        ],
        compiler_params=params(0),
        cost_estimate=cost(50),
        name="recurrence_forward",
    )(*args)


def widen(array, width):
    short = width - array.shape[-1]
    if short == 0:
        return array
    return jnp.pad(array, [(0, 0)] * (array.ndim - 1) + [(0, short)])


def per_device(
    stream,
    norm_in,
    w_branch,
    w_input,
    conv_kernel,
    conv_bias,
    gate_r,
    bias_r,
    gate_i,
    bias_i,
    decay_param,
    w_out,
    norm_mlp,
    w_gate,
    w_up,
    w_down,
    state_init,
    conv_init,
    fresh_rows,
    out_grad,
):
    seqs, span, model = stream.shape
    channels = w_branch.shape[1]
    mlp_dev = w_gate.shape[1]
    heads, head_width = gate_r.shape[:2]
    taps = conv_kernel.shape[0]
    edge = taps - 1
    rows = seqs * span
    devices = lax.axis_size("seq")
    position = lax.axis_index("seq")
    width = -(-channels // 128) * 128

    flat_in = stream.reshape(rows, model)
    flat_grad = out_grad.reshape(rows, model)
    w_branch_p = widen(w_branch, width)
    w_input_p = widen(w_input, width)
    w_out_p = jnp.pad(w_out, ((0, width - channels), (0, 0))) if width > channels else w_out
    taps_p = widen(conv_kernel, width)
    def line(value):
        return widen(value, width)

    (
        normed,
        branch,
        padded,
        pre,
        hidden,
        mixed,
        carry,
        sums,
        gates,
        rates,
        ends,
    ) = recurrence_forward(
        span,
        flat_in,
        w_input_p,
        w_branch_p,
        norm_in[None],
        taps_p,
        line(conv_bias),
        line(decay_param),
        line(bias_r),
        line(bias_i),
        gate_r,
        gate_i,
        fresh_rows,
        widen(state_init, width),
        widen(jnp.swapaxes(conv_init, 0, 1), width),
    )
    made = middle_call(mixed, w_out_p, flat_in, flat_grad, norm_mlp[None], w_gate, w_up, w_down)
    block_part, resid_low, own_grad, mlp_grads, rest, own, norm_mlp_acc = made[5:]
    mlp_grads = lax.psum_scatter(mlp_grads, "seq", scatter_dimension=1, tiled=True)
    block_out, rec_grads, grad_branch, input_low, first_rows, acc, blocks = backward_call(
        span,
        heads,
        head_width,
        block_part,
        own,
        resid_low,
        w_out_p,
        branch,
        hidden,
        pre,
        padded,
        normed,
        mixed,
        rest,
        gates,
        w_branch_p,
        w_input_p,
        carry,
        sums,
        taps_p,
        rates,
    )

    rec_grads, grad_branch, mlp_grads = lax.optimization_barrier(
        (rec_grads, grad_branch, mlp_grads)
    )
    rec_grads = lax.psum_scatter(rec_grads, "seq", scatter_dimension=1, tiled=True)

    stream_grad, norm_grads, small = last_call(
        first_rows,
        own_grad,
        flat_in,
        grad_branch,
        input_low,
        w_branch_p,
        w_input_p,
        norm_in[None],
        norm_mlp_acc,
        acc,
        ends,
        blocks,
    )
    (
        block_out,
        stream_grad,
        w_gate_grad,
        w_up_grad,
        w_branch_grad,
        w_input_grad,
        w_down_grad,
        w_out_grad,
        gate_r_grad,
        gate_i_grad,
        taps_grad,
        conv_bias_grad,
        bias_r_grad,
        bias_i_grad,
        decay_grad,
        norm_in_grad,
        norm_mlp_grad,
        final_state,
        final_conv,
    ) = finish_call(
        seqs,
        heads,
        head_width,
        edge,
        block_out,
        stream_grad,
        mlp_grads,
        rec_grads,
        small,
        norm_grads,
        line(decay_param),
    )
    return (
        block_out.reshape(stream.shape),
        stream_grad.reshape(stream.shape),
        norm_in_grad,
        w_branch_grad[:, :channels],
        w_input_grad[:, :channels],
        taps_grad[:, :channels],
        conv_bias_grad[:channels],
        gate_r_grad,
        bias_r_grad[:channels],
        gate_i_grad,
        bias_i_grad[:channels],
        decay_grad[:channels],
        w_out_grad[:channels],
        norm_mlp_grad,
        w_gate_grad,
        w_up_grad,
        w_down_grad,
        final_state[:, :channels],
        jnp.swapaxes(final_conv, 0, 1)[:, :, :channels],
    )


def solution(mesh):
    seq_rows = P(None, "seq", None)
    columns = P(None, "mp")
    channel = P("mp")
    return jax.shard_map(
        per_device,
        mesh=mesh,
        in_specs=(
            seq_rows,
            P(),
            columns,
            columns,
            columns,
            channel,
            P("mp", None, None),
            channel,
            P("mp", None, None),
            channel,
            channel,
            P("mp", None),
            P(),
            columns,
            columns,
            P("mp", None),
            columns,
            P(None, None, "mp"),
            P(),
            seq_rows,
        ),
        out_specs=(
            seq_rows,
            seq_rows,
            P(),
            P("seq", "mp"),
            P("seq", "mp"),
            columns,
            channel,
            P("mp", None, None),
            channel,
            P("mp", None, None),
            channel,
            channel,
            P("mp", "seq"),
            P(),
            P("seq", "mp"),
            P("seq", "mp"),
            P("mp", "seq"),
            columns,
            P(None, None, "mp"),
        ),
        check_vma=False,
    )
```
